32 devices in a mesh: dp: 4 (over y, x), seq: 4 (over z), head: 2 (over core).
Axes of the slice: x: 2, y: 2, z: 4, core: 2. Of those that a mesh axis runs over, the one named last changes fastest.
Arguments:
- states: bfloat16 [4, 512, 2432], P('dp', 'seq'), may hold values from -6 to 6
- adjoint: float32 [4, 512, 2432], P('dp', 'seq'), may hold values from -16 to 16
- text_kv: bfloat16 [4, 32, 2, 1280], P('dp', 'seq', None, 'head'), may hold values from -125 to 125
- text_len: int32 [4], P('dp'), may hold values from 8 to 32, as said below
- step_index: int32 [4], P('dp'), may hold values from 0 to 27
- modulation: float32 [28, 3, 2432], replicated, may hold values from -3 to 3
- w_qkv: bfloat16 [2432, 3, 1280], P('dp', None, 'head'), may hold values from -0.125 to 0.125
- qk_gain: float32 [2, 64], replicated, may hold values from 0.1 to 1.9
- w_out: bfloat16 [1280, 2432], P('head', 'dp'), may hold values from -0.15625 to 0.15625
Outputs:
- pulled: float32 [4, 512, 2432], P('dp', 'seq', 'head')
The draws below stay inside these ranges and needn't reach their ends.
Inputs may be any that keep to these rules, and one draw needn't show every extreme that they name: `text_len`: some trajectory has all 32 text tokens and some has 8.
All inputs are finite; a program needn't handle non-finite values.
Results may differ from the reference program's by a relative error of at most 0.02.
The reference program's roundings to bfloat16 on the way (of `modulated`, `queries`, `cotangent`, `out_grad`, `grad_scores`, `grad_query` and `stacked`) count: a program that leaves them out, or rounds other values in their place, can miss the bound.
Values may be sent and summed in bfloat16 or wider, within the bound.
No kernel may reach another device: no remote copies, remote signals or barrier semaphores. Data moves between devices by JAX's collectives and lax.ppermute only.
A program may use at most 192 MiB of HBM per device.

```python
import jax
import jax.numpy as jnp
from jax import lax

D = 2432
HEADS = 20
HD = 64
TABLE = 28
B = 4
IMG = 512
TXT = 32


def draw_adjoint(key, part):
    key = jax.random.fold_in(key, 11)
    noise_base = jnp.clip(jax.random.normal(key, (B, IMG, D), jnp.float32), -4.0, 4.0)
    growth = 2.0
    rising = 1.0 + growth * jnp.arange(IMG, dtype=jnp.float32) / max(IMG - 1, 1)
    return noise_base * rising[None, :, None]


def value_spread(key):
    return jax.random.uniform(key, (B, TXT), jnp.float32, 0.5, 3.0)


def draw_text_kv(key, part):
    key = jax.random.fold_in(key, 12)
    full_shape = (B, TXT, 2, HEADS * HD)
    spread = value_spread(jax.random.fold_in(key, 5))
    noise_base = jnp.clip(jax.random.normal(key, full_shape, jnp.float32), -4.0, 4.0)
    key_factor = jnp.ones((B, TXT), jnp.float32)
    factors = jnp.stack([key_factor, spread], axis=2)
    return (noise_base * factors[:, :, :, None]).astype(jnp.bfloat16)


def draw_text_len(key, part):
    key = jax.random.fold_in(key, 13)
    lengths = jax.random.randint(key, (B,), TXT // 4, TXT + 1)
    return lengths.at[0].set(TXT).at[B - 1].set(TXT // 4)


def draw_step_index(key, part):
    key = jax.random.fold_in(key, 14)
    chosen = jax.random.randint(key, (B,), 0, TABLE)
    return chosen.at[0].set(TABLE - 1).at[B - 1].set(0)


def shard_levels(key, shape, shards, low, top_value):
    factor_of, own = 1.0, jax.random.fold_in(key, 6)
    for position, parts in shards:
        steps = jnp.exp(jax.random.uniform(jax.random.fold_in(own, position), (parts,), jnp.float32, low / len(shards), top_value / len(shards)))
        factor_of = factor_of * jnp.repeat(steps, shape[position] // parts).reshape([-1 if axis == position else 1 for axis in range(len(shape))])
    return factor_of


def noise(stream_key, extent, deviation, reach, shards=(), held_as=jnp.bfloat16):
    gain = shard_levels(stream_key, extent, shards, -0.22, 0.18) if shards else 1.0
    values = jax.random.normal(stream_key, extent, jnp.float32) * deviation * gain
    return jnp.minimum(jnp.maximum(values, -reach), reach).astype(held_as)


def setup_inputs(seed: int = 0) -> dict:
    streams_of = jax.random.split(jax.random.key(seed), 10)
    return {
        "states": noise(streams_of[0], (B, IMG, D), 1.0, 6.0, ((0, 4), (1, 4))),
        "adjoint": draw_adjoint(jax.random.fold_in(streams_of[9], 71), 0),
        "text_kv": draw_text_kv(jax.random.fold_in(streams_of[9], 71), 0),
        "text_len": draw_text_len(jax.random.fold_in(streams_of[9], 71), 0),
        "step_index": draw_step_index(jax.random.fold_in(streams_of[9], 71), 0),
        "modulation": noise(streams_of[5], (TABLE, 3, D), 0.5, 3.0, (), jnp.float32),
        "w_qkv": noise(streams_of[6], (D, 3, HEADS * HD), D ** -0.5, 0.125, ((0, 4), (2, 2))),
        "qk_gain": jnp.clip(1.0 + 0.18 * jax.random.normal(streams_of[7], (2, HD), jnp.float32), 0.1, 1.9),
        "w_out": noise(streams_of[8], (HEADS * HD, D), (HEADS * HD) ** -0.5, 0.15625, ((0, 2), (1, 4))),
    }


def qk_normalize(values, gains):
    inverse = lax.rsqrt(lax.optimization_barrier(jnp.mean(values * values, axis=-1, keepdims=True)) + 1e-06)
    return ((values * inverse * gains).astype(jnp.bfloat16), inverse)

def qk_backward(values, inverse, cotangent, gains):
    scaled = cotangent.astype(jnp.float32) * gains
    return scaled * inverse - values * lax.optimization_barrier(jnp.mean(scaled * values, axis=-1, keepdims=True)) * inverse ** 3

def head_major(tensor):
    return jnp.transpose(tensor, (1, 0, 2))

def one_sample(hidden_state, adjoint_rows, text_pair, text_count, step_number, modulation, w_qkv, qk_gain, w_out):
    tok_count, model_width = hidden_state.shape
    inner_width = w_qkv.shape[2]
    head_count = inner_width // HD
    score_scale = HD ** (-0.5)
    squares = jnp.sum(adjoint_rows * adjoint_rows)
    clip_limit = 0.5 * (tok_count * model_width) ** 0.5
    clip_scale = jnp.minimum(1.0, clip_limit / jnp.sqrt(squares + 1e-06))
    table_row = lax.dynamic_index_in_dim(modulation, step_number, 0, keepdims=False)
    offset_row = table_row[0]
    stretch = table_row[1]
    gating = table_row[2]
    widened = hidden_state.astype(jnp.float32)
    centered = widened - lax.optimization_barrier(jnp.mean(widened, axis=-1, keepdims=True))
    inv_std = lax.rsqrt(lax.optimization_barrier(jnp.mean(centered * centered, axis=-1, keepdims=True)) + 1e-06)
    normed = centered * inv_std
    modulated = (normed * (1.0 + stretch) + offset_row).astype(jnp.bfloat16)
    projected = jnp.dot(modulated, w_qkv.reshape(model_width, 3 * inner_width), preferred_element_type=jnp.float32)
    projected = projected.reshape(tok_count, 3, head_count, HD)
    queries, query_inv = qk_normalize(projected[:, 0], qk_gain[0])
    own_keys, key_inv = qk_normalize(projected[:, 1], qk_gain[1])
    own_values = projected[:, 2].astype(jnp.bfloat16)
    cotangent = (gating * (clip_scale * adjoint_rows)).astype(jnp.bfloat16)
    out_grad = jnp.dot(cotangent, w_out.T, preferred_element_type=jnp.float32).astype(jnp.bfloat16)
    out_grad = out_grad.reshape(tok_count, head_count, HD)
    text_keys = text_pair[:, 0].reshape(-1, head_count, HD)
    text_values = text_pair[:, 1].reshape(-1, head_count, HD)
    text_total = text_keys.shape[0]
    allowed = jnp.concatenate([jnp.ones((tok_count,), dtype=bool), jnp.arange(text_total, dtype=jnp.int32) < text_count])
    key_rows = jnp.concatenate([own_keys, text_keys], axis=0)
    value_rows = jnp.concatenate([own_values, text_values], axis=0)

    def per_head(operands):
        query_head, key_head, value_head, grad_head = operands
        scores = jnp.dot(query_head, key_head.T, preferred_element_type=jnp.float32) * score_scale
        scores = jnp.where(allowed[None, :], scores, -1e+30)
        row_max = lax.optimization_barrier(jnp.max(scores, axis=-1, keepdims=True))
        log_total = row_max + jnp.log(lax.optimization_barrier(jnp.sum(jnp.exp(scores - row_max), axis=-1, keepdims=True)))
        weights = jnp.exp(scores - log_total)
        grad_weights = jnp.dot(grad_head, value_head.T, preferred_element_type=jnp.float32)
        delta_row = lax.optimization_barrier(jnp.sum(weights * grad_weights, axis=-1, keepdims=True))
        grad_scores = (weights * (grad_weights - delta_row)).astype(jnp.bfloat16)
        rounded = weights.astype(jnp.bfloat16)
        grad_query = (jnp.dot(grad_scores, key_head, preferred_element_type=jnp.float32) * score_scale).astype(jnp.bfloat16)
        grad_key = (jnp.dot(grad_scores.T, query_head, preferred_element_type=jnp.float32)[:tok_count] * score_scale).astype(jnp.bfloat16)
        grad_value = jnp.dot(rounded.T, grad_head, preferred_element_type=jnp.float32)[:tok_count].astype(jnp.bfloat16)
        return (grad_query, grad_key, grad_value)
    head_grads = lax.map(per_head, (head_major(queries), head_major(key_rows), head_major(value_rows), head_major(out_grad)))
    grad_query = head_major(head_grads[0])
    grad_key = head_major(head_grads[1])
    grad_value = head_major(head_grads[2])
    raw_query = qk_backward(projected[:, 0], query_inv, grad_query, qk_gain[0])
    raw_key = qk_backward(projected[:, 1], key_inv, grad_key, qk_gain[1])
    stacked = jnp.stack([raw_query, raw_key, grad_value.astype(jnp.float32)], axis=1).astype(jnp.bfloat16)
    grad_modulated = jnp.dot(stacked.reshape(tok_count, 3 * inner_width), w_qkv.reshape(model_width, 3 * inner_width).T, preferred_element_type=jnp.float32)
    grad_scaled = grad_modulated * (1.0 + stretch)
    grad_state = inv_std * (grad_scaled - lax.optimization_barrier(jnp.mean(grad_scaled, axis=-1, keepdims=True)) - normed * lax.optimization_barrier(jnp.mean(grad_scaled * normed, axis=-1, keepdims=True)))
    return clip_scale * adjoint_rows + grad_state

def reference(states, adjoint, text_kv, text_len, step_index, modulation, w_qkv, qk_gain, w_out):
    results = []
    for sample in range(states.shape[0]):
        results.append(one_sample(states[sample], adjoint[sample], text_kv[sample], text_len[sample], step_index[sample], modulation, w_qkv, qk_gain, w_out))
    return jnp.stack(results)
```

```python
import functools

import jax
import jax.numpy as jnp
from jax import lax
from jax.experimental import pallas as pl
from jax.experimental.pallas import tpu as pltpu
from jax.sharding import PartitionSpec as P

HD = 64
TEXT_PAD = 128
NT = (((1,), (1,)), ((), ()))
TN = (((0,), (0,)), ((), ()))


def line_ring(count):
    return [0] + list(range(1, count, 2)) + [i for i in range(count - 1, 0, -1) if i % 2 == 0]


def ring_pairs(order):
    return [(order[i], order[(i + 1) % len(order)]) for i in range(len(order))]


def ring_place(order, index):
    place = jnp.int32(0)
    for position, member in enumerate(order):
        place = jnp.where(index == member, jnp.int32(position), place)
    return place


def ring_member(order, place):
    member = jnp.int32(order[0])
    for position, value in enumerate(order):
        member = jnp.where(place == position, jnp.int32(value), member)
    return member


def block_kernel(
    slots, blocks, rows, shard, width,
    scalars, gain, bias, text, *refs,
):
    count = blocks
    shards_w = width // shard
    refs = list(refs)
    take = lambda n: [refs.pop(0) for _ in range(n)]
    mod_in = take(2 * count - 1)
    cot_in = take(2 * count - 1)
    w_in = take(shards_w)
    mine_out, theirs_out = take(2)
    w_all, mod_all, cot_all, sems = take(4)
    q_all, k_all, v_all, d_all, raw_q, raw_k, grad_k, grad_v, stacked = take(9)
    inner = slots * HD
    half_rows = rows // 2
    core = scalars[0]
    copies = []

    def start(source, target):
        copy = pltpu.make_async_copy(source, target, sems.at[len(copies)])
        copy.start()
        copies.append(copy)

    for k in range(shards_w):
        offset = pl.multiple_of(scalars[1 + k] * shard, 16)
        start(w_in[k], w_all.at[pl.ds(offset, shard)])
    for source, target in ((mod_in, mod_all), (cot_in, cot_all)):
        start(source[0], target.at[pl.ds(0, rows)])
        for j in range(1, count):
            near = pl.multiple_of(j * rows + core * half_rows, 16)
            far = pl.multiple_of(j * rows + (1 - core) * half_rows, 16)
            start(source[2 * j - 1], target.at[pl.ds(near, half_rows)])
            start(source[2 * j], target.at[pl.ds(far, half_rows)])
    for copy in copies:
        copy.wait()

    gain_q = gain[0:1, :]
    gain_k = gain[1:2, :]
    score_scale = HD ** (-0.5)

    def inverse_rms(raw):
        return lax.rsqrt(jnp.mean(raw * raw, axis=-1, keepdims=True) + 1e-06)

    @pl.loop(0, count)
    def project(b):
        here = pl.ds(pl.multiple_of(b * rows, rows), rows)
        projected = jnp.dot(
            mod_all[here, :], w_all[:, : 3 * inner], preferred_element_type=jnp.float32
        )
        out_grad = jnp.dot(
            cot_all[here, :], w_all[:, 3 * inner :], preferred_element_type=jnp.float32
        )
        for i in range(slots):
            query = projected[:, i * HD : (i + 1) * HD]
            key = projected[:, inner + i * HD : inner + (i + 1) * HD]
            value = projected[:, 2 * inner + i * HD : 2 * inner + (i + 1) * HD]
            raw_q[i, here, :] = query
            raw_k[i, here, :] = key
            q_all[i, here, :] = (query * inverse_rms(query) * gain_q).astype(jnp.bfloat16)
            k_all[i, here, :] = (key * inverse_rms(key) * gain_k).astype(jnp.bfloat16)
            v_all[i, here, :] = value.astype(jnp.bfloat16)
            d_all[i, here, :] = out_grad[:, i * HD : (i + 1) * HD].astype(jnp.bfloat16)

    grad_k[...] = jnp.zeros_like(grad_k)
    grad_v[...] = jnp.zeros_like(grad_v)

    def norm_backward(raw, cotangent, gains):
        inverse = inverse_rms(raw)
        scaled = cotangent.astype(jnp.float32) * gains
        return (
            scaled * inverse
            - raw * jnp.mean(scaled * raw, axis=-1, keepdims=True) * (inverse * inverse * inverse)
        )

    def dot(a, b, dims):
        return lax.dot_general(a, b, dims, preferred_element_type=jnp.float32)

    NN = (((1,), (0,)), ((), ()))

    @pl.loop(0, count)
    def attend(b):
        here = pl.ds(pl.multiple_of(b * rows, rows), rows)
        for i in range(slots):
            query = q_all[i, here, :]
            grad = d_all[i, here, :]
            keys, values = k_all[i], v_all[i]
            text_keys, text_values = text[0, i], text[1, i]
            scores = dot(query, keys, NT) * score_scale
            text_scores = dot(query, text_keys, NT) * score_scale + bias[0:1, :]
            row_max = jnp.maximum(
                jnp.max(scores, axis=-1, keepdims=True), jnp.max(text_scores, axis=-1, keepdims=True)
            )
            exps = jnp.exp(scores - row_max)
            text_exps = jnp.exp(text_scores - row_max)
            total = jnp.sum(exps, axis=-1, keepdims=True) + jnp.sum(text_exps, axis=-1, keepdims=True)
            inverse = 1.0 / total
            weights = exps * inverse
            text_weights = text_exps * inverse
            grad_w = dot(grad, values, NT)
            text_grad_w = dot(grad, text_values, NT)
            delta = jnp.sum(weights * grad_w, axis=-1, keepdims=True) + jnp.sum(
                text_weights * text_grad_w, axis=-1, keepdims=True
            )
            grad_s = (weights * (grad_w - delta)).astype(jnp.bfloat16)
            text_grad_s = (text_weights * (text_grad_w - delta)).astype(jnp.bfloat16)
            grad_q = dot(grad_s, keys, NN) + dot(text_grad_s, text_keys, NN)
            grad_q = (grad_q * score_scale).astype(jnp.bfloat16)
            grad_k[i] += dot(grad_s, query, TN)
            grad_v[i] += dot(weights.astype(jnp.bfloat16), grad, TN)
            valid = scalars[1 + shards_w + i] > 0
            raw_grad = norm_backward(raw_q[i, here, :], grad_q, gain_q)
            stacked[here, i * HD : (i + 1) * HD] = jnp.where(valid, raw_grad, 0.0)

    @pl.loop(0, count)
    def backward(b):
        here = pl.ds(pl.multiple_of(b * rows, rows), rows)
        for i in range(slots):
            valid = scalars[1 + shards_w + i] > 0
            key_grad = (grad_k[i, here, :] * score_scale).astype(jnp.bfloat16)
            raw_grad = norm_backward(raw_k[i, here, :], key_grad, gain_k)
            stacked[here, inner + i * HD : inner + (i + 1) * HD] = jnp.where(valid, raw_grad, 0.0)
            stacked[here, 2 * inner + i * HD : 2 * inner + (i + 1) * HD] = jnp.where(
                valid, grad_v[i, here, :], 0.0
            )
        left = stacked[here, :].astype(jnp.bfloat16)
        half = width // 2
        mine = pl.ds(pl.multiple_of(core * half, 16), half)
        theirs = pl.ds(pl.multiple_of((1 - core) * half, 16), half)
        mine_out[here, :] = dot(left, w_all[mine, : 3 * inner], NT)
        theirs_out[here, :] = dot(left, w_all[theirs, : 3 * inner], NT).astype(jnp.bfloat16)


def block_call(scalars, gain, bias, text, mod, cot, weights, slots, rows):
    count = (len(mod) + 1) // 2
    shard = weights[0].shape[0]
    width = mod[0].shape[1]
    tokens = rows * count
    inner = slots * HD
    anywhere = pl.BlockSpec(memory_space=pl.ANY)
    vmem = pl.BlockSpec(memory_space=pltpu.VMEM)
    f32, bf16 = jnp.float32, jnp.bfloat16
    return pl.pallas_call(
        functools.partial(block_kernel, slots, count, rows, shard, width),
        out_shape=(
            jax.ShapeDtypeStruct((tokens, width // 2), f32),
            jax.ShapeDtypeStruct((tokens, width // 2), bf16),
        ),
        in_specs=[pl.BlockSpec(memory_space=pltpu.SMEM), vmem, vmem, vmem]
        + [anywhere] * (len(mod) + len(cot) + len(weights)),
        out_specs=(vmem, vmem),
        scratch_shapes=[
            pltpu.VMEM((width, 4 * inner), bf16),
            pltpu.VMEM((tokens, width), bf16),
            pltpu.VMEM((tokens, width), bf16),
            pltpu.SemaphoreType.DMA((len(mod) + len(cot) + len(weights),)),
        ]
        + [pltpu.VMEM((slots, tokens, HD), bf16)] * 4
        + [pltpu.VMEM((slots, tokens, HD), f32)] * 4
        + [pltpu.VMEM((tokens, 3 * inner), f32)],
        compiler_params=pltpu.CompilerParams(vmem_limit_bytes=44 * 1024 * 1024),
        cost_estimate=pl.CostEstimate(
            flops=2 * tokens * width * 7 * inner + 10 * tokens * tokens * inner,
            bytes_accessed=2 * (2 * tokens * width + 4 * width * inner) + 3 * tokens * width,
            transcendentals=slots * tokens * tokens,
        ),
    )(scalars, gain, bias, text, *mod, *cot, *weights)


def shards_by_head(states, adjoint, text_kv, text_len, step_index, modulation, w_qkv, qk_gain, w_out):
    hidden_state = states[0]
    adjoint_rows = adjoint[0]
    tok_count, model_width = hidden_state.shape
    seq_count = lax.axis_size("seq")
    dp_count = lax.axis_size("dp")
    head_count = lax.axis_size("head")
    inner_dev = w_qkv.shape[2]
    heads_dev = inner_dev // HD
    shard = w_qkv.shape[0]
    slots = -(-heads_dev // seq_count)
    inner = slots * HD
    core = lax.axis_index("head")
    seq_index = lax.axis_index("seq")

    seq_order = line_ring(seq_count)
    seq_place = ring_place(seq_order, seq_index)
    seq_next = ring_pairs(seq_order)
    dp_order = line_ring(dp_count)
    dp_place = ring_place(dp_order, lax.axis_index("dp"))
    dp_next = [
        (a * head_count + c, b * head_count + c) if c % 2 == 0 else (b * head_count + c, a * head_count + c)
        for a, b in ring_pairs(dp_order)
        for c in range(head_count)
    ]
    swap = [(0, 1), (1, 0)]

    first = seq_index * heads_dev // seq_count
    stop = (seq_index + 1) * heads_dev // seq_count
    window = jnp.minimum(first, heads_dev - slots)
    valid = [((window + i >= first) & (window + i < stop)).astype(jnp.int32) for i in range(slots)]

    squares = jnp.sum(adjoint_rows * adjoint_rows)
    total = squares
    for k in range(1, seq_count):
        pairs = [(seq_order[i], seq_order[(i + k) % seq_count]) for i in range(seq_count)]
        total = total + lax.ppermute(squares, "seq", pairs)
    clip_limit = 0.5 * (tok_count * seq_count * model_width) ** 0.5
    clip_scale = jnp.minimum(1.0, clip_limit / jnp.sqrt(total + 1e-06))

    own_w = jnp.concatenate(
        [
            lax.dynamic_slice_in_dim(w_qkv, window * HD, inner, 2).reshape(shard, 3 * inner),
            lax.dynamic_slice_in_dim(w_out, window * HD, inner, 0).T,
        ],
        axis=1,
    )
    weights = [own_w]
    for k in range(1, dp_count):
        weights.append(lax.ppermute(weights[-1], ("dp", "head"), dp_next))
    direction = jnp.where(core == 0, -1, 1)
    w_index = [
        ring_member(dp_order, (dp_place + direction * k + dp_count) % dp_count) for k in range(dp_count)
    ]

    table_row = lax.dynamic_index_in_dim(modulation, step_index[0], 0, keepdims=False)
    offset_row = table_row[0]
    stretch = table_row[1]
    gating = table_row[2]
    widened = hidden_state.astype(jnp.float32)
    centered = widened - jnp.mean(widened, axis=-1, keepdims=True)
    inv_std = lax.rsqrt(jnp.mean(centered * centered, axis=-1, keepdims=True) + 1e-06)
    normed = centered * inv_std
    modulated = (normed * (1.0 + stretch) + offset_row).astype(jnp.bfloat16)
    cotangent = (gating * (clip_scale * adjoint_rows)).astype(jnp.bfloat16)

    half_rows = tok_count // 2

    def gather(rows):
        pieces = [rows]
        moving = lax.dynamic_slice_in_dim(rows, core * half_rows, half_rows, 0)
        for k in range(1, seq_count):
            moving = lax.ppermute(moving, "seq", seq_next)
            pieces += [moving, lax.ppermute(moving, "head", swap)]
        return pieces

    mod_pieces = gather(modulated)
    cot_pieces = gather(cotangent)

    text_local = text_kv[0]
    text_dev = text_local.shape[0]
    text_pieces = [text_local]
    for k in range(1, seq_count):
        pairs = [(seq_order[i], seq_order[(i + k) % seq_count]) for i in range(seq_count)]
        text_pieces.append(lax.ppermute(text_local, "seq", pairs))
    text_rows = jnp.concatenate(text_pieces, axis=0)
    text_total = text_dev * seq_count
    text_rows = lax.dynamic_slice_in_dim(text_rows, window * HD, inner, 2)
    text_rows = text_rows.reshape(text_total, 2, slots, HD).transpose(1, 2, 0, 3)
    text_rows = jnp.pad(text_rows, ((0, 0), (0, 0), (0, TEXT_PAD - text_total), (0, 0)))
    owners = jnp.stack(
        [ring_member(seq_order, (seq_place - k + seq_count) % seq_count) for k in range(seq_count)]
    )
    text_ids = (owners[:, None] * text_dev + jnp.arange(text_dev, dtype=jnp.int32)[None, :]).reshape(-1)
    bias = jnp.where(text_ids < text_len[0], 0.0, -1e30).astype(jnp.float32)
    bias = jnp.pad(bias, (0, TEXT_PAD - text_total), constant_values=-1e30)[None, :]

    scalars = jnp.stack([core.astype(jnp.int32)] + w_index + valid).astype(jnp.int32)
    mine, theirs = block_call(
        scalars, qk_gain, bias, text_rows, mod_pieces, cot_pieces, weights, slots, tok_count
    )

    def chip_sum(j):
        here = slice(j * tok_count, (j + 1) * tok_count)
        return mine[here] + lax.ppermute(theirs[here], "head", swap).astype(jnp.float32)

    moving = chip_sum(1).astype(jnp.bfloat16)
    for j in range(2, seq_count):
        moving = lax.ppermute(moving, "seq", seq_next)
        moving = (chip_sum(j) + moving.astype(jnp.float32)).astype(jnp.bfloat16)
    moving = lax.ppermute(moving, "seq", seq_next)
    grad_share = chip_sum(0) + moving.astype(jnp.float32)

    half_width = model_width // head_count
    first_col = core * half_width
    normed_share = lax.dynamic_slice_in_dim(normed, first_col, half_width, 1)
    stretch_share = lax.dynamic_slice_in_dim(stretch, first_col, half_width, 0)
    adjoint_share = lax.dynamic_slice_in_dim(adjoint_rows, first_col, half_width, 1)
    grad_scaled = grad_share * (1.0 + stretch_share)
    row_sums = jnp.stack(
        [jnp.sum(grad_scaled, axis=-1), jnp.sum(grad_scaled * normed_share, axis=-1)], axis=-1
    )
    row_sums = row_sums + lax.ppermute(row_sums, "head", swap)
    grad_state = inv_std * (
        grad_scaled - row_sums[:, 0:1] / model_width - normed_share * row_sums[:, 1:2] / model_width
    )
    pulled = clip_scale * adjoint_share + grad_state
    return pulled[None]


def qk_normalize(values, gains):
    inverse = lax.rsqrt(jnp.mean(values * values, axis=-1, keepdims=True) + 1e-06)
    return ((values * inverse * gains).astype(jnp.bfloat16), inverse)


def qk_backward(values, inverse, cotangent, gains):
    scaled = cotangent.astype(jnp.float32) * gains
    return (
        scaled * inverse - values * jnp.mean(scaled * values, axis=-1, keepdims=True) * inverse**3
    )


def shards_by_row(states, adjoint, text_kv, text_len, step_index, modulation, w_qkv, qk_gain, w_out):
    hidden_state = states[0]
    adjoint_rows = adjoint[0]
    tok_count, model_width = hidden_state.shape
    seq_count = lax.axis_size("seq")
    inner_dev = w_qkv.shape[2]
    heads_dev = inner_dev // HD
    score_scale = HD ** (-0.5)
    squares = lax.psum(jnp.sum(adjoint_rows * adjoint_rows), "seq")
    clip_limit = 0.5 * (tok_count * seq_count * model_width) ** 0.5
    clip_scale = jnp.minimum(1.0, clip_limit / jnp.sqrt(squares + 1e-06))
    table_row = lax.dynamic_index_in_dim(modulation, step_index[0], 0, keepdims=False)
    offset_row = table_row[0]
    stretch = table_row[1]
    gating = table_row[2]
    widened = hidden_state.astype(jnp.float32)
    centered = widened - jnp.mean(widened, axis=-1, keepdims=True)
    inv_std = lax.rsqrt(jnp.mean(centered * centered, axis=-1, keepdims=True) + 1e-06)
    normed = centered * inv_std
    modulated = (normed * (1.0 + stretch) + offset_row).astype(jnp.bfloat16)
    cotangent = (gating * (clip_scale * adjoint_rows)).astype(jnp.bfloat16)
    contract_last = (((1,), (1,)), ((), ()))
    full_weight = lax.all_gather(w_qkv, "dp", axis=0, tiled=True).reshape(
        model_width, 3 * inner_dev
    )
    projected = jnp.dot(modulated, full_weight, preferred_element_type=jnp.float32)
    out_raw = lax.dot_general(
        cotangent,
        lax.all_gather(w_out, "dp", axis=1, tiled=True),
        contract_last,
        preferred_element_type=jnp.float32,
    )
    projected = projected.reshape(tok_count, 3, heads_dev, HD)
    queries, query_inv = qk_normalize(projected[:, 0], qk_gain[0])
    own_keys, key_inv = qk_normalize(projected[:, 1], qk_gain[1])
    own_values = projected[:, 2].astype(jnp.bfloat16)
    out_grad = out_raw.astype(jnp.bfloat16).reshape(tok_count, heads_dev, HD)
    text_keys = text_kv[0, :, 0, :]
    text_values = text_kv[0, :, 1, :]
    text_dev = text_keys.shape[0]
    rows_dev = tok_count + text_dev
    key_local = jnp.concatenate([own_keys.reshape(tok_count, inner_dev), text_keys], axis=0)
    value_local = jnp.concatenate([own_values.reshape(tok_count, inner_dev), text_values], axis=0)
    key_all, value_all = (
        lax.all_gather(key_local, "seq", axis=0, tiled=True),
        lax.all_gather(value_local, "seq", axis=0, tiled=True),
    )
    all_rows = rows_dev * seq_count
    row_ids = jnp.arange(all_rows, dtype=jnp.int32)
    owner = row_ids // rows_dev
    within = row_ids % rows_dev
    allowed = (within < tok_count) | (owner * text_dev + within - tok_count < text_len[0])
    group = 1
    while group * 2 * rows_dev <= 512 and seq_count % (group * 2) == 0:
        group = group * 2
    block_rows = group * rows_dev
    block_count = all_rows // block_rows
    key_blocks = key_all.reshape(block_count, block_rows, heads_dev, HD)
    value_blocks = value_all.reshape(block_count, block_rows, heads_dev, HD)
    mask_blocks = allowed.reshape(block_count, block_rows)

    def block_scores(key_block, mask_block):
        scores = (
            jnp.einsum("qhd,khd->qhk", queries, key_block, preferred_element_type=jnp.float32)
            * score_scale
        )
        return jnp.where(mask_block[None, None, :], scores, -1e30)

    def first_pass(carry, block):
        row_max, row_sum, row_dot = carry
        key_block, value_block, mask_block = block
        scores = block_scores(key_block, mask_block)
        new_max = jnp.maximum(row_max, jnp.max(scores, axis=-1))
        rescale = jnp.exp(row_max - new_max)
        exps = jnp.exp(scores - new_max[:, :, None])
        grad_weights = jnp.einsum(
            "qhd,khd->qhk", out_grad, value_block, preferred_element_type=jnp.float32
        )
        return (
            (
                new_max,
                row_sum * rescale + jnp.sum(exps, axis=-1),
                row_dot * rescale + jnp.sum(exps * grad_weights, axis=-1),
            ),
            None,
        )

    start_state = (
        jnp.full((tok_count, heads_dev), -1e30, jnp.float32),
        jnp.zeros((tok_count, heads_dev), jnp.float32),
        jnp.zeros((tok_count, heads_dev), jnp.float32),
    )
    (row_max, row_sum, row_dot), unused = lax.scan(
        first_pass, start_state, (key_blocks, value_blocks, mask_blocks)
    )
    log_total = row_max + jnp.log(row_sum)
    delta_row = row_dot / row_sum

    def second_pass(running, block):
        key_block, value_block, mask_block = block
        weights = jnp.exp(block_scores(key_block, mask_block) - log_total[:, :, None])
        grad_weights = jnp.einsum(
            "qhd,khd->qhk", out_grad, value_block, preferred_element_type=jnp.float32
        )
        grad_scores = (weights * (grad_weights - delta_row[:, :, None])).astype(jnp.bfloat16)
        return (
            running
            + jnp.einsum(
                "qhk,khd->qhd", grad_scores, key_block, preferred_element_type=jnp.float32
            ),
            None,
        )

    query_sum, unused = lax.scan(
        second_pass,
        jnp.zeros((tok_count, heads_dev, HD), jnp.float32),
        (key_blocks, value_blocks, mask_blocks),
    )
    grad_query = (query_sum * score_scale).astype(jnp.bfloat16)
    log_all, delta_all = (
        lax.all_gather(log_total, "seq", axis=0, tiled=True),
        lax.all_gather(delta_row, "seq", axis=0, tiled=True),
    )
    local_ids = jnp.arange(rows_dev, dtype=jnp.int32)
    local_allowed = (local_ids < tok_count) | (
        lax.axis_index("seq") * text_dev + local_ids - tok_count < text_len[0]
    )
    key_three = key_local.reshape(rows_dev, heads_dev, HD)
    value_three = value_local.reshape(rows_dev, heads_dev, HD)
    query_piece = lax.all_gather(queries.reshape(tok_count, inner_dev), "seq", axis=0, tiled=True)
    grad_piece = lax.all_gather(out_grad.reshape(tok_count, inner_dev), "seq", axis=0, tiled=True)
    piece_rows = query_piece.shape[0]
    query_rows = query_piece.reshape(piece_rows, heads_dev, HD)
    grad_rows = grad_piece.reshape(piece_rows, heads_dev, HD)
    scores = (
        jnp.einsum("qhd,khd->qhk", query_rows, key_three, preferred_element_type=jnp.float32)
        * score_scale
    )
    scores = jnp.where(local_allowed[None, None, :], scores, -1e30)
    weights = jnp.exp(scores - log_all[:, :, None])
    grad_weights = jnp.einsum(
        "qhd,khd->qhk", grad_rows, value_three, preferred_element_type=jnp.float32
    )
    grad_scores = (weights * (grad_weights - delta_all[:, :, None])).astype(jnp.bfloat16)
    rounded = weights.astype(jnp.bfloat16)
    key_sum = jnp.einsum(
        "qhk,qhd->khd", grad_scores, query_rows, preferred_element_type=jnp.float32
    )
    value_sum = jnp.einsum("qhk,qhd->khd", rounded, grad_rows, preferred_element_type=jnp.float32)
    key_sum, value_sum = (key_sum, value_sum)
    grad_key = (key_sum[:tok_count] * score_scale).astype(jnp.bfloat16)
    grad_value = value_sum[:tok_count].astype(jnp.bfloat16)
    raw_query = qk_backward(projected[:, 0], query_inv, grad_query, qk_gain[0])
    raw_key = qk_backward(projected[:, 1], key_inv, grad_key, qk_gain[1])
    stacked = jnp.stack([raw_query, raw_key, grad_value.astype(jnp.float32)], axis=1).astype(
        jnp.bfloat16
    )
    stacked = stacked.reshape(tok_count, 3 * inner_dev)
    partial_grad = lax.dot_general(
        stacked, full_weight, contract_last, preferred_element_type=jnp.float32
    )
    half_width = model_width // lax.axis_size("head")
    first_col = lax.axis_index("head") * half_width
    grad_share = lax.psum_scatter(
        partial_grad.astype(jnp.bfloat16), "head", scatter_dimension=1, tiled=True
    ).astype(jnp.float32)
    normed_share = lax.dynamic_slice_in_dim(normed, first_col, half_width, 1)
    stretch_share = lax.dynamic_slice_in_dim(stretch, first_col, half_width, 0)
    adjoint_share = lax.dynamic_slice_in_dim(adjoint_rows, first_col, half_width, 1)
    grad_scaled = grad_share * (1.0 + stretch_share)
    row_sums = jnp.stack(
        [jnp.sum(grad_scaled, axis=-1), jnp.sum(grad_scaled * normed_share, axis=-1)], axis=-1
    )
    row_sums = lax.psum(row_sums, "head")
    grad_state = inv_std * (
        grad_scaled - row_sums[:, 0:1] / model_width - normed_share * row_sums[:, 1:2] / model_width
    )
    pulled = clip_scale * adjoint_share + grad_state
    return pulled[None]


def solution(mesh):
    in_specs = (
        P("dp", "seq", None),
        P("dp", "seq", None),
        P("dp", "seq", None, "head"),
        P("dp"),
        P("dp"),
        P(),
        P("dp", None, "head"),
        P(),
        P("head", "dp"),
    )
    out_specs = P("dp", "seq", "head")
    by_head = mesh.shape["seq"] <= 8 and mesh.shape["head"] == 2
    shards = shards_by_head if by_head else shards_by_row
    return jax.shard_map(shards, mesh=mesh, in_specs=in_specs, out_specs=out_specs, check_vma=False)
```

```python
import functools

import jax
import jax.numpy as jnp
from jax import lax
from jax.experimental import pallas as pl
from jax.experimental.pallas import tpu as pltpu
from jax.sharding import PartitionSpec as P

HD = 64
NT = (((1,), (1,)), ((), ()))
NN = (((1,), (0,)), ((), ()))


def line_ring(count):
    return [0] + list(range(1, count, 2)) + [i for i in range(count - 1, 0, -1) if i % 2 == 0]


def ring_pairs(order):
    return [(order[i], order[(i + 1) % len(order)]) for i in range(len(order))]


def ring_place(order, index):
    place = jnp.int32(0)
    for position, member in enumerate(order):
        place = jnp.where(index == member, jnp.int32(position), place)
    return place


def ring_member(order, place):
    member = jnp.int32(order[0])
    for position, value in enumerate(order):
        member = jnp.where(place == position, jnp.int32(value), member)
    return member


def dot(a, b, dims):
    return lax.dot_general(a, b, dims, preferred_element_type=jnp.float32)


def inverse_rms(raw):
    return lax.rsqrt(jnp.mean(raw * raw, axis=-1, keepdims=True) + 1e-06)


def norm_backward(raw, cotangent, gains):
    inverse = inverse_rms(raw)
    scaled = cotangent.astype(jnp.float32) * gains
    return (
        scaled * inverse
        - raw * jnp.mean(scaled * raw, axis=-1, keepdims=True) * (inverse * inverse * inverse)
    )


def spec(space):
    return pl.BlockSpec(memory_space=space)


def modulate_kernel(core_ref, states, offset, stretch, out):
    widened = states[...].astype(jnp.float32)
    centered = widened - jnp.mean(widened, axis=-1, keepdims=True)
    inv_std = lax.rsqrt(jnp.mean(centered * centered, axis=-1, keepdims=True) + 1e-06)
    out[...] = (centered * inv_std * (1.0 + stretch[...]) + offset[...]).astype(jnp.bfloat16)


def modulate_half(core, states, offset, stretch):
    rows, width = states.shape
    half = rows // 2
    return pl.pallas_call(
        modulate_kernel,
        out_shape=jax.ShapeDtypeStruct((half, width), jnp.bfloat16),
        grid_spec=pltpu.PrefetchScalarGridSpec(
            num_scalar_prefetch=1,
            grid=(1,),
            in_specs=[
                pl.BlockSpec((half, width), lambda i, core: (core[0], 0)),
                pl.BlockSpec((1, width), lambda i, core: (0, 0)),
                pl.BlockSpec((1, width), lambda i, core: (0, 0)),
            ],
            out_specs=pl.BlockSpec((half, width), lambda i, core: (0, 0)),
        ),
        cost_estimate=pl.CostEstimate(flops=8 * half * width, bytes_accessed=4 * half * width, transcendentals=0),
    )(core[None], states, offset, stretch)


def attention_kernel(slots, count, rows, shard, width, w_parts, scalars, gain, bias, text, text_t, *refs):
    dp_count = width // shard
    refs = list(refs)
    take = lambda n: [refs.pop(0) for _ in range(n)]
    mod_in = take(2 * count - 1)
    cot_in = take(2 * count - 1)
    w_in = take(w_parts * dp_count)
    mine_out, theirs_out, stacked_out = take(3)
    w_all, mod_all, cot_all, sems = take(4)
    q_all, k_all, v_all, d_all, k_t = take(5)
    raw_q, raw_k, grad_k, grad_v, back_q, stacked = take(6)
    inner = slots * HD
    half_rows = rows // 2
    tokens = rows * count
    core = scalars[0]
    copies = []

    def start(source, target):
        copy = pltpu.make_async_copy(source, target, sems.at[len(copies)])
        copy.start()
        copies.append(copy)
        return copy

    part_width = 4 * inner // w_parts
    w_copies = []
    for k in range(dp_count):
        offset = pl.multiple_of(scalars[1 + k] * shard, 16)
        for part in range(w_parts):
            columns = pl.ds(part * part_width, part_width)
            w_copies.append(start(w_in[part * dp_count + k], w_all.at[pl.ds(offset, shard), columns]))
    row_copies = []
    for j in range(count):
        these = []
        for source, target in ((mod_in, mod_all), (cot_in, cot_all)):
            if j == 0:
                these.append(start(source[0], target.at[pl.ds(0, rows)]))
                continue
            near = pl.multiple_of(j * rows + core * half_rows, 16)
            far = pl.multiple_of(j * rows + (1 - core) * half_rows, 16)
            these.append(start(source[2 * j - 1], target.at[pl.ds(near, half_rows)]))
            these.append(start(source[2 * j], target.at[pl.ds(far, half_rows)]))
        row_copies.append(these)

    gain_q = gain[0:1, :]
    gain_k = gain[1:2, :]
    score_scale = HD ** (-0.5)
    grad_k[...] = jnp.zeros_like(grad_k)
    grad_v[...] = jnp.zeros_like(grad_v)
    for copy in w_copies:
        copy.wait()

    span = 2 * rows
    for b in range(count // 2):
        for copy in row_copies[2 * b] + row_copies[2 * b + 1]:
            copy.wait()
        here = slice(b * span, (b + 1) * span)
        projected = jnp.dot(
            mod_all[here, :], w_all[:, : 3 * inner], preferred_element_type=jnp.float32
        )
        out_grad = jnp.dot(
            cot_all[here, :], w_all[:, 3 * inner :], preferred_element_type=jnp.float32
        )
        for i in range(slots):
            query = projected[:, i * HD : (i + 1) * HD]
            key = projected[:, inner + i * HD : inner + (i + 1) * HD]
            value = projected[:, 2 * inner + i * HD : 2 * inner + (i + 1) * HD]
            raw_q[i, here, :] = query
            raw_k[i, here, :] = key
            query = query * inverse_rms(query) * gain_q
            q_all[i, here, :] = (query * score_scale).astype(jnp.bfloat16)
            key = key * inverse_rms(key) * gain_k
            k_all[i, here, :] = key.astype(jnp.bfloat16)
            k_t[i, :, here] = key.T.astype(jnp.bfloat16)
            v_all[i, here, :] = value.astype(jnp.bfloat16)
            d_all[i, here, :] = out_grad[:, i * HD : (i + 1) * HD].astype(jnp.bfloat16)

    @pl.loop(0, slots * (count // 2))
    def attend(t):
        i = t // (count // 2)
        here = pl.ds(pl.multiple_of(t % (count // 2) * span, span), span)
        query = q_all[i, here, :]
        grad = d_all[i, here, :]
        scores = dot(k_all[i], query, NT)
        text_scores = dot(text[0, i], query, NT) + bias[...]
        col_max = jnp.maximum(
            jnp.max(scores, axis=0, keepdims=True), jnp.max(text_scores, axis=0, keepdims=True)
        )
        exps = jnp.exp(scores - col_max)
        text_exps = jnp.exp(text_scores - col_max)
        total = jnp.sum(exps, axis=0, keepdims=True) + jnp.sum(text_exps, axis=0, keepdims=True)
        inverse = 1.0 / total
        grad_w = dot(v_all[i], grad, NT)
        text_grad_w = dot(text[1, i], grad, NT)
        delta = inverse * (
            jnp.sum(exps * grad_w, axis=0, keepdims=True)
            + jnp.sum(text_exps * text_grad_w, axis=0, keepdims=True)
        )
        weights = exps * inverse
        grad_s = (weights * (grad_w - delta)).astype(jnp.bfloat16)
        text_grad_s = (text_exps * inverse * (text_grad_w - delta)).astype(jnp.bfloat16)
        grad_k[i] += dot(grad_s, query, NN)
        grad_v[i] += dot(weights.astype(jnp.bfloat16), grad, NN)
        grad_q = dot(k_t[i], grad_s, NN) + dot(text_t[i], text_grad_s, NN)
        grad_q = (grad_q.T * score_scale).astype(jnp.bfloat16)
        back_q[i, here, :] = norm_backward(raw_q[i, here, :], grad_q, gain_q)

    for i in range(slots):
        valid = scalars[1 + dp_count + i] > 0
        back_k = norm_backward(raw_k[i], grad_k[i].astype(jnp.bfloat16), gain_k)
        stacked[:, i * HD : (i + 1) * HD] = jnp.where(valid, back_q[i], 0.0)
        stacked[:, inner + i * HD : inner + (i + 1) * HD] = jnp.where(valid, back_k, 0.0)
        stacked[:, 2 * inner + i * HD : 2 * inner + (i + 1) * HD] = jnp.where(valid, grad_v[i], 0.0)
    stacked_out[...] = stacked[...].astype(jnp.bfloat16)
    half = width // 2
    mine = pl.ds(pl.multiple_of(core * half, 16), half)
    theirs = pl.ds(pl.multiple_of((1 - core) * half, 16), half)
    left = stacked_out[rows : 2 * rows, :]
    theirs_out[...] = dot(left, w_all[theirs, : 3 * inner], NT).astype(jnp.bfloat16)
    mine_out[...] = dot(left, w_all[mine, : 3 * inner], NT)


def attention_call(scalars, gain, bias, text, text_t, mod, cot, weights, slots, rows, w_parts):
    count = (len(mod) + 1) // 2
    shard = weights[0].shape[0]
    width = mod[0].shape[1]
    tokens = rows * count
    inner = slots * HD
    f32, bf16 = jnp.float32, jnp.bfloat16
    vmem, anywhere = spec(pltpu.VMEM), spec(pl.ANY)
    pieces = len(mod) + len(cot) + len(weights)
    return pl.pallas_call(
        functools.partial(attention_kernel, slots, count, rows, shard, width, w_parts),
        out_shape=(
            jax.ShapeDtypeStruct((rows, width // 2), f32),
            jax.ShapeDtypeStruct((rows, width // 2), bf16),
            jax.ShapeDtypeStruct((tokens, 3 * inner), bf16),
        ),
        in_specs=[spec(pltpu.SMEM), vmem, vmem, vmem, vmem] + [anywhere] * pieces,
        out_specs=(vmem, vmem, vmem),
        scratch_shapes=[
            pltpu.VMEM((width, 4 * inner), bf16),
            pltpu.VMEM((tokens, width), bf16),
            pltpu.VMEM((tokens, width), bf16),
            pltpu.SemaphoreType.DMA((pieces,)),
        ]
        + [pltpu.VMEM((slots, tokens, HD), bf16)] * 4
        + [pltpu.VMEM((slots, HD, tokens), bf16)]
        + [pltpu.VMEM((slots, tokens, HD), f32)] * 5
        + [pltpu.VMEM((tokens, 3 * inner), f32)],
        compiler_params=pltpu.CompilerParams(vmem_limit_bytes=44 * 1024 * 1024),
        cost_estimate=pl.CostEstimate(
            flops=2 * tokens * width * 4 * inner + 10 * tokens * tokens * inner,
            bytes_accessed=2 * (2 * tokens * width + 4 * width * inner) + 3 * tokens * width,
            transcendentals=slots * tokens * tokens,
        ),
    )(scalars, gain, bias, text, text_t, *mod, *cot, *weights)


def backward_kernel(order, rows, shard, width, inner, part_width, scalars, stacked, *refs):
    dp_count = width // shard
    refs = list(refs)
    w_parts = -(-3 * inner // part_width)
    w_in = refs[: w_parts * dp_count]
    outs = refs[w_parts * dp_count : -2]
    w_all, sems = refs[-2:]
    core = scalars[0]
    copies = []
    for k in range(dp_count):
        offset = pl.multiple_of(scalars[1 + k] * shard, 16)
        for part in range(w_parts):
            columns = pl.ds(part * part_width, part_width)
            copy = pltpu.make_async_copy(
                w_in[part * dp_count + k],
                w_all.at[pl.ds(offset, shard), columns],
                sems.at[len(copies)],
            )
            copy.start()
            copies.append(copy)
    for copy in copies:
        copy.wait()
    half = width // 2
    mine = pl.ds(pl.multiple_of(core * half, 16), half)
    theirs = pl.ds(pl.multiple_of((1 - core) * half, 16), half)
    left = jnp.concatenate([stacked[j * rows : (j + 1) * rows, :] for j in order], axis=0)
    theirs_all = dot(left, w_all[theirs, : 3 * inner], NT)
    mine_all = dot(left, w_all[mine, : 3 * inner], NT)
    for n in range(len(order)):
        outs[2 * n][...] = mine_all[n * rows : (n + 1) * rows]
        outs[2 * n + 1][...] = theirs_all[n * rows : (n + 1) * rows].astype(jnp.bfloat16)


def backward_call(scalars, stacked, weights, order, rows, width, part_width):
    inner = stacked.shape[1] // 3
    shard = weights[0].shape[0]
    f32, bf16 = jnp.float32, jnp.bfloat16
    vmem, anywhere = spec(pltpu.VMEM), spec(pl.ANY)
    return pl.pallas_call(
        functools.partial(backward_kernel, order, rows, shard, width, inner, part_width),
        out_shape=tuple(
            jax.ShapeDtypeStruct((rows, width // 2), dtype) for _ in order for dtype in (f32, bf16)
        ),
        in_specs=[spec(pltpu.SMEM), vmem] + [anywhere] * len(weights),
        out_specs=(vmem,) * (2 * len(order)),
        scratch_shapes=[
            pltpu.VMEM((width, part_width * (-(-3 * inner // part_width))), bf16),
            pltpu.SemaphoreType.DMA((len(weights),)),
        ],
        compiler_params=pltpu.CompilerParams(vmem_limit_bytes=40 * 1024 * 1024),
        cost_estimate=pl.CostEstimate(
            flops=2 * len(order) * rows * width * 3 * inner,
            bytes_accessed=2 * width * 3 * inner + 3 * len(order) * rows * width,
            transcendentals=0,
        ),
    )(scalars, stacked, *weights)


def sums_kernel(mine, theirs, near, far, stretch, normed, grad_out, sums_out):
    half = near.shape[0]
    total = mine[...] + theirs[...].astype(jnp.float32)
    for part, moving in enumerate((near, far)):
        here = slice(part * half, (part + 1) * half)
        grad = (total[here] + moving[...].astype(jnp.float32)) * stretch[...]
        grad_out[here, :] = grad
        first = jnp.sum(grad, axis=-1, keepdims=True)
        second = jnp.sum(grad * normed[here, :], axis=-1, keepdims=True)
        lane = lax.broadcasted_iota(jnp.int32, (half, 128), 1)
        sums_out[here, :] = jnp.where(lane == 0, first, second)


def last_kernel(width, grad, sums, other, normed, base, inv_std, out):
    total = (sums[...] + other[...]) * (1.0 / width)
    out[...] = base[...] + inv_std[...] * (
        grad[...] - total[:, 0:1] - normed[...] * total[:, 1:2]
    )


def shards_by_head(states, adjoint, text_kv, text_len, step_index, modulation, w_qkv, qk_gain, w_out):
    hidden_state = states[0]
    adjoint_rows = adjoint[0]
    tok_count, model_width = hidden_state.shape
    seq_count = lax.axis_size("seq")
    dp_count = lax.axis_size("dp")
    head_count = lax.axis_size("head")
    inner_dev = w_qkv.shape[2]
    heads_dev = inner_dev // HD
    shard = w_qkv.shape[0]
    slots = -(-heads_dev // seq_count)
    inner = slots * HD
    half_rows = tok_count // 2
    core = lax.axis_index("head").astype(jnp.int32)
    seq_index = lax.axis_index("seq")

    seq_order = line_ring(seq_count)
    seq_place = ring_place(seq_order, seq_index)
    seq_next = ring_pairs(seq_order)
    dp_order = line_ring(dp_count)
    dp_place = ring_place(dp_order, lax.axis_index("dp"))
    dp_next = [
        (a * head_count + c, b * head_count + c) if c % 2 == 0 else (b * head_count + c, a * head_count + c)
        for a, b in ring_pairs(dp_order)
        for c in range(head_count)
    ]
    swap = [(0, 1), (1, 0)]

    first = seq_index * heads_dev // seq_count
    stop = (seq_index + 1) * heads_dev // seq_count
    window = jnp.minimum(first, heads_dev - slots)
    valid = [((window + i >= first) & (window + i < stop)).astype(jnp.int32) for i in range(slots)]

    table_row = lax.dynamic_index_in_dim(modulation, step_index[0], 0, keepdims=False)
    offset_row = table_row[0]
    stretch = table_row[1]
    gating = table_row[2]

    mod_half = modulate_half(core, hidden_state, offset_row[None], stretch[None])

    def gather(moving):
        pieces = []
        for k in range(1, seq_count):
            moving = lax.ppermute(moving, "seq", seq_next)
            pieces += [moving, lax.ppermute(moving, "head", swap)]
        return pieces

    mod_pieces = gather(mod_half)

    w_qkv, w_out, mod_half = lax.optimization_barrier((w_qkv, w_out, mod_half))
    take = lambda c: lax.dynamic_slice(w_qkv, (0, c, window * HD), (shard, 1, inner))[:, 0]
    own_parts = [
        jnp.concatenate([take(0), take(1)], axis=1),
        jnp.concatenate([take(2), lax.dynamic_slice_in_dim(w_out, window * HD, inner, 0).T], axis=1),
    ]
    weights = []
    for part in own_parts:
        chain = [part]
        for k in range(1, dp_count):
            chain.append(lax.ppermute(chain[-1], ("dp", "head"), dp_next))
        weights += chain
    direction = jnp.where(core == 0, -1, 1)
    w_index = [
        ring_member(dp_order, (dp_place + direction * k + dp_count) % dp_count) for k in range(dp_count)
    ]

    adjoint_rows, hidden_state, *_ = lax.optimization_barrier((adjoint_rows, hidden_state, *own_parts))
    squares = jnp.sum(adjoint_rows * adjoint_rows)
    text_dev = text_kv.shape[1]
    text_local = text_kv[0].transpose(1, 0, 2).reshape(2 * text_dev, inner_dev).astype(jnp.float32)
    packet = jnp.concatenate([text_local, jnp.full((8, inner_dev), squares)], axis=0)
    packets = [packet]
    for k in range(1, seq_count):
        pairs = [(seq_order[i], seq_order[(i + k) % seq_count]) for i in range(seq_count)]
        packets.append(lax.ppermute(packet, "seq", pairs))
    total = sum(one[2 * text_dev, 0] for one in packets)
    clip_limit = 0.5 * (tok_count * seq_count * model_width) ** 0.5
    clip_scale = jnp.minimum(1.0, clip_limit / jnp.sqrt(total + 1e-06))

    cotangent = (gating * (clip_scale * adjoint_rows)).astype(jnp.bfloat16)
    cot_pieces = [cotangent] + gather(
        lax.dynamic_slice_in_dim(cotangent, core * half_rows, half_rows, 0)
    )

    widened = hidden_state.astype(jnp.float32)
    centered = widened - jnp.mean(widened, axis=-1, keepdims=True)
    inv_std = lax.rsqrt(jnp.mean(centered * centered, axis=-1, keepdims=True) + 1e-06)
    normed = centered * inv_std
    modulated = (normed * (1.0 + stretch) + offset_row).astype(jnp.bfloat16)
    mod_pieces = [modulated] + mod_pieces

    text_rows = jnp.concatenate([one[: 2 * text_dev] for one in packets], axis=0).astype(jnp.bfloat16)
    text_rows = lax.dynamic_slice_in_dim(text_rows, window * HD, inner, 1)
    text_rows = text_rows.reshape(seq_count, 2, text_dev, slots, HD).transpose(1, 3, 0, 2, 4)
    text_rows = text_rows.reshape(2, slots, seq_count * text_dev, HD)
    text_t = text_rows[0].transpose(0, 2, 1)
    owners = jnp.stack(
        [ring_member(seq_order, (seq_place - k + seq_count) % seq_count) for k in range(seq_count)]
    )
    text_ids = (owners[:, None] * text_dev + jnp.arange(text_dev, dtype=jnp.int32)[None, :]).reshape(-1)
    bias = jnp.where(text_ids < text_len[0], 0.0, -1e30).astype(jnp.float32)
    bias = jnp.broadcast_to(bias[:, None], (seq_count * text_dev, 2 * tok_count))

    scalars = jnp.stack([core] + w_index + valid).astype(jnp.int32)
    mine, theirs, stacked = attention_call(
        scalars, qk_gain, bias, text_rows, text_t, mod_pieces, cot_pieces, weights, slots, tok_count, 2
    )
    order = list(range(2, seq_count)) + [0]
    rest = backward_call(scalars, stacked, weights, order, tok_count, model_width, 2 * inner)

    def chip_sum(mine, theirs):
        return mine + lax.ppermute(theirs, "head", swap).astype(jnp.float32)

    def split(rows):
        return rows[:half_rows], rows[half_rows:]

    moving = [part.astype(jnp.bfloat16) for part in split(chip_sum(mine, theirs))]
    for j in range(2, seq_count):
        moving = [lax.ppermute(part, "seq", seq_next) for part in moving]
        own = split(chip_sum(rest[2 * (j - 2)], rest[2 * (j - 2) + 1]))
        moving = [
            (a + b.astype(jnp.float32)).astype(jnp.bfloat16) for a, b in zip(own, moving)
        ]
    moving = [lax.ppermute(part, "seq", seq_next) for part in moving]

    half_width = model_width // head_count
    first_col = core * half_width
    normed_share = lax.dynamic_slice_in_dim(normed, first_col, half_width, 1)
    stretch_share = lax.dynamic_slice_in_dim(stretch, first_col, half_width, 0)[None]
    base = clip_scale * lax.dynamic_slice_in_dim(adjoint_rows, first_col, half_width, 1)
    vmem = spec(pltpu.VMEM)
    share = jax.ShapeDtypeStruct((tok_count, half_width), jnp.float32)
    grad_scaled, sums = pl.pallas_call(
        sums_kernel,
        out_shape=(share, jax.ShapeDtypeStruct((tok_count, 128), jnp.float32)),
        in_specs=[vmem] * 6,
        out_specs=(vmem, vmem),
    )(rest[-2], lax.ppermute(rest[-1], "head", swap), *moving, 1.0 + stretch_share, normed_share)
    other = lax.ppermute(sums, "head", swap)
    pulled = pl.pallas_call(
        functools.partial(last_kernel, model_width),
        out_shape=share,
        in_specs=[vmem] * 6,
        out_specs=vmem,
    )(grad_scaled, sums, other, normed_share, base, inv_std)
    return pulled[None]


def qk_normalize(values, gains):
    inverse = lax.rsqrt(jnp.mean(values * values, axis=-1, keepdims=True) + 1e-06)
    return ((values * inverse * gains).astype(jnp.bfloat16), inverse)


def qk_backward(values, inverse, cotangent, gains):
    scaled = cotangent.astype(jnp.float32) * gains
    return (
        scaled * inverse - values * jnp.mean(scaled * values, axis=-1, keepdims=True) * inverse**3
    )


def shards_by_row(states, adjoint, text_kv, text_len, step_index, modulation, w_qkv, qk_gain, w_out):
    hidden_state = states[0]
    adjoint_rows = adjoint[0]
    tok_count, model_width = hidden_state.shape
    seq_count = lax.axis_size("seq")
    inner_dev = w_qkv.shape[2]
    heads_dev = inner_dev // HD
    score_scale = HD ** (-0.5)
    squares = lax.psum(jnp.sum(adjoint_rows * adjoint_rows), "seq")
    clip_limit = 0.5 * (tok_count * seq_count * model_width) ** 0.5
    clip_scale = jnp.minimum(1.0, clip_limit / jnp.sqrt(squares + 1e-06))
    table_row = lax.dynamic_index_in_dim(modulation, step_index[0], 0, keepdims=False)
    offset_row = table_row[0]
    stretch = table_row[1]
    gating = table_row[2]
    widened = hidden_state.astype(jnp.float32)
    centered = widened - jnp.mean(widened, axis=-1, keepdims=True)
    inv_std = lax.rsqrt(jnp.mean(centered * centered, axis=-1, keepdims=True) + 1e-06)
    normed = centered * inv_std
    modulated = (normed * (1.0 + stretch) + offset_row).astype(jnp.bfloat16)
    cotangent = (gating * (clip_scale * adjoint_rows)).astype(jnp.bfloat16)
    contract_last = (((1,), (1,)), ((), ()))
    full_weight = lax.all_gather(w_qkv, "dp", axis=0, tiled=True).reshape(
        model_width, 3 * inner_dev
    )
    projected = jnp.dot(modulated, full_weight, preferred_element_type=jnp.float32)
    out_raw = lax.dot_general(
        cotangent,
        lax.all_gather(w_out, "dp", axis=1, tiled=True),
        contract_last,
        preferred_element_type=jnp.float32,
    )
    projected = projected.reshape(tok_count, 3, heads_dev, HD)
    queries, query_inv = qk_normalize(projected[:, 0], qk_gain[0])
    own_keys, key_inv = qk_normalize(projected[:, 1], qk_gain[1])
    own_values = projected[:, 2].astype(jnp.bfloat16)
    out_grad = out_raw.astype(jnp.bfloat16).reshape(tok_count, heads_dev, HD)
    text_keys = text_kv[0, :, 0, :]
    text_values = text_kv[0, :, 1, :]
    text_dev = text_keys.shape[0]
    rows_dev = tok_count + text_dev
    key_local = jnp.concatenate([own_keys.reshape(tok_count, inner_dev), text_keys], axis=0)
    value_local = jnp.concatenate([own_values.reshape(tok_count, inner_dev), text_values], axis=0)
    key_all, value_all = (
        lax.all_gather(key_local, "seq", axis=0, tiled=True),
        lax.all_gather(value_local, "seq", axis=0, tiled=True),
    )
    all_rows = rows_dev * seq_count
    row_ids = jnp.arange(all_rows, dtype=jnp.int32)
    owner = row_ids // rows_dev
    within = row_ids % rows_dev
    allowed = (within < tok_count) | (owner * text_dev + within - tok_count < text_len[0])
    group = 1
    while group * 2 * rows_dev <= 512 and seq_count % (group * 2) == 0:
        group = group * 2
    block_rows = group * rows_dev
    block_count = all_rows // block_rows
    key_blocks = key_all.reshape(block_count, block_rows, heads_dev, HD)
    value_blocks = value_all.reshape(block_count, block_rows, heads_dev, HD)
    mask_blocks = allowed.reshape(block_count, block_rows)

    def block_scores(key_block, mask_block):
        scores = (
            jnp.einsum("qhd,khd->qhk", queries, key_block, preferred_element_type=jnp.float32)
            * score_scale
        )
        return jnp.where(mask_block[None, None, :], scores, -1e30)

    def first_pass(carry, block):
        row_max, row_sum, row_dot = carry
        key_block, value_block, mask_block = block
        scores = block_scores(key_block, mask_block)
        new_max = jnp.maximum(row_max, jnp.max(scores, axis=-1))
        rescale = jnp.exp(row_max - new_max)
        exps = jnp.exp(scores - new_max[:, :, None])
        grad_weights = jnp.einsum(
            "qhd,khd->qhk", out_grad, value_block, preferred_element_type=jnp.float32
        )
        return (
            (
                new_max,
                row_sum * rescale + jnp.sum(exps, axis=-1),
                row_dot * rescale + jnp.sum(exps * grad_weights, axis=-1),
            ),
            None,
        )

    start_state = (
        jnp.full((tok_count, heads_dev), -1e30, jnp.float32),
        jnp.zeros((tok_count, heads_dev), jnp.float32),
        jnp.zeros((tok_count, heads_dev), jnp.float32),
    )
    (row_max, row_sum, row_dot), unused = lax.scan(
        first_pass, start_state, (key_blocks, value_blocks, mask_blocks)
    )
    log_total = row_max + jnp.log(row_sum)
    delta_row = row_dot / row_sum

    def second_pass(running, block):
        key_block, value_block, mask_block = block
        weights = jnp.exp(block_scores(key_block, mask_block) - log_total[:, :, None])
        grad_weights = jnp.einsum(
            "qhd,khd->qhk", out_grad, value_block, preferred_element_type=jnp.float32
        )
        grad_scores = (weights * (grad_weights - delta_row[:, :, None])).astype(jnp.bfloat16)
        return (
            running
            + jnp.einsum(
                "qhk,khd->qhd", grad_scores, key_block, preferred_element_type=jnp.float32
            ),
            None,
        )

    query_sum, unused = lax.scan(
        second_pass,
        jnp.zeros((tok_count, heads_dev, HD), jnp.float32),
        (key_blocks, value_blocks, mask_blocks),
    )
    grad_query = (query_sum * score_scale).astype(jnp.bfloat16)
    log_all, delta_all = (
        lax.all_gather(log_total, "seq", axis=0, tiled=True),
        lax.all_gather(delta_row, "seq", axis=0, tiled=True),
    )
    local_ids = jnp.arange(rows_dev, dtype=jnp.int32)
    local_allowed = (local_ids < tok_count) | (
        lax.axis_index("seq") * text_dev + local_ids - tok_count < text_len[0]
    )
    key_three = key_local.reshape(rows_dev, heads_dev, HD)
    value_three = value_local.reshape(rows_dev, heads_dev, HD)
    query_piece = lax.all_gather(queries.reshape(tok_count, inner_dev), "seq", axis=0, tiled=True)
    grad_piece = lax.all_gather(out_grad.reshape(tok_count, inner_dev), "seq", axis=0, tiled=True)
    piece_rows = query_piece.shape[0]
    query_rows = query_piece.reshape(piece_rows, heads_dev, HD)
    grad_rows = grad_piece.reshape(piece_rows, heads_dev, HD)
    scores = (
        jnp.einsum("qhd,khd->qhk", query_rows, key_three, preferred_element_type=jnp.float32)
        * score_scale
    )
    scores = jnp.where(local_allowed[None, None, :], scores, -1e30)
    weights = jnp.exp(scores - log_all[:, :, None])
    grad_weights = jnp.einsum(
        "qhd,khd->qhk", grad_rows, value_three, preferred_element_type=jnp.float32
    )
    grad_scores = (weights * (grad_weights - delta_all[:, :, None])).astype(jnp.bfloat16)
    rounded = weights.astype(jnp.bfloat16)
    key_sum = jnp.einsum(
        "qhk,qhd->khd", grad_scores, query_rows, preferred_element_type=jnp.float32
    )
    value_sum = jnp.einsum("qhk,qhd->khd", rounded, grad_rows, preferred_element_type=jnp.float32)
    key_sum, value_sum = (key_sum, value_sum)
    grad_key = (key_sum[:tok_count] * score_scale).astype(jnp.bfloat16)
    grad_value = value_sum[:tok_count].astype(jnp.bfloat16)
    raw_query = qk_backward(projected[:, 0], query_inv, grad_query, qk_gain[0])
    raw_key = qk_backward(projected[:, 1], key_inv, grad_key, qk_gain[1])
    stacked = jnp.stack([raw_query, raw_key, grad_value.astype(jnp.float32)], axis=1).astype(
        jnp.bfloat16
    )
    stacked = stacked.reshape(tok_count, 3 * inner_dev)
    partial_grad = lax.dot_general(
        stacked, full_weight, contract_last, preferred_element_type=jnp.float32
    )
    half_width = model_width // lax.axis_size("head")
    first_col = lax.axis_index("head") * half_width
    grad_share = lax.psum_scatter(
        partial_grad.astype(jnp.bfloat16), "head", scatter_dimension=1, tiled=True
    ).astype(jnp.float32)
    normed_share = lax.dynamic_slice_in_dim(normed, first_col, half_width, 1)
    stretch_share = lax.dynamic_slice_in_dim(stretch, first_col, half_width, 0)
    adjoint_share = lax.dynamic_slice_in_dim(adjoint_rows, first_col, half_width, 1)
    grad_scaled = grad_share * (1.0 + stretch_share)
    row_sums = jnp.stack(
        [jnp.sum(grad_scaled, axis=-1), jnp.sum(grad_scaled * normed_share, axis=-1)], axis=-1
    )
    row_sums = lax.psum(row_sums, "head")
    grad_state = inv_std * (
        grad_scaled - row_sums[:, 0:1] / model_width - normed_share * row_sums[:, 1:2] / model_width
    )
    pulled = clip_scale * adjoint_share + grad_state
    return pulled[None]


def solution(mesh):
    in_specs = (
        P("dp", "seq", None),
        P("dp", "seq", None),
        P("dp", "seq", None, "head"),
        P("dp"),
        P("dp"),
        P(),
        P("dp", None, "head"),
        P(),
        P("head", "dp"),
    )
    out_specs = P("dp", "seq", "head")
    by_head = mesh.shape["seq"] <= 8 and mesh.shape["head"] == 2
    shards = shards_by_head if by_head else shards_by_row
    return jax.shard_map(shards, mesh=mesh, in_specs=in_specs, out_specs=out_specs, check_vma=False)
```

```python
import functools

import jax
import jax.numpy as jnp
from jax import lax
from jax.experimental import pallas as pl
from jax.experimental.pallas import tpu as pltpu
from jax.sharding import PartitionSpec as P

HD = 64
NT = (((1,), (1,)), ((), ()))
NN = (((1,), (0,)), ((), ()))


def line_ring(count):
    return [0] + list(range(1, count, 2)) + [i for i in range(count - 1, 0, -1) if i % 2 == 0]


def ring_pairs(order):
    return [(order[i], order[(i + 1) % len(order)]) for i in range(len(order))]


def ring_place(order, index):
    place = jnp.int32(0)
    for position, member in enumerate(order):
        place = jnp.where(index == member, jnp.int32(position), place)
    return place


def ring_member(order, place):
    member = jnp.int32(order[0])
    for position, value in enumerate(order):
        member = jnp.where(place == position, jnp.int32(value), member)
    return member


def dot(a, b, dims):
    return lax.dot_general(a, b, dims, preferred_element_type=jnp.float32)


def inverse_rms(raw):
    return lax.rsqrt(jnp.mean(raw * raw, axis=-1, keepdims=True) + 1e-06)


def norm_backward(raw, cotangent, gains):
    inverse = inverse_rms(raw)
    scaled = cotangent.astype(jnp.float32) * gains
    return (
        scaled * inverse
        - raw * jnp.mean(scaled * raw, axis=-1, keepdims=True) * (inverse * inverse * inverse)
    )


def spec(space):
    return pl.BlockSpec(memory_space=space)


def first_kernel(step, core, states, table, out, rows_out):
    rows = [table[c, pl.ds(step[0], 1), :] for c in range(3)]
    widened = states[...].astype(jnp.float32)
    centered = widened - jnp.mean(widened, axis=-1, keepdims=True)
    inv_std = lax.rsqrt(jnp.mean(centered * centered, axis=-1, keepdims=True) + 1e-06)
    out[...] = (centered * inv_std * (1.0 + rows[1]) + rows[0]).astype(jnp.bfloat16)
    for c in range(3):
        rows_out[c : c + 1, :] = rows[c]


def first_call(step, core, states, table):
    rows, width = states.shape
    half = rows // 2
    whole = lambda *shape: pl.BlockSpec(shape, lambda i, step, core: (0,) * len(shape))
    return pl.pallas_call(
        first_kernel,
        out_shape=(
            jax.ShapeDtypeStruct((half, width), jnp.bfloat16),
            jax.ShapeDtypeStruct((8, width), jnp.float32),
        ),
        grid_spec=pltpu.PrefetchScalarGridSpec(
            num_scalar_prefetch=2,
            grid=(1,),
            in_specs=[
                pl.BlockSpec((half, width), lambda i, step, core: (core[0], 0)),
                whole(*table.shape),
            ],
            out_specs=(whole(half, width), whole(8, width)),
        ),
        cost_estimate=pl.CostEstimate(flops=8 * half * width, bytes_accessed=8 * half * width, transcendentals=0),
    )(step, core, states, table)


def pick_half(core, rows):
    half = rows.shape[1] // 2
    return jnp.where(core == 0, rows[:, :half], rows[:, half:])


def modulate_kernel(core, states, table_rows, out, normed_out, stretch_out, inv_out):
    widened = states[...].astype(jnp.float32)
    centered = widened - jnp.mean(widened, axis=-1, keepdims=True)
    inv_std = lax.rsqrt(jnp.mean(centered * centered, axis=-1, keepdims=True) + 1e-06)
    normed = centered * inv_std
    scale = 1.0 + table_rows[1:2, :]
    out[...] = (normed * scale + table_rows[0:1, :]).astype(jnp.bfloat16)
    normed_out[...] = pick_half(core[0], normed)
    stretch_out[...] = pick_half(core[0], scale)
    inv_out[...] = jnp.broadcast_to(inv_std, inv_out.shape)


def cotangent_kernel(limit, text_rows, core, adjoint, table_rows, *refs):
    packets, (out, half_out, base_out) = refs[:-3], refs[-3:]
    squares = packets[0][text_rows : text_rows + 1, 0:1]
    for packet in packets[1:]:
        squares = squares + packet[text_rows : text_rows + 1, 0:1]
    clip_scale = jnp.minimum(1.0, limit / jnp.sqrt(squares + 1e-06))
    gating = table_rows[2:3, :]
    clipped = clip_scale * adjoint[...]
    out[...] = (gating * clipped).astype(jnp.bfloat16)
    base_out[...] = pick_half(core[0], clipped)
    half = half_out.shape[0]
    own = adjoint[pl.ds(pl.multiple_of(core[0] * half, 8), half), :]
    half_out[...] = (gating * (clip_scale * own)).astype(jnp.bfloat16)


class Copies:
    def __init__(self, sems):
        self.sems = sems
        self.count = 0

    def start(self, source, target):
        copy = pltpu.make_async_copy(source, target, self.sems.at[self.count])
        copy.start()
        self.count += 1
        return copy

    def weights(self, scalars, w_in, w_all, shard):
        half = shard // 2
        starts = [
            (scalars[1] * shard, shard),
            (scalars[2] * shard, shard),
            (scalars[3] * shard, shard),
            (scalars[4] * shard, half),
            (scalars[4] * shard + half, half),
        ]
        return [
            self.start(piece, w_all.at[pl.ds(pl.multiple_of(first, 16), size)])
            for piece, (first, size) in zip(w_in, starts)
        ]

    def rows(self, core, pieces, target, rows):
        half = rows // 2
        copies = [[self.start(pieces[0], target.at[pl.ds(0, rows)])]]
        for j in range(1, (len(pieces) + 1) // 2):
            near = pl.multiple_of(j * rows + core * half, 16)
            far = pl.multiple_of(j * rows + (1 - core) * half, 16)
            copies.append(
                [
                    self.start(pieces[2 * j - 1], target.at[pl.ds(near, half)]),
                    self.start(pieces[2 * j], target.at[pl.ds(far, half)]),
                ]
            )
        return copies


def project_kernel(slots, count, rows, shard, width, text_dev, scalars, gain, *refs):
    refs = list(refs)
    take = lambda n: [refs.pop(0) for _ in range(n)]
    packets = take(count)
    mod_in = take(2 * count - 1)
    w_in = take(5)
    q_all, k_all, v_all, k_t, raw_q, raw_k, text, text_t = take(8)
    w_all, mod_all, sems = take(3)
    inner = slots * HD
    core = scalars[0]
    copies = Copies(sems)
    w_copies = copies.weights(scalars, w_in, w_all, shard)
    row_copies = copies.rows(core, mod_in, mod_all, rows)

    lanes = packets[0].shape[1]
    shift = lax.rem(lanes - scalars[5] * HD, lanes)
    for part in range(2):
        found = [
            pltpu.roll(one[part * text_dev : (part + 1) * text_dev, :], shift, 1) for one in packets
        ]
        found = jnp.concatenate(found, axis=0)
        for i in range(slots):
            one = found[:, i * HD : (i + 1) * HD]
            text[part, i] = one.astype(jnp.bfloat16)
            if part == 0:
                text_t[i] = one.T.astype(jnp.bfloat16)

    gain_q = gain[0:1, :]
    gain_k = gain[1:2, :]
    score_scale = HD ** (-0.5)
    for copy in w_copies:
        copy.wait()
    span = 2 * rows
    for b in range(count // 2):
        for copy in row_copies[2 * b] + row_copies[2 * b + 1]:
            copy.wait()
        here = slice(b * span, (b + 1) * span)
        projected = jnp.dot(
            mod_all[here, :], w_all[:, : 3 * inner], preferred_element_type=jnp.float32
        )
        for i in range(slots):
            query = projected[:, i * HD : (i + 1) * HD]
            key = projected[:, inner + i * HD : inner + (i + 1) * HD]
            value = projected[:, 2 * inner + i * HD : 2 * inner + (i + 1) * HD]
            raw_q[i, here, :] = query
            raw_k[i, here, :] = key
            query = query * inverse_rms(query) * gain_q
            q_all[i, here, :] = (query * score_scale).astype(jnp.bfloat16)
            key = key * inverse_rms(key) * gain_k
            k_all[i, here, :] = key.astype(jnp.bfloat16)
            k_t[i, :, here] = key.T.astype(jnp.bfloat16)
            v_all[i, here, :] = value.astype(jnp.bfloat16)


def attend_kernel(slots, count, rows, shard, width, text_dev, scalars, gain, *refs):
    refs = list(refs)
    take = lambda n: [refs.pop(0) for _ in range(n)]
    q_all, k_all, v_all, k_t, raw_q, raw_k, text, text_t = take(8)
    cot_in = take(2 * count - 1)
    w_in = take(5)
    mine_near, mine_far, theirs_near, theirs_far, stacked_out = take(5)
    w_all, cot_all, sems = take(3)
    d_all, grad_k, grad_v, back_q, stacked = take(5)
    inner = slots * HD
    core = scalars[0]
    copies = Copies(sems)
    w_copies = copies.weights(scalars, w_in, w_all, shard)
    row_copies = copies.rows(core, cot_in, cot_all, rows)
    gain_q = gain[0:1, :]
    gain_k = gain[1:2, :]
    score_scale = HD ** (-0.5)
    span = 2 * rows

    text_rows = count * text_dev
    row = lax.broadcasted_iota(jnp.int32, (text_rows, span), 0)
    text_id = row
    for k in range(count):
        inside = (row >= k * text_dev) & (row < (k + 1) * text_dev)
        text_id = jnp.where(inside, row + (scalars[7 + k] - k) * text_dev, text_id)
    bias = jnp.where(text_id < scalars[6], 0.0, -1e30)

    for copy in w_copies:
        copy.wait()
    for b in range(count // 2):
        for copy in row_copies[2 * b] + row_copies[2 * b + 1]:
            copy.wait()
        here = slice(b * span, (b + 1) * span)
        out_grad = jnp.dot(
            cot_all[here, :], w_all[:, 3 * inner :], preferred_element_type=jnp.float32
        )
        for i in range(slots):
            d_all[i, here, :] = out_grad[:, i * HD : (i + 1) * HD].astype(jnp.bfloat16)

    grad_k[...] = jnp.zeros_like(grad_k)
    grad_v[...] = jnp.zeros_like(grad_v)

    @pl.loop(0, slots * (count // 2))
    def attend(t):
        i = t // (count // 2)
        here = pl.ds(pl.multiple_of(t % (count // 2) * span, span), span)
        query = q_all[i, here, :]
        grad = d_all[i, here, :]
        scores = dot(k_all[i], query, NT)
        text_scores = dot(text[0, i], query, NT) + bias
        col_max = jnp.maximum(
            jnp.max(scores, axis=0, keepdims=True), jnp.max(text_scores, axis=0, keepdims=True)
        )
        exps = jnp.exp(scores - col_max)
        text_exps = jnp.exp(text_scores - col_max)
        total = jnp.sum(exps, axis=0, keepdims=True) + jnp.sum(text_exps, axis=0, keepdims=True)
        inverse = 1.0 / total
        grad_w = dot(v_all[i], grad, NT)
        text_grad_w = dot(text[1, i], grad, NT)
        delta = inverse * (
            jnp.sum(exps * grad_w, axis=0, keepdims=True)
            + jnp.sum(text_exps * text_grad_w, axis=0, keepdims=True)
        )
        weights = exps * inverse
        grad_s = (weights * (grad_w - delta)).astype(jnp.bfloat16)
        text_grad_s = (text_exps * inverse * (text_grad_w - delta)).astype(jnp.bfloat16)
        grad_k[i] += dot(grad_s, query, NN)
        grad_v[i] += dot(weights.astype(jnp.bfloat16), grad, NN)
        grad_q = dot(k_t[i], grad_s, NN) + dot(text_t[i], text_grad_s, NN)
        grad_q = (grad_q.T * score_scale).astype(jnp.bfloat16)
        back_q[i, here, :] = norm_backward(raw_q[i, here, :], grad_q, gain_q)

    for i in range(slots):
        valid = scalars[7 + count + i] > 0
        back_k = norm_backward(raw_k[i], grad_k[i].astype(jnp.bfloat16), gain_k)
        stacked[:, i * HD : (i + 1) * HD] = jnp.where(valid, back_q[i], 0.0)
        stacked[:, inner + i * HD : inner + (i + 1) * HD] = jnp.where(valid, back_k, 0.0)
        stacked[:, 2 * inner + i * HD : 2 * inner + (i + 1) * HD] = jnp.where(valid, grad_v[i], 0.0)
    stacked_out[...] = stacked[...].astype(jnp.bfloat16)
    half = width // 2
    mine = pl.ds(pl.multiple_of(core * half, 16), half)
    theirs = pl.ds(pl.multiple_of((1 - core) * half, 16), half)
    left = stacked_out[rows : 2 * rows, :]
    theirs_all = dot(left, w_all[theirs, : 3 * inner], NT).astype(jnp.bfloat16)
    theirs_near[...] = theirs_all[: rows // 2]
    theirs_far[...] = theirs_all[rows // 2 :]
    mine_all = dot(left, w_all[mine, : 3 * inner], NT)
    mine_near[...] = mine_all[: rows // 2]
    mine_far[...] = mine_all[rows // 2 :]


def project_call(scalars, gain, packets, mod, weights, slots, rows, text_dev):
    count = len(packets)
    shard, columns = weights[0].shape
    width = mod[0].shape[1]
    tokens = rows * count
    text_rows = text_dev * count
    f32, bf16 = jnp.float32, jnp.bfloat16
    vmem, hbm = spec(pltpu.VMEM), spec(pltpu.HBM)
    by_token = (slots, tokens, HD)
    shapes = [(by_token, bf16)] * 3 + [((slots, HD, tokens), bf16)] + [(by_token, f32)] * 2
    shapes += [((2, slots, text_rows, HD), bf16), ((slots, HD, text_rows), bf16)]
    return pl.pallas_call(
        functools.partial(project_kernel, slots, count, rows, shard, width, text_dev),
        out_shape=tuple(jax.ShapeDtypeStruct(*one) for one in shapes),
        in_specs=[spec(pltpu.SMEM), vmem] + [vmem] * count + [hbm] * (len(mod) + len(weights)),
        out_specs=(vmem,) * len(shapes),
        scratch_shapes=[
            pltpu.VMEM((width, columns), bf16),
            pltpu.VMEM((tokens, width), bf16),
            pltpu.SemaphoreType.DMA((len(mod) + len(weights),)),
        ],
        compiler_params=pltpu.CompilerParams(vmem_limit_bytes=40 * 1024 * 1024),
        cost_estimate=pl.CostEstimate(
            flops=2 * tokens * width * 3 * slots * HD,
            bytes_accessed=2 * (tokens * width + columns * width) + 4 * tokens * columns,
            transcendentals=0,
        ),
    )(scalars, gain, *packets, *mod, *weights)


def attend_call(scalars, gain, operands, cot, weights, slots, rows, text_dev):
    count = (len(cot) + 1) // 2
    shard, columns = weights[0].shape
    width = cot[0].shape[1]
    tokens = rows * count
    inner = slots * HD
    f32, bf16 = jnp.float32, jnp.bfloat16
    vmem, hbm = spec(pltpu.VMEM), spec(pltpu.HBM)
    part = (rows // 2, width // 2)
    shapes = [(part, f32)] * 2 + [(part, bf16)] * 2 + [((tokens, 3 * inner), bf16)]
    return pl.pallas_call(
        functools.partial(attend_kernel, slots, count, rows, shard, width, text_dev),
        out_shape=tuple(jax.ShapeDtypeStruct(*one) for one in shapes),
        in_specs=[spec(pltpu.SMEM), vmem] + [vmem] * len(operands) + [hbm] * (len(cot) + len(weights)),
        out_specs=(vmem,) * len(shapes),
        scratch_shapes=[
            pltpu.VMEM((width, columns), bf16),
            pltpu.VMEM((tokens, width), bf16),
            pltpu.SemaphoreType.DMA((len(cot) + len(weights),)),
            pltpu.VMEM((slots, tokens, HD), bf16),
        ]
        + [pltpu.VMEM((slots, tokens, HD), f32)] * 3
        + [pltpu.VMEM((tokens, 3 * inner), f32)],
        compiler_params=pltpu.CompilerParams(vmem_limit_bytes=40 * 1024 * 1024),
        cost_estimate=pl.CostEstimate(
            flops=2 * tokens * width * inner + 10 * tokens * tokens * inner + 2 * rows * width * 3 * inner,
            bytes_accessed=2 * (tokens * width + columns * width),
            transcendentals=slots * tokens * tokens,
        ),
    )(scalars, gain, *operands, *cot, *weights)


def backward_kernel(order, rows, shard, width, inner, scalars, stacked, *refs):
    w_in, outs, (w_all, sems) = refs[:5], refs[5:-2], refs[-2:]
    core = scalars[0]
    for copy in Copies(sems).weights(scalars, w_in, w_all, shard):
        copy.wait()
    half = width // 2
    mine = pl.ds(pl.multiple_of(core * half, 16), half)
    theirs = pl.ds(pl.multiple_of((1 - core) * half, 16), half)
    left = jnp.concatenate([stacked[j * rows : (j + 1) * rows, :] for j in order], axis=0)
    theirs_all = dot(left, w_all[theirs, : 3 * inner], NT).astype(jnp.bfloat16)
    mine_all = dot(left, w_all[mine, : 3 * inner], NT)
    part = rows // 2
    for n in range(len(order)):
        for m in range(2):
            here = slice(n * rows + m * part, n * rows + (m + 1) * part)
            outs[4 * n + m][...] = mine_all[here]
            outs[4 * n + 2 + m][...] = theirs_all[here]


def backward_call(scalars, stacked, weights, order, rows, width):
    inner = stacked.shape[1] // 3
    shard, columns = weights[0].shape
    f32, bf16 = jnp.float32, jnp.bfloat16
    vmem, hbm = spec(pltpu.VMEM), spec(pltpu.HBM)
    part = (rows // 2, width // 2)
    shapes = ([(part, f32)] * 2 + [(part, bf16)] * 2) * len(order)
    return pl.pallas_call(
        functools.partial(backward_kernel, order, rows, shard, width, inner),
        out_shape=tuple(jax.ShapeDtypeStruct(*one) for one in shapes),
        in_specs=[spec(pltpu.SMEM), vmem] + [hbm] * len(weights),
        out_specs=(vmem,) * len(shapes),
        scratch_shapes=[
            pltpu.VMEM((width, columns), bf16),
            pltpu.SemaphoreType.DMA((len(weights),)),
        ],
        compiler_params=pltpu.CompilerParams(vmem_limit_bytes=40 * 1024 * 1024),
        cost_estimate=pl.CostEstimate(
            flops=2 * len(order) * rows * width * 3 * inner,
            bytes_accessed=2 * width * columns + 3 * len(order) * rows * width,
            transcendentals=0,
        ),
    )(scalars, stacked, *weights)


def sums_kernel(mine_near, mine_far, theirs_near, theirs_far, near, far, scale, normed, grad_out, sums_out):
    half = near.shape[0]
    parts = ((mine_near, theirs_near, near), (mine_far, theirs_far, far))
    for part, (mine, theirs, moving) in enumerate(parts):
        here = slice(part * half, (part + 1) * half)
        grad = mine[...] + theirs[...].astype(jnp.float32) + moving[...].astype(jnp.float32)
        grad = grad * scale[...]
        grad_out[here, :] = grad
        first = jnp.sum(grad, axis=-1, keepdims=True)
        second = jnp.sum(grad * normed[here, :], axis=-1, keepdims=True)
        lane = lax.broadcasted_iota(jnp.int32, (half, 128), 1)
        sums_out[here, :] = jnp.where(lane == 0, first, second)


def last_kernel(width, grad, sums, other, normed, base, inv_std, out):
    total = (sums[...] + other[...]) * (1.0 / width)
    rows = base[...] + inv_std[:, 0:1] * (
        grad[...] - total[:, 0:1] - normed[...] * total[:, 1:2]
    )
    out[...] = rows.T


def local_call(kernel, shapes, scalar_count, *operands):
    vmem = spec(pltpu.VMEM)
    return pl.pallas_call(
        kernel,
        out_shape=tuple(jax.ShapeDtypeStruct(*one) for one in shapes),
        in_specs=[spec(pltpu.SMEM)] * scalar_count + [vmem] * (len(operands) - scalar_count),
        out_specs=(vmem,) * len(shapes),
        compiler_params=pltpu.CompilerParams(vmem_limit_bytes=24 * 1024 * 1024),
        cost_estimate=pl.CostEstimate(
            flops=sum(one.size for one in operands),
            bytes_accessed=sum(one.size * one.dtype.itemsize for one in operands),
            transcendentals=0,
        ),
    )(*operands)


def shards_by_head(states, adjoint, text_kv, text_len, step_index, modulation, w_qkv, qk_gain, w_out):
    hidden_state = states[0]
    adjoint_rows = adjoint[0]
    tok_count, model_width = hidden_state.shape
    seq_count = lax.axis_size("seq")
    inner_dev = w_qkv.shape[2]
    heads_dev = inner_dev // HD
    shard = w_qkv.shape[0]
    slots = -(-heads_dev // seq_count)
    inner = slots * HD
    half_rows = tok_count // 2
    half_width = model_width // 2
    f32, bf16 = jnp.float32, jnp.bfloat16
    core = lax.axis_index("head").astype(jnp.int32)
    seq_index = lax.axis_index("seq")
    dp_index = lax.axis_index("dp")
    pin = lax.optimization_barrier

    seq_order = line_ring(seq_count)
    seq_place = ring_place(seq_order, seq_index)
    seq_next = ring_pairs(seq_order)
    swap = [(0, 1), (1, 0)]
    along_x = [(p, p ^ 1) for p in range(4)]
    along_y = [(p, p ^ 2) for p in range(4)]

    first = seq_index * heads_dev // seq_count
    stop = (seq_index + 1) * heads_dev // seq_count
    window = jnp.minimum(first, heads_dev - slots)
    valid = [(window + i >= first) & (window + i < stop) for i in range(slots)]
    owners = [ring_member(seq_order, (seq_place - k + seq_count) % seq_count) for k in range(seq_count)]
    w_index = [dp_index, dp_index ^ 1, dp_index ^ 2, dp_index ^ 3]
    scalars = [core] + w_index + [window, text_len[0]] + owners + valid
    scalars = jnp.stack([one.astype(jnp.int32) for one in scalars])

    def step(moving):
        return lax.ppermute(moving, "seq", seq_next)

    def other_core(moving):
        return lax.ppermute(moving, "head", swap)

    mod_half, table_rows = first_call(step_index, core[None], hidden_state, modulation.transpose(1, 0, 2))
    mod_one = step(mod_half)

    w_qkv, w_out, mod_half = pin((w_qkv, w_out, mod_half))
    take = lambda c: lax.dynamic_slice(w_qkv, (0, c, window * HD), (shard, 1, inner))[:, 0]
    own_w = jnp.concatenate(
        [take(0), take(1), take(2), lax.dynamic_slice_in_dim(w_out, window * HD, inner, 0).T], axis=1
    )
    w_x = lax.ppermute(own_w, "dp", along_x)
    w_y = lax.ppermute(own_w, "dp", along_y)

    adjoint_rows, text_local, mod_one, own_w = pin((adjoint_rows, text_kv[0], mod_one, own_w))
    squares = jnp.sum(adjoint_rows * adjoint_rows)
    text_dev = text_local.shape[0]
    text_local = text_local.transpose(1, 0, 2).reshape(2 * text_dev, inner_dev).astype(f32)
    packet = jnp.concatenate([text_local, jnp.full((8, inner_dev), squares)], axis=0)
    packets = [packet]
    for k in range(1, seq_count):
        pairs = [(seq_order[i], seq_order[(i + k) % seq_count]) for i in range(seq_count)]
        packets.append(lax.ppermute(packet, "seq", pairs))
    clip_limit = 0.5 * (tok_count * seq_count * model_width) ** 0.5
    cotangent, cot_half, base = local_call(
        functools.partial(cotangent_kernel, clip_limit, 2 * text_dev),
        [((tok_count, model_width), bf16), ((half_rows, model_width), bf16), ((tok_count, half_width), f32)],
        1,
        core[None],
        adjoint_rows,
        table_rows,
        *packets,
    )

    mod_steps = [mod_one]
    for k in range(2, seq_count):
        mod_steps.append(step(mod_steps[-1]))
    cot_half, mod_steps[1] = pin((cot_half, mod_steps[1]))
    cot_steps = [step(cot_half)]
    modulated, normed_share, scale_share, inv_std = local_call(
        modulate_kernel,
        [
            ((tok_count, model_width), bf16),
            ((tok_count, half_width), f32),
            ((1, half_width), f32),
            ((tok_count, 128), f32),
        ],
        1,
        core[None],
        hidden_state,
        table_rows,
    )
    moving, w_x, w_y, modulated = pin((cot_steps[0], w_x, w_y, modulated))
    w_d = [
        lax.ppermute(w_x[: shard // 2], "dp", along_y),
        lax.ppermute(w_y[shard // 2 :], "dp", along_x),
    ]
    cot_steps[0] = moving
    for k in range(2, seq_count):
        cot_steps.append(step(cot_steps[-1]))

    def pieces(own, steps):
        return [own] + [one for moved in steps for one in (moved, other_core(moved))]

    weights = [own_w, w_x, w_y] + w_d
    operands = project_call(
        scalars, qk_gain, packets, pieces(modulated, mod_steps), weights, slots, tok_count, text_dev
    )
    *mine, stacked = attend_call(
        scalars, qk_gain, operands, pieces(cotangent, cot_steps), weights, slots, tok_count, text_dev
    )

    def chip_sums(mine):
        return [a + other_core(b).astype(f32) for a, b in zip(mine[:2], mine[2:])]

    moving = [part.astype(bf16) for part in chip_sums(mine)]
    stacked, *moving = pin((stacked, *moving))
    order = list(range(2, seq_count)) + [0]
    rest = backward_call(scalars, stacked, weights, order, tok_count, model_width)
    for j in range(2, seq_count):
        moving = [step(part) for part in moving]
        own = chip_sums(rest[4 * (j - 2) : 4 * (j - 1)])
        moving = [(a + b.astype(f32)).astype(bf16) for a, b in zip(own, moving)]
    moving = [step(part) for part in moving]

    own = rest[-4:]
    grad_scaled, sums = local_call(
        sums_kernel,
        [((tok_count, half_width), f32), ((tok_count, 128), f32)],
        0,
        *own[:2],
        *[other_core(one) for one in own[2:]],
        *moving,
        scale_share,
        normed_share,
    )
    (pulled,) = local_call(
        functools.partial(last_kernel, model_width),
        [((half_width, tok_count), f32)],
        0,
        grad_scaled,
        sums,
        other_core(sums),
        normed_share,
        base,
        inv_std,
    )
    return pulled.T[None]


def qk_normalize(values, gains):
    inverse = lax.rsqrt(jnp.mean(values * values, axis=-1, keepdims=True) + 1e-06)
    return ((values * inverse * gains).astype(jnp.bfloat16), inverse)


def qk_backward(values, inverse, cotangent, gains):
    scaled = cotangent.astype(jnp.float32) * gains
    return (
        scaled * inverse - values * jnp.mean(scaled * values, axis=-1, keepdims=True) * inverse**3
    )


def shards_by_row(states, adjoint, text_kv, text_len, step_index, modulation, w_qkv, qk_gain, w_out):
    hidden_state = states[0]
    adjoint_rows = adjoint[0]
    tok_count, model_width = hidden_state.shape
    seq_count = lax.axis_size("seq")
    inner_dev = w_qkv.shape[2]
    heads_dev = inner_dev // HD
    score_scale = HD ** (-0.5)
    squares = lax.psum(jnp.sum(adjoint_rows * adjoint_rows), "seq")
    clip_limit = 0.5 * (tok_count * seq_count * model_width) ** 0.5
    clip_scale = jnp.minimum(1.0, clip_limit / jnp.sqrt(squares + 1e-06))
    table_row = lax.dynamic_index_in_dim(modulation, step_index[0], 0, keepdims=False)
    offset_row = table_row[0]
    stretch = table_row[1]
    gating = table_row[2]
    widened = hidden_state.astype(jnp.float32)
    centered = widened - jnp.mean(widened, axis=-1, keepdims=True)
    inv_std = lax.rsqrt(jnp.mean(centered * centered, axis=-1, keepdims=True) + 1e-06)
    normed = centered * inv_std
    modulated = (normed * (1.0 + stretch) + offset_row).astype(jnp.bfloat16)
    cotangent = (gating * (clip_scale * adjoint_rows)).astype(jnp.bfloat16)
    contract_last = (((1,), (1,)), ((), ()))
    full_weight = lax.all_gather(w_qkv, "dp", axis=0, tiled=True).reshape(
        model_width, 3 * inner_dev
    )
    projected = jnp.dot(modulated, full_weight, preferred_element_type=jnp.float32)
    out_raw = lax.dot_general(
        cotangent,
        lax.all_gather(w_out, "dp", axis=1, tiled=True),
        contract_last,
        preferred_element_type=jnp.float32,
    )
    projected = projected.reshape(tok_count, 3, heads_dev, HD)
    queries, query_inv = qk_normalize(projected[:, 0], qk_gain[0])
    own_keys, key_inv = qk_normalize(projected[:, 1], qk_gain[1])
    own_values = projected[:, 2].astype(jnp.bfloat16)
    out_grad = out_raw.astype(jnp.bfloat16).reshape(tok_count, heads_dev, HD)
    text_keys = text_kv[0, :, 0, :]
    text_values = text_kv[0, :, 1, :]
    text_dev = text_keys.shape[0]
    rows_dev = tok_count + text_dev
    key_local = jnp.concatenate([own_keys.reshape(tok_count, inner_dev), text_keys], axis=0)
    value_local = jnp.concatenate([own_values.reshape(tok_count, inner_dev), text_values], axis=0)
    key_all, value_all = (
        lax.all_gather(key_local, "seq", axis=0, tiled=True),
        lax.all_gather(value_local, "seq", axis=0, tiled=True),
    )
    all_rows = rows_dev * seq_count
    row_ids = jnp.arange(all_rows, dtype=jnp.int32)
    owner = row_ids // rows_dev
    within = row_ids % rows_dev
    allowed = (within < tok_count) | (owner * text_dev + within - tok_count < text_len[0])
    group = 1
    while group * 2 * rows_dev <= 512 and seq_count % (group * 2) == 0:
        group = group * 2
    block_rows = group * rows_dev
    block_count = all_rows // block_rows
    key_blocks = key_all.reshape(block_count, block_rows, heads_dev, HD)
    value_blocks = value_all.reshape(block_count, block_rows, heads_dev, HD)
    mask_blocks = allowed.reshape(block_count, block_rows)

    def block_scores(key_block, mask_block):
        scores = (
            jnp.einsum("qhd,khd->qhk", queries, key_block, preferred_element_type=jnp.float32)
            * score_scale
        )
        return jnp.where(mask_block[None, None, :], scores, -1e30)

    def first_pass(carry, block):
        row_max, row_sum, row_dot = carry
        key_block, value_block, mask_block = block
        scores = block_scores(key_block, mask_block)
        new_max = jnp.maximum(row_max, jnp.max(scores, axis=-1))
        rescale = jnp.exp(row_max - new_max)
        exps = jnp.exp(scores - new_max[:, :, None])
        grad_weights = jnp.einsum(
            "qhd,khd->qhk", out_grad, value_block, preferred_element_type=jnp.float32
        )
        return (
            (
                new_max,
                row_sum * rescale + jnp.sum(exps, axis=-1),
                row_dot * rescale + jnp.sum(exps * grad_weights, axis=-1),
            ),
            None,
        )

    start_state = (
        jnp.full((tok_count, heads_dev), -1e30, jnp.float32),
        jnp.zeros((tok_count, heads_dev), jnp.float32),
        jnp.zeros((tok_count, heads_dev), jnp.float32),
    )
    (row_max, row_sum, row_dot), unused = lax.scan(
        first_pass, start_state, (key_blocks, value_blocks, mask_blocks)
    )
    log_total = row_max + jnp.log(row_sum)
    delta_row = row_dot / row_sum

    def second_pass(running, block):
        key_block, value_block, mask_block = block
        weights = jnp.exp(block_scores(key_block, mask_block) - log_total[:, :, None])
        grad_weights = jnp.einsum(
            "qhd,khd->qhk", out_grad, value_block, preferred_element_type=jnp.float32
        )
        grad_scores = (weights * (grad_weights - delta_row[:, :, None])).astype(jnp.bfloat16)
        return (
            running
            + jnp.einsum(
                "qhk,khd->qhd", grad_scores, key_block, preferred_element_type=jnp.float32
            ),
            None,
        )

    query_sum, unused = lax.scan(
        second_pass,
        jnp.zeros((tok_count, heads_dev, HD), jnp.float32),
        (key_blocks, value_blocks, mask_blocks),
    )
    grad_query = (query_sum * score_scale).astype(jnp.bfloat16)
    log_all, delta_all = (
        lax.all_gather(log_total, "seq", axis=0, tiled=True),
        lax.all_gather(delta_row, "seq", axis=0, tiled=True),
    )
    local_ids = jnp.arange(rows_dev, dtype=jnp.int32)
    local_allowed = (local_ids < tok_count) | (
        lax.axis_index("seq") * text_dev + local_ids - tok_count < text_len[0]
    )
    key_three = key_local.reshape(rows_dev, heads_dev, HD)
    value_three = value_local.reshape(rows_dev, heads_dev, HD)
    query_piece = lax.all_gather(queries.reshape(tok_count, inner_dev), "seq", axis=0, tiled=True)
    grad_piece = lax.all_gather(out_grad.reshape(tok_count, inner_dev), "seq", axis=0, tiled=True)
    piece_rows = query_piece.shape[0]
    query_rows = query_piece.reshape(piece_rows, heads_dev, HD)
    grad_rows = grad_piece.reshape(piece_rows, heads_dev, HD)
    scores = (
        jnp.einsum("qhd,khd->qhk", query_rows, key_three, preferred_element_type=jnp.float32)
        * score_scale
    )
    scores = jnp.where(local_allowed[None, None, :], scores, -1e30)
    weights = jnp.exp(scores - log_all[:, :, None])
    grad_weights = jnp.einsum(
        "qhd,khd->qhk", grad_rows, value_three, preferred_element_type=jnp.float32
    )
    grad_scores = (weights * (grad_weights - delta_all[:, :, None])).astype(jnp.bfloat16)
    rounded = weights.astype(jnp.bfloat16)
    key_sum = jnp.einsum(
        "qhk,qhd->khd", grad_scores, query_rows, preferred_element_type=jnp.float32
    )
    value_sum = jnp.einsum("qhk,qhd->khd", rounded, grad_rows, preferred_element_type=jnp.float32)
    key_sum, value_sum = (key_sum, value_sum)
    grad_key = (key_sum[:tok_count] * score_scale).astype(jnp.bfloat16)
    grad_value = value_sum[:tok_count].astype(jnp.bfloat16)
    raw_query = qk_backward(projected[:, 0], query_inv, grad_query, qk_gain[0])
    raw_key = qk_backward(projected[:, 1], key_inv, grad_key, qk_gain[1])
    stacked = jnp.stack([raw_query, raw_key, grad_value.astype(jnp.float32)], axis=1).astype(
        jnp.bfloat16
    )
    stacked = stacked.reshape(tok_count, 3 * inner_dev)
    partial_grad = lax.dot_general(
        stacked, full_weight, contract_last, preferred_element_type=jnp.float32
    )
    half_width = model_width // lax.axis_size("head")
    first_col = lax.axis_index("head") * half_width
    grad_share = lax.psum_scatter(
        partial_grad.astype(jnp.bfloat16), "head", scatter_dimension=1, tiled=True
    ).astype(jnp.float32)
    normed_share = lax.dynamic_slice_in_dim(normed, first_col, half_width, 1)
    stretch_share = lax.dynamic_slice_in_dim(stretch, first_col, half_width, 0)
    adjoint_share = lax.dynamic_slice_in_dim(adjoint_rows, first_col, half_width, 1)
    grad_scaled = grad_share * (1.0 + stretch_share)
    row_sums = jnp.stack(
        [jnp.sum(grad_scaled, axis=-1), jnp.sum(grad_scaled * normed_share, axis=-1)], axis=-1
    )
    row_sums = lax.psum(row_sums, "head")
    grad_state = inv_std * (
        grad_scaled - row_sums[:, 0:1] / model_width - normed_share * row_sums[:, 1:2] / model_width
    )
    pulled = clip_scale * adjoint_share + grad_state
    return pulled[None]


def solution(mesh):
    in_specs = (
        P("dp", "seq", None),
        P("dp", "seq", None),
        P("dp", "seq", None, "head"),
        P("dp"),
        P("dp"),
        P(),
        P("dp", None, "head"),
        P(),
        P("head", "dp"),
    )
    out_specs = P("dp", "seq", "head")
    by_head = mesh.shape["seq"] == 4 and mesh.shape["dp"] == 4 and mesh.shape["head"] == 2
    shards = shards_by_head if by_head else shards_by_row
    return jax.shard_map(shards, mesh=mesh, in_specs=in_specs, out_specs=out_specs, check_vma=False)
```

```python
import functools

import jax
import jax.numpy as jnp
from jax import lax
from jax.experimental import pallas as pl
from jax.experimental.pallas import tpu as pltpu
from jax.sharding import PartitionSpec as P

HD = 64
NT = (((1,), (1,)), ((), ()))
NN = (((1,), (0,)), ((), ()))


def line_ring(count):
    return [0] + list(range(1, count, 2)) + [i for i in range(count - 1, 0, -1) if i % 2 == 0]


def ring_pairs(order):
    return [(order[i], order[(i + 1) % len(order)]) for i in range(len(order))]


def ring_place(order, index):
    place = jnp.int32(0)
    for position, member in enumerate(order):
        place = jnp.where(index == member, jnp.int32(position), place)
    return place


def ring_member(order, place):
    member = jnp.int32(order[0])
    for position, value in enumerate(order):
        member = jnp.where(place == position, jnp.int32(value), member)
    return member


def dot(a, b, dims):
    return lax.dot_general(a, b, dims, preferred_element_type=jnp.float32)


def inverse_rms(raw):
    return lax.rsqrt(jnp.mean(raw * raw, axis=-1, keepdims=True) + 1e-06)


def norm_backward(raw, cotangent, gains):
    inverse = inverse_rms(raw)
    scaled = cotangent.astype(jnp.float32) * gains
    return (
        scaled * inverse
        - raw * jnp.mean(scaled * raw, axis=-1, keepdims=True) * (inverse * inverse * inverse)
    )


def spec(space):
    return pl.BlockSpec(memory_space=space)


def first_kernel(step, core, states, table, out, rows_out):
    rows = [table[c, pl.ds(step[0], 1), :] for c in range(3)]
    widened = states[...].astype(jnp.float32)
    centered = widened - jnp.mean(widened, axis=-1, keepdims=True)
    inv_std = lax.rsqrt(jnp.mean(centered * centered, axis=-1, keepdims=True) + 1e-06)
    out[...] = (centered * inv_std * (1.0 + rows[1]) + rows[0]).astype(jnp.bfloat16)
    for c in range(3):
        rows_out[c : c + 1, :] = rows[c]


def first_call(step, core, states, table):
    rows, width = states.shape
    half = rows // 2
    whole = lambda *shape: pl.BlockSpec(shape, lambda i, step, core: (0,) * len(shape))
    return pl.pallas_call(
        first_kernel,
        out_shape=(
            jax.ShapeDtypeStruct((half, width), jnp.bfloat16),
            jax.ShapeDtypeStruct((8, width), jnp.float32),
        ),
        grid_spec=pltpu.PrefetchScalarGridSpec(
            num_scalar_prefetch=2,
            grid=(1,),
            in_specs=[
                pl.BlockSpec((half, width), lambda i, step, core: (core[0], 0)),
                whole(*table.shape),
            ],
            out_specs=(whole(half, width), whole(8, width)),
        ),
        cost_estimate=pl.CostEstimate(flops=8 * half * width, bytes_accessed=8 * half * width, transcendentals=0),
    )(step, core, states, table)


def pick_half(core, rows):
    half = rows.shape[1] // 2
    return jnp.where(core == 0, rows[:, :half], rows[:, half:])


def modulate_kernel(core, states, table_rows, out, normed_out, stretch_out, inv_out):
    widened = states[...].astype(jnp.float32)
    centered = widened - jnp.mean(widened, axis=-1, keepdims=True)
    inv_std = lax.rsqrt(jnp.mean(centered * centered, axis=-1, keepdims=True) + 1e-06)
    normed = centered * inv_std
    scale = 1.0 + table_rows[1:2, :]
    out[...] = (normed * scale + table_rows[0:1, :]).astype(jnp.bfloat16)
    normed_out[...] = pick_half(core[0], normed)
    stretch_out[...] = pick_half(core[0], scale)
    inv_out[...] = jnp.broadcast_to(inv_std, inv_out.shape)


def cotangent_kernel(limit, text_rows, core, adjoint, table_rows, *refs):
    packets, (out, half_out, base_out) = refs[:-3], refs[-3:]
    squares = packets[0][text_rows : text_rows + 1, 0:1]
    for packet in packets[1:]:
        squares = squares + packet[text_rows : text_rows + 1, 0:1]
    clip_scale = jnp.minimum(1.0, limit / jnp.sqrt(squares + 1e-06))
    gating = table_rows[2:3, :]
    clipped = clip_scale * adjoint[...]
    out[...] = (gating * clipped).astype(jnp.bfloat16)
    base_out[...] = pick_half(core[0], clipped)
    half = half_out.shape[0]
    own = adjoint[pl.ds(pl.multiple_of(core[0] * half, 8), half), :]
    half_out[...] = (gating * (clip_scale * own)).astype(jnp.bfloat16)


class Copies:
    def __init__(self, sems):
        self.sems = sems
        self.count = 0

    def start(self, source, target):
        copy = pltpu.make_async_copy(source, target, self.sems.at[self.count])
        copy.start()
        self.count += 1
        return copy

    def weights(self, scalars, w_in, w_all, shard):
        parts = len(w_in) // 4
        columns = w_all.shape[1] // parts
        return [
            self.start(
                w_in[part * 4 + k],
                w_all.at[
                    pl.ds(pl.multiple_of(scalars[1 + k] * shard, 16), shard),
                    pl.ds(part * columns, columns),
                ],
            )
            for part in range(parts)
            for k in range(4)
        ]

    def rows(self, core, pieces, target, rows):
        half = rows // 2
        copies = [[self.start(pieces[0], target.at[pl.ds(0, rows)])]]
        for j in range(1, (len(pieces) + 1) // 2):
            near = pl.multiple_of(j * rows + core * half, 16)
            far = pl.multiple_of(j * rows + (1 - core) * half, 16)
            copies.append(
                [
                    self.start(pieces[2 * j - 1], target.at[pl.ds(near, half)]),
                    self.start(pieces[2 * j], target.at[pl.ds(far, half)]),
                ]
            )
        return copies


def project_kernel(slots, count, rows, shard, width, text_dev, scalars, gain, *refs):
    refs = list(refs)
    take = lambda n: [refs.pop(0) for _ in range(n)]
    packets = take(count)
    mod_in = take(2 * count - 1)
    w_in = take(8)
    q_all, k_all, v_all, k_t, raw_q, raw_k, text, text_t, w_keep, w_give = take(10)
    w_all, mod_all, sems = take(3)
    inner = slots * HD
    core = scalars[0]
    copies = Copies(sems)
    w_copies = copies.weights(scalars, w_in, w_all, shard)
    row_copies = copies.rows(core, mod_in, mod_all, rows)

    lanes = packets[0].shape[1]
    shift = lax.rem(lanes - scalars[5] * HD, lanes)
    for part in range(2):
        found = [
            pltpu.roll(one[part * text_dev : (part + 1) * text_dev, :], shift, 1) for one in packets
        ]
        found = jnp.concatenate(found, axis=0)
        for i in range(slots):
            one = found[:, i * HD : (i + 1) * HD]
            text[part, i] = one.astype(jnp.bfloat16)
            if part == 0:
                text_t[i] = one.T.astype(jnp.bfloat16)

    gain_q = gain[0:1, :]
    gain_k = gain[1:2, :]
    score_scale = HD ** (-0.5)
    for copy in w_copies:
        copy.wait()
    half = width // 2
    w_keep[...] = w_all[pl.ds(pl.multiple_of(core * half, 16), half), : 3 * inner]
    w_give[...] = w_all[pl.ds(pl.multiple_of((1 - core) * half, 16), half), : 3 * inner]
    span = 2 * rows
    for b in range(count // 2):
        for copy in row_copies[2 * b] + row_copies[2 * b + 1]:
            copy.wait()
        here = slice(b * span, (b + 1) * span)
        projected = jnp.dot(
            mod_all[here, :], w_all[:, : 3 * inner], preferred_element_type=jnp.float32
        )
        for i in range(slots):
            query = projected[:, i * HD : (i + 1) * HD]
            key = projected[:, inner + i * HD : inner + (i + 1) * HD]
            value = projected[:, 2 * inner + i * HD : 2 * inner + (i + 1) * HD]
            raw_q[i, here, :] = query
            raw_k[i, here, :] = key
            query = query * inverse_rms(query) * gain_q
            q_all[i, here, :] = (query * score_scale).astype(jnp.bfloat16)
            key = key * inverse_rms(key) * gain_k
            k_all[i, here, :] = key.astype(jnp.bfloat16)
            k_t[i, :, here] = key.T.astype(jnp.bfloat16)
            v_all[i, here, :] = value.astype(jnp.bfloat16)


def attend_kernel(slots, count, rows, shard, width, text_dev, scalars, gain, *refs):
    refs = list(refs)
    take = lambda n: [refs.pop(0) for _ in range(n)]
    q_all, k_all, v_all, k_t, raw_q, raw_k, text, text_t = take(8)
    cot_in = take(2 * count - 1)
    w_in = take(4)
    first_out, rest_out = take(2)
    w_all, cot_all, sems = take(3)
    d_all, grad_k, grad_v, back_q, stacked = take(5)
    inner = slots * HD
    core = scalars[0]
    copies = Copies(sems)
    w_copies = copies.weights(scalars, w_in, w_all, shard)
    row_copies = copies.rows(core, cot_in, cot_all, rows)
    gain_q = gain[0:1, :]
    gain_k = gain[1:2, :]
    score_scale = HD ** (-0.5)
    span = 2 * rows

    text_rows = count * text_dev
    row = lax.broadcasted_iota(jnp.int32, (text_rows, span), 0)
    text_id = row
    for k in range(count):
        inside = (row >= k * text_dev) & (row < (k + 1) * text_dev)
        text_id = jnp.where(inside, row + (scalars[7 + k] - k) * text_dev, text_id)
    bias = jnp.where(text_id < scalars[6], 0.0, -1e30)

    for copy in w_copies:
        copy.wait()
    for b in range(count // 2):
        for copy in row_copies[2 * b] + row_copies[2 * b + 1]:
            copy.wait()
        here = slice(b * span, (b + 1) * span)
        out_grad = jnp.dot(
            cot_all[here, :], w_all[:, inner:], preferred_element_type=jnp.float32
        )
        for i in range(slots):
            d_all[i, here, :] = out_grad[:, i * HD : (i + 1) * HD].astype(jnp.bfloat16)

    grad_k[...] = jnp.zeros_like(grad_k)
    grad_v[...] = jnp.zeros_like(grad_v)

    @pl.loop(0, slots * (count // 2))
    def attend(t):
        i = t // (count // 2)
        here = pl.ds(pl.multiple_of(t % (count // 2) * span, span), span)
        query = q_all[i, here, :]
        grad = d_all[i, here, :]
        scores = dot(k_all[i], query, NT)
        text_scores = dot(text[0, i], query, NT) + bias
        col_max = jnp.maximum(
            jnp.max(scores, axis=0, keepdims=True), jnp.max(text_scores, axis=0, keepdims=True)
        )
        exps = jnp.exp(scores - col_max)
        text_exps = jnp.exp(text_scores - col_max)
        total = jnp.sum(exps, axis=0, keepdims=True) + jnp.sum(text_exps, axis=0, keepdims=True)
        inverse = 1.0 / total
        grad_w = dot(v_all[i], grad, NT)
        text_grad_w = dot(text[1, i], grad, NT)
        delta = inverse * (
            jnp.sum(exps * grad_w, axis=0, keepdims=True)
            + jnp.sum(text_exps * text_grad_w, axis=0, keepdims=True)
        )
        weights = exps * inverse
        grad_s = (weights * (grad_w - delta)).astype(jnp.bfloat16)
        text_grad_s = (text_exps * inverse * (text_grad_w - delta)).astype(jnp.bfloat16)
        grad_k[i] += dot(grad_s, query, NN)
        grad_v[i] += dot(weights.astype(jnp.bfloat16), grad, NN)
        grad_q = dot(k_t[i], grad_s, NN) + dot(text_t[i], text_grad_s, NN)
        grad_q = (grad_q.T * score_scale).astype(jnp.bfloat16)
        back_q[i, here, :] = norm_backward(raw_q[i, here, :], grad_q, gain_q)

    for i in range(slots):
        valid = scalars[7 + count + i] > 0
        back_k = norm_backward(raw_k[i], grad_k[i].astype(jnp.bfloat16), gain_k)
        stacked[:, i * HD : (i + 1) * HD] = jnp.where(valid, back_q[i], 0.0)
        stacked[:, inner + i * HD : inner + (i + 1) * HD] = jnp.where(valid, back_k, 0.0)
        stacked[:, 2 * inner + i * HD : 2 * inner + (i + 1) * HD] = jnp.where(valid, grad_v[i], 0.0)
    first_out[...] = stacked[rows : 2 * rows, :].astype(jnp.bfloat16)
    rest_out[: (count - 2) * rows, :] = stacked[2 * rows :, :].astype(jnp.bfloat16)
    rest_out[(count - 2) * rows :, :] = stacked[:rows, :].astype(jnp.bfloat16)


def project_call(scalars, gain, packets, mod, weights, slots, rows, text_dev):
    count = len(packets)
    shard = weights[0].shape[0]
    columns = 4 * slots * HD
    width = mod[0].shape[1]
    tokens = rows * count
    text_rows = text_dev * count
    f32, bf16 = jnp.float32, jnp.bfloat16
    vmem, hbm = spec(pltpu.VMEM), spec(pl.ANY)
    by_token = (slots, tokens, HD)
    shapes = [(by_token, bf16)] * 3 + [((slots, HD, tokens), bf16)] + [(by_token, f32)] * 2
    shapes += [((2, slots, text_rows, HD), bf16), ((slots, HD, text_rows), bf16)]
    shapes += [((width // 2, 3 * slots * HD), bf16)] * 2
    return pl.pallas_call(
        functools.partial(project_kernel, slots, count, rows, shard, width, text_dev),
        out_shape=tuple(jax.ShapeDtypeStruct(*one) for one in shapes),
        in_specs=[spec(pltpu.SMEM), vmem] + [vmem] * count + [hbm] * (len(mod) + len(weights)),
        out_specs=(vmem,) * len(shapes),
        scratch_shapes=[
            pltpu.VMEM((width, columns), bf16),
            pltpu.VMEM((tokens, width), bf16),
            pltpu.SemaphoreType.DMA((len(mod) + len(weights),)),
        ],
        compiler_params=pltpu.CompilerParams(vmem_limit_bytes=28 * 1024 * 1024),
        cost_estimate=pl.CostEstimate(
            flops=2 * tokens * width * 3 * slots * HD,
            bytes_accessed=2 * (tokens * width + columns * width) + 4 * tokens * columns,
            transcendentals=0,
        ),
    )(scalars, gain, *packets, *mod, *weights)


def attend_call(scalars, gain, operands, cot, weights, slots, rows, text_dev):
    count = (len(cot) + 1) // 2
    shard, columns = weights[0].shape
    width = cot[0].shape[1]
    tokens = rows * count
    inner = slots * HD
    f32, bf16 = jnp.float32, jnp.bfloat16
    vmem, hbm = spec(pltpu.VMEM), spec(pl.ANY)
    shapes = [((rows, 3 * inner), bf16), ((tokens - rows, 3 * inner), bf16)]
    return pl.pallas_call(
        functools.partial(attend_kernel, slots, count, rows, shard, width, text_dev),
        out_shape=tuple(jax.ShapeDtypeStruct(*one) for one in shapes),
        in_specs=[spec(pltpu.SMEM), vmem] + [vmem] * len(operands) + [hbm] * (len(cot) + len(weights)),
        out_specs=(vmem,) * len(shapes),
        scratch_shapes=[
            pltpu.VMEM((width, columns), bf16),
            pltpu.VMEM((tokens, width), bf16),
            pltpu.SemaphoreType.DMA((len(cot) + len(weights),)),
            pltpu.VMEM((slots, tokens, HD), bf16),
        ]
        + [pltpu.VMEM((slots, tokens, HD), f32)] * 3
        + [pltpu.VMEM((tokens, 3 * inner), f32)],
        compiler_params=pltpu.CompilerParams(vmem_limit_bytes=28 * 1024 * 1024),
        cost_estimate=pl.CostEstimate(
            flops=2 * tokens * width * inner + 10 * tokens * tokens * inner,
            bytes_accessed=2 * (tokens * width + columns * width),
            transcendentals=slots * tokens * tokens,
        ),
    )(scalars, gain, *operands, *cot, *weights)


def backward_kernel(own, other, w_own, w_other, *outs):
    total = dot(own[...], w_own[...], NT) + dot(other[...], w_other[...], NT)
    part = outs[0].shape[0]
    for n, out in enumerate(outs):
        out[...] = total[n * part : (n + 1) * part].astype(out.dtype)


def backward_call(own, other, w_own, w_other, part, dtype):
    rows, inner = own.shape
    half = w_own.shape[0]
    vmem = spec(pltpu.VMEM)
    return pl.pallas_call(
        backward_kernel,
        out_shape=(jax.ShapeDtypeStruct((part, half), dtype),) * (rows // part),
        in_specs=[vmem] * 4,
        out_specs=(vmem,) * (rows // part),
        compiler_params=pltpu.CompilerParams(vmem_limit_bytes=28 * 1024 * 1024),
        cost_estimate=pl.CostEstimate(
            flops=4 * rows * half * inner,
            bytes_accessed=4 * (rows + half) * inner + 4 * rows * half,
            transcendentals=0,
        ),
    )(own, other, w_own, w_other)


def sums_kernel(own_near, own_far, near, far, scale, normed, grad_out, sums_out):
    half = near.shape[0]
    for part, (own, moving) in enumerate(((own_near, near), (own_far, far))):
        here = slice(part * half, (part + 1) * half)
        grad = (own[...] + moving[...].astype(jnp.float32)) * scale[...]
        grad_out[here, :] = grad
        first = jnp.sum(grad, axis=-1, keepdims=True)
        second = jnp.sum(grad * normed[here, :], axis=-1, keepdims=True)
        lane = lax.broadcasted_iota(jnp.int32, (half, 128), 1)
        sums_out[here, :] = jnp.where(lane == 0, first, second)


def last_kernel(width, grad, sums, other, normed, base, inv_std, out):
    total = (sums[...] + other[...]) * (1.0 / width)
    rows = base[...] + inv_std[:, 0:1] * (
        grad[...] - total[:, 0:1] - normed[...] * total[:, 1:2]
    )
    out[...] = rows.T


def local_call(kernel, shapes, scalar_count, *operands):
    vmem = spec(pltpu.VMEM)
    return pl.pallas_call(
        kernel,
        out_shape=tuple(jax.ShapeDtypeStruct(*one) for one in shapes),
        in_specs=[spec(pltpu.SMEM)] * scalar_count + [vmem] * (len(operands) - scalar_count),
        out_specs=(vmem,) * len(shapes),
        compiler_params=pltpu.CompilerParams(vmem_limit_bytes=24 * 1024 * 1024),
        cost_estimate=pl.CostEstimate(
            flops=sum(one.size for one in operands),
            bytes_accessed=sum(one.size * one.dtype.itemsize for one in operands),
            transcendentals=0,
        ),
    )(*operands)


def shards_by_head(states, adjoint, text_kv, text_len, step_index, modulation, w_qkv, qk_gain, w_out):
    hidden_state = states[0]
    adjoint_rows = adjoint[0]
    tok_count, model_width = hidden_state.shape
    seq_count = lax.axis_size("seq")
    inner_dev = w_qkv.shape[2]
    heads_dev = inner_dev // HD
    shard = w_qkv.shape[0]
    slots = -(-heads_dev // seq_count)
    inner = slots * HD
    half_rows = tok_count // 2
    half_width = model_width // 2
    f32, bf16 = jnp.float32, jnp.bfloat16
    core = lax.axis_index("head").astype(jnp.int32)
    seq_index = lax.axis_index("seq")
    dp_index = lax.axis_index("dp")
    pin = lax.optimization_barrier

    seq_order = line_ring(seq_count)
    seq_place = ring_place(seq_order, seq_index)
    seq_next = ring_pairs(seq_order)
    swap = [(0, 1), (1, 0)]
    dp_order = line_ring(4)
    dp_place = ring_place(dp_order, dp_index)
    dp_next = [
        (2 * a, 2 * b) if c == 0 else (2 * b + 1, 2 * a + 1)
        for a, b in ring_pairs(dp_order)
        for c in range(2)
    ]

    first = seq_index * heads_dev // seq_count
    stop = (seq_index + 1) * heads_dev // seq_count
    window = jnp.minimum(first, heads_dev - slots)
    valid = [(window + i >= first) & (window + i < stop) for i in range(slots)]
    owners = [ring_member(seq_order, (seq_place - k + seq_count) % seq_count) for k in range(seq_count)]
    direction = jnp.where(core == 0, 3, 1)
    w_index = [ring_member(dp_order, (dp_place + direction * k) % 4) for k in range(4)]
    scalars = [core] + w_index + [window, text_len[0]] + owners + valid
    scalars = jnp.stack([one.astype(jnp.int32) for one in scalars])

    def step(moving):
        return lax.ppermute(moving, "seq", seq_next)

    def other_core(moving):
        return lax.ppermute(moving, "head", swap)

    mod_half, table_rows = first_call(step_index, core[None], hidden_state, modulation.transpose(1, 0, 2))
    mod_one = step(mod_half)

    w_qkv, w_out, mod_half = pin((w_qkv, w_out, mod_half))
    take = lambda c: lax.dynamic_slice(w_qkv, (0, c, window * HD), (shard, 1, inner))[:, 0]
    own_parts = [
        jnp.concatenate([take(0), take(1)], axis=1),
        jnp.concatenate([take(2), lax.dynamic_slice_in_dim(w_out, window * HD, inner, 0).T], axis=1),
    ]

    def w_step(moving):
        return lax.ppermute(moving, ("dp", "head"), dp_next)

    w_one = [w_step(part) for part in own_parts]
    w_two = [w_step(part) for part in w_one]
    w_three = [w_step(part) for part in w_two]

    adjoint_rows, text_local, *own_parts = pin((adjoint_rows, text_kv[0], *own_parts))
    squares = jnp.sum(adjoint_rows * adjoint_rows)
    text_dev = text_local.shape[0]
    text_local = text_local.transpose(1, 0, 2).reshape(2 * text_dev, inner_dev).astype(f32)
    packet = jnp.concatenate([text_local, jnp.full((8, inner_dev), squares)], axis=0)
    packets = [packet]
    for k in range(1, seq_count):
        pairs = [(seq_order[i], seq_order[(i + k) % seq_count]) for i in range(seq_count)]
        packets.append(lax.ppermute(packet, "seq", pairs))
    clip_limit = 0.5 * (tok_count * seq_count * model_width) ** 0.5
    cotangent, cot_half, base = local_call(
        functools.partial(cotangent_kernel, clip_limit, 2 * text_dev),
        [((tok_count, model_width), bf16), ((half_rows, model_width), bf16), ((tok_count, half_width), f32)],
        1,
        core[None],
        adjoint_rows,
        table_rows,
        *packets,
    )

    mod_steps = [mod_one]
    for k in range(2, seq_count):
        mod_steps.append(step(mod_steps[-1]))
    cot_half, mod_steps[0], w_one[0] = pin((cot_half, mod_steps[0], w_one[0]))
    cot_steps = [step(cot_half)]
    modulated, normed_share, scale_share, inv_std = local_call(
        modulate_kernel,
        [
            ((tok_count, model_width), bf16),
            ((tok_count, half_width), f32),
            ((1, half_width), f32),
            ((tok_count, 128), f32),
        ],
        1,
        core[None],
        hidden_state,
        table_rows,
    )
    moving, mod_steps[1], w_one[1], w_two[0], modulated = pin(
        (cot_steps[0], mod_steps[1], w_one[1], w_two[0], modulated)
    )
    cot_steps.append(step(moving))
    moving, mod_steps[2], w_two[1] = pin((cot_steps[1], mod_steps[2], w_two[1]))
    cot_steps.append(step(moving))

    def pieces(own, steps):
        return [own] + [one for moved in steps for one in (moved, other_core(moved))]

    weights = [one[part] for part in range(2) for one in (own_parts, w_one, w_two, w_three)]
    *operands, w_keep, w_give = project_call(
        scalars, qk_gain, packets, pieces(modulated, mod_steps), weights, slots, tok_count, text_dev
    )
    cot_pieces = pieces(cotangent, cot_steps)
    w_give, cot_pieces[-1] = pin((w_give, cot_pieces[-1]))
    w_other = other_core(w_give)
    first, rest = attend_call(
        scalars, qk_gain, operands, cot_pieces, weights[4:], slots, tok_count, text_dev
    )
    other_first, other_rest = other_core(first), other_core(rest)
    moving = backward_call(first, other_first, w_keep, w_other, half_rows, bf16)
    rest, other_rest, *moving = pin((rest, other_rest, *moving))
    own = backward_call(rest, other_rest, w_keep, w_other, half_rows, f32)
    for j in range(2, seq_count):
        moving = [step(part) for part in moving]
        moving = [
            (a + b.astype(f32)).astype(bf16) for a, b in zip(own[2 * (j - 2) : 2 * (j - 1)], moving)
        ]
    moving = [step(part) for part in moving]

    grad_scaled, sums = local_call(
        sums_kernel,
        [((tok_count, half_width), f32), ((tok_count, 128), f32)],
        0,
        *own[-2:],
        *moving,
        scale_share,
        normed_share,
    )
    (pulled,) = local_call(
        functools.partial(last_kernel, model_width),
        [((half_width, tok_count), f32)],
        0,
        grad_scaled,
        sums,
        other_core(sums),
        normed_share,
        base,
        inv_std,
    )
    return pulled.T[None]


def qk_normalize(values, gains):
    inverse = lax.rsqrt(jnp.mean(values * values, axis=-1, keepdims=True) + 1e-06)
    return ((values * inverse * gains).astype(jnp.bfloat16), inverse)


def qk_backward(values, inverse, cotangent, gains):
    scaled = cotangent.astype(jnp.float32) * gains
    return (
        scaled * inverse - values * jnp.mean(scaled * values, axis=-1, keepdims=True) * inverse**3
    )


def shards_by_row(states, adjoint, text_kv, text_len, step_index, modulation, w_qkv, qk_gain, w_out):
    hidden_state = states[0]
    adjoint_rows = adjoint[0]
    tok_count, model_width = hidden_state.shape
    seq_count = lax.axis_size("seq")
    inner_dev = w_qkv.shape[2]
    heads_dev = inner_dev // HD
    score_scale = HD ** (-0.5)
    squares = lax.psum(jnp.sum(adjoint_rows * adjoint_rows), "seq")
    clip_limit = 0.5 * (tok_count * seq_count * model_width) ** 0.5
    clip_scale = jnp.minimum(1.0, clip_limit / jnp.sqrt(squares + 1e-06))
    table_row = lax.dynamic_index_in_dim(modulation, step_index[0], 0, keepdims=False)
    offset_row = table_row[0]
    stretch = table_row[1]
    gating = table_row[2]
    widened = hidden_state.astype(jnp.float32)
    centered = widened - jnp.mean(widened, axis=-1, keepdims=True)
    inv_std = lax.rsqrt(jnp.mean(centered * centered, axis=-1, keepdims=True) + 1e-06)
    normed = centered * inv_std
    modulated = (normed * (1.0 + stretch) + offset_row).astype(jnp.bfloat16)
    cotangent = (gating * (clip_scale * adjoint_rows)).astype(jnp.bfloat16)
    contract_last = (((1,), (1,)), ((), ()))
    full_weight = lax.all_gather(w_qkv, "dp", axis=0, tiled=True).reshape(
        model_width, 3 * inner_dev
    )
    projected = jnp.dot(modulated, full_weight, preferred_element_type=jnp.float32)
    out_raw = lax.dot_general(
        cotangent,
        lax.all_gather(w_out, "dp", axis=1, tiled=True),
        contract_last,
        preferred_element_type=jnp.float32,
    )
    projected = projected.reshape(tok_count, 3, heads_dev, HD)
    queries, query_inv = qk_normalize(projected[:, 0], qk_gain[0])
    own_keys, key_inv = qk_normalize(projected[:, 1], qk_gain[1])
    own_values = projected[:, 2].astype(jnp.bfloat16)
    out_grad = out_raw.astype(jnp.bfloat16).reshape(tok_count, heads_dev, HD)
    text_keys = text_kv[0, :, 0, :]
    text_values = text_kv[0, :, 1, :]
    text_dev = text_keys.shape[0]
    rows_dev = tok_count + text_dev
    key_local = jnp.concatenate([own_keys.reshape(tok_count, inner_dev), text_keys], axis=0)
    value_local = jnp.concatenate([own_values.reshape(tok_count, inner_dev), text_values], axis=0)
    key_all, value_all = (
        lax.all_gather(key_local, "seq", axis=0, tiled=True),
        lax.all_gather(value_local, "seq", axis=0, tiled=True),
    )
    all_rows = rows_dev * seq_count
    row_ids = jnp.arange(all_rows, dtype=jnp.int32)
    owner = row_ids // rows_dev
    within = row_ids % rows_dev
    allowed = (within < tok_count) | (owner * text_dev + within - tok_count < text_len[0])
    group = 1
    while group * 2 * rows_dev <= 512 and seq_count % (group * 2) == 0:
        group = group * 2
    block_rows = group * rows_dev
    block_count = all_rows // block_rows
    key_blocks = key_all.reshape(block_count, block_rows, heads_dev, HD)
    value_blocks = value_all.reshape(block_count, block_rows, heads_dev, HD)
    mask_blocks = allowed.reshape(block_count, block_rows)

    def block_scores(key_block, mask_block):
        scores = (
            jnp.einsum("qhd,khd->qhk", queries, key_block, preferred_element_type=jnp.float32)
            * score_scale
        )
        return jnp.where(mask_block[None, None, :], scores, -1e30)

    def first_pass(carry, block):
        row_max, row_sum, row_dot = carry
        key_block, value_block, mask_block = block
        scores = block_scores(key_block, mask_block)
        new_max = jnp.maximum(row_max, jnp.max(scores, axis=-1))
        rescale = jnp.exp(row_max - new_max)
        exps = jnp.exp(scores - new_max[:, :, None])
        grad_weights = jnp.einsum(
            "qhd,khd->qhk", out_grad, value_block, preferred_element_type=jnp.float32
        )
        return (
            (
                new_max,
                row_sum * rescale + jnp.sum(exps, axis=-1),
                row_dot * rescale + jnp.sum(exps * grad_weights, axis=-1),
            ),
            None,
        )

    start_state = (
        jnp.full((tok_count, heads_dev), -1e30, jnp.float32),
        jnp.zeros((tok_count, heads_dev), jnp.float32),
        jnp.zeros((tok_count, heads_dev), jnp.float32),
    )
    (row_max, row_sum, row_dot), unused = lax.scan(
        first_pass, start_state, (key_blocks, value_blocks, mask_blocks)
    )
    log_total = row_max + jnp.log(row_sum)
    delta_row = row_dot / row_sum

    def second_pass(running, block):
        key_block, value_block, mask_block = block
        weights = jnp.exp(block_scores(key_block, mask_block) - log_total[:, :, None])
        grad_weights = jnp.einsum(
            "qhd,khd->qhk", out_grad, value_block, preferred_element_type=jnp.float32
        )
        grad_scores = (weights * (grad_weights - delta_row[:, :, None])).astype(jnp.bfloat16)
        return (
            running
            + jnp.einsum(
                "qhk,khd->qhd", grad_scores, key_block, preferred_element_type=jnp.float32
            ),
            None,
        )

    query_sum, unused = lax.scan(
        second_pass,
        jnp.zeros((tok_count, heads_dev, HD), jnp.float32),
        (key_blocks, value_blocks, mask_blocks),
    )
    grad_query = (query_sum * score_scale).astype(jnp.bfloat16)
    log_all, delta_all = (
        lax.all_gather(log_total, "seq", axis=0, tiled=True),
        lax.all_gather(delta_row, "seq", axis=0, tiled=True),
    )
    local_ids = jnp.arange(rows_dev, dtype=jnp.int32)
    local_allowed = (local_ids < tok_count) | (
        lax.axis_index("seq") * text_dev + local_ids - tok_count < text_len[0]
    )
    key_three = key_local.reshape(rows_dev, heads_dev, HD)
    value_three = value_local.reshape(rows_dev, heads_dev, HD)
    query_piece = lax.all_gather(queries.reshape(tok_count, inner_dev), "seq", axis=0, tiled=True)
    grad_piece = lax.all_gather(out_grad.reshape(tok_count, inner_dev), "seq", axis=0, tiled=True)
    piece_rows = query_piece.shape[0]
    query_rows = query_piece.reshape(piece_rows, heads_dev, HD)
    grad_rows = grad_piece.reshape(piece_rows, heads_dev, HD)
    scores = (
        jnp.einsum("qhd,khd->qhk", query_rows, key_three, preferred_element_type=jnp.float32)
        * score_scale
    )
    scores = jnp.where(local_allowed[None, None, :], scores, -1e30)
    weights = jnp.exp(scores - log_all[:, :, None])
    grad_weights = jnp.einsum(
        "qhd,khd->qhk", grad_rows, value_three, preferred_element_type=jnp.float32
    )
    grad_scores = (weights * (grad_weights - delta_all[:, :, None])).astype(jnp.bfloat16)
    rounded = weights.astype(jnp.bfloat16)
    key_sum = jnp.einsum(
        "qhk,qhd->khd", grad_scores, query_rows, preferred_element_type=jnp.float32
    )
    value_sum = jnp.einsum("qhk,qhd->khd", rounded, grad_rows, preferred_element_type=jnp.float32)
    key_sum, value_sum = (key_sum, value_sum)
    grad_key = (key_sum[:tok_count] * score_scale).astype(jnp.bfloat16)
    grad_value = value_sum[:tok_count].astype(jnp.bfloat16)
    raw_query = qk_backward(projected[:, 0], query_inv, grad_query, qk_gain[0])
    raw_key = qk_backward(projected[:, 1], key_inv, grad_key, qk_gain[1])
    stacked = jnp.stack([raw_query, raw_key, grad_value.astype(jnp.float32)], axis=1).astype(
        jnp.bfloat16
    )
    stacked = stacked.reshape(tok_count, 3 * inner_dev)
    partial_grad = lax.dot_general(
        stacked, full_weight, contract_last, preferred_element_type=jnp.float32
    )
    half_width = model_width // lax.axis_size("head")
    first_col = lax.axis_index("head") * half_width
    grad_share = lax.psum_scatter(
        partial_grad.astype(jnp.bfloat16), "head", scatter_dimension=1, tiled=True
    ).astype(jnp.float32)
    normed_share = lax.dynamic_slice_in_dim(normed, first_col, half_width, 1)
    stretch_share = lax.dynamic_slice_in_dim(stretch, first_col, half_width, 0)
    adjoint_share = lax.dynamic_slice_in_dim(adjoint_rows, first_col, half_width, 1)
    grad_scaled = grad_share * (1.0 + stretch_share)
    row_sums = jnp.stack(
        [jnp.sum(grad_scaled, axis=-1), jnp.sum(grad_scaled * normed_share, axis=-1)], axis=-1
    )
    row_sums = lax.psum(row_sums, "head")
    grad_state = inv_std * (
        grad_scaled - row_sums[:, 0:1] / model_width - normed_share * row_sums[:, 1:2] / model_width
    )
    pulled = clip_scale * adjoint_share + grad_state
    return pulled[None]


def solution(mesh):
    in_specs = (
        P("dp", "seq", None),
        P("dp", "seq", None),
        P("dp", "seq", None, "head"),
        P("dp"),
        P("dp"),
        P(),
        P("dp", None, "head"),
        P(),
        P("head", "dp"),
    )
    out_specs = P("dp", "seq", "head")
    by_head = mesh.shape["seq"] == 4 and mesh.shape["dp"] == 4 and mesh.shape["head"] == 2
    shards = shards_by_head if by_head else shards_by_row
    return jax.shard_map(shards, mesh=mesh, in_specs=in_specs, out_specs=out_specs, check_vma=False)
```

```python
import functools

import jax
import jax.numpy as jnp
from jax import lax
from jax.experimental import pallas as pl
from jax.experimental.pallas import tpu as pltpu
from jax.sharding import PartitionSpec as P

HD = 64
GRANT = 60 * 1024 * 1024
NT = (((1,), (1,)), ((), ()))
NN = (((1,), (0,)), ((), ()))


def line_ring(count):
    return [0] + list(range(1, count, 2)) + [i for i in range(count - 1, 0, -1) if i % 2 == 0]


def ring_pairs(order):
    return [(order[i], order[(i + 1) % len(order)]) for i in range(len(order))]


def ring_place(order, index):
    place = jnp.int32(0)
    for position, member in enumerate(order):
        place = jnp.where(index == member, jnp.int32(position), place)
    return place


def ring_member(order, place):
    member = jnp.int32(order[0])
    for position, value in enumerate(order):
        member = jnp.where(place == position, jnp.int32(value), member)
    return member


def dot(a, b, dims):
    return lax.dot_general(a, b, dims, preferred_element_type=jnp.float32)


def inverse_rms(raw):
    return lax.rsqrt(jnp.mean(raw * raw, axis=-1, keepdims=True) + 1e-06)


def norm_backward(raw, cotangent, gains):
    inverse = inverse_rms(raw)
    scaled = cotangent.astype(jnp.float32) * gains
    return (
        scaled * inverse
        - raw * jnp.mean(scaled * raw, axis=-1, keepdims=True) * (inverse * inverse * inverse)
    )


def whole_tiles(columns):
    return -(-columns // 128) * 128


def spec(space):
    return pl.BlockSpec(memory_space=space)


def first_kernel(step, core, states, table, out, rows_out):
    rows = [table[c, pl.ds(step[0], 1), :] for c in range(3)]
    widened = states[...].astype(jnp.float32)
    centered = widened - jnp.mean(widened, axis=-1, keepdims=True)
    inv_std = lax.rsqrt(jnp.mean(centered * centered, axis=-1, keepdims=True) + 1e-06)
    out[...] = (centered * inv_std * (1.0 + rows[1]) + rows[0]).astype(jnp.bfloat16)
    for c in range(3):
        rows_out[c : c + 1, :] = rows[c]


def first_call(step, core, states, table):
    rows, width = states.shape
    half = rows // 2
    whole = lambda *shape: pl.BlockSpec(shape, lambda i, step, core: (0,) * len(shape))
    return pl.pallas_call(
        first_kernel,
        out_shape=(
            jax.ShapeDtypeStruct((half, width), jnp.bfloat16),
            jax.ShapeDtypeStruct((8, width), jnp.float32),
        ),
        grid_spec=pltpu.PrefetchScalarGridSpec(
            num_scalar_prefetch=2,
            grid=(1,),
            in_specs=[
                pl.BlockSpec((half, width), lambda i, step, core: (core[0], 0)),
                whole(*table.shape),
            ],
            out_specs=(whole(half, width), whole(8, width)),
        ),
        compiler_params=pltpu.CompilerParams(vmem_limit_bytes=GRANT),
        cost_estimate=pl.CostEstimate(flops=8 * half * width, bytes_accessed=8 * half * width, transcendentals=0),
    )(step, core, states, table)


def pick_half(core, rows):
    half = rows.shape[1] // 2
    return jnp.where(core == 0, rows[:, :half], rows[:, half:])


def modulate_kernel(core, states, table_rows, out, normed_out, stretch_out, inv_out):
    widened = states[...].astype(jnp.float32)
    centered = widened - jnp.mean(widened, axis=-1, keepdims=True)
    inv_std = lax.rsqrt(jnp.mean(centered * centered, axis=-1, keepdims=True) + 1e-06)
    normed = centered * inv_std
    scale = 1.0 + table_rows[1:2, :]
    out[...] = (normed * scale + table_rows[0:1, :]).astype(jnp.bfloat16)
    normed_out[...] = pick_half(core[0], normed)
    stretch_out[...] = pick_half(core[0], scale)
    inv_out[...] = jnp.broadcast_to(inv_std, inv_out.shape)


def cotangent_kernel(limit, text_rows, core, adjoint, table_rows, *refs):
    packets, (out, half_out, base_out) = refs[:-3], refs[-3:]
    squares = packets[0][text_rows : text_rows + 1, 0:1]
    for packet in packets[1:]:
        squares = squares + packet[text_rows : text_rows + 1, 0:1]
    clip_scale = jnp.minimum(1.0, limit / jnp.sqrt(squares + 1e-06))
    gating = table_rows[2:3, :]
    clipped = clip_scale * adjoint[...]
    out[...] = (gating * clipped).astype(jnp.bfloat16)
    base_out[...] = pick_half(core[0], clipped)
    half = half_out.shape[0]
    own = adjoint[pl.ds(pl.multiple_of(core[0] * half, 8), half), :]
    half_out[...] = (gating * (clip_scale * own)).astype(jnp.bfloat16)


class Copies:
    def __init__(self, sems):
        self.sems = sems
        self.count = 0

    def start(self, source, target):
        copy = pltpu.make_async_copy(source, target, self.sems.at[self.count])
        copy.start()
        self.count += 1
        return copy

    def weights(self, scalars, w_in, w_all, shard):
        parts = len(w_in) // 4
        columns = w_all.shape[1] // parts
        return [
            self.start(
                w_in[part * 4 + k],
                w_all.at[
                    pl.ds(pl.multiple_of(scalars[1 + k] * shard, 16), shard),
                    pl.ds(part * columns, columns),
                ],
            )
            for part in range(parts)
            for k in range(4)
        ]

    def rows(self, core, pieces, target, rows):
        half = rows // 2
        copies = [[self.start(pieces[0], target.at[pl.ds(0, rows)])]]
        for j in range(1, (len(pieces) + 1) // 2):
            near = pl.multiple_of(j * rows + core * half, 16)
            far = pl.multiple_of(j * rows + (1 - core) * half, 16)
            copies.append(
                [
                    self.start(pieces[2 * j - 1], target.at[pl.ds(near, half)]),
                    self.start(pieces[2 * j], target.at[pl.ds(far, half)]),
                ]
            )
        return copies


def project_kernel(slots, count, rows, shard, width, text_dev, scalars, gain, *refs):
    refs = list(refs)
    take = lambda n: [refs.pop(0) for _ in range(n)]
    packets = take(count)
    mod_in = take(2 * count - 1)
    w_in = take(8)
    q_all, k_all, v_all, k_t, raw_q, raw_k, text, text_t, w_keep, w_give = take(10)
    w_all, mod_all, sems = take(3)
    inner = slots * HD
    core = scalars[0]
    copies = Copies(sems)
    w_copies = copies.weights(scalars, w_in, w_all, shard)
    row_copies = copies.rows(core, mod_in, mod_all, rows)

    lanes = packets[0].shape[1]
    shift = lax.rem(lanes - scalars[5] * HD, lanes)
    for part in range(2):
        found = [
            pltpu.roll(one[part * text_dev : (part + 1) * text_dev, :], shift, 1) for one in packets
        ]
        found = jnp.concatenate(found, axis=0)
        for i in range(slots):
            one = found[:, i * HD : (i + 1) * HD]
            text[part, i] = one.astype(jnp.bfloat16)
            if part == 0:
                text_t[i] = one.T.astype(jnp.bfloat16)

    gain_q = gain[0:1, :]
    gain_k = gain[1:2, :]
    score_scale = HD ** (-0.5)
    for copy in w_copies:
        copy.wait()
    half = width // 2
    columns = w_keep.shape[1]
    w_keep[...] = w_all[pl.ds(pl.multiple_of(core * half, 16), half), :columns]
    w_give[...] = w_all[pl.ds(pl.multiple_of((1 - core) * half, 16), half), :columns]
    span = 2 * rows
    for b in range(count // 2):
        for copy in row_copies[2 * b] + row_copies[2 * b + 1]:
            copy.wait()
        here = slice(b * span, (b + 1) * span)
        projected = jnp.dot(
            mod_all[here, :], w_all[:, : 3 * inner], preferred_element_type=jnp.float32
        )
        for i in range(slots):
            query = projected[:, i * HD : (i + 1) * HD]
            key = projected[:, inner + i * HD : inner + (i + 1) * HD]
            value = projected[:, 2 * inner + i * HD : 2 * inner + (i + 1) * HD]
            raw_q[i, here, :] = query
            raw_k[i, here, :] = key
            query = query * inverse_rms(query) * gain_q
            q_all[i, here, :] = (query * score_scale).astype(jnp.bfloat16)
            key = key * inverse_rms(key) * gain_k
            k_all[i, here, :] = key.astype(jnp.bfloat16)
            k_t[i, :, here] = key.T.astype(jnp.bfloat16)
            v_all[i, here, :] = value.astype(jnp.bfloat16)


def attend_kernel(slots, count, rows, shard, width, text_dev, scalars, gain, *refs):
    refs = list(refs)
    take = lambda n: [refs.pop(0) for _ in range(n)]
    projected = take(8)
    cot_in = take(2 * count - 1)
    w_in = take(4)
    first_out, rest_out = take(2)
    w_all, cot_all, sems = take(3)
    d_all, grad_k, grad_v, back_q, stacked = take(5)
    q_all, k_all, v_all, k_t, raw_q, raw_k, text, text_t = refs
    inner = slots * HD
    tokens = rows * count
    core = scalars[0]
    copies = Copies(sems)
    w_copies = copies.weights(scalars, w_in, w_all, shard)
    row_copies = copies.rows(core, cot_in, cot_all, rows)
    local_copies = [copies.start(*one) for one in zip(projected, refs)]
    gain_q = gain[0:1, :]
    gain_k = gain[1:2, :]
    score_scale = HD ** (-0.5)
    span = 2 * rows

    text_rows = count * text_dev
    row = lax.broadcasted_iota(jnp.int32, (text_rows, span), 0)
    text_id = row
    for k in range(count):
        inside = (row >= k * text_dev) & (row < (k + 1) * text_dev)
        text_id = jnp.where(inside, row + (scalars[7 + k] - k) * text_dev, text_id)
    bias = jnp.where(text_id < scalars[6], 0.0, -1e30)

    for copy in w_copies:
        copy.wait()
    for b in range(count // 2):
        for copy in row_copies[2 * b] + row_copies[2 * b + 1]:
            copy.wait()
        here = slice(b * span, (b + 1) * span)
        out_grad = jnp.dot(
            cot_all[here, :], w_all[:, inner:], preferred_element_type=jnp.float32
        )
        for i in range(slots):
            d_all[i, here, :] = out_grad[:, i * HD : (i + 1) * HD].astype(jnp.bfloat16)

    grad_k[...] = jnp.zeros_like(grad_k)
    grad_v[...] = jnp.zeros_like(grad_v)
    if stacked.shape[1] > 3 * inner:
        stacked[:, 3 * inner :] = jnp.zeros((tokens, stacked.shape[1] - 3 * inner), jnp.float32)
    for copy in local_copies:
        copy.wait()

    @pl.loop(0, slots * (count // 2))
    def attend(t):
        i = t // (count // 2)
        here = pl.ds(pl.multiple_of(t % (count // 2) * span, span), span)
        query = q_all[i, here, :]
        grad = d_all[i, here, :]
        scores = dot(k_all[i], query, NT)
        text_scores = dot(text[0, i], query, NT) + bias
        col_max = jnp.maximum(
            jnp.max(scores, axis=0, keepdims=True), jnp.max(text_scores, axis=0, keepdims=True)
        )
        exps = jnp.exp(scores - col_max)
        text_exps = jnp.exp(text_scores - col_max)
        total = jnp.sum(exps, axis=0, keepdims=True) + jnp.sum(text_exps, axis=0, keepdims=True)
        inverse = 1.0 / total
        grad_w = dot(v_all[i], grad, NT)
        text_grad_w = dot(text[1, i], grad, NT)
        delta = inverse * (
            jnp.sum(exps * grad_w, axis=0, keepdims=True)
            + jnp.sum(text_exps * text_grad_w, axis=0, keepdims=True)
        )
        weights = exps * inverse
        grad_s = (weights * (grad_w - delta)).astype(jnp.bfloat16)
        text_grad_s = (text_exps * inverse * (text_grad_w - delta)).astype(jnp.bfloat16)
        grad_k[i] += dot(grad_s, query, NN)
        grad_v[i] += dot(weights.astype(jnp.bfloat16), grad, NN)
        grad_q = dot(k_t[i], grad_s, NN) + dot(text_t[i], text_grad_s, NN)
        grad_q = (grad_q.T * score_scale).astype(jnp.bfloat16)
        back_q[i, here, :] = norm_backward(raw_q[i, here, :], grad_q, gain_q)

    for i in range(slots):
        valid = scalars[7 + count + i] > 0
        back_k = norm_backward(raw_k[i], grad_k[i].astype(jnp.bfloat16), gain_k)
        stacked[:, i * HD : (i + 1) * HD] = jnp.where(valid, back_q[i], 0.0)
        stacked[:, inner + i * HD : inner + (i + 1) * HD] = jnp.where(valid, back_k, 0.0)
        stacked[:, 2 * inner + i * HD : 2 * inner + (i + 1) * HD] = jnp.where(valid, grad_v[i], 0.0)
    first_out[...] = stacked[rows : 2 * rows, :].astype(jnp.bfloat16)
    rest_out[: (count - 2) * rows, :] = stacked[2 * rows :, :].astype(jnp.bfloat16)
    rest_out[(count - 2) * rows :, :] = stacked[:rows, :].astype(jnp.bfloat16)


def project_call(scalars, gain, packets, mod, weights, slots, rows, text_dev):
    count = len(packets)
    shard = weights[0].shape[0]
    columns = 4 * slots * HD
    width = mod[0].shape[1]
    tokens = rows * count
    text_rows = text_dev * count
    f32, bf16 = jnp.float32, jnp.bfloat16
    vmem, hbm = spec(pltpu.VMEM), spec(pl.ANY)
    by_token = (slots, tokens, HD)
    shapes = [(by_token, bf16)] * 3 + [((slots, HD, tokens), bf16)] + [(by_token, f32)] * 2
    shapes += [((2, slots, text_rows, HD), bf16), ((slots, HD, text_rows), bf16)]
    shapes += [((width // 2, whole_tiles(3 * slots * HD)), bf16)] * 2
    return pl.pallas_call(
        functools.partial(project_kernel, slots, count, rows, shard, width, text_dev),
        out_shape=tuple(jax.ShapeDtypeStruct(*one) for one in shapes),
        in_specs=[spec(pltpu.SMEM), vmem] + [vmem] * count + [hbm] * (len(mod) + len(weights)),
        out_specs=(vmem,) * len(shapes),
        scratch_shapes=[
            pltpu.VMEM((width, columns), bf16),
            pltpu.VMEM((tokens, width), bf16),
            pltpu.SemaphoreType.DMA((len(mod) + len(weights),)),
        ],
        compiler_params=pltpu.CompilerParams(vmem_limit_bytes=GRANT),
        cost_estimate=pl.CostEstimate(
            flops=2 * tokens * width * 3 * slots * HD,
            bytes_accessed=2 * (tokens * width + columns * width) + 4 * tokens * columns,
            transcendentals=0,
        ),
    )(scalars, gain, *packets, *mod, *weights)


def attend_call(scalars, gain, operands, cot, weights, slots, rows, text_dev):
    count = (len(cot) + 1) // 2
    shard, columns = weights[0].shape
    width = cot[0].shape[1]
    tokens = rows * count
    inner = slots * HD
    f32, bf16 = jnp.float32, jnp.bfloat16
    vmem, hbm = spec(pltpu.VMEM), spec(pl.ANY)
    stacked = whole_tiles(3 * inner)
    shapes = [((rows, stacked), bf16), ((tokens - rows, stacked), bf16)]
    return pl.pallas_call(
        functools.partial(attend_kernel, slots, count, rows, shard, width, text_dev),
        out_shape=tuple(jax.ShapeDtypeStruct(*one) for one in shapes),
        in_specs=[spec(pltpu.SMEM), vmem] + [hbm] * (len(operands) + len(cot) + len(weights)),
        out_specs=(vmem,) * len(shapes),
        scratch_shapes=[
            pltpu.VMEM((width, columns), bf16),
            pltpu.VMEM((tokens, width), bf16),
            pltpu.SemaphoreType.DMA((len(operands) + len(cot) + len(weights),)),
            pltpu.VMEM((slots, tokens, HD), bf16),
        ]
        + [pltpu.VMEM((slots, tokens, HD), f32)] * 3
        + [pltpu.VMEM((tokens, stacked), f32)]
        + [pltpu.VMEM(one.shape, one.dtype) for one in operands],
        compiler_params=pltpu.CompilerParams(vmem_limit_bytes=GRANT),
        cost_estimate=pl.CostEstimate(
            flops=2 * tokens * width * inner + 10 * tokens * tokens * inner,
            bytes_accessed=2 * (tokens * width + columns * width),
            transcendentals=slots * tokens * tokens,
        ),
    )(scalars, gain, *operands, *cot, *weights)


def backward_kernel(own, other, w_own, w_other, *outs):
    total = dot(own[...], w_own[...], NT) + dot(other[...], w_other[...], NT)
    part = outs[0].shape[0]
    for n, out in enumerate(outs):
        out[...] = total[n * part : (n + 1) * part].astype(out.dtype)


def backward_call(own, other, w_own, w_other, part, dtype):
    rows, inner = own.shape
    half = w_own.shape[0]
    vmem = spec(pltpu.VMEM)
    return pl.pallas_call(
        backward_kernel,
        out_shape=(jax.ShapeDtypeStruct((part, half), dtype),) * (rows // part),
        in_specs=[vmem] * 4,
        out_specs=(vmem,) * (rows // part),
        compiler_params=pltpu.CompilerParams(vmem_limit_bytes=GRANT),
        cost_estimate=pl.CostEstimate(
            flops=4 * rows * half * inner,
            bytes_accessed=4 * (rows + half) * inner + 4 * rows * half,
            transcendentals=0,
        ),
    )(own, other, w_own, w_other)


def sums_kernel(own_near, own_far, near, far, scale, normed, grad_out, sums_out):
    half = near.shape[0]
    for part, (own, moving) in enumerate(((own_near, near), (own_far, far))):
        here = slice(part * half, (part + 1) * half)
        grad = (own[...] + moving[...].astype(jnp.float32)) * scale[...]
        grad_out[here, :] = grad
        first = jnp.sum(grad, axis=-1, keepdims=True)
        second = jnp.sum(grad * normed[here, :], axis=-1, keepdims=True)
        lane = lax.broadcasted_iota(jnp.int32, (half, 128), 1)
        sums_out[here, :] = jnp.where(lane == 0, first, second)


def last_kernel(width, grad, sums, other, normed, base, inv_std, out):
    total = (sums[...] + other[...]) * (1.0 / width)
    rows = base[...] + inv_std[:, 0:1] * (
        grad[...] - total[:, 0:1] - normed[...] * total[:, 1:2]
    )
    out[...] = rows.T


def local_call(kernel, shapes, scalar_count, *operands):
    vmem = spec(pltpu.VMEM)
    return pl.pallas_call(
        kernel,
        out_shape=tuple(jax.ShapeDtypeStruct(*one) for one in shapes),
        in_specs=[spec(pltpu.SMEM)] * scalar_count + [vmem] * (len(operands) - scalar_count),
        out_specs=(vmem,) * len(shapes),
        compiler_params=pltpu.CompilerParams(vmem_limit_bytes=GRANT),
        cost_estimate=pl.CostEstimate(
            flops=sum(one.size for one in operands),
            bytes_accessed=sum(one.size * one.dtype.itemsize for one in operands),
            transcendentals=0,
        ),
    )(*operands)


def shards_by_head(states, adjoint, text_kv, text_len, step_index, modulation, w_qkv, qk_gain, w_out):
    hidden_state = states[0]
    adjoint_rows = adjoint[0]
    tok_count, model_width = hidden_state.shape
    seq_count = lax.axis_size("seq")
    inner_dev = w_qkv.shape[2]
    heads_dev = inner_dev // HD
    shard = w_qkv.shape[0]
    slots = -(-heads_dev // seq_count)
    inner = slots * HD
    half_rows = tok_count // 2
    half_width = model_width // 2
    f32, bf16 = jnp.float32, jnp.bfloat16
    core = lax.axis_index("head").astype(jnp.int32)
    seq_index = lax.axis_index("seq")
    dp_index = lax.axis_index("dp")
    pin = lax.optimization_barrier

    seq_order = line_ring(seq_count)
    seq_place = ring_place(seq_order, seq_index)
    seq_next = ring_pairs(seq_order)
    swap = [(0, 1), (1, 0)]
    dp_order = line_ring(4)
    dp_place = ring_place(dp_order, dp_index)
    dp_next = [
        (2 * a, 2 * b) if c == 0 else (2 * b + 1, 2 * a + 1)
        for a, b in ring_pairs(dp_order)
        for c in range(2)
    ]

    first = seq_index * heads_dev // seq_count
    stop = (seq_index + 1) * heads_dev // seq_count
    window = jnp.minimum(first, heads_dev - slots)
    valid = [(window + i >= first) & (window + i < stop) for i in range(slots)]
    owners = [ring_member(seq_order, (seq_place - k + seq_count) % seq_count) for k in range(seq_count)]
    direction = jnp.where(core == 0, 3, 1)
    w_index = [ring_member(dp_order, (dp_place + direction * k) % 4) for k in range(4)]
    scalars = [core] + w_index + [window, text_len[0]] + owners + valid
    scalars = jnp.stack([one.astype(jnp.int32) for one in scalars])

    def step(moving):
        return lax.ppermute(moving, "seq", seq_next)

    def other_core(moving):
        return lax.ppermute(moving, "head", swap)

    mod_half, table_rows = first_call(step_index, core[None], hidden_state, modulation.transpose(1, 0, 2))
    mod_one = step(mod_half)

    w_qkv, w_out, mod_half = pin((w_qkv, w_out, mod_half))
    take = lambda c: lax.dynamic_slice(w_qkv, (0, c, window * HD), (shard, 1, inner))[:, 0]
    own_parts = [
        jnp.concatenate([take(0), take(1)], axis=1),
        jnp.concatenate([take(2), lax.dynamic_slice_in_dim(w_out, window * HD, inner, 0).T], axis=1),
    ]

    def w_step(moving):
        return lax.ppermute(moving, ("dp", "head"), dp_next)

    w_one = [w_step(part) for part in own_parts]

    adjoint_rows, text_local, *own_parts = pin((adjoint_rows, text_kv[0], *own_parts))
    squares = jnp.sum(adjoint_rows * adjoint_rows)
    squares, mod_one, w_one[0] = pin((squares, mod_one, w_one[0]))
    mod_two = step(mod_one)
    text_dev = text_local.shape[0]
    text_local = text_local.transpose(1, 0, 2).reshape(2 * text_dev, inner_dev).astype(f32)
    packet = jnp.concatenate([text_local, jnp.full((8, inner_dev), squares)], axis=0)
    packets = [packet]
    for k in range(1, seq_count):
        pairs = [(seq_order[i], seq_order[(i + k) % seq_count]) for i in range(seq_count)]
        packets.append(lax.ppermute(packet, "seq", pairs))
    w_two = [w_step(w_one[0])]
    mod_two, w_one[1], *packets = pin((mod_two, w_one[1], *packets))
    mod_three = step(mod_two)
    w_two.append(w_step(w_one[1]))
    clip_limit = 0.5 * (tok_count * seq_count * model_width) ** 0.5
    cotangent, cot_half, base = local_call(
        functools.partial(cotangent_kernel, clip_limit, 2 * text_dev),
        [((tok_count, model_width), bf16), ((half_rows, model_width), bf16), ((tok_count, half_width), f32)],
        1,
        core[None],
        adjoint_rows,
        table_rows,
        *packets,
    )

    mod_steps = [mod_one, mod_two, mod_three]
    cot_steps = [step(cot_half)]
    modulated, normed_share, scale_share, inv_std = local_call(
        modulate_kernel,
        [
            ((tok_count, model_width), bf16),
            ((tok_count, half_width), f32),
            ((1, half_width), f32),
            ((tok_count, 128), f32),
        ],
        1,
        core[None],
        hidden_state,
        table_rows,
    )
    moving, w_two[0], w_two[1], mod_steps[2], modulated = pin(
        (cot_steps[0], w_two[0], w_two[1], mod_steps[2], modulated)
    )
    w_three = [w_step(part) for part in w_two]
    cot_steps.append(step(moving))
    moving, w_three[0] = pin((cot_steps[1], w_three[0]))
    cot_steps.append(step(moving))

    def pieces(own, steps):
        return [own] + [one for moved in steps for one in (moved, other_core(moved))]

    weights = [one[part] for part in range(2) for one in (own_parts, w_one, w_two, w_three)]
    *operands, w_keep, w_give = project_call(
        scalars, qk_gain, packets, pieces(modulated, mod_steps), weights, slots, tok_count, text_dev
    )
    cot_pieces = pieces(cotangent, cot_steps)
    w_give, cot_pieces[-1] = pin((w_give, cot_pieces[-1]))
    w_other = other_core(w_give)
    first, rest = attend_call(
        scalars, qk_gain, operands, cot_pieces, weights[4:], slots, tok_count, text_dev
    )
    other_first, other_rest = other_core(first), other_core(rest)
    moving = backward_call(first, other_first, w_keep, w_other, half_rows, bf16)
    rest, other_rest, *moving = pin((rest, other_rest, *moving))
    own = backward_call(rest, other_rest, w_keep, w_other, half_rows, f32)
    for j in range(2, seq_count):
        moving = [step(part) for part in moving]
        moving = [
            (a + b.astype(f32)).astype(bf16) for a, b in zip(own[2 * (j - 2) : 2 * (j - 1)], moving)
        ]
    moving = [step(part) for part in moving]

    grad_scaled, sums = local_call(
        sums_kernel,
        [((tok_count, half_width), f32), ((tok_count, 128), f32)],
        0,
        *own[-2:],
        *moving,
        scale_share,
        normed_share,
    )
    (pulled,) = local_call(
        functools.partial(last_kernel, model_width),
        [((half_width, tok_count), f32)],
        0,
        grad_scaled,
        sums,
        other_core(sums),
        normed_share,
        base,
        inv_std,
    )
    return pulled.T[None]


def qk_normalize(values, gains):
    inverse = lax.rsqrt(jnp.mean(values * values, axis=-1, keepdims=True) + 1e-06)
    return ((values * inverse * gains).astype(jnp.bfloat16), inverse)


def qk_backward(values, inverse, cotangent, gains):
    scaled = cotangent.astype(jnp.float32) * gains
    return (
        scaled * inverse - values * jnp.mean(scaled * values, axis=-1, keepdims=True) * inverse**3
    )


def shards_by_row(states, adjoint, text_kv, text_len, step_index, modulation, w_qkv, qk_gain, w_out):
    hidden_state = states[0]
    adjoint_rows = adjoint[0]
    tok_count, model_width = hidden_state.shape
    seq_count = lax.axis_size("seq")
    inner_dev = w_qkv.shape[2]
    heads_dev = inner_dev // HD
    score_scale = HD ** (-0.5)
    squares = lax.psum(jnp.sum(adjoint_rows * adjoint_rows), "seq")
    clip_limit = 0.5 * (tok_count * seq_count * model_width) ** 0.5
    clip_scale = jnp.minimum(1.0, clip_limit / jnp.sqrt(squares + 1e-06))
    table_row = lax.dynamic_index_in_dim(modulation, step_index[0], 0, keepdims=False)
    offset_row = table_row[0]
    stretch = table_row[1]
    gating = table_row[2]
    widened = hidden_state.astype(jnp.float32)
    centered = widened - jnp.mean(widened, axis=-1, keepdims=True)
    inv_std = lax.rsqrt(jnp.mean(centered * centered, axis=-1, keepdims=True) + 1e-06)
    normed = centered * inv_std
    modulated = (normed * (1.0 + stretch) + offset_row).astype(jnp.bfloat16)
    cotangent = (gating * (clip_scale * adjoint_rows)).astype(jnp.bfloat16)
    contract_last = (((1,), (1,)), ((), ()))
    full_weight = lax.all_gather(w_qkv, "dp", axis=0, tiled=True).reshape(
        model_width, 3 * inner_dev
    )
    projected = jnp.dot(modulated, full_weight, preferred_element_type=jnp.float32)
    out_raw = lax.dot_general(
        cotangent,
        lax.all_gather(w_out, "dp", axis=1, tiled=True),
        contract_last,
        preferred_element_type=jnp.float32,
    )
    projected = projected.reshape(tok_count, 3, heads_dev, HD)
    queries, query_inv = qk_normalize(projected[:, 0], qk_gain[0])
    own_keys, key_inv = qk_normalize(projected[:, 1], qk_gain[1])
    own_values = projected[:, 2].astype(jnp.bfloat16)
    out_grad = out_raw.astype(jnp.bfloat16).reshape(tok_count, heads_dev, HD)
    text_keys = text_kv[0, :, 0, :]
    text_values = text_kv[0, :, 1, :]
    text_dev = text_keys.shape[0]
    rows_dev = tok_count + text_dev
    key_local = jnp.concatenate([own_keys.reshape(tok_count, inner_dev), text_keys], axis=0)
    value_local = jnp.concatenate([own_values.reshape(tok_count, inner_dev), text_values], axis=0)
    key_all, value_all = (
        lax.all_gather(key_local, "seq", axis=0, tiled=True),
        lax.all_gather(value_local, "seq", axis=0, tiled=True),
    )
    all_rows = rows_dev * seq_count
    row_ids = jnp.arange(all_rows, dtype=jnp.int32)
    owner = row_ids // rows_dev
    within = row_ids % rows_dev
    allowed = (within < tok_count) | (owner * text_dev + within - tok_count < text_len[0])
    group = 1
    while group * 2 * rows_dev <= 512 and seq_count % (group * 2) == 0:
        group = group * 2
    block_rows = group * rows_dev
    block_count = all_rows // block_rows
    key_blocks = key_all.reshape(block_count, block_rows, heads_dev, HD)
    value_blocks = value_all.reshape(block_count, block_rows, heads_dev, HD)
    mask_blocks = allowed.reshape(block_count, block_rows)

    def block_scores(key_block, mask_block):
        scores = (
            jnp.einsum("qhd,khd->qhk", queries, key_block, preferred_element_type=jnp.float32)
            * score_scale
        )
        return jnp.where(mask_block[None, None, :], scores, -1e30)

    def first_pass(carry, block):
        row_max, row_sum, row_dot = carry
        key_block, value_block, mask_block = block
        scores = block_scores(key_block, mask_block)
        new_max = jnp.maximum(row_max, jnp.max(scores, axis=-1))
        rescale = jnp.exp(row_max - new_max)
        exps = jnp.exp(scores - new_max[:, :, None])
        grad_weights = jnp.einsum(
            "qhd,khd->qhk", out_grad, value_block, preferred_element_type=jnp.float32
        )
        return (
            (
                new_max,
                row_sum * rescale + jnp.sum(exps, axis=-1),
                row_dot * rescale + jnp.sum(exps * grad_weights, axis=-1),
            ),
            None,
        )

    start_state = (
        jnp.full((tok_count, heads_dev), -1e30, jnp.float32),
        jnp.zeros((tok_count, heads_dev), jnp.float32),
        jnp.zeros((tok_count, heads_dev), jnp.float32),
    )
    (row_max, row_sum, row_dot), unused = lax.scan(
        first_pass, start_state, (key_blocks, value_blocks, mask_blocks)
    )
    log_total = row_max + jnp.log(row_sum)
    delta_row = row_dot / row_sum

    def second_pass(running, block):
        key_block, value_block, mask_block = block
        weights = jnp.exp(block_scores(key_block, mask_block) - log_total[:, :, None])
        grad_weights = jnp.einsum(
            "qhd,khd->qhk", out_grad, value_block, preferred_element_type=jnp.float32
        )
        grad_scores = (weights * (grad_weights - delta_row[:, :, None])).astype(jnp.bfloat16)
        return (
            running
            + jnp.einsum(
                "qhk,khd->qhd", grad_scores, key_block, preferred_element_type=jnp.float32
            ),
            None,
        )

    query_sum, unused = lax.scan(
        second_pass,
        jnp.zeros((tok_count, heads_dev, HD), jnp.float32),
        (key_blocks, value_blocks, mask_blocks),
    )
    grad_query = (query_sum * score_scale).astype(jnp.bfloat16)
    log_all, delta_all = (
        lax.all_gather(log_total, "seq", axis=0, tiled=True),
        lax.all_gather(delta_row, "seq", axis=0, tiled=True),
    )
    local_ids = jnp.arange(rows_dev, dtype=jnp.int32)
    local_allowed = (local_ids < tok_count) | (
        lax.axis_index("seq") * text_dev + local_ids - tok_count < text_len[0]
    )
    key_three = key_local.reshape(rows_dev, heads_dev, HD)
    value_three = value_local.reshape(rows_dev, heads_dev, HD)
    query_piece = lax.all_gather(queries.reshape(tok_count, inner_dev), "seq", axis=0, tiled=True)
    grad_piece = lax.all_gather(out_grad.reshape(tok_count, inner_dev), "seq", axis=0, tiled=True)
    piece_rows = query_piece.shape[0]
    query_rows = query_piece.reshape(piece_rows, heads_dev, HD)
    grad_rows = grad_piece.reshape(piece_rows, heads_dev, HD)
    scores = (
        jnp.einsum("qhd,khd->qhk", query_rows, key_three, preferred_element_type=jnp.float32)
        * score_scale
    )
    scores = jnp.where(local_allowed[None, None, :], scores, -1e30)
    weights = jnp.exp(scores - log_all[:, :, None])
    grad_weights = jnp.einsum(
        "qhd,khd->qhk", grad_rows, value_three, preferred_element_type=jnp.float32
    )
    grad_scores = (weights * (grad_weights - delta_all[:, :, None])).astype(jnp.bfloat16)
    rounded = weights.astype(jnp.bfloat16)
    key_sum = jnp.einsum(
        "qhk,qhd->khd", grad_scores, query_rows, preferred_element_type=jnp.float32
    )
    value_sum = jnp.einsum("qhk,qhd->khd", rounded, grad_rows, preferred_element_type=jnp.float32)
    key_sum, value_sum = (key_sum, value_sum)
    grad_key = (key_sum[:tok_count] * score_scale).astype(jnp.bfloat16)
    grad_value = value_sum[:tok_count].astype(jnp.bfloat16)
    raw_query = qk_backward(projected[:, 0], query_inv, grad_query, qk_gain[0])
    raw_key = qk_backward(projected[:, 1], key_inv, grad_key, qk_gain[1])
    stacked = jnp.stack([raw_query, raw_key, grad_value.astype(jnp.float32)], axis=1).astype(
        jnp.bfloat16
    )
    stacked = stacked.reshape(tok_count, 3 * inner_dev)
    partial_grad = lax.dot_general(
        stacked, full_weight, contract_last, preferred_element_type=jnp.float32
    )
    half_width = model_width // lax.axis_size("head")
    first_col = lax.axis_index("head") * half_width
    grad_share = lax.psum_scatter(
        partial_grad.astype(jnp.bfloat16), "head", scatter_dimension=1, tiled=True
    ).astype(jnp.float32)
    normed_share = lax.dynamic_slice_in_dim(normed, first_col, half_width, 1)
    stretch_share = lax.dynamic_slice_in_dim(stretch, first_col, half_width, 0)
    adjoint_share = lax.dynamic_slice_in_dim(adjoint_rows, first_col, half_width, 1)
    grad_scaled = grad_share * (1.0 + stretch_share)
    row_sums = jnp.stack(
        [jnp.sum(grad_scaled, axis=-1), jnp.sum(grad_scaled * normed_share, axis=-1)], axis=-1
    )
    row_sums = lax.psum(row_sums, "head")
    grad_state = inv_std * (
        grad_scaled - row_sums[:, 0:1] / model_width - normed_share * row_sums[:, 1:2] / model_width
    )
    pulled = clip_scale * adjoint_share + grad_state
    return pulled[None]


def solution(mesh):
    in_specs = (
        P("dp", "seq", None),
        P("dp", "seq", None),
        P("dp", "seq", None, "head"),
        P("dp"),
        P("dp"),
        P(),
        P("dp", None, "head"),
        P(),
        P("head", "dp"),
    )
    out_specs = P("dp", "seq", "head")
    by_head = mesh.shape["seq"] == 4 and mesh.shape["dp"] == 4 and mesh.shape["head"] == 2
    shards = shards_by_head if by_head else shards_by_row
    return jax.shard_map(shards, mesh=mesh, in_specs=in_specs, out_specs=out_specs, check_vma=False)
```

```python
import functools

import jax
import jax.numpy as jnp
from jax import lax
from jax.experimental import pallas as pl
from jax.experimental.pallas import tpu as pltpu
from jax.sharding import PartitionSpec as P

HD = 64
GRANT = 60 * 1024 * 1024
SMALL_GRANT = 24 * 1024 * 1024
NT = (((1,), (1,)), ((), ()))
NN = (((1,), (0,)), ((), ()))


def line_ring(count):
    return [0] + list(range(1, count, 2)) + [i for i in range(count - 1, 0, -1) if i % 2 == 0]


def ring_pairs(order):
    return [(order[i], order[(i + 1) % len(order)]) for i in range(len(order))]


def ring_place(order, index):
    place = jnp.int32(0)
    for position, member in enumerate(order):
        place = jnp.where(index == member, jnp.int32(position), place)
    return place


def ring_member(order, place):
    member = jnp.int32(order[0])
    for position, value in enumerate(order):
        member = jnp.where(place == position, jnp.int32(value), member)
    return member


def dot(a, b, dims):
    return lax.dot_general(a, b, dims, preferred_element_type=jnp.float32)


def inverse_rms(raw):
    return lax.rsqrt(jnp.mean(raw * raw, axis=-1, keepdims=True) + 1e-06)


def norm_backward(raw, cotangent, gains):
    inverse = inverse_rms(raw)
    scaled = cotangent.astype(jnp.float32) * gains
    return (
        scaled * inverse
        - raw * jnp.mean(scaled * raw, axis=-1, keepdims=True) * (inverse * inverse * inverse)
    )


def whole_tiles(columns):
    return -(-columns // 128) * 128


def spec(space):
    return pl.BlockSpec(memory_space=space)


def first_kernel(step, core, states, table, out, rows_out):
    rows = [table[c, pl.ds(step[0], 1), :] for c in range(3)]
    widened = states[...].astype(jnp.float32)
    centered = widened - jnp.mean(widened, axis=-1, keepdims=True)
    inv_std = lax.rsqrt(jnp.mean(centered * centered, axis=-1, keepdims=True) + 1e-06)
    out[...] = (centered * inv_std * (1.0 + rows[1]) + rows[0]).astype(jnp.bfloat16)
    for c in range(3):
        rows_out[c : c + 1, :] = rows[c]


def first_call(step, core, states, table):
    rows, width = states.shape
    half = rows // 2
    whole = lambda *shape: pl.BlockSpec(shape, lambda i, step, core: (0,) * len(shape))
    return pl.pallas_call(
        first_kernel,
        out_shape=(
            jax.ShapeDtypeStruct((half, width), jnp.bfloat16),
            jax.ShapeDtypeStruct((8, width), jnp.float32),
        ),
        grid_spec=pltpu.PrefetchScalarGridSpec(
            num_scalar_prefetch=2,
            grid=(1,),
            in_specs=[
                pl.BlockSpec((half, width), lambda i, step, core: (core[0], 0)),
                whole(*table.shape),
            ],
            out_specs=(whole(half, width), whole(8, width)),
        ),
        compiler_params=pltpu.CompilerParams(vmem_limit_bytes=GRANT),
        cost_estimate=pl.CostEstimate(flops=8 * half * width, bytes_accessed=8 * half * width, transcendentals=0),
    )(step, core, states, table)


def pick_half(core, rows):
    half = rows.shape[1] // 2
    return jnp.where(core == 0, rows[:, :half], rows[:, half:])


def modulate_kernel(core, states, table_rows, out, normed_out, stretch_out, inv_out):
    widened = states[...].astype(jnp.float32)
    centered = widened - jnp.mean(widened, axis=-1, keepdims=True)
    inv_std = lax.rsqrt(jnp.mean(centered * centered, axis=-1, keepdims=True) + 1e-06)
    normed = centered * inv_std
    scale = 1.0 + table_rows[1:2, :]
    out[...] = (normed * scale + table_rows[0:1, :]).astype(jnp.bfloat16)
    normed_out[...] = pick_half(core[0], normed)
    stretch_out[...] = pick_half(core[0], scale)
    inv_out[...] = jnp.broadcast_to(inv_std, inv_out.shape)


def cotangent_kernel(limit, text_rows, core, adjoint, table_rows, *refs):
    packets, (out, half_out, base_out) = refs[:-3], refs[-3:]
    squares = packets[0][text_rows : text_rows + 1, 0:1]
    for packet in packets[1:]:
        squares = squares + packet[text_rows : text_rows + 1, 0:1]
    clip_scale = jnp.minimum(1.0, limit / jnp.sqrt(squares + 1e-06))
    gating = table_rows[2:3, :]
    clipped = clip_scale * adjoint[...]
    out[...] = (gating * clipped).astype(jnp.bfloat16)
    base_out[...] = pick_half(core[0], clipped)
    half = half_out.shape[0]
    own = adjoint[pl.ds(pl.multiple_of(core[0] * half, 8), half), :]
    half_out[...] = (gating * (clip_scale * own)).astype(jnp.bfloat16)


class Copies:
    def __init__(self, sems):
        self.sems = sems
        self.count = 0

    def start(self, source, target):
        copy = pltpu.make_async_copy(source, target, self.sems.at[self.count])
        copy.start()
        self.count += 1
        return copy

    def weights(self, scalars, w_in, w_all, shard):
        half = shard // 2
        places = [
            (scalars[1] * shard, shard),
            (scalars[2] * shard, shard),
            (scalars[3] * shard, shard),
            (scalars[4] * shard, half),
            (scalars[4] * shard + half, half),
        ]
        return [
            self.start(piece, w_all.at[pl.ds(pl.multiple_of(first, 16), size)])
            for piece, (first, size) in zip(w_in, places)
        ]

    def rows(self, core, pieces, target, rows):
        half, quarter = rows // 2, rows // 4
        copies = [self.start(pieces[0], target.at[pl.ds(0, rows)])]
        places = [(rows, half), (3 * rows, half), (2 * rows, quarter), (2 * rows + quarter, quarter)]
        for n, (first, size) in enumerate(places):
            for m, holder in enumerate((core, 1 - core)):
                there = pl.ds(pl.multiple_of(first + holder * half, 16), size)
                copies.append(self.start(pieces[1 + 2 * n + m], target.at[there]))
        return copies


def project_kernel(slots, count, rows, shard, width, text_dev, scalars, gain, *refs):
    refs = list(refs)
    take = lambda n: [refs.pop(0) for _ in range(n)]
    packets = take(count)
    mod_in = take(9)
    w_in = take(5)
    q_all, k_all, v_all, k_t, raw_q, raw_k, text, text_t, w_keep, w_give = take(10)
    w_all, mod_all, sems = take(3)
    inner = slots * HD
    core = scalars[0]
    copies = Copies(sems)
    w_copies = copies.weights(scalars, w_in, w_all, shard)
    row_copies = copies.rows(core, mod_in, mod_all, rows)

    lanes = packets[0].shape[1]
    shift = lax.rem(lanes - scalars[5] * HD, lanes)
    for part in range(2):
        found = [
            pltpu.roll(one[part * text_dev : (part + 1) * text_dev, :], shift, 1) for one in packets
        ]
        found = jnp.concatenate(found, axis=0)
        for i in range(slots):
            one = found[:, i * HD : (i + 1) * HD]
            text[part, i] = one.astype(jnp.bfloat16)
            if part == 0:
                text_t[i] = one.T.astype(jnp.bfloat16)

    gain_q = gain[0:1, :]
    gain_k = gain[1:2, :]
    score_scale = HD ** (-0.5)
    for copy in w_copies + row_copies:
        copy.wait()
    half = width // 2
    columns = w_keep.shape[1]
    w_keep[...] = w_all[pl.ds(pl.multiple_of(core * half, 16), half), :columns]
    w_give[...] = w_all[pl.ds(pl.multiple_of((1 - core) * half, 16), half), :columns]
    span = 2 * rows
    for b in range(count // 2):
        here = slice(b * span, (b + 1) * span)
        projected = jnp.dot(
            mod_all[here, :], w_all[:, : 3 * inner], preferred_element_type=jnp.float32
        )
        for i in range(slots):
            query = projected[:, i * HD : (i + 1) * HD]
            key = projected[:, inner + i * HD : inner + (i + 1) * HD]
            value = projected[:, 2 * inner + i * HD : 2 * inner + (i + 1) * HD]
            raw_q[i, here, :] = query
            raw_k[i, here, :] = key
            query = query * inverse_rms(query) * gain_q
            q_all[i, here, :] = (query * score_scale).astype(jnp.bfloat16)
            key = key * inverse_rms(key) * gain_k
            k_all[i, here, :] = key.astype(jnp.bfloat16)
            k_t[i, :, here] = key.T.astype(jnp.bfloat16)
            v_all[i, here, :] = value.astype(jnp.bfloat16)


def attend_kernel(slots, count, rows, shard, width, text_dev, scalars, gain, *refs):
    refs = list(refs)
    take = lambda n: [refs.pop(0) for _ in range(n)]
    projected = take(8)
    cot_in = take(9)
    w_in = take(5)
    first_out, rest_out = take(2)
    w_all, cot_all, sems = take(3)
    d_all, grad_k, grad_v, back_q, stacked = take(5)
    q_all, k_all, v_all, k_t, raw_q, raw_k, text, text_t = refs
    inner = slots * HD
    tokens = rows * count
    core = scalars[0]
    copies = Copies(sems)
    w_copies = copies.weights(scalars, w_in, w_all, shard)
    row_copies = copies.rows(core, cot_in, cot_all, rows)
    local_copies = [copies.start(*one) for one in zip(projected, refs)]
    gain_q = gain[0:1, :]
    gain_k = gain[1:2, :]
    score_scale = HD ** (-0.5)
    span = 2 * rows

    text_rows = count * text_dev
    row = lax.broadcasted_iota(jnp.int32, (text_rows, span), 0)
    text_id = row
    for k in range(count):
        inside = (row >= k * text_dev) & (row < (k + 1) * text_dev)
        text_id = jnp.where(inside, row + (scalars[7 + k] - k) * text_dev, text_id)
    bias = jnp.where(text_id < scalars[6], 0.0, -1e30)

    for copy in w_copies + row_copies:
        copy.wait()
    for b in range(count // 2):
        here = slice(b * span, (b + 1) * span)
        out_grad = jnp.dot(
            cot_all[here, :], w_all[:, 3 * inner :], preferred_element_type=jnp.float32
        )
        for i in range(slots):
            d_all[i, here, :] = out_grad[:, i * HD : (i + 1) * HD].astype(jnp.bfloat16)

    grad_k[...] = jnp.zeros_like(grad_k)
    grad_v[...] = jnp.zeros_like(grad_v)
    if stacked.shape[1] > 3 * inner:
        stacked[:, 3 * inner :] = jnp.zeros((tokens, stacked.shape[1] - 3 * inner), jnp.float32)
    for copy in local_copies:
        copy.wait()

    @pl.loop(0, slots * (count // 2))
    def attend(t):
        i = t // (count // 2)
        here = pl.ds(pl.multiple_of(t % (count // 2) * span, span), span)
        query = q_all[i, here, :]
        grad = d_all[i, here, :]
        scores = dot(k_all[i], query, NT)
        text_scores = dot(text[0, i], query, NT) + bias
        col_max = jnp.maximum(
            jnp.max(scores, axis=0, keepdims=True), jnp.max(text_scores, axis=0, keepdims=True)
        )
        exps = jnp.exp(scores - col_max)
        text_exps = jnp.exp(text_scores - col_max)
        total = jnp.sum(exps, axis=0, keepdims=True) + jnp.sum(text_exps, axis=0, keepdims=True)
        inverse = 1.0 / total
        grad_w = dot(v_all[i], grad, NT)
        text_grad_w = dot(text[1, i], grad, NT)
        delta = inverse * (
            jnp.sum(exps * grad_w, axis=0, keepdims=True)
            + jnp.sum(text_exps * text_grad_w, axis=0, keepdims=True)
        )
        weights = exps * inverse
        grad_s = (weights * (grad_w - delta)).astype(jnp.bfloat16)
        text_grad_s = (text_exps * inverse * (text_grad_w - delta)).astype(jnp.bfloat16)
        grad_k[i] += dot(grad_s, query, NN)
        grad_v[i] += dot(weights.astype(jnp.bfloat16), grad, NN)
        grad_q = dot(k_t[i], grad_s, NN) + dot(text_t[i], text_grad_s, NN)
        grad_q = (grad_q.T * score_scale).astype(jnp.bfloat16)
        back_q[i, here, :] = norm_backward(raw_q[i, here, :], grad_q, gain_q)

    for i in range(slots):
        valid = scalars[7 + count + i] > 0
        back_k = norm_backward(raw_k[i], grad_k[i].astype(jnp.bfloat16), gain_k)
        stacked[:, i * HD : (i + 1) * HD] = jnp.where(valid, back_q[i], 0.0)
        stacked[:, inner + i * HD : inner + (i + 1) * HD] = jnp.where(valid, back_k, 0.0)
        stacked[:, 2 * inner + i * HD : 2 * inner + (i + 1) * HD] = jnp.where(valid, grad_v[i], 0.0)
    first_out[...] = stacked[rows : 2 * rows, :].astype(jnp.bfloat16)
    rest_out[: (count - 2) * rows, :] = stacked[2 * rows :, :].astype(jnp.bfloat16)
    rest_out[(count - 2) * rows :, :] = stacked[:rows, :].astype(jnp.bfloat16)


def project_call(scalars, gain, packets, mod, weights, slots, rows, text_dev):
    count = len(packets)
    shard = weights[0].shape[0]
    columns = 4 * slots * HD
    width = mod[0].shape[1]
    tokens = rows * count
    text_rows = text_dev * count
    f32, bf16 = jnp.float32, jnp.bfloat16
    vmem, hbm = spec(pltpu.VMEM), spec(pl.ANY)
    by_token = (slots, tokens, HD)
    shapes = [(by_token, bf16)] * 3 + [((slots, HD, tokens), bf16)] + [(by_token, f32)] * 2
    shapes += [((2, slots, text_rows, HD), bf16), ((slots, HD, text_rows), bf16)]
    shapes += [((width // 2, whole_tiles(3 * slots * HD)), bf16)] * 2
    return pl.pallas_call(
        functools.partial(project_kernel, slots, count, rows, shard, width, text_dev),
        out_shape=tuple(jax.ShapeDtypeStruct(*one) for one in shapes),
        in_specs=[spec(pltpu.SMEM), vmem] + [vmem] * count + [hbm] * (len(mod) + len(weights)),
        out_specs=(vmem,) * len(shapes),
        scratch_shapes=[
            pltpu.VMEM((width, columns), bf16),
            pltpu.VMEM((tokens, width), bf16),
            pltpu.SemaphoreType.DMA((len(mod) + len(weights),)),
        ],
        compiler_params=pltpu.CompilerParams(vmem_limit_bytes=GRANT),
        cost_estimate=pl.CostEstimate(
            flops=2 * tokens * width * 3 * slots * HD,
            bytes_accessed=2 * (tokens * width + columns * width) + 4 * tokens * columns,
            transcendentals=0,
        ),
    )(scalars, gain, *packets, *mod, *weights)


def attend_call(scalars, gain, operands, cot, weights, slots, rows, text_dev):
    count = operands[0].shape[1] // rows
    shard, columns = weights[0].shape
    width = cot[0].shape[1]
    tokens = rows * count
    inner = slots * HD
    f32, bf16 = jnp.float32, jnp.bfloat16
    vmem, hbm = spec(pltpu.VMEM), spec(pl.ANY)
    stacked = whole_tiles(3 * inner)
    shapes = [((rows, stacked), bf16), ((tokens - rows, stacked), bf16)]
    return pl.pallas_call(
        functools.partial(attend_kernel, slots, count, rows, shard, width, text_dev),
        out_shape=tuple(jax.ShapeDtypeStruct(*one) for one in shapes),
        in_specs=[spec(pltpu.SMEM), vmem] + [hbm] * (len(operands) + len(cot) + len(weights)),
        out_specs=(vmem,) * len(shapes),
        scratch_shapes=[
            pltpu.VMEM((width, columns), bf16),
            pltpu.VMEM((tokens, width), bf16),
            pltpu.SemaphoreType.DMA((len(operands) + len(cot) + len(weights),)),
            pltpu.VMEM((slots, tokens, HD), bf16),
        ]
        + [pltpu.VMEM((slots, tokens, HD), f32)] * 3
        + [pltpu.VMEM((tokens, stacked), f32)]
        + [pltpu.VMEM(one.shape, one.dtype) for one in operands],
        compiler_params=pltpu.CompilerParams(vmem_limit_bytes=GRANT),
        cost_estimate=pl.CostEstimate(
            flops=2 * tokens * width * inner + 10 * tokens * tokens * inner,
            bytes_accessed=2 * (tokens * width + columns * width),
            transcendentals=slots * tokens * tokens,
        ),
    )(scalars, gain, *operands, *cot, *weights)


def backward_kernel(own, other, w_own, w_other, *outs):
    total = dot(own[...], w_own[...], NT) + dot(other[...], w_other[...], NT)
    part = outs[0].shape[0]
    for n, out in enumerate(outs):
        out[...] = total[n * part : (n + 1) * part].astype(out.dtype)


def backward_call(own, other, w_own, w_other, part, dtype):
    rows, inner = own.shape
    half = w_own.shape[0]
    vmem = spec(pltpu.VMEM)
    return pl.pallas_call(
        backward_kernel,
        out_shape=(jax.ShapeDtypeStruct((part, half), dtype),) * (rows // part),
        in_specs=[vmem] * 4,
        out_specs=(vmem,) * (rows // part),
        compiler_params=pltpu.CompilerParams(vmem_limit_bytes=SMALL_GRANT),
        cost_estimate=pl.CostEstimate(
            flops=4 * rows * half * inner,
            bytes_accessed=4 * (rows + half) * inner + 4 * rows * half,
            transcendentals=0,
        ),
    )(own, other, w_own, w_other)


def sums_kernel(own_near, own_far, near, far, scale, normed, grad_out, sums_out):
    half = near.shape[0]
    for part, (own, moving) in enumerate(((own_near, near), (own_far, far))):
        here = slice(part * half, (part + 1) * half)
        grad = (own[...] + moving[...].astype(jnp.float32)) * scale[...]
        grad_out[here, :] = grad
        first = jnp.sum(grad, axis=-1, keepdims=True)
        second = jnp.sum(grad * normed[here, :], axis=-1, keepdims=True)
        lane = lax.broadcasted_iota(jnp.int32, (half, 128), 1)
        sums_out[here, :] = jnp.where(lane == 0, first, second)


def last_kernel(width, grad, sums, other, normed, base, inv_std, out):
    total = (sums[...] + other[...]) * (1.0 / width)
    rows = base[...] + inv_std[:, 0:1] * (
        grad[...] - total[:, 0:1] - normed[...] * total[:, 1:2]
    )
    out[...] = rows.T


def local_call(kernel, shapes, scalar_count, *operands):
    vmem = spec(pltpu.VMEM)
    return pl.pallas_call(
        kernel,
        out_shape=tuple(jax.ShapeDtypeStruct(*one) for one in shapes),
        in_specs=[spec(pltpu.SMEM)] * scalar_count + [vmem] * (len(operands) - scalar_count),
        out_specs=(vmem,) * len(shapes),
        compiler_params=pltpu.CompilerParams(vmem_limit_bytes=SMALL_GRANT),
        cost_estimate=pl.CostEstimate(
            flops=sum(one.size for one in operands),
            bytes_accessed=sum(one.size * one.dtype.itemsize for one in operands),
            transcendentals=0,
        ),
    )(*operands)


def shards_by_head(states, adjoint, text_kv, text_len, step_index, modulation, w_qkv, qk_gain, w_out):
    hidden_state = states[0]
    adjoint_rows = adjoint[0]
    tok_count, model_width = hidden_state.shape
    seq_count = lax.axis_size("seq")
    inner_dev = w_qkv.shape[2]
    heads_dev = inner_dev // HD
    shard = w_qkv.shape[0]
    slots = -(-heads_dev // seq_count)
    inner = slots * HD
    half_rows = tok_count // 2
    half_width = model_width // 2
    f32, bf16 = jnp.float32, jnp.bfloat16
    core = lax.axis_index("head").astype(jnp.int32)
    seq_index = lax.axis_index("seq")
    dp_index = lax.axis_index("dp")
    pin = lax.optimization_barrier

    seq_order = line_ring(seq_count)
    seq_place = ring_place(seq_order, seq_index)
    seq_next = ring_pairs(seq_order)
    swap = [(0, 1), (1, 0)]
    along_x = [(p, p ^ 1) for p in range(4)]
    along_y = [(p, p ^ 2) for p in range(4)]

    first = seq_index * heads_dev // seq_count
    stop = (seq_index + 1) * heads_dev // seq_count
    window = jnp.minimum(first, heads_dev - slots)
    valid = [(window + i >= first) & (window + i < stop) for i in range(slots)]
    owners = [ring_member(seq_order, (seq_place - k + seq_count) % seq_count) for k in range(seq_count)]
    w_index = [dp_index, dp_index ^ 1, dp_index ^ 2, dp_index ^ 3]
    scalars = [core] + w_index + [window, text_len[0]] + owners + valid
    scalars = jnp.stack([one.astype(jnp.int32) for one in scalars])

    def step(moving):
        return lax.ppermute(moving, "seq", seq_next)

    def other_core(moving):
        return lax.ppermute(moving, "head", swap)

    def step_back(moving):
        return lax.ppermute(moving, "seq", [(b, a) for a, b in seq_next])

    quarter = half_rows // 2

    def spread(moving):
        return [step(moving), step_back(moving)]

    def pass_on(received):
        return [step(received[0][:quarter]), step_back(received[1][quarter:])]

    mod_half, table_rows = first_call(step_index, core[None], hidden_state, modulation.transpose(1, 0, 2))
    mod_near = spread(mod_half)

    w_qkv, w_out, mod_half = pin((w_qkv, w_out, mod_half))
    take = lambda c: lax.dynamic_slice(w_qkv, (0, c, window * HD), (shard, 1, inner))[:, 0]
    own_w = jnp.concatenate(
        [take(0), take(1), take(2), lax.dynamic_slice_in_dim(w_out, window * HD, inner, 0).T], axis=1
    )
    own_w, mod_near[0] = pin((own_w, mod_near[0]))
    w_x = lax.ppermute(own_w, "dp", along_x)
    w_y = lax.ppermute(own_w, "dp", along_y)

    adjoint_rows, text_local, own_w = pin((adjoint_rows, text_kv[0], own_w))
    squares = jnp.sum(adjoint_rows * adjoint_rows)
    squares, mod_near[1] = pin((squares, mod_near[1]))
    text_dev = text_local.shape[0]
    text_local = text_local.transpose(1, 0, 2).reshape(2 * text_dev, inner_dev).astype(f32)
    packet = jnp.concatenate([text_local, jnp.full((8, inner_dev), squares)], axis=0)
    packets = [packet]
    for k in range(1, seq_count):
        pairs = [(seq_order[i], seq_order[(i + k) % seq_count]) for i in range(seq_count)]
        packets.append(lax.ppermute(packet, "seq", pairs))
    mod_far = pass_on(mod_near)
    *packets, mod_near[0], mod_near[1] = pin((*packets, *mod_near))
    clip_limit = 0.5 * (tok_count * seq_count * model_width) ** 0.5
    cotangent, cot_half, base = local_call(
        functools.partial(cotangent_kernel, clip_limit, 2 * text_dev),
        [((tok_count, model_width), bf16), ((half_rows, model_width), bf16), ((tok_count, half_width), f32)],
        1,
        core[None],
        adjoint_rows,
        table_rows,
        *packets,
    )

    cot_half, mod_far[0] = pin((cot_half, mod_far[0]))
    cot_near = spread(cot_half)
    modulated, normed_share, scale_share, inv_std = local_call(
        modulate_kernel,
        [
            ((tok_count, model_width), bf16),
            ((tok_count, half_width), f32),
            ((1, half_width), f32),
            ((tok_count, 128), f32),
        ],
        1,
        core[None],
        hidden_state,
        table_rows,
    )
    w_x, w_y, modulated = pin((w_x, w_y, modulated))
    w_diagonal = [
        lax.ppermute(w_x[: shard // 2], "dp", along_y),
        lax.ppermute(w_y[shard // 2 :], "dp", along_x),
    ]
    *cot_near, modulated = pin((*cot_near, modulated))
    cot_far = pass_on(cot_near)

    def pieces(own, received):
        return [own] + [one for moved in received for one in (moved, other_core(moved))]

    weights = [own_w, w_x, w_y] + w_diagonal
    mod_pieces, cot_pieces = pieces(modulated, mod_near + mod_far), pieces(cotangent, cot_near)
    *cot_pieces, mod_pieces[-1] = pin((*cot_pieces, mod_pieces[-1]))
    *operands, w_keep, w_give = project_call(
        scalars, qk_gain, packets, mod_pieces, weights, slots, tok_count, text_dev
    )
    w_give, cot_far[0], cot_far[1] = pin((w_give, *cot_far))
    cot_pieces += pieces(None, cot_far)[1:]
    w_give, *cot_pieces = pin((w_give, *cot_pieces))
    w_other = other_core(w_give)
    first, rest = attend_call(
        scalars, qk_gain, operands, cot_pieces, weights, slots, tok_count, text_dev
    )
    other_first, other_rest = other_core(first), other_core(rest)
    moving = backward_call(first, other_first, w_keep, w_other, half_rows, bf16)
    rest, other_rest, *moving = pin((rest, other_rest, *moving))
    own = backward_call(rest, other_rest, w_keep, w_other, half_rows, f32)
    for j in range(2, seq_count):
        moving = [step(part) for part in moving]
        moving = [
            (a + b.astype(f32)).astype(bf16) for a, b in zip(own[2 * (j - 2) : 2 * (j - 1)], moving)
        ]
    moving = [step(part) for part in moving]

    grad_scaled, sums = local_call(
        sums_kernel,
        [((tok_count, half_width), f32), ((tok_count, 128), f32)],
        0,
        *own[-2:],
        *moving,
        scale_share,
        normed_share,
    )
    (pulled,) = local_call(
        functools.partial(last_kernel, model_width),
        [((half_width, tok_count), f32)],
        0,
        grad_scaled,
        sums,
        other_core(sums),
        normed_share,
        base,
        inv_std,
    )
    return pulled.T[None]


def qk_normalize(values, gains):
    inverse = lax.rsqrt(jnp.mean(values * values, axis=-1, keepdims=True) + 1e-06)
    return ((values * inverse * gains).astype(jnp.bfloat16), inverse)


def qk_backward(values, inverse, cotangent, gains):
    scaled = cotangent.astype(jnp.float32) * gains
    return (
        scaled * inverse - values * jnp.mean(scaled * values, axis=-1, keepdims=True) * inverse**3
    )


def shards_by_row(states, adjoint, text_kv, text_len, step_index, modulation, w_qkv, qk_gain, w_out):
    hidden_state = states[0]
    adjoint_rows = adjoint[0]
    tok_count, model_width = hidden_state.shape
    seq_count = lax.axis_size("seq")
    inner_dev = w_qkv.shape[2]
    heads_dev = inner_dev // HD
    score_scale = HD ** (-0.5)
    squares = lax.psum(jnp.sum(adjoint_rows * adjoint_rows), "seq")
    clip_limit = 0.5 * (tok_count * seq_count * model_width) ** 0.5
    clip_scale = jnp.minimum(1.0, clip_limit / jnp.sqrt(squares + 1e-06))
    table_row = lax.dynamic_index_in_dim(modulation, step_index[0], 0, keepdims=False)
    offset_row = table_row[0]
    stretch = table_row[1]
    gating = table_row[2]
    widened = hidden_state.astype(jnp.float32)
    centered = widened - jnp.mean(widened, axis=-1, keepdims=True)
    inv_std = lax.rsqrt(jnp.mean(centered * centered, axis=-1, keepdims=True) + 1e-06)
    normed = centered * inv_std
    modulated = (normed * (1.0 + stretch) + offset_row).astype(jnp.bfloat16)
    cotangent = (gating * (clip_scale * adjoint_rows)).astype(jnp.bfloat16)
    contract_last = (((1,), (1,)), ((), ()))
    full_weight = lax.all_gather(w_qkv, "dp", axis=0, tiled=True).reshape(
        model_width, 3 * inner_dev
    )
    projected = jnp.dot(modulated, full_weight, preferred_element_type=jnp.float32)
    out_raw = lax.dot_general(
        cotangent,
        lax.all_gather(w_out, "dp", axis=1, tiled=True),
        contract_last,
        preferred_element_type=jnp.float32,
    )
    projected = projected.reshape(tok_count, 3, heads_dev, HD)
    queries, query_inv = qk_normalize(projected[:, 0], qk_gain[0])
    own_keys, key_inv = qk_normalize(projected[:, 1], qk_gain[1])
    own_values = projected[:, 2].astype(jnp.bfloat16)
    out_grad = out_raw.astype(jnp.bfloat16).reshape(tok_count, heads_dev, HD)
    text_keys = text_kv[0, :, 0, :]
    text_values = text_kv[0, :, 1, :]
    text_dev = text_keys.shape[0]
    rows_dev = tok_count + text_dev
    key_local = jnp.concatenate([own_keys.reshape(tok_count, inner_dev), text_keys], axis=0)
    value_local = jnp.concatenate([own_values.reshape(tok_count, inner_dev), text_values], axis=0)
    key_all, value_all = (
        lax.all_gather(key_local, "seq", axis=0, tiled=True),
        lax.all_gather(value_local, "seq", axis=0, tiled=True),
    )
    all_rows = rows_dev * seq_count
    row_ids = jnp.arange(all_rows, dtype=jnp.int32)
    owner = row_ids // rows_dev
    within = row_ids % rows_dev
    allowed = (within < tok_count) | (owner * text_dev + within - tok_count < text_len[0])
    group = 1
    while group * 2 * rows_dev <= 512 and seq_count % (group * 2) == 0:
        group = group * 2
    block_rows = group * rows_dev
    block_count = all_rows // block_rows
    key_blocks = key_all.reshape(block_count, block_rows, heads_dev, HD)
    value_blocks = value_all.reshape(block_count, block_rows, heads_dev, HD)
    mask_blocks = allowed.reshape(block_count, block_rows)

    def block_scores(key_block, mask_block):
        scores = (
            jnp.einsum("qhd,khd->qhk", queries, key_block, preferred_element_type=jnp.float32)
            * score_scale
        )
        return jnp.where(mask_block[None, None, :], scores, -1e30)

    def first_pass(carry, block):
        row_max, row_sum, row_dot = carry
        key_block, value_block, mask_block = block
        scores = block_scores(key_block, mask_block)
        new_max = jnp.maximum(row_max, jnp.max(scores, axis=-1))
        rescale = jnp.exp(row_max - new_max)
        exps = jnp.exp(scores - new_max[:, :, None])
        grad_weights = jnp.einsum(
            "qhd,khd->qhk", out_grad, value_block, preferred_element_type=jnp.float32
        )
        return (
            (
                new_max,
                row_sum * rescale + jnp.sum(exps, axis=-1),
                row_dot * rescale + jnp.sum(exps * grad_weights, axis=-1),
            ),
            None,
        )

    start_state = (
        jnp.full((tok_count, heads_dev), -1e30, jnp.float32),
        jnp.zeros((tok_count, heads_dev), jnp.float32),
        jnp.zeros((tok_count, heads_dev), jnp.float32),
    )
    (row_max, row_sum, row_dot), unused = lax.scan(
        first_pass, start_state, (key_blocks, value_blocks, mask_blocks)
    )
    log_total = row_max + jnp.log(row_sum)
    delta_row = row_dot / row_sum

    def second_pass(running, block):
        key_block, value_block, mask_block = block
        weights = jnp.exp(block_scores(key_block, mask_block) - log_total[:, :, None])
        grad_weights = jnp.einsum(
            "qhd,khd->qhk", out_grad, value_block, preferred_element_type=jnp.float32
        )
        grad_scores = (weights * (grad_weights - delta_row[:, :, None])).astype(jnp.bfloat16)
        return (
            running
            + jnp.einsum(
                "qhk,khd->qhd", grad_scores, key_block, preferred_element_type=jnp.float32
            ),
            None,
        )

    query_sum, unused = lax.scan(
        second_pass,
        jnp.zeros((tok_count, heads_dev, HD), jnp.float32),
        (key_blocks, value_blocks, mask_blocks),
    )
    grad_query = (query_sum * score_scale).astype(jnp.bfloat16)
    log_all, delta_all = (
        lax.all_gather(log_total, "seq", axis=0, tiled=True),
        lax.all_gather(delta_row, "seq", axis=0, tiled=True),
    )
    local_ids = jnp.arange(rows_dev, dtype=jnp.int32)
    local_allowed = (local_ids < tok_count) | (
        lax.axis_index("seq") * text_dev + local_ids - tok_count < text_len[0]
    )
    key_three = key_local.reshape(rows_dev, heads_dev, HD)
    value_three = value_local.reshape(rows_dev, heads_dev, HD)
    query_piece = lax.all_gather(queries.reshape(tok_count, inner_dev), "seq", axis=0, tiled=True)
    grad_piece = lax.all_gather(out_grad.reshape(tok_count, inner_dev), "seq", axis=0, tiled=True)
    piece_rows = query_piece.shape[0]
    query_rows = query_piece.reshape(piece_rows, heads_dev, HD)
    grad_rows = grad_piece.reshape(piece_rows, heads_dev, HD)
    scores = (
        jnp.einsum("qhd,khd->qhk", query_rows, key_three, preferred_element_type=jnp.float32)
        * score_scale
    )
    scores = jnp.where(local_allowed[None, None, :], scores, -1e30)
    weights = jnp.exp(scores - log_all[:, :, None])
    grad_weights = jnp.einsum(
        "qhd,khd->qhk", grad_rows, value_three, preferred_element_type=jnp.float32
    )
    grad_scores = (weights * (grad_weights - delta_all[:, :, None])).astype(jnp.bfloat16)
    rounded = weights.astype(jnp.bfloat16)
    key_sum = jnp.einsum(
        "qhk,qhd->khd", grad_scores, query_rows, preferred_element_type=jnp.float32
    )
    value_sum = jnp.einsum("qhk,qhd->khd", rounded, grad_rows, preferred_element_type=jnp.float32)
    key_sum, value_sum = (key_sum, value_sum)
    grad_key = (key_sum[:tok_count] * score_scale).astype(jnp.bfloat16)
    grad_value = value_sum[:tok_count].astype(jnp.bfloat16)
    raw_query = qk_backward(projected[:, 0], query_inv, grad_query, qk_gain[0])
    raw_key = qk_backward(projected[:, 1], key_inv, grad_key, qk_gain[1])
    stacked = jnp.stack([raw_query, raw_key, grad_value.astype(jnp.float32)], axis=1).astype(
        jnp.bfloat16
    )
    stacked = stacked.reshape(tok_count, 3 * inner_dev)
    partial_grad = lax.dot_general(
        stacked, full_weight, contract_last, preferred_element_type=jnp.float32
    )
    half_width = model_width // lax.axis_size("head")
    first_col = lax.axis_index("head") * half_width
    grad_share = lax.psum_scatter(
        partial_grad.astype(jnp.bfloat16), "head", scatter_dimension=1, tiled=True
    ).astype(jnp.float32)
    normed_share = lax.dynamic_slice_in_dim(normed, first_col, half_width, 1)
    stretch_share = lax.dynamic_slice_in_dim(stretch, first_col, half_width, 0)
    adjoint_share = lax.dynamic_slice_in_dim(adjoint_rows, first_col, half_width, 1)
    grad_scaled = grad_share * (1.0 + stretch_share)
    row_sums = jnp.stack(
        [jnp.sum(grad_scaled, axis=-1), jnp.sum(grad_scaled * normed_share, axis=-1)], axis=-1
    )
    row_sums = lax.psum(row_sums, "head")
    grad_state = inv_std * (
        grad_scaled - row_sums[:, 0:1] / model_width - normed_share * row_sums[:, 1:2] / model_width
    )
    pulled = clip_scale * adjoint_share + grad_state
    return pulled[None]


def solution(mesh):
    in_specs = (
        P("dp", "seq", None),
        P("dp", "seq", None),
        P("dp", "seq", None, "head"),
        P("dp"),
        P("dp"),
        P(),
        P("dp", None, "head"),
        P(),
        P("head", "dp"),
    )
    out_specs = P("dp", "seq", "head")
    by_head = mesh.shape["seq"] == 4 and mesh.shape["dp"] == 4 and mesh.shape["head"] == 2
    shards = shards_by_head if by_head else shards_by_row
    return jax.shard_map(shards, mesh=mesh, in_specs=in_specs, out_specs=out_specs, check_vma=False)
```

```python
import functools

import jax
import jax.numpy as jnp
from jax import lax
from jax.experimental import pallas as pl
from jax.experimental.pallas import tpu as pltpu
from jax.sharding import PartitionSpec as P

HD = 64
GRANT = 60 * 1024 * 1024
SMALL_GRANT = 24 * 1024 * 1024
EXTRA = 128
NT = (((1,), (1,)), ((), ()))
NN = (((1,), (0,)), ((), ()))


def line_ring(count):
    return [0] + list(range(1, count, 2)) + [i for i in range(count - 1, 0, -1) if i % 2 == 0]


def ring_pairs(order):
    return [(order[i], order[(i + 1) % len(order)]) for i in range(len(order))]


def ring_place(order, index):
    place = jnp.int32(0)
    for position, member in enumerate(order):
        place = jnp.where(index == member, jnp.int32(position), place)
    return place


def ring_member(order, place):
    member = jnp.int32(order[0])
    for position, value in enumerate(order):
        member = jnp.where(place == position, jnp.int32(value), member)
    return member


def dot(a, b, dims):
    return lax.dot_general(a, b, dims, preferred_element_type=jnp.float32)


def inverse_rms(raw):
    return lax.rsqrt(jnp.mean(raw * raw, axis=-1, keepdims=True) + 1e-06)


def norm_backward(raw, cotangent, gains):
    inverse = inverse_rms(raw)
    scaled = cotangent.astype(jnp.float32) * gains
    return (
        scaled * inverse
        - raw * jnp.mean(scaled * raw, axis=-1, keepdims=True) * (inverse * inverse * inverse)
    )


def whole_tiles(columns):
    return -(-columns // 128) * 128


def spec(space):
    return pl.BlockSpec(memory_space=space)


def text_columns(text, part):
    rows = text[...].astype(jnp.float32)[:, part, :]
    return [rows[:, c * EXTRA : (c + 1) * EXTRA] for c in range(rows.shape[1] // EXTRA)]


def extra_columns(blocks, rows):
    filled = sum(one.shape[0] for one in blocks)
    blocks = blocks + [jnp.zeros((rows - filled, EXTRA), jnp.float32)]
    return jnp.concatenate(blocks, axis=0).astype(jnp.bfloat16)


def first_kernel(step, core, states, table, adjoint, text, out, rows_out, extra_out):
    rows = [table[c, pl.ds(step[0], 1), :] for c in range(3)]
    widened = states[...].astype(jnp.float32)
    centered = widened - jnp.mean(widened, axis=-1, keepdims=True)
    inv_std = lax.rsqrt(jnp.mean(centered * centered, axis=-1, keepdims=True) + 1e-06)
    half, width = states.shape
    out[:, :width] = (centered * inv_std * (1.0 + rows[1]) + rows[0]).astype(jnp.bfloat16)
    for c in range(3):
        rows_out[c : c + 1, :] = rows[c]
    squares = jnp.sum(adjoint[...] * adjoint[...], axis=0, keepdims=True)
    squares = jnp.sum(squares, axis=1, keepdims=True)
    terms = []
    for n in range(3):
        terms.append(squares.astype(jnp.bfloat16).astype(jnp.float32))
        squares = squares - terms[-1]
    lane = lax.broadcasted_iota(jnp.int32, (8, EXTRA), 1)
    sums = jnp.where(lane == 0, terms[0], jnp.where(lane == 1, terms[1], jnp.where(lane == 2, terms[2], 0.0)))
    extra = extra_columns(text_columns(text, 0) + [sums], half)
    out[:, width:] = extra
    extra_out[...] = extra


def first_call(step, core, states, table, adjoint, text):
    rows, width = states.shape
    half = rows // 2
    whole = lambda *shape: pl.BlockSpec(shape, lambda i, step, core: (0,) * len(shape))
    return pl.pallas_call(
        first_kernel,
        out_shape=(
            jax.ShapeDtypeStruct((half, width + EXTRA), jnp.bfloat16),
            jax.ShapeDtypeStruct((8, width), jnp.float32),
            jax.ShapeDtypeStruct((half, EXTRA), jnp.bfloat16),
        ),
        grid_spec=pltpu.PrefetchScalarGridSpec(
            num_scalar_prefetch=2,
            grid=(1,),
            in_specs=[
                pl.BlockSpec((half, width), lambda i, step, core: (core[0], 0)),
                whole(*table.shape),
                whole(*adjoint.shape),
                whole(*text.shape),
            ],
            out_specs=(whole(half, width + EXTRA), whole(8, width), whole(half, EXTRA)),
        ),
        compiler_params=pltpu.CompilerParams(vmem_limit_bytes=GRANT),
        cost_estimate=pl.CostEstimate(flops=8 * half * width, bytes_accessed=16 * half * width, transcendentals=0),
    )(step, core, states, table, adjoint, text)


def pick_half(core, rows):
    half = rows.shape[1] // 2
    return jnp.where(core == 0, rows[:, :half], rows[:, half:])


def modulate_kernel(core, states, table_rows, extra, out, normed_out, stretch_out, inv_out):
    widened = states[...].astype(jnp.float32)
    centered = widened - jnp.mean(widened, axis=-1, keepdims=True)
    inv_std = lax.rsqrt(jnp.mean(centered * centered, axis=-1, keepdims=True) + 1e-06)
    normed = centered * inv_std
    scale = 1.0 + table_rows[1:2, :]
    rows, width = states.shape
    out[:, :width] = (normed * scale + table_rows[0:1, :]).astype(jnp.bfloat16)
    for n in range(2):
        out[n * rows // 2 : (n + 1) * rows // 2, width:] = extra[...]
    normed_out[...] = pick_half(core[0], normed)
    stretch_out[...] = pick_half(core[0], scale)
    inv_out[...] = jnp.broadcast_to(inv_std, inv_out.shape)


def cotangent_kernel(limit, core, adjoint, table_rows, text, extra, previous, following, opposite, out, half_out, base_out):
    quarter = opposite.shape[0]
    first = 2 * quarter - opposite.shape[0]
    row = 8 * (text.shape[2] // EXTRA)
    squares = None
    for terms in (extra[...], previous[...], following[...]):
        terms = terms.astype(jnp.float32)[row : row + 1, :]
        squares = terms if squares is None else squares + terms
    squares = squares + opposite[...].astype(jnp.float32)[row - first : row - first + 1, :]
    squares = jnp.sum(squares, axis=1, keepdims=True)
    clip_scale = jnp.minimum(1.0, limit / jnp.sqrt(squares + 1e-06))
    gating = table_rows[2:3, :]
    clipped = clip_scale * adjoint[...]
    rows, width = adjoint.shape
    half = rows // 2
    columns = extra_columns(text_columns(text, 1), half)
    out[:, :width] = (gating * clipped).astype(jnp.bfloat16)
    for n in range(2):
        out[n * half : (n + 1) * half, width:] = columns
    base_out[...] = pick_half(core[0], clipped)
    own = adjoint[pl.ds(pl.multiple_of(core[0] * half, 8), half), :]
    half_out[:, :width] = (gating * (clip_scale * own)).astype(jnp.bfloat16)
    half_out[:, width:] = columns


def cotangent_call(limit, core, adjoint, table_rows, text, extra, previous, following, opposite):
    rows, width = adjoint.shape
    bf16 = jnp.bfloat16
    block = width // EXTRA
    whole = lambda one: pl.BlockSpec(one.shape, lambda i, core: (0,) * one.ndim)
    tail = lambda one: pl.BlockSpec((one.shape[0], EXTRA), lambda i, core: (0, block))
    outs = (
        jax.ShapeDtypeStruct((rows, width + EXTRA), bf16),
        jax.ShapeDtypeStruct((rows // 2, width + EXTRA), bf16),
        jax.ShapeDtypeStruct((rows, width // 2), jnp.float32),
    )
    return pl.pallas_call(
        functools.partial(cotangent_kernel, limit),
        out_shape=outs,
        grid_spec=pltpu.PrefetchScalarGridSpec(
            num_scalar_prefetch=1,
            grid=(1,),
            in_specs=[whole(adjoint), whole(table_rows), whole(text), whole(extra)]
            + [tail(one) for one in (previous, following, opposite)],
            out_specs=tuple(whole(one) for one in outs),
        ),
        compiler_params=pltpu.CompilerParams(vmem_limit_bytes=SMALL_GRANT),
        cost_estimate=pl.CostEstimate(flops=4 * rows * width, bytes_accessed=12 * rows * width, transcendentals=0),
    )(core, adjoint, table_rows, text, extra, previous, following, opposite)


class Copies:
    def __init__(self, sems):
        self.sems = sems
        self.count = 0

    def start(self, source, target):
        copy = pltpu.make_async_copy(source, target, self.sems.at[self.count])
        copy.start()
        self.count += 1
        return copy

    def weights(self, scalars, w_in, w_all, shard, columns=None):
        half = shard // 2
        places = [
            (scalars[1] * shard, shard),
            (scalars[2] * shard, shard),
            (scalars[3] * shard, shard),
            (scalars[4] * shard, half),
            (scalars[4] * shard + half, half),
        ]
        return [
            self.start(
                piece if columns is None else piece.at[:, columns],
                w_all.at[pl.ds(pl.multiple_of(first, 16), size)],
            )
            for piece, (first, size) in zip(w_in, places)
        ]

    def rows(self, core, pieces, target, rows):
        half, quarter = rows // 2, rows // 4
        copies = [self.start(pieces[0], target.at[pl.ds(0, rows)])]
        places = [(rows, half), (3 * rows, half), (2 * rows, quarter), (2 * rows + quarter, quarter)]
        for n, (first, size) in enumerate(places):
            for m, holder in enumerate((core, 1 - core)):
                there = pl.ds(pl.multiple_of(first + holder * half, 16), size)
                copies.append(self.start(pieces[1 + 2 * n + m], target.at[there]))
        return copies


def window_heads(scalars, count, rows, text_dev, gathered, width, extra, text, text_t=None):
    half = rows // 2
    for k in range(count):
        there = pl.ds(pl.multiple_of(k * rows + scalars[0] * half, 16), half)
        extra[k] = gathered[there, width:].astype(jnp.float32)
    for i in range(text.shape[0]):
        head = scalars[5] + i
        first = pl.ds(pl.multiple_of(head // 2 * text_dev, 8), text_dev)
        found = jnp.concatenate([extra[k, first, :] for k in range(count)], axis=0)
        found = jnp.where(head % 2 == 0, found[:, :HD], found[:, HD:])
        text[i] = found.astype(jnp.bfloat16)
        if text_t is not None:
            text_t[i] = found.T.astype(jnp.bfloat16)


def project_kernel(slots, count, rows, shard, width, text_dev, scalars, gain, *refs):
    refs = list(refs)
    take = lambda n: [refs.pop(0) for _ in range(n)]
    mod_in = take(9)
    w_in = take(5)
    q_all, k_all, v_all, k_t, raw_q, raw_k, text, text_t, w_keep, w_give = take(10)
    w_all, mod_all, sems, extra = take(4)
    inner = slots * HD
    core = scalars[0]
    copies = Copies(sems)
    w_copies = copies.weights(scalars, w_in, w_all, shard)
    row_copies = copies.rows(core, mod_in, mod_all, rows)

    gain_q = gain[0:1, :]
    gain_k = gain[1:2, :]
    score_scale = HD ** (-0.5)
    for copy in w_copies + row_copies:
        copy.wait()
    half = width // 2
    window_heads(scalars, count, rows, text_dev, mod_all, width, extra, text, text_t)
    columns = w_keep.shape[1]
    w_keep[...] = w_all[pl.ds(pl.multiple_of(core * half, 16), half), :columns]
    w_give[...] = w_all[pl.ds(pl.multiple_of((1 - core) * half, 16), half), :columns]
    span = 2 * rows
    for b in range(count // 2):
        here = slice(b * span, (b + 1) * span)
        projected = jnp.dot(
            mod_all[here, :width], w_all[:, : 3 * inner], preferred_element_type=jnp.float32
        )
        for i in range(slots):
            query = projected[:, i * HD : (i + 1) * HD]
            key = projected[:, inner + i * HD : inner + (i + 1) * HD]
            value = projected[:, 2 * inner + i * HD : 2 * inner + (i + 1) * HD]
            raw_q[i, here, :] = query
            raw_k[i, here, :] = key
            query = query * inverse_rms(query) * gain_q
            q_all[i, here, :] = (query * score_scale).astype(jnp.bfloat16)
            key = key * inverse_rms(key) * gain_k
            k_all[i, here, :] = key.astype(jnp.bfloat16)
            k_t[i, :, here] = key.T.astype(jnp.bfloat16)
            v_all[i, here, :] = value.astype(jnp.bfloat16)


def attend_kernel(slots, count, rows, shard, width, text_dev, columns, scalars, gain, *refs):
    refs = list(refs)
    take = lambda n: [refs.pop(0) for _ in range(n)]
    projected = take(8)
    cot_in = take(9)
    w_in = take(5)
    first_out, rest_out = take(2)
    w_out, cot_all, sems, extra, values_text = take(5)
    d_all, back_q, back_k, back_v, stacked = take(5)
    q_all, k_all, v_all, k_t, raw_q, raw_k, text, text_t = refs
    inner = slots * HD
    tokens = rows * count
    core = scalars[0]
    copies = Copies(sems)
    w_copies = copies.weights(scalars, w_in, w_out, shard, columns)
    row_copies = copies.rows(core, cot_in, cot_all, rows)
    local_copies = [copies.start(*one) for one in zip(projected, refs)]
    gain_q = gain[0:1, :]
    gain_k = gain[1:2, :]
    score_scale = HD ** (-0.5)
    span = 2 * rows

    text_rows = count * text_dev
    row = lax.broadcasted_iota(jnp.int32, (text_rows, span), 0)
    text_id = row
    for k in range(count):
        inside = (row >= k * text_dev) & (row < (k + 1) * text_dev)
        text_id = jnp.where(inside, row + (scalars[7 + k] - k) * text_dev, text_id)
    bias = jnp.where(text_id < scalars[6], 0.0, -1e30)
    stacked[:, 3 * inner :] = jnp.zeros((tokens, stacked.shape[1] - 3 * inner), jnp.float32)

    for copy in w_copies + row_copies:
        copy.wait()
    window_heads(scalars, count, rows, text_dev, cot_all, width, extra, values_text)
    for b in range(count // 2):
        here = slice(b * span, (b + 1) * span)
        out_grad = jnp.dot(cot_all[here, :width], w_out[...], preferred_element_type=jnp.float32)
        out_grad = out_grad[:, out_grad.shape[1] - inner :]
        for i in range(slots):
            d_all[i, here, :] = out_grad[:, i * HD : (i + 1) * HD].astype(jnp.bfloat16)
    for copy in local_copies:
        copy.wait()

    @pl.loop(0, slots)
    def attend(i):
        grad_k, grad_v = 0.0, 0.0
        for b in range(count // 2):
            here = slice(b * span, (b + 1) * span)
            query = q_all[i, here, :]
            grad = d_all[i, here, :]
            scores = dot(k_all[i], query, NT)
            text_scores = dot(text[i], query, NT) + bias
            col_max = jnp.maximum(
                jnp.max(scores, axis=0, keepdims=True), jnp.max(text_scores, axis=0, keepdims=True)
            )
            exps = jnp.exp(scores - col_max)
            text_exps = jnp.exp(text_scores - col_max)
            total = jnp.sum(exps, axis=0, keepdims=True) + jnp.sum(text_exps, axis=0, keepdims=True)
            inverse = 1.0 / total
            grad_w = dot(v_all[i], grad, NT)
            text_grad_w = dot(values_text[i], grad, NT)
            delta = inverse * (
                jnp.sum(exps * grad_w, axis=0, keepdims=True)
                + jnp.sum(text_exps * text_grad_w, axis=0, keepdims=True)
            )
            weights = exps * inverse
            grad_s = (weights * (grad_w - delta)).astype(jnp.bfloat16)
            text_grad_s = (text_exps * inverse * (text_grad_w - delta)).astype(jnp.bfloat16)
            grad_k += dot(grad_s, query, NN)
            grad_v += dot(weights.astype(jnp.bfloat16), grad, NN)
            grad_q = dot(k_t[i], grad_s, NN) + dot(text_t[i], text_grad_s, NN)
            grad_q = (grad_q.T * score_scale).astype(jnp.bfloat16)
            back_q[i, here, :] = norm_backward(raw_q[i, here, :], grad_q, gain_q)
        back_k[i] = norm_backward(raw_k[i], grad_k.astype(jnp.bfloat16), gain_k)
        back_v[i] = grad_v

    for i in range(slots):
        valid = scalars[7 + count + i] > 0
        for n, part in enumerate((back_q, back_k, back_v)):
            there = n * inner + i * HD
            stacked[:, there : there + HD] = jnp.where(valid, part[i], 0.0)
    first_out[...] = stacked[rows : 2 * rows, :].astype(jnp.bfloat16)
    rest_out[: (count - 2) * rows, :] = stacked[2 * rows :, :].astype(jnp.bfloat16)
    rest_out[(count - 2) * rows :, :] = stacked[:rows, :].astype(jnp.bfloat16)


def project_call(scalars, gain, mod, weights, slots, rows, text_dev, count):
    shard = weights[0].shape[0]
    columns = 4 * slots * HD
    width = mod[0].shape[1] - EXTRA
    tokens = rows * count
    text_rows = text_dev * count
    f32, bf16 = jnp.float32, jnp.bfloat16
    vmem, hbm = spec(pltpu.VMEM), spec(pl.ANY)
    by_token = (slots, tokens, HD)
    shapes = [(by_token, bf16)] * 3 + [((slots, HD, tokens), bf16)] + [(by_token, f32)] * 2
    shapes += [((slots, text_rows, HD), bf16), ((slots, HD, text_rows), bf16)]
    shapes += [((width // 2, whole_tiles(3 * slots * HD)), bf16)] * 2
    return pl.pallas_call(
        functools.partial(project_kernel, slots, count, rows, shard, width, text_dev),
        out_shape=tuple(jax.ShapeDtypeStruct(*one) for one in shapes),
        in_specs=[spec(pltpu.SMEM), vmem] + [hbm] * (len(mod) + len(weights)),
        out_specs=(vmem,) * len(shapes),
        scratch_shapes=[
            pltpu.VMEM((width, columns), bf16),
            pltpu.VMEM((tokens, width + EXTRA), bf16),
            pltpu.SemaphoreType.DMA((len(mod) + len(weights),)),
            pltpu.VMEM((count, rows // 2, EXTRA), f32),
        ],
        compiler_params=pltpu.CompilerParams(vmem_limit_bytes=GRANT),
        cost_estimate=pl.CostEstimate(
            flops=2 * tokens * width * 3 * slots * HD,
            bytes_accessed=2 * (tokens * width + columns * width) + 4 * tokens * columns,
            transcendentals=0,
        ),
    )(scalars, gain, *mod, *weights)


def attend_call(scalars, gain, operands, cot, weights, slots, rows, text_dev):
    count = operands[0].shape[1] // rows
    shard, columns = weights[0].shape
    width = cot[0].shape[1] - EXTRA
    tokens = rows * count
    inner = slots * HD
    stacked = whole_tiles(3 * inner)
    first = 3 * inner // 128 * 128
    window = slice(first, columns)
    f32, bf16 = jnp.float32, jnp.bfloat16
    vmem, hbm = spec(pltpu.VMEM), spec(pl.ANY)
    by_token = (slots, tokens, HD)
    shapes = [((rows, stacked), bf16), ((tokens - rows, stacked), bf16)]
    return pl.pallas_call(
        functools.partial(attend_kernel, slots, count, rows, shard, width, text_dev, window),
        out_shape=tuple(jax.ShapeDtypeStruct(*one) for one in shapes),
        in_specs=[spec(pltpu.SMEM), vmem] + [hbm] * (len(operands) + len(cot) + len(weights)),
        out_specs=(vmem,) * len(shapes),
        scratch_shapes=[
            pltpu.VMEM((width, columns - first), bf16),
            pltpu.VMEM((tokens, width + EXTRA), bf16),
            pltpu.SemaphoreType.DMA((len(operands) + len(cot) + len(weights),)),
            pltpu.VMEM((count, rows // 2, EXTRA), f32),
            pltpu.VMEM((slots, text_dev * count, HD), bf16),
            pltpu.VMEM(by_token, bf16),
        ]
        + [pltpu.VMEM(by_token, f32)] * 3
        + [pltpu.VMEM((tokens, stacked), f32)]
        + [pltpu.VMEM(one.shape, one.dtype) for one in operands],
        compiler_params=pltpu.CompilerParams(vmem_limit_bytes=GRANT),
        cost_estimate=pl.CostEstimate(
            flops=2 * tokens * width * inner + 10 * tokens * tokens * inner,
            bytes_accessed=2 * (tokens * width + columns * width),
            transcendentals=slots * tokens * tokens,
        ),
    )(scalars, gain, *operands, *cot, *weights)


def backward_kernel(own, other, w_own, w_other, *outs):
    total = dot(own[...], w_own[...], NT) + dot(other[...], w_other[...], NT)
    part = outs[0].shape[0]
    for n, out in enumerate(outs):
        out[...] = total[n * part : (n + 1) * part].astype(out.dtype)


def backward_call(own, other, w_own, w_other, part, dtype):
    rows, inner = own.shape
    half = w_own.shape[0]
    vmem = spec(pltpu.VMEM)
    return pl.pallas_call(
        backward_kernel,
        out_shape=(jax.ShapeDtypeStruct((part, half), dtype),) * (rows // part),
        in_specs=[vmem] * 4,
        out_specs=(vmem,) * (rows // part),
        compiler_params=pltpu.CompilerParams(vmem_limit_bytes=SMALL_GRANT),
        cost_estimate=pl.CostEstimate(
            flops=4 * rows * half * inner,
            bytes_accessed=4 * (rows + half) * inner + 4 * rows * half,
            transcendentals=0,
        ),
    )(own, other, w_own, w_other)


def sums_kernel(own_near, own_far, near, far, scale, normed, grad_out, sums_out):
    half = near.shape[0]
    for part, (own, moving) in enumerate(((own_near, near), (own_far, far))):
        here = slice(part * half, (part + 1) * half)
        grad = (own[...] + moving[...].astype(jnp.float32)) * scale[...]
        grad_out[here, :] = grad
        first = jnp.sum(grad, axis=-1, keepdims=True)
        second = jnp.sum(grad * normed[here, :], axis=-1, keepdims=True)
        lane = lax.broadcasted_iota(jnp.int32, (half, 128), 1)
        sums_out[here, :] = jnp.where(lane == 0, first, second)


def last_kernel(width, grad, sums, other, normed, base, inv_std, out):
    total = (sums[...] + other[...]) * (1.0 / width)
    rows = base[...] + inv_std[:, 0:1] * (
        grad[...] - total[:, 0:1] - normed[...] * total[:, 1:2]
    )
    out[...] = rows.T


def local_call(kernel, shapes, scalar_count, *operands):
    vmem = spec(pltpu.VMEM)
    return pl.pallas_call(
        kernel,
        out_shape=tuple(jax.ShapeDtypeStruct(*one) for one in shapes),
        in_specs=[spec(pltpu.SMEM)] * scalar_count + [vmem] * (len(operands) - scalar_count),
        out_specs=(vmem,) * len(shapes),
        compiler_params=pltpu.CompilerParams(vmem_limit_bytes=SMALL_GRANT),
        cost_estimate=pl.CostEstimate(
            flops=sum(one.size for one in operands),
            bytes_accessed=sum(one.size * one.dtype.itemsize for one in operands),
            transcendentals=0,
        ),
    )(*operands)


def shards_by_head(states, adjoint, text_kv, text_len, step_index, modulation, w_qkv, qk_gain, w_out):
    hidden_state = states[0]
    adjoint_rows = adjoint[0]
    tok_count, model_width = hidden_state.shape
    seq_count = lax.axis_size("seq")
    inner_dev = w_qkv.shape[2]
    heads_dev = inner_dev // HD
    shard = w_qkv.shape[0]
    slots = -(-heads_dev // seq_count)
    inner = slots * HD
    half_rows = tok_count // 2
    half_width = model_width // 2
    f32, bf16 = jnp.float32, jnp.bfloat16
    core = lax.axis_index("head").astype(jnp.int32)
    seq_index = lax.axis_index("seq")
    dp_index = lax.axis_index("dp")
    pin = lax.optimization_barrier

    seq_order = line_ring(seq_count)
    seq_place = ring_place(seq_order, seq_index)
    seq_next = ring_pairs(seq_order)
    swap = [(0, 1), (1, 0)]
    along_x = [(p, p ^ 1) for p in range(4)]
    along_y = [(p, p ^ 2) for p in range(4)]

    first = seq_index * heads_dev // seq_count
    stop = (seq_index + 1) * heads_dev // seq_count
    window = jnp.minimum(first, heads_dev - slots)
    valid = [(window + i >= first) & (window + i < stop) for i in range(slots)]
    owners = [ring_member(seq_order, (seq_place - k + seq_count) % seq_count) for k in range(seq_count)]
    w_index = [dp_index, dp_index ^ 1, dp_index ^ 2, dp_index ^ 3]
    scalars = [core] + w_index + [window, text_len[0]] + owners + valid
    scalars = jnp.stack([one.astype(jnp.int32) for one in scalars])

    def step(moving):
        return lax.ppermute(moving, "seq", seq_next)

    def other_core(moving):
        return lax.ppermute(moving, "head", swap)

    def step_back(moving):
        return lax.ppermute(moving, "seq", [(b, a) for a, b in seq_next])

    quarter = half_rows // 2

    def spread(moving):
        return [step(moving), step_back(moving)]

    def pass_on(received):
        return [step(received[0][:quarter]), step_back(received[1][quarter:])]

    mod_half, table_rows, extra = first_call(
        step_index, core[None], hidden_state, modulation.transpose(1, 0, 2), adjoint_rows, text_kv[0]
    )
    mod_near = spread(mod_half)

    w_qkv, w_out, mod_half = pin((w_qkv, w_out, mod_half))
    take = lambda c: lax.dynamic_slice(w_qkv, (0, c, window * HD), (shard, 1, inner))[:, 0]
    own_w = jnp.concatenate(
        [take(0), take(1), take(2), lax.dynamic_slice_in_dim(w_out, window * HD, inner, 0).T], axis=1
    )
    w_x = lax.ppermute(own_w, "dp", along_x)
    w_y = lax.ppermute(own_w, "dp", along_y)

    text_dev = text_kv.shape[1]
    mod_far = pass_on(mod_near)
    clip_limit = 0.5 * (tok_count * seq_count * model_width) ** 0.5
    cotangent, cot_half, base = cotangent_call(
        clip_limit, core[None], adjoint_rows, table_rows, text_kv[0], extra, *mod_near, mod_far[1]
    )
    cot_near = spread(cot_half)
    modulated, normed_share, scale_share, inv_std = local_call(
        modulate_kernel,
        [
            ((tok_count, model_width + EXTRA), bf16),
            ((tok_count, half_width), f32),
            ((1, half_width), f32),
            ((tok_count, 128), f32),
        ],
        1,
        core[None],
        hidden_state,
        table_rows,
        extra,
    )
    def pieces(own, received):
        return [own] + [one for moved in received for one in (moved, other_core(moved))]

    mod_pieces = pieces(modulated, mod_near + mod_far)
    w_x, w_y, *mod_pieces = pin((w_x, w_y, *mod_pieces))
    w_diagonal = [
        lax.ppermute(w_x[: shard // 2], "dp", along_y),
        lax.ppermute(w_y[shard // 2 :], "dp", along_x),
    ]
    cot_far = pass_on(cot_near)

    weights = [own_w, w_x, w_y] + w_diagonal
    cot_pieces = pieces(cotangent, cot_near)
    *cot_pieces, mod_pieces[-1] = pin((*cot_pieces, mod_pieces[-1]))
    *operands, w_keep, w_give = project_call(
        scalars, qk_gain, mod_pieces, weights, slots, tok_count, text_dev, seq_count
    )
    w_give, cot_far[0], cot_far[1] = pin((w_give, *cot_far))
    cot_pieces += pieces(None, cot_far)[1:]
    w_give, *cot_pieces = pin((w_give, *cot_pieces))
    w_other = other_core(w_give)
    first, rest = attend_call(
        scalars, qk_gain, operands, cot_pieces, weights, slots, tok_count, text_dev
    )
    other_first, other_rest = other_core(first), other_core(rest)
    moving = backward_call(first, other_first, w_keep, w_other, half_rows, bf16)
    rest, other_rest, *moving = pin((rest, other_rest, *moving))
    own = backward_call(rest, other_rest, w_keep, w_other, half_rows, f32)
    for j in range(2, seq_count):
        moving = [step(part) for part in moving]
        moving = [
            (a + b.astype(f32)).astype(bf16) for a, b in zip(own[2 * (j - 2) : 2 * (j - 1)], moving)
        ]
    moving = [step(part) for part in moving]

    grad_scaled, sums = local_call(
        sums_kernel,
        [((tok_count, half_width), f32), ((tok_count, 128), f32)],
        0,
        *own[-2:],
        *moving,
        scale_share,
        normed_share,
    )
    (pulled,) = local_call(
        functools.partial(last_kernel, model_width),
        [((half_width, tok_count), f32)],
        0,
        grad_scaled,
        sums,
        other_core(sums),
        normed_share,
        base,
        inv_std,
    )
    return pulled.T[None]


def qk_normalize(values, gains):
    inverse = lax.rsqrt(jnp.mean(values * values, axis=-1, keepdims=True) + 1e-06)
    return ((values * inverse * gains).astype(jnp.bfloat16), inverse)


def qk_backward(values, inverse, cotangent, gains):
    scaled = cotangent.astype(jnp.float32) * gains
    return (
        scaled * inverse - values * jnp.mean(scaled * values, axis=-1, keepdims=True) * inverse**3
    )


def shards_by_row(states, adjoint, text_kv, text_len, step_index, modulation, w_qkv, qk_gain, w_out):
    hidden_state = states[0]
    adjoint_rows = adjoint[0]
    tok_count, model_width = hidden_state.shape
    seq_count = lax.axis_size("seq")
    inner_dev = w_qkv.shape[2]
    heads_dev = inner_dev // HD
    score_scale = HD ** (-0.5)
    squares = lax.psum(jnp.sum(adjoint_rows * adjoint_rows), "seq")
    clip_limit = 0.5 * (tok_count * seq_count * model_width) ** 0.5
    clip_scale = jnp.minimum(1.0, clip_limit / jnp.sqrt(squares + 1e-06))
    table_row = lax.dynamic_index_in_dim(modulation, step_index[0], 0, keepdims=False)
    offset_row = table_row[0]
    stretch = table_row[1]
    gating = table_row[2]
    widened = hidden_state.astype(jnp.float32)
    centered = widened - jnp.mean(widened, axis=-1, keepdims=True)
    inv_std = lax.rsqrt(jnp.mean(centered * centered, axis=-1, keepdims=True) + 1e-06)
    normed = centered * inv_std
    modulated = (normed * (1.0 + stretch) + offset_row).astype(jnp.bfloat16)
    cotangent = (gating * (clip_scale * adjoint_rows)).astype(jnp.bfloat16)
    contract_last = (((1,), (1,)), ((), ()))
    full_weight = lax.all_gather(w_qkv, "dp", axis=0, tiled=True).reshape(
        model_width, 3 * inner_dev
    )
    projected = jnp.dot(modulated, full_weight, preferred_element_type=jnp.float32)
    out_raw = lax.dot_general(
        cotangent,
        lax.all_gather(w_out, "dp", axis=1, tiled=True),
        contract_last,
        preferred_element_type=jnp.float32,
    )
    projected = projected.reshape(tok_count, 3, heads_dev, HD)
    queries, query_inv = qk_normalize(projected[:, 0], qk_gain[0])
    own_keys, key_inv = qk_normalize(projected[:, 1], qk_gain[1])
    own_values = projected[:, 2].astype(jnp.bfloat16)
    out_grad = out_raw.astype(jnp.bfloat16).reshape(tok_count, heads_dev, HD)
    text_keys = text_kv[0, :, 0, :]
    text_values = text_kv[0, :, 1, :]
    text_dev = text_keys.shape[0]
    rows_dev = tok_count + text_dev
    key_local = jnp.concatenate([own_keys.reshape(tok_count, inner_dev), text_keys], axis=0)
    value_local = jnp.concatenate([own_values.reshape(tok_count, inner_dev), text_values], axis=0)
    key_all, value_all = (
        lax.all_gather(key_local, "seq", axis=0, tiled=True),
        lax.all_gather(value_local, "seq", axis=0, tiled=True),
    )
    all_rows = rows_dev * seq_count
    row_ids = jnp.arange(all_rows, dtype=jnp.int32)
    owner = row_ids // rows_dev
    within = row_ids % rows_dev
    allowed = (within < tok_count) | (owner * text_dev + within - tok_count < text_len[0])
    group = 1
    while group * 2 * rows_dev <= 512 and seq_count % (group * 2) == 0:
        group = group * 2
    block_rows = group * rows_dev
    block_count = all_rows // block_rows
    key_blocks = key_all.reshape(block_count, block_rows, heads_dev, HD)
    value_blocks = value_all.reshape(block_count, block_rows, heads_dev, HD)
    mask_blocks = allowed.reshape(block_count, block_rows)

    def block_scores(key_block, mask_block):
        scores = (
            jnp.einsum("qhd,khd->qhk", queries, key_block, preferred_element_type=jnp.float32)
            * score_scale
        )
        return jnp.where(mask_block[None, None, :], scores, -1e30)

    def first_pass(carry, block):
        row_max, row_sum, row_dot = carry
        key_block, value_block, mask_block = block
        scores = block_scores(key_block, mask_block)
        new_max = jnp.maximum(row_max, jnp.max(scores, axis=-1))
        rescale = jnp.exp(row_max - new_max)
        exps = jnp.exp(scores - new_max[:, :, None])
        grad_weights = jnp.einsum(
            "qhd,khd->qhk", out_grad, value_block, preferred_element_type=jnp.float32
        )
        return (
            (
                new_max,
                row_sum * rescale + jnp.sum(exps, axis=-1),
                row_dot * rescale + jnp.sum(exps * grad_weights, axis=-1),
            ),
            None,
        )

    start_state = (
        jnp.full((tok_count, heads_dev), -1e30, jnp.float32),
        jnp.zeros((tok_count, heads_dev), jnp.float32),
        jnp.zeros((tok_count, heads_dev), jnp.float32),
    )
    (row_max, row_sum, row_dot), unused = lax.scan(
        first_pass, start_state, (key_blocks, value_blocks, mask_blocks)
    )
    log_total = row_max + jnp.log(row_sum)
    delta_row = row_dot / row_sum

    def second_pass(running, block):
        key_block, value_block, mask_block = block
        weights = jnp.exp(block_scores(key_block, mask_block) - log_total[:, :, None])
        grad_weights = jnp.einsum(
            "qhd,khd->qhk", out_grad, value_block, preferred_element_type=jnp.float32
        )
        grad_scores = (weights * (grad_weights - delta_row[:, :, None])).astype(jnp.bfloat16)
        return (
            running
            + jnp.einsum(
                "qhk,khd->qhd", grad_scores, key_block, preferred_element_type=jnp.float32
            ),
            None,
        )

    query_sum, unused = lax.scan(
        second_pass,
        jnp.zeros((tok_count, heads_dev, HD), jnp.float32),
        (key_blocks, value_blocks, mask_blocks),
    )
    grad_query = (query_sum * score_scale).astype(jnp.bfloat16)
    log_all, delta_all = (
        lax.all_gather(log_total, "seq", axis=0, tiled=True),
        lax.all_gather(delta_row, "seq", axis=0, tiled=True),
    )
    local_ids = jnp.arange(rows_dev, dtype=jnp.int32)
    local_allowed = (local_ids < tok_count) | (
        lax.axis_index("seq") * text_dev + local_ids - tok_count < text_len[0]
    )
    key_three = key_local.reshape(rows_dev, heads_dev, HD)
    value_three = value_local.reshape(rows_dev, heads_dev, HD)
    query_piece = lax.all_gather(queries.reshape(tok_count, inner_dev), "seq", axis=0, tiled=True)
    grad_piece = lax.all_gather(out_grad.reshape(tok_count, inner_dev), "seq", axis=0, tiled=True)
    piece_rows = query_piece.shape[0]
    query_rows = query_piece.reshape(piece_rows, heads_dev, HD)
    grad_rows = grad_piece.reshape(piece_rows, heads_dev, HD)
    scores = (
        jnp.einsum("qhd,khd->qhk", query_rows, key_three, preferred_element_type=jnp.float32)
        * score_scale
    )
    scores = jnp.where(local_allowed[None, None, :], scores, -1e30)
    weights = jnp.exp(scores - log_all[:, :, None])
    grad_weights = jnp.einsum(
        "qhd,khd->qhk", grad_rows, value_three, preferred_element_type=jnp.float32
    )
    grad_scores = (weights * (grad_weights - delta_all[:, :, None])).astype(jnp.bfloat16)
    rounded = weights.astype(jnp.bfloat16)
    key_sum = jnp.einsum(
        "qhk,qhd->khd", grad_scores, query_rows, preferred_element_type=jnp.float32
    )
    value_sum = jnp.einsum("qhk,qhd->khd", rounded, grad_rows, preferred_element_type=jnp.float32)
    key_sum, value_sum = (key_sum, value_sum)
    grad_key = (key_sum[:tok_count] * score_scale).astype(jnp.bfloat16)
    grad_value = value_sum[:tok_count].astype(jnp.bfloat16)
    raw_query = qk_backward(projected[:, 0], query_inv, grad_query, qk_gain[0])
    raw_key = qk_backward(projected[:, 1], key_inv, grad_key, qk_gain[1])
    stacked = jnp.stack([raw_query, raw_key, grad_value.astype(jnp.float32)], axis=1).astype(
        jnp.bfloat16
    )
    stacked = stacked.reshape(tok_count, 3 * inner_dev)
    partial_grad = lax.dot_general(
        stacked, full_weight, contract_last, preferred_element_type=jnp.float32
    )
    half_width = model_width // lax.axis_size("head")
    first_col = lax.axis_index("head") * half_width
    grad_share = lax.psum_scatter(
        partial_grad.astype(jnp.bfloat16), "head", scatter_dimension=1, tiled=True
    ).astype(jnp.float32)
    normed_share = lax.dynamic_slice_in_dim(normed, first_col, half_width, 1)
    stretch_share = lax.dynamic_slice_in_dim(stretch, first_col, half_width, 0)
    adjoint_share = lax.dynamic_slice_in_dim(adjoint_rows, first_col, half_width, 1)
    grad_scaled = grad_share * (1.0 + stretch_share)
    row_sums = jnp.stack(
        [jnp.sum(grad_scaled, axis=-1), jnp.sum(grad_scaled * normed_share, axis=-1)], axis=-1
    )
    row_sums = lax.psum(row_sums, "head")
    grad_state = inv_std * (
        grad_scaled - row_sums[:, 0:1] / model_width - normed_share * row_sums[:, 1:2] / model_width
    )
    pulled = clip_scale * adjoint_share + grad_state
    return pulled[None]


def solution(mesh):
    in_specs = (
        P("dp", "seq", None),
        P("dp", "seq", None),
        P("dp", "seq", None, "head"),
        P("dp"),
        P("dp"),
        P(),
        P("dp", None, "head"),
        P(),
        P("head", "dp"),
    )
    out_specs = P("dp", "seq", "head")
    by_head = mesh.shape["seq"] == 4 and mesh.shape["dp"] == 4 and mesh.shape["head"] == 2
    shards = shards_by_head if by_head else shards_by_row
    return jax.shard_map(shards, mesh=mesh, in_specs=in_specs, out_specs=out_specs, check_vma=False)
```

```python
import functools

import jax
import jax.numpy as jnp
from jax import lax
from jax.experimental import pallas as pl
from jax.experimental.pallas import tpu as pltpu
from jax.sharding import PartitionSpec as P

HD = 64
GRANT = 60 * 1024 * 1024
SMALL_GRANT = 24 * 1024 * 1024
EXTRA = 128
NT = (((1,), (1,)), ((), ()))
NN = (((1,), (0,)), ((), ()))


def line_ring(count):
    return [0] + list(range(1, count, 2)) + [i for i in range(count - 1, 0, -1) if i % 2 == 0]


def ring_pairs(order):
    return [(order[i], order[(i + 1) % len(order)]) for i in range(len(order))]


def ring_place(order, index):
    place = jnp.int32(0)
    for position, member in enumerate(order):
        place = jnp.where(index == member, jnp.int32(position), place)
    return place


def ring_member(order, place):
    member = jnp.int32(order[0])
    for position, value in enumerate(order):
        member = jnp.where(place == position, jnp.int32(value), member)
    return member


def dot(a, b, dims):
    return lax.dot_general(a, b, dims, preferred_element_type=jnp.float32)


def inverse_rms(raw):
    return lax.rsqrt(jnp.mean(raw * raw, axis=-1, keepdims=True) + 1e-06)


def norm_backward(raw, cotangent, gains):
    inverse = inverse_rms(raw)
    scaled = cotangent.astype(jnp.float32) * gains
    return (
        scaled * inverse
        - raw * jnp.mean(scaled * raw, axis=-1, keepdims=True) * (inverse * inverse * inverse)
    )


def whole_tiles(columns):
    return -(-columns // 128) * 128


def spec(space):
    return pl.BlockSpec(memory_space=space)


def text_columns(text, part):
    rows = text[...].astype(jnp.float32)[:, part, :]
    return [rows[:, c * EXTRA : (c + 1) * EXTRA] for c in range(rows.shape[1] // EXTRA)]


def extra_columns(blocks, rows):
    filled = sum(one.shape[0] for one in blocks)
    blocks = blocks + [jnp.zeros((rows - filled, EXTRA), jnp.float32)]
    return jnp.concatenate(blocks, axis=0).astype(jnp.bfloat16)


def first_kernel(step, core, states, table, adjoint, text, out, rows_out, extra_out):
    rows = [table[c, pl.ds(step[0], 1), :] for c in range(3)]
    widened = states[...].astype(jnp.float32)
    centered = widened - jnp.mean(widened, axis=-1, keepdims=True)
    inv_std = lax.rsqrt(jnp.mean(centered * centered, axis=-1, keepdims=True) + 1e-06)
    half, width = states.shape
    out[:, :width] = (centered * inv_std * (1.0 + rows[1]) + rows[0]).astype(jnp.bfloat16)
    for c in range(3):
        rows_out[c : c + 1, :] = rows[c]
    squares = jnp.sum(adjoint[...] * adjoint[...], axis=0, keepdims=True)
    squares = jnp.sum(squares, axis=1, keepdims=True)
    terms = []
    for n in range(3):
        terms.append(squares.astype(jnp.bfloat16).astype(jnp.float32))
        squares = squares - terms[-1]
    lane = lax.broadcasted_iota(jnp.int32, (8, EXTRA), 1)
    sums = jnp.where(lane == 0, terms[0], jnp.where(lane == 1, terms[1], jnp.where(lane == 2, terms[2], 0.0)))
    extra = extra_columns(text_columns(text, 0) + [sums], half)
    out[:, width:] = extra
    extra_out[...] = extra


def first_call(step, core, states, table, adjoint, text):
    rows, width = states.shape
    half = rows // 2
    whole = lambda *shape: pl.BlockSpec(shape, lambda i, step, core: (0,) * len(shape))
    return pl.pallas_call(
        first_kernel,
        out_shape=(
            jax.ShapeDtypeStruct((half, width + EXTRA), jnp.bfloat16),
            jax.ShapeDtypeStruct((8, width), jnp.float32),
            jax.ShapeDtypeStruct((half, EXTRA), jnp.bfloat16),
        ),
        grid_spec=pltpu.PrefetchScalarGridSpec(
            num_scalar_prefetch=2,
            grid=(1,),
            in_specs=[
                pl.BlockSpec((half, width), lambda i, step, core: (core[0], 0)),
                whole(*table.shape),
                whole(*adjoint.shape),
                whole(*text.shape),
            ],
            out_specs=(whole(half, width + EXTRA), whole(8, width), whole(half, EXTRA)),
        ),
        compiler_params=pltpu.CompilerParams(vmem_limit_bytes=GRANT),
        cost_estimate=pl.CostEstimate(flops=8 * half * width, bytes_accessed=16 * half * width, transcendentals=0),
    )(step, core, states, table, adjoint, text)


def pick_half(core, rows):
    half = rows.shape[1] // 2
    return jnp.where(core == 0, rows[:, :half], rows[:, half:])


def modulate_kernel(core, states, table_rows, extra, out, normed_out, stretch_out, inv_out):
    widened = states[...].astype(jnp.float32)
    centered = widened - jnp.mean(widened, axis=-1, keepdims=True)
    inv_std = lax.rsqrt(jnp.mean(centered * centered, axis=-1, keepdims=True) + 1e-06)
    normed = centered * inv_std
    scale = 1.0 + table_rows[1:2, :]
    rows, width = states.shape
    out[:, :width] = (normed * scale + table_rows[0:1, :]).astype(jnp.bfloat16)
    for n in range(2):
        out[n * rows // 2 : (n + 1) * rows // 2, width:] = extra[...]
    normed_out[...] = pick_half(core[0], normed)
    stretch_out[...] = pick_half(core[0], scale)
    inv_out[...] = jnp.broadcast_to(inv_std, inv_out.shape)


def cotangent_kernel(limit, core, adjoint, table_rows, text, extra, previous, following, opposite, out, half_out, base_out):
    quarter = opposite.shape[0]
    first = 2 * quarter - opposite.shape[0]
    row = 8 * (text.shape[2] // EXTRA)
    squares = None
    for terms in (extra[...], previous[...], following[...]):
        terms = terms.astype(jnp.float32)[row : row + 1, :]
        squares = terms if squares is None else squares + terms
    squares = squares + opposite[...].astype(jnp.float32)[row - first : row - first + 1, :]
    squares = jnp.sum(squares, axis=1, keepdims=True)
    clip_scale = jnp.minimum(1.0, limit / jnp.sqrt(squares + 1e-06))
    gating = table_rows[2:3, :]
    clipped = clip_scale * adjoint[...]
    rows, width = adjoint.shape
    half = rows // 2
    columns = extra_columns(text_columns(text, 1), half)
    out[:, :width] = (gating * clipped).astype(jnp.bfloat16)
    for n in range(2):
        out[n * half : (n + 1) * half, width:] = columns
    base_out[...] = pick_half(core[0], clipped)
    own = adjoint[pl.ds(pl.multiple_of(core[0] * half, 8), half), :]
    half_out[:, :width] = (gating * (clip_scale * own)).astype(jnp.bfloat16)
    half_out[:, width:] = columns


def cotangent_call(limit, core, adjoint, table_rows, text, extra, previous, following, opposite):
    rows, width = adjoint.shape
    bf16 = jnp.bfloat16
    block = width // EXTRA
    whole = lambda one: pl.BlockSpec(one.shape, lambda i, core: (0,) * one.ndim)
    tail = lambda one: pl.BlockSpec((one.shape[0], EXTRA), lambda i, core: (0, block))
    outs = (
        jax.ShapeDtypeStruct((rows, width + EXTRA), bf16),
        jax.ShapeDtypeStruct((rows // 2, width + EXTRA), bf16),
        jax.ShapeDtypeStruct((rows, width // 2), jnp.float32),
    )
    return pl.pallas_call(
        functools.partial(cotangent_kernel, limit),
        out_shape=outs,
        grid_spec=pltpu.PrefetchScalarGridSpec(
            num_scalar_prefetch=1,
            grid=(1,),
            in_specs=[whole(adjoint), whole(table_rows), whole(text), whole(extra)]
            + [tail(one) for one in (previous, following, opposite)],
            out_specs=tuple(whole(one) for one in outs),
        ),
        compiler_params=pltpu.CompilerParams(vmem_limit_bytes=SMALL_GRANT),
        cost_estimate=pl.CostEstimate(flops=4 * rows * width, bytes_accessed=12 * rows * width, transcendentals=0),
    )(core, adjoint, table_rows, text, extra, previous, following, opposite)


class Copies:
    def __init__(self, sems):
        self.sems = sems
        self.count = 0

    def start(self, source, target):
        copy = pltpu.make_async_copy(source, target, self.sems.at[self.count])
        copy.start()
        self.count += 1
        return copy

    def weights(self, scalars, w_in, w_all, shard, first=0):
        half = shard // 2
        places = [(1, 0, shard), (2, 0, shard), (3, 0, shard), (4, 0, half), (4, half, half)]
        columns = w_in[0].shape[1] - first
        copies = []
        for n, piece in enumerate(w_in):
            k, offset, size = places[n % 5]
            there = pl.ds(pl.multiple_of(scalars[k] * shard + offset, 16), size)
            target = w_all.at[there, pl.ds(n // 5 * columns, columns)]
            copies.append(self.start(piece.at[:, pl.ds(first, columns)], target))
        return copies

    def weight_halves(self, scalars, w_in, keep, give, shard):
        half = shard // 2
        places = [(1, 0, shard), (2, 0, shard), (3, 0, shard), (4, 0, half), (4, half, half)]
        part = w_in[0].shape[1]
        copies = []
        for n, piece in enumerate(w_in):
            k, offset, size = places[n % 5]
            first = n // 5 * part
            columns = min(part, keep.shape[1] - first)
            source = piece.at[:, pl.ds(0, columns)]
            owner = scalars[k]
            there = pl.ds(pl.multiple_of(owner % 2 * shard + offset, 16), size)
            sem = self.sems.at[self.count]
            self.count += 1
            kept = pltpu.make_async_copy(source, keep.at[there, pl.ds(first, columns)], sem)
            given = pltpu.make_async_copy(source, give.at[there, pl.ds(first, columns)], sem)
            pl.when(owner // 2 == scalars[0])(kept.start)
            pl.when(owner // 2 != scalars[0])(given.start)
            copies.append(kept)
        return copies

    def rows(self, core, pieces, target, rows):
        half, quarter = rows // 2, rows // 4
        copies = [self.start(pieces[0], target.at[pl.ds(0, rows)])]
        places = [(rows, half), (3 * rows, half), (2 * rows, quarter), (2 * rows + quarter, quarter)]
        for n, (first, size) in enumerate(places):
            for m, holder in enumerate((core, 1 - core)):
                there = pl.ds(pl.multiple_of(first + holder * half, 16), size)
                copies.append(self.start(pieces[1 + 2 * n + m], target.at[there]))
        return copies


def window_heads(scalars, count, rows, text_dev, gathered, width, extra, text, text_t=None):
    half = rows // 2
    for k in range(count):
        there = pl.ds(pl.multiple_of(k * rows + scalars[0] * half, 16), half)
        extra[k] = gathered[there, width:].astype(jnp.float32)
    for i in range(text.shape[0]):
        head = scalars[5] + i
        first = pl.ds(pl.multiple_of(head // 2 * text_dev, 8), text_dev)
        found = jnp.concatenate([extra[k, first, :] for k in range(count)], axis=0)
        found = jnp.where(head % 2 == 0, found[:, :HD], found[:, HD:])
        text[i] = found.astype(jnp.bfloat16)
        if text_t is not None:
            text_t[i] = found.T.astype(jnp.bfloat16)


def project_kernel(slots, count, rows, shard, width, text_dev, scalars, gain, *refs):
    refs = list(refs)
    take = lambda n: [refs.pop(0) for _ in range(n)]
    mod_in = take(9)
    w_in = take(5)
    q_all, k_all, v_all, k_t, raw_q, raw_k, text, text_t, w_keep, w_give = take(10)
    w_all, mod_all, sems, extra = take(4)
    inner = slots * HD
    core = scalars[0]
    copies = Copies(sems)
    w_copies = copies.weights(scalars, w_in, w_all, shard)
    row_copies = copies.rows(core, mod_in, mod_all, rows)

    gain_q = gain[0:1, :]
    gain_k = gain[1:2, :]
    score_scale = HD ** (-0.5)
    half_copies = copies.weight_halves(scalars, w_in, w_keep, w_give, shard)
    for copy in w_copies + row_copies:
        copy.wait()
    window_heads(scalars, count, rows, text_dev, mod_all, width, extra, text, text_t)
    span = 2 * rows
    for b in range(count // 2):
        here = slice(b * span, (b + 1) * span)
        projected = jnp.dot(
            mod_all[here, :width], w_all[:, : 3 * inner], preferred_element_type=jnp.float32
        )
        for i in range(slots):
            query = projected[:, i * HD : (i + 1) * HD]
            key = projected[:, inner + i * HD : inner + (i + 1) * HD]
            value = projected[:, 2 * inner + i * HD : 2 * inner + (i + 1) * HD]
            raw_q[i, here, :] = query
            raw_k[i, here, :] = key
            query = query * inverse_rms(query) * gain_q
            q_all[i, here, :] = (query * score_scale).astype(jnp.bfloat16)
            key = key * inverse_rms(key) * gain_k
            k_all[i, here, :] = key.astype(jnp.bfloat16)
            k_t[i, :, here] = key.T.astype(jnp.bfloat16)
            v_all[i, here, :] = value.astype(jnp.bfloat16)
    for copy in half_copies:
        copy.wait()


def attend_kernel(slots, count, rows, shard, width, text_dev, first_column, scalars, gain, *refs):
    refs = list(refs)
    take = lambda n: [refs.pop(0) for _ in range(n)]
    projected = take(10)
    cot_in = take(9)
    w_in = take(5)
    mine_out, theirs_out, rest_out = take(3)
    w_out, cot_all, sems, extra, values_text = take(5)
    d_all, back_q, back_k, back_v, stacked = take(5)
    q_all, k_all, v_all, k_t, raw_q, raw_k, text, text_t, w_keep, w_give = refs
    inner = slots * HD
    tokens = rows * count
    core = scalars[0]
    copies = Copies(sems)
    w_copies = copies.weights(scalars, w_in, w_out, shard, first_column)
    row_copies = copies.rows(core, cot_in, cot_all, rows)
    local_copies = [copies.start(*one) for one in zip(projected, refs)]
    gain_q = gain[0:1, :]
    gain_k = gain[1:2, :]
    score_scale = HD ** (-0.5)
    span = 2 * rows

    text_rows = count * text_dev
    row = lax.broadcasted_iota(jnp.int32, (text_rows, span), 0)
    text_id = row
    for k in range(count):
        inside = (row >= k * text_dev) & (row < (k + 1) * text_dev)
        text_id = jnp.where(inside, row + (scalars[7 + k] - k) * text_dev, text_id)
    bias = jnp.where(text_id < scalars[6], 0.0, -1e30)
    stacked[:, 3 * inner :] = jnp.zeros((tokens, stacked.shape[1] - 3 * inner), jnp.float32)

    for copy in w_copies:
        copy.wait()
    arrivals = [row_copies[:3], row_copies[3:]]
    for b in range(count // 2):
        for copy in arrivals[b]:
            copy.wait()
        here = slice(b * span, (b + 1) * span)
        out_grad = jnp.dot(cot_all[here, :width], w_out[...], preferred_element_type=jnp.float32)
        out_grad = out_grad[:, out_grad.shape[1] - inner :]
        for i in range(slots):
            d_all[i, here, :] = out_grad[:, i * HD : (i + 1) * HD].astype(jnp.bfloat16)
    window_heads(scalars, count, rows, text_dev, cot_all, width, extra, values_text)
    for copy in local_copies[:8]:
        copy.wait()

    @pl.loop(0, slots)
    def attend(i):
        grad_k, grad_v = 0.0, 0.0
        for b in range(count // 2):
            here = slice(b * span, (b + 1) * span)
            query = q_all[i, here, :]
            grad = d_all[i, here, :]
            scores = dot(k_all[i], query, NT)
            text_scores = dot(text[i], query, NT) + bias
            col_max = jnp.maximum(
                jnp.max(scores, axis=0, keepdims=True), jnp.max(text_scores, axis=0, keepdims=True)
            )
            exps = jnp.exp(scores - col_max)
            text_exps = jnp.exp(text_scores - col_max)
            total = jnp.sum(exps, axis=0, keepdims=True) + jnp.sum(text_exps, axis=0, keepdims=True)
            inverse = 1.0 / total
            grad_w = dot(v_all[i], grad, NT)
            text_grad_w = dot(values_text[i], grad, NT)
            delta = inverse * (
                jnp.sum(exps * grad_w, axis=0, keepdims=True)
                + jnp.sum(text_exps * text_grad_w, axis=0, keepdims=True)
            )
            weights = exps * inverse
            grad_s = (weights * (grad_w - delta)).astype(jnp.bfloat16)
            text_grad_s = (text_exps * inverse * (text_grad_w - delta)).astype(jnp.bfloat16)
            grad_k += dot(grad_s, query, NN)
            grad_v += dot(weights.astype(jnp.bfloat16), grad, NN)
            grad_q = dot(k_t[i], grad_s, NN) + dot(text_t[i], text_grad_s, NN)
            grad_q = (grad_q.T * score_scale).astype(jnp.bfloat16)
            back_q[i, here, :] = norm_backward(raw_q[i, here, :], grad_q, gain_q)
        back_k[i] = norm_backward(raw_k[i], grad_k.astype(jnp.bfloat16), gain_k)
        back_v[i] = grad_v

    for i in range(slots):
        valid = scalars[7 + count + i] > 0
        for n, part in enumerate((back_q, back_k, back_v)):
            there = n * inner + i * HD
            stacked[:, there : there + HD] = jnp.where(valid, part[i], 0.0)
    first = stacked[rows : 2 * rows, :].astype(jnp.bfloat16)
    rest_out[: (count - 2) * rows, :] = stacked[2 * rows :, :].astype(jnp.bfloat16)
    rest_out[(count - 2) * rows :, :] = stacked[:rows, :].astype(jnp.bfloat16)
    for copy in local_copies[8:]:
        copy.wait()
    theirs_out[...] = dot(first, w_give[...], NT).astype(jnp.bfloat16)
    mine_out[...] = dot(first, w_keep[...], NT)


def project_call(scalars, gain, mod, weights, slots, rows, text_dev, count):
    shard = weights[0].shape[0]
    columns = 4 * slots * HD
    width = mod[0].shape[1] - EXTRA
    tokens = rows * count
    text_rows = text_dev * count
    f32, bf16 = jnp.float32, jnp.bfloat16
    vmem, hbm = spec(pltpu.VMEM), spec(pl.ANY)
    by_token = (slots, tokens, HD)
    shapes = [(by_token, bf16)] * 3 + [((slots, HD, tokens), bf16)] + [(by_token, f32)] * 2
    shapes += [((slots, text_rows, HD), bf16), ((slots, HD, text_rows), bf16)]
    shapes += [((width // 2, whole_tiles(3 * slots * HD)), bf16)] * 2
    return pl.pallas_call(
        functools.partial(project_kernel, slots, count, rows, shard, width, text_dev),
        out_shape=tuple(jax.ShapeDtypeStruct(*one) for one in shapes),
        in_specs=[spec(pltpu.SMEM), vmem] + [hbm] * (len(mod) + len(weights)),
        out_specs=(vmem,) * (len(shapes) - 2) + (hbm,) * 2,
        scratch_shapes=[
            pltpu.VMEM((width, columns), bf16),
            pltpu.VMEM((tokens, width + EXTRA), bf16),
            pltpu.SemaphoreType.DMA((len(mod) + 2 * len(weights),)),
            pltpu.VMEM((count, rows // 2, EXTRA), f32),
        ],
        compiler_params=pltpu.CompilerParams(vmem_limit_bytes=GRANT),
        cost_estimate=pl.CostEstimate(
            flops=2 * tokens * width * 3 * slots * HD,
            bytes_accessed=2 * (tokens * width + columns * width) + 4 * tokens * columns,
            transcendentals=0,
        ),
    )(scalars, gain, *mod, *weights)


def attend_call(scalars, gain, operands, cot, weights, slots, rows, text_dev):
    count = operands[0].shape[1] // rows
    shard, columns = weights[0].shape
    width = cot[0].shape[1] - EXTRA
    tokens = rows * count
    inner = slots * HD
    stacked = whole_tiles(3 * inner)
    first = (columns - inner) // 128 * 128
    f32, bf16 = jnp.float32, jnp.bfloat16
    vmem, hbm = spec(pltpu.VMEM), spec(pl.ANY)
    by_token = (slots, tokens, HD)
    shapes = [((rows, width // 2), f32), ((rows, width // 2), bf16), ((tokens - rows, stacked), bf16)]
    return pl.pallas_call(
        functools.partial(attend_kernel, slots, count, rows, shard, width, text_dev, first),
        out_shape=tuple(jax.ShapeDtypeStruct(*one) for one in shapes),
        in_specs=[spec(pltpu.SMEM), vmem] + [hbm] * (len(operands) + len(cot) + len(weights)),
        out_specs=(vmem,) * len(shapes),
        scratch_shapes=[
            pltpu.VMEM((width, columns - first), bf16),
            pltpu.VMEM((tokens, width + EXTRA), bf16),
            pltpu.SemaphoreType.DMA((len(operands) + len(cot) + len(weights),)),
            pltpu.VMEM((count, rows // 2, EXTRA), f32),
            pltpu.VMEM((slots, text_dev * count, HD), bf16),
            pltpu.VMEM(by_token, bf16),
        ]
        + [pltpu.VMEM(by_token, f32)] * 3
        + [pltpu.VMEM((tokens, stacked), f32)]
        + [pltpu.VMEM(one.shape, one.dtype) for one in operands],
        compiler_params=pltpu.CompilerParams(vmem_limit_bytes=GRANT),
        cost_estimate=pl.CostEstimate(
            flops=2 * tokens * width * inner + 10 * tokens * tokens * inner,
            bytes_accessed=2 * (tokens * width + columns * width),
            transcendentals=slots * tokens * tokens,
        ),
    )(scalars, gain, *operands, *cot, *weights)


def backward_kernel(own, other, w_own, w_other, *outs):
    total = dot(own[...], w_own[...], NT) + dot(other[...], w_other[...], NT)
    part = outs[0].shape[0]
    for n, out in enumerate(outs):
        out[...] = total[n * part : (n + 1) * part].astype(out.dtype)


def backward_call(own, other, w_own, w_other, part, dtype):
    rows, inner = own.shape
    half = w_own.shape[0]
    vmem = spec(pltpu.VMEM)
    return pl.pallas_call(
        backward_kernel,
        out_shape=(jax.ShapeDtypeStruct((part, half), dtype),) * (rows // part),
        in_specs=[vmem] * 4,
        out_specs=(vmem,) * (rows // part),
        compiler_params=pltpu.CompilerParams(vmem_limit_bytes=SMALL_GRANT),
        cost_estimate=pl.CostEstimate(
            flops=4 * rows * half * inner,
            bytes_accessed=4 * (rows + half) * inner + 4 * rows * half,
            transcendentals=0,
        ),
    )(own, other, w_own, w_other)


def sums_kernel(own_near, own_far, near, far, scale, normed, grad_out, sums_out):
    half = near.shape[0]
    for part, (own, moving) in enumerate(((own_near, near), (own_far, far))):
        here = slice(part * half, (part + 1) * half)
        grad = (own[...] + moving[...].astype(jnp.float32)) * scale[...]
        grad_out[here, :] = grad
        first = jnp.sum(grad, axis=-1, keepdims=True)
        second = jnp.sum(grad * normed[here, :], axis=-1, keepdims=True)
        lane = lax.broadcasted_iota(jnp.int32, (half, 128), 1)
        sums_out[here, :] = jnp.where(lane == 0, first, second)


def last_kernel(width, grad, sums, other, normed, base, inv_std, out):
    total = (sums[...] + other[...]) * (1.0 / width)
    rows = base[...] + inv_std[:, 0:1] * (
        grad[...] - total[:, 0:1] - normed[...] * total[:, 1:2]
    )
    out[...] = rows.T


def local_call(kernel, shapes, scalar_count, *operands):
    vmem = spec(pltpu.VMEM)
    return pl.pallas_call(
        kernel,
        out_shape=tuple(jax.ShapeDtypeStruct(*one) for one in shapes),
        in_specs=[spec(pltpu.SMEM)] * scalar_count + [vmem] * (len(operands) - scalar_count),
        out_specs=(vmem,) * len(shapes),
        compiler_params=pltpu.CompilerParams(vmem_limit_bytes=SMALL_GRANT),
        cost_estimate=pl.CostEstimate(
            flops=sum(one.size for one in operands),
            bytes_accessed=sum(one.size * one.dtype.itemsize for one in operands),
            transcendentals=0,
        ),
    )(*operands)


def shards_by_head(states, adjoint, text_kv, text_len, step_index, modulation, w_qkv, qk_gain, w_out):
    hidden_state = states[0]
    adjoint_rows = adjoint[0]
    tok_count, model_width = hidden_state.shape
    seq_count = lax.axis_size("seq")
    inner_dev = w_qkv.shape[2]
    heads_dev = inner_dev // HD
    shard = w_qkv.shape[0]
    slots = -(-heads_dev // seq_count)
    inner = slots * HD
    half_rows = tok_count // 2
    half_width = model_width // 2
    f32, bf16 = jnp.float32, jnp.bfloat16
    core = lax.axis_index("head").astype(jnp.int32)
    seq_index = lax.axis_index("seq")
    dp_index = lax.axis_index("dp")
    pin = lax.optimization_barrier

    seq_order = line_ring(seq_count)
    seq_place = ring_place(seq_order, seq_index)
    seq_next = ring_pairs(seq_order)
    swap = [(0, 1), (1, 0)]
    along_x = [(p, p ^ 1) for p in range(4)]
    along_y = [(p, p ^ 2) for p in range(4)]

    first = seq_index * heads_dev // seq_count
    stop = (seq_index + 1) * heads_dev // seq_count
    window = jnp.minimum(first, heads_dev - slots)
    valid = [(window + i >= first) & (window + i < stop) for i in range(slots)]
    owners = [ring_member(seq_order, (seq_place - k + seq_count) % seq_count) for k in range(seq_count)]
    w_index = [dp_index, dp_index ^ 1, dp_index ^ 2, dp_index ^ 3]
    scalars = [core] + w_index + [window, text_len[0]] + owners + valid
    scalars = jnp.stack([one.astype(jnp.int32) for one in scalars])

    def step(moving):
        return lax.ppermute(moving, "seq", seq_next)

    def other_core(moving):
        return lax.ppermute(moving, "head", swap)

    def step_back(moving):
        return lax.ppermute(moving, "seq", [(b, a) for a, b in seq_next])

    quarter = half_rows // 2

    def spread(moving):
        return [step(moving), step_back(moving)]

    def pass_on(received):
        return [step(received[0][:quarter]), step_back(received[1][quarter:])]

    mod_half, table_rows, extra = first_call(
        step_index, core[None], hidden_state, modulation.transpose(1, 0, 2), adjoint_rows, text_kv[0]
    )
    mod_near = spread(mod_half)

    w_qkv, w_out, mod_half = pin((w_qkv, w_out, mod_half))
    take = lambda c: lax.dynamic_slice(w_qkv, (0, c, window * HD), (shard, 1, inner))[:, 0]
    own_w = [
        jnp.concatenate(
            [take(0), take(1), take(2), lax.dynamic_slice_in_dim(w_out, window * HD, inner, 0).T], axis=1
        )
    ]
    w_near = [lax.ppermute(part, "dp", pairs) for part in own_w for pairs in (along_x, along_y)]

    text_dev = text_kv.shape[1]
    mod_far = pass_on(mod_near)
    clip_limit = 0.5 * (tok_count * seq_count * model_width) ** 0.5
    cotangent, cot_half, base = cotangent_call(
        clip_limit, scalars, adjoint_rows, table_rows, text_kv[0], extra, *mod_near, mod_far[1]
    )
    cot_half, mod_far[0] = pin((cot_half, mod_far[0]))
    cot_near = spread(cot_half)
    modulated, normed_share, scale_share, inv_std = local_call(
        modulate_kernel,
        [
            ((tok_count, model_width + EXTRA), bf16),
            ((tok_count, half_width), f32),
            ((1, half_width), f32),
            ((tok_count, 128), f32),
        ],
        1,
        core[None],
        hidden_state,
        table_rows,
        extra,
    )
    def pieces(own, received):
        return [own] + [one for moved in received for one in (moved, other_core(moved))]

    mod_pieces = pieces(modulated, mod_near + mod_far)
    *w_near, mod_pieces = pin((*w_near, mod_pieces))
    weights = []
    for n, part in enumerate(own_w):
        w_x, w_y = w_near[2 * n : 2 * n + 2]
        weights += [
            part,
            w_x,
            w_y,
            lax.ppermute(w_x[: shard // 2], "dp", along_y),
            lax.ppermute(w_y[shard // 2 :], "dp", along_x),
        ]
    cot_far = pass_on(cot_near)

    cot_pieces = pieces(cotangent, cot_near)
    *cot_pieces, mod_pieces[-1] = pin((*cot_pieces, mod_pieces[-1]))
    *operands, w_keep, w_give = project_call(
        scalars, qk_gain, mod_pieces, weights, slots, tok_count, text_dev, seq_count
    )
    w_give, cot_far[0], cot_far[1] = pin((w_give, *cot_far))
    cot_pieces += pieces(None, cot_far)[1:]
    given, *cot_pieces = pin((w_give, *cot_pieces))
    w_other = other_core(given)
    mine, theirs, rest = attend_call(
        scalars, qk_gain, operands + [w_keep, w_give], cot_pieces, weights, slots, tok_count, text_dev
    )
    first = (mine + other_core(theirs).astype(f32)).astype(bf16)
    moving = [first[:half_rows], first[half_rows:]]
    other_rest = other_core(rest)
    rest, other_rest, *_ = pin((rest, other_rest, *moving))
    own = backward_call(rest, other_rest, w_keep, w_other, half_rows, f32)
    for j in range(2, seq_count):
        moving = [step(part) for part in moving]
        moving = [
            (a + b.astype(f32)).astype(bf16) for a, b in zip(own[2 * (j - 2) : 2 * (j - 1)], moving)
        ]
    moving = [step(part) for part in moving]

    grad_scaled, sums = local_call(
        sums_kernel,
        [((tok_count, half_width), f32), ((tok_count, 128), f32)],
        0,
        *own[-2:],
        *moving,
        scale_share,
        normed_share,
    )
    (pulled,) = local_call(
        functools.partial(last_kernel, model_width),
        [((half_width, tok_count), f32)],
        0,
        grad_scaled,
        sums,
        other_core(sums),
        normed_share,
        base,
        inv_std,
    )
    return pulled.T[None]


def qk_normalize(values, gains):
    inverse = lax.rsqrt(jnp.mean(values * values, axis=-1, keepdims=True) + 1e-06)
    return ((values * inverse * gains).astype(jnp.bfloat16), inverse)


def qk_backward(values, inverse, cotangent, gains):
    scaled = cotangent.astype(jnp.float32) * gains
    return (
        scaled * inverse - values * jnp.mean(scaled * values, axis=-1, keepdims=True) * inverse**3
    )


def shards_by_row(states, adjoint, text_kv, text_len, step_index, modulation, w_qkv, qk_gain, w_out):
    hidden_state = states[0]
    adjoint_rows = adjoint[0]
    tok_count, model_width = hidden_state.shape
    seq_count = lax.axis_size("seq")
    inner_dev = w_qkv.shape[2]
    heads_dev = inner_dev // HD
    score_scale = HD ** (-0.5)
    squares = lax.psum(jnp.sum(adjoint_rows * adjoint_rows), "seq")
    clip_limit = 0.5 * (tok_count * seq_count * model_width) ** 0.5
    clip_scale = jnp.minimum(1.0, clip_limit / jnp.sqrt(squares + 1e-06))
    table_row = lax.dynamic_index_in_dim(modulation, step_index[0], 0, keepdims=False)
    offset_row = table_row[0]
    stretch = table_row[1]
    gating = table_row[2]
    widened = hidden_state.astype(jnp.float32)
    centered = widened - jnp.mean(widened, axis=-1, keepdims=True)
    inv_std = lax.rsqrt(jnp.mean(centered * centered, axis=-1, keepdims=True) + 1e-06)
    normed = centered * inv_std
    modulated = (normed * (1.0 + stretch) + offset_row).astype(jnp.bfloat16)
    cotangent = (gating * (clip_scale * adjoint_rows)).astype(jnp.bfloat16)
    contract_last = (((1,), (1,)), ((), ()))
    full_weight = lax.all_gather(w_qkv, "dp", axis=0, tiled=True).reshape(
        model_width, 3 * inner_dev
    )
    projected = jnp.dot(modulated, full_weight, preferred_element_type=jnp.float32)
    out_raw = lax.dot_general(
        cotangent,
        lax.all_gather(w_out, "dp", axis=1, tiled=True),
        contract_last,
        preferred_element_type=jnp.float32,
    )
    projected = projected.reshape(tok_count, 3, heads_dev, HD)
    queries, query_inv = qk_normalize(projected[:, 0], qk_gain[0])
    own_keys, key_inv = qk_normalize(projected[:, 1], qk_gain[1])
    own_values = projected[:, 2].astype(jnp.bfloat16)
    out_grad = out_raw.astype(jnp.bfloat16).reshape(tok_count, heads_dev, HD)
    text_keys = text_kv[0, :, 0, :]
    text_values = text_kv[0, :, 1, :]
    text_dev = text_keys.shape[0]
    rows_dev = tok_count + text_dev
    key_local = jnp.concatenate([own_keys.reshape(tok_count, inner_dev), text_keys], axis=0)
    value_local = jnp.concatenate([own_values.reshape(tok_count, inner_dev), text_values], axis=0)
    key_all, value_all = (
        lax.all_gather(key_local, "seq", axis=0, tiled=True),
        lax.all_gather(value_local, "seq", axis=0, tiled=True),
    )
    all_rows = rows_dev * seq_count
    row_ids = jnp.arange(all_rows, dtype=jnp.int32)
    owner = row_ids // rows_dev
    within = row_ids % rows_dev
    allowed = (within < tok_count) | (owner * text_dev + within - tok_count < text_len[0])
    group = 1
    while group * 2 * rows_dev <= 512 and seq_count % (group * 2) == 0:
        group = group * 2
    block_rows = group * rows_dev
    block_count = all_rows // block_rows
    key_blocks = key_all.reshape(block_count, block_rows, heads_dev, HD)
    value_blocks = value_all.reshape(block_count, block_rows, heads_dev, HD)
    mask_blocks = allowed.reshape(block_count, block_rows)

    def block_scores(key_block, mask_block):
        scores = (
            jnp.einsum("qhd,khd->qhk", queries, key_block, preferred_element_type=jnp.float32)
            * score_scale
        )
        return jnp.where(mask_block[None, None, :], scores, -1e30)

    def first_pass(carry, block):
        row_max, row_sum, row_dot = carry
        key_block, value_block, mask_block = block
        scores = block_scores(key_block, mask_block)
        new_max = jnp.maximum(row_max, jnp.max(scores, axis=-1))
        rescale = jnp.exp(row_max - new_max)
        exps = jnp.exp(scores - new_max[:, :, None])
        grad_weights = jnp.einsum(
            "qhd,khd->qhk", out_grad, value_block, preferred_element_type=jnp.float32
        )
        return (
            (
                new_max,
                row_sum * rescale + jnp.sum(exps, axis=-1),
                row_dot * rescale + jnp.sum(exps * grad_weights, axis=-1),
            ),
            None,
        )

    start_state = (
        jnp.full((tok_count, heads_dev), -1e30, jnp.float32),
        jnp.zeros((tok_count, heads_dev), jnp.float32),
        jnp.zeros((tok_count, heads_dev), jnp.float32),
    )
    (row_max, row_sum, row_dot), unused = lax.scan(
        first_pass, start_state, (key_blocks, value_blocks, mask_blocks)
    )
    log_total = row_max + jnp.log(row_sum)
    delta_row = row_dot / row_sum

    def second_pass(running, block):
        key_block, value_block, mask_block = block
        weights = jnp.exp(block_scores(key_block, mask_block) - log_total[:, :, None])
        grad_weights = jnp.einsum(
            "qhd,khd->qhk", out_grad, value_block, preferred_element_type=jnp.float32
        )
        grad_scores = (weights * (grad_weights - delta_row[:, :, None])).astype(jnp.bfloat16)
        return (
            running
            + jnp.einsum(
                "qhk,khd->qhd", grad_scores, key_block, preferred_element_type=jnp.float32
            ),
            None,
        )

    query_sum, unused = lax.scan(
        second_pass,
        jnp.zeros((tok_count, heads_dev, HD), jnp.float32),
        (key_blocks, value_blocks, mask_blocks),
    )
    grad_query = (query_sum * score_scale).astype(jnp.bfloat16)
    log_all, delta_all = (
        lax.all_gather(log_total, "seq", axis=0, tiled=True),
        lax.all_gather(delta_row, "seq", axis=0, tiled=True),
    )
    local_ids = jnp.arange(rows_dev, dtype=jnp.int32)
    local_allowed = (local_ids < tok_count) | (
        lax.axis_index("seq") * text_dev + local_ids - tok_count < text_len[0]
    )
    key_three = key_local.reshape(rows_dev, heads_dev, HD)
    value_three = value_local.reshape(rows_dev, heads_dev, HD)
    query_piece = lax.all_gather(queries.reshape(tok_count, inner_dev), "seq", axis=0, tiled=True)
    grad_piece = lax.all_gather(out_grad.reshape(tok_count, inner_dev), "seq", axis=0, tiled=True)
    piece_rows = query_piece.shape[0]
    query_rows = query_piece.reshape(piece_rows, heads_dev, HD)
    grad_rows = grad_piece.reshape(piece_rows, heads_dev, HD)
    scores = (
        jnp.einsum("qhd,khd->qhk", query_rows, key_three, preferred_element_type=jnp.float32)
        * score_scale
    )
    scores = jnp.where(local_allowed[None, None, :], scores, -1e30)
    weights = jnp.exp(scores - log_all[:, :, None])
    grad_weights = jnp.einsum(
        "qhd,khd->qhk", grad_rows, value_three, preferred_element_type=jnp.float32
    )
    grad_scores = (weights * (grad_weights - delta_all[:, :, None])).astype(jnp.bfloat16)
    rounded = weights.astype(jnp.bfloat16)
    key_sum = jnp.einsum(
        "qhk,qhd->khd", grad_scores, query_rows, preferred_element_type=jnp.float32
    )
    value_sum = jnp.einsum("qhk,qhd->khd", rounded, grad_rows, preferred_element_type=jnp.float32)
    key_sum, value_sum = (key_sum, value_sum)
    grad_key = (key_sum[:tok_count] * score_scale).astype(jnp.bfloat16)
    grad_value = value_sum[:tok_count].astype(jnp.bfloat16)
    raw_query = qk_backward(projected[:, 0], query_inv, grad_query, qk_gain[0])
    raw_key = qk_backward(projected[:, 1], key_inv, grad_key, qk_gain[1])
    stacked = jnp.stack([raw_query, raw_key, grad_value.astype(jnp.float32)], axis=1).astype(
        jnp.bfloat16
    )
    stacked = stacked.reshape(tok_count, 3 * inner_dev)
    partial_grad = lax.dot_general(
        stacked, full_weight, contract_last, preferred_element_type=jnp.float32
    )
    half_width = model_width // lax.axis_size("head")
    first_col = lax.axis_index("head") * half_width
    grad_share = lax.psum_scatter(
        partial_grad.astype(jnp.bfloat16), "head", scatter_dimension=1, tiled=True
    ).astype(jnp.float32)
    normed_share = lax.dynamic_slice_in_dim(normed, first_col, half_width, 1)
    stretch_share = lax.dynamic_slice_in_dim(stretch, first_col, half_width, 0)
    adjoint_share = lax.dynamic_slice_in_dim(adjoint_rows, first_col, half_width, 1)
    grad_scaled = grad_share * (1.0 + stretch_share)
    row_sums = jnp.stack(
        [jnp.sum(grad_scaled, axis=-1), jnp.sum(grad_scaled * normed_share, axis=-1)], axis=-1
    )
    row_sums = lax.psum(row_sums, "head")
    grad_state = inv_std * (
        grad_scaled - row_sums[:, 0:1] / model_width - normed_share * row_sums[:, 1:2] / model_width
    )
    pulled = clip_scale * adjoint_share + grad_state
    return pulled[None]


def solution(mesh):
    in_specs = (
        P("dp", "seq", None),
        P("dp", "seq", None),
        P("dp", "seq", None, "head"),
        P("dp"),
        P("dp"),
        P(),
        P("dp", None, "head"),
        P(),
        P("head", "dp"),
    )
    out_specs = P("dp", "seq", "head")
    by_head = mesh.shape["seq"] == 4 and mesh.shape["dp"] == 4 and mesh.shape["head"] == 2
    shards = shards_by_head if by_head else shards_by_row
    return jax.shard_map(shards, mesh=mesh, in_specs=in_specs, out_specs=out_specs, check_vma=False)
```

```python
import functools

import jax
import jax.numpy as jnp
from jax import lax
from jax.experimental import pallas as pl
from jax.experimental.pallas import tpu as pltpu
from jax.sharding import PartitionSpec as P

HD = 64
GRANT = 60 * 1024 * 1024
SMALL_GRANT = 24 * 1024 * 1024
EXTRA = 128
NT = (((1,), (1,)), ((), ()))
NN = (((1,), (0,)), ((), ()))


def line_ring(count):
    return [0] + list(range(1, count, 2)) + [i for i in range(count - 1, 0, -1) if i % 2 == 0]


def ring_pairs(order):
    return [(order[i], order[(i + 1) % len(order)]) for i in range(len(order))]


def ring_place(order, index):
    place = jnp.int32(0)
    for position, member in enumerate(order):
        place = jnp.where(index == member, jnp.int32(position), place)
    return place


def ring_member(order, place):
    member = jnp.int32(order[0])
    for position, value in enumerate(order):
        member = jnp.where(place == position, jnp.int32(value), member)
    return member


def dot(a, b, dims):
    return lax.dot_general(a, b, dims, preferred_element_type=jnp.float32)


def inverse_rms(raw):
    return lax.rsqrt(jnp.mean(raw * raw, axis=-1, keepdims=True) + 1e-06)


def norm_backward(raw, cotangent, gains):
    inverse = inverse_rms(raw)
    scaled = cotangent.astype(jnp.float32) * gains
    return (
        scaled * inverse
        - raw * jnp.mean(scaled * raw, axis=-1, keepdims=True) * (inverse * inverse * inverse)
    )


def whole_tiles(columns):
    return -(-columns // 128) * 128


def spec(space):
    return pl.BlockSpec(memory_space=space)


def text_columns(text, part):
    rows = text[...].astype(jnp.float32)[:, part, :]
    return [rows[:, c * EXTRA : (c + 1) * EXTRA] for c in range(rows.shape[1] // EXTRA)]


def extra_columns(blocks, rows):
    filled = sum(one.shape[0] for one in blocks)
    blocks = blocks + [jnp.zeros((rows - filled, EXTRA), jnp.float32)]
    return jnp.concatenate(blocks, axis=0).astype(jnp.bfloat16)


def first_kernel(step, core, states, table, adjoint, text, out, rows_out, extra_out):
    rows = [table[c, pl.ds(step[0], 1), :] for c in range(3)]
    widened = states[...].astype(jnp.float32)
    centered = widened - jnp.mean(widened, axis=-1, keepdims=True)
    inv_std = lax.rsqrt(jnp.mean(centered * centered, axis=-1, keepdims=True) + 1e-06)
    half, width = states.shape
    out[:, :width] = (centered * inv_std * (1.0 + rows[1]) + rows[0]).astype(jnp.bfloat16)
    for c in range(3):
        rows_out[c : c + 1, :] = rows[c]
    squares = jnp.sum(adjoint[...] * adjoint[...], axis=0, keepdims=True)
    squares = jnp.sum(squares, axis=1, keepdims=True)
    terms = []
    for n in range(3):
        terms.append(squares.astype(jnp.bfloat16).astype(jnp.float32))
        squares = squares - terms[-1]
    lane = lax.broadcasted_iota(jnp.int32, (8, EXTRA), 1)
    sums = jnp.where(lane == 0, terms[0], jnp.where(lane == 1, terms[1], jnp.where(lane == 2, terms[2], 0.0)))
    extra = extra_columns(text_columns(text, 0) + [sums], half)
    out[:, width:] = extra
    extra_out[...] = extra


def first_call(step, core, states, table, adjoint, text):
    rows, width = states.shape
    half = rows // 2
    whole = lambda *shape: pl.BlockSpec(shape, lambda i, step, core: (0,) * len(shape))
    return pl.pallas_call(
        first_kernel,
        out_shape=(
            jax.ShapeDtypeStruct((half, width + EXTRA), jnp.bfloat16),
            jax.ShapeDtypeStruct((8, width), jnp.float32),
            jax.ShapeDtypeStruct((half, EXTRA), jnp.bfloat16),
        ),
        grid_spec=pltpu.PrefetchScalarGridSpec(
            num_scalar_prefetch=2,
            grid=(1,),
            in_specs=[
                pl.BlockSpec((half, width), lambda i, step, core: (core[0], 0)),
                whole(*table.shape),
                whole(*adjoint.shape),
                whole(*text.shape),
            ],
            out_specs=(whole(half, width + EXTRA), whole(8, width), whole(half, EXTRA)),
        ),
        compiler_params=pltpu.CompilerParams(vmem_limit_bytes=GRANT),
        cost_estimate=pl.CostEstimate(flops=8 * half * width, bytes_accessed=16 * half * width, transcendentals=0),
    )(step, core, states, table, adjoint, text)


def pick_half(core, rows):
    half = rows.shape[1] // 2
    return jnp.where(core == 0, rows[:, :half], rows[:, half:])


def modulate_kernel(core, states, table_rows, extra, out, normed_out, stretch_out, inv_out):
    widened = states[...].astype(jnp.float32)
    centered = widened - jnp.mean(widened, axis=-1, keepdims=True)
    inv_std = lax.rsqrt(jnp.mean(centered * centered, axis=-1, keepdims=True) + 1e-06)
    normed = centered * inv_std
    scale = 1.0 + table_rows[1:2, :]
    rows, width = states.shape
    out[:, :width] = (normed * scale + table_rows[0:1, :]).astype(jnp.bfloat16)
    for n in range(2):
        out[n * rows // 2 : (n + 1) * rows // 2, width:] = extra[...]
    normed_out[...] = pick_half(core[0], normed)
    stretch_out[...] = pick_half(core[0], scale)
    inv_out[...] = jnp.broadcast_to(inv_std, inv_out.shape)


def cotangent_kernel(limit, core, adjoint, table_rows, text, extra, previous, following, opposite, out, half_out, base_out):
    quarter = opposite.shape[0]
    first = 2 * quarter - opposite.shape[0]
    row = 8 * (text.shape[2] // EXTRA)
    squares = None
    for terms in (extra[...], previous[...], following[...]):
        terms = terms.astype(jnp.float32)[row : row + 1, :]
        squares = terms if squares is None else squares + terms
    squares = squares + opposite[...].astype(jnp.float32)[row - first : row - first + 1, :]
    squares = jnp.sum(squares, axis=1, keepdims=True)
    clip_scale = jnp.minimum(1.0, limit / jnp.sqrt(squares + 1e-06))
    gating = table_rows[2:3, :]
    clipped = clip_scale * adjoint[...]
    rows, width = adjoint.shape
    half = rows // 2
    columns = extra_columns(text_columns(text, 1), half)
    out[:, :width] = (gating * clipped).astype(jnp.bfloat16)
    for n in range(2):
        out[n * half : (n + 1) * half, width:] = columns
    base_out[...] = pick_half(core[0], clipped)
    own = adjoint[pl.ds(pl.multiple_of(core[0] * half, 8), half), :]
    half_out[:, :width] = (gating * (clip_scale * own)).astype(jnp.bfloat16)
    half_out[:, width:] = columns


def cotangent_call(limit, core, adjoint, table_rows, text, extra, previous, following, opposite):
    rows, width = adjoint.shape
    bf16 = jnp.bfloat16
    block = width // EXTRA
    whole = lambda one: pl.BlockSpec(one.shape, lambda i, core: (0,) * one.ndim)
    tail = lambda one: pl.BlockSpec((one.shape[0], EXTRA), lambda i, core: (0, block))
    outs = (
        jax.ShapeDtypeStruct((rows, width + EXTRA), bf16),
        jax.ShapeDtypeStruct((rows // 2, width + EXTRA), bf16),
        jax.ShapeDtypeStruct((rows, width // 2), jnp.float32),
    )
    return pl.pallas_call(
        functools.partial(cotangent_kernel, limit),
        out_shape=outs,
        grid_spec=pltpu.PrefetchScalarGridSpec(
            num_scalar_prefetch=1,
            grid=(1,),
            in_specs=[whole(adjoint), whole(table_rows), whole(text), whole(extra)]
            + [tail(one) for one in (previous, following, opposite)],
            out_specs=tuple(whole(one) for one in outs),
        ),
        compiler_params=pltpu.CompilerParams(vmem_limit_bytes=SMALL_GRANT),
        cost_estimate=pl.CostEstimate(flops=4 * rows * width, bytes_accessed=12 * rows * width, transcendentals=0),
    )(core, adjoint, table_rows, text, extra, previous, following, opposite)


class Copies:
    def __init__(self, sems):
        self.sems = sems
        self.count = 0

    def start(self, source, target):
        copy = pltpu.make_async_copy(source, target, self.sems.at[self.count])
        copy.start()
        self.count += 1
        return copy

    def weights(self, scalars, w_in, w_all, shard, first=0):
        half = shard // 2
        places = [(1, 0, shard), (2, 0, shard), (3, 0, shard), (4, 0, half), (4, half, half)]
        columns = w_in[0].shape[1] - first
        copies = []
        for n, piece in enumerate(w_in):
            k, offset, size = places[n % 5]
            there = pl.ds(pl.multiple_of(scalars[k] * shard + offset, 16), size)
            target = w_all.at[there, pl.ds(n // 5 * columns, columns)]
            copies.append(self.start(piece.at[:, pl.ds(first, columns)], target))
        return copies

    def rows(self, core, pieces, target, rows):
        half, quarter = rows // 2, rows // 4
        copies = [self.start(pieces[0], target.at[pl.ds(0, rows)])]
        places = [(rows, half), (3 * rows, half), (2 * rows, quarter), (2 * rows + quarter, quarter)]
        for n, (first, size) in enumerate(places):
            for m, holder in enumerate((core, 1 - core)):
                there = pl.ds(pl.multiple_of(first + holder * half, 16), size)
                copies.append(self.start(pieces[1 + 2 * n + m], target.at[there]))
        return copies


def window_heads(scalars, count, rows, text_dev, gathered, width, extra, text, text_t=None):
    half = rows // 2
    for k in range(count):
        there = pl.ds(pl.multiple_of(k * rows + scalars[0] * half, 16), half)
        extra[k] = gathered[there, width:].astype(jnp.float32)
    for i in range(text.shape[0]):
        head = scalars[5] + i
        first = pl.ds(pl.multiple_of(head // 2 * text_dev, 8), text_dev)
        found = jnp.concatenate([extra[k, first, :] for k in range(count)], axis=0)
        found = jnp.where(head % 2 == 0, found[:, :HD], found[:, HD:])
        text[i] = found.astype(jnp.bfloat16)
        if text_t is not None:
            text_t[i] = found.T.astype(jnp.bfloat16)


def project_kernel(slots, count, rows, shard, width, text_dev, scalars, gain, *refs):
    refs = list(refs)
    take = lambda n: [refs.pop(0) for _ in range(n)]
    mod_in = take(9)
    w_in = take(5)
    q_all, k_all, v_all, k_t, raw_q, raw_k, text, text_t, w_keep, w_give = take(10)
    w_all, mod_all, sems, extra = take(4)
    inner = slots * HD
    core = scalars[0]
    copies = Copies(sems)
    w_copies = copies.weights(scalars, w_in, w_all, shard)
    row_copies = copies.rows(core, mod_in, mod_all, rows)

    gain_q = gain[0:1, :]
    gain_k = gain[1:2, :]
    score_scale = HD ** (-0.5)
    for copy in w_copies:
        copy.wait()
    half = width // 2
    columns = pl.ds(0, w_keep.shape[1])
    half_copies = [
        copies.start(w_all.at[pl.ds(pl.multiple_of(holder * half, 16), half), columns], target)
        for holder, target in ((core, w_keep), (1 - core, w_give))
    ]
    for copy in row_copies:
        copy.wait()
    window_heads(scalars, count, rows, text_dev, mod_all, width, extra, text, text_t)
    span = 2 * rows
    for b in range(count // 2):
        here = slice(b * span, (b + 1) * span)
        projected = jnp.dot(
            mod_all[here, :width], w_all[:, : 3 * inner], preferred_element_type=jnp.float32
        )
        for i in range(slots):
            query = projected[:, i * HD : (i + 1) * HD]
            key = projected[:, inner + i * HD : inner + (i + 1) * HD]
            value = projected[:, 2 * inner + i * HD : 2 * inner + (i + 1) * HD]
            raw_q[i, here, :] = query
            raw_k[i, here, :] = key
            query = query * inverse_rms(query) * gain_q
            q_all[i, here, :] = (query * score_scale).astype(jnp.bfloat16)
            key = key * inverse_rms(key) * gain_k
            k_all[i, here, :] = key.astype(jnp.bfloat16)
            k_t[i, :, here] = key.T.astype(jnp.bfloat16)
            v_all[i, here, :] = value.astype(jnp.bfloat16)
    for copy in half_copies:
        copy.wait()


def attend_kernel(slots, count, rows, shard, width, text_dev, first_column, scalars, gain, *refs):
    refs = list(refs)
    take = lambda n: [refs.pop(0) for _ in range(n)]
    projected = take(10)
    cot_in = take(9)
    w_in = take(5)
    mine_out, theirs_out, rest_out = take(3)
    w_out, cot_all, sems, extra, values_text = take(5)
    d_all, back_q, back_k, back_v, stacked = take(5)
    q_all, k_all, v_all, k_t, raw_q, raw_k, text, text_t, w_keep, w_give = refs
    inner = slots * HD
    tokens = rows * count
    core = scalars[0]
    copies = Copies(sems)
    w_copies = copies.weights(scalars, w_in, w_out, shard, first_column)
    row_copies = copies.rows(core, cot_in, cot_all, rows)
    local_copies = [copies.start(*one) for one in zip(projected, refs)]
    gain_q = gain[0:1, :]
    gain_k = gain[1:2, :]
    score_scale = HD ** (-0.5)
    span = 2 * rows

    text_rows = count * text_dev
    row = lax.broadcasted_iota(jnp.int32, (text_rows, span), 0)
    text_id = row
    for k in range(count):
        inside = (row >= k * text_dev) & (row < (k + 1) * text_dev)
        text_id = jnp.where(inside, row + (scalars[7 + k] - k) * text_dev, text_id)
    bias = jnp.where(text_id < scalars[6], 0.0, -1e30)
    stacked[:, 3 * inner :] = jnp.zeros((tokens, stacked.shape[1] - 3 * inner), jnp.float32)

    for copy in w_copies:
        copy.wait()
    arrivals = [row_copies[:3], row_copies[3:]]
    for b in range(count // 2):
        for copy in arrivals[b]:
            copy.wait()
        here = slice(b * span, (b + 1) * span)
        out_grad = jnp.dot(cot_all[here, :width], w_out[...], preferred_element_type=jnp.float32)
        out_grad = out_grad[:, out_grad.shape[1] - inner :]
        for i in range(slots):
            d_all[i, here, :] = out_grad[:, i * HD : (i + 1) * HD].astype(jnp.bfloat16)
    window_heads(scalars, count, rows, text_dev, cot_all, width, extra, values_text)
    for copy in local_copies[:8]:
        copy.wait()

    @pl.loop(0, slots)
    def attend(i):
        grad_k, grad_v = 0.0, 0.0
        for b in range(count // 2):
            here = slice(b * span, (b + 1) * span)
            query = q_all[i, here, :]
            grad = d_all[i, here, :]
            scores = dot(k_all[i], query, NT)
            text_scores = dot(text[i], query, NT) + bias
            col_max = jnp.maximum(
                jnp.max(scores, axis=0, keepdims=True), jnp.max(text_scores, axis=0, keepdims=True)
            )
            exps = jnp.exp(scores - col_max)
            text_exps = jnp.exp(text_scores - col_max)
            total = jnp.sum(exps, axis=0, keepdims=True) + jnp.sum(text_exps, axis=0, keepdims=True)
            inverse = 1.0 / total
            grad_w = dot(v_all[i], grad, NT)
            text_grad_w = dot(values_text[i], grad, NT)
            delta = inverse * (
                jnp.sum(exps * grad_w, axis=0, keepdims=True)
                + jnp.sum(text_exps * text_grad_w, axis=0, keepdims=True)
            )
            weights = exps * inverse
            grad_s = (weights * (grad_w - delta)).astype(jnp.bfloat16)
            text_grad_s = (text_exps * inverse * (text_grad_w - delta)).astype(jnp.bfloat16)
            grad_k += dot(grad_s, query, NN)
            grad_v += dot(weights.astype(jnp.bfloat16), grad, NN)
            grad_q = dot(k_t[i], grad_s, NN) + dot(text_t[i], text_grad_s, NN)
            grad_q = (grad_q.T * score_scale).astype(jnp.bfloat16)
            back_q[i, here, :] = norm_backward(raw_q[i, here, :], grad_q, gain_q)
        back_k[i] = norm_backward(raw_k[i], grad_k.astype(jnp.bfloat16), gain_k)
        back_v[i] = grad_v

    for i in range(slots):
        valid = scalars[7 + count + i] > 0
        for n, part in enumerate((back_q, back_k, back_v)):
            there = n * inner + i * HD
            stacked[:, there : there + HD] = jnp.where(valid, part[i], 0.0)
    first = stacked[rows : 2 * rows, :].astype(jnp.bfloat16)
    rest_out[: (count - 2) * rows, :] = stacked[2 * rows :, :].astype(jnp.bfloat16)
    rest_out[(count - 2) * rows :, :] = stacked[:rows, :].astype(jnp.bfloat16)
    for copy in local_copies[8:]:
        copy.wait()
    theirs_out[...] = dot(first, w_give[...], NT).astype(jnp.bfloat16)
    mine_out[...] = dot(first, w_keep[...], NT)


def project_call(scalars, gain, mod, weights, slots, rows, text_dev, count):
    shard = weights[0].shape[0]
    columns = 4 * slots * HD
    width = mod[0].shape[1] - EXTRA
    tokens = rows * count
    text_rows = text_dev * count
    f32, bf16 = jnp.float32, jnp.bfloat16
    vmem, hbm = spec(pltpu.VMEM), spec(pl.ANY)
    by_token = (slots, tokens, HD)
    shapes = [(by_token, bf16)] * 3 + [((slots, HD, tokens), bf16)] + [(by_token, f32)] * 2
    shapes += [((slots, text_rows, HD), bf16), ((slots, HD, text_rows), bf16)]
    shapes += [((width // 2, whole_tiles(3 * slots * HD)), bf16)] * 2
    return pl.pallas_call(
        functools.partial(project_kernel, slots, count, rows, shard, width, text_dev),
        out_shape=tuple(jax.ShapeDtypeStruct(*one) for one in shapes),
        in_specs=[spec(pltpu.SMEM), vmem] + [hbm] * (len(mod) + len(weights)),
        out_specs=(vmem,) * (len(shapes) - 2) + (hbm,) * 2,
        scratch_shapes=[
            pltpu.VMEM((width, columns), bf16),
            pltpu.VMEM((tokens, width + EXTRA), bf16),
            pltpu.SemaphoreType.DMA((len(mod) + len(weights) + 2,)),
            pltpu.VMEM((count, rows // 2, EXTRA), f32),
        ],
        compiler_params=pltpu.CompilerParams(vmem_limit_bytes=GRANT),
        cost_estimate=pl.CostEstimate(
            flops=2 * tokens * width * 3 * slots * HD,
            bytes_accessed=2 * (tokens * width + columns * width) + 4 * tokens * columns,
            transcendentals=0,
        ),
    )(scalars, gain, *mod, *weights)


def attend_call(scalars, gain, operands, cot, weights, slots, rows, text_dev):
    count = operands[0].shape[1] // rows
    shard, columns = weights[0].shape
    width = cot[0].shape[1] - EXTRA
    tokens = rows * count
    inner = slots * HD
    stacked = whole_tiles(3 * inner)
    first = (columns - inner) // 128 * 128
    f32, bf16 = jnp.float32, jnp.bfloat16
    vmem, hbm = spec(pltpu.VMEM), spec(pl.ANY)
    by_token = (slots, tokens, HD)
    shapes = [((rows, width // 2), f32), ((rows, width // 2), bf16), ((tokens - rows, stacked), bf16)]
    return pl.pallas_call(
        functools.partial(attend_kernel, slots, count, rows, shard, width, text_dev, first),
        out_shape=tuple(jax.ShapeDtypeStruct(*one) for one in shapes),
        in_specs=[spec(pltpu.SMEM), vmem] + [hbm] * (len(operands) + len(cot) + len(weights)),
        out_specs=(vmem,) * len(shapes),
        scratch_shapes=[
            pltpu.VMEM((width, columns - first), bf16),
            pltpu.VMEM((tokens, width + EXTRA), bf16),
            pltpu.SemaphoreType.DMA((len(operands) + len(cot) + len(weights),)),
            pltpu.VMEM((count, rows // 2, EXTRA), f32),
            pltpu.VMEM((slots, text_dev * count, HD), bf16),
            pltpu.VMEM(by_token, bf16),
        ]
        + [pltpu.VMEM(by_token, f32)] * 3
        + [pltpu.VMEM((tokens, stacked), f32)]
        + [pltpu.VMEM(one.shape, one.dtype) for one in operands],
        compiler_params=pltpu.CompilerParams(vmem_limit_bytes=GRANT),
        cost_estimate=pl.CostEstimate(
            flops=2 * tokens * width * inner + 10 * tokens * tokens * inner,
            bytes_accessed=2 * (tokens * width + columns * width),
            transcendentals=slots * tokens * tokens,
        ),
    )(scalars, gain, *operands, *cot, *weights)


def backward_kernel(own, other, w_own, w_other, *outs):
    total = dot(own[...], w_own[...], NT) + dot(other[...], w_other[...], NT)
    part = outs[0].shape[0]
    for n, out in enumerate(outs):
        out[...] = total[n * part : (n + 1) * part].astype(out.dtype)


def backward_call(own, other, w_own, w_other, part, dtype):
    rows, inner = own.shape
    half = w_own.shape[0]
    vmem = spec(pltpu.VMEM)
    return pl.pallas_call(
        backward_kernel,
        out_shape=(jax.ShapeDtypeStruct((part, half), dtype),) * (rows // part),
        in_specs=[vmem] * 4,
        out_specs=(vmem,) * (rows // part),
        compiler_params=pltpu.CompilerParams(vmem_limit_bytes=SMALL_GRANT),
        cost_estimate=pl.CostEstimate(
            flops=4 * rows * half * inner,
            bytes_accessed=4 * (rows + half) * inner + 4 * rows * half,
            transcendentals=0,
        ),
    )(own, other, w_own, w_other)


def sums_kernel(own_near, own_far, near, far, scale, normed, grad_out, sums_out):
    half = near.shape[0]
    for part, (own, moving) in enumerate(((own_near, near), (own_far, far))):
        here = slice(part * half, (part + 1) * half)
        grad = (own[...] + moving[...].astype(jnp.float32)) * scale[...]
        grad_out[here, :] = grad
        first = jnp.sum(grad, axis=-1, keepdims=True)
        second = jnp.sum(grad * normed[here, :], axis=-1, keepdims=True)
        lane = lax.broadcasted_iota(jnp.int32, (half, 128), 1)
        sums_out[here, :] = jnp.where(lane == 0, first, second)


def last_kernel(width, grad, sums, other, normed, base, inv_std, out):
    total = (sums[...] + other[...]) * (1.0 / width)
    rows = base[...] + inv_std[:, 0:1] * (
        grad[...] - total[:, 0:1] - normed[...] * total[:, 1:2]
    )
    out[...] = rows.T


def local_call(kernel, shapes, scalar_count, *operands):
    vmem = spec(pltpu.VMEM)
    return pl.pallas_call(
        kernel,
        out_shape=tuple(jax.ShapeDtypeStruct(*one) for one in shapes),
        in_specs=[spec(pltpu.SMEM)] * scalar_count + [vmem] * (len(operands) - scalar_count),
        out_specs=(vmem,) * len(shapes),
        compiler_params=pltpu.CompilerParams(vmem_limit_bytes=SMALL_GRANT),
        cost_estimate=pl.CostEstimate(
            flops=sum(one.size for one in operands),
            bytes_accessed=sum(one.size * one.dtype.itemsize for one in operands),
            transcendentals=0,
        ),
    )(*operands)


def shards_by_head(states, adjoint, text_kv, text_len, step_index, modulation, w_qkv, qk_gain, w_out):
    hidden_state = states[0]
    adjoint_rows = adjoint[0]
    tok_count, model_width = hidden_state.shape
    seq_count = lax.axis_size("seq")
    inner_dev = w_qkv.shape[2]
    heads_dev = inner_dev // HD
    shard = w_qkv.shape[0]
    slots = -(-heads_dev // seq_count)
    inner = slots * HD
    half_rows = tok_count // 2
    half_width = model_width // 2
    f32, bf16 = jnp.float32, jnp.bfloat16
    core = lax.axis_index("head").astype(jnp.int32)
    seq_index = lax.axis_index("seq")
    dp_index = lax.axis_index("dp")
    pin = lax.optimization_barrier

    seq_order = line_ring(seq_count)
    seq_place = ring_place(seq_order, seq_index)
    seq_next = ring_pairs(seq_order)
    swap = [(0, 1), (1, 0)]
    along_x = [(p, p ^ 1) for p in range(4)]
    along_y = [(p, p ^ 2) for p in range(4)]

    first = seq_index * heads_dev // seq_count
    stop = (seq_index + 1) * heads_dev // seq_count
    window = jnp.minimum(first, heads_dev - slots)
    valid = [(window + i >= first) & (window + i < stop) for i in range(slots)]
    owners = [ring_member(seq_order, (seq_place - k + seq_count) % seq_count) for k in range(seq_count)]
    w_index = [dp_index, dp_index ^ 1, dp_index ^ 2, dp_index ^ 3]
    scalars = [core] + w_index + [window, text_len[0]] + owners + valid
    scalars = jnp.stack([one.astype(jnp.int32) for one in scalars])

    def step(moving):
        return lax.ppermute(moving, "seq", seq_next)

    def other_core(moving):
        return lax.ppermute(moving, "head", swap)

    def step_back(moving):
        return lax.ppermute(moving, "seq", [(b, a) for a, b in seq_next])

    quarter = half_rows // 2

    def spread(moving):
        return [step(moving), step_back(moving)]

    def pass_on(received):
        return [step(received[0][:quarter]), step_back(received[1][quarter:])]

    mod_half, table_rows, extra = first_call(
        step_index, core[None], hidden_state, modulation.transpose(1, 0, 2), adjoint_rows, text_kv[0]
    )
    mod_near = spread(mod_half)

    w_qkv, w_out, mod_half = pin((w_qkv, w_out, mod_half))
    take = lambda c: lax.dynamic_slice(w_qkv, (0, c, window * HD), (shard, 1, inner))[:, 0]
    own_w = [
        jnp.concatenate(
            [take(0), take(1), take(2), lax.dynamic_slice_in_dim(w_out, window * HD, inner, 0).T], axis=1
        )
    ]
    w_near = [lax.ppermute(part, "dp", pairs) for part in own_w for pairs in (along_x, along_y)]

    text_dev = text_kv.shape[1]
    mod_far = pass_on(mod_near)
    clip_limit = 0.5 * (tok_count * seq_count * model_width) ** 0.5
    cotangent, cot_half, base = cotangent_call(
        clip_limit, scalars, adjoint_rows, table_rows, text_kv[0], extra, *mod_near, mod_far[1]
    )
    cot_half, mod_far[0] = pin((cot_half, mod_far[0]))
    cot_near = spread(cot_half)
    modulated, normed_share, scale_share, inv_std = local_call(
        modulate_kernel,
        [
            ((tok_count, model_width + EXTRA), bf16),
            ((tok_count, half_width), f32),
            ((1, half_width), f32),
            ((tok_count, 128), f32),
        ],
        1,
        core[None],
        hidden_state,
        table_rows,
        extra,
    )
    def pieces(own, received):
        return [own] + [one for moved in received for one in (moved, other_core(moved))]

    mod_pieces = pieces(modulated, mod_near + mod_far)
    *w_near, mod_pieces = pin((*w_near, mod_pieces))
    weights = []
    for n, part in enumerate(own_w):
        w_x, w_y = w_near[2 * n : 2 * n + 2]
        weights += [
            part,
            w_x,
            w_y,
            lax.ppermute(w_x[: shard // 2], "dp", along_y),
            lax.ppermute(w_y[shard // 2 :], "dp", along_x),
        ]
    cot_far = pass_on(cot_near)

    cot_pieces = pieces(cotangent, cot_near)
    *cot_pieces, mod_pieces[-1] = pin((*cot_pieces, mod_pieces[-1]))
    *operands, w_keep, w_give = project_call(
        scalars, qk_gain, mod_pieces, weights, slots, tok_count, text_dev, seq_count
    )
    w_give, cot_far[0], cot_far[1] = pin((w_give, *cot_far))
    cot_pieces += pieces(None, cot_far)[1:]
    given, *cot_pieces = pin((w_give, *cot_pieces))
    w_other = other_core(given)
    mine, theirs, rest = attend_call(
        scalars, qk_gain, operands + [w_keep, w_give], cot_pieces, weights, slots, tok_count, text_dev
    )
    first = (mine + other_core(theirs).astype(f32)).astype(bf16)
    moving = [first[:half_rows], first[half_rows:]]
    other_rest = other_core(rest)
    rest, other_rest, *_ = pin((rest, other_rest, *moving))
    own = backward_call(rest, other_rest, w_keep, w_other, half_rows, f32)
    for j in range(2, seq_count):
        moving = [step(part) for part in moving]
        moving = [
            (a + b.astype(f32)).astype(bf16) for a, b in zip(own[2 * (j - 2) : 2 * (j - 1)], moving)
        ]
    moving = [step(part) for part in moving]

    grad_scaled, sums = local_call(
        sums_kernel,
        [((tok_count, half_width), f32), ((tok_count, 128), f32)],
        0,
        *own[-2:],
        *moving,
        scale_share,
        normed_share,
    )
    (pulled,) = local_call(
        functools.partial(last_kernel, model_width),
        [((half_width, tok_count), f32)],
        0,
        grad_scaled,
        sums,
        other_core(sums),
        normed_share,
        base,
        inv_std,
    )
    return pulled.T[None]


def qk_normalize(values, gains):
    inverse = lax.rsqrt(jnp.mean(values * values, axis=-1, keepdims=True) + 1e-06)
    return ((values * inverse * gains).astype(jnp.bfloat16), inverse)


def qk_backward(values, inverse, cotangent, gains):
    scaled = cotangent.astype(jnp.float32) * gains
    return (
        scaled * inverse - values * jnp.mean(scaled * values, axis=-1, keepdims=True) * inverse**3
    )


def shards_by_row(states, adjoint, text_kv, text_len, step_index, modulation, w_qkv, qk_gain, w_out):
    hidden_state = states[0]
    adjoint_rows = adjoint[0]
    tok_count, model_width = hidden_state.shape
    seq_count = lax.axis_size("seq")
    inner_dev = w_qkv.shape[2]
    heads_dev = inner_dev // HD
    score_scale = HD ** (-0.5)
    squares = lax.psum(jnp.sum(adjoint_rows * adjoint_rows), "seq")
    clip_limit = 0.5 * (tok_count * seq_count * model_width) ** 0.5
    clip_scale = jnp.minimum(1.0, clip_limit / jnp.sqrt(squares + 1e-06))
    table_row = lax.dynamic_index_in_dim(modulation, step_index[0], 0, keepdims=False)
    offset_row = table_row[0]
    stretch = table_row[1]
    gating = table_row[2]
    widened = hidden_state.astype(jnp.float32)
    centered = widened - jnp.mean(widened, axis=-1, keepdims=True)
    inv_std = lax.rsqrt(jnp.mean(centered * centered, axis=-1, keepdims=True) + 1e-06)
    normed = centered * inv_std
    modulated = (normed * (1.0 + stretch) + offset_row).astype(jnp.bfloat16)
    cotangent = (gating * (clip_scale * adjoint_rows)).astype(jnp.bfloat16)
    contract_last = (((1,), (1,)), ((), ()))
    full_weight = lax.all_gather(w_qkv, "dp", axis=0, tiled=True).reshape(
        model_width, 3 * inner_dev
    )
    projected = jnp.dot(modulated, full_weight, preferred_element_type=jnp.float32)
    out_raw = lax.dot_general(
        cotangent,
        lax.all_gather(w_out, "dp", axis=1, tiled=True),
        contract_last,
        preferred_element_type=jnp.float32,
    )
    projected = projected.reshape(tok_count, 3, heads_dev, HD)
    queries, query_inv = qk_normalize(projected[:, 0], qk_gain[0])
    own_keys, key_inv = qk_normalize(projected[:, 1], qk_gain[1])
    own_values = projected[:, 2].astype(jnp.bfloat16)
    out_grad = out_raw.astype(jnp.bfloat16).reshape(tok_count, heads_dev, HD)
    text_keys = text_kv[0, :, 0, :]
    text_values = text_kv[0, :, 1, :]
    text_dev = text_keys.shape[0]
    rows_dev = tok_count + text_dev
    key_local = jnp.concatenate([own_keys.reshape(tok_count, inner_dev), text_keys], axis=0)
    value_local = jnp.concatenate([own_values.reshape(tok_count, inner_dev), text_values], axis=0)
    key_all, value_all = (
        lax.all_gather(key_local, "seq", axis=0, tiled=True),
        lax.all_gather(value_local, "seq", axis=0, tiled=True),
    )
    all_rows = rows_dev * seq_count
    row_ids = jnp.arange(all_rows, dtype=jnp.int32)
    owner = row_ids // rows_dev
    within = row_ids % rows_dev
    allowed = (within < tok_count) | (owner * text_dev + within - tok_count < text_len[0])
    group = 1
    while group * 2 * rows_dev <= 512 and seq_count % (group * 2) == 0:
        group = group * 2
    block_rows = group * rows_dev
    block_count = all_rows // block_rows
    key_blocks = key_all.reshape(block_count, block_rows, heads_dev, HD)
    value_blocks = value_all.reshape(block_count, block_rows, heads_dev, HD)
    mask_blocks = allowed.reshape(block_count, block_rows)

    def block_scores(key_block, mask_block):
        scores = (
            jnp.einsum("qhd,khd->qhk", queries, key_block, preferred_element_type=jnp.float32)
            * score_scale
        )
        return jnp.where(mask_block[None, None, :], scores, -1e30)

    def first_pass(carry, block):
        row_max, row_sum, row_dot = carry
        key_block, value_block, mask_block = block
        scores = block_scores(key_block, mask_block)
        new_max = jnp.maximum(row_max, jnp.max(scores, axis=-1))
        rescale = jnp.exp(row_max - new_max)
        exps = jnp.exp(scores - new_max[:, :, None])
        grad_weights = jnp.einsum(
            "qhd,khd->qhk", out_grad, value_block, preferred_element_type=jnp.float32
        )
        return (
            (
                new_max,
                row_sum * rescale + jnp.sum(exps, axis=-1),
                row_dot * rescale + jnp.sum(exps * grad_weights, axis=-1),
            ),
            None,
        )

    start_state = (
        jnp.full((tok_count, heads_dev), -1e30, jnp.float32),
        jnp.zeros((tok_count, heads_dev), jnp.float32),
        jnp.zeros((tok_count, heads_dev), jnp.float32),
    )
    (row_max, row_sum, row_dot), unused = lax.scan(
        first_pass, start_state, (key_blocks, value_blocks, mask_blocks)
    )
    log_total = row_max + jnp.log(row_sum)
    delta_row = row_dot / row_sum

    def second_pass(running, block):
        key_block, value_block, mask_block = block
        weights = jnp.exp(block_scores(key_block, mask_block) - log_total[:, :, None])
        grad_weights = jnp.einsum(
            "qhd,khd->qhk", out_grad, value_block, preferred_element_type=jnp.float32
        )
        grad_scores = (weights * (grad_weights - delta_row[:, :, None])).astype(jnp.bfloat16)
        return (
            running
            + jnp.einsum(
                "qhk,khd->qhd", grad_scores, key_block, preferred_element_type=jnp.float32
            ),
            None,
        )

    query_sum, unused = lax.scan(
        second_pass,
        jnp.zeros((tok_count, heads_dev, HD), jnp.float32),
        (key_blocks, value_blocks, mask_blocks),
    )
    grad_query = (query_sum * score_scale).astype(jnp.bfloat16)
    log_all, delta_all = (
        lax.all_gather(log_total, "seq", axis=0, tiled=True),
        lax.all_gather(delta_row, "seq", axis=0, tiled=True),
    )
    local_ids = jnp.arange(rows_dev, dtype=jnp.int32)
    local_allowed = (local_ids < tok_count) | (
        lax.axis_index("seq") * text_dev + local_ids - tok_count < text_len[0]
    )
    key_three = key_local.reshape(rows_dev, heads_dev, HD)
    value_three = value_local.reshape(rows_dev, heads_dev, HD)
    query_piece = lax.all_gather(queries.reshape(tok_count, inner_dev), "seq", axis=0, tiled=True)
    grad_piece = lax.all_gather(out_grad.reshape(tok_count, inner_dev), "seq", axis=0, tiled=True)
    piece_rows = query_piece.shape[0]
    query_rows = query_piece.reshape(piece_rows, heads_dev, HD)
    grad_rows = grad_piece.reshape(piece_rows, heads_dev, HD)
    scores = (
        jnp.einsum("qhd,khd->qhk", query_rows, key_three, preferred_element_type=jnp.float32)
        * score_scale
    )
    scores = jnp.where(local_allowed[None, None, :], scores, -1e30)
    weights = jnp.exp(scores - log_all[:, :, None])
    grad_weights = jnp.einsum(
        "qhd,khd->qhk", grad_rows, value_three, preferred_element_type=jnp.float32
    )
    grad_scores = (weights * (grad_weights - delta_all[:, :, None])).astype(jnp.bfloat16)
    rounded = weights.astype(jnp.bfloat16)
    key_sum = jnp.einsum(
        "qhk,qhd->khd", grad_scores, query_rows, preferred_element_type=jnp.float32
    )
    value_sum = jnp.einsum("qhk,qhd->khd", rounded, grad_rows, preferred_element_type=jnp.float32)
    key_sum, value_sum = (key_sum, value_sum)
    grad_key = (key_sum[:tok_count] * score_scale).astype(jnp.bfloat16)
    grad_value = value_sum[:tok_count].astype(jnp.bfloat16)
    raw_query = qk_backward(projected[:, 0], query_inv, grad_query, qk_gain[0])
    raw_key = qk_backward(projected[:, 1], key_inv, grad_key, qk_gain[1])
    stacked = jnp.stack([raw_query, raw_key, grad_value.astype(jnp.float32)], axis=1).astype(
        jnp.bfloat16
    )
    stacked = stacked.reshape(tok_count, 3 * inner_dev)
    partial_grad = lax.dot_general(
        stacked, full_weight, contract_last, preferred_element_type=jnp.float32
    )
    half_width = model_width // lax.axis_size("head")
    first_col = lax.axis_index("head") * half_width
    grad_share = lax.psum_scatter(
        partial_grad.astype(jnp.bfloat16), "head", scatter_dimension=1, tiled=True
    ).astype(jnp.float32)
    normed_share = lax.dynamic_slice_in_dim(normed, first_col, half_width, 1)
    stretch_share = lax.dynamic_slice_in_dim(stretch, first_col, half_width, 0)
    adjoint_share = lax.dynamic_slice_in_dim(adjoint_rows, first_col, half_width, 1)
    grad_scaled = grad_share * (1.0 + stretch_share)
    row_sums = jnp.stack(
        [jnp.sum(grad_scaled, axis=-1), jnp.sum(grad_scaled * normed_share, axis=-1)], axis=-1
    )
    row_sums = lax.psum(row_sums, "head")
    grad_state = inv_std * (
        grad_scaled - row_sums[:, 0:1] / model_width - normed_share * row_sums[:, 1:2] / model_width
    )
    pulled = clip_scale * adjoint_share + grad_state
    return pulled[None]


def solution(mesh):
    in_specs = (
        P("dp", "seq", None),
        P("dp", "seq", None),
        P("dp", "seq", None, "head"),
        P("dp"),
        P("dp"),
        P(),
        P("dp", None, "head"),
        P(),
        P("head", "dp"),
    )
    out_specs = P("dp", "seq", "head")
    by_head = mesh.shape["seq"] == 4 and mesh.shape["dp"] == 4 and mesh.shape["head"] == 2
    shards = shards_by_head if by_head else shards_by_row
    return jax.shard_map(shards, mesh=mesh, in_specs=in_specs, out_specs=out_specs, check_vma=False)
```

```python
import functools

import jax
import jax.numpy as jnp
from jax import lax
from jax.experimental import pallas as pl
from jax.experimental.pallas import tpu as pltpu
from jax.sharding import PartitionSpec as P

HD = 64
GRANT = 60 * 1024 * 1024
SMALL_GRANT = 24 * 1024 * 1024
EXTRA = 128
NT = (((1,), (1,)), ((), ()))
NN = (((1,), (0,)), ((), ()))


def line_ring(count):
    return [0] + list(range(1, count, 2)) + [i for i in range(count - 1, 0, -1) if i % 2 == 0]


def ring_pairs(order):
    return [(order[i], order[(i + 1) % len(order)]) for i in range(len(order))]


def ring_place(order, index):
    place = jnp.int32(0)
    for position, member in enumerate(order):
        place = jnp.where(index == member, jnp.int32(position), place)
    return place


def ring_member(order, place):
    member = jnp.int32(order[0])
    for position, value in enumerate(order):
        member = jnp.where(place == position, jnp.int32(value), member)
    return member


def dot(a, b, dims):
    return lax.dot_general(a, b, dims, preferred_element_type=jnp.float32)


def inverse_rms(raw):
    return lax.rsqrt(jnp.mean(raw * raw, axis=-1, keepdims=True) + 1e-06)


def norm_backward(raw, cotangent, gains):
    inverse = inverse_rms(raw)
    scaled = cotangent.astype(jnp.float32) * gains
    return (
        scaled * inverse
        - raw * jnp.mean(scaled * raw, axis=-1, keepdims=True) * (inverse * inverse * inverse)
    )


def whole_tiles(columns):
    return -(-columns // 128) * 128


def spec(space):
    return pl.BlockSpec(memory_space=space)


def text_columns(text, part):
    rows = text[...].astype(jnp.float32)[:, part, :]
    return [rows[:, c * EXTRA : (c + 1) * EXTRA] for c in range(rows.shape[1] // EXTRA)]


def extra_columns(blocks, rows):
    filled = sum(one.shape[0] for one in blocks)
    blocks = blocks + [jnp.zeros((rows - filled, EXTRA), jnp.float32)]
    return jnp.concatenate(blocks, axis=0).astype(jnp.bfloat16)


def first_kernel(step, core, states, table, adjoint, text, out, rows_out, extra_out, sums_out):
    rows = [table[c, pl.ds(step[0], 1), :] for c in range(3)]
    widened = states[...].astype(jnp.float32)
    centered = widened - jnp.mean(widened, axis=-1, keepdims=True)
    inv_std = lax.rsqrt(jnp.mean(centered * centered, axis=-1, keepdims=True) + 1e-06)
    half, width = states.shape
    out[:, :width] = (centered * inv_std * (1.0 + rows[1]) + rows[0]).astype(jnp.bfloat16)
    for c in range(3):
        rows_out[c : c + 1, :] = rows[c]
    squares = jnp.sum(adjoint[...] * adjoint[...], axis=0, keepdims=True)
    squares = jnp.sum(squares, axis=1, keepdims=True)
    sums_out[...] = jnp.broadcast_to(squares, sums_out.shape)
    terms = []
    for n in range(3):
        terms.append(squares.astype(jnp.bfloat16).astype(jnp.float32))
        squares = squares - terms[-1]
    lane = lax.broadcasted_iota(jnp.int32, (8, EXTRA), 1)
    sums = jnp.where(lane == 0, terms[0], jnp.where(lane == 1, terms[1], jnp.where(lane == 2, terms[2], 0.0)))
    extra = extra_columns(text_columns(text, 0) + [sums], half)
    out[:, width:] = extra
    extra_out[...] = extra


def first_call(step, core, states, table, adjoint, text):
    rows, width = states.shape
    half = rows // 2
    whole = lambda *shape: pl.BlockSpec(shape, lambda i, step, core: (0,) * len(shape))
    return pl.pallas_call(
        first_kernel,
        out_shape=(
            jax.ShapeDtypeStruct((half, width + EXTRA), jnp.bfloat16),
            jax.ShapeDtypeStruct((8, width), jnp.float32),
            jax.ShapeDtypeStruct((half, EXTRA), jnp.bfloat16),
            jax.ShapeDtypeStruct((8, EXTRA), jnp.float32),
        ),
        grid_spec=pltpu.PrefetchScalarGridSpec(
            num_scalar_prefetch=2,
            grid=(1,),
            in_specs=[
                pl.BlockSpec((half, width), lambda i, step, core: (core[0], 0)),
                whole(*table.shape),
                whole(*adjoint.shape),
                whole(*text.shape),
            ],
            out_specs=(whole(half, width + EXTRA), whole(8, width), whole(half, EXTRA), whole(8, EXTRA)),
        ),
        compiler_params=pltpu.CompilerParams(vmem_limit_bytes=GRANT),
        cost_estimate=pl.CostEstimate(flops=8 * half * width, bytes_accessed=16 * half * width, transcendentals=0),
    )(step, core, states, table, adjoint, text)


def pick_half(core, rows):
    half = rows.shape[1] // 2
    return jnp.where(core == 0, rows[:, :half], rows[:, half:])


def modulate_kernel(core, states, table_rows, extra, out, normed_out, stretch_out, inv_out):
    widened = states[...].astype(jnp.float32)
    centered = widened - jnp.mean(widened, axis=-1, keepdims=True)
    inv_std = lax.rsqrt(jnp.mean(centered * centered, axis=-1, keepdims=True) + 1e-06)
    normed = centered * inv_std
    scale = 1.0 + table_rows[1:2, :]
    rows, width = states.shape
    out[:, :width] = (normed * scale + table_rows[0:1, :]).astype(jnp.bfloat16)
    for n in range(2):
        out[n * rows // 2 : (n + 1) * rows // 2, width:] = extra[...]
    normed_out[...] = pick_half(core[0], normed)
    stretch_out[...] = pick_half(core[0], scale)
    inv_out[...] = jnp.broadcast_to(inv_std, inv_out.shape)


def cotangent_kernel(limit, core, adjoint, table_rows, text, extra, previous, following, opposite, out, half_out, base_out):
    row = 8 * (text.shape[2] // EXTRA)
    squares = 0.0
    for terms in (extra, previous, following):
        squares = squares + terms[...].astype(jnp.float32)[row : row + 1, :]
    squares = jnp.sum(squares, axis=1, keepdims=True) + opposite[0:1, 0:1]
    clip_scale = jnp.minimum(1.0, limit / jnp.sqrt(squares + 1e-06))
    gating = table_rows[2:3, :]
    clipped = clip_scale * adjoint[...]
    rows, width = adjoint.shape
    half = rows // 2
    columns = extra_columns(text_columns(text, 1), half)
    out[:, :width] = (gating * clipped).astype(jnp.bfloat16)
    for n in range(2):
        out[n * half : (n + 1) * half, width:] = columns
    base_out[...] = pick_half(core[0], clipped)
    own = adjoint[pl.ds(pl.multiple_of(core[0] * half, 8), half), :]
    half_out[:, :width] = (gating * (clip_scale * own)).astype(jnp.bfloat16)
    half_out[:, width:] = columns


def cotangent_call(limit, core, adjoint, table_rows, text, extra, previous, following, opposite):
    rows, width = adjoint.shape
    bf16 = jnp.bfloat16
    block = width // EXTRA
    whole = lambda one: pl.BlockSpec(one.shape, lambda i, core: (0,) * one.ndim)
    tail = lambda one: pl.BlockSpec((one.shape[0], EXTRA), lambda i, core: (0, block))
    outs = (
        jax.ShapeDtypeStruct((rows, width + EXTRA), bf16),
        jax.ShapeDtypeStruct((rows // 2, width + EXTRA), bf16),
        jax.ShapeDtypeStruct((rows, width // 2), jnp.float32),
    )
    return pl.pallas_call(
        functools.partial(cotangent_kernel, limit),
        out_shape=outs,
        grid_spec=pltpu.PrefetchScalarGridSpec(
            num_scalar_prefetch=1,
            grid=(1,),
            in_specs=[whole(adjoint), whole(table_rows), whole(text), whole(extra)]
            + [tail(one) for one in (previous, following)]
            + [whole(opposite)],
            out_specs=tuple(whole(one) for one in outs),
        ),
        compiler_params=pltpu.CompilerParams(vmem_limit_bytes=GRANT),
        cost_estimate=pl.CostEstimate(flops=4 * rows * width, bytes_accessed=12 * rows * width, transcendentals=0),
    )(core, adjoint, table_rows, text, extra, previous, following, opposite)


class Copies:
    def __init__(self, sems):
        self.sems = sems
        self.count = 0

    def start(self, source, target):
        copy = pltpu.make_async_copy(source, target, self.sems.at[self.count])
        copy.start()
        self.count += 1
        return copy

    def weights(self, scalars, w_in, w_all, shard, first=0):
        columns = w_in[0].shape[1] - first
        return [
            self.start(
                piece.at[:, pl.ds(first, columns)],
                w_all.at[
                    pl.ds(pl.multiple_of(scalars[1 + n % 4] * shard, 16), shard),
                    pl.ds(n // 4 * columns, columns),
                ],
            )
            for n, piece in enumerate(w_in)
        ]

    def rows(self, core, pieces, target, rows, block=0):
        half = rows // 2
        copies, there = [], 0
        pieces = list(pieces)
        while pieces:
            if pieces[0].shape[0] == rows:
                copies.append(self.start(pieces.pop(0), target.at[pl.ds(there, rows)]))
            else:
                for holder in (core, 1 - core):
                    place = pl.ds(pl.multiple_of(there + holder * half, 16), half)
                    copies.append(self.start(pieces.pop(0), target.at[place]))
            there += rows
        return copies


def window_heads(scalars, count, text_dev, extra, text, text_t=None):
    for i in range(text.shape[0]):
        head = scalars[5] + i
        first = pl.ds(pl.multiple_of(head // 2 * text_dev, 8), text_dev)
        found = jnp.concatenate([extra[k, first, :] for k in range(count)], axis=0)
        found = jnp.where(head % 2 == 0, found[:, :HD], found[:, HD:])
        text[i] = found.astype(jnp.bfloat16)
        if text_t is not None:
            text_t[i] = found.T.astype(jnp.bfloat16)


def project_kernel(slots, rows, shard, width, halves, scalars, gain, *refs):
    refs = list(refs)
    take = lambda n: [refs.pop(0) for _ in range(n)]
    w_in = take(8)
    w_all, mod_all, sems = refs[-3:]
    targets = refs[-5:-3] if halves else []
    q_all, k_all, v_all, k_t, raw_q, raw_k = refs[-9 - len(targets) : -3 - len(targets)]
    mod_in = refs[: -9 - len(targets)]
    inner = slots * HD
    core = scalars[0]
    copies = Copies(sems)
    w_copies = copies.weights(scalars, w_in, w_all, shard)
    row_copies = copies.rows(core, mod_in, mod_all, rows)
    gain_q = gain[0:1, :]
    gain_k = gain[1:2, :]
    score_scale = HD ** (-0.5)
    for copy in w_copies:
        copy.wait()
    half = width // 2
    half_copies = [
        copies.start(
            w_all.at[pl.ds(pl.multiple_of(holder * half, 16), half), pl.ds(0, target.shape[1])], target
        )
        for holder, target in zip((core, 1 - core), targets)
    ]
    for copy in row_copies:
        copy.wait()
    projected = jnp.dot(
        mod_all[:, :width], w_all[:, : 3 * inner], preferred_element_type=jnp.float32
    )
    for i in range(slots):
        query = projected[:, i * HD : (i + 1) * HD]
        key = projected[:, inner + i * HD : inner + (i + 1) * HD]
        value = projected[:, 2 * inner + i * HD : 2 * inner + (i + 1) * HD]
        raw_q[i] = query
        raw_k[i] = key
        query = query * inverse_rms(query) * gain_q
        q_all[i] = (query * score_scale).astype(jnp.bfloat16)
        key = key * inverse_rms(key) * gain_k
        k_all[i] = key.astype(jnp.bfloat16)
        k_t[i] = key.T.astype(jnp.bfloat16)
        v_all[i] = value.astype(jnp.bfloat16)
    for copy in half_copies:
        copy.wait()


def attend_kernel(slots, count, rows, shard, width, text_dev, first_column, scalars, gain, *refs):
    refs = list(refs)
    take = lambda n: [refs.pop(0) for _ in range(n)]
    projected = [take(6)]
    halves_in = take(2)
    near_in = take(count - 1)
    own_in = take(1)
    cot_in = take(2 * count - 1)
    w_in = take(4)
    mine_out, theirs_out, rest_out = take(3)
    w_out, cot_all, sems, extra, extra_f32, text, text_t, values_text = take(8)
    d_all, back_q, back_k, back_v, stacked = take(5)
    q_all, k_all, v_all, k_t, raw_q, raw_k, w_keep, w_give = refs
    inner = slots * HD
    tokens = rows * count
    core = scalars[0]
    copies = Copies(sems)
    w_copies = copies.weights(scalars, w_in, w_out, shard, first_column)
    row_copies = copies.rows(core, cot_in, cot_all, rows)
    span = 2 * rows
    columns = pl.ds(width, EXTRA)
    local_copies = [
        copies.start(piece if k == 0 else piece.at[:, columns], extra.at[k])
        for k, piece in enumerate(own_in + near_in)
    ]
    for b, part in enumerate(projected):
        for n, (source, target) in enumerate(zip(part, refs)):
            there = pl.ds(b * tokens, tokens)
            local_copies.append(copies.start(source, target.at[:, :, there] if n == 3 else target.at[:, there]))
    half_copies = [copies.start(*one) for one in zip(halves_in, (w_keep, w_give))]
    gain_q = gain[0:1, :]
    gain_k = gain[1:2, :]
    score_scale = HD ** (-0.5)

    text_rows = count * text_dev
    row = lax.broadcasted_iota(jnp.int32, (text_rows, span), 0)
    text_id = row
    for k in range(count):
        inside = (row >= k * text_dev) & (row < (k + 1) * text_dev)
        text_id = jnp.where(inside, row + (scalars[7 + k] - k) * text_dev, text_id)
    bias = jnp.where(text_id < scalars[6], 0.0, -1e30)
    stacked[:, 3 * inner :] = jnp.zeros((tokens, stacked.shape[1] - 3 * inner), jnp.float32)

    for copy in w_copies:
        copy.wait()
    arrivals = [row_copies[:3], row_copies[3:]]
    for b in range(count // 2):
        for copy in arrivals[b]:
            copy.wait()
        here = slice(b * span, (b + 1) * span)
        out_grad = jnp.dot(cot_all[here, :width], w_out[...], preferred_element_type=jnp.float32)
        out_grad = out_grad[:, out_grad.shape[1] - inner :]
        for i in range(slots):
            d_all[i, here, :] = out_grad[:, i * HD : (i + 1) * HD].astype(jnp.bfloat16)
    for copy in local_copies:
        copy.wait()
    for k in range(count):
        extra_f32[k] = extra[k].astype(jnp.float32)
    window_heads(scalars, count, text_dev, extra_f32, text, text_t)
    for k in range(count):
        there = pl.ds(pl.multiple_of(k * rows + core * (rows // 2), 16), rows // 2)
        extra_f32[k] = cot_all[there, width:].astype(jnp.float32)
    window_heads(scalars, count, text_dev, extra_f32, values_text)

    @pl.loop(0, slots)
    def attend(i):
        grad_k, grad_v = 0.0, 0.0
        for b in range(count // 2):
            here = slice(b * span, (b + 1) * span)
            query = q_all[i, here, :]
            grad = d_all[i, here, :]
            scores = dot(k_all[i], query, NT)
            text_scores = dot(text[i], query, NT) + bias
            col_max = jnp.maximum(
                jnp.max(scores, axis=0, keepdims=True), jnp.max(text_scores, axis=0, keepdims=True)
            )
            exps = jnp.exp(scores - col_max)
            text_exps = jnp.exp(text_scores - col_max)
            total = jnp.sum(exps, axis=0, keepdims=True) + jnp.sum(text_exps, axis=0, keepdims=True)
            inverse = 1.0 / total
            grad_w = dot(v_all[i], grad, NT)
            text_grad_w = dot(values_text[i], grad, NT)
            delta = inverse * (
                jnp.sum(exps * grad_w, axis=0, keepdims=True)
                + jnp.sum(text_exps * text_grad_w, axis=0, keepdims=True)
            )
            weights = exps * inverse
            grad_s = (weights * (grad_w - delta)).astype(jnp.bfloat16)
            text_grad_s = (text_exps * inverse * (text_grad_w - delta)).astype(jnp.bfloat16)
            grad_k += dot(grad_s, query, NN)
            grad_v += dot(weights.astype(jnp.bfloat16), grad, NN)
            grad_q = dot(k_t[i], grad_s, NN) + dot(text_t[i], text_grad_s, NN)
            grad_q = (grad_q.T * score_scale).astype(jnp.bfloat16)
            back_q[i, here, :] = norm_backward(raw_q[i, here, :], grad_q, gain_q)
        back_k[i] = norm_backward(raw_k[i], grad_k.astype(jnp.bfloat16), gain_k)
        back_v[i] = grad_v

    for i in range(slots):
        valid = scalars[7 + count + i] > 0
        for n, part in enumerate((back_q, back_k, back_v)):
            there = n * inner + i * HD
            stacked[:, there : there + HD] = jnp.where(valid, part[i], 0.0)
    first = stacked[rows : 2 * rows, :].astype(jnp.bfloat16)
    rest_out[: (count - 2) * rows, :] = stacked[2 * rows :, :].astype(jnp.bfloat16)
    rest_out[(count - 2) * rows :, :] = stacked[:rows, :].astype(jnp.bfloat16)
    for copy in half_copies:
        copy.wait()
    theirs_out[...] = dot(first, w_give[...], NT).astype(jnp.bfloat16)
    mine_out[...] = dot(first, w_keep[...], NT)


def project_call(scalars, gain, mod, weights, slots, rows, tokens, halves):
    shard = weights[0].shape[0]
    columns = 4 * slots * HD
    width = mod[0].shape[1] - EXTRA
    f32, bf16 = jnp.float32, jnp.bfloat16
    vmem, hbm = spec(pltpu.VMEM), spec(pl.ANY)
    by_token = (slots, tokens, HD)
    shapes = [(by_token, bf16)] * 3 + [((slots, HD, tokens), bf16)] + [(by_token, f32)] * 2
    specs = [vmem] * len(shapes)
    if halves:
        shapes += [((width // 2, whole_tiles(3 * slots * HD)), bf16)] * 2
        specs += [hbm] * 2
    return pl.pallas_call(
        functools.partial(project_kernel, slots, rows, shard, width, halves),
        out_shape=tuple(jax.ShapeDtypeStruct(*one) for one in shapes),
        in_specs=[spec(pltpu.SMEM), vmem] + [hbm] * (len(mod) + len(weights)),
        out_specs=tuple(specs),
        scratch_shapes=[
            pltpu.VMEM((width, columns), bf16),
            pltpu.VMEM((tokens, width + EXTRA), bf16),
            pltpu.SemaphoreType.DMA((len(mod) + len(weights) + 2,)),
        ],
        compiler_params=pltpu.CompilerParams(vmem_limit_bytes=GRANT),
        cost_estimate=pl.CostEstimate(
            flops=2 * tokens * width * 3 * slots * HD,
            bytes_accessed=2 * (tokens * width + columns * width) + 4 * tokens * columns,
            transcendentals=0,
        ),
    )(scalars, gain, *weights, *mod)


def attend_call(scalars, gain, projected, halves, near, own, cot, weights, slots, rows, text_dev):
    count = len(near) + 1
    shard, columns = weights[0].shape
    width = cot[0].shape[1] - EXTRA
    tokens = rows * count
    inner = slots * HD
    stacked = whole_tiles(3 * inner)
    first = (columns - inner) // 128 * 128
    f32, bf16 = jnp.float32, jnp.bfloat16
    vmem, hbm = spec(pltpu.VMEM), spec(pl.ANY)
    by_token = (slots, tokens, HD)
    text_rows = text_dev * count
    shapes = [((rows, width // 2), f32), ((rows, width // 2), bf16), ((tokens - rows, stacked), bf16)]
    operands = [one for part in projected for one in part] + list(halves) + list(near) + [own]
    operands += list(cot) + list(weights)
    return pl.pallas_call(
        functools.partial(attend_kernel, slots, count, rows, shard, width, text_dev, first),
        out_shape=tuple(jax.ShapeDtypeStruct(*one) for one in shapes),
        in_specs=[spec(pltpu.SMEM), vmem] + [hbm] * len(operands),
        out_specs=(vmem,) * len(shapes),
        scratch_shapes=[
            pltpu.VMEM((width, columns - first), bf16),
            pltpu.VMEM((tokens, width + EXTRA), bf16),
            pltpu.SemaphoreType.DMA((len(operands),)),
            pltpu.VMEM((count, rows // 2, EXTRA), bf16),
            pltpu.VMEM((count, rows // 2, EXTRA), f32),
            pltpu.VMEM((slots, text_rows, HD), bf16),
            pltpu.VMEM((slots, HD, text_rows), bf16),
            pltpu.VMEM((slots, text_rows, HD), bf16),
            pltpu.VMEM(by_token, bf16),
        ]
        + [pltpu.VMEM(by_token, f32)] * 3
        + [pltpu.VMEM((tokens, stacked), f32)]
        + [pltpu.VMEM(by_token, bf16)] * 3
        + [pltpu.VMEM((slots, HD, tokens), bf16)]
        + [pltpu.VMEM(by_token, f32)] * 2
        + [pltpu.VMEM(one.shape, one.dtype) for one in halves],
        compiler_params=pltpu.CompilerParams(vmem_limit_bytes=GRANT),
        cost_estimate=pl.CostEstimate(
            flops=2 * tokens * width * inner + 10 * tokens * tokens * inner,
            bytes_accessed=2 * (tokens * width + columns * width),
            transcendentals=slots * tokens * tokens,
        ),
    )(scalars, gain, *operands)


def backward_kernel(own, other, w_own, w_other, *outs):
    total = dot(own[...], w_own[...], NT) + dot(other[...], w_other[...], NT)
    part = outs[0].shape[0]
    for n, out in enumerate(outs):
        out[...] = total[n * part : (n + 1) * part].astype(out.dtype)


def backward_call(own, other, w_own, w_other, part, dtype):
    rows, inner = own.shape
    half = w_own.shape[0]
    vmem = spec(pltpu.VMEM)
    return pl.pallas_call(
        backward_kernel,
        out_shape=(jax.ShapeDtypeStruct((part, half), dtype),) * (rows // part),
        in_specs=[vmem] * 4,
        out_specs=(vmem,) * (rows // part),
        compiler_params=pltpu.CompilerParams(vmem_limit_bytes=SMALL_GRANT),
        cost_estimate=pl.CostEstimate(
            flops=4 * rows * half * inner,
            bytes_accessed=4 * (rows + half) * inner + 4 * rows * half,
            transcendentals=0,
        ),
    )(own, other, w_own, w_other)


def sums_kernel(own_near, own_far, near, far, scale, normed, grad_out, sums_out):
    half = near.shape[0]
    for part, (own, moving) in enumerate(((own_near, near), (own_far, far))):
        here = slice(part * half, (part + 1) * half)
        grad = (own[...] + moving[...].astype(jnp.float32)) * scale[...]
        grad_out[here, :] = grad
        first = jnp.sum(grad, axis=-1, keepdims=True)
        second = jnp.sum(grad * normed[here, :], axis=-1, keepdims=True)
        lane = lax.broadcasted_iota(jnp.int32, (half, 128), 1)
        sums_out[here, :] = jnp.where(lane == 0, first, second)


def last_kernel(width, grad, sums, other, normed, base, inv_std, out):
    total = (sums[...] + other[...]) * (1.0 / width)
    rows = base[...] + inv_std[:, 0:1] * (
        grad[...] - total[:, 0:1] - normed[...] * total[:, 1:2]
    )
    out[...] = rows.T


def local_call(kernel, shapes, scalar_count, *operands, grant=SMALL_GRANT, passes=1):
    vmem = spec(pltpu.VMEM)
    return pl.pallas_call(
        kernel,
        out_shape=tuple(jax.ShapeDtypeStruct(*one) for one in shapes),
        in_specs=[spec(pltpu.SMEM)] * scalar_count + [vmem] * (len(operands) - scalar_count),
        out_specs=(vmem,) * len(shapes),
        compiler_params=pltpu.CompilerParams(vmem_limit_bytes=grant),
        cost_estimate=pl.CostEstimate(
            flops=sum(one.size for one in operands),
            bytes_accessed=passes * sum(one.size * one.dtype.itemsize for one in operands),
            transcendentals=0,
        ),
    )(*operands)


def shards_by_head(states, adjoint, text_kv, text_len, step_index, modulation, w_qkv, qk_gain, w_out):
    hidden_state = states[0]
    adjoint_rows = adjoint[0]
    tok_count, model_width = hidden_state.shape
    seq_count = lax.axis_size("seq")
    inner_dev = w_qkv.shape[2]
    heads_dev = inner_dev // HD
    shard = w_qkv.shape[0]
    slots = -(-heads_dev // seq_count)
    inner = slots * HD
    half_rows = tok_count // 2
    half_width = model_width // 2
    f32, bf16 = jnp.float32, jnp.bfloat16
    core = lax.axis_index("head").astype(jnp.int32)
    seq_index = lax.axis_index("seq")
    dp_index = lax.axis_index("dp")
    pin = lax.optimization_barrier

    seq_order = line_ring(seq_count)
    seq_place = ring_place(seq_order, seq_index)
    seq_next = ring_pairs(seq_order)
    swap = [(0, 1), (1, 0)]
    first_way = [(2 * p + c, 2 * (p ^ (1 + c)) + c) for p in range(4) for c in range(2)]
    second_way = [(2 * p + c, 2 * (p ^ (2 - c)) + c) for p in range(4) for c in range(2)]

    first = seq_index * heads_dev // seq_count
    stop = (seq_index + 1) * heads_dev // seq_count
    window = jnp.minimum(first, heads_dev - slots)
    valid = [(window + i >= first) & (window + i < stop) for i in range(slots)]
    owners = [ring_member(seq_order, (seq_place - k + seq_count) % seq_count) for k in range(seq_count)]
    w_index = [dp_index, dp_index ^ (1 + core), dp_index ^ (2 - core), dp_index ^ 3]
    scalars = [core] + w_index + [window, text_len[0]] + owners + valid
    scalars = jnp.stack([one.astype(jnp.int32) for one in scalars])

    def step(moving):
        return lax.ppermute(moving, "seq", seq_next)

    def other_core(moving):
        return lax.ppermute(moving, "head", swap)

    def step_back(moving):
        return lax.ppermute(moving, "seq", [(b, a) for a, b in seq_next])

    mod_half, table_rows, extra, sums = first_call(
        step_index, core[None], hidden_state, modulation.transpose(1, 0, 2), adjoint_rows, text_kv[0]
    )
    mod_previous, mod_next = step(mod_half), step_back(mod_half)
    across = [(seq_order[i], seq_order[(i + 2) % 4]) for i in range(4)]
    sums = lax.ppermute(sums, "seq", across)

    w_qkv, w_out, mod_half = pin((w_qkv, w_out, mod_half))
    take = lambda c: lax.dynamic_slice(w_qkv, (0, c, window * HD), (shard, 1, inner))[:, 0]
    own_w = [
        jnp.concatenate([take(0), take(1)], axis=1),
        jnp.concatenate([take(2), lax.dynamic_slice_in_dim(w_out, window * HD, inner, 0).T], axis=1),
    ]
    w_first = [lax.ppermute(part, ("dp", "head"), first_way) for part in own_w]
    w_second = [lax.ppermute(part, ("dp", "head"), second_way) for part in own_w]

    text_dev = text_kv.shape[1]
    mod_opposite = step(mod_previous)
    clip_limit = 0.5 * (tok_count * seq_count * model_width) ** 0.5
    cotangent, cot_half, base = cotangent_call(
        clip_limit, scalars, adjoint_rows, table_rows, text_kv[0], extra, mod_previous, mod_next, sums
    )
    mod_opposite = pin((mod_opposite, cot_half))[0]
    cot_previous, cot_next = step(cot_half), step_back(cot_half)
    modulated, normed_share, scale_share, inv_std = local_call(
        modulate_kernel,
        [
            ((tok_count, model_width + EXTRA), bf16),
            ((tok_count, half_width), f32),
            ((1, half_width), f32),
            ((tok_count, 128), f32),
        ],
        1,
        core[None],
        hidden_state,
        table_rows,
        extra,
        grant=GRANT,
    )
    def both(moved):
        return [moved, other_core(moved)]

    near_pieces = [modulated] + both(mod_previous)
    far_pieces = both(mod_opposite) + both(mod_next)
    w_first, w_second, near_pieces, far_pieces, _ = pin((w_first, w_second, near_pieces, far_pieces, cot_half))
    w_diagonal = [lax.ppermute(part, ("dp", "head"), second_way) for part in w_first]
    weights = [part[n] for n in range(2) for part in (own_w, w_first, w_second, w_diagonal)]

    *projected, w_keep, w_give = project_call(
        scalars, qk_gain, near_pieces + far_pieces, weights, slots, tok_count, seq_count * tok_count, True
    )
    cot_opposite = step(cot_previous)
    cot_pieces = [cotangent] + both(cot_previous) + both(cot_next)
    w_give, cot_opposite, *cot_pieces = pin((w_give, cot_opposite, *cot_pieces))
    cot_pieces = cot_pieces[:3] + both(cot_opposite) + cot_pieces[3:]
    given, *cot_pieces = pin((w_give, *cot_pieces))
    w_other = other_core(given)
    mine, theirs, rest = attend_call(
        scalars,
        qk_gain,
        [projected],
        [w_keep, w_give],
        [mod_previous, mod_opposite, mod_next],
        extra,
        cot_pieces,
        weights[4:],
        slots,
        tok_count,
        text_dev,
    )
    first = (mine + other_core(theirs).astype(f32)).astype(bf16)
    moving = [first[:half_rows], first[half_rows:]]
    other_rest = other_core(rest)
    rest, other_rest, *_ = pin((rest, other_rest, *moving))
    own = backward_call(rest, other_rest, w_keep, w_other, half_rows, f32)
    for j in range(2, seq_count):
        moving = [step(part) for part in moving]
        moving = [
            (a + b.astype(f32)).astype(bf16) for a, b in zip(own[2 * (j - 2) : 2 * (j - 1)], moving)
        ]
    moving = [step(part) for part in moving]

    grad_scaled, sums = local_call(
        sums_kernel,
        [((tok_count, half_width), f32), ((tok_count, 128), f32)],
        0,
        *own[-2:],
        *moving,
        scale_share,
        normed_share,
    )
    (pulled,) = local_call(
        functools.partial(last_kernel, model_width),
        [((half_width, tok_count), f32)],
        0,
        grad_scaled,
        sums,
        other_core(sums),
        normed_share,
        base,
        inv_std,
    )
    return pulled.T[None]


def qk_normalize(values, gains):
    inverse = lax.rsqrt(jnp.mean(values * values, axis=-1, keepdims=True) + 1e-06)
    return ((values * inverse * gains).astype(jnp.bfloat16), inverse)


def qk_backward(values, inverse, cotangent, gains):
    scaled = cotangent.astype(jnp.float32) * gains
    return (
        scaled * inverse - values * jnp.mean(scaled * values, axis=-1, keepdims=True) * inverse**3
    )


def shards_by_row(states, adjoint, text_kv, text_len, step_index, modulation, w_qkv, qk_gain, w_out):
    hidden_state = states[0]
    adjoint_rows = adjoint[0]
    tok_count, model_width = hidden_state.shape
    seq_count = lax.axis_size("seq")
    inner_dev = w_qkv.shape[2]
    heads_dev = inner_dev // HD
    score_scale = HD ** (-0.5)
    squares = lax.psum(jnp.sum(adjoint_rows * adjoint_rows), "seq")
    clip_limit = 0.5 * (tok_count * seq_count * model_width) ** 0.5
    clip_scale = jnp.minimum(1.0, clip_limit / jnp.sqrt(squares + 1e-06))
    table_row = lax.dynamic_index_in_dim(modulation, step_index[0], 0, keepdims=False)
    offset_row = table_row[0]
    stretch = table_row[1]
    gating = table_row[2]
    widened = hidden_state.astype(jnp.float32)
    centered = widened - jnp.mean(widened, axis=-1, keepdims=True)
    inv_std = lax.rsqrt(jnp.mean(centered * centered, axis=-1, keepdims=True) + 1e-06)
    normed = centered * inv_std
    modulated = (normed * (1.0 + stretch) + offset_row).astype(jnp.bfloat16)
    cotangent = (gating * (clip_scale * adjoint_rows)).astype(jnp.bfloat16)
    contract_last = (((1,), (1,)), ((), ()))
    full_weight = lax.all_gather(w_qkv, "dp", axis=0, tiled=True).reshape(
        model_width, 3 * inner_dev
    )
    projected = jnp.dot(modulated, full_weight, preferred_element_type=jnp.float32)
    out_raw = lax.dot_general(
        cotangent,
        lax.all_gather(w_out, "dp", axis=1, tiled=True),
        contract_last,
        preferred_element_type=jnp.float32,
    )
    projected = projected.reshape(tok_count, 3, heads_dev, HD)
    queries, query_inv = qk_normalize(projected[:, 0], qk_gain[0])
    own_keys, key_inv = qk_normalize(projected[:, 1], qk_gain[1])
    own_values = projected[:, 2].astype(jnp.bfloat16)
    out_grad = out_raw.astype(jnp.bfloat16).reshape(tok_count, heads_dev, HD)
    text_keys = text_kv[0, :, 0, :]
    text_values = text_kv[0, :, 1, :]
    text_dev = text_keys.shape[0]
    rows_dev = tok_count + text_dev
    key_local = jnp.concatenate([own_keys.reshape(tok_count, inner_dev), text_keys], axis=0)
    value_local = jnp.concatenate([own_values.reshape(tok_count, inner_dev), text_values], axis=0)
    key_all, value_all = (
        lax.all_gather(key_local, "seq", axis=0, tiled=True),
        lax.all_gather(value_local, "seq", axis=0, tiled=True),
    )
    all_rows = rows_dev * seq_count
    row_ids = jnp.arange(all_rows, dtype=jnp.int32)
    owner = row_ids // rows_dev
    within = row_ids % rows_dev
    allowed = (within < tok_count) | (owner * text_dev + within - tok_count < text_len[0])
    group = 1
    while group * 2 * rows_dev <= 512 and seq_count % (group * 2) == 0:
        group = group * 2
    block_rows = group * rows_dev
    block_count = all_rows // block_rows
    key_blocks = key_all.reshape(block_count, block_rows, heads_dev, HD)
    value_blocks = value_all.reshape(block_count, block_rows, heads_dev, HD)
    mask_blocks = allowed.reshape(block_count, block_rows)

    def block_scores(key_block, mask_block):
        scores = (
            jnp.einsum("qhd,khd->qhk", queries, key_block, preferred_element_type=jnp.float32)
            * score_scale
        )
        return jnp.where(mask_block[None, None, :], scores, -1e30)

    def first_pass(carry, block):
        row_max, row_sum, row_dot = carry
        key_block, value_block, mask_block = block
        scores = block_scores(key_block, mask_block)
        new_max = jnp.maximum(row_max, jnp.max(scores, axis=-1))
        rescale = jnp.exp(row_max - new_max)
        exps = jnp.exp(scores - new_max[:, :, None])
        grad_weights = jnp.einsum(
            "qhd,khd->qhk", out_grad, value_block, preferred_element_type=jnp.float32
        )
        return (
            (
                new_max,
                row_sum * rescale + jnp.sum(exps, axis=-1),
                row_dot * rescale + jnp.sum(exps * grad_weights, axis=-1),
            ),
            None,
        )

    start_state = (
        jnp.full((tok_count, heads_dev), -1e30, jnp.float32),
        jnp.zeros((tok_count, heads_dev), jnp.float32),
        jnp.zeros((tok_count, heads_dev), jnp.float32),
    )
    (row_max, row_sum, row_dot), unused = lax.scan(
        first_pass, start_state, (key_blocks, value_blocks, mask_blocks)
    )
    log_total = row_max + jnp.log(row_sum)
    delta_row = row_dot / row_sum

    def second_pass(running, block):
        key_block, value_block, mask_block = block
        weights = jnp.exp(block_scores(key_block, mask_block) - log_total[:, :, None])
        grad_weights = jnp.einsum(
            "qhd,khd->qhk", out_grad, value_block, preferred_element_type=jnp.float32
        )
        grad_scores = (weights * (grad_weights - delta_row[:, :, None])).astype(jnp.bfloat16)
        return (
            running
            + jnp.einsum(
                "qhk,khd->qhd", grad_scores, key_block, preferred_element_type=jnp.float32
            ),
            None,
        )

    query_sum, unused = lax.scan(
        second_pass,
        jnp.zeros((tok_count, heads_dev, HD), jnp.float32),
        (key_blocks, value_blocks, mask_blocks),
    )
    grad_query = (query_sum * score_scale).astype(jnp.bfloat16)
    log_all, delta_all = (
        lax.all_gather(log_total, "seq", axis=0, tiled=True),
        lax.all_gather(delta_row, "seq", axis=0, tiled=True),
    )
    local_ids = jnp.arange(rows_dev, dtype=jnp.int32)
    local_allowed = (local_ids < tok_count) | (
        lax.axis_index("seq") * text_dev + local_ids - tok_count < text_len[0]
    )
    key_three = key_local.reshape(rows_dev, heads_dev, HD)
    value_three = value_local.reshape(rows_dev, heads_dev, HD)
    query_piece = lax.all_gather(queries.reshape(tok_count, inner_dev), "seq", axis=0, tiled=True)
    grad_piece = lax.all_gather(out_grad.reshape(tok_count, inner_dev), "seq", axis=0, tiled=True)
    piece_rows = query_piece.shape[0]
    query_rows = query_piece.reshape(piece_rows, heads_dev, HD)
    grad_rows = grad_piece.reshape(piece_rows, heads_dev, HD)
    scores = (
        jnp.einsum("qhd,khd->qhk", query_rows, key_three, preferred_element_type=jnp.float32)
        * score_scale
    )
    scores = jnp.where(local_allowed[None, None, :], scores, -1e30)
    weights = jnp.exp(scores - log_all[:, :, None])
    grad_weights = jnp.einsum(
        "qhd,khd->qhk", grad_rows, value_three, preferred_element_type=jnp.float32
    )
    grad_scores = (weights * (grad_weights - delta_all[:, :, None])).astype(jnp.bfloat16)
    rounded = weights.astype(jnp.bfloat16)
    key_sum = jnp.einsum(
        "qhk,qhd->khd", grad_scores, query_rows, preferred_element_type=jnp.float32
    )
    value_sum = jnp.einsum("qhk,qhd->khd", rounded, grad_rows, preferred_element_type=jnp.float32)
    key_sum, value_sum = (key_sum, value_sum)
    grad_key = (key_sum[:tok_count] * score_scale).astype(jnp.bfloat16)
    grad_value = value_sum[:tok_count].astype(jnp.bfloat16)
    raw_query = qk_backward(projected[:, 0], query_inv, grad_query, qk_gain[0])
    raw_key = qk_backward(projected[:, 1], key_inv, grad_key, qk_gain[1])
    stacked = jnp.stack([raw_query, raw_key, grad_value.astype(jnp.float32)], axis=1).astype(
        jnp.bfloat16
    )
    stacked = stacked.reshape(tok_count, 3 * inner_dev)
    partial_grad = lax.dot_general(
        stacked, full_weight, contract_last, preferred_element_type=jnp.float32
    )
    half_width = model_width // lax.axis_size("head")
    first_col = lax.axis_index("head") * half_width
    grad_share = lax.psum_scatter(
        partial_grad.astype(jnp.bfloat16), "head", scatter_dimension=1, tiled=True
    ).astype(jnp.float32)
    normed_share = lax.dynamic_slice_in_dim(normed, first_col, half_width, 1)
    stretch_share = lax.dynamic_slice_in_dim(stretch, first_col, half_width, 0)
    adjoint_share = lax.dynamic_slice_in_dim(adjoint_rows, first_col, half_width, 1)
    grad_scaled = grad_share * (1.0 + stretch_share)
    row_sums = jnp.stack(
        [jnp.sum(grad_scaled, axis=-1), jnp.sum(grad_scaled * normed_share, axis=-1)], axis=-1
    )
    row_sums = lax.psum(row_sums, "head")
    grad_state = inv_std * (
        grad_scaled - row_sums[:, 0:1] / model_width - normed_share * row_sums[:, 1:2] / model_width
    )
    pulled = clip_scale * adjoint_share + grad_state
    return pulled[None]


def solution(mesh):
    in_specs = (
        P("dp", "seq", None),
        P("dp", "seq", None),
        P("dp", "seq", None, "head"),
        P("dp"),
        P("dp"),
        P(),
        P("dp", None, "head"),
        P(),
        P("head", "dp"),
    )
    out_specs = P("dp", "seq", "head")
    by_head = mesh.shape["seq"] == 4 and mesh.shape["dp"] == 4 and mesh.shape["head"] == 2
    shards = shards_by_head if by_head else shards_by_row
    return jax.shard_map(shards, mesh=mesh, in_specs=in_specs, out_specs=out_specs, check_vma=False)
```

```python
import functools

import jax
import jax.numpy as jnp
from jax import lax
from jax.experimental import pallas as pl
from jax.experimental.pallas import tpu as pltpu
from jax.sharding import PartitionSpec as P

HD = 64
GRANT = 60 * 1024 * 1024
SMALL_GRANT = 24 * 1024 * 1024
EXTRA = 128
NT = (((1,), (1,)), ((), ()))
NN = (((1,), (0,)), ((), ()))


def line_ring(count):
    return [0] + list(range(1, count, 2)) + [i for i in range(count - 1, 0, -1) if i % 2 == 0]


def ring_pairs(order):
    return [(order[i], order[(i + 1) % len(order)]) for i in range(len(order))]


def ring_place(order, index):
    place = jnp.int32(0)
    for position, member in enumerate(order):
        place = jnp.where(index == member, jnp.int32(position), place)
    return place


def ring_member(order, place):
    member = jnp.int32(order[0])
    for position, value in enumerate(order):
        member = jnp.where(place == position, jnp.int32(value), member)
    return member


def dot(a, b, dims):
    return lax.dot_general(a, b, dims, preferred_element_type=jnp.float32)


def equal_blocks(columns, block):
    row = lax.broadcasted_iota(jnp.int32, (columns, columns), 0)
    column = lax.broadcasted_iota(jnp.int32, (columns, columns), 1)
    return jnp.where(row // block == column // block, 1.0, 0.0).astype(jnp.bfloat16)


def head_means(values):
    ones = equal_blocks(values.shape[1], HD)
    total = 0.0
    for n in range(3):
        term = values.astype(jnp.bfloat16)
        total = total + dot(term, ones, NN)
        if n < 2:
            values = values - term.astype(jnp.float32)
    return total * (1.0 / HD)


def head_gains(gain, slots):
    return jnp.concatenate([gain[0:1, :]] * slots + [gain[1:2, :]] * slots, axis=1)


def whole_tiles(columns):
    return -(-columns // 128) * 128


def spec(space):
    return pl.BlockSpec(memory_space=space)


def text_columns(text, part):
    rows = text[...].astype(jnp.float32)[:, part, :]
    return [rows[:, c * EXTRA : (c + 1) * EXTRA] for c in range(rows.shape[1] // EXTRA)]


def extra_columns(blocks, rows):
    filled = sum(one.shape[0] for one in blocks)
    blocks = blocks + [jnp.zeros((rows - filled, EXTRA), jnp.float32)]
    return jnp.concatenate(blocks, axis=0).astype(jnp.bfloat16)


def first_kernel(step, core, states, table, adjoint, text, out, rows_out, extra_out):
    rows = [table[c, pl.ds(step[0], 1), :] for c in range(3)]
    widened = states[...].astype(jnp.float32)
    centered = widened - jnp.mean(widened, axis=-1, keepdims=True)
    inv_std = lax.rsqrt(jnp.mean(centered * centered, axis=-1, keepdims=True) + 1e-06)
    half, width = states.shape
    out[:, :width] = (centered * inv_std * (1.0 + rows[1]) + rows[0]).astype(jnp.bfloat16)
    for c in range(3):
        rows_out[c : c + 1, :] = rows[c]
    squares = jnp.sum(adjoint[...] * adjoint[...], axis=0, keepdims=True)
    squares = jnp.sum(squares, axis=1, keepdims=True)
    terms = []
    for n in range(3):
        terms.append(squares.astype(jnp.bfloat16).astype(jnp.float32))
        squares = squares - terms[-1]
    lane = lax.broadcasted_iota(jnp.int32, (8, EXTRA), 1)
    sums = jnp.where(lane == 0, terms[0], jnp.where(lane == 1, terms[1], jnp.where(lane == 2, terms[2], 0.0)))
    extra = extra_columns(text_columns(text, 0) + [sums], half)
    out[:, width:] = extra
    extra_out[...] = extra


def first_call(step, core, states, table, adjoint, text):
    rows, width = states.shape
    half = rows // 2
    whole = lambda *shape: pl.BlockSpec(shape, lambda i, step, core: (0,) * len(shape))
    return pl.pallas_call(
        first_kernel,
        out_shape=(
            jax.ShapeDtypeStruct((half, width + EXTRA), jnp.bfloat16),
            jax.ShapeDtypeStruct((8, width), jnp.float32),
            jax.ShapeDtypeStruct((half, EXTRA), jnp.bfloat16),
        ),
        grid_spec=pltpu.PrefetchScalarGridSpec(
            num_scalar_prefetch=2,
            grid=(1,),
            in_specs=[
                pl.BlockSpec((half, width), lambda i, step, core: (core[0], 0)),
                whole(*table.shape),
                whole(*adjoint.shape),
                whole(*text.shape),
            ],
            out_specs=(whole(half, width + EXTRA), whole(8, width), whole(half, EXTRA)),
        ),
        compiler_params=pltpu.CompilerParams(vmem_limit_bytes=GRANT),
        cost_estimate=pl.CostEstimate(flops=8 * half * width, bytes_accessed=16 * half * width, transcendentals=0),
    )(step, core, states, table, adjoint, text)


def pick_half(core, rows):
    half = rows.shape[1] // 2
    return jnp.where(core == 0, rows[:, :half], rows[:, half:])


def modulate_kernel(core, states, table_rows, extra, out, normed_out, stretch_out, inv_out):
    widened = states[...].astype(jnp.float32)
    centered = widened - jnp.mean(widened, axis=-1, keepdims=True)
    inv_std = lax.rsqrt(jnp.mean(centered * centered, axis=-1, keepdims=True) + 1e-06)
    normed = centered * inv_std
    scale = 1.0 + table_rows[1:2, :]
    rows, width = states.shape
    out[:, :width] = (normed * scale + table_rows[0:1, :]).astype(jnp.bfloat16)
    for n in range(2):
        out[n * rows // 2 : (n + 1) * rows // 2, width:] = extra[...]
    normed_out[...] = pick_half(core[0], normed)
    stretch_out[...] = pick_half(core[0], scale)
    inv_out[...] = jnp.broadcast_to(inv_std, inv_out.shape)


def cotangent_kernel(limit, core, adjoint, table_rows, text, extra, previous, following, opposite, out, half_out, base_out):
    quarter = opposite.shape[0]
    first = 2 * quarter - opposite.shape[0]
    row = 8 * (text.shape[2] // EXTRA)
    squares = None
    for terms in (extra[...], previous[...], following[...]):
        terms = terms.astype(jnp.float32)[row : row + 1, :]
        squares = terms if squares is None else squares + terms
    squares = squares + opposite[...].astype(jnp.float32)[row - first : row - first + 1, :]
    squares = jnp.sum(squares, axis=1, keepdims=True)
    clip_scale = jnp.minimum(1.0, limit / jnp.sqrt(squares + 1e-06))
    gating = table_rows[2:3, :]
    clipped = clip_scale * adjoint[...]
    rows, width = adjoint.shape
    half = rows // 2
    columns = extra_columns(text_columns(text, 1), half)
    out[:, :width] = (gating * clipped).astype(jnp.bfloat16)
    for n in range(2):
        out[n * half : (n + 1) * half, width:] = columns
    base_out[...] = pick_half(core[0], clipped)
    own = adjoint[pl.ds(pl.multiple_of(core[0] * half, 8), half), :]
    half_out[:, :width] = (gating * (clip_scale * own)).astype(jnp.bfloat16)
    half_out[:, width:] = columns


def cotangent_call(limit, core, adjoint, table_rows, text, extra, previous, following, opposite):
    rows, width = adjoint.shape
    bf16 = jnp.bfloat16
    block = width // EXTRA
    whole = lambda one: pl.BlockSpec(one.shape, lambda i, core: (0,) * one.ndim)
    tail = lambda one: pl.BlockSpec((one.shape[0], EXTRA), lambda i, core: (0, block))
    outs = (
        jax.ShapeDtypeStruct((rows, width + EXTRA), bf16),
        jax.ShapeDtypeStruct((rows // 2, width + EXTRA), bf16),
        jax.ShapeDtypeStruct((rows, width // 2), jnp.float32),
    )
    return pl.pallas_call(
        functools.partial(cotangent_kernel, limit),
        out_shape=outs,
        grid_spec=pltpu.PrefetchScalarGridSpec(
            num_scalar_prefetch=1,
            grid=(1,),
            in_specs=[whole(adjoint), whole(table_rows), whole(text), whole(extra)]
            + [tail(one) for one in (previous, following, opposite)],
            out_specs=tuple(whole(one) for one in outs),
        ),
        compiler_params=pltpu.CompilerParams(vmem_limit_bytes=SMALL_GRANT),
        cost_estimate=pl.CostEstimate(flops=4 * rows * width, bytes_accessed=12 * rows * width, transcendentals=0),
    )(core, adjoint, table_rows, text, extra, previous, following, opposite)


class Copies:
    def __init__(self, sems):
        self.sems = sems
        self.count = 0

    def start(self, source, target):
        copy = pltpu.make_async_copy(source, target, self.sems.at[self.count])
        copy.start()
        self.count += 1
        return copy

    def weights(self, scalars, w_in, w_all, shard, first=0):
        half = shard // 2
        places = [(1, 0, shard), (2, 0, shard), (3, 0, shard), (4, 0, half), (4, half, half)]
        columns = w_in[0].shape[1] - first
        copies = []
        for n, piece in enumerate(w_in):
            k, offset, size = places[n % 5]
            there = pl.ds(pl.multiple_of(scalars[k] * shard + offset, 16), size)
            target = w_all.at[there, pl.ds(n // 5 * columns, columns)]
            copies.append(self.start(piece.at[:, pl.ds(first, columns)], target))
        return copies

    def rows(self, core, pieces, target, rows):
        half = rows // 2
        copies = [self.start(pieces[0], target.at[pl.ds(0, rows)])]
        places = [(rows, half), (3 * rows, half)]
        parts = (len(pieces) - 5) // 2
        places += [(2 * rows + n * half // parts, half // parts) for n in range(parts)]
        for n, (first, size) in enumerate(places):
            for m, holder in enumerate((core, 1 - core)):
                there = pl.ds(pl.multiple_of(first + holder * half, 16), size)
                copies.append(self.start(pieces[1 + 2 * n + m], target.at[there]))
        return copies


def window_heads(scalars, count, rows, text_dev, gathered, width, extra, text, text_t=None):
    half = rows // 2
    for k in range(count):
        there = pl.ds(pl.multiple_of(k * rows + scalars[0] * half, 16), half)
        extra[k] = gathered[there, width:].astype(jnp.float32)
    for i in range(text.shape[0]):
        head = scalars[5] + i
        first = pl.ds(pl.multiple_of(head // 2 * text_dev, 8), text_dev)
        found = jnp.concatenate([extra[k, first, :] for k in range(count)], axis=0)
        found = jnp.where(head % 2 == 0, found[:, :HD], found[:, HD:])
        text[i] = found.astype(jnp.bfloat16)
        if text_t is not None:
            text_t[i] = found.T.astype(jnp.bfloat16)


def project_kernel(slots, count, rows, shard, width, text_dev, scalars, gain, *refs):
    refs = list(refs)
    take = lambda n: [refs.pop(0) for _ in range(n)]
    mod_in = take(9)
    w_in = take(5)
    qkv, k_t, raw_all, inv_all, text, text_t, w_keep, w_give = take(8)
    w_all, mod_all, sems, extra = take(4)
    inner = slots * HD
    core = scalars[0]
    copies = Copies(sems)
    w_copies = copies.weights(scalars, w_in, w_all, shard)
    row_copies = copies.rows(core, mod_in, mod_all, rows)

    lane = lax.broadcasted_iota(jnp.int32, (1, 2 * inner), 1)
    gains = head_gains(gain, slots) * jnp.where(lane < inner, HD ** (-0.5), 1.0)
    identity = equal_blocks(inner, 1)
    for copy in w_copies:
        copy.wait()
    half = width // 2
    columns = pl.ds(0, w_keep.shape[1])
    half_copies = [
        copies.start(w_all.at[pl.ds(pl.multiple_of(holder * half, 16), half), columns], target)
        for holder, target in ((core, w_keep), (1 - core, w_give))
    ]
    for copy in row_copies:
        copy.wait()
    window_heads(scalars, count, rows, text_dev, mod_all, width, extra, text, text_t)
    span = 2 * rows
    for b in range(count // 2):
        here = slice(b * span, (b + 1) * span)
        projected = jnp.dot(
            mod_all[here, :width], w_all[:, : 3 * inner], preferred_element_type=jnp.float32
        )
        raw = projected[:, : 2 * inner]
        inverse = lax.rsqrt(head_means(raw * raw) + 1e-06)
        raw_all[here, :] = raw
        inv_all[here, :] = inverse
        qkv[here, : 2 * inner] = (raw * inverse * gains).astype(jnp.bfloat16)
        qkv[here, 2 * inner :] = projected[:, 2 * inner :].astype(jnp.bfloat16)
        k_t[:, here] = dot(identity, qkv[here, inner : 2 * inner], NT).astype(jnp.bfloat16)
    for copy in half_copies:
        copy.wait()


def attend_kernel(slots, count, rows, shard, width, text_dev, first_column, scalars, gain, *refs):
    refs = list(refs)
    take = lambda n: [refs.pop(0) for _ in range(n)]
    projected = take(8)
    cot_in = take(7)
    w_in = take(5)
    mine_out, theirs_out, rest_out = take(3)
    w_out, cot_all, sems, extra, values_text = take(5)
    d_all, grads, stacked = take(3)
    qkv, k_t, raw_all, inv_all, text, text_t, w_keep, w_give = refs
    inner = slots * HD
    tokens = rows * count
    core = scalars[0]
    copies = Copies(sems)
    w_copies = copies.weights(scalars, w_in, w_out, shard, first_column)
    row_copies = copies.rows(core, cot_in, cot_all, rows)
    local_copies = [copies.start(*one) for one in zip(projected, refs)]
    score_scale = HD ** (-0.5)
    span = 2 * rows

    text_rows = count * text_dev
    row = lax.broadcasted_iota(jnp.int32, (text_rows, span), 0)
    text_id = row
    for k in range(count):
        inside = (row >= k * text_dev) & (row < (k + 1) * text_dev)
        text_id = jnp.where(inside, row + (scalars[7 + k] - k) * text_dev, text_id)
    bias = jnp.where(text_id < scalars[6], 0.0, -1e30)

    for copy in w_copies:
        copy.wait()
    arrivals = [row_copies[:3], row_copies[3:]]
    for b in range(count // 2):
        for copy in arrivals[b]:
            copy.wait()
        here = slice(b * span, (b + 1) * span)
        out_grad = jnp.dot(cot_all[here, :width], w_out[...], preferred_element_type=jnp.float32)
        d_all[here, :] = out_grad.astype(jnp.bfloat16)
    window_heads(scalars, count, rows, text_dev, cot_all, width, extra, values_text)
    for copy in local_copies[:6]:
        copy.wait()

    d_first = d_all.shape[1] - inner
    for i in range(slots):
        columns = [slice(n * inner + i * HD, n * inner + (i + 1) * HD) for n in range(3)]
        keys, values = qkv[:, columns[1]], qkv[:, columns[2]]
        keys_t = k_t[i * HD : (i + 1) * HD, :]
        grad_k, grad_v = 0.0, 0.0
        for b in range(count // 2):
            here = slice(b * span, (b + 1) * span)
            query = qkv[here, columns[0]]
            grad = d_all[here, d_first + i * HD : d_first + (i + 1) * HD]
            scores = dot(keys, query, NT)
            text_scores = dot(text[i], query, NT) + bias
            col_max = jnp.maximum(
                jnp.max(scores, axis=0, keepdims=True), jnp.max(text_scores, axis=0, keepdims=True)
            )
            exps = jnp.exp(scores - col_max)
            text_exps = jnp.exp(text_scores - col_max)
            total = jnp.sum(exps, axis=0, keepdims=True) + jnp.sum(text_exps, axis=0, keepdims=True)
            inverse = 1.0 / total
            grad_w = dot(values, grad, NT)
            text_grad_w = dot(values_text[i], grad, NT)
            delta = inverse * (
                jnp.sum(exps * grad_w, axis=0, keepdims=True)
                + jnp.sum(text_exps * text_grad_w, axis=0, keepdims=True)
            )
            weights = exps * inverse
            grad_s = (weights * (grad_w - delta)).astype(jnp.bfloat16)
            text_grad_s = (text_exps * inverse * (text_grad_w - delta)).astype(jnp.bfloat16)
            grad_k += dot(grad_s, query, NN)
            grad_v += dot(weights.astype(jnp.bfloat16), grad, NN)
            grad_q = dot(keys_t, grad_s, NN) + dot(text_t[i], text_grad_s, NN)
            grads[here, columns[0]] = grad_q.T * score_scale
        grads[:, columns[1]] = grad_k
        grads[:, columns[2]] = grad_v

    lane = lax.broadcasted_iota(jnp.int32, (1, inner), 1)
    mine = jnp.zeros((1, inner), jnp.float32)
    for i in range(slots):
        inside = (lane >= i * HD) & (lane < (i + 1) * HD) & (scalars[7 + count + i] > 0)
        mine = jnp.where(inside, 1.0, mine)
    gains = head_gains(gain, slots)
    for b in range(count // 2):
        here = slice(b * span, (b + 1) * span)
        scaled = grads[here, : 2 * inner].astype(jnp.bfloat16).astype(jnp.float32) * gains
        raw, inverse = raw_all[here, :], inv_all[here, :]
        back = scaled * inverse - raw * head_means(scaled * raw) * (inverse * inverse * inverse)
        valid = jnp.concatenate([mine, mine], axis=1) > 0.0
        stacked[here, : 2 * inner] = jnp.where(valid, back, 0.0).astype(jnp.bfloat16)
        back = jnp.where(mine > 0.0, grads[here, 2 * inner :], 0.0).astype(jnp.bfloat16)
        stacked[here, 2 * inner : 3 * inner] = back
    stacked[:, 3 * inner :] = jnp.zeros((tokens, stacked.shape[1] - 3 * inner), jnp.bfloat16)
    first = stacked[rows : 2 * rows, :]
    rest_out[: (count - 2) * rows, :] = stacked[2 * rows :, :]
    rest_out[(count - 2) * rows :, :] = stacked[:rows, :]
    for copy in local_copies[6:]:
        copy.wait()
    theirs_out[...] = dot(first, w_give[...], NT).astype(jnp.bfloat16)
    mine_out[...] = dot(first, w_keep[...], NT)


def project_call(scalars, gain, mod, weights, slots, rows, text_dev, count):
    shard = weights[0].shape[0]
    columns = 4 * slots * HD
    width = mod[0].shape[1] - EXTRA
    tokens = rows * count
    text_rows = text_dev * count
    f32, bf16 = jnp.float32, jnp.bfloat16
    vmem, hbm = spec(pltpu.VMEM), spec(pl.ANY)
    inner = slots * HD
    shapes = [((tokens, 3 * inner), bf16), ((inner, tokens), bf16)] + [((tokens, 2 * inner), f32)] * 2
    shapes += [((slots, text_rows, HD), bf16), ((slots, HD, text_rows), bf16)]
    shapes += [((width // 2, whole_tiles(3 * slots * HD)), bf16)] * 2
    return pl.pallas_call(
        functools.partial(project_kernel, slots, count, rows, shard, width, text_dev),
        out_shape=tuple(jax.ShapeDtypeStruct(*one) for one in shapes),
        in_specs=[spec(pltpu.SMEM), vmem] + [hbm] * (len(mod) + len(weights)),
        out_specs=(vmem,) * (len(shapes) - 2) + (hbm,) * 2,
        scratch_shapes=[
            pltpu.VMEM((width, columns), bf16),
            pltpu.VMEM((tokens, width + EXTRA), bf16),
            pltpu.SemaphoreType.DMA((len(mod) + len(weights) + 2,)),
            pltpu.VMEM((count, rows // 2, EXTRA), f32),
        ],
        compiler_params=pltpu.CompilerParams(vmem_limit_bytes=GRANT),
        cost_estimate=pl.CostEstimate(
            flops=2 * tokens * width * 3 * slots * HD,
            bytes_accessed=2 * (tokens * width + columns * width) + 4 * tokens * columns,
            transcendentals=0,
        ),
    )(scalars, gain, *mod, *weights)


def attend_call(scalars, gain, operands, cot, weights, slots, rows, text_dev):
    count = operands[0].shape[0] // rows
    shard, columns = weights[0].shape
    width = cot[0].shape[1] - EXTRA
    tokens = rows * count
    inner = slots * HD
    stacked = whole_tiles(3 * inner)
    first = (columns - inner) // 128 * 128
    f32, bf16 = jnp.float32, jnp.bfloat16
    vmem, hbm = spec(pltpu.VMEM), spec(pl.ANY)
    shapes = [((rows, width // 2), f32), ((rows, width // 2), bf16), ((tokens - rows, stacked), bf16)]
    return pl.pallas_call(
        functools.partial(attend_kernel, slots, count, rows, shard, width, text_dev, first),
        out_shape=tuple(jax.ShapeDtypeStruct(*one) for one in shapes),
        in_specs=[spec(pltpu.SMEM), vmem] + [hbm] * (len(operands) + len(cot) + len(weights)),
        out_specs=(vmem,) * len(shapes),
        scratch_shapes=[
            pltpu.VMEM((width, columns - first), bf16),
            pltpu.VMEM((tokens, width + EXTRA), bf16),
            pltpu.SemaphoreType.DMA((len(operands) + len(cot) + len(weights),)),
            pltpu.VMEM((count, rows // 2, EXTRA), f32),
            pltpu.VMEM((slots, text_dev * count, HD), bf16),
            pltpu.VMEM((tokens, columns - first), bf16),
            pltpu.VMEM((tokens, 3 * inner), f32),
            pltpu.VMEM((tokens, stacked), bf16),
        ]
        + [pltpu.VMEM(one.shape, one.dtype) for one in operands],
        compiler_params=pltpu.CompilerParams(vmem_limit_bytes=GRANT),
        cost_estimate=pl.CostEstimate(
            flops=2 * tokens * width * inner + 10 * tokens * tokens * inner,
            bytes_accessed=2 * (tokens * width + columns * width),
            transcendentals=slots * tokens * tokens,
        ),
    )(scalars, gain, *operands, *cot, *weights)


def backward_kernel(own, other, w_own, w_other, *outs):
    total = dot(own[...], w_own[...], NT) + dot(other[...], w_other[...], NT)
    part = outs[0].shape[0]
    for n, out in enumerate(outs):
        out[...] = total[n * part : (n + 1) * part].astype(out.dtype)


def backward_call(own, other, w_own, w_other, part, dtype):
    rows, inner = own.shape
    half = w_own.shape[0]
    vmem = spec(pltpu.VMEM)
    return pl.pallas_call(
        backward_kernel,
        out_shape=(jax.ShapeDtypeStruct((part, half), dtype),) * (rows // part),
        in_specs=[vmem] * 4,
        out_specs=(vmem,) * (rows // part),
        compiler_params=pltpu.CompilerParams(vmem_limit_bytes=SMALL_GRANT),
        cost_estimate=pl.CostEstimate(
            flops=4 * rows * half * inner,
            bytes_accessed=4 * (rows + half) * inner + 4 * rows * half,
            transcendentals=0,
        ),
    )(own, other, w_own, w_other)


def sums_kernel(own_near, own_far, near, far, scale, normed, grad_out, sums_out):
    half = near.shape[0]
    for part, (own, moving) in enumerate(((own_near, near), (own_far, far))):
        here = slice(part * half, (part + 1) * half)
        grad = (own[...] + moving[...].astype(jnp.float32)) * scale[...]
        grad_out[here, :] = grad
        first = jnp.sum(grad, axis=-1, keepdims=True)
        second = jnp.sum(grad * normed[here, :], axis=-1, keepdims=True)
        lane = lax.broadcasted_iota(jnp.int32, (half, 128), 1)
        sums_out[here, :] = jnp.where(lane == 0, first, second)


def last_kernel(width, grad, sums, other, normed, base, inv_std, out):
    total = (sums[...] + other[...]) * (1.0 / width)
    rows = base[...] + inv_std[:, 0:1] * (
        grad[...] - total[:, 0:1] - normed[...] * total[:, 1:2]
    )
    out[...] = rows.T


def local_call(kernel, shapes, scalar_count, *operands):
    vmem = spec(pltpu.VMEM)
    return pl.pallas_call(
        kernel,
        out_shape=tuple(jax.ShapeDtypeStruct(*one) for one in shapes),
        in_specs=[spec(pltpu.SMEM)] * scalar_count + [vmem] * (len(operands) - scalar_count),
        out_specs=(vmem,) * len(shapes),
        compiler_params=pltpu.CompilerParams(vmem_limit_bytes=SMALL_GRANT),
        cost_estimate=pl.CostEstimate(
            flops=sum(one.size for one in operands),
            bytes_accessed=sum(one.size * one.dtype.itemsize for one in operands),
            transcendentals=0,
        ),
    )(*operands)


def shards_by_head(states, adjoint, text_kv, text_len, step_index, modulation, w_qkv, qk_gain, w_out):
    hidden_state = states[0]
    adjoint_rows = adjoint[0]
    tok_count, model_width = hidden_state.shape
    seq_count = lax.axis_size("seq")
    inner_dev = w_qkv.shape[2]
    heads_dev = inner_dev // HD
    shard = w_qkv.shape[0]
    slots = -(-heads_dev // seq_count)
    inner = slots * HD
    half_rows = tok_count // 2
    half_width = model_width // 2
    f32, bf16 = jnp.float32, jnp.bfloat16
    core = lax.axis_index("head").astype(jnp.int32)
    seq_index = lax.axis_index("seq")
    dp_index = lax.axis_index("dp")
    pin = lax.optimization_barrier

    seq_order = line_ring(seq_count)
    seq_place = ring_place(seq_order, seq_index)
    seq_next = ring_pairs(seq_order)
    swap = [(0, 1), (1, 0)]
    along_x = [(p, p ^ 1) for p in range(4)]
    along_y = [(p, p ^ 2) for p in range(4)]

    first = seq_index * heads_dev // seq_count
    stop = (seq_index + 1) * heads_dev // seq_count
    window = jnp.minimum(first, heads_dev - slots)
    valid = [(window + i >= first) & (window + i < stop) for i in range(slots)]
    owners = [ring_member(seq_order, (seq_place - k + seq_count) % seq_count) for k in range(seq_count)]
    w_index = [dp_index, dp_index ^ 1, dp_index ^ 2, dp_index ^ 3]
    scalars = [core] + w_index + [window, text_len[0]] + owners + valid
    scalars = jnp.stack([one.astype(jnp.int32) for one in scalars])

    def step(moving):
        return lax.ppermute(moving, "seq", seq_next)

    def other_core(moving):
        return lax.ppermute(moving, "head", swap)

    def step_back(moving):
        return lax.ppermute(moving, "seq", [(b, a) for a, b in seq_next])

    quarter = half_rows // 2

    def spread(moving):
        return [step(moving), step_back(moving)]

    def pass_on(received):
        return [step(received[0][:quarter]), step_back(received[1][quarter:])]

    mod_half, table_rows, extra = first_call(
        step_index, core[None], hidden_state, modulation.transpose(1, 0, 2), adjoint_rows, text_kv[0]
    )
    mod_near = spread(mod_half)

    w_qkv, w_out, mod_half = pin((w_qkv, w_out, mod_half))
    take = lambda c: lax.dynamic_slice(w_qkv, (0, c, window * HD), (shard, 1, inner))[:, 0]
    own_w = [
        jnp.concatenate(
            [take(0), take(1), take(2), lax.dynamic_slice_in_dim(w_out, window * HD, inner, 0).T], axis=1
        )
    ]
    w_near = [lax.ppermute(part, "dp", pairs) for part in own_w for pairs in (along_x, along_y)]

    text_dev = text_kv.shape[1]
    mod_far = pass_on(mod_near)
    clip_limit = 0.5 * (tok_count * seq_count * model_width) ** 0.5
    cotangent, cot_half, base = cotangent_call(
        clip_limit, scalars, adjoint_rows, table_rows, text_kv[0], extra, *mod_near, mod_far[1]
    )
    cot_half, mod_far[0] = pin((cot_half, mod_far[0]))
    cot_near = spread(cot_half)
    modulated, normed_share, scale_share, inv_std = local_call(
        modulate_kernel,
        [
            ((tok_count, model_width + EXTRA), bf16),
            ((tok_count, half_width), f32),
            ((1, half_width), f32),
            ((tok_count, 128), f32),
        ],
        1,
        core[None],
        hidden_state,
        table_rows,
        extra,
    )
    def pieces(own, received):
        return [own] + [one for moved in received for one in (moved, other_core(moved))]

    mod_pieces = pieces(modulated, mod_near + mod_far)
    *w_near, mod_pieces = pin((*w_near, mod_pieces))
    weights = []
    for n, part in enumerate(own_w):
        w_x, w_y = w_near[2 * n : 2 * n + 2]
        weights += [
            part,
            w_x,
            w_y,
            lax.ppermute(w_x[: shard // 2], "dp", along_y),
            lax.ppermute(w_y[shard // 2 :], "dp", along_x),
        ]
    cot_far = [step(cot_near[0])]

    cot_pieces = pieces(cotangent, cot_near)
    *cot_pieces, mod_pieces[-1] = pin((*cot_pieces, mod_pieces[-1]))
    *operands, w_keep, w_give = project_call(
        scalars, qk_gain, mod_pieces, weights, slots, tok_count, text_dev, seq_count
    )
    w_give, cot_far[0] = pin((w_give, *cot_far))
    cot_pieces += pieces(None, cot_far)[1:]
    given, *cot_pieces = pin((w_give, *cot_pieces))
    w_other = other_core(given)
    mine, theirs, rest = attend_call(
        scalars, qk_gain, operands + [w_keep, w_give], cot_pieces, weights, slots, tok_count, text_dev
    )
    first = (mine + other_core(theirs).astype(f32)).astype(bf16)
    moving = [first[:half_rows], first[half_rows:]]
    other_rest = other_core(rest)
    rest, other_rest, *_ = pin((rest, other_rest, *moving))
    own = backward_call(rest, other_rest, w_keep, w_other, half_rows, f32)
    for j in range(2, seq_count):
        moving = [step(part) for part in moving]
        moving = [
            (a + b.astype(f32)).astype(bf16) for a, b in zip(own[2 * (j - 2) : 2 * (j - 1)], moving)
        ]
    moving = [step(part) for part in moving]

    grad_scaled, sums = local_call(
        sums_kernel,
        [((tok_count, half_width), f32), ((tok_count, 128), f32)],
        0,
        *own[-2:],
        *moving,
        scale_share,
        normed_share,
    )
    (pulled,) = local_call(
        functools.partial(last_kernel, model_width),
        [((half_width, tok_count), f32)],
        0,
        grad_scaled,
        sums,
        other_core(sums),
        normed_share,
        base,
        inv_std,
    )
    return pulled.T[None]


def qk_normalize(values, gains):
    inverse = lax.rsqrt(jnp.mean(values * values, axis=-1, keepdims=True) + 1e-06)
    return ((values * inverse * gains).astype(jnp.bfloat16), inverse)


def qk_backward(values, inverse, cotangent, gains):
    scaled = cotangent.astype(jnp.float32) * gains
    return (
        scaled * inverse - values * jnp.mean(scaled * values, axis=-1, keepdims=True) * inverse**3
    )


def shards_by_row(states, adjoint, text_kv, text_len, step_index, modulation, w_qkv, qk_gain, w_out):
    hidden_state = states[0]
    adjoint_rows = adjoint[0]
    tok_count, model_width = hidden_state.shape
    seq_count = lax.axis_size("seq")
    inner_dev = w_qkv.shape[2]
    heads_dev = inner_dev // HD
    score_scale = HD ** (-0.5)
    squares = lax.psum(jnp.sum(adjoint_rows * adjoint_rows), "seq")
    clip_limit = 0.5 * (tok_count * seq_count * model_width) ** 0.5
    clip_scale = jnp.minimum(1.0, clip_limit / jnp.sqrt(squares + 1e-06))
    table_row = lax.dynamic_index_in_dim(modulation, step_index[0], 0, keepdims=False)
    offset_row = table_row[0]
    stretch = table_row[1]
    gating = table_row[2]
    widened = hidden_state.astype(jnp.float32)
    centered = widened - jnp.mean(widened, axis=-1, keepdims=True)
    inv_std = lax.rsqrt(jnp.mean(centered * centered, axis=-1, keepdims=True) + 1e-06)
    normed = centered * inv_std
    modulated = (normed * (1.0 + stretch) + offset_row).astype(jnp.bfloat16)
    cotangent = (gating * (clip_scale * adjoint_rows)).astype(jnp.bfloat16)
    contract_last = (((1,), (1,)), ((), ()))
    full_weight = lax.all_gather(w_qkv, "dp", axis=0, tiled=True).reshape(
        model_width, 3 * inner_dev
    )
    projected = jnp.dot(modulated, full_weight, preferred_element_type=jnp.float32)
    out_raw = lax.dot_general(
        cotangent,
        lax.all_gather(w_out, "dp", axis=1, tiled=True),
        contract_last,
        preferred_element_type=jnp.float32,
    )
    projected = projected.reshape(tok_count, 3, heads_dev, HD)
    queries, query_inv = qk_normalize(projected[:, 0], qk_gain[0])
    own_keys, key_inv = qk_normalize(projected[:, 1], qk_gain[1])
    own_values = projected[:, 2].astype(jnp.bfloat16)
    out_grad = out_raw.astype(jnp.bfloat16).reshape(tok_count, heads_dev, HD)
    text_keys = text_kv[0, :, 0, :]
    text_values = text_kv[0, :, 1, :]
    text_dev = text_keys.shape[0]
    rows_dev = tok_count + text_dev
    key_local = jnp.concatenate([own_keys.reshape(tok_count, inner_dev), text_keys], axis=0)
    value_local = jnp.concatenate([own_values.reshape(tok_count, inner_dev), text_values], axis=0)
    key_all, value_all = (
        lax.all_gather(key_local, "seq", axis=0, tiled=True),
        lax.all_gather(value_local, "seq", axis=0, tiled=True),
    )
    all_rows = rows_dev * seq_count
    row_ids = jnp.arange(all_rows, dtype=jnp.int32)
    owner = row_ids // rows_dev
    within = row_ids % rows_dev
    allowed = (within < tok_count) | (owner * text_dev + within - tok_count < text_len[0])
    group = 1
    while group * 2 * rows_dev <= 512 and seq_count % (group * 2) == 0:
        group = group * 2
    block_rows = group * rows_dev
    block_count = all_rows // block_rows
    key_blocks = key_all.reshape(block_count, block_rows, heads_dev, HD)
    value_blocks = value_all.reshape(block_count, block_rows, heads_dev, HD)
    mask_blocks = allowed.reshape(block_count, block_rows)

    def block_scores(key_block, mask_block):
        scores = (
            jnp.einsum("qhd,khd->qhk", queries, key_block, preferred_element_type=jnp.float32)
            * score_scale
        )
        return jnp.where(mask_block[None, None, :], scores, -1e30)

    def first_pass(carry, block):
        row_max, row_sum, row_dot = carry
        key_block, value_block, mask_block = block
        scores = block_scores(key_block, mask_block)
        new_max = jnp.maximum(row_max, jnp.max(scores, axis=-1))
        rescale = jnp.exp(row_max - new_max)
        exps = jnp.exp(scores - new_max[:, :, None])
        grad_weights = jnp.einsum(
            "qhd,khd->qhk", out_grad, value_block, preferred_element_type=jnp.float32
        )
        return (
            (
                new_max,
                row_sum * rescale + jnp.sum(exps, axis=-1),
                row_dot * rescale + jnp.sum(exps * grad_weights, axis=-1),
            ),
            None,
        )

    start_state = (
        jnp.full((tok_count, heads_dev), -1e30, jnp.float32),
        jnp.zeros((tok_count, heads_dev), jnp.float32),
        jnp.zeros((tok_count, heads_dev), jnp.float32),
    )
    (row_max, row_sum, row_dot), unused = lax.scan(
        first_pass, start_state, (key_blocks, value_blocks, mask_blocks)
    )
    log_total = row_max + jnp.log(row_sum)
    delta_row = row_dot / row_sum

    def second_pass(running, block):
        key_block, value_block, mask_block = block
        weights = jnp.exp(block_scores(key_block, mask_block) - log_total[:, :, None])
        grad_weights = jnp.einsum(
            "qhd,khd->qhk", out_grad, value_block, preferred_element_type=jnp.float32
        )
        grad_scores = (weights * (grad_weights - delta_row[:, :, None])).astype(jnp.bfloat16)
        return (
            running
            + jnp.einsum(
                "qhk,khd->qhd", grad_scores, key_block, preferred_element_type=jnp.float32
            ),
            None,
        )

    query_sum, unused = lax.scan(
        second_pass,
        jnp.zeros((tok_count, heads_dev, HD), jnp.float32),
        (key_blocks, value_blocks, mask_blocks),
    )
    grad_query = (query_sum * score_scale).astype(jnp.bfloat16)
    log_all, delta_all = (
        lax.all_gather(log_total, "seq", axis=0, tiled=True),
        lax.all_gather(delta_row, "seq", axis=0, tiled=True),
    )
    local_ids = jnp.arange(rows_dev, dtype=jnp.int32)
    local_allowed = (local_ids < tok_count) | (
        lax.axis_index("seq") * text_dev + local_ids - tok_count < text_len[0]
    )
    key_three = key_local.reshape(rows_dev, heads_dev, HD)
    value_three = value_local.reshape(rows_dev, heads_dev, HD)
    query_piece = lax.all_gather(queries.reshape(tok_count, inner_dev), "seq", axis=0, tiled=True)
    grad_piece = lax.all_gather(out_grad.reshape(tok_count, inner_dev), "seq", axis=0, tiled=True)
    piece_rows = query_piece.shape[0]
    query_rows = query_piece.reshape(piece_rows, heads_dev, HD)
    grad_rows = grad_piece.reshape(piece_rows, heads_dev, HD)
    scores = (
        jnp.einsum("qhd,khd->qhk", query_rows, key_three, preferred_element_type=jnp.float32)
        * score_scale
    )
    scores = jnp.where(local_allowed[None, None, :], scores, -1e30)
    weights = jnp.exp(scores - log_all[:, :, None])
    grad_weights = jnp.einsum(
        "qhd,khd->qhk", grad_rows, value_three, preferred_element_type=jnp.float32
    )
    grad_scores = (weights * (grad_weights - delta_all[:, :, None])).astype(jnp.bfloat16)
    rounded = weights.astype(jnp.bfloat16)
    key_sum = jnp.einsum(
        "qhk,qhd->khd", grad_scores, query_rows, preferred_element_type=jnp.float32
    )
    value_sum = jnp.einsum("qhk,qhd->khd", rounded, grad_rows, preferred_element_type=jnp.float32)
    key_sum, value_sum = (key_sum, value_sum)
    grad_key = (key_sum[:tok_count] * score_scale).astype(jnp.bfloat16)
    grad_value = value_sum[:tok_count].astype(jnp.bfloat16)
    raw_query = qk_backward(projected[:, 0], query_inv, grad_query, qk_gain[0])
    raw_key = qk_backward(projected[:, 1], key_inv, grad_key, qk_gain[1])
    stacked = jnp.stack([raw_query, raw_key, grad_value.astype(jnp.float32)], axis=1).astype(
        jnp.bfloat16
    )
    stacked = stacked.reshape(tok_count, 3 * inner_dev)
    partial_grad = lax.dot_general(
        stacked, full_weight, contract_last, preferred_element_type=jnp.float32
    )
    half_width = model_width // lax.axis_size("head")
    first_col = lax.axis_index("head") * half_width
    grad_share = lax.psum_scatter(
        partial_grad.astype(jnp.bfloat16), "head", scatter_dimension=1, tiled=True
    ).astype(jnp.float32)
    normed_share = lax.dynamic_slice_in_dim(normed, first_col, half_width, 1)
    stretch_share = lax.dynamic_slice_in_dim(stretch, first_col, half_width, 0)
    adjoint_share = lax.dynamic_slice_in_dim(adjoint_rows, first_col, half_width, 1)
    grad_scaled = grad_share * (1.0 + stretch_share)
    row_sums = jnp.stack(
        [jnp.sum(grad_scaled, axis=-1), jnp.sum(grad_scaled * normed_share, axis=-1)], axis=-1
    )
    row_sums = lax.psum(row_sums, "head")
    grad_state = inv_std * (
        grad_scaled - row_sums[:, 0:1] / model_width - normed_share * row_sums[:, 1:2] / model_width
    )
    pulled = clip_scale * adjoint_share + grad_state
    return pulled[None]


def solution(mesh):
    in_specs = (
        P("dp", "seq", None),
        P("dp", "seq", None),
        P("dp", "seq", None, "head"),
        P("dp"),
        P("dp"),
        P(),
        P("dp", None, "head"),
        P(),
        P("head", "dp"),
    )
    out_specs = P("dp", "seq", "head")
    by_head = mesh.shape["seq"] == 4 and mesh.shape["dp"] == 4 and mesh.shape["head"] == 2
    shards = shards_by_head if by_head else shards_by_row
    return jax.shard_map(shards, mesh=mesh, in_specs=in_specs, out_specs=out_specs, check_vma=False)
```

```python
import functools

import jax
import jax.numpy as jnp
from jax import lax
from jax.experimental import pallas as pl
from jax.experimental.pallas import tpu as pltpu
from jax.sharding import PartitionSpec as P

HD = 64
GRANT = 60 * 1024 * 1024
SMALL_GRANT = 24 * 1024 * 1024
EXTRA = 128
NT = (((1,), (1,)), ((), ()))
NN = (((1,), (0,)), ((), ()))


def line_ring(count):
    return [0] + list(range(1, count, 2)) + [i for i in range(count - 1, 0, -1) if i % 2 == 0]


def ring_pairs(order):
    return [(order[i], order[(i + 1) % len(order)]) for i in range(len(order))]


def ring_place(order, index):
    place = jnp.int32(0)
    for position, member in enumerate(order):
        place = jnp.where(index == member, jnp.int32(position), place)
    return place


def ring_member(order, place):
    member = jnp.int32(order[0])
    for position, value in enumerate(order):
        member = jnp.where(place == position, jnp.int32(value), member)
    return member


def dot(a, b, dims):
    return lax.dot_general(a, b, dims, preferred_element_type=jnp.float32)


def equal_blocks(columns, block):
    row = lax.broadcasted_iota(jnp.int32, (columns, columns), 0)
    column = lax.broadcasted_iota(jnp.int32, (columns, columns), 1)
    return jnp.where(row // block == column // block, 1.0, 0.0).astype(jnp.bfloat16)


def head_means(values):
    ones = equal_blocks(values.shape[1], HD)
    total = 0.0
    for n in range(3):
        term = values.astype(jnp.bfloat16)
        total = total + dot(term, ones, NN)
        if n < 2:
            values = values - term.astype(jnp.float32)
    return total * (1.0 / HD)


def head_gains(gain, slots):
    return jnp.concatenate([gain[0:1, :]] * slots + [gain[1:2, :]] * slots, axis=1)


def whole_tiles(columns):
    return -(-columns // 128) * 128


def spec(space):
    return pl.BlockSpec(memory_space=space)


def text_columns(text, part):
    rows = text[...].astype(jnp.float32)[:, part, :]
    return [rows[:, c * EXTRA : (c + 1) * EXTRA] for c in range(rows.shape[1] // EXTRA)]


def extra_columns(blocks, rows):
    filled = sum(one.shape[0] for one in blocks)
    blocks = blocks + [jnp.zeros((rows - filled, EXTRA), jnp.float32)]
    return jnp.concatenate(blocks, axis=0).astype(jnp.bfloat16)


def first_kernel(step, core, states, table, adjoint, text, out, rows_out, extra_out):
    rows = [table[c, pl.ds(step[0], 1), :] for c in range(3)]
    widened = states[...].astype(jnp.float32)
    centered = widened - jnp.mean(widened, axis=-1, keepdims=True)
    inv_std = lax.rsqrt(jnp.mean(centered * centered, axis=-1, keepdims=True) + 1e-06)
    half, width = states.shape
    out[:, :width] = (centered * inv_std * (1.0 + rows[1]) + rows[0]).astype(jnp.bfloat16)
    for c in range(3):
        rows_out[c : c + 1, :] = rows[c]
    squares = jnp.sum(adjoint[...] * adjoint[...], axis=0, keepdims=True)
    squares = jnp.sum(squares, axis=1, keepdims=True)
    terms = []
    for n in range(3):
        terms.append(squares.astype(jnp.bfloat16).astype(jnp.float32))
        squares = squares - terms[-1]
    lane = lax.broadcasted_iota(jnp.int32, (8, EXTRA), 1)
    sums = jnp.where(lane == 0, terms[0], jnp.where(lane == 1, terms[1], jnp.where(lane == 2, terms[2], 0.0)))
    extra = extra_columns(text_columns(text, 0) + [sums], half)
    out[:, width:] = extra
    extra_out[...] = extra


def first_call(step, core, states, table, adjoint, text):
    rows, width = states.shape
    half = rows // 2
    whole = lambda *shape: pl.BlockSpec(shape, lambda i, step, core: (0,) * len(shape))
    return pl.pallas_call(
        first_kernel,
        out_shape=(
            jax.ShapeDtypeStruct((half, width + EXTRA), jnp.bfloat16),
            jax.ShapeDtypeStruct((8, width), jnp.float32),
            jax.ShapeDtypeStruct((half, EXTRA), jnp.bfloat16),
        ),
        grid_spec=pltpu.PrefetchScalarGridSpec(
            num_scalar_prefetch=2,
            grid=(1,),
            in_specs=[
                pl.BlockSpec((half, width), lambda i, step, core: (core[0], 0)),
                whole(*table.shape),
                whole(*adjoint.shape),
                whole(*text.shape),
            ],
            out_specs=(whole(half, width + EXTRA), whole(8, width), whole(half, EXTRA)),
        ),
        compiler_params=pltpu.CompilerParams(vmem_limit_bytes=GRANT),
        cost_estimate=pl.CostEstimate(flops=8 * half * width, bytes_accessed=16 * half * width, transcendentals=0),
    )(step, core, states, table, adjoint, text)


def pick_half(core, rows):
    half = rows.shape[1] // 2
    return jnp.where(core == 0, rows[:, :half], rows[:, half:])


def modulate_kernel(core, states, table_rows, extra, out, normed_out, stretch_out, inv_out):
    widened = states[...].astype(jnp.float32)
    centered = widened - jnp.mean(widened, axis=-1, keepdims=True)
    inv_std = lax.rsqrt(jnp.mean(centered * centered, axis=-1, keepdims=True) + 1e-06)
    normed = centered * inv_std
    scale = 1.0 + table_rows[1:2, :]
    rows, width = states.shape
    out[:, :width] = (normed * scale + table_rows[0:1, :]).astype(jnp.bfloat16)
    for n in range(2):
        out[n * rows // 2 : (n + 1) * rows // 2, width:] = extra[...]
    normed_out[...] = pick_half(core[0], normed)
    stretch_out[...] = pick_half(core[0], scale)
    inv_out[...] = jnp.broadcast_to(inv_std, inv_out.shape)


def cotangent_kernel(limit, core, adjoint, table_rows, text, extra, previous, following, opposite, out, half_out, base_out):
    quarter = opposite.shape[0]
    first = 2 * quarter - opposite.shape[0]
    row = 8 * (text.shape[2] // EXTRA)
    squares = None
    for terms in (extra[...], previous[...], following[...]):
        terms = terms.astype(jnp.float32)[row : row + 1, :]
        squares = terms if squares is None else squares + terms
    squares = squares + opposite[...].astype(jnp.float32)[row - first : row - first + 1, :]
    squares = jnp.sum(squares, axis=1, keepdims=True)
    clip_scale = jnp.minimum(1.0, limit / jnp.sqrt(squares + 1e-06))
    gating = table_rows[2:3, :]
    clipped = clip_scale * adjoint[...]
    rows, width = adjoint.shape
    half = rows // 2
    columns = extra_columns(text_columns(text, 1), half)
    out[:, :width] = (gating * clipped).astype(jnp.bfloat16)
    for n in range(2):
        out[n * half : (n + 1) * half, width:] = columns
    base_out[...] = pick_half(core[0], clipped)
    own = adjoint[pl.ds(pl.multiple_of(core[0] * half, 8), half), :]
    half_out[:, :width] = (gating * (clip_scale * own)).astype(jnp.bfloat16)
    half_out[:, width:] = columns


def cotangent_call(limit, core, adjoint, table_rows, text, extra, previous, following, opposite):
    rows, width = adjoint.shape
    bf16 = jnp.bfloat16
    block = width // EXTRA
    whole = lambda one: pl.BlockSpec(one.shape, lambda i, core: (0,) * one.ndim)
    tail = lambda one: pl.BlockSpec((one.shape[0], EXTRA), lambda i, core: (0, block))
    outs = (
        jax.ShapeDtypeStruct((rows, width + EXTRA), bf16),
        jax.ShapeDtypeStruct((rows // 2, width + EXTRA), bf16),
        jax.ShapeDtypeStruct((rows, width // 2), jnp.float32),
    )
    return pl.pallas_call(
        functools.partial(cotangent_kernel, limit),
        out_shape=outs,
        grid_spec=pltpu.PrefetchScalarGridSpec(
            num_scalar_prefetch=1,
            grid=(1,),
            in_specs=[whole(adjoint), whole(table_rows), whole(text), whole(extra)]
            + [tail(one) for one in (previous, following, opposite)],
            out_specs=tuple(whole(one) for one in outs),
        ),
        compiler_params=pltpu.CompilerParams(vmem_limit_bytes=SMALL_GRANT),
        cost_estimate=pl.CostEstimate(flops=4 * rows * width, bytes_accessed=12 * rows * width, transcendentals=0),
    )(core, adjoint, table_rows, text, extra, previous, following, opposite)


class Copies:
    def __init__(self, sems):
        self.sems = sems
        self.count = 0

    def start(self, source, target):
        copy = pltpu.make_async_copy(source, target, self.sems.at[self.count])
        copy.start()
        self.count += 1
        return copy

    def weights(self, scalars, w_in, w_all, shard, first=0):
        columns = w_in[0].shape[1] - first
        return [
            self.start(
                piece.at[:, pl.ds(first, columns)],
                w_all.at[
                    pl.ds(pl.multiple_of(scalars[1 + n % 4] * shard, 16), shard),
                    pl.ds(n // 4 * columns, columns),
                ],
            )
            for n, piece in enumerate(w_in)
        ]

    def rows(self, core, pieces, target, rows):
        half = rows // 2
        copies = [self.start(pieces[0], target.at[pl.ds(0, rows)])]
        places = [(rows, half), (3 * rows, half)]
        parts = (len(pieces) - 5) // 2
        places += [(2 * rows + n * half // parts, half // parts) for n in range(parts)]
        for n, (first, size) in enumerate(places):
            for m, holder in enumerate((core, 1 - core)):
                there = pl.ds(pl.multiple_of(first + holder * half, 16), size)
                copies.append(self.start(pieces[1 + 2 * n + m], target.at[there]))
        return copies


def window_heads(scalars, count, rows, text_dev, gathered, width, extra, text, text_t=None):
    half = rows // 2
    for k in range(count):
        there = pl.ds(pl.multiple_of(k * rows + scalars[0] * half, 16), half)
        extra[k] = gathered[there, width:].astype(jnp.float32)
    for i in range(text.shape[0]):
        head = scalars[5] + i
        first = pl.ds(pl.multiple_of(head // 2 * text_dev, 8), text_dev)
        found = jnp.concatenate([extra[k, first, :] for k in range(count)], axis=0)
        found = jnp.where(head % 2 == 0, found[:, :HD], found[:, HD:])
        text[i] = found.astype(jnp.bfloat16)
        if text_t is not None:
            text_t[i] = found.T.astype(jnp.bfloat16)


def project_kernel(slots, count, rows, shard, width, text_dev, scalars, gain, *refs):
    refs = list(refs)
    take = lambda n: [refs.pop(0) for _ in range(n)]
    mod_in = take(9)
    w_in = take(8)
    qkv, k_t, raw_all, inv_all, text, text_t, w_keep, w_give = take(8)
    w_all, mod_all, sems, extra = take(4)
    inner = slots * HD
    core = scalars[0]
    copies = Copies(sems)
    w_copies = copies.weights(scalars, w_in, w_all, shard)
    row_copies = copies.rows(core, mod_in, mod_all, rows)

    lane = lax.broadcasted_iota(jnp.int32, (1, 2 * inner), 1)
    gains = head_gains(gain, slots) * jnp.where(lane < inner, HD ** (-0.5), 1.0)
    identity = equal_blocks(inner, 1)
    for copy in w_copies:
        copy.wait()
    half = width // 2
    columns = pl.ds(0, w_keep.shape[1])
    half_copies = [
        copies.start(w_all.at[pl.ds(pl.multiple_of(holder * half, 16), half), columns], target)
        for holder, target in ((core, w_keep), (1 - core, w_give))
    ]
    for copy in row_copies:
        copy.wait()
    window_heads(scalars, count, rows, text_dev, mod_all, width, extra, text, text_t)
    span = 2 * rows
    for b in range(count // 2):
        here = slice(b * span, (b + 1) * span)
        projected = jnp.dot(
            mod_all[here, :width], w_all[:, : 3 * inner], preferred_element_type=jnp.float32
        )
        raw = projected[:, : 2 * inner]
        inverse = lax.rsqrt(head_means(raw * raw) + 1e-06)
        raw_all[here, :] = raw
        inv_all[here, :] = inverse
        qkv[here, : 2 * inner] = (raw * inverse * gains).astype(jnp.bfloat16)
        qkv[here, 2 * inner :] = projected[:, 2 * inner :].astype(jnp.bfloat16)
        k_t[:, here] = dot(identity, qkv[here, inner : 2 * inner], NT).astype(jnp.bfloat16)
    for copy in half_copies:
        copy.wait()


def attend_kernel(slots, count, rows, shard, width, text_dev, first_column, scalars, gain, *refs):
    refs = list(refs)
    take = lambda n: [refs.pop(0) for _ in range(n)]
    projected = take(8)
    cot_in = take(7)
    w_in = take(4)
    mine_out, theirs_out, rest_out = take(3)
    w_out, cot_all, sems, extra, values_text = take(5)
    d_all, grads, stacked = take(3)
    qkv, k_t, raw_all, inv_all, text, text_t, w_keep, w_give = refs
    inner = slots * HD
    tokens = rows * count
    core = scalars[0]
    copies = Copies(sems)
    w_copies = copies.weights(scalars, w_in, w_out, shard, first_column)
    row_copies = copies.rows(core, cot_in, cot_all, rows)
    local_copies = [copies.start(*one) for one in zip(projected, refs)]
    score_scale = HD ** (-0.5)
    span = 2 * rows

    text_rows = count * text_dev
    row = lax.broadcasted_iota(jnp.int32, (text_rows, span), 0)
    text_id = row
    for k in range(count):
        inside = (row >= k * text_dev) & (row < (k + 1) * text_dev)
        text_id = jnp.where(inside, row + (scalars[7 + k] - k) * text_dev, text_id)
    bias = jnp.where(text_id < scalars[6], 0.0, -1e30)

    for copy in w_copies:
        copy.wait()
    arrivals = [row_copies[:3], row_copies[3:]]
    for b in range(count // 2):
        for copy in arrivals[b]:
            copy.wait()
        here = slice(b * span, (b + 1) * span)
        out_grad = jnp.dot(cot_all[here, :width], w_out[...], preferred_element_type=jnp.float32)
        d_all[here, :] = out_grad.astype(jnp.bfloat16)
    window_heads(scalars, count, rows, text_dev, cot_all, width, extra, values_text)
    for copy in local_copies[:6]:
        copy.wait()

    d_first = d_all.shape[1] - inner
    for i in range(slots):
        columns = [slice(n * inner + i * HD, n * inner + (i + 1) * HD) for n in range(3)]
        keys, values = qkv[:, columns[1]], qkv[:, columns[2]]
        keys_t = k_t[i * HD : (i + 1) * HD, :]
        grad_k, grad_v = 0.0, 0.0
        for b in range(count // 2):
            here = slice(b * span, (b + 1) * span)
            query = qkv[here, columns[0]]
            grad = d_all[here, d_first + i * HD : d_first + (i + 1) * HD]
            scores = dot(keys, query, NT)
            text_scores = dot(text[i], query, NT) + bias
            col_max = jnp.maximum(
                jnp.max(scores, axis=0, keepdims=True), jnp.max(text_scores, axis=0, keepdims=True)
            )
            exps = jnp.exp(scores - col_max)
            text_exps = jnp.exp(text_scores - col_max)
            total = jnp.sum(exps, axis=0, keepdims=True) + jnp.sum(text_exps, axis=0, keepdims=True)
            inverse = 1.0 / total
            grad_w = dot(values, grad, NT)
            text_grad_w = dot(values_text[i], grad, NT)
            delta = inverse * (
                jnp.sum(exps * grad_w, axis=0, keepdims=True)
                + jnp.sum(text_exps * text_grad_w, axis=0, keepdims=True)
            )
            weights = exps * inverse
            grad_s = (weights * (grad_w - delta)).astype(jnp.bfloat16)
            text_grad_s = (text_exps * inverse * (text_grad_w - delta)).astype(jnp.bfloat16)
            grad_k += dot(grad_s, query, NN)
            grad_v += dot(weights.astype(jnp.bfloat16), grad, NN)
            grad_q = dot(keys_t, grad_s, NN) + dot(text_t[i], text_grad_s, NN)
            grads[here, columns[0]] = grad_q.T * score_scale
        grads[:, columns[1]] = grad_k
        grads[:, columns[2]] = grad_v

    lane = lax.broadcasted_iota(jnp.int32, (1, inner), 1)
    mine = jnp.zeros((1, inner), jnp.float32)
    for i in range(slots):
        inside = (lane >= i * HD) & (lane < (i + 1) * HD) & (scalars[7 + count + i] > 0)
        mine = jnp.where(inside, 1.0, mine)
    gains = head_gains(gain, slots)
    for b in range(count // 2):
        here = slice(b * span, (b + 1) * span)
        scaled = grads[here, : 2 * inner].astype(jnp.bfloat16).astype(jnp.float32) * gains
        raw, inverse = raw_all[here, :], inv_all[here, :]
        back = scaled * inverse - raw * head_means(scaled * raw) * (inverse * inverse * inverse)
        valid = jnp.concatenate([mine, mine], axis=1) > 0.0
        stacked[here, : 2 * inner] = jnp.where(valid, back, 0.0).astype(jnp.bfloat16)
        back = jnp.where(mine > 0.0, grads[here, 2 * inner :], 0.0).astype(jnp.bfloat16)
        stacked[here, 2 * inner : 3 * inner] = back
    stacked[:, 3 * inner :] = jnp.zeros((tokens, stacked.shape[1] - 3 * inner), jnp.bfloat16)
    first = stacked[rows : 2 * rows, :]
    rest_out[: (count - 2) * rows, :] = stacked[2 * rows :, :]
    rest_out[(count - 2) * rows :, :] = stacked[:rows, :]
    for copy in local_copies[6:]:
        copy.wait()
    theirs_out[...] = dot(first, w_give[...], NT).astype(jnp.bfloat16)
    mine_out[...] = dot(first, w_keep[...], NT)


def project_call(scalars, gain, mod, weights, slots, rows, text_dev, count):
    shard = weights[0].shape[0]
    columns = 4 * slots * HD
    width = mod[0].shape[1] - EXTRA
    tokens = rows * count
    text_rows = text_dev * count
    f32, bf16 = jnp.float32, jnp.bfloat16
    vmem, hbm = spec(pltpu.VMEM), spec(pl.ANY)
    inner = slots * HD
    shapes = [((tokens, 3 * inner), bf16), ((inner, tokens), bf16)] + [((tokens, 2 * inner), f32)] * 2
    shapes += [((slots, text_rows, HD), bf16), ((slots, HD, text_rows), bf16)]
    shapes += [((width // 2, whole_tiles(3 * slots * HD)), bf16)] * 2
    return pl.pallas_call(
        functools.partial(project_kernel, slots, count, rows, shard, width, text_dev),
        out_shape=tuple(jax.ShapeDtypeStruct(*one) for one in shapes),
        in_specs=[spec(pltpu.SMEM), vmem] + [hbm] * (len(mod) + len(weights)),
        out_specs=(vmem,) * (len(shapes) - 2) + (hbm,) * 2,
        scratch_shapes=[
            pltpu.VMEM((width, columns), bf16),
            pltpu.VMEM((tokens, width + EXTRA), bf16),
            pltpu.SemaphoreType.DMA((len(mod) + len(weights) + 2,)),
            pltpu.VMEM((count, rows // 2, EXTRA), f32),
        ],
        compiler_params=pltpu.CompilerParams(vmem_limit_bytes=GRANT),
        cost_estimate=pl.CostEstimate(
            flops=2 * tokens * width * 3 * slots * HD,
            bytes_accessed=2 * (tokens * width + columns * width) + 4 * tokens * columns,
            transcendentals=0,
        ),
    )(scalars, gain, *mod, *weights)


def attend_call(scalars, gain, operands, cot, weights, slots, rows, text_dev):
    count = operands[0].shape[0] // rows
    shard, columns = weights[0].shape
    width = cot[0].shape[1] - EXTRA
    tokens = rows * count
    inner = slots * HD
    stacked = whole_tiles(3 * inner)
    first = (columns - inner) // 128 * 128
    f32, bf16 = jnp.float32, jnp.bfloat16
    vmem, hbm = spec(pltpu.VMEM), spec(pl.ANY)
    shapes = [((rows, width // 2), f32), ((rows, width // 2), bf16), ((tokens - rows, stacked), bf16)]
    return pl.pallas_call(
        functools.partial(attend_kernel, slots, count, rows, shard, width, text_dev, first),
        out_shape=tuple(jax.ShapeDtypeStruct(*one) for one in shapes),
        in_specs=[spec(pltpu.SMEM), vmem] + [hbm] * (len(operands) + len(cot) + len(weights)),
        out_specs=(vmem,) * len(shapes),
        scratch_shapes=[
            pltpu.VMEM((width, columns - first), bf16),
            pltpu.VMEM((tokens, width + EXTRA), bf16),
            pltpu.SemaphoreType.DMA((len(operands) + len(cot) + len(weights),)),
            pltpu.VMEM((count, rows // 2, EXTRA), f32),
            pltpu.VMEM((slots, text_dev * count, HD), bf16),
            pltpu.VMEM((tokens, columns - first), bf16),
            pltpu.VMEM((tokens, 3 * inner), f32),
            pltpu.VMEM((tokens, stacked), bf16),
        ]
        + [pltpu.VMEM(one.shape, one.dtype) for one in operands],
        compiler_params=pltpu.CompilerParams(vmem_limit_bytes=GRANT),
        cost_estimate=pl.CostEstimate(
            flops=2 * tokens * width * inner + 10 * tokens * tokens * inner,
            bytes_accessed=2 * (tokens * width + columns * width),
            transcendentals=slots * tokens * tokens,
        ),
    )(scalars, gain, *operands, *cot, *weights)


def backward_kernel(own, other, w_own, w_other, *outs):
    total = dot(own[...], w_own[...], NT) + dot(other[...], w_other[...], NT)
    part = outs[0].shape[0]
    for n, out in enumerate(outs):
        out[...] = total[n * part : (n + 1) * part].astype(out.dtype)


def backward_call(own, other, w_own, w_other, part, dtype):
    rows, inner = own.shape
    half = w_own.shape[0]
    vmem = spec(pltpu.VMEM)
    return pl.pallas_call(
        backward_kernel,
        out_shape=(jax.ShapeDtypeStruct((part, half), dtype),) * (rows // part),
        in_specs=[vmem] * 4,
        out_specs=(vmem,) * (rows // part),
        compiler_params=pltpu.CompilerParams(vmem_limit_bytes=SMALL_GRANT),
        cost_estimate=pl.CostEstimate(
            flops=4 * rows * half * inner,
            bytes_accessed=4 * (rows + half) * inner + 4 * rows * half,
            transcendentals=0,
        ),
    )(own, other, w_own, w_other)


def sums_kernel(own_near, own_far, near, far, scale, normed, grad_out, sums_out):
    half = near.shape[0]
    for part, (own, moving) in enumerate(((own_near, near), (own_far, far))):
        here = slice(part * half, (part + 1) * half)
        grad = (own[...] + moving[...].astype(jnp.float32)) * scale[...]
        grad_out[here, :] = grad
        first = jnp.sum(grad, axis=-1, keepdims=True)
        second = jnp.sum(grad * normed[here, :], axis=-1, keepdims=True)
        lane = lax.broadcasted_iota(jnp.int32, (half, 128), 1)
        sums_out[here, :] = jnp.where(lane == 0, first, second)


def last_kernel(width, grad, sums, other, normed, base, inv_std, out):
    total = (sums[...] + other[...]) * (1.0 / width)
    rows = base[...] + inv_std[:, 0:1] * (
        grad[...] - total[:, 0:1] - normed[...] * total[:, 1:2]
    )
    out[...] = rows.T


def local_call(kernel, shapes, scalar_count, *operands):
    vmem = spec(pltpu.VMEM)
    return pl.pallas_call(
        kernel,
        out_shape=tuple(jax.ShapeDtypeStruct(*one) for one in shapes),
        in_specs=[spec(pltpu.SMEM)] * scalar_count + [vmem] * (len(operands) - scalar_count),
        out_specs=(vmem,) * len(shapes),
        compiler_params=pltpu.CompilerParams(vmem_limit_bytes=SMALL_GRANT),
        cost_estimate=pl.CostEstimate(
            flops=sum(one.size for one in operands),
            bytes_accessed=sum(one.size * one.dtype.itemsize for one in operands),
            transcendentals=0,
        ),
    )(*operands)


def shards_by_head(states, adjoint, text_kv, text_len, step_index, modulation, w_qkv, qk_gain, w_out):
    hidden_state = states[0]
    adjoint_rows = adjoint[0]
    tok_count, model_width = hidden_state.shape
    seq_count = lax.axis_size("seq")
    inner_dev = w_qkv.shape[2]
    heads_dev = inner_dev // HD
    shard = w_qkv.shape[0]
    slots = -(-heads_dev // seq_count)
    inner = slots * HD
    half_rows = tok_count // 2
    half_width = model_width // 2
    f32, bf16 = jnp.float32, jnp.bfloat16
    core = lax.axis_index("head").astype(jnp.int32)
    seq_index = lax.axis_index("seq")
    dp_index = lax.axis_index("dp")
    pin = lax.optimization_barrier

    seq_order = line_ring(seq_count)
    seq_place = ring_place(seq_order, seq_index)
    seq_next = ring_pairs(seq_order)
    swap = [(0, 1), (1, 0)]
    first_way = [(2 * p + c, 2 * (p ^ (1 + c)) + c) for p in range(4) for c in range(2)]
    second_way = [(2 * p + c, 2 * (p ^ (2 - c)) + c) for p in range(4) for c in range(2)]

    first = seq_index * heads_dev // seq_count
    stop = (seq_index + 1) * heads_dev // seq_count
    window = jnp.minimum(first, heads_dev - slots)
    valid = [(window + i >= first) & (window + i < stop) for i in range(slots)]
    owners = [ring_member(seq_order, (seq_place - k + seq_count) % seq_count) for k in range(seq_count)]
    w_index = [dp_index, dp_index ^ (1 + core), dp_index ^ (2 - core), dp_index ^ 3]
    scalars = [core] + w_index + [window, text_len[0]] + owners + valid
    scalars = jnp.stack([one.astype(jnp.int32) for one in scalars])

    def step(moving):
        return lax.ppermute(moving, "seq", seq_next)

    def other_core(moving):
        return lax.ppermute(moving, "head", swap)

    def step_back(moving):
        return lax.ppermute(moving, "seq", [(b, a) for a, b in seq_next])

    quarter = half_rows // 2

    def spread(moving):
        return [step(moving), step_back(moving)]

    def pass_on(received):
        return [step(received[0][:quarter]), step_back(received[1][quarter:])]

    mod_half, table_rows, extra = first_call(
        step_index, core[None], hidden_state, modulation.transpose(1, 0, 2), adjoint_rows, text_kv[0]
    )
    mod_near = spread(mod_half)

    w_qkv, w_out, mod_half = pin((w_qkv, w_out, mod_half))
    take = lambda c: lax.dynamic_slice(w_qkv, (0, c, window * HD), (shard, 1, inner))[:, 0]
    own_w = [
        jnp.concatenate([take(0), take(1)], axis=1),
        jnp.concatenate([take(2), lax.dynamic_slice_in_dim(w_out, window * HD, inner, 0).T], axis=1),
    ]
    w_first = [lax.ppermute(part, ("dp", "head"), first_way) for part in own_w]
    w_second = [lax.ppermute(part, ("dp", "head"), second_way) for part in own_w]

    text_dev = text_kv.shape[1]
    mod_far = pass_on(mod_near)
    clip_limit = 0.5 * (tok_count * seq_count * model_width) ** 0.5
    extra, *w_first = pin((extra, *w_first))
    cotangent, cot_half, base = cotangent_call(
        clip_limit, scalars, adjoint_rows, table_rows, text_kv[0], extra, *mod_near, mod_far[1]
    )
    cot_half, mod_far[0] = pin((cot_half, mod_far[0]))
    cot_near = spread(cot_half)
    modulated, normed_share, scale_share, inv_std = local_call(
        modulate_kernel,
        [
            ((tok_count, model_width + EXTRA), bf16),
            ((tok_count, half_width), f32),
            ((1, half_width), f32),
            ((tok_count, 128), f32),
        ],
        1,
        core[None],
        hidden_state,
        table_rows,
        extra,
    )
    def pieces(own, received):
        return [own] + [one for moved in received for one in (moved, other_core(moved))]

    mod_far = list(pin((*mod_far, modulated))[:2])
    mod_pieces = pieces(modulated, mod_near + mod_far)
    w_diagonal = [lax.ppermute(part, ("dp", "head"), second_way) for part in w_first]
    weights = [part[n] for n in range(2) for part in (own_w, w_first, w_second, w_diagonal)]
    cot_near[0] = pin((cot_near[0], w_second, w_diagonal))[0]
    cot_far = [step(cot_near[0])]

    cot_pieces = pieces(cotangent, cot_near)
    *cot_pieces, mod_pieces[-1] = pin((*cot_pieces, mod_pieces[-1]))
    *operands, w_keep, w_give = project_call(
        scalars, qk_gain, mod_pieces, weights, slots, tok_count, text_dev, seq_count
    )
    w_give, cot_far[0] = pin((w_give, *cot_far))
    cot_pieces += pieces(None, cot_far)[1:]
    given, *cot_pieces = pin((w_give, *cot_pieces))
    w_other = other_core(given)
    mine, theirs, rest = attend_call(
        scalars, qk_gain, operands + [w_keep, w_give], cot_pieces, weights[4:], slots, tok_count, text_dev
    )
    first = (mine + other_core(theirs).astype(f32)).astype(bf16)
    moving = [first[:half_rows], first[half_rows:]]
    other_rest = other_core(rest)
    rest, other_rest, *_ = pin((rest, other_rest, *moving))
    own = backward_call(rest, other_rest, w_keep, w_other, half_rows, f32)
    for j in range(2, seq_count):
        moving = [step(part) for part in moving]
        moving = [
            (a + b.astype(f32)).astype(bf16) for a, b in zip(own[2 * (j - 2) : 2 * (j - 1)], moving)
        ]
    moving = [step(part) for part in moving]

    grad_scaled, sums = local_call(
        sums_kernel,
        [((tok_count, half_width), f32), ((tok_count, 128), f32)],
        0,
        *own[-2:],
        *moving,
        scale_share,
        normed_share,
    )
    (pulled,) = local_call(
        functools.partial(last_kernel, model_width),
        [((half_width, tok_count), f32)],
        0,
        grad_scaled,
        sums,
        other_core(sums),
        normed_share,
        base,
        inv_std,
    )
    return pulled.T[None]


def qk_normalize(values, gains):
    inverse = lax.rsqrt(jnp.mean(values * values, axis=-1, keepdims=True) + 1e-06)
    return ((values * inverse * gains).astype(jnp.bfloat16), inverse)


def qk_backward(values, inverse, cotangent, gains):
    scaled = cotangent.astype(jnp.float32) * gains
    return (
        scaled * inverse - values * jnp.mean(scaled * values, axis=-1, keepdims=True) * inverse**3
    )


def shards_by_row(states, adjoint, text_kv, text_len, step_index, modulation, w_qkv, qk_gain, w_out):
    hidden_state = states[0]
    adjoint_rows = adjoint[0]
    tok_count, model_width = hidden_state.shape
    seq_count = lax.axis_size("seq")
    inner_dev = w_qkv.shape[2]
    heads_dev = inner_dev // HD
    score_scale = HD ** (-0.5)
    squares = lax.psum(jnp.sum(adjoint_rows * adjoint_rows), "seq")
    clip_limit = 0.5 * (tok_count * seq_count * model_width) ** 0.5
    clip_scale = jnp.minimum(1.0, clip_limit / jnp.sqrt(squares + 1e-06))
    table_row = lax.dynamic_index_in_dim(modulation, step_index[0], 0, keepdims=False)
    offset_row = table_row[0]
    stretch = table_row[1]
    gating = table_row[2]
    widened = hidden_state.astype(jnp.float32)
    centered = widened - jnp.mean(widened, axis=-1, keepdims=True)
    inv_std = lax.rsqrt(jnp.mean(centered * centered, axis=-1, keepdims=True) + 1e-06)
    normed = centered * inv_std
    modulated = (normed * (1.0 + stretch) + offset_row).astype(jnp.bfloat16)
    cotangent = (gating * (clip_scale * adjoint_rows)).astype(jnp.bfloat16)
    contract_last = (((1,), (1,)), ((), ()))
    full_weight = lax.all_gather(w_qkv, "dp", axis=0, tiled=True).reshape(
        model_width, 3 * inner_dev
    )
    projected = jnp.dot(modulated, full_weight, preferred_element_type=jnp.float32)
    out_raw = lax.dot_general(
        cotangent,
        lax.all_gather(w_out, "dp", axis=1, tiled=True),
        contract_last,
        preferred_element_type=jnp.float32,
    )
    projected = projected.reshape(tok_count, 3, heads_dev, HD)
    queries, query_inv = qk_normalize(projected[:, 0], qk_gain[0])
    own_keys, key_inv = qk_normalize(projected[:, 1], qk_gain[1])
    own_values = projected[:, 2].astype(jnp.bfloat16)
    out_grad = out_raw.astype(jnp.bfloat16).reshape(tok_count, heads_dev, HD)
    text_keys = text_kv[0, :, 0, :]
    text_values = text_kv[0, :, 1, :]
    text_dev = text_keys.shape[0]
    rows_dev = tok_count + text_dev
    key_local = jnp.concatenate([own_keys.reshape(tok_count, inner_dev), text_keys], axis=0)
    value_local = jnp.concatenate([own_values.reshape(tok_count, inner_dev), text_values], axis=0)
    key_all, value_all = (
        lax.all_gather(key_local, "seq", axis=0, tiled=True),
        lax.all_gather(value_local, "seq", axis=0, tiled=True),
    )
    all_rows = rows_dev * seq_count
    row_ids = jnp.arange(all_rows, dtype=jnp.int32)
    owner = row_ids // rows_dev
    within = row_ids % rows_dev
    allowed = (within < tok_count) | (owner * text_dev + within - tok_count < text_len[0])
    group = 1
    while group * 2 * rows_dev <= 512 and seq_count % (group * 2) == 0:
        group = group * 2
    block_rows = group * rows_dev
    block_count = all_rows // block_rows
    key_blocks = key_all.reshape(block_count, block_rows, heads_dev, HD)
    value_blocks = value_all.reshape(block_count, block_rows, heads_dev, HD)
    mask_blocks = allowed.reshape(block_count, block_rows)

    def block_scores(key_block, mask_block):
        scores = (
            jnp.einsum("qhd,khd->qhk", queries, key_block, preferred_element_type=jnp.float32)
            * score_scale
        )
        return jnp.where(mask_block[None, None, :], scores, -1e30)

    def first_pass(carry, block):
        row_max, row_sum, row_dot = carry
        key_block, value_block, mask_block = block
        scores = block_scores(key_block, mask_block)
        new_max = jnp.maximum(row_max, jnp.max(scores, axis=-1))
        rescale = jnp.exp(row_max - new_max)
        exps = jnp.exp(scores - new_max[:, :, None])
        grad_weights = jnp.einsum(
            "qhd,khd->qhk", out_grad, value_block, preferred_element_type=jnp.float32
        )
        return (
            (
                new_max,
                row_sum * rescale + jnp.sum(exps, axis=-1),
                row_dot * rescale + jnp.sum(exps * grad_weights, axis=-1),
            ),
            None,
        )

    start_state = (
        jnp.full((tok_count, heads_dev), -1e30, jnp.float32),
        jnp.zeros((tok_count, heads_dev), jnp.float32),
        jnp.zeros((tok_count, heads_dev), jnp.float32),
    )
    (row_max, row_sum, row_dot), unused = lax.scan(
        first_pass, start_state, (key_blocks, value_blocks, mask_blocks)
    )
    log_total = row_max + jnp.log(row_sum)
    delta_row = row_dot / row_sum

    def second_pass(running, block):
        key_block, value_block, mask_block = block
        weights = jnp.exp(block_scores(key_block, mask_block) - log_total[:, :, None])
        grad_weights = jnp.einsum(
            "qhd,khd->qhk", out_grad, value_block, preferred_element_type=jnp.float32
        )
        grad_scores = (weights * (grad_weights - delta_row[:, :, None])).astype(jnp.bfloat16)
        return (
            running
            + jnp.einsum(
                "qhk,khd->qhd", grad_scores, key_block, preferred_element_type=jnp.float32
            ),
            None,
        )

    query_sum, unused = lax.scan(
        second_pass,
        jnp.zeros((tok_count, heads_dev, HD), jnp.float32),
        (key_blocks, value_blocks, mask_blocks),
    )
    grad_query = (query_sum * score_scale).astype(jnp.bfloat16)
    log_all, delta_all = (
        lax.all_gather(log_total, "seq", axis=0, tiled=True),
        lax.all_gather(delta_row, "seq", axis=0, tiled=True),
    )
    local_ids = jnp.arange(rows_dev, dtype=jnp.int32)
    local_allowed = (local_ids < tok_count) | (
        lax.axis_index("seq") * text_dev + local_ids - tok_count < text_len[0]
    )
    key_three = key_local.reshape(rows_dev, heads_dev, HD)
    value_three = value_local.reshape(rows_dev, heads_dev, HD)
    query_piece = lax.all_gather(queries.reshape(tok_count, inner_dev), "seq", axis=0, tiled=True)
    grad_piece = lax.all_gather(out_grad.reshape(tok_count, inner_dev), "seq", axis=0, tiled=True)
    piece_rows = query_piece.shape[0]
    query_rows = query_piece.reshape(piece_rows, heads_dev, HD)
    grad_rows = grad_piece.reshape(piece_rows, heads_dev, HD)
    scores = (
        jnp.einsum("qhd,khd->qhk", query_rows, key_three, preferred_element_type=jnp.float32)
        * score_scale
    )
    scores = jnp.where(local_allowed[None, None, :], scores, -1e30)
    weights = jnp.exp(scores - log_all[:, :, None])
    grad_weights = jnp.einsum(
        "qhd,khd->qhk", grad_rows, value_three, preferred_element_type=jnp.float32
    )
    grad_scores = (weights * (grad_weights - delta_all[:, :, None])).astype(jnp.bfloat16)
    rounded = weights.astype(jnp.bfloat16)
    key_sum = jnp.einsum(
        "qhk,qhd->khd", grad_scores, query_rows, preferred_element_type=jnp.float32
    )
    value_sum = jnp.einsum("qhk,qhd->khd", rounded, grad_rows, preferred_element_type=jnp.float32)
    key_sum, value_sum = (key_sum, value_sum)
    grad_key = (key_sum[:tok_count] * score_scale).astype(jnp.bfloat16)
    grad_value = value_sum[:tok_count].astype(jnp.bfloat16)
    raw_query = qk_backward(projected[:, 0], query_inv, grad_query, qk_gain[0])
    raw_key = qk_backward(projected[:, 1], key_inv, grad_key, qk_gain[1])
    stacked = jnp.stack([raw_query, raw_key, grad_value.astype(jnp.float32)], axis=1).astype(
        jnp.bfloat16
    )
    stacked = stacked.reshape(tok_count, 3 * inner_dev)
    partial_grad = lax.dot_general(
        stacked, full_weight, contract_last, preferred_element_type=jnp.float32
    )
    half_width = model_width // lax.axis_size("head")
    first_col = lax.axis_index("head") * half_width
    grad_share = lax.psum_scatter(
        partial_grad.astype(jnp.bfloat16), "head", scatter_dimension=1, tiled=True
    ).astype(jnp.float32)
    normed_share = lax.dynamic_slice_in_dim(normed, first_col, half_width, 1)
    stretch_share = lax.dynamic_slice_in_dim(stretch, first_col, half_width, 0)
    adjoint_share = lax.dynamic_slice_in_dim(adjoint_rows, first_col, half_width, 1)
    grad_scaled = grad_share * (1.0 + stretch_share)
    row_sums = jnp.stack(
        [jnp.sum(grad_scaled, axis=-1), jnp.sum(grad_scaled * normed_share, axis=-1)], axis=-1
    )
    row_sums = lax.psum(row_sums, "head")
    grad_state = inv_std * (
        grad_scaled - row_sums[:, 0:1] / model_width - normed_share * row_sums[:, 1:2] / model_width
    )
    pulled = clip_scale * adjoint_share + grad_state
    return pulled[None]


def solution(mesh):
    in_specs = (
        P("dp", "seq", None),
        P("dp", "seq", None),
        P("dp", "seq", None, "head"),
        P("dp"),
        P("dp"),
        P(),
        P("dp", None, "head"),
        P(),
        P("head", "dp"),
    )
    out_specs = P("dp", "seq", "head")
    by_head = mesh.shape["seq"] == 4 and mesh.shape["dp"] == 4 and mesh.shape["head"] == 2
    shards = shards_by_head if by_head else shards_by_row
    return jax.shard_map(shards, mesh=mesh, in_specs=in_specs, out_specs=out_specs, check_vma=False)
```

```python
import functools

import jax
import jax.numpy as jnp
from jax import lax
from jax.experimental import pallas as pl
from jax.experimental.pallas import tpu as pltpu
from jax.sharding import PartitionSpec as P

HD = 64
GRANT = 60 * 1024 * 1024
SMALL_GRANT = 24 * 1024 * 1024
EXTRA = 128
NT = (((1,), (1,)), ((), ()))
NN = (((1,), (0,)), ((), ()))


def line_ring(count):
    return [0] + list(range(1, count, 2)) + [i for i in range(count - 1, 0, -1) if i % 2 == 0]


def ring_pairs(order):
    return [(order[i], order[(i + 1) % len(order)]) for i in range(len(order))]


def ring_place(order, index):
    place = jnp.int32(0)
    for position, member in enumerate(order):
        place = jnp.where(index == member, jnp.int32(position), place)
    return place


def ring_member(order, place):
    member = jnp.int32(order[0])
    for position, value in enumerate(order):
        member = jnp.where(place == position, jnp.int32(value), member)
    return member


def dot(a, b, dims):
    return lax.dot_general(a, b, dims, preferred_element_type=jnp.float32)


def equal_blocks(columns, block):
    row = lax.broadcasted_iota(jnp.int32, (columns, columns), 0)
    column = lax.broadcasted_iota(jnp.int32, (columns, columns), 1)
    return jnp.where(row // block == column // block, 1.0, 0.0).astype(jnp.bfloat16)


def head_means(values):
    ones = equal_blocks(values.shape[1], HD)
    total = 0.0
    for n in range(3):
        term = values.astype(jnp.bfloat16)
        total = total + dot(term, ones, NN)
        if n < 2:
            values = values - term.astype(jnp.float32)
    return total * (1.0 / HD)


def head_gains(gain, slots):
    return jnp.concatenate([gain[0:1, :]] * slots + [gain[1:2, :]] * slots, axis=1)


def whole_tiles(columns):
    return -(-columns // 128) * 128


def spec(space):
    return pl.BlockSpec(memory_space=space)


def text_columns(text, part):
    rows = text[...].astype(jnp.float32)[:, part, :]
    return [rows[:, c * EXTRA : (c + 1) * EXTRA] for c in range(rows.shape[1] // EXTRA)]


def extra_columns(blocks, rows):
    filled = sum(one.shape[0] for one in blocks)
    blocks = blocks + [jnp.zeros((rows - filled, EXTRA), jnp.float32)]
    return jnp.concatenate(blocks, axis=0).astype(jnp.bfloat16)


def first_kernel(step, core, states, table, adjoint, text, out, rows_out, extra_out):
    rows = [table[c, pl.ds(step[0] % 8, 1), :] for c in range(3)]
    widened = states[...].astype(jnp.float32)
    centered = widened - jnp.mean(widened, axis=-1, keepdims=True)
    inv_std = lax.rsqrt(jnp.mean(centered * centered, axis=-1, keepdims=True) + 1e-06)
    half, width = states.shape
    out[:, :width] = (centered * inv_std * (1.0 + rows[1]) + rows[0]).astype(jnp.bfloat16)
    for c in range(3):
        rows_out[c : c + 1, :] = rows[c]
    squares = jnp.sum(adjoint[...] * adjoint[...], axis=0, keepdims=True)
    squares = jnp.sum(squares, axis=1, keepdims=True)
    terms = []
    for n in range(3):
        terms.append(squares.astype(jnp.bfloat16).astype(jnp.float32))
        squares = squares - terms[-1]
    lane = lax.broadcasted_iota(jnp.int32, (8, EXTRA), 1)
    sums = jnp.where(lane == 0, terms[0], jnp.where(lane == 1, terms[1], jnp.where(lane == 2, terms[2], 0.0)))
    extra = extra_columns(text_columns(text, 0) + [sums], half)
    out[:, width:] = extra
    extra_out[...] = extra


def first_call(step, core, states, table, adjoint, text):
    rows, width = states.shape
    half = rows // 2
    whole = lambda *shape: pl.BlockSpec(shape, lambda i, step, core: (0,) * len(shape))
    return pl.pallas_call(
        first_kernel,
        out_shape=(
            jax.ShapeDtypeStruct((half, width + EXTRA), jnp.bfloat16),
            jax.ShapeDtypeStruct((8, width), jnp.float32),
            jax.ShapeDtypeStruct((half, EXTRA), jnp.bfloat16),
        ),
        grid_spec=pltpu.PrefetchScalarGridSpec(
            num_scalar_prefetch=2,
            grid=(1,),
            in_specs=[
                pl.BlockSpec((half, width), lambda i, step, core: (core[0], 0)),
                pl.BlockSpec((3, 8, width), lambda i, step, core: (0, step[0] // 8, 0)),
                whole(*adjoint.shape),
                whole(*text.shape),
            ],
            out_specs=(whole(half, width + EXTRA), whole(8, width), whole(half, EXTRA)),
        ),
        compiler_params=pltpu.CompilerParams(vmem_limit_bytes=GRANT),
        cost_estimate=pl.CostEstimate(flops=8 * half * width, bytes_accessed=16 * half * width, transcendentals=0),
    )(step, core, states, table, adjoint, text)


def pick_half(core, rows):
    half = rows.shape[1] // 2
    return jnp.where(core == 0, rows[:, :half], rows[:, half:])


def modulate_kernel(core, states, table_rows, extra, out, normed_out, stretch_out, inv_out):
    widened = states[...].astype(jnp.float32)
    centered = widened - jnp.mean(widened, axis=-1, keepdims=True)
    inv_std = lax.rsqrt(jnp.mean(centered * centered, axis=-1, keepdims=True) + 1e-06)
    normed = centered * inv_std
    scale = 1.0 + table_rows[1:2, :]
    rows, width = states.shape
    out[:, :width] = (normed * scale + table_rows[0:1, :]).astype(jnp.bfloat16)
    for n in range(2):
        out[n * rows // 2 : (n + 1) * rows // 2, width:] = extra[...]
    normed_out[...] = pick_half(core[0], normed)
    stretch_out[...] = pick_half(core[0], scale)
    inv_out[...] = jnp.broadcast_to(inv_std, inv_out.shape)


def cotangent_kernel(limit, core, adjoint, table_rows, text, extra, previous, following, opposite, out, half_out, base_out):
    quarter = opposite.shape[0]
    first = 2 * quarter - opposite.shape[0]
    row = 8 * (text.shape[2] // EXTRA)
    squares = None
    for terms in (extra[...], previous[...], following[...]):
        terms = terms.astype(jnp.float32)[row : row + 1, :]
        squares = terms if squares is None else squares + terms
    squares = squares + opposite[...].astype(jnp.float32)[row - first : row - first + 1, :]
    squares = jnp.sum(squares, axis=1, keepdims=True)
    clip_scale = jnp.minimum(1.0, limit / jnp.sqrt(squares + 1e-06))
    gating = table_rows[2:3, :]
    clipped = clip_scale * adjoint[...]
    rows, width = adjoint.shape
    half = rows // 2
    columns = extra_columns(text_columns(text, 1), half)
    out[:, :width] = (gating * clipped).astype(jnp.bfloat16)
    for n in range(2):
        out[n * half : (n + 1) * half, width:] = columns
    base_out[...] = pick_half(core[0], clipped)
    own = adjoint[pl.ds(pl.multiple_of(core[0] * half, 8), half), :]
    half_out[:, :width] = (gating * (clip_scale * own)).astype(jnp.bfloat16)
    half_out[:, width:] = columns


def cotangent_call(limit, core, adjoint, table_rows, text, extra, previous, following, opposite):
    rows, width = adjoint.shape
    bf16 = jnp.bfloat16
    block = width // EXTRA
    whole = lambda one: pl.BlockSpec(one.shape, lambda i, core: (0,) * one.ndim)
    tail = lambda one: pl.BlockSpec((one.shape[0], EXTRA), lambda i, core: (0, block))
    outs = (
        jax.ShapeDtypeStruct((rows, width + EXTRA), bf16),
        jax.ShapeDtypeStruct((rows // 2, width + EXTRA), bf16),
        jax.ShapeDtypeStruct((rows, width // 2), jnp.float32),
    )
    return pl.pallas_call(
        functools.partial(cotangent_kernel, limit),
        out_shape=outs,
        grid_spec=pltpu.PrefetchScalarGridSpec(
            num_scalar_prefetch=1,
            grid=(1,),
            in_specs=[whole(adjoint), whole(table_rows), whole(text), whole(extra)]
            + [tail(one) for one in (previous, following, opposite)],
            out_specs=tuple(whole(one) for one in outs),
        ),
        compiler_params=pltpu.CompilerParams(vmem_limit_bytes=SMALL_GRANT),
        cost_estimate=pl.CostEstimate(flops=4 * rows * width, bytes_accessed=12 * rows * width, transcendentals=0),
    )(core, adjoint, table_rows, text, extra, previous, following, opposite)


class Copies:
    def __init__(self, sems):
        self.sems = sems
        self.count = 0

    def start(self, source, target):
        copy = pltpu.make_async_copy(source, target, self.sems.at[self.count])
        copy.start()
        self.count += 1
        return copy

    def weights(self, scalars, w_in, w_all, shard, first=0):
        columns = w_in[0].shape[1] - first
        return [
            self.start(
                piece.at[:, pl.ds(first, columns)],
                w_all.at[
                    pl.ds(pl.multiple_of(scalars[1 + n % 4] * shard, 16), shard),
                    pl.ds(n // 4 * columns, columns),
                ],
            )
            for n, piece in enumerate(w_in)
        ]

    def rows(self, core, pieces, target, rows):
        half = rows // 2
        copies = [self.start(pieces[0], target.at[pl.ds(0, rows)])]
        places = [(rows, half), (3 * rows, half)]
        parts = (len(pieces) - 5) // 2
        places += [(2 * rows + n * half // parts, half // parts) for n in range(parts)]
        for n, (first, size) in enumerate(places):
            for m, holder in enumerate((core, 1 - core)):
                there = pl.ds(pl.multiple_of(first + holder * half, 16), size)
                copies.append(self.start(pieces[1 + 2 * n + m], target.at[there]))
        return copies


def window_heads(scalars, count, rows, text_dev, gathered, width, extra, text, text_t=None):
    half = rows // 2
    for k in range(count):
        there = pl.ds(pl.multiple_of(k * rows + scalars[0] * half, 16), half)
        extra[k] = gathered[there, width:].astype(jnp.float32)
    for i in range(text.shape[0]):
        head = scalars[5] + i
        first = pl.ds(pl.multiple_of(head // 2 * text_dev, 8), text_dev)
        found = jnp.concatenate([extra[k, first, :] for k in range(count)], axis=0)
        found = jnp.where(head % 2 == 0, found[:, :HD], found[:, HD:])
        text[i] = found.astype(jnp.bfloat16)
        if text_t is not None:
            text_t[i] = found.T.astype(jnp.bfloat16)


def project_kernel(slots, count, rows, shard, width, text_dev, scalars, gain, *refs):
    refs = list(refs)
    take = lambda n: [refs.pop(0) for _ in range(n)]
    mod_in = take(9)
    w_in = take(8)
    qkv, k_t, raw_all, inv_all, text, text_t, w_keep, w_give = take(8)
    w_all, mod_all, sems, extra = take(4)
    inner = slots * HD
    core = scalars[0]
    copies = Copies(sems)
    w_copies = copies.weights(scalars, w_in, w_all, shard)
    row_copies = copies.rows(core, mod_in, mod_all, rows)

    lane = lax.broadcasted_iota(jnp.int32, (1, 2 * inner), 1)
    gains = head_gains(gain, slots) * jnp.where(lane < inner, HD ** (-0.5), 1.0)
    identity = equal_blocks(inner, 1)
    for copy in w_copies:
        copy.wait()
    half = width // 2
    columns = pl.ds(0, w_keep.shape[1])
    half_copies = [
        copies.start(w_all.at[pl.ds(pl.multiple_of(holder * half, 16), half), columns], target)
        for holder, target in ((core, w_keep), (1 - core, w_give))
    ]
    for copy in row_copies:
        copy.wait()
    window_heads(scalars, count, rows, text_dev, mod_all, width, extra, text, text_t)
    span = 2 * rows
    for b in range(count // 2):
        here = slice(b * span, (b + 1) * span)
        projected = jnp.dot(
            mod_all[here, :width], w_all[:, : 3 * inner], preferred_element_type=jnp.float32
        )
        raw = projected[:, : 2 * inner]
        inverse = lax.rsqrt(head_means(raw * raw) + 1e-06)
        raw_all[here, :] = raw
        inv_all[here, :] = inverse
        qkv[here, : 2 * inner] = (raw * inverse * gains).astype(jnp.bfloat16)
        qkv[here, 2 * inner :] = projected[:, 2 * inner :].astype(jnp.bfloat16)
        k_t[:, here] = dot(identity, qkv[here, inner : 2 * inner], NT).astype(jnp.bfloat16)
    for copy in half_copies:
        copy.wait()


def attend_kernel(slots, count, rows, shard, width, text_dev, first_column, scalars, gain, *refs):
    refs = list(refs)
    take = lambda n: [refs.pop(0) for _ in range(n)]
    projected = take(8)
    cot_in = take(7)
    w_in = take(4)
    mine_out, theirs_out, rest_out = take(3)
    w_out, cot_all, sems, extra, values_text = take(5)
    d_all, grads, stacked = take(3)
    qkv, k_t, raw_all, inv_all, text, text_t, w_keep, w_give = refs
    inner = slots * HD
    tokens = rows * count
    core = scalars[0]
    copies = Copies(sems)
    w_copies = copies.weights(scalars, w_in, w_out, shard, first_column)
    row_copies = copies.rows(core, cot_in, cot_all, rows)
    local_copies = [copies.start(*one) for one in zip(projected, refs)]
    score_scale = HD ** (-0.5)
    span = 2 * rows

    text_rows = count * text_dev
    row = lax.broadcasted_iota(jnp.int32, (text_rows, span), 0)
    text_id = row
    for k in range(count):
        inside = (row >= k * text_dev) & (row < (k + 1) * text_dev)
        text_id = jnp.where(inside, row + (scalars[7 + k] - k) * text_dev, text_id)
    bias = jnp.where(text_id < scalars[6], 0.0, -1e30)

    for copy in w_copies:
        copy.wait()
    arrivals = [row_copies[:3], row_copies[3:]]
    for b in range(count // 2):
        for copy in arrivals[b]:
            copy.wait()
        here = slice(b * span, (b + 1) * span)
        out_grad = jnp.dot(cot_all[here, :width], w_out[...], preferred_element_type=jnp.float32)
        d_all[here, :] = out_grad.astype(jnp.bfloat16)
    window_heads(scalars, count, rows, text_dev, cot_all, width, extra, values_text)
    for copy in local_copies[:6]:
        copy.wait()

    d_first = d_all.shape[1] - inner
    for i in range(slots):
        columns = [slice(n * inner + i * HD, n * inner + (i + 1) * HD) for n in range(3)]
        keys, values = qkv[:, columns[1]], qkv[:, columns[2]]
        keys_t = k_t[i * HD : (i + 1) * HD, :]
        grad_k, grad_v = 0.0, 0.0
        for b in range(count // 2):
            here = slice(b * span, (b + 1) * span)
            query = qkv[here, columns[0]]
            grad = d_all[here, d_first + i * HD : d_first + (i + 1) * HD]
            scores = dot(keys, query, NT)
            text_scores = dot(text[i], query, NT) + bias
            col_max = jnp.maximum(
                jnp.max(scores, axis=0, keepdims=True), jnp.max(text_scores, axis=0, keepdims=True)
            )
            exps = jnp.exp(scores - col_max)
            text_exps = jnp.exp(text_scores - col_max)
            total = jnp.sum(exps, axis=0, keepdims=True) + jnp.sum(text_exps, axis=0, keepdims=True)
            inverse = 1.0 / total
            grad_w = dot(values, grad, NT)
            text_grad_w = dot(values_text[i], grad, NT)
            delta = inverse * (
                jnp.sum(exps * grad_w, axis=0, keepdims=True)
                + jnp.sum(text_exps * text_grad_w, axis=0, keepdims=True)
            )
            weights = exps * inverse
            grad_s = (weights * (grad_w - delta)).astype(jnp.bfloat16)
            text_grad_s = (text_exps * inverse * (text_grad_w - delta)).astype(jnp.bfloat16)
            grad_k += dot(grad_s, query, NN)
            grad_v += dot(weights.astype(jnp.bfloat16), grad, NN)
            grad_q = dot(keys_t, grad_s, NN) + dot(text_t[i], text_grad_s, NN)
            grads[here, columns[0]] = grad_q.T * score_scale
        grads[:, columns[1]] = grad_k
        grads[:, columns[2]] = grad_v

    lane = lax.broadcasted_iota(jnp.int32, (1, inner), 1)
    mine = jnp.zeros((1, inner), jnp.float32)
    for i in range(slots):
        inside = (lane >= i * HD) & (lane < (i + 1) * HD) & (scalars[7 + count + i] > 0)
        mine = jnp.where(inside, 1.0, mine)
    gains = head_gains(gain, slots)
    for b in range(count // 2):
        here = slice(b * span, (b + 1) * span)
        scaled = grads[here, : 2 * inner].astype(jnp.bfloat16).astype(jnp.float32) * gains
        raw, inverse = raw_all[here, :], inv_all[here, :]
        back = scaled * inverse - raw * head_means(scaled * raw) * (inverse * inverse * inverse)
        valid = jnp.concatenate([mine, mine], axis=1) > 0.0
        stacked[here, : 2 * inner] = jnp.where(valid, back, 0.0).astype(jnp.bfloat16)
        back = jnp.where(mine > 0.0, grads[here, 2 * inner :], 0.0).astype(jnp.bfloat16)
        stacked[here, 2 * inner : 3 * inner] = back
    stacked[:, 3 * inner :] = jnp.zeros((tokens, stacked.shape[1] - 3 * inner), jnp.bfloat16)
    first = stacked[rows : 2 * rows, :]
    rest_out[: (count - 2) * rows, :] = stacked[2 * rows :, :]
    rest_out[(count - 2) * rows :, :] = stacked[:rows, :]
    for copy in local_copies[6:]:
        copy.wait()
    theirs_out[...] = dot(first, w_give[...], NT).astype(jnp.bfloat16)
    mine_out[...] = dot(first, w_keep[...], NT)


def project_call(scalars, gain, mod, weights, slots, rows, text_dev, count):
    shard = weights[0].shape[0]
    columns = 4 * slots * HD
    width = mod[0].shape[1] - EXTRA
    tokens = rows * count
    text_rows = text_dev * count
    f32, bf16 = jnp.float32, jnp.bfloat16
    vmem, hbm = spec(pltpu.VMEM), spec(pl.ANY)
    inner = slots * HD
    shapes = [((tokens, 3 * inner), bf16), ((inner, tokens), bf16)] + [((tokens, 2 * inner), f32)] * 2
    shapes += [((slots, text_rows, HD), bf16), ((slots, HD, text_rows), bf16)]
    shapes += [((width // 2, whole_tiles(3 * slots * HD)), bf16)] * 2
    return pl.pallas_call(
        functools.partial(project_kernel, slots, count, rows, shard, width, text_dev),
        out_shape=tuple(jax.ShapeDtypeStruct(*one) for one in shapes),
        in_specs=[spec(pltpu.SMEM), vmem] + [hbm] * (len(mod) + len(weights)),
        out_specs=(vmem,) * (len(shapes) - 2) + (hbm,) * 2,
        scratch_shapes=[
            pltpu.VMEM((width, columns), bf16),
            pltpu.VMEM((tokens, width + EXTRA), bf16),
            pltpu.SemaphoreType.DMA((len(mod) + len(weights) + 2,)),
            pltpu.VMEM((count, rows // 2, EXTRA), f32),
        ],
        compiler_params=pltpu.CompilerParams(vmem_limit_bytes=GRANT),
        cost_estimate=pl.CostEstimate(
            flops=2 * tokens * width * 3 * slots * HD,
            bytes_accessed=2 * (tokens * width + columns * width) + 4 * tokens * columns,
            transcendentals=0,
        ),
    )(scalars, gain, *mod, *weights)


def attend_call(scalars, gain, operands, cot, weights, slots, rows, text_dev):
    count = operands[0].shape[0] // rows
    shard, columns = weights[0].shape
    width = cot[0].shape[1] - EXTRA
    tokens = rows * count
    inner = slots * HD
    stacked = whole_tiles(3 * inner)
    first = (columns - inner) // 128 * 128
    f32, bf16 = jnp.float32, jnp.bfloat16
    vmem, hbm = spec(pltpu.VMEM), spec(pl.ANY)
    shapes = [((rows, width // 2), f32), ((rows, width // 2), bf16), ((tokens - rows, stacked), bf16)]
    return pl.pallas_call(
        functools.partial(attend_kernel, slots, count, rows, shard, width, text_dev, first),
        out_shape=tuple(jax.ShapeDtypeStruct(*one) for one in shapes),
        in_specs=[spec(pltpu.SMEM), vmem] + [hbm] * (len(operands) + len(cot) + len(weights)),
        out_specs=(vmem,) * len(shapes),
        scratch_shapes=[
            pltpu.VMEM((width, columns - first), bf16),
            pltpu.VMEM((tokens, width + EXTRA), bf16),
            pltpu.SemaphoreType.DMA((len(operands) + len(cot) + len(weights),)),
            pltpu.VMEM((count, rows // 2, EXTRA), f32),
            pltpu.VMEM((slots, text_dev * count, HD), bf16),
            pltpu.VMEM((tokens, columns - first), bf16),
            pltpu.VMEM((tokens, 3 * inner), f32),
            pltpu.VMEM((tokens, stacked), bf16),
        ]
        + [pltpu.VMEM(one.shape, one.dtype) for one in operands],
        compiler_params=pltpu.CompilerParams(vmem_limit_bytes=GRANT),
        cost_estimate=pl.CostEstimate(
            flops=2 * tokens * width * inner + 10 * tokens * tokens * inner,
            bytes_accessed=2 * (tokens * width + columns * width),
            transcendentals=slots * tokens * tokens,
        ),
    )(scalars, gain, *operands, *cot, *weights)


def backward_kernel(own, other, w_own, w_other, *outs):
    total = dot(own[...], w_own[...], NT) + dot(other[...], w_other[...], NT)
    part = outs[0].shape[0]
    for n, out in enumerate(outs):
        out[...] = total[n * part : (n + 1) * part].astype(out.dtype)


def backward_call(own, other, w_own, w_other, part, dtype):
    rows, inner = own.shape
    half = w_own.shape[0]
    vmem = spec(pltpu.VMEM)
    return pl.pallas_call(
        backward_kernel,
        out_shape=(jax.ShapeDtypeStruct((part, half), dtype),) * (rows // part),
        in_specs=[vmem] * 4,
        out_specs=(vmem,) * (rows // part),
        compiler_params=pltpu.CompilerParams(vmem_limit_bytes=SMALL_GRANT),
        cost_estimate=pl.CostEstimate(
            flops=4 * rows * half * inner,
            bytes_accessed=4 * (rows + half) * inner + 4 * rows * half,
            transcendentals=0,
        ),
    )(own, other, w_own, w_other)


def sums_kernel(own_near, own_far, near, far, scale, normed, grad_out, sums_out):
    half = near.shape[0]
    for part, (own, moving) in enumerate(((own_near, near), (own_far, far))):
        here = slice(part * half, (part + 1) * half)
        grad = (own[...] + moving[...].astype(jnp.float32)) * scale[...]
        grad_out[here, :] = grad
        first = jnp.sum(grad, axis=-1, keepdims=True)
        second = jnp.sum(grad * normed[here, :], axis=-1, keepdims=True)
        lane = lax.broadcasted_iota(jnp.int32, (half, 128), 1)
        sums_out[here, :] = jnp.where(lane == 0, first, second)


def last_kernel(width, grad, sums, other, normed, base, inv_std, out):
    total = (sums[...] + other[...]) * (1.0 / width)
    rows = base[...] + inv_std[:, 0:1] * (
        grad[...] - total[:, 0:1] - normed[...] * total[:, 1:2]
    )
    out[...] = rows.T


def local_call(kernel, shapes, scalar_count, *operands):
    vmem = spec(pltpu.VMEM)
    return pl.pallas_call(
        kernel,
        out_shape=tuple(jax.ShapeDtypeStruct(*one) for one in shapes),
        in_specs=[spec(pltpu.SMEM)] * scalar_count + [vmem] * (len(operands) - scalar_count),
        out_specs=(vmem,) * len(shapes),
        compiler_params=pltpu.CompilerParams(vmem_limit_bytes=SMALL_GRANT),
        cost_estimate=pl.CostEstimate(
            flops=sum(one.size for one in operands),
            bytes_accessed=sum(one.size * one.dtype.itemsize for one in operands),
            transcendentals=0,
        ),
    )(*operands)


def shards_by_head(states, adjoint, text_kv, text_len, step_index, modulation, w_qkv, qk_gain, w_out):
    hidden_state = states[0]
    adjoint_rows = adjoint[0]
    tok_count, model_width = hidden_state.shape
    seq_count = lax.axis_size("seq")
    inner_dev = w_qkv.shape[2]
    heads_dev = inner_dev // HD
    shard = w_qkv.shape[0]
    slots = -(-heads_dev // seq_count)
    inner = slots * HD
    half_rows = tok_count // 2
    half_width = model_width // 2
    f32, bf16 = jnp.float32, jnp.bfloat16
    core = lax.axis_index("head").astype(jnp.int32)
    seq_index = lax.axis_index("seq")
    dp_index = lax.axis_index("dp")
    pin = lax.optimization_barrier

    seq_order = line_ring(seq_count)
    seq_place = ring_place(seq_order, seq_index)
    seq_next = ring_pairs(seq_order)
    swap = [(0, 1), (1, 0)]
    first_way = [(2 * p + c, 2 * (p ^ (1 + c)) + c) for p in range(4) for c in range(2)]
    second_way = [(2 * p + c, 2 * (p ^ (2 - c)) + c) for p in range(4) for c in range(2)]

    first = seq_index * heads_dev // seq_count
    stop = (seq_index + 1) * heads_dev // seq_count
    window = jnp.minimum(first, heads_dev - slots)
    valid = [(window + i >= first) & (window + i < stop) for i in range(slots)]
    owners = [ring_member(seq_order, (seq_place - k + seq_count) % seq_count) for k in range(seq_count)]
    w_index = [dp_index, dp_index ^ (1 + core), dp_index ^ (2 - core), dp_index ^ 3]
    scalars = [core] + w_index + [window, text_len[0]] + owners + valid
    scalars = jnp.stack([one.astype(jnp.int32) for one in scalars])

    def step(moving):
        return lax.ppermute(moving, "seq", seq_next)

    def other_core(moving):
        return lax.ppermute(moving, "head", swap)

    def step_back(moving):
        return lax.ppermute(moving, "seq", [(b, a) for a, b in seq_next])

    quarter = half_rows // 2

    def spread(moving):
        return [step(moving), step_back(moving)]

    def pass_on(received):
        return [step(received[0][:quarter]), step_back(received[1][quarter:])]

    mod_half, table_rows, extra = first_call(
        step_index, core[None], hidden_state, modulation.transpose(1, 0, 2), adjoint_rows, text_kv[0]
    )
    mod_near = spread(mod_half)

    w_qkv, w_out, mod_half = pin((w_qkv, w_out, mod_half))
    take = lambda c: lax.dynamic_slice(w_qkv, (0, c, window * HD), (shard, 1, inner))[:, 0]
    own_w = [
        jnp.concatenate([take(0), take(1)], axis=1),
        jnp.concatenate([take(2), lax.dynamic_slice_in_dim(w_out, window * HD, inner, 0).T], axis=1),
    ]
    w_first = [lax.ppermute(part, ("dp", "head"), first_way) for part in own_w]
    w_second = [lax.ppermute(part, ("dp", "head"), second_way) for part in own_w]

    text_dev = text_kv.shape[1]
    mod_far = pass_on(mod_near)
    clip_limit = 0.5 * (tok_count * seq_count * model_width) ** 0.5
    extra, *w_first = pin((extra, *w_first))
    cotangent, cot_half, base = cotangent_call(
        clip_limit, scalars, adjoint_rows, table_rows, text_kv[0], extra, *mod_near, mod_far[1]
    )
    cot_half, mod_far[0] = pin((cot_half, mod_far[0]))
    cot_near = spread(cot_half)
    modulated, normed_share, scale_share, inv_std = local_call(
        modulate_kernel,
        [
            ((tok_count, model_width + EXTRA), bf16),
            ((tok_count, half_width), f32),
            ((1, half_width), f32),
            ((tok_count, 128), f32),
        ],
        1,
        core[None],
        hidden_state,
        table_rows,
        extra,
    )
    def pieces(own, received):
        return [own] + [one for moved in received for one in (moved, other_core(moved))]

    mod_far = list(pin((*mod_far, modulated))[:2])
    mod_pieces = pieces(modulated, mod_near + mod_far)
    w_diagonal = [lax.ppermute(part, ("dp", "head"), second_way) for part in w_first]
    weights = [part[n] for n in range(2) for part in (own_w, w_first, w_second, w_diagonal)]
    cot_near[0], mod_pieces[5:] = pin((cot_near[0], mod_pieces[5:], w_second, w_diagonal))[:2]
    cot_far = [step(cot_near[0])]

    cot_pieces = pieces(cotangent, cot_near)
    *cot_pieces, mod_pieces[-1] = pin((*cot_pieces, mod_pieces[-1]))
    *operands, w_keep, w_give = project_call(
        scalars, qk_gain, mod_pieces, weights, slots, tok_count, text_dev, seq_count
    )
    w_give, cot_far[0] = pin((w_give, *cot_far))
    cot_pieces += pieces(None, cot_far)[1:]
    given, *cot_pieces = pin((w_give, *cot_pieces))
    w_other = other_core(given)
    mine, theirs, rest = attend_call(
        scalars, qk_gain, operands + [w_keep, w_give], cot_pieces, weights[4:], slots, tok_count, text_dev
    )
    first = (mine + other_core(theirs).astype(f32)).astype(bf16)
    moving = [first[:half_rows], first[half_rows:]]
    other_rest = other_core(rest)
    rest, other_rest, *_ = pin((rest, other_rest, *moving))
    own = backward_call(rest, other_rest, w_keep, w_other, half_rows, f32)
    for j in range(2, seq_count):
        moving = [step(part) for part in moving]
        moving = [
            (a + b.astype(f32)).astype(bf16) for a, b in zip(own[2 * (j - 2) : 2 * (j - 1)], moving)
        ]
    moving = [step(part) for part in moving]

    grad_scaled, sums = local_call(
        sums_kernel,
        [((tok_count, half_width), f32), ((tok_count, 128), f32)],
        0,
        *own[-2:],
        *moving,
        scale_share,
        normed_share,
    )
    (pulled,) = local_call(
        functools.partial(last_kernel, model_width),
        [((half_width, tok_count), f32)],
        0,
        grad_scaled,
        sums,
        other_core(sums),
        normed_share,
        base,
        inv_std,
    )
    return pulled.T[None]


def qk_normalize(values, gains):
    inverse = lax.rsqrt(jnp.mean(values * values, axis=-1, keepdims=True) + 1e-06)
    return ((values * inverse * gains).astype(jnp.bfloat16), inverse)


def qk_backward(values, inverse, cotangent, gains):
    scaled = cotangent.astype(jnp.float32) * gains
    return (
        scaled * inverse - values * jnp.mean(scaled * values, axis=-1, keepdims=True) * inverse**3
    )


def shards_by_row(states, adjoint, text_kv, text_len, step_index, modulation, w_qkv, qk_gain, w_out):
    hidden_state = states[0]
    adjoint_rows = adjoint[0]
    tok_count, model_width = hidden_state.shape
    seq_count = lax.axis_size("seq")
    inner_dev = w_qkv.shape[2]
    heads_dev = inner_dev // HD
    score_scale = HD ** (-0.5)
    squares = lax.psum(jnp.sum(adjoint_rows * adjoint_rows), "seq")
    clip_limit = 0.5 * (tok_count * seq_count * model_width) ** 0.5
    clip_scale = jnp.minimum(1.0, clip_limit / jnp.sqrt(squares + 1e-06))
    table_row = lax.dynamic_index_in_dim(modulation, step_index[0], 0, keepdims=False)
    offset_row = table_row[0]
    stretch = table_row[1]
    gating = table_row[2]
    widened = hidden_state.astype(jnp.float32)
    centered = widened - jnp.mean(widened, axis=-1, keepdims=True)
    inv_std = lax.rsqrt(jnp.mean(centered * centered, axis=-1, keepdims=True) + 1e-06)
    normed = centered * inv_std
    modulated = (normed * (1.0 + stretch) + offset_row).astype(jnp.bfloat16)
    cotangent = (gating * (clip_scale * adjoint_rows)).astype(jnp.bfloat16)
    contract_last = (((1,), (1,)), ((), ()))
    full_weight = lax.all_gather(w_qkv, "dp", axis=0, tiled=True).reshape(
        model_width, 3 * inner_dev
    )
    projected = jnp.dot(modulated, full_weight, preferred_element_type=jnp.float32)
    out_raw = lax.dot_general(
        cotangent,
        lax.all_gather(w_out, "dp", axis=1, tiled=True),
        contract_last,
        preferred_element_type=jnp.float32,
    )
    projected = projected.reshape(tok_count, 3, heads_dev, HD)
    queries, query_inv = qk_normalize(projected[:, 0], qk_gain[0])
    own_keys, key_inv = qk_normalize(projected[:, 1], qk_gain[1])
    own_values = projected[:, 2].astype(jnp.bfloat16)
    out_grad = out_raw.astype(jnp.bfloat16).reshape(tok_count, heads_dev, HD)
    text_keys = text_kv[0, :, 0, :]
    text_values = text_kv[0, :, 1, :]
    text_dev = text_keys.shape[0]
    rows_dev = tok_count + text_dev
    key_local = jnp.concatenate([own_keys.reshape(tok_count, inner_dev), text_keys], axis=0)
    value_local = jnp.concatenate([own_values.reshape(tok_count, inner_dev), text_values], axis=0)
    key_all, value_all = (
        lax.all_gather(key_local, "seq", axis=0, tiled=True),
        lax.all_gather(value_local, "seq", axis=0, tiled=True),
    )
    all_rows = rows_dev * seq_count
    row_ids = jnp.arange(all_rows, dtype=jnp.int32)
    owner = row_ids // rows_dev
    within = row_ids % rows_dev
    allowed = (within < tok_count) | (owner * text_dev + within - tok_count < text_len[0])
    group = 1
    while group * 2 * rows_dev <= 512 and seq_count % (group * 2) == 0:
        group = group * 2
    block_rows = group * rows_dev
    block_count = all_rows // block_rows
    key_blocks = key_all.reshape(block_count, block_rows, heads_dev, HD)
    value_blocks = value_all.reshape(block_count, block_rows, heads_dev, HD)
    mask_blocks = allowed.reshape(block_count, block_rows)

    def block_scores(key_block, mask_block):
        scores = (
            jnp.einsum("qhd,khd->qhk", queries, key_block, preferred_element_type=jnp.float32)
            * score_scale
        )
        return jnp.where(mask_block[None, None, :], scores, -1e30)

    def first_pass(carry, block):
        row_max, row_sum, row_dot = carry
        key_block, value_block, mask_block = block
        scores = block_scores(key_block, mask_block)
        new_max = jnp.maximum(row_max, jnp.max(scores, axis=-1))
        rescale = jnp.exp(row_max - new_max)
        exps = jnp.exp(scores - new_max[:, :, None])
        grad_weights = jnp.einsum(
            "qhd,khd->qhk", out_grad, value_block, preferred_element_type=jnp.float32
        )
        return (
            (
                new_max,
                row_sum * rescale + jnp.sum(exps, axis=-1),
                row_dot * rescale + jnp.sum(exps * grad_weights, axis=-1),
            ),
            None,
        )

    start_state = (
        jnp.full((tok_count, heads_dev), -1e30, jnp.float32),
        jnp.zeros((tok_count, heads_dev), jnp.float32),
        jnp.zeros((tok_count, heads_dev), jnp.float32),
    )
    (row_max, row_sum, row_dot), unused = lax.scan(
        first_pass, start_state, (key_blocks, value_blocks, mask_blocks)
    )
    log_total = row_max + jnp.log(row_sum)
    delta_row = row_dot / row_sum

    def second_pass(running, block):
        key_block, value_block, mask_block = block
        weights = jnp.exp(block_scores(key_block, mask_block) - log_total[:, :, None])
        grad_weights = jnp.einsum(
            "qhd,khd->qhk", out_grad, value_block, preferred_element_type=jnp.float32
        )
        grad_scores = (weights * (grad_weights - delta_row[:, :, None])).astype(jnp.bfloat16)
        return (
            running
            + jnp.einsum(
                "qhk,khd->qhd", grad_scores, key_block, preferred_element_type=jnp.float32
            ),
            None,
        )

    query_sum, unused = lax.scan(
        second_pass,
        jnp.zeros((tok_count, heads_dev, HD), jnp.float32),
        (key_blocks, value_blocks, mask_blocks),
    )
    grad_query = (query_sum * score_scale).astype(jnp.bfloat16)
    log_all, delta_all = (
        lax.all_gather(log_total, "seq", axis=0, tiled=True),
        lax.all_gather(delta_row, "seq", axis=0, tiled=True),
    )
    local_ids = jnp.arange(rows_dev, dtype=jnp.int32)
    local_allowed = (local_ids < tok_count) | (
        lax.axis_index("seq") * text_dev + local_ids - tok_count < text_len[0]
    )
    key_three = key_local.reshape(rows_dev, heads_dev, HD)
    value_three = value_local.reshape(rows_dev, heads_dev, HD)
    query_piece = lax.all_gather(queries.reshape(tok_count, inner_dev), "seq", axis=0, tiled=True)
    grad_piece = lax.all_gather(out_grad.reshape(tok_count, inner_dev), "seq", axis=0, tiled=True)
    piece_rows = query_piece.shape[0]
    query_rows = query_piece.reshape(piece_rows, heads_dev, HD)
    grad_rows = grad_piece.reshape(piece_rows, heads_dev, HD)
    scores = (
        jnp.einsum("qhd,khd->qhk", query_rows, key_three, preferred_element_type=jnp.float32)
        * score_scale
    )
    scores = jnp.where(local_allowed[None, None, :], scores, -1e30)
    weights = jnp.exp(scores - log_all[:, :, None])
    grad_weights = jnp.einsum(
        "qhd,khd->qhk", grad_rows, value_three, preferred_element_type=jnp.float32
    )
    grad_scores = (weights * (grad_weights - delta_all[:, :, None])).astype(jnp.bfloat16)
    rounded = weights.astype(jnp.bfloat16)
    key_sum = jnp.einsum(
        "qhk,qhd->khd", grad_scores, query_rows, preferred_element_type=jnp.float32
    )
    value_sum = jnp.einsum("qhk,qhd->khd", rounded, grad_rows, preferred_element_type=jnp.float32)
    key_sum, value_sum = (key_sum, value_sum)
    grad_key = (key_sum[:tok_count] * score_scale).astype(jnp.bfloat16)
    grad_value = value_sum[:tok_count].astype(jnp.bfloat16)
    raw_query = qk_backward(projected[:, 0], query_inv, grad_query, qk_gain[0])
    raw_key = qk_backward(projected[:, 1], key_inv, grad_key, qk_gain[1])
    stacked = jnp.stack([raw_query, raw_key, grad_value.astype(jnp.float32)], axis=1).astype(
        jnp.bfloat16
    )
    stacked = stacked.reshape(tok_count, 3 * inner_dev)
    partial_grad = lax.dot_general(
        stacked, full_weight, contract_last, preferred_element_type=jnp.float32
    )
    half_width = model_width // lax.axis_size("head")
    first_col = lax.axis_index("head") * half_width
    grad_share = lax.psum_scatter(
        partial_grad.astype(jnp.bfloat16), "head", scatter_dimension=1, tiled=True
    ).astype(jnp.float32)
    normed_share = lax.dynamic_slice_in_dim(normed, first_col, half_width, 1)
    stretch_share = lax.dynamic_slice_in_dim(stretch, first_col, half_width, 0)
    adjoint_share = lax.dynamic_slice_in_dim(adjoint_rows, first_col, half_width, 1)
    grad_scaled = grad_share * (1.0 + stretch_share)
    row_sums = jnp.stack(
        [jnp.sum(grad_scaled, axis=-1), jnp.sum(grad_scaled * normed_share, axis=-1)], axis=-1
    )
    row_sums = lax.psum(row_sums, "head")
    grad_state = inv_std * (
        grad_scaled - row_sums[:, 0:1] / model_width - normed_share * row_sums[:, 1:2] / model_width
    )
    pulled = clip_scale * adjoint_share + grad_state
    return pulled[None]


def solution(mesh):
    in_specs = (
        P("dp", "seq", None),
        P("dp", "seq", None),
        P("dp", "seq", None, "head"),
        P("dp"),
        P("dp"),
        P(),
        P("dp", None, "head"),
        P(),
        P("head", "dp"),
    )
    out_specs = P("dp", "seq", "head")
    by_head = mesh.shape["seq"] == 4 and mesh.shape["dp"] == 4 and mesh.shape["head"] == 2
    shards = shards_by_head if by_head else shards_by_row
    return jax.shard_map(shards, mesh=mesh, in_specs=in_specs, out_specs=out_specs, check_vma=False)
```

```python
import functools

import jax
import jax.numpy as jnp
from jax import lax
from jax.experimental import pallas as pl
from jax.experimental.pallas import tpu as pltpu
from jax.sharding import PartitionSpec as P

HD = 64
GRANT = 60 * 1024 * 1024
SMALL_GRANT = 24 * 1024 * 1024
EXTRA = 128
NT = (((1,), (1,)), ((), ()))
NN = (((1,), (0,)), ((), ()))


def line_ring(count):
    return [0] + list(range(1, count, 2)) + [i for i in range(count - 1, 0, -1) if i % 2 == 0]


def ring_pairs(order):
    return [(order[i], order[(i + 1) % len(order)]) for i in range(len(order))]


def ring_place(order, index):
    place = jnp.int32(0)
    for position, member in enumerate(order):
        place = jnp.where(index == member, jnp.int32(position), place)
    return place


def ring_member(order, place):
    member = jnp.int32(order[0])
    for position, value in enumerate(order):
        member = jnp.where(place == position, jnp.int32(value), member)
    return member


def dot(a, b, dims):
    return lax.dot_general(a, b, dims, preferred_element_type=jnp.float32)


def equal_blocks(columns, block):
    row = lax.broadcasted_iota(jnp.int32, (columns, columns), 0)
    column = lax.broadcasted_iota(jnp.int32, (columns, columns), 1)
    return jnp.where(row // block == column // block, 1.0, 0.0).astype(jnp.bfloat16)


def head_means(values):
    ones = equal_blocks(values.shape[1], HD)
    total = 0.0
    for n in range(3):
        term = values.astype(jnp.bfloat16)
        total = total + dot(term, ones, NN)
        if n < 2:
            values = values - term.astype(jnp.float32)
    return total * (1.0 / HD)


def head_gains(gain, slots):
    return jnp.concatenate([gain[0:1, :]] * slots + [gain[1:2, :]] * slots, axis=1)


def whole_tiles(columns):
    return -(-columns // 128) * 128


def spec(space):
    return pl.BlockSpec(memory_space=space)


def text_columns(text, part):
    rows = text[...].astype(jnp.float32)[:, part, :]
    return [rows[:, c * EXTRA : (c + 1) * EXTRA] for c in range(rows.shape[1] // EXTRA)]


def extra_columns(blocks, rows):
    filled = sum(one.shape[0] for one in blocks)
    blocks = blocks + [jnp.zeros((rows - filled, EXTRA), jnp.float32)]
    return jnp.concatenate(blocks, axis=0).astype(jnp.bfloat16)


def first_kernel(step, core, states, table, adjoint, text, out, rows_out, extra_out):
    rows = [table[c, pl.ds(step[0], 1), :] for c in range(3)]
    widened = states[...].astype(jnp.float32)
    centered = widened - jnp.mean(widened, axis=-1, keepdims=True)
    inv_std = lax.rsqrt(jnp.mean(centered * centered, axis=-1, keepdims=True) + 1e-06)
    half, width = states.shape
    out[:, :width] = (centered * inv_std * (1.0 + rows[1]) + rows[0]).astype(jnp.bfloat16)
    for c in range(3):
        rows_out[c : c + 1, :] = rows[c]
    squares = jnp.sum(adjoint[...] * adjoint[...], axis=0, keepdims=True)
    squares = jnp.sum(squares, axis=1, keepdims=True)
    terms = []
    for n in range(3):
        terms.append(squares.astype(jnp.bfloat16).astype(jnp.float32))
        squares = squares - terms[-1]
    lane = lax.broadcasted_iota(jnp.int32, (8, EXTRA), 1)
    sums = jnp.where(lane == 0, terms[0], jnp.where(lane == 1, terms[1], jnp.where(lane == 2, terms[2], 0.0)))
    extra = extra_columns(text_columns(text, 0) + [sums], half)
    out[:, width:] = extra
    extra_out[...] = extra


def first_call(step, core, states, table, adjoint, text):
    rows, width = states.shape
    half = rows // 2
    whole = lambda *shape: pl.BlockSpec(shape, lambda i, step, core: (0,) * len(shape))
    return pl.pallas_call(
        first_kernel,
        out_shape=(
            jax.ShapeDtypeStruct((half, width + EXTRA), jnp.bfloat16),
            jax.ShapeDtypeStruct((8, width), jnp.float32),
            jax.ShapeDtypeStruct((half, EXTRA), jnp.bfloat16),
        ),
        grid_spec=pltpu.PrefetchScalarGridSpec(
            num_scalar_prefetch=2,
            grid=(1,),
            in_specs=[
                pl.BlockSpec((half, width), lambda i, step, core: (core[0], 0)),
                whole(*table.shape),
                whole(*adjoint.shape),
                whole(*text.shape),
            ],
            out_specs=(whole(half, width + EXTRA), whole(8, width), whole(half, EXTRA)),
        ),
        compiler_params=pltpu.CompilerParams(vmem_limit_bytes=GRANT),
        cost_estimate=pl.CostEstimate(flops=8 * half * width, bytes_accessed=16 * half * width, transcendentals=0),
    )(step, core, states, table, adjoint, text)


def pick_half(core, rows):
    half = rows.shape[1] // 2
    return jnp.where(core == 0, rows[:, :half], rows[:, half:])


def cotangent_kernel(limit, core, adjoint, table_rows, text, extra, previous, following, opposite, out, clip_out):
    first = previous.shape[0] - opposite.shape[0]
    row = 8 * (text.shape[2] // EXTRA)
    squares = opposite[...].astype(jnp.float32)[row - first : row - first + 1, :]
    for terms in (extra, previous, following):
        squares = squares + terms[...].astype(jnp.float32)[row : row + 1, :]
    squares = jnp.sum(squares, axis=1, keepdims=True)
    clip_scale = jnp.minimum(1.0, limit / jnp.sqrt(squares + 1e-06))
    half, width = adjoint.shape
    out[:, :width] = (table_rows[2:3, :] * (clip_scale * adjoint[...])).astype(jnp.bfloat16)
    out[:, width:] = extra_columns(text_columns(text, 1), half)
    clip_out[...] = jnp.broadcast_to(clip_scale, clip_out.shape)


def cotangent_call(limit, core, adjoint, table_rows, text, extra, previous, following, opposite):
    rows, width = adjoint.shape
    half = rows // 2
    block = width // EXTRA
    whole = lambda one: pl.BlockSpec(one.shape, lambda i, core: (0,) * one.ndim)
    tail = lambda one: pl.BlockSpec((one.shape[0], EXTRA), lambda i, core: (0, block))
    outs = (
        jax.ShapeDtypeStruct((half, width + EXTRA), jnp.bfloat16),
        jax.ShapeDtypeStruct((8, EXTRA), jnp.float32),
    )
    return pl.pallas_call(
        functools.partial(cotangent_kernel, limit),
        out_shape=outs,
        grid_spec=pltpu.PrefetchScalarGridSpec(
            num_scalar_prefetch=1,
            grid=(1,),
            in_specs=[pl.BlockSpec((half, width), lambda i, core: (core[0], 0))]
            + [whole(table_rows), whole(text), whole(extra)]
            + [tail(one) for one in (previous, following, opposite)],
            out_specs=tuple(whole(one) for one in outs),
        ),
        compiler_params=pltpu.CompilerParams(vmem_limit_bytes=GRANT),
        cost_estimate=pl.CostEstimate(flops=4 * half * width, bytes_accessed=6 * half * width, transcendentals=0),
    )(core, adjoint, table_rows, text, extra, previous, following, opposite)


def own_kernel(
    core, states, adjoint, table_rows, text, extra, clip, out, cot_out, normed_out, stretch_out, inv_out, base_out
):
    rows, width = states.shape
    half = rows // 2
    widened = states[...].astype(jnp.float32)
    centered = widened - jnp.mean(widened, axis=-1, keepdims=True)
    inv_std = lax.rsqrt(jnp.mean(centered * centered, axis=-1, keepdims=True) + 1e-06)
    normed = centered * inv_std
    scale = 1.0 + table_rows[1:2, :]
    out[:, :width] = (normed * scale + table_rows[0:1, :]).astype(jnp.bfloat16)
    normed_out[...] = pick_half(core[0], normed)
    stretch_out[...] = pick_half(core[0], scale)
    inv_out[...] = jnp.broadcast_to(inv_std, inv_out.shape)
    clipped = clip[0:1, 0:1] * adjoint[...]
    cot_out[:, :width] = (table_rows[2:3, :] * clipped).astype(jnp.bfloat16)
    base_out[...] = pick_half(core[0], clipped)
    columns = extra_columns(text_columns(text, 1), half)
    for n in range(2):
        out[n * half : (n + 1) * half, width:] = extra[...]
        cot_out[n * half : (n + 1) * half, width:] = columns


class Copies:
    def __init__(self, sems):
        self.sems = sems
        self.count = 0

    def start(self, source, target):
        copy = pltpu.make_async_copy(source, target, self.sems.at[self.count])
        copy.start()
        self.count += 1
        return copy

    def weights(self, scalars, w_in, w_all, shard, first=0):
        columns = w_in[0].shape[1] - first
        return [
            self.start(
                piece.at[:, pl.ds(first, columns)],
                w_all.at[
                    pl.ds(pl.multiple_of(scalars[1 + n % 4] * shard, 16), shard),
                    pl.ds(n // 4 * columns, columns),
                ],
            )
            for n, piece in enumerate(w_in)
        ]

    def rows(self, core, pieces, target, rows):
        half = rows // 2
        copies = [self.start(pieces[0], target.at[pl.ds(0, rows)])]
        places = [(rows, half), (3 * rows, half)]
        parts = (len(pieces) - 5) // 2
        places += [(2 * rows + n * half // parts, half // parts) for n in range(parts)]
        for n, (first, size) in enumerate(places):
            for m, holder in enumerate((core, 1 - core)):
                there = pl.ds(pl.multiple_of(first + holder * half, 16), size)
                copies.append(self.start(pieces[1 + 2 * n + m], target.at[there]))
        return copies


def window_heads(scalars, count, rows, text_dev, gathered, width, extra, text, text_t=None):
    half = rows // 2
    for k in range(count):
        there = pl.ds(pl.multiple_of(k * rows + scalars[0] * half, 16), half)
        extra[k] = gathered[there, width:].astype(jnp.float32)
    for i in range(text.shape[0]):
        head = scalars[5] + i
        first = pl.ds(pl.multiple_of(head // 2 * text_dev, 8), text_dev)
        found = jnp.concatenate([extra[k, first, :] for k in range(count)], axis=0)
        found = jnp.where(head % 2 == 0, found[:, :HD], found[:, HD:])
        text[i] = found.astype(jnp.bfloat16)
        if text_t is not None:
            text_t[i] = found.T.astype(jnp.bfloat16)


def project_kernel(slots, count, rows, shard, width, text_dev, scalars, gain, *refs):
    refs = list(refs)
    take = lambda n: [refs.pop(0) for _ in range(n)]
    mod_in = take(9)
    w_in = take(8)
    qkv, k_t, raw_all, inv_all, text, text_t, w_keep, w_give = take(8)
    w_all, mod_all, sems, extra = take(4)
    inner = slots * HD
    core = scalars[0]
    copies = Copies(sems)
    w_copies = copies.weights(scalars, w_in, w_all, shard)
    row_copies = copies.rows(core, mod_in, mod_all, rows)

    lane = lax.broadcasted_iota(jnp.int32, (1, 2 * inner), 1)
    gains = head_gains(gain, slots) * jnp.where(lane < inner, HD ** (-0.5), 1.0)
    identity = equal_blocks(inner, 1)
    for copy in w_copies:
        copy.wait()
    half = width // 2
    columns = pl.ds(0, w_keep.shape[1])
    half_copies = [
        copies.start(w_all.at[pl.ds(pl.multiple_of(holder * half, 16), half), columns], target)
        for holder, target in ((core, w_keep), (1 - core, w_give))
    ]
    for copy in row_copies:
        copy.wait()
    window_heads(scalars, count, rows, text_dev, mod_all, width, extra, text, text_t)
    span = 2 * rows
    for b in range(count // 2):
        here = slice(b * span, (b + 1) * span)
        projected = jnp.dot(
            mod_all[here, :width], w_all[:, : 3 * inner], preferred_element_type=jnp.float32
        )
        raw = projected[:, : 2 * inner]
        inverse = lax.rsqrt(head_means(raw * raw) + 1e-06)
        raw_all[here, :] = raw
        inv_all[here, :] = inverse
        qkv[here, : 2 * inner] = (raw * inverse * gains).astype(jnp.bfloat16)
        qkv[here, 2 * inner :] = projected[:, 2 * inner :].astype(jnp.bfloat16)
        k_t[:, here] = dot(identity, qkv[here, inner : 2 * inner], NT).astype(jnp.bfloat16)
    for copy in half_copies:
        copy.wait()


def attend_kernel(slots, count, rows, shard, width, text_dev, first_column, scalars, gain, *refs):
    refs = list(refs)
    take = lambda n: [refs.pop(0) for _ in range(n)]
    projected = take(8)
    cot_in = take(7)
    w_in = take(4)
    mine_out, theirs_out, rest_out = take(3)
    w_out, cot_all, sems, extra, values_text = take(5)
    d_all, grads, stacked = take(3)
    qkv, k_t, raw_all, inv_all, text, text_t, w_keep, w_give = refs
    inner = slots * HD
    tokens = rows * count
    core = scalars[0]
    copies = Copies(sems)
    w_copies = copies.weights(scalars, w_in, w_out, shard, first_column)
    row_copies = copies.rows(core, cot_in, cot_all, rows)
    local_copies = [copies.start(*one) for one in zip(projected, refs)]
    score_scale = HD ** (-0.5)
    span = 2 * rows

    text_rows = count * text_dev
    row = lax.broadcasted_iota(jnp.int32, (text_rows, span), 0)
    text_id = row
    for k in range(count):
        inside = (row >= k * text_dev) & (row < (k + 1) * text_dev)
        text_id = jnp.where(inside, row + (scalars[7 + k] - k) * text_dev, text_id)
    bias = jnp.where(text_id < scalars[6], 0.0, -1e30)

    for copy in w_copies:
        copy.wait()
    arrivals = [row_copies[:3], row_copies[3:]]
    for b in range(count // 2):
        for copy in arrivals[b]:
            copy.wait()
        here = slice(b * span, (b + 1) * span)
        out_grad = jnp.dot(cot_all[here, :width], w_out[...], preferred_element_type=jnp.float32)
        d_all[here, :] = out_grad.astype(jnp.bfloat16)
    window_heads(scalars, count, rows, text_dev, cot_all, width, extra, values_text)
    for copy in local_copies[:6]:
        copy.wait()

    d_first = d_all.shape[1] - inner
    for i in range(slots):
        columns = [slice(n * inner + i * HD, n * inner + (i + 1) * HD) for n in range(3)]
        keys, values = qkv[:, columns[1]], qkv[:, columns[2]]
        keys_t = k_t[i * HD : (i + 1) * HD, :]
        grad_k, grad_v = 0.0, 0.0
        for b in range(count // 2):
            here = slice(b * span, (b + 1) * span)
            query = qkv[here, columns[0]]
            grad = d_all[here, d_first + i * HD : d_first + (i + 1) * HD]
            scores = dot(keys, query, NT)
            text_scores = dot(text[i], query, NT) + bias
            col_max = jnp.maximum(
                jnp.max(scores, axis=0, keepdims=True), jnp.max(text_scores, axis=0, keepdims=True)
            )
            exps = jnp.exp(scores - col_max)
            text_exps = jnp.exp(text_scores - col_max)
            total = jnp.sum(exps, axis=0, keepdims=True) + jnp.sum(text_exps, axis=0, keepdims=True)
            inverse = 1.0 / total
            grad_w = dot(values, grad, NT)
            text_grad_w = dot(values_text[i], grad, NT)
            delta = inverse * (
                jnp.sum(exps * grad_w, axis=0, keepdims=True)
                + jnp.sum(text_exps * text_grad_w, axis=0, keepdims=True)
            )
            weights = exps * inverse
            grad_s = (weights * (grad_w - delta)).astype(jnp.bfloat16)
            text_grad_s = (text_exps * inverse * (text_grad_w - delta)).astype(jnp.bfloat16)
            grad_k += dot(grad_s, query, NN)
            grad_v += dot(weights.astype(jnp.bfloat16), grad, NN)
            grad_q = dot(keys_t, grad_s, NN) + dot(text_t[i], text_grad_s, NN)
            grads[here, columns[0]] = grad_q.T * score_scale
        grads[:, columns[1]] = grad_k
        grads[:, columns[2]] = grad_v

    lane = lax.broadcasted_iota(jnp.int32, (1, inner), 1)
    mine = jnp.zeros((1, inner), jnp.float32)
    for i in range(slots):
        inside = (lane >= i * HD) & (lane < (i + 1) * HD) & (scalars[7 + count + i] > 0)
        mine = jnp.where(inside, 1.0, mine)
    gains = head_gains(gain, slots)
    for b in range(count // 2):
        here = slice(b * span, (b + 1) * span)
        scaled = grads[here, : 2 * inner].astype(jnp.bfloat16).astype(jnp.float32) * gains
        raw, inverse = raw_all[here, :], inv_all[here, :]
        back = scaled * inverse - raw * head_means(scaled * raw) * (inverse * inverse * inverse)
        valid = jnp.concatenate([mine, mine], axis=1) > 0.0
        stacked[here, : 2 * inner] = jnp.where(valid, back, 0.0).astype(jnp.bfloat16)
        back = jnp.where(mine > 0.0, grads[here, 2 * inner :], 0.0).astype(jnp.bfloat16)
        stacked[here, 2 * inner : 3 * inner] = back
    stacked[:, 3 * inner :] = jnp.zeros((tokens, stacked.shape[1] - 3 * inner), jnp.bfloat16)
    first = stacked[rows : 2 * rows, :]
    rest_out[: (count - 2) * rows, :] = stacked[2 * rows :, :]
    rest_out[(count - 2) * rows :, :] = stacked[:rows, :]
    for copy in local_copies[6:]:
        copy.wait()
    theirs_out[...] = dot(first, w_give[...], NT).astype(jnp.bfloat16)
    mine_out[...] = dot(first, w_keep[...], NT)


def project_call(scalars, gain, mod, weights, slots, rows, text_dev, count):
    shard = weights[0].shape[0]
    columns = 4 * slots * HD
    width = mod[0].shape[1] - EXTRA
    tokens = rows * count
    text_rows = text_dev * count
    f32, bf16 = jnp.float32, jnp.bfloat16
    vmem, hbm = spec(pltpu.VMEM), spec(pl.ANY)
    inner = slots * HD
    shapes = [((tokens, 3 * inner), bf16), ((inner, tokens), bf16)] + [((tokens, 2 * inner), f32)] * 2
    shapes += [((slots, text_rows, HD), bf16), ((slots, HD, text_rows), bf16)]
    shapes += [((width // 2, whole_tiles(3 * slots * HD)), bf16)] * 2
    return pl.pallas_call(
        functools.partial(project_kernel, slots, count, rows, shard, width, text_dev),
        out_shape=tuple(jax.ShapeDtypeStruct(*one) for one in shapes),
        in_specs=[spec(pltpu.SMEM), vmem] + [hbm] * (len(mod) + len(weights)),
        out_specs=(vmem,) * (len(shapes) - 2) + (hbm,) * 2,
        scratch_shapes=[
            pltpu.VMEM((width, columns), bf16),
            pltpu.VMEM((tokens, width + EXTRA), bf16),
            pltpu.SemaphoreType.DMA((len(mod) + len(weights) + 2,)),
            pltpu.VMEM((count, rows // 2, EXTRA), f32),
        ],
        compiler_params=pltpu.CompilerParams(vmem_limit_bytes=GRANT),
        cost_estimate=pl.CostEstimate(
            flops=2 * tokens * width * 3 * slots * HD,
            bytes_accessed=2 * (tokens * width + columns * width) + 4 * tokens * columns,
            transcendentals=0,
        ),
    )(scalars, gain, *mod, *weights)


def attend_call(scalars, gain, operands, cot, weights, slots, rows, text_dev):
    count = operands[0].shape[0] // rows
    shard, columns = weights[0].shape
    width = cot[0].shape[1] - EXTRA
    tokens = rows * count
    inner = slots * HD
    stacked = whole_tiles(3 * inner)
    first = (columns - inner) // 128 * 128
    f32, bf16 = jnp.float32, jnp.bfloat16
    vmem, hbm = spec(pltpu.VMEM), spec(pl.ANY)
    shapes = [((rows, width // 2), f32), ((rows, width // 2), bf16), ((tokens - rows, stacked), bf16)]
    return pl.pallas_call(
        functools.partial(attend_kernel, slots, count, rows, shard, width, text_dev, first),
        out_shape=tuple(jax.ShapeDtypeStruct(*one) for one in shapes),
        in_specs=[spec(pltpu.SMEM), vmem] + [hbm] * (len(operands) + len(cot) + len(weights)),
        out_specs=(vmem,) * len(shapes),
        scratch_shapes=[
            pltpu.VMEM((width, columns - first), bf16),
            pltpu.VMEM((tokens, width + EXTRA), bf16),
            pltpu.SemaphoreType.DMA((len(operands) + len(cot) + len(weights),)),
            pltpu.VMEM((count, rows // 2, EXTRA), f32),
            pltpu.VMEM((slots, text_dev * count, HD), bf16),
            pltpu.VMEM((tokens, columns - first), bf16),
            pltpu.VMEM((tokens, 3 * inner), f32),
            pltpu.VMEM((tokens, stacked), bf16),
        ]
        + [pltpu.VMEM(one.shape, one.dtype) for one in operands],
        compiler_params=pltpu.CompilerParams(vmem_limit_bytes=GRANT),
        cost_estimate=pl.CostEstimate(
            flops=2 * tokens * width * inner + 10 * tokens * tokens * inner,
            bytes_accessed=2 * (tokens * width + columns * width),
            transcendentals=slots * tokens * tokens,
        ),
    )(scalars, gain, *operands, *cot, *weights)


def backward_kernel(own, other, w_own, w_other, *outs):
    total = dot(own[...], w_own[...], NT) + dot(other[...], w_other[...], NT)
    part = outs[0].shape[0]
    for n, out in enumerate(outs):
        out[...] = total[n * part : (n + 1) * part].astype(out.dtype)


def backward_call(own, other, w_own, w_other, part, dtype):
    rows, inner = own.shape
    half = w_own.shape[0]
    vmem = spec(pltpu.VMEM)
    return pl.pallas_call(
        backward_kernel,
        out_shape=(jax.ShapeDtypeStruct((part, half), dtype),) * (rows // part),
        in_specs=[vmem] * 4,
        out_specs=(vmem,) * (rows // part),
        compiler_params=pltpu.CompilerParams(vmem_limit_bytes=SMALL_GRANT),
        cost_estimate=pl.CostEstimate(
            flops=4 * rows * half * inner,
            bytes_accessed=4 * (rows + half) * inner + 4 * rows * half,
            transcendentals=0,
        ),
    )(own, other, w_own, w_other)


def sums_kernel(own_near, own_far, near, far, scale, normed, grad_out, sums_out):
    half = near.shape[0]
    for part, (own, moving) in enumerate(((own_near, near), (own_far, far))):
        here = slice(part * half, (part + 1) * half)
        grad = (own[...] + moving[...].astype(jnp.float32)) * scale[...]
        grad_out[here, :] = grad
        first = jnp.sum(grad, axis=-1, keepdims=True)
        second = jnp.sum(grad * normed[here, :], axis=-1, keepdims=True)
        lane = lax.broadcasted_iota(jnp.int32, (half, 128), 1)
        sums_out[here, :] = jnp.where(lane == 0, first, second)


def last_kernel(width, grad, sums, other, normed, base, inv_std, out):
    total = (sums[...] + other[...]) * (1.0 / width)
    rows = base[...] + inv_std[:, 0:1] * (
        grad[...] - total[:, 0:1] - normed[...] * total[:, 1:2]
    )
    out[...] = rows.T


def local_call(kernel, shapes, scalar_count, *operands, grant=SMALL_GRANT):
    vmem = spec(pltpu.VMEM)
    return pl.pallas_call(
        kernel,
        out_shape=tuple(jax.ShapeDtypeStruct(*one) for one in shapes),
        in_specs=[spec(pltpu.SMEM)] * scalar_count + [vmem] * (len(operands) - scalar_count),
        out_specs=(vmem,) * len(shapes),
        compiler_params=pltpu.CompilerParams(vmem_limit_bytes=grant),
        cost_estimate=pl.CostEstimate(
            flops=sum(one.size for one in operands),
            bytes_accessed=sum(one.size * one.dtype.itemsize for one in operands),
            transcendentals=0,
        ),
    )(*operands)


def shards_by_head(states, adjoint, text_kv, text_len, step_index, modulation, w_qkv, qk_gain, w_out):
    hidden_state = states[0]
    adjoint_rows = adjoint[0]
    tok_count, model_width = hidden_state.shape
    seq_count = lax.axis_size("seq")
    inner_dev = w_qkv.shape[2]
    heads_dev = inner_dev // HD
    shard = w_qkv.shape[0]
    slots = -(-heads_dev // seq_count)
    inner = slots * HD
    half_rows = tok_count // 2
    half_width = model_width // 2
    f32, bf16 = jnp.float32, jnp.bfloat16
    core = lax.axis_index("head").astype(jnp.int32)
    seq_index = lax.axis_index("seq")
    dp_index = lax.axis_index("dp")
    pin = lax.optimization_barrier

    seq_order = line_ring(seq_count)
    seq_place = ring_place(seq_order, seq_index)
    seq_next = ring_pairs(seq_order)
    swap = [(0, 1), (1, 0)]
    first_way = [(2 * p + c, 2 * (p ^ (1 + c)) + c) for p in range(4) for c in range(2)]
    second_way = [(2 * p + c, 2 * (p ^ (2 - c)) + c) for p in range(4) for c in range(2)]

    first = seq_index * heads_dev // seq_count
    stop = (seq_index + 1) * heads_dev // seq_count
    window = jnp.minimum(first, heads_dev - slots)
    valid = [(window + i >= first) & (window + i < stop) for i in range(slots)]
    owners = [ring_member(seq_order, (seq_place - k + seq_count) % seq_count) for k in range(seq_count)]
    w_index = [dp_index, dp_index ^ (1 + core), dp_index ^ (2 - core), dp_index ^ 3]
    scalars = [core] + w_index + [window, text_len[0]] + owners + valid
    scalars = jnp.stack([one.astype(jnp.int32) for one in scalars])

    def step(moving):
        return lax.ppermute(moving, "seq", seq_next)

    def other_core(moving):
        return lax.ppermute(moving, "head", swap)

    def step_back(moving):
        return lax.ppermute(moving, "seq", [(b, a) for a, b in seq_next])

    quarter = half_rows // 2

    def spread(moving):
        return [step(moving), step_back(moving)]

    def pass_on(received):
        return [step(received[0][:quarter]), step_back(received[1][quarter:])]

    mod_half, table_rows, extra = first_call(
        step_index, core[None], hidden_state, modulation.transpose(1, 0, 2), adjoint_rows, text_kv[0]
    )
    mod_near = spread(mod_half)

    w_qkv, w_out, mod_half = pin((w_qkv, w_out, mod_half))
    take = lambda c: lax.dynamic_slice(w_qkv, (0, c, window * HD), (shard, 1, inner))[:, 0]
    own_w = [
        jnp.concatenate([take(0), take(1)], axis=1),
        jnp.concatenate([take(2), lax.dynamic_slice_in_dim(w_out, window * HD, inner, 0).T], axis=1),
    ]
    w_first = [lax.ppermute(part, ("dp", "head"), first_way) for part in own_w]
    w_second = [lax.ppermute(part, ("dp", "head"), second_way) for part in own_w]

    text_dev = text_kv.shape[1]
    mod_far = pass_on(mod_near)
    clip_limit = 0.5 * (tok_count * seq_count * model_width) ** 0.5
    extra, *w_first = pin((extra, *w_first))
    cot_half, clip = cotangent_call(
        clip_limit, scalars, adjoint_rows, table_rows, text_kv[0], extra, *mod_near, mod_far[1]
    )
    cot_half, mod_far[0] = pin((cot_half, mod_far[0]))
    cot_near = spread(cot_half)
    modulated, cotangent, normed_share, scale_share, inv_std, base = local_call(
        own_kernel,
        [((tok_count, model_width + EXTRA), bf16)] * 2
        + [
            ((tok_count, half_width), f32),
            ((1, half_width), f32),
            ((tok_count, 128), f32),
            ((tok_count, half_width), f32),
        ],
        1,
        core[None],
        hidden_state,
        adjoint_rows,
        table_rows,
        text_kv[0],
        extra,
        clip,
        grant=GRANT,
    )
    def pieces(own, received):
        return [own] + [one for moved in received for one in (moved, other_core(moved))]

    mod_far = list(pin((*mod_far, modulated))[:2])
    mod_pieces = pieces(modulated, mod_near + mod_far)
    w_diagonal = [lax.ppermute(part, ("dp", "head"), second_way) for part in w_first]
    weights = [part[n] for n in range(2) for part in (own_w, w_first, w_second, w_diagonal)]
    cot_near[0] = pin((cot_near[0], w_second, w_diagonal))[0]
    cot_far = [step(cot_near[0])]

    cot_pieces = pieces(cotangent, cot_near)
    *cot_pieces, mod_pieces[-1] = pin((*cot_pieces, mod_pieces[-1]))
    *operands, w_keep, w_give = project_call(
        scalars, qk_gain, mod_pieces, weights, slots, tok_count, text_dev, seq_count
    )
    w_give, cot_far[0] = pin((w_give, *cot_far))
    cot_pieces += pieces(None, cot_far)[1:]
    given, *cot_pieces = pin((w_give, *cot_pieces))
    w_other = other_core(given)
    mine, theirs, rest = attend_call(
        scalars, qk_gain, operands + [w_keep, w_give], cot_pieces, weights[4:], slots, tok_count, text_dev
    )
    first = (mine + other_core(theirs).astype(f32)).astype(bf16)
    moving = [first[:half_rows], first[half_rows:]]
    other_rest = other_core(rest)
    rest, other_rest, *_ = pin((rest, other_rest, *moving))
    own = backward_call(rest, other_rest, w_keep, w_other, half_rows, f32)
    for j in range(2, seq_count):
        moving = [step(part) for part in moving]
        moving = [
            (a + b.astype(f32)).astype(bf16) for a, b in zip(own[2 * (j - 2) : 2 * (j - 1)], moving)
        ]
    moving = [step(part) for part in moving]

    grad_scaled, sums = local_call(
        sums_kernel,
        [((tok_count, half_width), f32), ((tok_count, 128), f32)],
        0,
        *own[-2:],
        *moving,
        scale_share,
        normed_share,
    )
    (pulled,) = local_call(
        functools.partial(last_kernel, model_width),
        [((half_width, tok_count), f32)],
        0,
        grad_scaled,
        sums,
        other_core(sums),
        normed_share,
        base,
        inv_std,
    )
    return pulled.T[None]


def qk_normalize(values, gains):
    inverse = lax.rsqrt(jnp.mean(values * values, axis=-1, keepdims=True) + 1e-06)
    return ((values * inverse * gains).astype(jnp.bfloat16), inverse)


def qk_backward(values, inverse, cotangent, gains):
    scaled = cotangent.astype(jnp.float32) * gains
    return (
        scaled * inverse - values * jnp.mean(scaled * values, axis=-1, keepdims=True) * inverse**3
    )


def shards_by_row(states, adjoint, text_kv, text_len, step_index, modulation, w_qkv, qk_gain, w_out):
    hidden_state = states[0]
    adjoint_rows = adjoint[0]
    tok_count, model_width = hidden_state.shape
    seq_count = lax.axis_size("seq")
    inner_dev = w_qkv.shape[2]
    heads_dev = inner_dev // HD
    score_scale = HD ** (-0.5)
    squares = lax.psum(jnp.sum(adjoint_rows * adjoint_rows), "seq")
    clip_limit = 0.5 * (tok_count * seq_count * model_width) ** 0.5
    clip_scale = jnp.minimum(1.0, clip_limit / jnp.sqrt(squares + 1e-06))
    table_row = lax.dynamic_index_in_dim(modulation, step_index[0], 0, keepdims=False)
    offset_row = table_row[0]
    stretch = table_row[1]
    gating = table_row[2]
    widened = hidden_state.astype(jnp.float32)
    centered = widened - jnp.mean(widened, axis=-1, keepdims=True)
    inv_std = lax.rsqrt(jnp.mean(centered * centered, axis=-1, keepdims=True) + 1e-06)
    normed = centered * inv_std
    modulated = (normed * (1.0 + stretch) + offset_row).astype(jnp.bfloat16)
    cotangent = (gating * (clip_scale * adjoint_rows)).astype(jnp.bfloat16)
    contract_last = (((1,), (1,)), ((), ()))
    full_weight = lax.all_gather(w_qkv, "dp", axis=0, tiled=True).reshape(
        model_width, 3 * inner_dev
    )
    projected = jnp.dot(modulated, full_weight, preferred_element_type=jnp.float32)
    out_raw = lax.dot_general(
        cotangent,
        lax.all_gather(w_out, "dp", axis=1, tiled=True),
        contract_last,
        preferred_element_type=jnp.float32,
    )
    projected = projected.reshape(tok_count, 3, heads_dev, HD)
    queries, query_inv = qk_normalize(projected[:, 0], qk_gain[0])
    own_keys, key_inv = qk_normalize(projected[:, 1], qk_gain[1])
    own_values = projected[:, 2].astype(jnp.bfloat16)
    out_grad = out_raw.astype(jnp.bfloat16).reshape(tok_count, heads_dev, HD)
    text_keys = text_kv[0, :, 0, :]
    text_values = text_kv[0, :, 1, :]
    text_dev = text_keys.shape[0]
    rows_dev = tok_count + text_dev
    key_local = jnp.concatenate([own_keys.reshape(tok_count, inner_dev), text_keys], axis=0)
    value_local = jnp.concatenate([own_values.reshape(tok_count, inner_dev), text_values], axis=0)
    key_all, value_all = (
        lax.all_gather(key_local, "seq", axis=0, tiled=True),
        lax.all_gather(value_local, "seq", axis=0, tiled=True),
    )
    all_rows = rows_dev * seq_count
    row_ids = jnp.arange(all_rows, dtype=jnp.int32)
    owner = row_ids // rows_dev
    within = row_ids % rows_dev
    allowed = (within < tok_count) | (owner * text_dev + within - tok_count < text_len[0])
    group = 1
    while group * 2 * rows_dev <= 512 and seq_count % (group * 2) == 0:
        group = group * 2
    block_rows = group * rows_dev
    block_count = all_rows // block_rows
    key_blocks = key_all.reshape(block_count, block_rows, heads_dev, HD)
    value_blocks = value_all.reshape(block_count, block_rows, heads_dev, HD)
    mask_blocks = allowed.reshape(block_count, block_rows)

    def block_scores(key_block, mask_block):
        scores = (
            jnp.einsum("qhd,khd->qhk", queries, key_block, preferred_element_type=jnp.float32)
            * score_scale
        )
        return jnp.where(mask_block[None, None, :], scores, -1e30)

    def first_pass(carry, block):
        row_max, row_sum, row_dot = carry
        key_block, value_block, mask_block = block
        scores = block_scores(key_block, mask_block)
        new_max = jnp.maximum(row_max, jnp.max(scores, axis=-1))
        rescale = jnp.exp(row_max - new_max)
        exps = jnp.exp(scores - new_max[:, :, None])
        grad_weights = jnp.einsum(
            "qhd,khd->qhk", out_grad, value_block, preferred_element_type=jnp.float32
        )
        return (
            (
                new_max,
                row_sum * rescale + jnp.sum(exps, axis=-1),
                row_dot * rescale + jnp.sum(exps * grad_weights, axis=-1),
            ),
            None,
        )

    start_state = (
        jnp.full((tok_count, heads_dev), -1e30, jnp.float32),
        jnp.zeros((tok_count, heads_dev), jnp.float32),
        jnp.zeros((tok_count, heads_dev), jnp.float32),
    )
    (row_max, row_sum, row_dot), unused = lax.scan(
        first_pass, start_state, (key_blocks, value_blocks, mask_blocks)
    )
    log_total = row_max + jnp.log(row_sum)
    delta_row = row_dot / row_sum

    def second_pass(running, block):
        key_block, value_block, mask_block = block
        weights = jnp.exp(block_scores(key_block, mask_block) - log_total[:, :, None])
        grad_weights = jnp.einsum(
            "qhd,khd->qhk", out_grad, value_block, preferred_element_type=jnp.float32
        )
        grad_scores = (weights * (grad_weights - delta_row[:, :, None])).astype(jnp.bfloat16)
        return (
            running
            + jnp.einsum(
                "qhk,khd->qhd", grad_scores, key_block, preferred_element_type=jnp.float32
            ),
            None,
        )

    query_sum, unused = lax.scan(
        second_pass,
        jnp.zeros((tok_count, heads_dev, HD), jnp.float32),
        (key_blocks, value_blocks, mask_blocks),
    )
    grad_query = (query_sum * score_scale).astype(jnp.bfloat16)
    log_all, delta_all = (
        lax.all_gather(log_total, "seq", axis=0, tiled=True),
        lax.all_gather(delta_row, "seq", axis=0, tiled=True),
    )
    local_ids = jnp.arange(rows_dev, dtype=jnp.int32)
    local_allowed = (local_ids < tok_count) | (
        lax.axis_index("seq") * text_dev + local_ids - tok_count < text_len[0]
    )
    key_three = key_local.reshape(rows_dev, heads_dev, HD)
    value_three = value_local.reshape(rows_dev, heads_dev, HD)
    query_piece = lax.all_gather(queries.reshape(tok_count, inner_dev), "seq", axis=0, tiled=True)
    grad_piece = lax.all_gather(out_grad.reshape(tok_count, inner_dev), "seq", axis=0, tiled=True)
    piece_rows = query_piece.shape[0]
    query_rows = query_piece.reshape(piece_rows, heads_dev, HD)
    grad_rows = grad_piece.reshape(piece_rows, heads_dev, HD)
    scores = (
        jnp.einsum("qhd,khd->qhk", query_rows, key_three, preferred_element_type=jnp.float32)
        * score_scale
    )
    scores = jnp.where(local_allowed[None, None, :], scores, -1e30)
    weights = jnp.exp(scores - log_all[:, :, None])
    grad_weights = jnp.einsum(
        "qhd,khd->qhk", grad_rows, value_three, preferred_element_type=jnp.float32
    )
    grad_scores = (weights * (grad_weights - delta_all[:, :, None])).astype(jnp.bfloat16)
    rounded = weights.astype(jnp.bfloat16)
    key_sum = jnp.einsum(
        "qhk,qhd->khd", grad_scores, query_rows, preferred_element_type=jnp.float32
    )
    value_sum = jnp.einsum("qhk,qhd->khd", rounded, grad_rows, preferred_element_type=jnp.float32)
    key_sum, value_sum = (key_sum, value_sum)
    grad_key = (key_sum[:tok_count] * score_scale).astype(jnp.bfloat16)
    grad_value = value_sum[:tok_count].astype(jnp.bfloat16)
    raw_query = qk_backward(projected[:, 0], query_inv, grad_query, qk_gain[0])
    raw_key = qk_backward(projected[:, 1], key_inv, grad_key, qk_gain[1])
    stacked = jnp.stack([raw_query, raw_key, grad_value.astype(jnp.float32)], axis=1).astype(
        jnp.bfloat16
    )
    stacked = stacked.reshape(tok_count, 3 * inner_dev)
    partial_grad = lax.dot_general(
        stacked, full_weight, contract_last, preferred_element_type=jnp.float32
    )
    half_width = model_width // lax.axis_size("head")
    first_col = lax.axis_index("head") * half_width
    grad_share = lax.psum_scatter(
        partial_grad.astype(jnp.bfloat16), "head", scatter_dimension=1, tiled=True
    ).astype(jnp.float32)
    normed_share = lax.dynamic_slice_in_dim(normed, first_col, half_width, 1)
    stretch_share = lax.dynamic_slice_in_dim(stretch, first_col, half_width, 0)
    adjoint_share = lax.dynamic_slice_in_dim(adjoint_rows, first_col, half_width, 1)
    grad_scaled = grad_share * (1.0 + stretch_share)
    row_sums = jnp.stack(
        [jnp.sum(grad_scaled, axis=-1), jnp.sum(grad_scaled * normed_share, axis=-1)], axis=-1
    )
    row_sums = lax.psum(row_sums, "head")
    grad_state = inv_std * (
        grad_scaled - row_sums[:, 0:1] / model_width - normed_share * row_sums[:, 1:2] / model_width
    )
    pulled = clip_scale * adjoint_share + grad_state
    return pulled[None]


def solution(mesh):
    in_specs = (
        P("dp", "seq", None),
        P("dp", "seq", None),
        P("dp", "seq", None, "head"),
        P("dp"),
        P("dp"),
        P(),
        P("dp", None, "head"),
        P(),
        P("head", "dp"),
    )
    out_specs = P("dp", "seq", "head")
    by_head = mesh.shape["seq"] == 4 and mesh.shape["dp"] == 4 and mesh.shape["head"] == 2
    shards = shards_by_head if by_head else shards_by_row
    return jax.shard_map(shards, mesh=mesh, in_specs=in_specs, out_specs=out_specs, check_vma=False)
```

```python
import functools

import jax
import jax.numpy as jnp
from jax import lax
from jax.experimental import pallas as pl
from jax.experimental.pallas import tpu as pltpu
from jax.sharding import PartitionSpec as P

HD = 64
GRANT = 60 * 1024 * 1024
SMALL_GRANT = 24 * 1024 * 1024
EXTRA = 128
NT = (((1,), (1,)), ((), ()))
NN = (((1,), (0,)), ((), ()))


def line_ring(count):
    return [0] + list(range(1, count, 2)) + [i for i in range(count - 1, 0, -1) if i % 2 == 0]


def ring_pairs(order):
    return [(order[i], order[(i + 1) % len(order)]) for i in range(len(order))]


def ring_place(order, index):
    place = jnp.int32(0)
    for position, member in enumerate(order):
        place = jnp.where(index == member, jnp.int32(position), place)
    return place


def ring_member(order, place):
    member = jnp.int32(order[0])
    for position, value in enumerate(order):
        member = jnp.where(place == position, jnp.int32(value), member)
    return member


def dot(a, b, dims):
    return lax.dot_general(a, b, dims, preferred_element_type=jnp.float32)


def equal_blocks(columns, block):
    row = lax.broadcasted_iota(jnp.int32, (columns, columns), 0)
    column = lax.broadcasted_iota(jnp.int32, (columns, columns), 1)
    return jnp.where(row // block == column // block, 1.0, 0.0).astype(jnp.bfloat16)


def head_means(values):
    ones = equal_blocks(values.shape[1], HD)
    total = 0.0
    for n in range(3):
        term = values.astype(jnp.bfloat16)
        total = total + dot(term, ones, NN)
        if n < 2:
            values = values - term.astype(jnp.float32)
    return total * (1.0 / HD)


def head_gains(gain, slots):
    return jnp.concatenate([gain[0:1, :]] * slots + [gain[1:2, :]] * slots, axis=1)


def whole_tiles(columns):
    return -(-columns // 128) * 128


def spec(space):
    return pl.BlockSpec(memory_space=space)


def text_columns(text, part):
    rows = text[...].astype(jnp.float32)[:, part, :]
    return [rows[:, c * EXTRA : (c + 1) * EXTRA] for c in range(rows.shape[1] // EXTRA)]


def extra_columns(blocks, rows):
    filled = sum(one.shape[0] for one in blocks)
    blocks = blocks + [jnp.zeros((rows - filled, EXTRA), jnp.float32)]
    return jnp.concatenate(blocks, axis=0).astype(jnp.bfloat16)


def first_kernel(step, core, states, table, adjoint, text, out, rows_out, extra_out):
    rows = [table[c, pl.ds(step[0], 1), :] for c in range(3)]
    widened = states[...].astype(jnp.float32)
    centered = widened - jnp.mean(widened, axis=-1, keepdims=True)
    inv_std = lax.rsqrt(jnp.mean(centered * centered, axis=-1, keepdims=True) + 1e-06)
    half, width = states.shape
    out[:, :width] = (centered * inv_std * (1.0 + rows[1]) + rows[0]).astype(jnp.bfloat16)
    for c in range(3):
        rows_out[c : c + 1, :] = rows[c]
    squares = jnp.sum(adjoint[...] * adjoint[...], axis=0, keepdims=True)
    squares = jnp.sum(squares, axis=1, keepdims=True)
    terms = []
    for n in range(3):
        terms.append(squares.astype(jnp.bfloat16).astype(jnp.float32))
        squares = squares - terms[-1]
    lane = lax.broadcasted_iota(jnp.int32, (8, EXTRA), 1)
    sums = jnp.where(lane == 0, terms[0], jnp.where(lane == 1, terms[1], jnp.where(lane == 2, terms[2], 0.0)))
    extra = extra_columns(text_columns(text, 0) + [sums], half)
    out[:, width:] = extra
    extra_out[...] = extra


def first_call(step, core, states, table, adjoint, text):
    rows, width = states.shape
    half = rows // 2
    whole = lambda *shape: pl.BlockSpec(shape, lambda i, step, core: (0,) * len(shape))
    return pl.pallas_call(
        first_kernel,
        out_shape=(
            jax.ShapeDtypeStruct((half, width + EXTRA), jnp.bfloat16),
            jax.ShapeDtypeStruct((8, width), jnp.float32),
            jax.ShapeDtypeStruct((half, EXTRA), jnp.bfloat16),
        ),
        grid_spec=pltpu.PrefetchScalarGridSpec(
            num_scalar_prefetch=2,
            grid=(1,),
            in_specs=[
                pl.BlockSpec((half, width), lambda i, step, core: (core[0], 0)),
                whole(*table.shape),
                whole(*adjoint.shape),
                whole(*text.shape),
            ],
            out_specs=(whole(half, width + EXTRA), whole(8, width), whole(half, EXTRA)),
        ),
        compiler_params=pltpu.CompilerParams(vmem_limit_bytes=GRANT),
        cost_estimate=pl.CostEstimate(flops=8 * half * width, bytes_accessed=16 * half * width, transcendentals=0),
    )(step, core, states, table, adjoint, text)


def pick_half(core, rows):
    half = rows.shape[1] // 2
    return jnp.where(core == 0, rows[:, :half], rows[:, half:])


def cotangent_kernel(limit, core, adjoint, table_rows, text, extra, previous, following, opposite, out, clip_out):
    first = previous.shape[0] - opposite.shape[0]
    row = 8 * (text.shape[2] // EXTRA)
    squares = opposite[...].astype(jnp.float32)[row - first : row - first + 1, :]
    for terms in (extra, previous, following):
        squares = squares + terms[...].astype(jnp.float32)[row : row + 1, :]
    squares = jnp.sum(squares, axis=1, keepdims=True)
    clip_scale = jnp.minimum(1.0, limit / jnp.sqrt(squares + 1e-06))
    half, width = adjoint.shape
    out[:, :width] = (table_rows[2:3, :] * (clip_scale * adjoint[...])).astype(jnp.bfloat16)
    out[:, width:] = extra_columns(text_columns(text, 1), half)
    clip_out[...] = jnp.broadcast_to(clip_scale, clip_out.shape)


def cotangent_call(limit, core, adjoint, table_rows, text, extra, previous, following, opposite):
    rows, width = adjoint.shape
    half = rows // 2
    block = width // EXTRA
    whole = lambda one: pl.BlockSpec(one.shape, lambda i, core: (0,) * one.ndim)
    tail = lambda one: pl.BlockSpec((one.shape[0], EXTRA), lambda i, core: (0, block))
    outs = (
        jax.ShapeDtypeStruct((half, width + EXTRA), jnp.bfloat16),
        jax.ShapeDtypeStruct((8, EXTRA), jnp.float32),
    )
    return pl.pallas_call(
        functools.partial(cotangent_kernel, limit),
        out_shape=outs,
        grid_spec=pltpu.PrefetchScalarGridSpec(
            num_scalar_prefetch=1,
            grid=(1,),
            in_specs=[pl.BlockSpec((half, width), lambda i, core: (core[0], 0))]
            + [whole(table_rows), whole(text), whole(extra)]
            + [tail(one) for one in (previous, following, opposite)],
            out_specs=tuple(whole(one) for one in outs),
        ),
        compiler_params=pltpu.CompilerParams(vmem_limit_bytes=GRANT),
        cost_estimate=pl.CostEstimate(flops=4 * half * width, bytes_accessed=6 * half * width, transcendentals=0),
    )(core, adjoint, table_rows, text, extra, previous, following, opposite)


def own_kernel(
    core, states, adjoint, table_rows, text, extra, clip, out, cot_out, normed_out, stretch_out, inv_out, base_out
):
    rows, width = states.shape
    half = rows // 2
    widened = states[...].astype(jnp.float32)
    centered = widened - jnp.mean(widened, axis=-1, keepdims=True)
    inv_std = lax.rsqrt(jnp.mean(centered * centered, axis=-1, keepdims=True) + 1e-06)
    normed = centered * inv_std
    scale = 1.0 + table_rows[1:2, :]
    out[:, :width] = (normed * scale + table_rows[0:1, :]).astype(jnp.bfloat16)
    normed_out[...] = pick_half(core[0], normed)
    stretch_out[...] = pick_half(core[0], scale)
    inv_out[...] = jnp.broadcast_to(inv_std, inv_out.shape)
    clipped = clip[0:1, 0:1] * adjoint[...]
    cot_out[:, :width] = (table_rows[2:3, :] * clipped).astype(jnp.bfloat16)
    base_out[...] = pick_half(core[0], clipped)
    columns = extra_columns(text_columns(text, 1), half)
    for n in range(2):
        out[n * half : (n + 1) * half, width:] = extra[...]
        cot_out[n * half : (n + 1) * half, width:] = columns


class Copies:
    def __init__(self, sems):
        self.sems = sems
        self.count = 0

    def start(self, source, target):
        copy = pltpu.make_async_copy(source, target, self.sems.at[self.count])
        copy.start()
        self.count += 1
        return copy

    def weights(self, scalars, w_in, w_all, shard, first=0):
        columns = w_in[0].shape[1] - first
        return [
            self.start(
                piece.at[:, pl.ds(first, columns)],
                w_all.at[
                    pl.ds(pl.multiple_of(scalars[1 + n % 4] * shard, 16), shard),
                    pl.ds(n // 4 * columns, columns),
                ],
            )
            for n, piece in enumerate(w_in)
        ]

    def rows(self, core, pieces, target, rows):
        half = rows // 2
        copies = [self.start(pieces[0], target.at[pl.ds(0, rows)])]
        places = [(rows, half), (3 * rows, half)]
        parts = (len(pieces) - 5) // 2
        places += [(2 * rows + n * half // parts, half // parts) for n in range(parts)]
        for n, (first, size) in enumerate(places):
            for m, holder in enumerate((core, 1 - core)):
                there = pl.ds(pl.multiple_of(first + holder * half, 16), size)
                copies.append(self.start(pieces[1 + 2 * n + m], target.at[there]))
        return copies


def window_heads(scalars, count, rows, text_dev, gathered, width, extra, text, text_t=None):
    half = rows // 2
    for k in range(count):
        there = pl.ds(pl.multiple_of(k * rows + scalars[0] * half, 16), half)
        extra[k] = gathered[there, width:].astype(jnp.float32)
    for i in range(text.shape[0]):
        head = scalars[5] + i
        first = pl.ds(pl.multiple_of(head // 2 * text_dev, 8), text_dev)
        found = jnp.concatenate([extra[k, first, :] for k in range(count)], axis=0)
        found = jnp.where(head % 2 == 0, found[:, :HD], found[:, HD:])
        text[i] = found.astype(jnp.bfloat16)
        if text_t is not None:
            text_t[i] = found.T.astype(jnp.bfloat16)


def project_kernel(slots, count, rows, shard, width, text_dev, scalars, gain, *refs):
    refs = list(refs)
    take = lambda n: [refs.pop(0) for _ in range(n)]
    mod_in = take(9)
    w_in = take(8)
    qkv, k_t, raw_all, inv_all, text, text_t, w_keep, w_give = take(8)
    w_all, mod_all, sems, extra, qkv_s, k_t_s, raw_s, inv_s = take(8)
    inner = slots * HD
    core = scalars[0]
    copies = Copies(sems)
    w_copies = copies.weights(scalars, w_in, w_all, shard)
    row_copies = copies.rows(core, mod_in, mod_all, rows)

    lane = lax.broadcasted_iota(jnp.int32, (1, 2 * inner), 1)
    gains = head_gains(gain, slots) * jnp.where(lane < inner, HD ** (-0.5), 1.0)
    identity = equal_blocks(inner, 1)
    for copy in w_copies + row_copies[:3]:
        copy.wait()
    span = 2 * rows
    out_copies = []
    for b in range(count // 2):
        here = slice(b * span, (b + 1) * span)
        there = pl.ds(b * span, span)
        projected = jnp.dot(
            mod_all[here, :width], w_all[:, : 3 * inner], preferred_element_type=jnp.float32
        )
        raw = projected[:, : 2 * inner]
        inverse = lax.rsqrt(head_means(raw * raw) + 1e-06)
        raw_s[here, :] = raw
        inv_s[here, :] = inverse
        qkv_s[here, : 2 * inner] = (raw * inverse * gains).astype(jnp.bfloat16)
        qkv_s[here, 2 * inner :] = projected[:, 2 * inner :].astype(jnp.bfloat16)
        k_t_s[:, here] = dot(identity, qkv_s[here, inner : 2 * inner], NT).astype(jnp.bfloat16)
        for source, target in ((qkv_s, qkv), (raw_s, raw_all), (inv_s, inv_all)):
            out_copies.append(copies.start(source.at[there], target.at[there]))
        out_copies.append(copies.start(k_t_s.at[:, there], k_t.at[:, there]))
        if b == 0:
            half = width // 2
            columns = pl.ds(0, w_keep.shape[1])
            for holder, target in ((core, w_keep), (1 - core, w_give)):
                source = w_all.at[pl.ds(pl.multiple_of(holder * half, 16), half), columns]
                out_copies.append(copies.start(source, target))
            for copy in row_copies[3:]:
                copy.wait()
            window_heads(scalars, count, rows, text_dev, mod_all, width, extra, text, text_t)
    for copy in out_copies:
        copy.wait()


def attend_kernel(slots, count, rows, shard, width, text_dev, first_column, scalars, gain, *refs):
    refs = list(refs)
    take = lambda n: [refs.pop(0) for _ in range(n)]
    projected = take(8)
    cot_in = take(7)
    w_in = take(4)
    mine_out, theirs_out, rest_out = take(3)
    w_out, cot_all, sems, extra, values_text = take(5)
    d_all, grads, stacked = take(3)
    qkv, k_t, raw_all, inv_all, text, text_t, w_keep, w_give = refs
    inner = slots * HD
    tokens = rows * count
    core = scalars[0]
    copies = Copies(sems)
    w_copies = copies.weights(scalars, w_in, w_out, shard, first_column)
    row_copies = copies.rows(core, cot_in, cot_all, rows)
    pairs = list(zip(projected, refs))
    local_copies = [copies.start(*pairs[n]) for n in (0, 1, 4, 5)]
    score_scale = HD ** (-0.5)
    span = 2 * rows

    text_rows = count * text_dev
    row = lax.broadcasted_iota(jnp.int32, (text_rows, span), 0)
    text_id = row
    for k in range(count):
        inside = (row >= k * text_dev) & (row < (k + 1) * text_dev)
        text_id = jnp.where(inside, row + (scalars[7 + k] - k) * text_dev, text_id)
    bias = jnp.where(text_id < scalars[6], 0.0, -1e30)

    for copy in w_copies:
        copy.wait()
    arrivals = [row_copies[:3], row_copies[3:]]
    for b in range(count // 2):
        for copy in arrivals[b]:
            copy.wait()
        here = slice(b * span, (b + 1) * span)
        out_grad = jnp.dot(cot_all[here, :width], w_out[...], preferred_element_type=jnp.float32)
        d_all[here, :] = out_grad.astype(jnp.bfloat16)
    window_heads(scalars, count, rows, text_dev, cot_all, width, extra, values_text)
    late_copies = [copies.start(*pairs[n]) for n in (2, 3, 6, 7)]
    for copy in local_copies:
        copy.wait()

    d_first = d_all.shape[1] - inner
    for i in range(slots):
        columns = [slice(n * inner + i * HD, n * inner + (i + 1) * HD) for n in range(3)]
        keys, values = qkv[:, columns[1]], qkv[:, columns[2]]
        keys_t = k_t[i * HD : (i + 1) * HD, :]
        grad_k, grad_v = 0.0, 0.0
        for b in range(count // 2):
            here = slice(b * span, (b + 1) * span)
            query = qkv[here, columns[0]]
            grad = d_all[here, d_first + i * HD : d_first + (i + 1) * HD]
            scores = dot(keys, query, NT)
            text_scores = dot(text[i], query, NT) + bias
            col_max = jnp.maximum(
                jnp.max(scores, axis=0, keepdims=True), jnp.max(text_scores, axis=0, keepdims=True)
            )
            exps = jnp.exp(scores - col_max)
            text_exps = jnp.exp(text_scores - col_max)
            total = jnp.sum(exps, axis=0, keepdims=True) + jnp.sum(text_exps, axis=0, keepdims=True)
            inverse = 1.0 / total
            grad_w = dot(values, grad, NT)
            text_grad_w = dot(values_text[i], grad, NT)
            delta = inverse * (
                jnp.sum(exps * grad_w, axis=0, keepdims=True)
                + jnp.sum(text_exps * text_grad_w, axis=0, keepdims=True)
            )
            weights = exps * inverse
            grad_s = (weights * (grad_w - delta)).astype(jnp.bfloat16)
            text_grad_s = (text_exps * inverse * (text_grad_w - delta)).astype(jnp.bfloat16)
            grad_k += dot(grad_s, query, NN)
            grad_v += dot(weights.astype(jnp.bfloat16), grad, NN)
            grad_q = dot(keys_t, grad_s, NN) + dot(text_t[i], text_grad_s, NN)
            grads[here, columns[0]] = grad_q.T * score_scale
        grads[:, columns[1]] = grad_k
        grads[:, columns[2]] = grad_v

    lane = lax.broadcasted_iota(jnp.int32, (1, inner), 1)
    mine = jnp.zeros((1, inner), jnp.float32)
    for i in range(slots):
        inside = (lane >= i * HD) & (lane < (i + 1) * HD) & (scalars[7 + count + i] > 0)
        mine = jnp.where(inside, 1.0, mine)
    gains = head_gains(gain, slots)
    for copy in late_copies[:2]:
        copy.wait()
    for b in range(count // 2):
        here = slice(b * span, (b + 1) * span)
        scaled = grads[here, : 2 * inner].astype(jnp.bfloat16).astype(jnp.float32) * gains
        raw, inverse = raw_all[here, :], inv_all[here, :]
        back = scaled * inverse - raw * head_means(scaled * raw) * (inverse * inverse * inverse)
        valid = jnp.concatenate([mine, mine], axis=1) > 0.0
        stacked[here, : 2 * inner] = jnp.where(valid, back, 0.0).astype(jnp.bfloat16)
        back = jnp.where(mine > 0.0, grads[here, 2 * inner :], 0.0).astype(jnp.bfloat16)
        stacked[here, 2 * inner : 3 * inner] = back
    stacked[:, 3 * inner :] = jnp.zeros((tokens, stacked.shape[1] - 3 * inner), jnp.bfloat16)
    first = stacked[rows : 2 * rows, :]
    rest_out[: (count - 2) * rows, :] = stacked[2 * rows :, :]
    rest_out[(count - 2) * rows :, :] = stacked[:rows, :]
    for copy in late_copies[2:]:
        copy.wait()
    theirs_out[...] = dot(first, w_give[...], NT).astype(jnp.bfloat16)
    mine_out[...] = dot(first, w_keep[...], NT)


def project_call(scalars, gain, mod, weights, slots, rows, text_dev, count):
    shard = weights[0].shape[0]
    columns = 4 * slots * HD
    width = mod[0].shape[1] - EXTRA
    tokens = rows * count
    text_rows = text_dev * count
    f32, bf16 = jnp.float32, jnp.bfloat16
    vmem, hbm = spec(pltpu.VMEM), spec(pl.ANY)
    inner = slots * HD
    shapes = [((tokens, 3 * inner), bf16), ((inner, tokens), bf16)] + [((tokens, 2 * inner), f32)] * 2
    shapes += [((slots, text_rows, HD), bf16), ((slots, HD, text_rows), bf16)]
    shapes += [((width // 2, whole_tiles(3 * slots * HD)), bf16)] * 2
    return pl.pallas_call(
        functools.partial(project_kernel, slots, count, rows, shard, width, text_dev),
        out_shape=tuple(jax.ShapeDtypeStruct(*one) for one in shapes),
        in_specs=[spec(pltpu.SMEM), vmem] + [hbm] * (len(mod) + len(weights)),
        out_specs=(hbm,) * 4 + (vmem,) * 2 + (hbm,) * 2,
        scratch_shapes=[
            pltpu.VMEM((width, columns), bf16),
            pltpu.VMEM((tokens, width + EXTRA), bf16),
            pltpu.SemaphoreType.DMA((len(mod) + len(weights) + 10,)),
            pltpu.VMEM((count, rows // 2, EXTRA), f32),
        ]
        + [pltpu.VMEM(*one) for one in shapes[:4]],
        compiler_params=pltpu.CompilerParams(vmem_limit_bytes=GRANT),
        cost_estimate=pl.CostEstimate(
            flops=2 * tokens * width * 3 * slots * HD,
            bytes_accessed=2 * (tokens * width + columns * width) + 4 * tokens * columns,
            transcendentals=0,
        ),
    )(scalars, gain, *mod, *weights)


def attend_call(scalars, gain, operands, cot, weights, slots, rows, text_dev):
    count = operands[0].shape[0] // rows
    shard, columns = weights[0].shape
    width = cot[0].shape[1] - EXTRA
    tokens = rows * count
    inner = slots * HD
    stacked = whole_tiles(3 * inner)
    first = (columns - inner) // 128 * 128
    f32, bf16 = jnp.float32, jnp.bfloat16
    vmem, hbm = spec(pltpu.VMEM), spec(pl.ANY)
    shapes = [((rows, width // 2), f32), ((rows, width // 2), bf16), ((tokens - rows, stacked), bf16)]
    return pl.pallas_call(
        functools.partial(attend_kernel, slots, count, rows, shard, width, text_dev, first),
        out_shape=tuple(jax.ShapeDtypeStruct(*one) for one in shapes),
        in_specs=[spec(pltpu.SMEM), vmem] + [hbm] * (len(operands) + len(cot) + len(weights)),
        out_specs=(vmem,) * len(shapes),
        scratch_shapes=[
            pltpu.VMEM((width, columns - first), bf16),
            pltpu.VMEM((tokens, width + EXTRA), bf16),
            pltpu.SemaphoreType.DMA((len(operands) + len(cot) + len(weights),)),
            pltpu.VMEM((count, rows // 2, EXTRA), f32),
            pltpu.VMEM((slots, text_dev * count, HD), bf16),
            pltpu.VMEM((tokens, columns - first), bf16),
            pltpu.VMEM((tokens, 3 * inner), f32),
            pltpu.VMEM((tokens, stacked), bf16),
        ]
        + [pltpu.VMEM(one.shape, one.dtype) for one in operands],
        compiler_params=pltpu.CompilerParams(vmem_limit_bytes=GRANT),
        cost_estimate=pl.CostEstimate(
            flops=2 * tokens * width * inner + 10 * tokens * tokens * inner,
            bytes_accessed=2 * (tokens * width + columns * width),
            transcendentals=slots * tokens * tokens,
        ),
    )(scalars, gain, *operands, *cot, *weights)


def backward_kernel(own, other, w_own, w_other, *outs):
    total = dot(own[...], w_own[...], NT) + dot(other[...], w_other[...], NT)
    part = outs[0].shape[0]
    for n, out in enumerate(outs):
        out[...] = total[n * part : (n + 1) * part].astype(out.dtype)


def backward_call(own, other, w_own, w_other, part, dtype):
    rows, inner = own.shape
    half = w_own.shape[0]
    vmem = spec(pltpu.VMEM)
    return pl.pallas_call(
        backward_kernel,
        out_shape=(jax.ShapeDtypeStruct((part, half), dtype),) * (rows // part),
        in_specs=[vmem] * 4,
        out_specs=(vmem,) * (rows // part),
        compiler_params=pltpu.CompilerParams(vmem_limit_bytes=SMALL_GRANT),
        cost_estimate=pl.CostEstimate(
            flops=4 * rows * half * inner,
            bytes_accessed=4 * (rows + half) * inner + 4 * rows * half,
            transcendentals=0,
        ),
    )(own, other, w_own, w_other)


def sums_kernel(own_near, own_far, near, far, scale, normed, grad_out, sums_out):
    half = near.shape[0]
    for part, (own, moving) in enumerate(((own_near, near), (own_far, far))):
        here = slice(part * half, (part + 1) * half)
        grad = (own[...] + moving[...].astype(jnp.float32)) * scale[...]
        grad_out[here, :] = grad
        first = jnp.sum(grad, axis=-1, keepdims=True)
        second = jnp.sum(grad * normed[here, :], axis=-1, keepdims=True)
        lane = lax.broadcasted_iota(jnp.int32, (half, 128), 1)
        sums_out[here, :] = jnp.where(lane == 0, first, second)


def last_kernel(width, grad, sums, other, normed, base, inv_std, out):
    total = (sums[...] + other[...]) * (1.0 / width)
    rows = base[...] + inv_std[:, 0:1] * (
        grad[...] - total[:, 0:1] - normed[...] * total[:, 1:2]
    )
    out[...] = rows.T


def local_call(kernel, shapes, scalar_count, *operands, grant=SMALL_GRANT):
    vmem = spec(pltpu.VMEM)
    return pl.pallas_call(
        kernel,
        out_shape=tuple(jax.ShapeDtypeStruct(*one) for one in shapes),
        in_specs=[spec(pltpu.SMEM)] * scalar_count + [vmem] * (len(operands) - scalar_count),
        out_specs=(vmem,) * len(shapes),
        compiler_params=pltpu.CompilerParams(vmem_limit_bytes=grant),
        cost_estimate=pl.CostEstimate(
            flops=sum(one.size for one in operands),
            bytes_accessed=sum(one.size * one.dtype.itemsize for one in operands),
            transcendentals=0,
        ),
    )(*operands)


def shards_by_head(states, adjoint, text_kv, text_len, step_index, modulation, w_qkv, qk_gain, w_out):
    hidden_state = states[0]
    adjoint_rows = adjoint[0]
    tok_count, model_width = hidden_state.shape
    seq_count = lax.axis_size("seq")
    inner_dev = w_qkv.shape[2]
    heads_dev = inner_dev // HD
    shard = w_qkv.shape[0]
    slots = -(-heads_dev // seq_count)
    inner = slots * HD
    half_rows = tok_count // 2
    half_width = model_width // 2
    f32, bf16 = jnp.float32, jnp.bfloat16
    core = lax.axis_index("head").astype(jnp.int32)
    seq_index = lax.axis_index("seq")
    dp_index = lax.axis_index("dp")
    pin = lax.optimization_barrier

    seq_order = line_ring(seq_count)
    seq_place = ring_place(seq_order, seq_index)
    seq_next = ring_pairs(seq_order)
    swap = [(0, 1), (1, 0)]
    first_way = [(2 * p + c, 2 * (p ^ (1 + c)) + c) for p in range(4) for c in range(2)]
    second_way = [(2 * p + c, 2 * (p ^ (2 - c)) + c) for p in range(4) for c in range(2)]

    first = seq_index * heads_dev // seq_count
    stop = (seq_index + 1) * heads_dev // seq_count
    window = jnp.minimum(first, heads_dev - slots)
    valid = [(window + i >= first) & (window + i < stop) for i in range(slots)]
    owners = [ring_member(seq_order, (seq_place - k + seq_count) % seq_count) for k in range(seq_count)]
    w_index = [dp_index, dp_index ^ (1 + core), dp_index ^ (2 - core), dp_index ^ 3]
    scalars = [core] + w_index + [window, text_len[0]] + owners + valid
    scalars = jnp.stack([one.astype(jnp.int32) for one in scalars])

    def step(moving):
        return lax.ppermute(moving, "seq", seq_next)

    def other_core(moving):
        return lax.ppermute(moving, "head", swap)

    def step_back(moving):
        return lax.ppermute(moving, "seq", [(b, a) for a, b in seq_next])

    quarter = half_rows // 2

    def spread(moving):
        return [step(moving), step_back(moving)]

    def pass_on(received):
        return [step(received[0][:quarter]), step_back(received[1][quarter:])]

    mod_half, table_rows, extra = first_call(
        step_index, core[None], hidden_state, modulation.transpose(1, 0, 2), adjoint_rows, text_kv[0]
    )
    mod_near = spread(mod_half)

    w_qkv, w_out, mod_half = pin((w_qkv, w_out, mod_half))
    take = lambda c: lax.dynamic_slice(w_qkv, (0, c, window * HD), (shard, 1, inner))[:, 0]
    own_w = [
        jnp.concatenate([take(0), take(1)], axis=1),
        jnp.concatenate([take(2), lax.dynamic_slice_in_dim(w_out, window * HD, inner, 0).T], axis=1),
    ]
    w_first = [lax.ppermute(part, ("dp", "head"), first_way) for part in own_w]
    w_second = [lax.ppermute(part, ("dp", "head"), second_way) for part in own_w]

    text_dev = text_kv.shape[1]
    mod_far = pass_on(mod_near)
    clip_limit = 0.5 * (tok_count * seq_count * model_width) ** 0.5
    extra, *w_first = pin((extra, *w_first))
    cot_half, clip = cotangent_call(
        clip_limit, scalars, adjoint_rows, table_rows, text_kv[0], extra, *mod_near, mod_far[1]
    )
    cot_half, mod_far[0] = pin((cot_half, mod_far[0]))
    cot_near = spread(cot_half)
    modulated, cotangent, normed_share, scale_share, inv_std, base = local_call(
        own_kernel,
        [((tok_count, model_width + EXTRA), bf16)] * 2
        + [
            ((tok_count, half_width), f32),
            ((1, half_width), f32),
            ((tok_count, 128), f32),
            ((tok_count, half_width), f32),
        ],
        1,
        core[None],
        hidden_state,
        adjoint_rows,
        table_rows,
        text_kv[0],
        extra,
        clip,
        grant=GRANT,
    )
    def pieces(own, received):
        return [own] + [one for moved in received for one in (moved, other_core(moved))]

    mod_far = list(pin((*mod_far, modulated))[:2])
    mod_pieces = pieces(modulated, mod_near + mod_far)
    w_diagonal = [lax.ppermute(part, ("dp", "head"), second_way) for part in w_first]
    weights = [part[n] for n in range(2) for part in (own_w, w_first, w_second, w_diagonal)]
    cot_near[0] = pin((cot_near[0], w_second, w_diagonal))[0]
    cot_far = [step(cot_near[0])]

    cot_pieces = pieces(cotangent, cot_near)
    *cot_pieces, mod_pieces[-1] = pin((*cot_pieces, mod_pieces[-1]))
    *operands, w_keep, w_give = project_call(
        scalars, qk_gain, mod_pieces, weights, slots, tok_count, text_dev, seq_count
    )
    w_give, cot_far[0] = pin((w_give, *cot_far))
    cot_pieces += pieces(None, cot_far)[1:]
    given, *cot_pieces = pin((w_give, *cot_pieces))
    w_other = other_core(given)
    mine, theirs, rest = attend_call(
        scalars, qk_gain, operands + [w_keep, w_give], cot_pieces, weights[4:], slots, tok_count, text_dev
    )
    first = (mine + other_core(theirs).astype(f32)).astype(bf16)
    moving = [first[:half_rows], first[half_rows:]]
    other_rest = other_core(rest)
    rest, other_rest, *_ = pin((rest, other_rest, *moving))
    own = backward_call(rest, other_rest, w_keep, w_other, half_rows, f32)
    for j in range(2, seq_count):
        moving = [step(part) for part in moving]
        moving = [
            (a + b.astype(f32)).astype(bf16) for a, b in zip(own[2 * (j - 2) : 2 * (j - 1)], moving)
        ]
    moving = [step(part) for part in moving]

    grad_scaled, sums = local_call(
        sums_kernel,
        [((tok_count, half_width), f32), ((tok_count, 128), f32)],
        0,
        *own[-2:],
        *moving,
        scale_share,
        normed_share,
    )
    (pulled,) = local_call(
        functools.partial(last_kernel, model_width),
        [((half_width, tok_count), f32)],
        0,
        grad_scaled,
        sums,
        other_core(sums),
        normed_share,
        base,
        inv_std,
    )
    return pulled.T[None]


def qk_normalize(values, gains):
    inverse = lax.rsqrt(jnp.mean(values * values, axis=-1, keepdims=True) + 1e-06)
    return ((values * inverse * gains).astype(jnp.bfloat16), inverse)


def qk_backward(values, inverse, cotangent, gains):
    scaled = cotangent.astype(jnp.float32) * gains
    return (
        scaled * inverse - values * jnp.mean(scaled * values, axis=-1, keepdims=True) * inverse**3
    )


def shards_by_row(states, adjoint, text_kv, text_len, step_index, modulation, w_qkv, qk_gain, w_out):
    hidden_state = states[0]
    adjoint_rows = adjoint[0]
    tok_count, model_width = hidden_state.shape
    seq_count = lax.axis_size("seq")
    inner_dev = w_qkv.shape[2]
    heads_dev = inner_dev // HD
    score_scale = HD ** (-0.5)
    squares = lax.psum(jnp.sum(adjoint_rows * adjoint_rows), "seq")
    clip_limit = 0.5 * (tok_count * seq_count * model_width) ** 0.5
    clip_scale = jnp.minimum(1.0, clip_limit / jnp.sqrt(squares + 1e-06))
    table_row = lax.dynamic_index_in_dim(modulation, step_index[0], 0, keepdims=False)
    offset_row = table_row[0]
    stretch = table_row[1]
    gating = table_row[2]
    widened = hidden_state.astype(jnp.float32)
    centered = widened - jnp.mean(widened, axis=-1, keepdims=True)
    inv_std = lax.rsqrt(jnp.mean(centered * centered, axis=-1, keepdims=True) + 1e-06)
    normed = centered * inv_std
    modulated = (normed * (1.0 + stretch) + offset_row).astype(jnp.bfloat16)
    cotangent = (gating * (clip_scale * adjoint_rows)).astype(jnp.bfloat16)
    contract_last = (((1,), (1,)), ((), ()))
    full_weight = lax.all_gather(w_qkv, "dp", axis=0, tiled=True).reshape(
        model_width, 3 * inner_dev
    )
    projected = jnp.dot(modulated, full_weight, preferred_element_type=jnp.float32)
    out_raw = lax.dot_general(
        cotangent,
        lax.all_gather(w_out, "dp", axis=1, tiled=True),
        contract_last,
        preferred_element_type=jnp.float32,
    )
    projected = projected.reshape(tok_count, 3, heads_dev, HD)
    queries, query_inv = qk_normalize(projected[:, 0], qk_gain[0])
    own_keys, key_inv = qk_normalize(projected[:, 1], qk_gain[1])
    own_values = projected[:, 2].astype(jnp.bfloat16)
    out_grad = out_raw.astype(jnp.bfloat16).reshape(tok_count, heads_dev, HD)
    text_keys = text_kv[0, :, 0, :]
    text_values = text_kv[0, :, 1, :]
    text_dev = text_keys.shape[0]
    rows_dev = tok_count + text_dev
    key_local = jnp.concatenate([own_keys.reshape(tok_count, inner_dev), text_keys], axis=0)
    value_local = jnp.concatenate([own_values.reshape(tok_count, inner_dev), text_values], axis=0)
    key_all, value_all = (
        lax.all_gather(key_local, "seq", axis=0, tiled=True),
        lax.all_gather(value_local, "seq", axis=0, tiled=True),
    )
    all_rows = rows_dev * seq_count
    row_ids = jnp.arange(all_rows, dtype=jnp.int32)
    owner = row_ids // rows_dev
    within = row_ids % rows_dev
    allowed = (within < tok_count) | (owner * text_dev + within - tok_count < text_len[0])
    group = 1
    while group * 2 * rows_dev <= 512 and seq_count % (group * 2) == 0:
        group = group * 2
    block_rows = group * rows_dev
    block_count = all_rows // block_rows
    key_blocks = key_all.reshape(block_count, block_rows, heads_dev, HD)
    value_blocks = value_all.reshape(block_count, block_rows, heads_dev, HD)
    mask_blocks = allowed.reshape(block_count, block_rows)

    def block_scores(key_block, mask_block):
        scores = (
            jnp.einsum("qhd,khd->qhk", queries, key_block, preferred_element_type=jnp.float32)
            * score_scale
        )
        return jnp.where(mask_block[None, None, :], scores, -1e30)

    def first_pass(carry, block):
        row_max, row_sum, row_dot = carry
        key_block, value_block, mask_block = block
        scores = block_scores(key_block, mask_block)
        new_max = jnp.maximum(row_max, jnp.max(scores, axis=-1))
        rescale = jnp.exp(row_max - new_max)
        exps = jnp.exp(scores - new_max[:, :, None])
        grad_weights = jnp.einsum(
            "qhd,khd->qhk", out_grad, value_block, preferred_element_type=jnp.float32
        )
        return (
            (
                new_max,
                row_sum * rescale + jnp.sum(exps, axis=-1),
                row_dot * rescale + jnp.sum(exps * grad_weights, axis=-1),
            ),
            None,
        )

    start_state = (
        jnp.full((tok_count, heads_dev), -1e30, jnp.float32),
        jnp.zeros((tok_count, heads_dev), jnp.float32),
        jnp.zeros((tok_count, heads_dev), jnp.float32),
    )
    (row_max, row_sum, row_dot), unused = lax.scan(
        first_pass, start_state, (key_blocks, value_blocks, mask_blocks)
    )
    log_total = row_max + jnp.log(row_sum)
    delta_row = row_dot / row_sum

    def second_pass(running, block):
        key_block, value_block, mask_block = block
        weights = jnp.exp(block_scores(key_block, mask_block) - log_total[:, :, None])
        grad_weights = jnp.einsum(
            "qhd,khd->qhk", out_grad, value_block, preferred_element_type=jnp.float32
        )
        grad_scores = (weights * (grad_weights - delta_row[:, :, None])).astype(jnp.bfloat16)
        return (
            running
            + jnp.einsum(
                "qhk,khd->qhd", grad_scores, key_block, preferred_element_type=jnp.float32
            ),
            None,
        )

    query_sum, unused = lax.scan(
        second_pass,
        jnp.zeros((tok_count, heads_dev, HD), jnp.float32),
        (key_blocks, value_blocks, mask_blocks),
    )
    grad_query = (query_sum * score_scale).astype(jnp.bfloat16)
    log_all, delta_all = (
        lax.all_gather(log_total, "seq", axis=0, tiled=True),
        lax.all_gather(delta_row, "seq", axis=0, tiled=True),
    )
    local_ids = jnp.arange(rows_dev, dtype=jnp.int32)
    local_allowed = (local_ids < tok_count) | (
        lax.axis_index("seq") * text_dev + local_ids - tok_count < text_len[0]
    )
    key_three = key_local.reshape(rows_dev, heads_dev, HD)
    value_three = value_local.reshape(rows_dev, heads_dev, HD)
    query_piece = lax.all_gather(queries.reshape(tok_count, inner_dev), "seq", axis=0, tiled=True)
    grad_piece = lax.all_gather(out_grad.reshape(tok_count, inner_dev), "seq", axis=0, tiled=True)
    piece_rows = query_piece.shape[0]
    query_rows = query_piece.reshape(piece_rows, heads_dev, HD)
    grad_rows = grad_piece.reshape(piece_rows, heads_dev, HD)
    scores = (
        jnp.einsum("qhd,khd->qhk", query_rows, key_three, preferred_element_type=jnp.float32)
        * score_scale
    )
    scores = jnp.where(local_allowed[None, None, :], scores, -1e30)
    weights = jnp.exp(scores - log_all[:, :, None])
    grad_weights = jnp.einsum(
        "qhd,khd->qhk", grad_rows, value_three, preferred_element_type=jnp.float32
    )
    grad_scores = (weights * (grad_weights - delta_all[:, :, None])).astype(jnp.bfloat16)
    rounded = weights.astype(jnp.bfloat16)
    key_sum = jnp.einsum(
        "qhk,qhd->khd", grad_scores, query_rows, preferred_element_type=jnp.float32
    )
    value_sum = jnp.einsum("qhk,qhd->khd", rounded, grad_rows, preferred_element_type=jnp.float32)
    key_sum, value_sum = (key_sum, value_sum)
    grad_key = (key_sum[:tok_count] * score_scale).astype(jnp.bfloat16)
    grad_value = value_sum[:tok_count].astype(jnp.bfloat16)
    raw_query = qk_backward(projected[:, 0], query_inv, grad_query, qk_gain[0])
    raw_key = qk_backward(projected[:, 1], key_inv, grad_key, qk_gain[1])
    stacked = jnp.stack([raw_query, raw_key, grad_value.astype(jnp.float32)], axis=1).astype(
        jnp.bfloat16
    )
    stacked = stacked.reshape(tok_count, 3 * inner_dev)
    partial_grad = lax.dot_general(
        stacked, full_weight, contract_last, preferred_element_type=jnp.float32
    )
    half_width = model_width // lax.axis_size("head")
    first_col = lax.axis_index("head") * half_width
    grad_share = lax.psum_scatter(
        partial_grad.astype(jnp.bfloat16), "head", scatter_dimension=1, tiled=True
    ).astype(jnp.float32)
    normed_share = lax.dynamic_slice_in_dim(normed, first_col, half_width, 1)
    stretch_share = lax.dynamic_slice_in_dim(stretch, first_col, half_width, 0)
    adjoint_share = lax.dynamic_slice_in_dim(adjoint_rows, first_col, half_width, 1)
    grad_scaled = grad_share * (1.0 + stretch_share)
    row_sums = jnp.stack(
        [jnp.sum(grad_scaled, axis=-1), jnp.sum(grad_scaled * normed_share, axis=-1)], axis=-1
    )
    row_sums = lax.psum(row_sums, "head")
    grad_state = inv_std * (
        grad_scaled - row_sums[:, 0:1] / model_width - normed_share * row_sums[:, 1:2] / model_width
    )
    pulled = clip_scale * adjoint_share + grad_state
    return pulled[None]


def solution(mesh):
    in_specs = (
        P("dp", "seq", None),
        P("dp", "seq", None),
        P("dp", "seq", None, "head"),
        P("dp"),
        P("dp"),
        P(),
        P("dp", None, "head"),
        P(),
        P("head", "dp"),
    )
    out_specs = P("dp", "seq", "head")
    by_head = mesh.shape["seq"] == 4 and mesh.shape["dp"] == 4 and mesh.shape["head"] == 2
    shards = shards_by_head if by_head else shards_by_row
    return jax.shard_map(shards, mesh=mesh, in_specs=in_specs, out_specs=out_specs, check_vma=False)
```

```python
import functools

import jax
import jax.numpy as jnp
from jax import lax
from jax.experimental import pallas as pl
from jax.experimental.pallas import tpu as pltpu
from jax.sharding import PartitionSpec as P

HD = 64
GRANT = 60 * 1024 * 1024
SMALL_GRANT = 24 * 1024 * 1024
EXTRA = 128
NT = (((1,), (1,)), ((), ()))
NN = (((1,), (0,)), ((), ()))


def line_ring(count):
    return [0] + list(range(1, count, 2)) + [i for i in range(count - 1, 0, -1) if i % 2 == 0]


def ring_pairs(order):
    return [(order[i], order[(i + 1) % len(order)]) for i in range(len(order))]


def ring_place(order, index):
    place = jnp.int32(0)
    for position, member in enumerate(order):
        place = jnp.where(index == member, jnp.int32(position), place)
    return place


def ring_member(order, place):
    member = jnp.int32(order[0])
    for position, value in enumerate(order):
        member = jnp.where(place == position, jnp.int32(value), member)
    return member


def dot(a, b, dims):
    return lax.dot_general(a, b, dims, preferred_element_type=jnp.float32)


def equal_blocks(columns, block):
    row = lax.broadcasted_iota(jnp.int32, (columns, columns), 0)
    column = lax.broadcasted_iota(jnp.int32, (columns, columns), 1)
    return jnp.where(row // block == column // block, 1.0, 0.0).astype(jnp.bfloat16)


def head_means(values):
    parts = []
    for first in range(0, values.shape[1], 256):
        part = values[:, first : first + 256]
        ones = equal_blocks(part.shape[1], HD)
        high = part.astype(jnp.bfloat16)
        low = (part - high.astype(jnp.float32)).astype(jnp.bfloat16)
        parts.append(dot(high, ones, NN) + dot(low, ones, NN))
    return jnp.concatenate(parts, axis=1) * (1.0 / HD)


def head_gains(gain, slots):
    return jnp.concatenate([gain[0:1, :]] * slots + [gain[1:2, :]] * slots, axis=1)


def whole_tiles(columns):
    return -(-columns // 128) * 128


def spec(space):
    return pl.BlockSpec(memory_space=space)


def text_columns(text, part):
    rows = text[...].astype(jnp.float32)[:, part, :]
    return [rows[:, c * EXTRA : (c + 1) * EXTRA] for c in range(rows.shape[1] // EXTRA)]


def extra_columns(blocks, rows):
    filled = sum(one.shape[0] for one in blocks)
    blocks = blocks + [jnp.zeros((rows - filled, EXTRA), jnp.float32)]
    return jnp.concatenate(blocks, axis=0).astype(jnp.bfloat16)


def first_kernel(step, core, states, table, adjoint, text, out, rows_out, extra_out):
    rows = [table[c, pl.ds(step[0], 1), :] for c in range(3)]
    widened = states[...].astype(jnp.float32)
    centered = widened - jnp.mean(widened, axis=-1, keepdims=True)
    inv_std = lax.rsqrt(jnp.mean(centered * centered, axis=-1, keepdims=True) + 1e-06)
    half, width = states.shape
    out[:, :width] = (centered * inv_std * (1.0 + rows[1]) + rows[0]).astype(jnp.bfloat16)
    for c in range(3):
        rows_out[c : c + 1, :] = rows[c]
    squares = jnp.sum(adjoint[...] * adjoint[...], axis=0, keepdims=True)
    squares = jnp.sum(squares, axis=1, keepdims=True)
    terms = []
    for n in range(3):
        terms.append(squares.astype(jnp.bfloat16).astype(jnp.float32))
        squares = squares - terms[-1]
    lane = lax.broadcasted_iota(jnp.int32, (8, EXTRA), 1)
    sums = jnp.where(lane == 0, terms[0], jnp.where(lane == 1, terms[1], jnp.where(lane == 2, terms[2], 0.0)))
    extra = extra_columns(text_columns(text, 0) + [sums], half)
    out[:, width:] = extra
    extra_out[...] = extra


def first_call(step, core, states, table, adjoint, text):
    rows, width = states.shape
    half = rows // 2
    whole = lambda *shape: pl.BlockSpec(shape, lambda i, step, core: (0,) * len(shape))
    return pl.pallas_call(
        first_kernel,
        out_shape=(
            jax.ShapeDtypeStruct((half, width + EXTRA), jnp.bfloat16),
            jax.ShapeDtypeStruct((8, width), jnp.float32),
            jax.ShapeDtypeStruct((half, EXTRA), jnp.bfloat16),
        ),
        grid_spec=pltpu.PrefetchScalarGridSpec(
            num_scalar_prefetch=2,
            grid=(1,),
            in_specs=[
                pl.BlockSpec((half, width), lambda i, step, core: (core[0], 0)),
                whole(*table.shape),
                whole(*adjoint.shape),
                whole(*text.shape),
            ],
            out_specs=(whole(half, width + EXTRA), whole(8, width), whole(half, EXTRA)),
        ),
        compiler_params=pltpu.CompilerParams(vmem_limit_bytes=GRANT),
        cost_estimate=pl.CostEstimate(flops=8 * half * width, bytes_accessed=16 * half * width, transcendentals=0),
    )(step, core, states, table, adjoint, text)


def pick_half(core, rows):
    half = rows.shape[1] // 2
    return jnp.where(core == 0, rows[:, :half], rows[:, half:])


def cotangent_kernel(limit, core, adjoint, table_rows, text, extra, previous, following, opposite, out, clip_out):
    first = previous.shape[0] - opposite.shape[0]
    row = 8 * (text.shape[2] // EXTRA)
    squares = opposite[...].astype(jnp.float32)[row - first : row - first + 1, :]
    for terms in (extra, previous, following):
        squares = squares + terms[...].astype(jnp.float32)[row : row + 1, :]
    squares = jnp.sum(squares, axis=1, keepdims=True)
    clip_scale = jnp.minimum(1.0, limit / jnp.sqrt(squares + 1e-06))
    half, width = adjoint.shape
    out[:, :width] = (table_rows[2:3, :] * (clip_scale * adjoint[...])).astype(jnp.bfloat16)
    out[:, width:] = extra_columns(text_columns(text, 1), half)
    clip_out[...] = jnp.broadcast_to(clip_scale, clip_out.shape)


def cotangent_call(limit, core, adjoint, table_rows, text, extra, previous, following, opposite):
    rows, width = adjoint.shape
    half = rows // 2
    block = width // EXTRA
    whole = lambda one: pl.BlockSpec(one.shape, lambda i, core: (0,) * one.ndim)
    tail = lambda one: pl.BlockSpec((one.shape[0], EXTRA), lambda i, core: (0, block))
    outs = (
        jax.ShapeDtypeStruct((half, width + EXTRA), jnp.bfloat16),
        jax.ShapeDtypeStruct((8, EXTRA), jnp.float32),
    )
    return pl.pallas_call(
        functools.partial(cotangent_kernel, limit),
        out_shape=outs,
        grid_spec=pltpu.PrefetchScalarGridSpec(
            num_scalar_prefetch=1,
            grid=(1,),
            in_specs=[pl.BlockSpec((half, width), lambda i, core: (core[0], 0))]
            + [whole(table_rows), whole(text), whole(extra)]
            + [tail(one) for one in (previous, following, opposite)],
            out_specs=tuple(whole(one) for one in outs),
        ),
        compiler_params=pltpu.CompilerParams(vmem_limit_bytes=GRANT),
        cost_estimate=pl.CostEstimate(flops=4 * half * width, bytes_accessed=6 * half * width, transcendentals=0),
    )(core, adjoint, table_rows, text, extra, previous, following, opposite)


def own_kernel(
    core, states, adjoint, table_rows, text, extra, clip, out, cot_out, normed_out, stretch_out, inv_out, base_out
):
    rows, width = states.shape
    half = rows // 2
    widened = states[...].astype(jnp.float32)
    centered = widened - jnp.mean(widened, axis=-1, keepdims=True)
    inv_std = lax.rsqrt(jnp.mean(centered * centered, axis=-1, keepdims=True) + 1e-06)
    normed = centered * inv_std
    scale = 1.0 + table_rows[1:2, :]
    out[:, :width] = (normed * scale + table_rows[0:1, :]).astype(jnp.bfloat16)
    normed_out[...] = pick_half(core[0], normed)
    stretch_out[...] = pick_half(core[0], scale)
    inv_out[...] = jnp.broadcast_to(inv_std, inv_out.shape)
    clipped = clip[0:1, 0:1] * adjoint[...]
    cot_out[:, :width] = (table_rows[2:3, :] * clipped).astype(jnp.bfloat16)
    base_out[...] = pick_half(core[0], clipped)
    columns = extra_columns(text_columns(text, 1), half)
    for n in range(2):
        out[n * half : (n + 1) * half, width:] = extra[...]
        cot_out[n * half : (n + 1) * half, width:] = columns


class Copies:
    def __init__(self, sems):
        self.sems = sems
        self.count = 0

    def start(self, source, target):
        copy = pltpu.make_async_copy(source, target, self.sems.at[self.count])
        copy.start()
        self.count += 1
        return copy

    def weights(self, scalars, w_in, w_all, shard, first=0):
        columns = w_in[0].shape[1] - first
        return [
            self.start(
                piece.at[:, pl.ds(first, columns)],
                w_all.at[
                    pl.ds(pl.multiple_of(scalars[1 + n % 4] * shard, 16), shard),
                    pl.ds(n // 4 * columns, columns),
                ],
            )
            for n, piece in enumerate(w_in)
        ]

    def rows(self, core, pieces, target, rows):
        half = rows // 2
        copies = [self.start(pieces[0], target.at[pl.ds(0, rows)])]
        places = [(rows, half), (3 * rows, half)]
        parts = (len(pieces) - 5) // 2
        places += [(2 * rows + n * half // parts, half // parts) for n in range(parts)]
        for n, (first, size) in enumerate(places):
            for m, holder in enumerate((core, 1 - core)):
                there = pl.ds(pl.multiple_of(first + holder * half, 16), size)
                copies.append(self.start(pieces[1 + 2 * n + m], target.at[there]))
        return copies


def window_heads(scalars, count, rows, text_dev, gathered, width, extra, text, text_t=None):
    half = rows // 2
    for k in range(count):
        there = pl.ds(pl.multiple_of(k * rows + scalars[0] * half, 16), half)
        extra[k] = gathered[there, width:].astype(jnp.float32)
    for i in range(text.shape[0]):
        head = scalars[5] + i
        first = pl.ds(pl.multiple_of(head // 2 * text_dev, 8), text_dev)
        found = jnp.concatenate([extra[k, first, :] for k in range(count)], axis=0)
        found = jnp.where(head % 2 == 0, found[:, :HD], found[:, HD:])
        text[i] = found.astype(jnp.bfloat16)
        if text_t is not None:
            text_t[i] = found.T.astype(jnp.bfloat16)


def project_kernel(slots, count, rows, shard, width, text_dev, scalars, gain, *refs):
    refs = list(refs)
    take = lambda n: [refs.pop(0) for _ in range(n)]
    mod_in = take(9)
    w_in = take(8)
    qkv, k_t, raw_all, inv_all, text, text_t, w_keep, w_give = take(8)
    w_all, mod_all, sems, extra, qkv_s, k_t_s, raw_s, inv_s = take(8)
    inner = slots * HD
    core = scalars[0]
    copies = Copies(sems)
    w_copies = copies.weights(scalars, w_in, w_all, shard)
    row_copies = copies.rows(core, mod_in, mod_all, rows)

    lane = lax.broadcasted_iota(jnp.int32, (1, 2 * inner), 1)
    gains = head_gains(gain, slots) * jnp.where(lane < inner, HD ** (-0.5), 1.0)
    identity = equal_blocks(inner, 1)
    for copy in w_copies:
        copy.wait()
    half = width // 2
    columns = pl.ds(0, w_keep.shape[1])
    out_copies = []
    for holder, target in ((core, w_keep), (1 - core, w_give)):
        source = w_all.at[pl.ds(pl.multiple_of(holder * half, 16), half), columns]
        out_copies.append(copies.start(source, target))
    for copy in row_copies:
        copy.wait()
    projected = jnp.dot(mod_all[:, :width], w_all[:, : 3 * inner], preferred_element_type=jnp.float32)
    raw = projected[:, : 2 * inner]
    raw_s[...] = raw
    out_copies.append(copies.start(raw_s, raw_all))
    inverse = lax.rsqrt(head_means(raw * raw) + 1e-06)
    inv_s[...] = inverse
    out_copies.append(copies.start(inv_s, inv_all))
    qkv_s[:, : 2 * inner] = (raw * inverse * gains).astype(jnp.bfloat16)
    qkv_s[:, 2 * inner :] = projected[:, 2 * inner :].astype(jnp.bfloat16)
    out_copies.append(copies.start(qkv_s, qkv))
    k_t_s[...] = dot(identity, qkv_s[:, inner : 2 * inner], NT).astype(jnp.bfloat16)
    out_copies.append(copies.start(k_t_s, k_t))
    window_heads(scalars, count, rows, text_dev, mod_all, width, extra, text, text_t)
    for copy in out_copies:
        copy.wait()


def attend_kernel(slots, count, rows, shard, width, text_dev, first_column, scalars, gain, *refs):
    refs = list(refs)
    take = lambda n: [refs.pop(0) for _ in range(n)]
    projected = take(8)
    cot_in = take(7)
    w_in = take(4)
    mine_out, theirs_out, rest_out = take(3)
    w_out, cot_all, sems, extra, values_text = take(5)
    d_all, grads, stacked = take(3)
    qkv, k_t, raw_all, inv_all, text, text_t, w_keep, w_give = refs
    inner = slots * HD
    tokens = rows * count
    core = scalars[0]
    copies = Copies(sems)
    w_copies = copies.weights(scalars, w_in, w_out, shard, first_column)
    row_copies = copies.rows(core, cot_in, cot_all, rows)
    pairs = list(zip(projected, refs))
    local_copies = [copies.start(*pairs[n]) for n in (0, 1, 4, 5)]
    score_scale = HD ** (-0.5)
    span = 2 * rows

    text_rows = count * text_dev
    row = lax.broadcasted_iota(jnp.int32, (text_rows, span), 0)
    text_id = row
    for k in range(count):
        inside = (row >= k * text_dev) & (row < (k + 1) * text_dev)
        text_id = jnp.where(inside, row + (scalars[7 + k] - k) * text_dev, text_id)
    bias = jnp.where(text_id < scalars[6], 0.0, -1e30)

    for copy in w_copies:
        copy.wait()
    for copy in row_copies:
        copy.wait()
    out_grad = jnp.dot(cot_all[:, :width], w_out[...], preferred_element_type=jnp.float32)
    d_all[...] = out_grad.astype(jnp.bfloat16)
    window_heads(scalars, count, rows, text_dev, cot_all, width, extra, values_text)
    late_copies = [copies.start(*pairs[n]) for n in (2, 3, 6, 7)]
    for copy in local_copies:
        copy.wait()

    d_first = d_all.shape[1] - inner
    for i in range(slots):
        columns = [slice(n * inner + i * HD, n * inner + (i + 1) * HD) for n in range(3)]
        keys, values = qkv[:, columns[1]], qkv[:, columns[2]]
        keys_t = k_t[i * HD : (i + 1) * HD, :]
        grad_k, grad_v = 0.0, 0.0
        for b in range(count // 2):
            here = slice(b * span, (b + 1) * span)
            query = qkv[here, columns[0]]
            grad = d_all[here, d_first + i * HD : d_first + (i + 1) * HD]
            scores = dot(keys, query, NT)
            text_scores = dot(text[i], query, NT) + bias
            col_max = jnp.maximum(
                jnp.max(scores, axis=0, keepdims=True), jnp.max(text_scores, axis=0, keepdims=True)
            )
            exps = jnp.exp(scores - col_max)
            text_exps = jnp.exp(text_scores - col_max)
            total = jnp.sum(exps, axis=0, keepdims=True) + jnp.sum(text_exps, axis=0, keepdims=True)
            inverse = 1.0 / total
            grad_w = dot(values, grad, NT)
            text_grad_w = dot(values_text[i], grad, NT)
            delta = inverse * (
                jnp.sum(exps * grad_w, axis=0, keepdims=True)
                + jnp.sum(text_exps * text_grad_w, axis=0, keepdims=True)
            )
            weights = exps * inverse
            grad_s = (weights * (grad_w - delta)).astype(jnp.bfloat16)
            text_grad_s = (text_exps * inverse * (text_grad_w - delta)).astype(jnp.bfloat16)
            grad_k += dot(grad_s, query, NN)
            grad_v += dot(weights.astype(jnp.bfloat16), grad, NN)
            grad_q = dot(keys_t, grad_s, NN) + dot(text_t[i], text_grad_s, NN)
            grads[here, columns[0]] = grad_q.T * score_scale
        grads[:, columns[1]] = grad_k
        grads[:, columns[2]] = grad_v

    lane = lax.broadcasted_iota(jnp.int32, (1, inner), 1)
    mine = jnp.zeros((1, inner), jnp.float32)
    for i in range(slots):
        inside = (lane >= i * HD) & (lane < (i + 1) * HD) & (scalars[7 + count + i] > 0)
        mine = jnp.where(inside, 1.0, mine)
    gains = head_gains(gain, slots)
    for copy in late_copies[:2]:
        copy.wait()
    for b in range(count // 2):
        here = slice(b * span, (b + 1) * span)
        scaled = grads[here, : 2 * inner].astype(jnp.bfloat16).astype(jnp.float32) * gains
        raw, inverse = raw_all[here, :], inv_all[here, :]
        back = scaled * inverse - raw * head_means(scaled * raw) * (inverse * inverse * inverse)
        valid = jnp.concatenate([mine, mine], axis=1) > 0.0
        stacked[here, : 2 * inner] = jnp.where(valid, back, 0.0).astype(jnp.bfloat16)
        back = jnp.where(mine > 0.0, grads[here, 2 * inner :], 0.0).astype(jnp.bfloat16)
        stacked[here, 2 * inner : 3 * inner] = back
    stacked[:, 3 * inner :] = jnp.zeros((tokens, stacked.shape[1] - 3 * inner), jnp.bfloat16)
    first = stacked[rows : 2 * rows, :]
    rest_out[: (count - 2) * rows, :] = stacked[2 * rows :, :]
    rest_out[(count - 2) * rows :, :] = stacked[:rows, :]
    for copy in late_copies[2:]:
        copy.wait()
    theirs_out[...] = dot(first, w_give[...], NT).astype(jnp.bfloat16)
    mine_out[...] = dot(first, w_keep[...], NT)


def project_call(scalars, gain, mod, weights, slots, rows, text_dev, count):
    shard = weights[0].shape[0]
    columns = 4 * slots * HD
    width = mod[0].shape[1] - EXTRA
    tokens = rows * count
    text_rows = text_dev * count
    f32, bf16 = jnp.float32, jnp.bfloat16
    vmem, hbm = spec(pltpu.VMEM), spec(pl.ANY)
    inner = slots * HD
    shapes = [((tokens, 3 * inner), bf16), ((inner, tokens), bf16)] + [((tokens, 2 * inner), f32)] * 2
    shapes += [((slots, text_rows, HD), bf16), ((slots, HD, text_rows), bf16)]
    shapes += [((width // 2, whole_tiles(3 * slots * HD)), bf16)] * 2
    return pl.pallas_call(
        functools.partial(project_kernel, slots, count, rows, shard, width, text_dev),
        out_shape=tuple(jax.ShapeDtypeStruct(*one) for one in shapes),
        in_specs=[spec(pltpu.SMEM), vmem] + [hbm] * (len(mod) + len(weights)),
        out_specs=(hbm,) * 4 + (vmem,) * 2 + (hbm,) * 2,
        scratch_shapes=[
            pltpu.VMEM((width, columns), bf16),
            pltpu.VMEM((tokens, width + EXTRA), bf16),
            pltpu.SemaphoreType.DMA((len(mod) + len(weights) + 10,)),
            pltpu.VMEM((count, rows // 2, EXTRA), f32),
        ]
        + [pltpu.VMEM(*one) for one in shapes[:4]],
        compiler_params=pltpu.CompilerParams(vmem_limit_bytes=GRANT),
        cost_estimate=pl.CostEstimate(
            flops=2 * tokens * width * 3 * slots * HD,
            bytes_accessed=2 * (tokens * width + columns * width) + 4 * tokens * columns,
            transcendentals=0,
        ),
    )(scalars, gain, *mod, *weights)


def attend_call(scalars, gain, operands, cot, weights, slots, rows, text_dev):
    count = operands[0].shape[0] // rows
    shard, columns = weights[0].shape
    width = cot[0].shape[1] - EXTRA
    tokens = rows * count
    inner = slots * HD
    stacked = whole_tiles(3 * inner)
    first = (columns - inner) // 128 * 128
    f32, bf16 = jnp.float32, jnp.bfloat16
    vmem, hbm = spec(pltpu.VMEM), spec(pl.ANY)
    shapes = [((rows, width // 2), f32), ((rows, width // 2), bf16), ((tokens - rows, stacked), bf16)]
    return pl.pallas_call(
        functools.partial(attend_kernel, slots, count, rows, shard, width, text_dev, first),
        out_shape=tuple(jax.ShapeDtypeStruct(*one) for one in shapes),
        in_specs=[spec(pltpu.SMEM), vmem] + [hbm] * (len(operands) + len(cot) + len(weights)),
        out_specs=(vmem,) * len(shapes),
        scratch_shapes=[
            pltpu.VMEM((width, columns - first), bf16),
            pltpu.VMEM((tokens, width + EXTRA), bf16),
            pltpu.SemaphoreType.DMA((len(operands) + len(cot) + len(weights),)),
            pltpu.VMEM((count, rows // 2, EXTRA), f32),
            pltpu.VMEM((slots, text_dev * count, HD), bf16),
            pltpu.VMEM((tokens, columns - first), bf16),
            pltpu.VMEM((tokens, 3 * inner), f32),
            pltpu.VMEM((tokens, stacked), bf16),
        ]
        + [pltpu.VMEM(one.shape, one.dtype) for one in operands],
        compiler_params=pltpu.CompilerParams(vmem_limit_bytes=GRANT),
        cost_estimate=pl.CostEstimate(
            flops=2 * tokens * width * inner + 10 * tokens * tokens * inner,
            bytes_accessed=2 * (tokens * width + columns * width),
            transcendentals=slots * tokens * tokens,
        ),
    )(scalars, gain, *operands, *cot, *weights)


def backward_kernel(own, other, w_own, w_other, *outs):
    total = dot(own[...], w_own[...], NT) + dot(other[...], w_other[...], NT)
    part = outs[0].shape[0]
    for n, out in enumerate(outs):
        out[...] = total[n * part : (n + 1) * part].astype(out.dtype)


def backward_call(own, other, w_own, w_other, part, dtype):
    rows, inner = own.shape
    half = w_own.shape[0]
    vmem = spec(pltpu.VMEM)
    return pl.pallas_call(
        backward_kernel,
        out_shape=(jax.ShapeDtypeStruct((part, half), dtype),) * (rows // part),
        in_specs=[vmem] * 4,
        out_specs=(vmem,) * (rows // part),
        compiler_params=pltpu.CompilerParams(vmem_limit_bytes=SMALL_GRANT),
        cost_estimate=pl.CostEstimate(
            flops=4 * rows * half * inner,
            bytes_accessed=4 * (rows + half) * inner + 4 * rows * half,
            transcendentals=0,
        ),
    )(own, other, w_own, w_other)


def sums_kernel(own_near, own_far, near, far, scale, normed, grad_out, sums_out):
    half = near.shape[0]
    for part, (own, moving) in enumerate(((own_near, near), (own_far, far))):
        here = slice(part * half, (part + 1) * half)
        grad = (own[...] + moving[...].astype(jnp.float32)) * scale[...]
        grad_out[here, :] = grad
        first = jnp.sum(grad, axis=-1, keepdims=True)
        second = jnp.sum(grad * normed[here, :], axis=-1, keepdims=True)
        lane = lax.broadcasted_iota(jnp.int32, (half, 128), 1)
        sums_out[here, :] = jnp.where(lane == 0, first, second)


def last_kernel(width, grad, sums, other, normed, base, inv_std, out):
    total = (sums[...] + other[...]) * (1.0 / width)
    rows = base[...] + inv_std[:, 0:1] * (
        grad[...] - total[:, 0:1] - normed[...] * total[:, 1:2]
    )
    out[...] = rows.T


def local_call(kernel, shapes, scalar_count, *operands, grant=SMALL_GRANT):
    vmem = spec(pltpu.VMEM)
    return pl.pallas_call(
        kernel,
        out_shape=tuple(jax.ShapeDtypeStruct(*one) for one in shapes),
        in_specs=[spec(pltpu.SMEM)] * scalar_count + [vmem] * (len(operands) - scalar_count),
        out_specs=(vmem,) * len(shapes),
        compiler_params=pltpu.CompilerParams(vmem_limit_bytes=grant),
        cost_estimate=pl.CostEstimate(
            flops=sum(one.size for one in operands),
            bytes_accessed=sum(one.size * one.dtype.itemsize for one in operands),
            transcendentals=0,
        ),
    )(*operands)


def shards_by_head(states, adjoint, text_kv, text_len, step_index, modulation, w_qkv, qk_gain, w_out):
    hidden_state = states[0]
    adjoint_rows = adjoint[0]
    tok_count, model_width = hidden_state.shape
    seq_count = lax.axis_size("seq")
    inner_dev = w_qkv.shape[2]
    heads_dev = inner_dev // HD
    shard = w_qkv.shape[0]
    slots = -(-heads_dev // seq_count)
    inner = slots * HD
    half_rows = tok_count // 2
    half_width = model_width // 2
    f32, bf16 = jnp.float32, jnp.bfloat16
    core = lax.axis_index("head").astype(jnp.int32)
    seq_index = lax.axis_index("seq")
    dp_index = lax.axis_index("dp")
    pin = lax.optimization_barrier

    seq_order = line_ring(seq_count)
    seq_place = ring_place(seq_order, seq_index)
    seq_next = ring_pairs(seq_order)
    swap = [(0, 1), (1, 0)]
    first_way = [(2 * p + c, 2 * (p ^ (1 + c)) + c) for p in range(4) for c in range(2)]
    second_way = [(2 * p + c, 2 * (p ^ (2 - c)) + c) for p in range(4) for c in range(2)]

    first = seq_index * heads_dev // seq_count
    stop = (seq_index + 1) * heads_dev // seq_count
    window = jnp.minimum(first, heads_dev - slots)
    valid = [(window + i >= first) & (window + i < stop) for i in range(slots)]
    owners = [ring_member(seq_order, (seq_place - k + seq_count) % seq_count) for k in range(seq_count)]
    w_index = [dp_index, dp_index ^ (1 + core), dp_index ^ (2 - core), dp_index ^ 3]
    scalars = [core] + w_index + [window, text_len[0]] + owners + valid
    scalars = jnp.stack([one.astype(jnp.int32) for one in scalars])

    def step(moving):
        return lax.ppermute(moving, "seq", seq_next)

    def other_core(moving):
        return lax.ppermute(moving, "head", swap)

    def step_back(moving):
        return lax.ppermute(moving, "seq", [(b, a) for a, b in seq_next])

    quarter = half_rows // 2

    def spread(moving):
        return [step(moving), step_back(moving)]

    def pass_on(received):
        return [step(received[0][:quarter]), step_back(received[1][quarter:])]

    mod_half, table_rows, extra = first_call(
        step_index, core[None], hidden_state, modulation.transpose(1, 0, 2), adjoint_rows, text_kv[0]
    )
    mod_near = spread(mod_half)

    w_qkv, w_out, mod_half = pin((w_qkv, w_out, mod_half))
    take = lambda c: lax.dynamic_slice(w_qkv, (0, c, window * HD), (shard, 1, inner))[:, 0]
    own_w = [
        jnp.concatenate([take(0), take(1)], axis=1),
        jnp.concatenate([take(2), lax.dynamic_slice_in_dim(w_out, window * HD, inner, 0).T], axis=1),
    ]
    w_first = [lax.ppermute(part, ("dp", "head"), first_way) for part in own_w]
    w_second = [lax.ppermute(part, ("dp", "head"), second_way) for part in own_w]

    text_dev = text_kv.shape[1]
    mod_far = pass_on(mod_near)
    clip_limit = 0.5 * (tok_count * seq_count * model_width) ** 0.5
    extra, *w_first = pin((extra, *w_first))
    cot_half, clip = cotangent_call(
        clip_limit, scalars, adjoint_rows, table_rows, text_kv[0], extra, *mod_near, mod_far[1]
    )
    cot_half, mod_far[0] = pin((cot_half, mod_far[0]))
    cot_near = spread(cot_half)
    modulated, cotangent, normed_share, scale_share, inv_std, base = local_call(
        own_kernel,
        [((tok_count, model_width + EXTRA), bf16)] * 2
        + [
            ((tok_count, half_width), f32),
            ((1, half_width), f32),
            ((tok_count, 128), f32),
            ((tok_count, half_width), f32),
        ],
        1,
        core[None],
        hidden_state,
        adjoint_rows,
        table_rows,
        text_kv[0],
        extra,
        clip,
        grant=GRANT,
    )
    def pieces(own, received):
        return [own] + [one for moved in received for one in (moved, other_core(moved))]

    mod_far = list(pin((*mod_far, modulated))[:2])
    mod_pieces = pieces(modulated, mod_near + mod_far)
    w_diagonal = [lax.ppermute(part, ("dp", "head"), second_way) for part in w_first]
    weights = [part[n] for n in range(2) for part in (own_w, w_first, w_second, w_diagonal)]
    cot_near[0] = pin((cot_near[0], w_second, w_diagonal))[0]
    cot_far = [step(cot_near[0])]

    cot_pieces = pieces(cotangent, cot_near)
    *cot_pieces, mod_pieces[-1] = pin((*cot_pieces, mod_pieces[-1]))
    *operands, w_keep, w_give = project_call(
        scalars, qk_gain, mod_pieces, weights, slots, tok_count, text_dev, seq_count
    )
    w_give, cot_far[0] = pin((w_give, *cot_far))
    cot_pieces += pieces(None, cot_far)[1:]
    given, *cot_pieces = pin((w_give, *cot_pieces))
    w_other = other_core(given)
    mine, theirs, rest = attend_call(
        scalars, qk_gain, operands + [w_keep, w_give], cot_pieces, weights[4:], slots, tok_count, text_dev
    )
    first = (mine + other_core(theirs).astype(f32)).astype(bf16)
    moving = [first[:half_rows], first[half_rows:]]
    other_rest = other_core(rest)
    rest, other_rest, *_ = pin((rest, other_rest, *moving))
    own = backward_call(rest, other_rest, w_keep, w_other, half_rows, f32)
    for j in range(2, seq_count):
        moving = [step(part) for part in moving]
        moving = [
            (a + b.astype(f32)).astype(bf16) for a, b in zip(own[2 * (j - 2) : 2 * (j - 1)], moving)
        ]
    moving = [step(part) for part in moving]

    grad_scaled, sums = local_call(
        sums_kernel,
        [((tok_count, half_width), f32), ((tok_count, 128), f32)],
        0,
        *own[-2:],
        *moving,
        scale_share,
        normed_share,
    )
    (pulled,) = local_call(
        functools.partial(last_kernel, model_width),
        [((half_width, tok_count), f32)],
        0,
        grad_scaled,
        sums,
        other_core(sums),
        normed_share,
        base,
        inv_std,
    )
    return pulled.T[None]


def qk_normalize(values, gains):
    inverse = lax.rsqrt(jnp.mean(values * values, axis=-1, keepdims=True) + 1e-06)
    return ((values * inverse * gains).astype(jnp.bfloat16), inverse)


def qk_backward(values, inverse, cotangent, gains):
    scaled = cotangent.astype(jnp.float32) * gains
    return (
        scaled * inverse - values * jnp.mean(scaled * values, axis=-1, keepdims=True) * inverse**3
    )


def shards_by_row(states, adjoint, text_kv, text_len, step_index, modulation, w_qkv, qk_gain, w_out):
    hidden_state = states[0]
    adjoint_rows = adjoint[0]
    tok_count, model_width = hidden_state.shape
    seq_count = lax.axis_size("seq")
    inner_dev = w_qkv.shape[2]
    heads_dev = inner_dev // HD
    score_scale = HD ** (-0.5)
    squares = lax.psum(jnp.sum(adjoint_rows * adjoint_rows), "seq")
    clip_limit = 0.5 * (tok_count * seq_count * model_width) ** 0.5
    clip_scale = jnp.minimum(1.0, clip_limit / jnp.sqrt(squares + 1e-06))
    table_row = lax.dynamic_index_in_dim(modulation, step_index[0], 0, keepdims=False)
    offset_row = table_row[0]
    stretch = table_row[1]
    gating = table_row[2]
    widened = hidden_state.astype(jnp.float32)
    centered = widened - jnp.mean(widened, axis=-1, keepdims=True)
    inv_std = lax.rsqrt(jnp.mean(centered * centered, axis=-1, keepdims=True) + 1e-06)
    normed = centered * inv_std
    modulated = (normed * (1.0 + stretch) + offset_row).astype(jnp.bfloat16)
    cotangent = (gating * (clip_scale * adjoint_rows)).astype(jnp.bfloat16)
    contract_last = (((1,), (1,)), ((), ()))
    full_weight = lax.all_gather(w_qkv, "dp", axis=0, tiled=True).reshape(
        model_width, 3 * inner_dev
    )
    projected = jnp.dot(modulated, full_weight, preferred_element_type=jnp.float32)
    out_raw = lax.dot_general(
        cotangent,
        lax.all_gather(w_out, "dp", axis=1, tiled=True),
        contract_last,
        preferred_element_type=jnp.float32,
    )
    projected = projected.reshape(tok_count, 3, heads_dev, HD)
    queries, query_inv = qk_normalize(projected[:, 0], qk_gain[0])
    own_keys, key_inv = qk_normalize(projected[:, 1], qk_gain[1])
    own_values = projected[:, 2].astype(jnp.bfloat16)
    out_grad = out_raw.astype(jnp.bfloat16).reshape(tok_count, heads_dev, HD)
    text_keys = text_kv[0, :, 0, :]
    text_values = text_kv[0, :, 1, :]
    text_dev = text_keys.shape[0]
    rows_dev = tok_count + text_dev
    key_local = jnp.concatenate([own_keys.reshape(tok_count, inner_dev), text_keys], axis=0)
    value_local = jnp.concatenate([own_values.reshape(tok_count, inner_dev), text_values], axis=0)
    key_all, value_all = (
        lax.all_gather(key_local, "seq", axis=0, tiled=True),
        lax.all_gather(value_local, "seq", axis=0, tiled=True),
    )
    all_rows = rows_dev * seq_count
    row_ids = jnp.arange(all_rows, dtype=jnp.int32)
    owner = row_ids // rows_dev
    within = row_ids % rows_dev
    allowed = (within < tok_count) | (owner * text_dev + within - tok_count < text_len[0])
    group = 1
    while group * 2 * rows_dev <= 512 and seq_count % (group * 2) == 0:
        group = group * 2
    block_rows = group * rows_dev
    block_count = all_rows // block_rows
    key_blocks = key_all.reshape(block_count, block_rows, heads_dev, HD)
    value_blocks = value_all.reshape(block_count, block_rows, heads_dev, HD)
    mask_blocks = allowed.reshape(block_count, block_rows)

    def block_scores(key_block, mask_block):
        scores = (
            jnp.einsum("qhd,khd->qhk", queries, key_block, preferred_element_type=jnp.float32)
            * score_scale
        )
        return jnp.where(mask_block[None, None, :], scores, -1e30)

    def first_pass(carry, block):
        row_max, row_sum, row_dot = carry
        key_block, value_block, mask_block = block
        scores = block_scores(key_block, mask_block)
        new_max = jnp.maximum(row_max, jnp.max(scores, axis=-1))
        rescale = jnp.exp(row_max - new_max)
        exps = jnp.exp(scores - new_max[:, :, None])
        grad_weights = jnp.einsum(
            "qhd,khd->qhk", out_grad, value_block, preferred_element_type=jnp.float32
        )
        return (
            (
                new_max,
                row_sum * rescale + jnp.sum(exps, axis=-1),
                row_dot * rescale + jnp.sum(exps * grad_weights, axis=-1),
            ),
            None,
        )

    start_state = (
        jnp.full((tok_count, heads_dev), -1e30, jnp.float32),
        jnp.zeros((tok_count, heads_dev), jnp.float32),
        jnp.zeros((tok_count, heads_dev), jnp.float32),
    )
    (row_max, row_sum, row_dot), unused = lax.scan(
        first_pass, start_state, (key_blocks, value_blocks, mask_blocks)
    )
    log_total = row_max + jnp.log(row_sum)
    delta_row = row_dot / row_sum

    def second_pass(running, block):
        key_block, value_block, mask_block = block
        weights = jnp.exp(block_scores(key_block, mask_block) - log_total[:, :, None])
        grad_weights = jnp.einsum(
            "qhd,khd->qhk", out_grad, value_block, preferred_element_type=jnp.float32
        )
        grad_scores = (weights * (grad_weights - delta_row[:, :, None])).astype(jnp.bfloat16)
        return (
            running
            + jnp.einsum(
                "qhk,khd->qhd", grad_scores, key_block, preferred_element_type=jnp.float32
            ),
            None,
        )

    query_sum, unused = lax.scan(
        second_pass,
        jnp.zeros((tok_count, heads_dev, HD), jnp.float32),
        (key_blocks, value_blocks, mask_blocks),
    )
    grad_query = (query_sum * score_scale).astype(jnp.bfloat16)
    log_all, delta_all = (
        lax.all_gather(log_total, "seq", axis=0, tiled=True),
        lax.all_gather(delta_row, "seq", axis=0, tiled=True),
    )
    local_ids = jnp.arange(rows_dev, dtype=jnp.int32)
    local_allowed = (local_ids < tok_count) | (
        lax.axis_index("seq") * text_dev + local_ids - tok_count < text_len[0]
    )
    key_three = key_local.reshape(rows_dev, heads_dev, HD)
    value_three = value_local.reshape(rows_dev, heads_dev, HD)
    query_piece = lax.all_gather(queries.reshape(tok_count, inner_dev), "seq", axis=0, tiled=True)
    grad_piece = lax.all_gather(out_grad.reshape(tok_count, inner_dev), "seq", axis=0, tiled=True)
    piece_rows = query_piece.shape[0]
    query_rows = query_piece.reshape(piece_rows, heads_dev, HD)
    grad_rows = grad_piece.reshape(piece_rows, heads_dev, HD)
    scores = (
        jnp.einsum("qhd,khd->qhk", query_rows, key_three, preferred_element_type=jnp.float32)
        * score_scale
    )
    scores = jnp.where(local_allowed[None, None, :], scores, -1e30)
    weights = jnp.exp(scores - log_all[:, :, None])
    grad_weights = jnp.einsum(
        "qhd,khd->qhk", grad_rows, value_three, preferred_element_type=jnp.float32
    )
    grad_scores = (weights * (grad_weights - delta_all[:, :, None])).astype(jnp.bfloat16)
    rounded = weights.astype(jnp.bfloat16)
    key_sum = jnp.einsum(
        "qhk,qhd->khd", grad_scores, query_rows, preferred_element_type=jnp.float32
    )
    value_sum = jnp.einsum("qhk,qhd->khd", rounded, grad_rows, preferred_element_type=jnp.float32)
    key_sum, value_sum = (key_sum, value_sum)
    grad_key = (key_sum[:tok_count] * score_scale).astype(jnp.bfloat16)
    grad_value = value_sum[:tok_count].astype(jnp.bfloat16)
    raw_query = qk_backward(projected[:, 0], query_inv, grad_query, qk_gain[0])
    raw_key = qk_backward(projected[:, 1], key_inv, grad_key, qk_gain[1])
    stacked = jnp.stack([raw_query, raw_key, grad_value.astype(jnp.float32)], axis=1).astype(
        jnp.bfloat16
    )
    stacked = stacked.reshape(tok_count, 3 * inner_dev)
    partial_grad = lax.dot_general(
        stacked, full_weight, contract_last, preferred_element_type=jnp.float32
    )
    half_width = model_width // lax.axis_size("head")
    first_col = lax.axis_index("head") * half_width
    grad_share = lax.psum_scatter(
        partial_grad.astype(jnp.bfloat16), "head", scatter_dimension=1, tiled=True
    ).astype(jnp.float32)
    normed_share = lax.dynamic_slice_in_dim(normed, first_col, half_width, 1)
    stretch_share = lax.dynamic_slice_in_dim(stretch, first_col, half_width, 0)
    adjoint_share = lax.dynamic_slice_in_dim(adjoint_rows, first_col, half_width, 1)
    grad_scaled = grad_share * (1.0 + stretch_share)
    row_sums = jnp.stack(
        [jnp.sum(grad_scaled, axis=-1), jnp.sum(grad_scaled * normed_share, axis=-1)], axis=-1
    )
    row_sums = lax.psum(row_sums, "head")
    grad_state = inv_std * (
        grad_scaled - row_sums[:, 0:1] / model_width - normed_share * row_sums[:, 1:2] / model_width
    )
    pulled = clip_scale * adjoint_share + grad_state
    return pulled[None]


def solution(mesh):
    in_specs = (
        P("dp", "seq", None),
        P("dp", "seq", None),
        P("dp", "seq", None, "head"),
        P("dp"),
        P("dp"),
        P(),
        P("dp", None, "head"),
        P(),
        P("head", "dp"),
    )
    out_specs = P("dp", "seq", "head")
    by_head = mesh.shape["seq"] == 4 and mesh.shape["dp"] == 4 and mesh.shape["head"] == 2
    shards = shards_by_head if by_head else shards_by_row
    return jax.shard_map(shards, mesh=mesh, in_specs=in_specs, out_specs=out_specs, check_vma=False)
```

```python
import functools

import jax
import jax.numpy as jnp
from jax import lax
from jax.experimental import pallas as pl
from jax.experimental.pallas import tpu as pltpu
from jax.sharding import PartitionSpec as P

HD = 64
GRANT = 60 * 1024 * 1024
MAIN_GRANT = 54 * 1024 * 1024
SMALL_GRANT = 24 * 1024 * 1024
EXTRA = 128
NT = (((1,), (1,)), ((), ()))
NN = (((1,), (0,)), ((), ()))


def line_ring(count):
    return [0] + list(range(1, count, 2)) + [i for i in range(count - 1, 0, -1) if i % 2 == 0]


def ring_pairs(order):
    return [(order[i], order[(i + 1) % len(order)]) for i in range(len(order))]


def ring_place(order, index):
    place = jnp.int32(0)
    for position, member in enumerate(order):
        place = jnp.where(index == member, jnp.int32(position), place)
    return place


def ring_member(order, place):
    member = jnp.int32(order[0])
    for position, value in enumerate(order):
        member = jnp.where(place == position, jnp.int32(value), member)
    return member


def dot(a, b, dims):
    return lax.dot_general(a, b, dims, preferred_element_type=jnp.float32)


def equal_blocks(columns, block):
    row = lax.broadcasted_iota(jnp.int32, (columns, columns), 0)
    column = lax.broadcasted_iota(jnp.int32, (columns, columns), 1)
    return jnp.where(row // block == column // block, 1.0, 0.0).astype(jnp.bfloat16)


def head_means(values):
    parts = []
    for first in range(0, values.shape[1], 256):
        part = values[:, first : first + 256]
        ones = equal_blocks(part.shape[1], HD)
        high = part.astype(jnp.bfloat16)
        low = (part - high.astype(jnp.float32)).astype(jnp.bfloat16)
        parts.append(dot(high, ones, NN) + dot(low, ones, NN))
    return jnp.concatenate(parts, axis=1) * (1.0 / HD)


def head_gains(gain, slots):
    return jnp.concatenate([gain[0:1, :]] * slots + [gain[1:2, :]] * slots, axis=1)


def whole_tiles(columns):
    return -(-columns // 128) * 128


def spec(space):
    return pl.BlockSpec(memory_space=space)


def text_columns(text, part):
    rows = text[...].astype(jnp.float32)[:, part, :]
    return [rows[:, c * EXTRA : (c + 1) * EXTRA] for c in range(rows.shape[1] // EXTRA)]


def extra_columns(blocks, rows):
    filled = sum(one.shape[0] for one in blocks)
    blocks = blocks + [jnp.zeros((rows - filled, EXTRA), jnp.float32)]
    return jnp.concatenate(blocks, axis=0).astype(jnp.bfloat16)


def first_kernel(step, core, states, table, adjoint, text, out, rows_out, extra_out):
    rows = [table[c, pl.ds(step[0], 1), :] for c in range(3)]
    widened = states[...].astype(jnp.float32)
    centered = widened - jnp.mean(widened, axis=-1, keepdims=True)
    inv_std = lax.rsqrt(jnp.mean(centered * centered, axis=-1, keepdims=True) + 1e-06)
    half, width = states.shape
    out[:, :width] = (centered * inv_std * (1.0 + rows[1]) + rows[0]).astype(jnp.bfloat16)
    for c in range(3):
        rows_out[c : c + 1, :] = rows[c]
    squares = jnp.sum(adjoint[...] * adjoint[...], axis=0, keepdims=True)
    squares = jnp.sum(squares, axis=1, keepdims=True)
    terms = []
    for n in range(3):
        terms.append(squares.astype(jnp.bfloat16).astype(jnp.float32))
        squares = squares - terms[-1]
    lane = lax.broadcasted_iota(jnp.int32, (8, EXTRA), 1)
    sums = jnp.where(lane == 0, terms[0], jnp.where(lane == 1, terms[1], jnp.where(lane == 2, terms[2], 0.0)))
    extra = extra_columns(text_columns(text, 0) + [sums], half)
    out[:, width:] = extra
    extra_out[...] = extra


def first_call(step, core, states, table, adjoint, text):
    rows, width = states.shape
    half = rows // 2
    whole = lambda *shape: pl.BlockSpec(shape, lambda i, step, core: (0,) * len(shape))
    return pl.pallas_call(
        first_kernel,
        out_shape=(
            jax.ShapeDtypeStruct((half, width + EXTRA), jnp.bfloat16),
            jax.ShapeDtypeStruct((8, width), jnp.float32),
            jax.ShapeDtypeStruct((half, EXTRA), jnp.bfloat16),
        ),
        grid_spec=pltpu.PrefetchScalarGridSpec(
            num_scalar_prefetch=2,
            grid=(1,),
            in_specs=[
                pl.BlockSpec((half, width), lambda i, step, core: (core[0], 0)),
                whole(*table.shape),
                whole(*adjoint.shape),
                whole(*text.shape),
            ],
            out_specs=(whole(half, width + EXTRA), whole(8, width), whole(half, EXTRA)),
        ),
        compiler_params=pltpu.CompilerParams(vmem_limit_bytes=GRANT),
        cost_estimate=pl.CostEstimate(flops=8 * half * width, bytes_accessed=16 * half * width, transcendentals=0),
    )(step, core, states, table, adjoint, text)


def pick_half(core, rows):
    half = rows.shape[1] // 2
    return jnp.where(core == 0, rows[:, :half], rows[:, half:])


def cotangent_kernel(limit, core, adjoint, table_rows, text, extra, previous, following, opposite, out, clip_out):
    first = previous.shape[0] - opposite.shape[0]
    row = 8 * (text.shape[2] // EXTRA)
    squares = opposite[...].astype(jnp.float32)[row - first : row - first + 1, :]
    for terms in (extra, previous, following):
        squares = squares + terms[...].astype(jnp.float32)[row : row + 1, :]
    squares = jnp.sum(squares, axis=1, keepdims=True)
    clip_scale = jnp.minimum(1.0, limit / jnp.sqrt(squares + 1e-06))
    half, width = adjoint.shape
    out[:, :width] = (table_rows[2:3, :] * (clip_scale * adjoint[...])).astype(jnp.bfloat16)
    out[:, width:] = extra_columns(text_columns(text, 1), half)
    clip_out[...] = jnp.broadcast_to(clip_scale, clip_out.shape)


def cotangent_call(limit, core, adjoint, table_rows, text, extra, previous, following, opposite):
    rows, width = adjoint.shape
    half = rows // 2
    block = width // EXTRA
    whole = lambda one: pl.BlockSpec(one.shape, lambda i, core: (0,) * one.ndim)
    tail = lambda one: pl.BlockSpec((one.shape[0], EXTRA), lambda i, core: (0, block))
    outs = (
        jax.ShapeDtypeStruct((half, width + EXTRA), jnp.bfloat16),
        jax.ShapeDtypeStruct((8, EXTRA), jnp.float32),
    )
    return pl.pallas_call(
        functools.partial(cotangent_kernel, limit),
        out_shape=outs,
        grid_spec=pltpu.PrefetchScalarGridSpec(
            num_scalar_prefetch=1,
            grid=(1,),
            in_specs=[pl.BlockSpec((half, width), lambda i, core: (core[0], 0))]
            + [whole(table_rows), whole(text), whole(extra)]
            + [tail(one) for one in (previous, following, opposite)],
            out_specs=tuple(whole(one) for one in outs),
        ),
        compiler_params=pltpu.CompilerParams(vmem_limit_bytes=GRANT),
        cost_estimate=pl.CostEstimate(flops=4 * half * width, bytes_accessed=6 * half * width, transcendentals=0),
    )(core, adjoint, table_rows, text, extra, previous, following, opposite)


def own_kernel(
    core, states, adjoint, table_rows, text, extra, clip, out, cot_out, normed_out, stretch_out, inv_out, base_out
):
    rows, width = states.shape
    half = rows // 2
    widened = states[...].astype(jnp.float32)
    centered = widened - jnp.mean(widened, axis=-1, keepdims=True)
    inv_std = lax.rsqrt(jnp.mean(centered * centered, axis=-1, keepdims=True) + 1e-06)
    normed = centered * inv_std
    scale = 1.0 + table_rows[1:2, :]
    out[:, :width] = (normed * scale + table_rows[0:1, :]).astype(jnp.bfloat16)
    normed_out[...] = pick_half(core[0], normed)
    stretch_out[...] = pick_half(core[0], scale)
    inv_out[...] = jnp.broadcast_to(inv_std, inv_out.shape)
    clipped = clip[0:1, 0:1] * adjoint[...]
    cot_out[:, :width] = (table_rows[2:3, :] * clipped).astype(jnp.bfloat16)
    base_out[...] = pick_half(core[0], clipped)
    columns = extra_columns(text_columns(text, 1), half)
    for n in range(2):
        out[n * half : (n + 1) * half, width:] = extra[...]
        cot_out[n * half : (n + 1) * half, width:] = columns


class Copies:
    def __init__(self, sems):
        self.sems = sems
        self.count = 0

    def start(self, source, target):
        copy = pltpu.make_async_copy(source, target, self.sems.at[self.count])
        copy.start()
        self.count += 1
        return copy

    def weights(self, scalars, w_in, w_all, shard, first=0):
        columns = w_in[0].shape[1] - first
        return [
            self.start(
                piece.at[:, pl.ds(first, columns)],
                w_all.at[
                    pl.ds(pl.multiple_of(scalars[1 + n % 4] * shard, 16), shard),
                    pl.ds(n // 4 * columns, columns),
                ],
            )
            for n, piece in enumerate(w_in)
        ]

    def rows(self, core, pieces, target, rows):
        half = rows // 2
        copies = [self.start(pieces[0], target.at[pl.ds(0, rows)])]
        places = [(rows, half), (3 * rows, half)]
        parts = (len(pieces) - 5) // 2
        places += [(2 * rows + n * half // parts, half // parts) for n in range(parts)]
        for n, (first, size) in enumerate(places):
            for m, holder in enumerate((core, 1 - core)):
                there = pl.ds(pl.multiple_of(first + holder * half, 16), size)
                copies.append(self.start(pieces[1 + 2 * n + m], target.at[there]))
        return copies


def window_heads(scalars, count, rows, text_dev, gathered, width, extra, text, text_t=None):
    half = rows // 2
    for k in range(count):
        there = pl.ds(pl.multiple_of(k * rows + scalars[0] * half, 16), half)
        extra[k] = gathered[there, width:].astype(jnp.float32)
    for i in range(text.shape[0]):
        head = scalars[5] + i
        first = pl.ds(pl.multiple_of(head // 2 * text_dev, 8), text_dev)
        found = jnp.concatenate([extra[k, first, :] for k in range(count)], axis=0)
        found = jnp.where(head % 2 == 0, found[:, :HD], found[:, HD:])
        text[i] = found.astype(jnp.bfloat16)
        if text_t is not None:
            text_t[i] = found.T.astype(jnp.bfloat16)


def project_kernel(slots, count, rows, shard, width, text_dev, scalars, gain, *refs):
    refs = list(refs)
    take = lambda n: [refs.pop(0) for _ in range(n)]
    mod_in = take(9)
    w_in = take(8)
    qkv, k_t, raw_all, inv_all, text, text_t, w_keep, w_give = take(8)
    w_all, mod_all, sems, extra, qkv_s, k_t_s, raw_s, inv_s = take(8)
    inner = slots * HD
    core = scalars[0]
    copies = Copies(sems)
    w_copies = copies.weights(scalars, w_in, w_all, shard)
    row_copies = copies.rows(core, mod_in, mod_all, rows)

    lane = lax.broadcasted_iota(jnp.int32, (1, 2 * inner), 1)
    gains = head_gains(gain, slots) * jnp.where(lane < inner, HD ** (-0.5), 1.0)
    identity = equal_blocks(inner, 1)
    for copy in w_copies:
        copy.wait()
    half = width // 2
    columns = pl.ds(0, w_keep.shape[1])
    out_copies = []
    for holder, target in ((core, w_keep), (1 - core, w_give)):
        source = w_all.at[pl.ds(pl.multiple_of(holder * half, 16), half), columns]
        out_copies.append(copies.start(source, target))
    for copy in row_copies:
        copy.wait()
    projected = jnp.dot(mod_all[:, :width], w_all[:, : 3 * inner], preferred_element_type=jnp.float32)
    raw = projected[:, : 2 * inner]
    raw_s[...] = raw
    out_copies.append(copies.start(raw_s, raw_all))
    inverse = lax.rsqrt(head_means(raw * raw) + 1e-06)
    inv_s[...] = inverse
    out_copies.append(copies.start(inv_s, inv_all))
    qkv_s[:, : 2 * inner] = (raw * inverse * gains).astype(jnp.bfloat16)
    qkv_s[:, 2 * inner :] = projected[:, 2 * inner :].astype(jnp.bfloat16)
    out_copies.append(copies.start(qkv_s, qkv))
    k_t_s[...] = dot(identity, qkv_s[:, inner : 2 * inner], NT).astype(jnp.bfloat16)
    out_copies.append(copies.start(k_t_s, k_t))
    window_heads(scalars, count, rows, text_dev, mod_all, width, extra, text, text_t)
    for copy in out_copies:
        copy.wait()


def attend_kernel(slots, count, rows, shard, width, text_dev, first_column, scalars, gain, *refs):
    refs = list(refs)
    take = lambda n: [refs.pop(0) for _ in range(n)]
    projected = take(8)
    cot_in = take(7)
    w_in = take(4)
    mine_out, theirs_out, rest_out = take(3)
    w_out, cot_all, sems, extra, values_text = take(5)
    d_all, grads, stacked = take(3)
    qkv, k_t, raw_all, inv_all, text, text_t, w_keep, w_give = refs
    inner = slots * HD
    tokens = rows * count
    core = scalars[0]
    copies = Copies(sems)
    w_copies = copies.weights(scalars, w_in, w_out, shard, first_column)
    row_copies = copies.rows(core, cot_in, cot_all, rows)
    pairs = list(zip(projected, refs))
    local_copies = [copies.start(*pairs[n]) for n in (0, 1, 4, 5)]
    score_scale = HD ** (-0.5)
    span = 2 * rows

    text_rows = count * text_dev
    row = lax.broadcasted_iota(jnp.int32, (text_rows, span), 0)
    text_id = row
    for k in range(count):
        inside = (row >= k * text_dev) & (row < (k + 1) * text_dev)
        text_id = jnp.where(inside, row + (scalars[7 + k] - k) * text_dev, text_id)
    bias = jnp.where(text_id < scalars[6], 0.0, -1e30)

    for copy in w_copies:
        copy.wait()
    for copy in row_copies:
        copy.wait()
    out_grad = jnp.dot(cot_all[:, :width], w_out[...], preferred_element_type=jnp.float32)
    d_all[...] = out_grad.astype(jnp.bfloat16)
    window_heads(scalars, count, rows, text_dev, cot_all, width, extra, values_text)
    late_copies = [copies.start(*pairs[n]) for n in (2, 3, 6, 7)]
    for copy in local_copies:
        copy.wait()

    d_first = d_all.shape[1] - inner
    for i in range(slots):
        columns = [slice(n * inner + i * HD, n * inner + (i + 1) * HD) for n in range(3)]
        keys, values = qkv[:, columns[1]], qkv[:, columns[2]]
        keys_t = k_t[i * HD : (i + 1) * HD, :]
        grad_k, grad_v = 0.0, 0.0
        for b in range(count // 2):
            here = slice(b * span, (b + 1) * span)
            query = qkv[here, columns[0]]
            grad = d_all[here, d_first + i * HD : d_first + (i + 1) * HD]
            scores = dot(keys, query, NT)
            text_scores = dot(text[i], query, NT) + bias
            col_max = jnp.maximum(
                jnp.max(scores, axis=0, keepdims=True), jnp.max(text_scores, axis=0, keepdims=True)
            )
            exps = jnp.exp(scores - col_max)
            text_exps = jnp.exp(text_scores - col_max)
            total = jnp.sum(exps, axis=0, keepdims=True) + jnp.sum(text_exps, axis=0, keepdims=True)
            inverse = 1.0 / total
            grad_w = dot(values, grad, NT)
            text_grad_w = dot(values_text[i], grad, NT)
            delta = inverse * (
                jnp.sum(exps * grad_w, axis=0, keepdims=True)
                + jnp.sum(text_exps * text_grad_w, axis=0, keepdims=True)
            )
            weights = exps * inverse
            grad_s = (weights * (grad_w - delta)).astype(jnp.bfloat16)
            text_grad_s = (text_exps * inverse * (text_grad_w - delta)).astype(jnp.bfloat16)
            grad_k += dot(grad_s, query, NN)
            grad_v += dot(weights.astype(jnp.bfloat16), grad, NN)
            grad_q = dot(keys_t, grad_s, NN) + dot(text_t[i], text_grad_s, NN)
            grads[here, columns[0]] = grad_q.T * score_scale
        grads[:, columns[1]] = grad_k
        grads[:, columns[2]] = grad_v

    lane = lax.broadcasted_iota(jnp.int32, (1, inner), 1)
    mine = jnp.zeros((1, inner), jnp.float32)
    for i in range(slots):
        inside = (lane >= i * HD) & (lane < (i + 1) * HD) & (scalars[7 + count + i] > 0)
        mine = jnp.where(inside, 1.0, mine)
    gains = head_gains(gain, slots)
    for copy in late_copies[:2]:
        copy.wait()
    for b in range(count // 2):
        here = slice(b * span, (b + 1) * span)
        scaled = grads[here, : 2 * inner].astype(jnp.bfloat16).astype(jnp.float32) * gains
        raw, inverse = raw_all[here, :], inv_all[here, :]
        back = scaled * inverse - raw * head_means(scaled * raw) * (inverse * inverse * inverse)
        valid = jnp.concatenate([mine, mine], axis=1) > 0.0
        stacked[here, : 2 * inner] = jnp.where(valid, back, 0.0).astype(jnp.bfloat16)
        back = jnp.where(mine > 0.0, grads[here, 2 * inner :], 0.0).astype(jnp.bfloat16)
        stacked[here, 2 * inner : 3 * inner] = back
    stacked[:, 3 * inner :] = jnp.zeros((tokens, stacked.shape[1] - 3 * inner), jnp.bfloat16)
    first = stacked[rows : 2 * rows, :]
    rest_out[: (count - 2) * rows, :] = stacked[2 * rows :, :]
    rest_out[(count - 2) * rows :, :] = stacked[:rows, :]
    for copy in late_copies[2:]:
        copy.wait()
    theirs_out[...] = dot(first, w_give[...], NT).astype(jnp.bfloat16)
    mine_out[...] = dot(first, w_keep[...], NT)


def project_call(scalars, gain, mod, weights, slots, rows, text_dev, count):
    shard = weights[0].shape[0]
    columns = 4 * slots * HD
    width = mod[0].shape[1] - EXTRA
    tokens = rows * count
    text_rows = text_dev * count
    f32, bf16 = jnp.float32, jnp.bfloat16
    vmem, hbm = spec(pltpu.VMEM), spec(pl.ANY)
    inner = slots * HD
    shapes = [((tokens, 3 * inner), bf16), ((inner, tokens), bf16)] + [((tokens, 2 * inner), f32)] * 2
    shapes += [((slots, text_rows, HD), bf16), ((slots, HD, text_rows), bf16)]
    shapes += [((width // 2, whole_tiles(3 * slots * HD)), bf16)] * 2
    return pl.pallas_call(
        functools.partial(project_kernel, slots, count, rows, shard, width, text_dev),
        out_shape=tuple(jax.ShapeDtypeStruct(*one) for one in shapes),
        in_specs=[spec(pltpu.SMEM), vmem] + [hbm] * (len(mod) + len(weights)),
        out_specs=(hbm,) * 4 + (vmem,) * 2 + (hbm,) * 2,
        scratch_shapes=[
            pltpu.VMEM((width, columns), bf16),
            pltpu.VMEM((tokens, width + EXTRA), bf16),
            pltpu.SemaphoreType.DMA((len(mod) + len(weights) + 10,)),
            pltpu.VMEM((count, rows // 2, EXTRA), f32),
        ]
        + [pltpu.VMEM(*one) for one in shapes[:4]],
        compiler_params=pltpu.CompilerParams(vmem_limit_bytes=MAIN_GRANT),
        cost_estimate=pl.CostEstimate(
            flops=2 * tokens * width * 3 * slots * HD,
            bytes_accessed=2 * (tokens * width + columns * width) + 4 * tokens * columns,
            transcendentals=0,
        ),
    )(scalars, gain, *mod, *weights)


def attend_call(scalars, gain, operands, cot, weights, slots, rows, text_dev):
    count = operands[0].shape[0] // rows
    shard, columns = weights[0].shape
    width = cot[0].shape[1] - EXTRA
    tokens = rows * count
    inner = slots * HD
    stacked = whole_tiles(3 * inner)
    first = (columns - inner) // 128 * 128
    f32, bf16 = jnp.float32, jnp.bfloat16
    vmem, hbm = spec(pltpu.VMEM), spec(pl.ANY)
    shapes = [((rows, width // 2), f32), ((rows, width // 2), bf16), ((tokens - rows, stacked), bf16)]
    return pl.pallas_call(
        functools.partial(attend_kernel, slots, count, rows, shard, width, text_dev, first),
        out_shape=tuple(jax.ShapeDtypeStruct(*one) for one in shapes),
        in_specs=[spec(pltpu.SMEM), vmem] + [hbm] * (len(operands) + len(cot) + len(weights)),
        out_specs=(vmem,) * len(shapes),
        scratch_shapes=[
            pltpu.VMEM((width, columns - first), bf16),
            pltpu.VMEM((tokens, width + EXTRA), bf16),
            pltpu.SemaphoreType.DMA((len(operands) + len(cot) + len(weights),)),
            pltpu.VMEM((count, rows // 2, EXTRA), f32),
            pltpu.VMEM((slots, text_dev * count, HD), bf16),
            pltpu.VMEM((tokens, columns - first), bf16),
            pltpu.VMEM((tokens, 3 * inner), f32),
            pltpu.VMEM((tokens, stacked), bf16),
        ]
        + [pltpu.VMEM(one.shape, one.dtype) for one in operands],
        compiler_params=pltpu.CompilerParams(vmem_limit_bytes=MAIN_GRANT),
        cost_estimate=pl.CostEstimate(
            flops=2 * tokens * width * inner + 10 * tokens * tokens * inner,
            bytes_accessed=2 * (tokens * width + columns * width),
            transcendentals=slots * tokens * tokens,
        ),
    )(scalars, gain, *operands, *cot, *weights)


def backward_kernel(own, other, w_own, w_other, *outs):
    total = dot(own[...], w_own[...], NT) + dot(other[...], w_other[...], NT)
    part = outs[0].shape[0]
    for n, out in enumerate(outs):
        out[...] = total[n * part : (n + 1) * part].astype(out.dtype)


def backward_call(own, other, w_own, w_other, part, dtype):
    rows, inner = own.shape
    half = w_own.shape[0]
    vmem = spec(pltpu.VMEM)
    return pl.pallas_call(
        backward_kernel,
        out_shape=(jax.ShapeDtypeStruct((part, half), dtype),) * (rows // part),
        in_specs=[vmem] * 4,
        out_specs=(vmem,) * (rows // part),
        compiler_params=pltpu.CompilerParams(vmem_limit_bytes=SMALL_GRANT),
        cost_estimate=pl.CostEstimate(
            flops=4 * rows * half * inner,
            bytes_accessed=4 * (rows + half) * inner + 4 * rows * half,
            transcendentals=0,
        ),
    )(own, other, w_own, w_other)


def sums_kernel(own_near, own_far, near, far, scale, normed, grad_out, sums_out):
    half = near.shape[0]
    for part, (own, moving) in enumerate(((own_near, near), (own_far, far))):
        here = slice(part * half, (part + 1) * half)
        grad = (own[...] + moving[...].astype(jnp.float32)) * scale[...]
        grad_out[here, :] = grad
        first = jnp.sum(grad, axis=-1, keepdims=True)
        second = jnp.sum(grad * normed[here, :], axis=-1, keepdims=True)
        lane = lax.broadcasted_iota(jnp.int32, (half, 128), 1)
        sums_out[here, :] = jnp.where(lane == 0, first, second)


def last_kernel(width, grad, sums, other, normed, base, inv_std, out):
    total = (sums[...] + other[...]) * (1.0 / width)
    rows = base[...] + inv_std[:, 0:1] * (
        grad[...] - total[:, 0:1] - normed[...] * total[:, 1:2]
    )
    out[...] = rows.T


def local_call(kernel, shapes, scalar_count, *operands, grant=SMALL_GRANT):
    vmem = spec(pltpu.VMEM)
    return pl.pallas_call(
        kernel,
        out_shape=tuple(jax.ShapeDtypeStruct(*one) for one in shapes),
        in_specs=[spec(pltpu.SMEM)] * scalar_count + [vmem] * (len(operands) - scalar_count),
        out_specs=(vmem,) * len(shapes),
        compiler_params=pltpu.CompilerParams(vmem_limit_bytes=grant),
        cost_estimate=pl.CostEstimate(
            flops=sum(one.size for one in operands),
            bytes_accessed=sum(one.size * one.dtype.itemsize for one in operands),
            transcendentals=0,
        ),
    )(*operands)


def shards_by_head(states, adjoint, text_kv, text_len, step_index, modulation, w_qkv, qk_gain, w_out):
    hidden_state = states[0]
    adjoint_rows = adjoint[0]
    tok_count, model_width = hidden_state.shape
    seq_count = lax.axis_size("seq")
    inner_dev = w_qkv.shape[2]
    heads_dev = inner_dev // HD
    shard = w_qkv.shape[0]
    slots = -(-heads_dev // seq_count)
    inner = slots * HD
    half_rows = tok_count // 2
    half_width = model_width // 2
    f32, bf16 = jnp.float32, jnp.bfloat16
    core = lax.axis_index("head").astype(jnp.int32)
    seq_index = lax.axis_index("seq")
    dp_index = lax.axis_index("dp")
    pin = lax.optimization_barrier

    seq_order = line_ring(seq_count)
    seq_place = ring_place(seq_order, seq_index)
    seq_next = ring_pairs(seq_order)
    swap = [(0, 1), (1, 0)]
    first_way = [(2 * p + c, 2 * (p ^ (1 + c)) + c) for p in range(4) for c in range(2)]
    second_way = [(2 * p + c, 2 * (p ^ (2 - c)) + c) for p in range(4) for c in range(2)]

    first = seq_index * heads_dev // seq_count
    stop = (seq_index + 1) * heads_dev // seq_count
    window = jnp.minimum(first, heads_dev - slots)
    valid = [(window + i >= first) & (window + i < stop) for i in range(slots)]
    owners = [ring_member(seq_order, (seq_place - k + seq_count) % seq_count) for k in range(seq_count)]
    w_index = [dp_index, dp_index ^ (1 + core), dp_index ^ (2 - core), dp_index ^ 3]
    scalars = [core] + w_index + [window, text_len[0]] + owners + valid
    scalars = jnp.stack([one.astype(jnp.int32) for one in scalars])

    def step(moving):
        return lax.ppermute(moving, "seq", seq_next)

    def other_core(moving):
        return lax.ppermute(moving, "head", swap)

    def step_back(moving):
        return lax.ppermute(moving, "seq", [(b, a) for a, b in seq_next])

    quarter = half_rows // 2

    def spread(moving):
        return [step(moving), step_back(moving)]

    def pass_on(received):
        return [step(received[0][:quarter]), step_back(received[1][quarter:])]

    mod_half, table_rows, extra = first_call(
        step_index, core[None], hidden_state, modulation.transpose(1, 0, 2), adjoint_rows, text_kv[0]
    )
    mod_near = spread(mod_half)

    w_qkv, w_out, mod_half = pin((w_qkv, w_out, mod_half))
    take = lambda c: lax.dynamic_slice(w_qkv, (0, c, window * HD), (shard, 1, inner))[:, 0]
    own_w = [
        jnp.concatenate([take(0), take(1)], axis=1),
        jnp.concatenate([take(2), lax.dynamic_slice_in_dim(w_out, window * HD, inner, 0).T], axis=1),
    ]
    w_first = [lax.ppermute(part, ("dp", "head"), first_way) for part in own_w]
    w_second = [lax.ppermute(part, ("dp", "head"), second_way) for part in own_w]

    text_dev = text_kv.shape[1]
    mod_far = pass_on(mod_near)
    clip_limit = 0.5 * (tok_count * seq_count * model_width) ** 0.5
    extra, *w_first = pin((extra, *w_first))
    cot_half, clip = cotangent_call(
        clip_limit, scalars, adjoint_rows, table_rows, text_kv[0], extra, *mod_near, mod_far[1]
    )
    cot_half, mod_far[0] = pin((cot_half, mod_far[0]))
    cot_near = spread(cot_half)
    modulated, cotangent, normed_share, scale_share, inv_std, base = local_call(
        own_kernel,
        [((tok_count, model_width + EXTRA), bf16)] * 2
        + [
            ((tok_count, half_width), f32),
            ((1, half_width), f32),
            ((tok_count, 128), f32),
            ((tok_count, half_width), f32),
        ],
        1,
        core[None],
        hidden_state,
        adjoint_rows,
        table_rows,
        text_kv[0],
        extra,
        clip,
        grant=GRANT,
    )
    def pieces(own, received):
        return [own] + [one for moved in received for one in (moved, other_core(moved))]

    mod_far = list(pin((*mod_far, modulated))[:2])
    mod_pieces = pieces(modulated, mod_near + mod_far)
    w_diagonal = [lax.ppermute(part, ("dp", "head"), second_way) for part in w_first]
    weights = [part[n] for n in range(2) for part in (own_w, w_first, w_second, w_diagonal)]
    cot_near[0] = pin((cot_near[0], w_second, w_diagonal))[0]
    cot_far = [step(cot_near[0])]

    cot_pieces = pieces(cotangent, cot_near)
    *cot_pieces, mod_pieces[-1] = pin((*cot_pieces, mod_pieces[-1]))
    *operands, w_keep, w_give = project_call(
        scalars, qk_gain, mod_pieces, weights, slots, tok_count, text_dev, seq_count
    )
    w_give, cot_far[0] = pin((w_give, *cot_far))
    cot_pieces += pieces(None, cot_far)[1:]
    given, *cot_pieces = pin((w_give, *cot_pieces))
    w_other = other_core(given)
    mine, theirs, rest = attend_call(
        scalars, qk_gain, operands + [w_keep, w_give], cot_pieces, weights[4:], slots, tok_count, text_dev
    )
    first = (mine + other_core(theirs).astype(f32)).astype(bf16)
    moving = [first[:half_rows], first[half_rows:]]
    other_rest = other_core(rest)
    rest, other_rest, *_ = pin((rest, other_rest, *moving))
    own = backward_call(rest, other_rest, w_keep, w_other, half_rows, f32)
    for j in range(2, seq_count):
        moving = [step(part) for part in moving]
        moving = [
            (a + b.astype(f32)).astype(bf16) for a, b in zip(own[2 * (j - 2) : 2 * (j - 1)], moving)
        ]
    moving = [step(part) for part in moving]

    grad_scaled, sums = local_call(
        sums_kernel,
        [((tok_count, half_width), f32), ((tok_count, 128), f32)],
        0,
        *own[-2:],
        *moving,
        scale_share,
        normed_share,
    )
    (pulled,) = local_call(
        functools.partial(last_kernel, model_width),
        [((half_width, tok_count), f32)],
        0,
        grad_scaled,
        sums,
        other_core(sums),
        normed_share,
        base,
        inv_std,
    )
    return pulled.T[None]


def qk_normalize(values, gains):
    inverse = lax.rsqrt(jnp.mean(values * values, axis=-1, keepdims=True) + 1e-06)
    return ((values * inverse * gains).astype(jnp.bfloat16), inverse)


def qk_backward(values, inverse, cotangent, gains):
    scaled = cotangent.astype(jnp.float32) * gains
    return (
        scaled * inverse - values * jnp.mean(scaled * values, axis=-1, keepdims=True) * inverse**3
    )


def shards_by_row(states, adjoint, text_kv, text_len, step_index, modulation, w_qkv, qk_gain, w_out):
    hidden_state = states[0]
    adjoint_rows = adjoint[0]
    tok_count, model_width = hidden_state.shape
    seq_count = lax.axis_size("seq")
    inner_dev = w_qkv.shape[2]
    heads_dev = inner_dev // HD
    score_scale = HD ** (-0.5)
    squares = lax.psum(jnp.sum(adjoint_rows * adjoint_rows), "seq")
    clip_limit = 0.5 * (tok_count * seq_count * model_width) ** 0.5
    clip_scale = jnp.minimum(1.0, clip_limit / jnp.sqrt(squares + 1e-06))
    table_row = lax.dynamic_index_in_dim(modulation, step_index[0], 0, keepdims=False)
    offset_row = table_row[0]
    stretch = table_row[1]
    gating = table_row[2]
    widened = hidden_state.astype(jnp.float32)
    centered = widened - jnp.mean(widened, axis=-1, keepdims=True)
    inv_std = lax.rsqrt(jnp.mean(centered * centered, axis=-1, keepdims=True) + 1e-06)
    normed = centered * inv_std
    modulated = (normed * (1.0 + stretch) + offset_row).astype(jnp.bfloat16)
    cotangent = (gating * (clip_scale * adjoint_rows)).astype(jnp.bfloat16)
    contract_last = (((1,), (1,)), ((), ()))
    full_weight = lax.all_gather(w_qkv, "dp", axis=0, tiled=True).reshape(
        model_width, 3 * inner_dev
    )
    projected = jnp.dot(modulated, full_weight, preferred_element_type=jnp.float32)
    out_raw = lax.dot_general(
        cotangent,
        lax.all_gather(w_out, "dp", axis=1, tiled=True),
        contract_last,
        preferred_element_type=jnp.float32,
    )
    projected = projected.reshape(tok_count, 3, heads_dev, HD)
    queries, query_inv = qk_normalize(projected[:, 0], qk_gain[0])
    own_keys, key_inv = qk_normalize(projected[:, 1], qk_gain[1])
    own_values = projected[:, 2].astype(jnp.bfloat16)
    out_grad = out_raw.astype(jnp.bfloat16).reshape(tok_count, heads_dev, HD)
    text_keys = text_kv[0, :, 0, :]
    text_values = text_kv[0, :, 1, :]
    text_dev = text_keys.shape[0]
    rows_dev = tok_count + text_dev
    key_local = jnp.concatenate([own_keys.reshape(tok_count, inner_dev), text_keys], axis=0)
    value_local = jnp.concatenate([own_values.reshape(tok_count, inner_dev), text_values], axis=0)
    key_all, value_all = (
        lax.all_gather(key_local, "seq", axis=0, tiled=True),
        lax.all_gather(value_local, "seq", axis=0, tiled=True),
    )
    all_rows = rows_dev * seq_count
    row_ids = jnp.arange(all_rows, dtype=jnp.int32)
    owner = row_ids // rows_dev
    within = row_ids % rows_dev
    allowed = (within < tok_count) | (owner * text_dev + within - tok_count < text_len[0])
    group = 1
    while group * 2 * rows_dev <= 512 and seq_count % (group * 2) == 0:
        group = group * 2
    block_rows = group * rows_dev
    block_count = all_rows // block_rows
    key_blocks = key_all.reshape(block_count, block_rows, heads_dev, HD)
    value_blocks = value_all.reshape(block_count, block_rows, heads_dev, HD)
    mask_blocks = allowed.reshape(block_count, block_rows)

    def block_scores(key_block, mask_block):
        scores = (
            jnp.einsum("qhd,khd->qhk", queries, key_block, preferred_element_type=jnp.float32)
            * score_scale
        )
        return jnp.where(mask_block[None, None, :], scores, -1e30)

    def first_pass(carry, block):
        row_max, row_sum, row_dot = carry
        key_block, value_block, mask_block = block
        scores = block_scores(key_block, mask_block)
        new_max = jnp.maximum(row_max, jnp.max(scores, axis=-1))
        rescale = jnp.exp(row_max - new_max)
        exps = jnp.exp(scores - new_max[:, :, None])
        grad_weights = jnp.einsum(
            "qhd,khd->qhk", out_grad, value_block, preferred_element_type=jnp.float32
        )
        return (
            (
                new_max,
                row_sum * rescale + jnp.sum(exps, axis=-1),
                row_dot * rescale + jnp.sum(exps * grad_weights, axis=-1),
            ),
            None,
        )

    start_state = (
        jnp.full((tok_count, heads_dev), -1e30, jnp.float32),
        jnp.zeros((tok_count, heads_dev), jnp.float32),
        jnp.zeros((tok_count, heads_dev), jnp.float32),
    )
    (row_max, row_sum, row_dot), unused = lax.scan(
        first_pass, start_state, (key_blocks, value_blocks, mask_blocks)
    )
    log_total = row_max + jnp.log(row_sum)
    delta_row = row_dot / row_sum

    def second_pass(running, block):
        key_block, value_block, mask_block = block
        weights = jnp.exp(block_scores(key_block, mask_block) - log_total[:, :, None])
        grad_weights = jnp.einsum(
            "qhd,khd->qhk", out_grad, value_block, preferred_element_type=jnp.float32
        )
        grad_scores = (weights * (grad_weights - delta_row[:, :, None])).astype(jnp.bfloat16)
        return (
            running
            + jnp.einsum(
                "qhk,khd->qhd", grad_scores, key_block, preferred_element_type=jnp.float32
            ),
            None,
        )

    query_sum, unused = lax.scan(
        second_pass,
        jnp.zeros((tok_count, heads_dev, HD), jnp.float32),
        (key_blocks, value_blocks, mask_blocks),
    )
    grad_query = (query_sum * score_scale).astype(jnp.bfloat16)
    log_all, delta_all = (
        lax.all_gather(log_total, "seq", axis=0, tiled=True),
        lax.all_gather(delta_row, "seq", axis=0, tiled=True),
    )
    local_ids = jnp.arange(rows_dev, dtype=jnp.int32)
    local_allowed = (local_ids < tok_count) | (
        lax.axis_index("seq") * text_dev + local_ids - tok_count < text_len[0]
    )
    key_three = key_local.reshape(rows_dev, heads_dev, HD)
    value_three = value_local.reshape(rows_dev, heads_dev, HD)
    query_piece = lax.all_gather(queries.reshape(tok_count, inner_dev), "seq", axis=0, tiled=True)
    grad_piece = lax.all_gather(out_grad.reshape(tok_count, inner_dev), "seq", axis=0, tiled=True)
    piece_rows = query_piece.shape[0]
    query_rows = query_piece.reshape(piece_rows, heads_dev, HD)
    grad_rows = grad_piece.reshape(piece_rows, heads_dev, HD)
    scores = (
        jnp.einsum("qhd,khd->qhk", query_rows, key_three, preferred_element_type=jnp.float32)
        * score_scale
    )
    scores = jnp.where(local_allowed[None, None, :], scores, -1e30)
    weights = jnp.exp(scores - log_all[:, :, None])
    grad_weights = jnp.einsum(
        "qhd,khd->qhk", grad_rows, value_three, preferred_element_type=jnp.float32
    )
    grad_scores = (weights * (grad_weights - delta_all[:, :, None])).astype(jnp.bfloat16)
    rounded = weights.astype(jnp.bfloat16)
    key_sum = jnp.einsum(
        "qhk,qhd->khd", grad_scores, query_rows, preferred_element_type=jnp.float32
    )
    value_sum = jnp.einsum("qhk,qhd->khd", rounded, grad_rows, preferred_element_type=jnp.float32)
    key_sum, value_sum = (key_sum, value_sum)
    grad_key = (key_sum[:tok_count] * score_scale).astype(jnp.bfloat16)
    grad_value = value_sum[:tok_count].astype(jnp.bfloat16)
    raw_query = qk_backward(projected[:, 0], query_inv, grad_query, qk_gain[0])
    raw_key = qk_backward(projected[:, 1], key_inv, grad_key, qk_gain[1])
    stacked = jnp.stack([raw_query, raw_key, grad_value.astype(jnp.float32)], axis=1).astype(
        jnp.bfloat16
    )
    stacked = stacked.reshape(tok_count, 3 * inner_dev)
    partial_grad = lax.dot_general(
        stacked, full_weight, contract_last, preferred_element_type=jnp.float32
    )
    half_width = model_width // lax.axis_size("head")
    first_col = lax.axis_index("head") * half_width
    grad_share = lax.psum_scatter(
        partial_grad.astype(jnp.bfloat16), "head", scatter_dimension=1, tiled=True
    ).astype(jnp.float32)
    normed_share = lax.dynamic_slice_in_dim(normed, first_col, half_width, 1)
    stretch_share = lax.dynamic_slice_in_dim(stretch, first_col, half_width, 0)
    adjoint_share = lax.dynamic_slice_in_dim(adjoint_rows, first_col, half_width, 1)
    grad_scaled = grad_share * (1.0 + stretch_share)
    row_sums = jnp.stack(
        [jnp.sum(grad_scaled, axis=-1), jnp.sum(grad_scaled * normed_share, axis=-1)], axis=-1
    )
    row_sums = lax.psum(row_sums, "head")
    grad_state = inv_std * (
        grad_scaled - row_sums[:, 0:1] / model_width - normed_share * row_sums[:, 1:2] / model_width
    )
    pulled = clip_scale * adjoint_share + grad_state
    return pulled[None]


def solution(mesh):
    in_specs = (
        P("dp", "seq", None),
        P("dp", "seq", None),
        P("dp", "seq", None, "head"),
        P("dp"),
        P("dp"),
        P(),
        P("dp", None, "head"),
        P(),
        P("head", "dp"),
    )
    out_specs = P("dp", "seq", "head")
    by_head = mesh.shape["seq"] == 4 and mesh.shape["dp"] == 4 and mesh.shape["head"] == 2
    shards = shards_by_head if by_head else shards_by_row
    return jax.shard_map(shards, mesh=mesh, in_specs=in_specs, out_specs=out_specs, check_vma=False)
```

```python
import functools

import jax
import jax.numpy as jnp
from jax import lax
from jax.experimental import pallas as pl
from jax.experimental.pallas import tpu as pltpu
from jax.sharding import PartitionSpec as P

HD = 64
GRANT = 60 * 1024 * 1024
MAIN_GRANT = 32 * 1024 * 1024
SMALL_GRANT = 24 * 1024 * 1024
EXTRA = 128
NT = (((1,), (1,)), ((), ()))
NN = (((1,), (0,)), ((), ()))


def line_ring(count):
    return [0] + list(range(1, count, 2)) + [i for i in range(count - 1, 0, -1) if i % 2 == 0]


def ring_pairs(order):
    return [(order[i], order[(i + 1) % len(order)]) for i in range(len(order))]


def ring_place(order, index):
    place = jnp.int32(0)
    for position, member in enumerate(order):
        place = jnp.where(index == member, jnp.int32(position), place)
    return place


def ring_member(order, place):
    member = jnp.int32(order[0])
    for position, value in enumerate(order):
        member = jnp.where(place == position, jnp.int32(value), member)
    return member


def dot(a, b, dims):
    return lax.dot_general(a, b, dims, preferred_element_type=jnp.float32)


def equal_blocks(columns, block):
    row = lax.broadcasted_iota(jnp.int32, (columns, columns), 0)
    column = lax.broadcasted_iota(jnp.int32, (columns, columns), 1)
    return jnp.where(row // block == column // block, 1.0, 0.0).astype(jnp.bfloat16)


def head_means(values):
    parts = []
    for first in range(0, values.shape[1], 256):
        part = values[:, first : first + 256]
        ones = equal_blocks(part.shape[1], HD)
        high = part.astype(jnp.bfloat16)
        low = (part - high.astype(jnp.float32)).astype(jnp.bfloat16)
        parts.append(dot(high, ones, NN) + dot(low, ones, NN))
    return jnp.concatenate(parts, axis=1) * (1.0 / HD)


def head_gains(gain, slots):
    return jnp.concatenate([gain[0:1, :]] * slots + [gain[1:2, :]] * slots, axis=1)


def whole_tiles(columns):
    return -(-columns // 128) * 128


def spec(space):
    return pl.BlockSpec(memory_space=space)


def text_columns(text, part):
    rows = text[...].astype(jnp.float32)[:, part, :]
    return [rows[:, c * EXTRA : (c + 1) * EXTRA] for c in range(rows.shape[1] // EXTRA)]


def extra_columns(blocks, rows):
    filled = sum(one.shape[0] for one in blocks)
    blocks = blocks + [jnp.zeros((rows - filled, EXTRA), jnp.float32)]
    return jnp.concatenate(blocks, axis=0).astype(jnp.bfloat16)


def first_kernel(step, core, states, table, adjoint, text, out, rows_out, extra_out, sums_out):
    rows = [table[c, pl.ds(step[0], 1), :] for c in range(3)]
    widened = states[...].astype(jnp.float32)
    centered = widened - jnp.mean(widened, axis=-1, keepdims=True)
    inv_std = lax.rsqrt(jnp.mean(centered * centered, axis=-1, keepdims=True) + 1e-06)
    half, width = states.shape
    out[:, :width] = (centered * inv_std * (1.0 + rows[1]) + rows[0]).astype(jnp.bfloat16)
    for c in range(3):
        rows_out[c : c + 1, :] = rows[c]
    squares = jnp.sum(adjoint[...] * adjoint[...], axis=0, keepdims=True)
    squares = jnp.sum(squares, axis=1, keepdims=True)
    sums_out[...] = jnp.broadcast_to(squares, sums_out.shape)
    terms = []
    for n in range(3):
        terms.append(squares.astype(jnp.bfloat16).astype(jnp.float32))
        squares = squares - terms[-1]
    lane = lax.broadcasted_iota(jnp.int32, (8, EXTRA), 1)
    sums = jnp.where(lane == 0, terms[0], jnp.where(lane == 1, terms[1], jnp.where(lane == 2, terms[2], 0.0)))
    extra = extra_columns(text_columns(text, 0) + [sums], half)
    out[:, width:] = extra
    extra_out[...] = extra


def first_call(step, core, states, table, adjoint, text):
    rows, width = states.shape
    half = rows // 2
    whole = lambda *shape: pl.BlockSpec(shape, lambda i, step, core: (0,) * len(shape))
    return pl.pallas_call(
        first_kernel,
        out_shape=(
            jax.ShapeDtypeStruct((half, width + EXTRA), jnp.bfloat16),
            jax.ShapeDtypeStruct((8, width), jnp.float32),
            jax.ShapeDtypeStruct((half, EXTRA), jnp.bfloat16),
            jax.ShapeDtypeStruct((8, EXTRA), jnp.float32),
        ),
        grid_spec=pltpu.PrefetchScalarGridSpec(
            num_scalar_prefetch=2,
            grid=(1,),
            in_specs=[
                pl.BlockSpec((half, width), lambda i, step, core: (core[0], 0)),
                whole(*table.shape),
                whole(*adjoint.shape),
                whole(*text.shape),
            ],
            out_specs=(whole(half, width + EXTRA), whole(8, width), whole(half, EXTRA), whole(8, EXTRA)),
        ),
        compiler_params=pltpu.CompilerParams(vmem_limit_bytes=GRANT),
        cost_estimate=pl.CostEstimate(flops=8 * half * width, bytes_accessed=16 * half * width, transcendentals=0),
    )(step, core, states, table, adjoint, text)


def pick_half(core, rows):
    half = rows.shape[1] // 2
    return jnp.where(core == 0, rows[:, :half], rows[:, half:])


def cotangent_kernel(limit, core, adjoint, table_rows, text, extra, previous, following, opposite, out, clip_out):
    row = 8 * (text.shape[2] // EXTRA)
    squares = 0.0
    for terms in (extra, previous, following):
        squares = squares + terms[...].astype(jnp.float32)[row : row + 1, :]
    squares = jnp.sum(squares, axis=1, keepdims=True) + opposite[0:1, 0:1]
    clip_scale = jnp.minimum(1.0, limit / jnp.sqrt(squares + 1e-06))
    half, width = adjoint.shape
    out[:, :width] = (table_rows[2:3, :] * (clip_scale * adjoint[...])).astype(jnp.bfloat16)
    out[:, width:] = extra_columns(text_columns(text, 1), half)
    clip_out[...] = jnp.broadcast_to(clip_scale, clip_out.shape)


def cotangent_call(limit, core, adjoint, table_rows, text, extra, previous, following, opposite):
    rows, width = adjoint.shape
    half = rows // 2
    block = width // EXTRA
    whole = lambda one: pl.BlockSpec(one.shape, lambda i, core: (0,) * one.ndim)
    tail = lambda one: pl.BlockSpec((one.shape[0], EXTRA), lambda i, core: (0, block))
    outs = (
        jax.ShapeDtypeStruct((half, width + EXTRA), jnp.bfloat16),
        jax.ShapeDtypeStruct((8, EXTRA), jnp.float32),
    )
    return pl.pallas_call(
        functools.partial(cotangent_kernel, limit),
        out_shape=outs,
        grid_spec=pltpu.PrefetchScalarGridSpec(
            num_scalar_prefetch=1,
            grid=(1,),
            in_specs=[pl.BlockSpec((half, width), lambda i, core: (core[0], 0))]
            + [whole(table_rows), whole(text), whole(extra)]
            + [tail(one) for one in (previous, following)]
            + [whole(opposite)],
            out_specs=tuple(whole(one) for one in outs),
        ),
        compiler_params=pltpu.CompilerParams(vmem_limit_bytes=GRANT),
        cost_estimate=pl.CostEstimate(flops=4 * half * width, bytes_accessed=6 * half * width, transcendentals=0),
    )(core, adjoint, table_rows, text, extra, previous, following, opposite)


def own_kernel(
    core, states, adjoint, table_rows, text, extra, clip, out, cot_out, normed_out, stretch_out, inv_out, base_out
):
    rows, width = states.shape
    half = rows // 2
    widened = states[...].astype(jnp.float32)
    centered = widened - jnp.mean(widened, axis=-1, keepdims=True)
    inv_std = lax.rsqrt(jnp.mean(centered * centered, axis=-1, keepdims=True) + 1e-06)
    normed = centered * inv_std
    scale = 1.0 + table_rows[1:2, :]
    out[:, :width] = (normed * scale + table_rows[0:1, :]).astype(jnp.bfloat16)
    normed_out[...] = pick_half(core[0], normed)
    stretch_out[...] = pick_half(core[0], scale)
    inv_out[...] = jnp.broadcast_to(inv_std, inv_out.shape)
    clipped = clip[0:1, 0:1] * adjoint[...]
    cot_out[:, :width] = (table_rows[2:3, :] * clipped).astype(jnp.bfloat16)
    base_out[...] = pick_half(core[0], clipped)
    columns = extra_columns(text_columns(text, 1), half)
    for n in range(2):
        out[n * half : (n + 1) * half, width:] = extra[...]
        cot_out[n * half : (n + 1) * half, width:] = columns


class Copies:
    def __init__(self, sems):
        self.sems = sems
        self.count = 0

    def start(self, source, target):
        copy = pltpu.make_async_copy(source, target, self.sems.at[self.count])
        copy.start()
        self.count += 1
        return copy

    def weights(self, scalars, w_in, w_all, shard, first=0):
        columns = w_in[0].shape[1] - first
        return [
            self.start(
                piece.at[:, pl.ds(first, columns)],
                w_all.at[
                    pl.ds(pl.multiple_of(scalars[1 + n % 4] * shard, 16), shard),
                    pl.ds(n // 4 * columns, columns),
                ],
            )
            for n, piece in enumerate(w_in)
        ]

    def rows(self, core, pieces, target, rows):
        half = rows // 2
        copies = [self.start(pieces[0], target.at[pl.ds(0, rows)])]
        places = [(rows, half), (3 * rows, half)]
        parts = (len(pieces) - 5) // 2
        places += [(2 * rows + n * half // parts, half // parts) for n in range(parts)]
        for n, (first, size) in enumerate(places):
            for m, holder in enumerate((core, 1 - core)):
                there = pl.ds(pl.multiple_of(first + holder * half, 16), size)
                copies.append(self.start(pieces[1 + 2 * n + m], target.at[there]))
        return copies


def window_heads(scalars, count, rows, text_dev, gathered, width, extra, text, text_t=None):
    half = rows // 2
    for k in range(count):
        there = pl.ds(pl.multiple_of(k * rows + scalars[0] * half, 16), half)
        extra[k] = gathered[there, width:].astype(jnp.float32)
    for i in range(text.shape[0]):
        head = scalars[5] + i
        first = pl.ds(pl.multiple_of(head // 2 * text_dev, 8), text_dev)
        found = jnp.concatenate([extra[k, first, :] for k in range(count)], axis=0)
        found = jnp.where(head % 2 == 0, found[:, :HD], found[:, HD:])
        text[i] = found.astype(jnp.bfloat16)
        if text_t is not None:
            text_t[i] = found.T.astype(jnp.bfloat16)


def project_kernel(slots, count, rows, shard, width, text_dev, scalars, gain, *refs):
    refs = list(refs)
    take = lambda n: [refs.pop(0) for _ in range(n)]
    mod_in = take(9)
    w_in = take(8)
    qkv, k_t, raw_all, inv_all, text, text_t, w_keep, w_give = take(8)
    w_all, mod_all, sems, extra, qkv_s, k_t_s, raw_s, inv_s = take(8)
    inner = slots * HD
    core = scalars[0]
    copies = Copies(sems)
    w_copies = copies.weights(scalars, w_in, w_all, shard)
    row_copies = copies.rows(core, mod_in, mod_all, rows)

    lane = lax.broadcasted_iota(jnp.int32, (1, 2 * inner), 1)
    gains = head_gains(gain, slots) * jnp.where(lane < inner, HD ** (-0.5), 1.0)
    identity = equal_blocks(inner, 1)
    for copy in w_copies:
        copy.wait()
    half = width // 2
    columns = pl.ds(0, w_keep.shape[1])
    out_copies = []
    for holder, target in ((core, w_keep), (1 - core, w_give)):
        source = w_all.at[pl.ds(pl.multiple_of(holder * half, 16), half), columns]
        out_copies.append(copies.start(source, target))
    for copy in row_copies:
        copy.wait()
    projected = jnp.dot(mod_all[:, :width], w_all[:, : 3 * inner], preferred_element_type=jnp.float32)
    raw = projected[:, : 2 * inner]
    raw_s[...] = raw
    out_copies.append(copies.start(raw_s, raw_all))
    inverse = lax.rsqrt(head_means(raw * raw) + 1e-06)
    inv_s[...] = inverse
    out_copies.append(copies.start(inv_s, inv_all))
    qkv_s[:, : 2 * inner] = (raw * inverse * gains).astype(jnp.bfloat16)
    qkv_s[:, 2 * inner :] = projected[:, 2 * inner :].astype(jnp.bfloat16)
    out_copies.append(copies.start(qkv_s, qkv))
    k_t_s[...] = dot(identity, qkv_s[:, inner : 2 * inner], NT).astype(jnp.bfloat16)
    out_copies.append(copies.start(k_t_s, k_t))
    window_heads(scalars, count, rows, text_dev, mod_all, width, extra, text, text_t)
    for copy in out_copies:
        copy.wait()


def attend_kernel(slots, count, rows, shard, width, text_dev, first_column, scalars, gain, *refs):
    refs = list(refs)
    take = lambda n: [refs.pop(0) for _ in range(n)]
    projected = take(8)
    cot_in = take(7)
    w_in = take(4)
    mine_out, theirs_out, rest_out = take(3)
    w_out, cot_all, sems, extra, values_text = take(5)
    d_all, grads, stacked = take(3)
    qkv, k_t, raw_all, inv_all, text, text_t, w_keep, w_give = refs
    inner = slots * HD
    tokens = rows * count
    core = scalars[0]
    copies = Copies(sems)
    w_copies = copies.weights(scalars, w_in, w_out, shard, first_column)
    row_copies = copies.rows(core, cot_in, cot_all, rows)
    pairs = list(zip(projected, refs))
    local_copies = [copies.start(*pairs[n]) for n in (0, 1, 4, 5)]
    score_scale = HD ** (-0.5)
    span = 2 * rows

    text_rows = count * text_dev
    row = lax.broadcasted_iota(jnp.int32, (text_rows, span), 0)
    text_id = row
    for k in range(count):
        inside = (row >= k * text_dev) & (row < (k + 1) * text_dev)
        text_id = jnp.where(inside, row + (scalars[7 + k] - k) * text_dev, text_id)
    bias = jnp.where(text_id < scalars[6], 0.0, -1e30)

    for copy in w_copies:
        copy.wait()
    for copy in row_copies:
        copy.wait()
    out_grad = jnp.dot(cot_all[:, :width], w_out[...], preferred_element_type=jnp.float32)
    d_all[...] = out_grad.astype(jnp.bfloat16)
    window_heads(scalars, count, rows, text_dev, cot_all, width, extra, values_text)
    late_copies = [copies.start(*pairs[n]) for n in (2, 3, 6, 7)]
    for copy in local_copies:
        copy.wait()

    d_first = d_all.shape[1] - inner
    for i in range(slots):
        columns = [slice(n * inner + i * HD, n * inner + (i + 1) * HD) for n in range(3)]
        keys, values = qkv[:, columns[1]], qkv[:, columns[2]]
        keys_t = k_t[i * HD : (i + 1) * HD, :]
        grad_k, grad_v = 0.0, 0.0
        for b in range(count // 2):
            here = slice(b * span, (b + 1) * span)
            query = qkv[here, columns[0]]
            grad = d_all[here, d_first + i * HD : d_first + (i + 1) * HD]
            scores = dot(keys, query, NT)
            text_scores = dot(text[i], query, NT) + bias
            col_max = jnp.maximum(
                jnp.max(scores, axis=0, keepdims=True), jnp.max(text_scores, axis=0, keepdims=True)
            )
            exps = jnp.exp(scores - col_max)
            text_exps = jnp.exp(text_scores - col_max)
            total = jnp.sum(exps, axis=0, keepdims=True) + jnp.sum(text_exps, axis=0, keepdims=True)
            inverse = 1.0 / total
            grad_w = dot(values, grad, NT)
            text_grad_w = dot(values_text[i], grad, NT)
            delta = inverse * (
                jnp.sum(exps * grad_w, axis=0, keepdims=True)
                + jnp.sum(text_exps * text_grad_w, axis=0, keepdims=True)
            )
            weights = exps * inverse
            grad_s = (weights * (grad_w - delta)).astype(jnp.bfloat16)
            text_grad_s = (text_exps * inverse * (text_grad_w - delta)).astype(jnp.bfloat16)
            grad_k += dot(grad_s, query, NN)
            grad_v += dot(weights.astype(jnp.bfloat16), grad, NN)
            grad_q = dot(keys_t, grad_s, NN) + dot(text_t[i], text_grad_s, NN)
            grads[here, columns[0]] = grad_q.T * score_scale
        grads[:, columns[1]] = grad_k
        grads[:, columns[2]] = grad_v

    lane = lax.broadcasted_iota(jnp.int32, (1, inner), 1)
    mine = jnp.zeros((1, inner), jnp.float32)
    for i in range(slots):
        inside = (lane >= i * HD) & (lane < (i + 1) * HD) & (scalars[7 + count + i] > 0)
        mine = jnp.where(inside, 1.0, mine)
    gains = head_gains(gain, slots)
    for copy in late_copies[:2]:
        copy.wait()
    for b in range(count // 2):
        here = slice(b * span, (b + 1) * span)
        scaled = grads[here, : 2 * inner].astype(jnp.bfloat16).astype(jnp.float32) * gains
        raw, inverse = raw_all[here, :], inv_all[here, :]
        back = scaled * inverse - raw * head_means(scaled * raw) * (inverse * inverse * inverse)
        valid = jnp.concatenate([mine, mine], axis=1) > 0.0
        stacked[here, : 2 * inner] = jnp.where(valid, back, 0.0).astype(jnp.bfloat16)
        back = jnp.where(mine > 0.0, grads[here, 2 * inner :], 0.0).astype(jnp.bfloat16)
        stacked[here, 2 * inner : 3 * inner] = back
    stacked[:, 3 * inner :] = jnp.zeros((tokens, stacked.shape[1] - 3 * inner), jnp.bfloat16)
    first = stacked[rows : 2 * rows, :]
    rest_out[: (count - 2) * rows, :] = stacked[2 * rows :, :]
    rest_out[(count - 2) * rows :, :] = stacked[:rows, :]
    for copy in late_copies[2:]:
        copy.wait()
    theirs_out[...] = dot(first, w_give[...], NT).astype(jnp.bfloat16)
    mine_out[...] = dot(first, w_keep[...], NT)


def project_call(scalars, gain, mod, weights, slots, rows, text_dev, count):
    shard = weights[0].shape[0]
    columns = 4 * slots * HD
    width = mod[0].shape[1] - EXTRA
    tokens = rows * count
    text_rows = text_dev * count
    f32, bf16 = jnp.float32, jnp.bfloat16
    vmem, hbm = spec(pltpu.VMEM), spec(pl.ANY)
    inner = slots * HD
    shapes = [((tokens, 3 * inner), bf16), ((inner, tokens), bf16)] + [((tokens, 2 * inner), f32)] * 2
    shapes += [((slots, text_rows, HD), bf16), ((slots, HD, text_rows), bf16)]
    shapes += [((width // 2, whole_tiles(3 * slots * HD)), bf16)] * 2
    return pl.pallas_call(
        functools.partial(project_kernel, slots, count, rows, shard, width, text_dev),
        out_shape=tuple(jax.ShapeDtypeStruct(*one) for one in shapes),
        in_specs=[spec(pltpu.SMEM), vmem] + [hbm] * (len(mod) + len(weights)),
        out_specs=(hbm,) * 4 + (vmem,) * 2 + (hbm,) * 2,
        scratch_shapes=[
            pltpu.VMEM((width, columns), bf16),
            pltpu.VMEM((tokens, width + EXTRA), bf16),
            pltpu.SemaphoreType.DMA((len(mod) + len(weights) + 10,)),
            pltpu.VMEM((count, rows // 2, EXTRA), f32),
        ]
        + [pltpu.VMEM(*one) for one in shapes[:4]],
        compiler_params=pltpu.CompilerParams(vmem_limit_bytes=GRANT),
        cost_estimate=pl.CostEstimate(
            flops=2 * tokens * width * 3 * slots * HD,
            bytes_accessed=2 * (tokens * width + columns * width) + 4 * tokens * columns,
            transcendentals=0,
        ),
    )(scalars, gain, *mod, *weights)


def attend_call(scalars, gain, operands, cot, weights, slots, rows, text_dev):
    count = operands[0].shape[0] // rows
    shard, columns = weights[0].shape
    width = cot[0].shape[1] - EXTRA
    tokens = rows * count
    inner = slots * HD
    stacked = whole_tiles(3 * inner)
    first = (columns - inner) // 128 * 128
    f32, bf16 = jnp.float32, jnp.bfloat16
    vmem, hbm = spec(pltpu.VMEM), spec(pltpu.HBM)
    shapes = [((rows, width // 2), f32), ((rows, width // 2), bf16), ((tokens - rows, stacked), bf16)]
    return pl.pallas_call(
        functools.partial(attend_kernel, slots, count, rows, shard, width, text_dev, first),
        out_shape=tuple(jax.ShapeDtypeStruct(*one) for one in shapes),
        in_specs=[spec(pltpu.SMEM), vmem] + [hbm] * (len(operands) + len(cot) + len(weights)),
        out_specs=(vmem,) * len(shapes),
        scratch_shapes=[
            pltpu.VMEM((width, columns - first), bf16),
            pltpu.VMEM((tokens, width + EXTRA), bf16),
            pltpu.SemaphoreType.DMA((len(operands) + len(cot) + len(weights),)),
            pltpu.VMEM((count, rows // 2, EXTRA), f32),
            pltpu.VMEM((slots, text_dev * count, HD), bf16),
            pltpu.VMEM((tokens, columns - first), bf16),
            pltpu.VMEM((tokens, 3 * inner), f32),
            pltpu.VMEM((tokens, stacked), bf16),
        ]
        + [pltpu.VMEM(one.shape, one.dtype) for one in operands],
        compiler_params=pltpu.CompilerParams(vmem_limit_bytes=MAIN_GRANT),
        cost_estimate=pl.CostEstimate(
            flops=2 * tokens * width * inner + 10 * tokens * tokens * inner,
            bytes_accessed=2 * (tokens * width + columns * width),
            transcendentals=slots * tokens * tokens,
        ),
    )(scalars, gain, *operands, *cot, *weights)


def backward_kernel(own, other, w_own, w_other, *outs):
    total = dot(own[...], w_own[...], NT) + dot(other[...], w_other[...], NT)
    part = outs[0].shape[0]
    for n, out in enumerate(outs):
        out[...] = total[n * part : (n + 1) * part].astype(out.dtype)


def backward_call(own, other, w_own, w_other, part, dtype):
    rows, inner = own.shape
    half = w_own.shape[0]
    vmem = spec(pltpu.VMEM)
    return pl.pallas_call(
        backward_kernel,
        out_shape=(jax.ShapeDtypeStruct((part, half), dtype),) * (rows // part),
        in_specs=[vmem] * 4,
        out_specs=(vmem,) * (rows // part),
        compiler_params=pltpu.CompilerParams(vmem_limit_bytes=SMALL_GRANT),
        cost_estimate=pl.CostEstimate(
            flops=4 * rows * half * inner,
            bytes_accessed=4 * (rows + half) * inner + 4 * rows * half,
            transcendentals=0,
        ),
    )(own, other, w_own, w_other)


def sums_kernel(own_near, own_far, near, far, scale, normed, grad_out, sums_out):
    half = near.shape[0]
    for part, (own, moving) in enumerate(((own_near, near), (own_far, far))):
        here = slice(part * half, (part + 1) * half)
        grad = (own[...] + moving[...].astype(jnp.float32)) * scale[...]
        grad_out[here, :] = grad
        first = jnp.sum(grad, axis=-1, keepdims=True)
        second = jnp.sum(grad * normed[here, :], axis=-1, keepdims=True)
        lane = lax.broadcasted_iota(jnp.int32, (half, 128), 1)
        sums_out[here, :] = jnp.where(lane == 0, first, second)


def last_kernel(width, grad, sums, other, normed, base, inv_std, out):
    total = (sums[...] + other[...]) * (1.0 / width)
    rows = base[...] + inv_std[:, 0:1] * (
        grad[...] - total[:, 0:1] - normed[...] * total[:, 1:2]
    )
    out[...] = rows.T


def local_call(kernel, shapes, scalar_count, *operands, grant=SMALL_GRANT):
    vmem = spec(pltpu.VMEM)
    return pl.pallas_call(
        kernel,
        out_shape=tuple(jax.ShapeDtypeStruct(*one) for one in shapes),
        in_specs=[spec(pltpu.SMEM)] * scalar_count + [vmem] * (len(operands) - scalar_count),
        out_specs=(vmem,) * len(shapes),
        compiler_params=pltpu.CompilerParams(vmem_limit_bytes=grant),
        cost_estimate=pl.CostEstimate(
            flops=sum(one.size for one in operands),
            bytes_accessed=sum(one.size * one.dtype.itemsize for one in operands),
            transcendentals=0,
        ),
    )(*operands)


def shards_by_head(states, adjoint, text_kv, text_len, step_index, modulation, w_qkv, qk_gain, w_out):
    hidden_state = states[0]
    adjoint_rows = adjoint[0]
    tok_count, model_width = hidden_state.shape
    seq_count = lax.axis_size("seq")
    inner_dev = w_qkv.shape[2]
    heads_dev = inner_dev // HD
    shard = w_qkv.shape[0]
    slots = -(-heads_dev // seq_count)
    inner = slots * HD
    half_rows = tok_count // 2
    half_width = model_width // 2
    f32, bf16 = jnp.float32, jnp.bfloat16
    core = lax.axis_index("head").astype(jnp.int32)
    seq_index = lax.axis_index("seq")
    dp_index = lax.axis_index("dp")
    pin = lax.optimization_barrier

    seq_order = line_ring(seq_count)
    seq_place = ring_place(seq_order, seq_index)
    seq_next = ring_pairs(seq_order)
    swap = [(0, 1), (1, 0)]
    first_way = [(2 * p + c, 2 * (p ^ (1 + c)) + c) for p in range(4) for c in range(2)]
    second_way = [(2 * p + c, 2 * (p ^ (2 - c)) + c) for p in range(4) for c in range(2)]

    first = seq_index * heads_dev // seq_count
    stop = (seq_index + 1) * heads_dev // seq_count
    window = jnp.minimum(first, heads_dev - slots)
    valid = [(window + i >= first) & (window + i < stop) for i in range(slots)]
    owners = [ring_member(seq_order, (seq_place - k + seq_count) % seq_count) for k in range(seq_count)]
    w_index = [dp_index, dp_index ^ (1 + core), dp_index ^ (2 - core), dp_index ^ 3]
    scalars = [core] + w_index + [window, text_len[0]] + owners + valid
    scalars = jnp.stack([one.astype(jnp.int32) for one in scalars])

    def step(moving):
        return lax.ppermute(moving, "seq", seq_next)

    def other_core(moving):
        return lax.ppermute(moving, "head", swap)

    def step_back(moving):
        return lax.ppermute(moving, "seq", [(b, a) for a, b in seq_next])

    quarter = half_rows // 2

    def spread(moving):
        return [step(moving), step_back(moving)]

    def pass_on(received):
        return [step(received[0][:quarter]), step_back(received[1][quarter:])]

    mod_half, table_rows, extra, sums = first_call(
        step_index, core[None], hidden_state, modulation.transpose(1, 0, 2), adjoint_rows, text_kv[0]
    )
    across = [(seq_order[i], seq_order[(i + 2) % 4]) for i in range(4)]
    mod_half, sums = pin((mod_half, lax.ppermute(sums, "seq", across)))
    mod_near = spread(mod_half)

    w_qkv, w_out, mod_half = pin((w_qkv, w_out, mod_half))
    take = lambda c: lax.dynamic_slice(w_qkv, (0, c, window * HD), (shard, 1, inner))[:, 0]
    own_w = [
        jnp.concatenate([take(0), take(1)], axis=1),
        jnp.concatenate([take(2), lax.dynamic_slice_in_dim(w_out, window * HD, inner, 0).T], axis=1),
    ]
    w_first = [lax.ppermute(part, ("dp", "head"), first_way) for part in own_w]
    w_second = [lax.ppermute(part, ("dp", "head"), second_way) for part in own_w]

    text_dev = text_kv.shape[1]
    mod_far = pass_on(mod_near)
    clip_limit = 0.5 * (tok_count * seq_count * model_width) ** 0.5
    extra, *w_first = pin((extra, *w_first))
    cot_half, clip = cotangent_call(
        clip_limit, scalars, adjoint_rows, table_rows, text_kv[0], extra, *mod_near, sums
    )
    cot_half, mod_far[0] = pin((cot_half, mod_far[0]))
    cot_near = spread(cot_half)
    modulated, cotangent, normed_share, scale_share, inv_std, base = local_call(
        own_kernel,
        [((tok_count, model_width + EXTRA), bf16)] * 2
        + [
            ((tok_count, half_width), f32),
            ((1, half_width), f32),
            ((tok_count, 128), f32),
            ((tok_count, half_width), f32),
        ],
        1,
        core[None],
        hidden_state,
        adjoint_rows,
        table_rows,
        text_kv[0],
        extra,
        clip,
        grant=GRANT,
    )
    def pieces(own, received):
        return [own] + [one for moved in received for one in (moved, other_core(moved))]

    mod_far = list(pin((*mod_far, modulated))[:2])
    mod_pieces = pieces(modulated, mod_near + mod_far)
    w_diagonal = [lax.ppermute(part, ("dp", "head"), second_way) for part in w_first]
    weights = [part[n] for n in range(2) for part in (own_w, w_first, w_second, w_diagonal)]
    cot_near[0] = pin((cot_near[0], w_second, w_diagonal))[0]
    cot_far = [step(cot_near[0])]

    cot_pieces = pieces(cotangent, cot_near)
    *cot_pieces, mod_pieces[-1] = pin((*cot_pieces, mod_pieces[-1]))
    *operands, w_keep, w_give = project_call(
        scalars, qk_gain, mod_pieces, weights, slots, tok_count, text_dev, seq_count
    )
    w_give, cot_far[0] = pin((w_give, *cot_far))
    cot_pieces += pieces(None, cot_far)[1:]
    given, *cot_pieces = pin((w_give, *cot_pieces))
    w_other = other_core(given)
    mine, theirs, rest = attend_call(
        scalars, qk_gain, operands + [w_keep, w_give], cot_pieces, weights[4:], slots, tok_count, text_dev
    )
    first = (mine + other_core(theirs).astype(f32)).astype(bf16)
    moving = [first[:half_rows], first[half_rows:]]
    other_rest = other_core(rest)
    rest, other_rest, *_ = pin((rest, other_rest, *moving))
    own = backward_call(rest, other_rest, w_keep, w_other, half_rows, f32)
    for j in range(2, seq_count):
        moving = [step(part) for part in moving]
        moving = [
            (a + b.astype(f32)).astype(bf16) for a, b in zip(own[2 * (j - 2) : 2 * (j - 1)], moving)
        ]
    moving = [step(part) for part in moving]

    grad_scaled, sums = local_call(
        sums_kernel,
        [((tok_count, half_width), f32), ((tok_count, 128), f32)],
        0,
        *own[-2:],
        *moving,
        scale_share,
        normed_share,
    )
    (pulled,) = local_call(
        functools.partial(last_kernel, model_width),
        [((half_width, tok_count), f32)],
        0,
        grad_scaled,
        sums,
        other_core(sums),
        normed_share,
        base,
        inv_std,
    )
    return pulled.T[None]


def qk_normalize(values, gains):
    inverse = lax.rsqrt(jnp.mean(values * values, axis=-1, keepdims=True) + 1e-06)
    return ((values * inverse * gains).astype(jnp.bfloat16), inverse)


def qk_backward(values, inverse, cotangent, gains):
    scaled = cotangent.astype(jnp.float32) * gains
    return (
        scaled * inverse - values * jnp.mean(scaled * values, axis=-1, keepdims=True) * inverse**3
    )


def shards_by_row(states, adjoint, text_kv, text_len, step_index, modulation, w_qkv, qk_gain, w_out):
    hidden_state = states[0]
    adjoint_rows = adjoint[0]
    tok_count, model_width = hidden_state.shape
    seq_count = lax.axis_size("seq")
    inner_dev = w_qkv.shape[2]
    heads_dev = inner_dev // HD
    score_scale = HD ** (-0.5)
    squares = lax.psum(jnp.sum(adjoint_rows * adjoint_rows), "seq")
    clip_limit = 0.5 * (tok_count * seq_count * model_width) ** 0.5
    clip_scale = jnp.minimum(1.0, clip_limit / jnp.sqrt(squares + 1e-06))
    table_row = lax.dynamic_index_in_dim(modulation, step_index[0], 0, keepdims=False)
    offset_row = table_row[0]
    stretch = table_row[1]
    gating = table_row[2]
    widened = hidden_state.astype(jnp.float32)
    centered = widened - jnp.mean(widened, axis=-1, keepdims=True)
    inv_std = lax.rsqrt(jnp.mean(centered * centered, axis=-1, keepdims=True) + 1e-06)
    normed = centered * inv_std
    modulated = (normed * (1.0 + stretch) + offset_row).astype(jnp.bfloat16)
    cotangent = (gating * (clip_scale * adjoint_rows)).astype(jnp.bfloat16)
    contract_last = (((1,), (1,)), ((), ()))
    full_weight = lax.all_gather(w_qkv, "dp", axis=0, tiled=True).reshape(
        model_width, 3 * inner_dev
    )
    projected = jnp.dot(modulated, full_weight, preferred_element_type=jnp.float32)
    out_raw = lax.dot_general(
        cotangent,
        lax.all_gather(w_out, "dp", axis=1, tiled=True),
        contract_last,
        preferred_element_type=jnp.float32,
    )
    projected = projected.reshape(tok_count, 3, heads_dev, HD)
    queries, query_inv = qk_normalize(projected[:, 0], qk_gain[0])
    own_keys, key_inv = qk_normalize(projected[:, 1], qk_gain[1])
    own_values = projected[:, 2].astype(jnp.bfloat16)
    out_grad = out_raw.astype(jnp.bfloat16).reshape(tok_count, heads_dev, HD)
    text_keys = text_kv[0, :, 0, :]
    text_values = text_kv[0, :, 1, :]
    text_dev = text_keys.shape[0]
    rows_dev = tok_count + text_dev
    key_local = jnp.concatenate([own_keys.reshape(tok_count, inner_dev), text_keys], axis=0)
    value_local = jnp.concatenate([own_values.reshape(tok_count, inner_dev), text_values], axis=0)
    key_all, value_all = (
        lax.all_gather(key_local, "seq", axis=0, tiled=True),
        lax.all_gather(value_local, "seq", axis=0, tiled=True),
    )
    all_rows = rows_dev * seq_count
    row_ids = jnp.arange(all_rows, dtype=jnp.int32)
    owner = row_ids // rows_dev
    within = row_ids % rows_dev
    allowed = (within < tok_count) | (owner * text_dev + within - tok_count < text_len[0])
    group = 1
    while group * 2 * rows_dev <= 512 and seq_count % (group * 2) == 0:
        group = group * 2
    block_rows = group * rows_dev
    block_count = all_rows // block_rows
    key_blocks = key_all.reshape(block_count, block_rows, heads_dev, HD)
    value_blocks = value_all.reshape(block_count, block_rows, heads_dev, HD)
    mask_blocks = allowed.reshape(block_count, block_rows)

    def block_scores(key_block, mask_block):
        scores = (
            jnp.einsum("qhd,khd->qhk", queries, key_block, preferred_element_type=jnp.float32)
            * score_scale
        )
        return jnp.where(mask_block[None, None, :], scores, -1e30)

    def first_pass(carry, block):
        row_max, row_sum, row_dot = carry
        key_block, value_block, mask_block = block
        scores = block_scores(key_block, mask_block)
        new_max = jnp.maximum(row_max, jnp.max(scores, axis=-1))
        rescale = jnp.exp(row_max - new_max)
        exps = jnp.exp(scores - new_max[:, :, None])
        grad_weights = jnp.einsum(
            "qhd,khd->qhk", out_grad, value_block, preferred_element_type=jnp.float32
        )
        return (
            (
                new_max,
                row_sum * rescale + jnp.sum(exps, axis=-1),
                row_dot * rescale + jnp.sum(exps * grad_weights, axis=-1),
            ),
            None,
        )

    start_state = (
        jnp.full((tok_count, heads_dev), -1e30, jnp.float32),
        jnp.zeros((tok_count, heads_dev), jnp.float32),
        jnp.zeros((tok_count, heads_dev), jnp.float32),
    )
    (row_max, row_sum, row_dot), unused = lax.scan(
        first_pass, start_state, (key_blocks, value_blocks, mask_blocks)
    )
    log_total = row_max + jnp.log(row_sum)
    delta_row = row_dot / row_sum

    def second_pass(running, block):
        key_block, value_block, mask_block = block
        weights = jnp.exp(block_scores(key_block, mask_block) - log_total[:, :, None])
        grad_weights = jnp.einsum(
            "qhd,khd->qhk", out_grad, value_block, preferred_element_type=jnp.float32
        )
        grad_scores = (weights * (grad_weights - delta_row[:, :, None])).astype(jnp.bfloat16)
        return (
            running
            + jnp.einsum(
                "qhk,khd->qhd", grad_scores, key_block, preferred_element_type=jnp.float32
            ),
            None,
        )

    query_sum, unused = lax.scan(
        second_pass,
        jnp.zeros((tok_count, heads_dev, HD), jnp.float32),
        (key_blocks, value_blocks, mask_blocks),
    )
    grad_query = (query_sum * score_scale).astype(jnp.bfloat16)
    log_all, delta_all = (
        lax.all_gather(log_total, "seq", axis=0, tiled=True),
        lax.all_gather(delta_row, "seq", axis=0, tiled=True),
    )
    local_ids = jnp.arange(rows_dev, dtype=jnp.int32)
    local_allowed = (local_ids < tok_count) | (
        lax.axis_index("seq") * text_dev + local_ids - tok_count < text_len[0]
    )
    key_three = key_local.reshape(rows_dev, heads_dev, HD)
    value_three = value_local.reshape(rows_dev, heads_dev, HD)
    query_piece = lax.all_gather(queries.reshape(tok_count, inner_dev), "seq", axis=0, tiled=True)
    grad_piece = lax.all_gather(out_grad.reshape(tok_count, inner_dev), "seq", axis=0, tiled=True)
    piece_rows = query_piece.shape[0]
    query_rows = query_piece.reshape(piece_rows, heads_dev, HD)
    grad_rows = grad_piece.reshape(piece_rows, heads_dev, HD)
    scores = (
        jnp.einsum("qhd,khd->qhk", query_rows, key_three, preferred_element_type=jnp.float32)
        * score_scale
    )
    scores = jnp.where(local_allowed[None, None, :], scores, -1e30)
    weights = jnp.exp(scores - log_all[:, :, None])
    grad_weights = jnp.einsum(
        "qhd,khd->qhk", grad_rows, value_three, preferred_element_type=jnp.float32
    )
    grad_scores = (weights * (grad_weights - delta_all[:, :, None])).astype(jnp.bfloat16)
    rounded = weights.astype(jnp.bfloat16)
    key_sum = jnp.einsum(
        "qhk,qhd->khd", grad_scores, query_rows, preferred_element_type=jnp.float32
    )
    value_sum = jnp.einsum("qhk,qhd->khd", rounded, grad_rows, preferred_element_type=jnp.float32)
    key_sum, value_sum = (key_sum, value_sum)
    grad_key = (key_sum[:tok_count] * score_scale).astype(jnp.bfloat16)
    grad_value = value_sum[:tok_count].astype(jnp.bfloat16)
    raw_query = qk_backward(projected[:, 0], query_inv, grad_query, qk_gain[0])
    raw_key = qk_backward(projected[:, 1], key_inv, grad_key, qk_gain[1])
    stacked = jnp.stack([raw_query, raw_key, grad_value.astype(jnp.float32)], axis=1).astype(
        jnp.bfloat16
    )
    stacked = stacked.reshape(tok_count, 3 * inner_dev)
    partial_grad = lax.dot_general(
        stacked, full_weight, contract_last, preferred_element_type=jnp.float32
    )
    half_width = model_width // lax.axis_size("head")
    first_col = lax.axis_index("head") * half_width
    grad_share = lax.psum_scatter(
        partial_grad.astype(jnp.bfloat16), "head", scatter_dimension=1, tiled=True
    ).astype(jnp.float32)
    normed_share = lax.dynamic_slice_in_dim(normed, first_col, half_width, 1)
    stretch_share = lax.dynamic_slice_in_dim(stretch, first_col, half_width, 0)
    adjoint_share = lax.dynamic_slice_in_dim(adjoint_rows, first_col, half_width, 1)
    grad_scaled = grad_share * (1.0 + stretch_share)
    row_sums = jnp.stack(
        [jnp.sum(grad_scaled, axis=-1), jnp.sum(grad_scaled * normed_share, axis=-1)], axis=-1
    )
    row_sums = lax.psum(row_sums, "head")
    grad_state = inv_std * (
        grad_scaled - row_sums[:, 0:1] / model_width - normed_share * row_sums[:, 1:2] / model_width
    )
    pulled = clip_scale * adjoint_share + grad_state
    return pulled[None]


def solution(mesh):
    in_specs = (
        P("dp", "seq", None),
        P("dp", "seq", None),
        P("dp", "seq", None, "head"),
        P("dp"),
        P("dp"),
        P(),
        P("dp", None, "head"),
        P(),
        P("head", "dp"),
    )
    out_specs = P("dp", "seq", "head")
    by_head = mesh.shape["seq"] == 4 and mesh.shape["dp"] == 4 and mesh.shape["head"] == 2
    shards = shards_by_head if by_head else shards_by_row
    return jax.shard_map(shards, mesh=mesh, in_specs=in_specs, out_specs=out_specs, check_vma=False)
```

```python
import functools

import jax
import jax.numpy as jnp
from jax import lax
from jax.experimental import pallas as pl
from jax.experimental.pallas import tpu as pltpu
from jax.sharding import PartitionSpec as P

HD = 64
GRANT = 60 * 1024 * 1024
SMALL_GRANT = 24 * 1024 * 1024
EXTRA = 128
NT = (((1,), (1,)), ((), ()))
NN = (((1,), (0,)), ((), ()))


def line_ring(count):
    return [0] + list(range(1, count, 2)) + [i for i in range(count - 1, 0, -1) if i % 2 == 0]


def ring_pairs(order):
    return [(order[i], order[(i + 1) % len(order)]) for i in range(len(order))]


def ring_place(order, index):
    place = jnp.int32(0)
    for position, member in enumerate(order):
        place = jnp.where(index == member, jnp.int32(position), place)
    return place


def ring_member(order, place):
    member = jnp.int32(order[0])
    for position, value in enumerate(order):
        member = jnp.where(place == position, jnp.int32(value), member)
    return member


def dot(a, b, dims):
    return lax.dot_general(a, b, dims, preferred_element_type=jnp.float32)


def equal_blocks(columns, block):
    row = lax.broadcasted_iota(jnp.int32, (columns, columns), 0)
    column = lax.broadcasted_iota(jnp.int32, (columns, columns), 1)
    return jnp.where(row // block == column // block, 1.0, 0.0).astype(jnp.bfloat16)


def head_means(values):
    parts = []
    for first in range(0, values.shape[1], 256):
        part = values[:, first : first + 256]
        ones = equal_blocks(part.shape[1], HD)
        high = part.astype(jnp.bfloat16)
        low = (part - high.astype(jnp.float32)).astype(jnp.bfloat16)
        parts.append(dot(high, ones, NN) + dot(low, ones, NN))
    return jnp.concatenate(parts, axis=1) * (1.0 / HD)


def head_gains(gain, slots):
    return jnp.concatenate([gain[0:1, :]] * slots + [gain[1:2, :]] * slots, axis=1)


def whole_tiles(columns):
    return -(-columns // 128) * 128


def spec(space):
    return pl.BlockSpec(memory_space=space)


def text_columns(text, part):
    rows = text[...].astype(jnp.float32)[:, part, :]
    return [rows[:, c * EXTRA : (c + 1) * EXTRA] for c in range(rows.shape[1] // EXTRA)]


def extra_columns(blocks, rows):
    filled = sum(one.shape[0] for one in blocks)
    blocks = blocks + [jnp.zeros((rows - filled, EXTRA), jnp.float32)]
    return jnp.concatenate(blocks, axis=0).astype(jnp.bfloat16)


def first_kernel(step, core, states, table, adjoint, text, out, rows_out, extra_out):
    rows = [table[c, pl.ds(step[0], 1), :] for c in range(3)]
    widened = states[...].astype(jnp.float32)
    centered = widened - jnp.mean(widened, axis=-1, keepdims=True)
    inv_std = lax.rsqrt(jnp.mean(centered * centered, axis=-1, keepdims=True) + 1e-06)
    half, width = states.shape
    out[:, :width] = (centered * inv_std * (1.0 + rows[1]) + rows[0]).astype(jnp.bfloat16)
    for c in range(3):
        rows_out[c : c + 1, :] = rows[c]
    squares = jnp.sum(adjoint[...] * adjoint[...], axis=0, keepdims=True)
    squares = jnp.sum(squares, axis=1, keepdims=True)
    terms = []
    for n in range(3):
        terms.append(squares.astype(jnp.bfloat16).astype(jnp.float32))
        squares = squares - terms[-1]
    lane = lax.broadcasted_iota(jnp.int32, (8, EXTRA), 1)
    sums = jnp.where(lane == 0, terms[0], jnp.where(lane == 1, terms[1], jnp.where(lane == 2, terms[2], 0.0)))
    extra = extra_columns(text_columns(text, 0) + [sums], half)
    out[:, width:] = extra
    extra_out[...] = extra


def first_call(step, core, states, table, adjoint, text):
    rows, width = states.shape
    half = rows // 2
    whole = lambda *shape: pl.BlockSpec(shape, lambda i, step, core: (0,) * len(shape))
    return pl.pallas_call(
        first_kernel,
        out_shape=(
            jax.ShapeDtypeStruct((half, width + EXTRA), jnp.bfloat16),
            jax.ShapeDtypeStruct((8, width), jnp.float32),
            jax.ShapeDtypeStruct((half, EXTRA), jnp.bfloat16),
        ),
        grid_spec=pltpu.PrefetchScalarGridSpec(
            num_scalar_prefetch=2,
            grid=(1,),
            in_specs=[
                pl.BlockSpec((half, width), lambda i, step, core: (core[0], 0)),
                whole(*table.shape),
                whole(*adjoint.shape),
                whole(*text.shape),
            ],
            out_specs=(whole(half, width + EXTRA), whole(8, width), whole(half, EXTRA)),
        ),
        compiler_params=pltpu.CompilerParams(vmem_limit_bytes=GRANT),
        cost_estimate=pl.CostEstimate(flops=8 * half * width, bytes_accessed=16 * half * width, transcendentals=0),
    )(step, core, states, table, adjoint, text)


def pick_half(core, rows):
    half = rows.shape[1] // 2
    return jnp.where(core == 0, rows[:, :half], rows[:, half:])


def cotangent_kernel(limit, core, adjoint, table_rows, text, extra, previous, following, opposite, out, clip_out):
    first = previous.shape[0] - opposite.shape[0]
    row = 8 * (text.shape[2] // EXTRA)
    squares = opposite[...].astype(jnp.float32)[row - first : row - first + 1, :]
    for terms in (extra, previous, following):
        squares = squares + terms[...].astype(jnp.float32)[row : row + 1, :]
    squares = jnp.sum(squares, axis=1, keepdims=True)
    clip_scale = jnp.minimum(1.0, limit / jnp.sqrt(squares + 1e-06))
    half, width = adjoint.shape
    out[:, :width] = (table_rows[2:3, :] * (clip_scale * adjoint[...])).astype(jnp.bfloat16)
    out[:, width:] = extra_columns(text_columns(text, 1), half)
    clip_out[...] = jnp.broadcast_to(clip_scale, clip_out.shape)


def cotangent_call(limit, core, adjoint, table_rows, text, extra, previous, following, opposite):
    rows, width = adjoint.shape
    half = rows // 2
    block = width // EXTRA
    whole = lambda one: pl.BlockSpec(one.shape, lambda i, core: (0,) * one.ndim)
    tail = lambda one: pl.BlockSpec((one.shape[0], EXTRA), lambda i, core: (0, block))
    outs = (
        jax.ShapeDtypeStruct((half, width + EXTRA), jnp.bfloat16),
        jax.ShapeDtypeStruct((8, EXTRA), jnp.float32),
    )
    return pl.pallas_call(
        functools.partial(cotangent_kernel, limit),
        out_shape=outs,
        grid_spec=pltpu.PrefetchScalarGridSpec(
            num_scalar_prefetch=1,
            grid=(1,),
            in_specs=[pl.BlockSpec((half, width), lambda i, core: (core[0], 0))]
            + [whole(table_rows), whole(text), whole(extra)]
            + [tail(one) for one in (previous, following, opposite)],
            out_specs=tuple(whole(one) for one in outs),
        ),
        compiler_params=pltpu.CompilerParams(vmem_limit_bytes=GRANT),
        cost_estimate=pl.CostEstimate(flops=4 * half * width, bytes_accessed=6 * half * width, transcendentals=0),
    )(core, adjoint, table_rows, text, extra, previous, following, opposite)


def own_kernel(
    core, states, adjoint, table_rows, text, extra, clip, out, cot_out, normed_out, stretch_out, inv_out, base_out
):
    rows, width = states.shape
    half = rows // 2
    widened = states[...].astype(jnp.float32)
    centered = widened - jnp.mean(widened, axis=-1, keepdims=True)
    inv_std = lax.rsqrt(jnp.mean(centered * centered, axis=-1, keepdims=True) + 1e-06)
    normed = centered * inv_std
    scale = 1.0 + table_rows[1:2, :]
    out[:, :width] = (normed * scale + table_rows[0:1, :]).astype(jnp.bfloat16)
    normed_out[...] = pick_half(core[0], normed)
    stretch_out[...] = pick_half(core[0], scale)
    inv_out[...] = jnp.broadcast_to(inv_std, inv_out.shape)
    clipped = clip[0:1, 0:1] * adjoint[...]
    cot_out[:, :width] = (table_rows[2:3, :] * clipped).astype(jnp.bfloat16)
    base_out[...] = pick_half(core[0], clipped)
    columns = extra_columns(text_columns(text, 1), half)
    for n in range(2):
        out[n * half : (n + 1) * half, width:] = extra[...]
        cot_out[n * half : (n + 1) * half, width:] = columns


class Copies:
    def __init__(self, sems):
        self.sems = sems
        self.count = 0

    def start(self, source, target):
        copy = pltpu.make_async_copy(source, target, self.sems.at[self.count])
        copy.start()
        self.count += 1
        return copy

    def weights(self, scalars, w_in, w_all, shard, first=0):
        part = w_in[0].shape[1]
        copies = []
        for n, piece in enumerate(w_in):
            there = n // 4 * (part - first)
            columns = min(part - first, w_all.shape[1] - there)
            copies.append(
                self.start(
                    piece.at[:, pl.ds(first, columns)],
                    w_all.at[
                        pl.ds(pl.multiple_of(scalars[1 + n % 4] * shard, 16), shard),
                        pl.ds(there, columns),
                    ],
                )
            )
        return copies

    def rows(self, core, pieces, target, rows):
        half = rows // 2
        copies = [self.start(pieces[0], target.at[pl.ds(0, rows)])]
        places = [(rows, half), (3 * rows, half)]
        parts = (len(pieces) - 5) // 2
        places += [(2 * rows + n * half // parts, half // parts) for n in range(parts)]
        for n, (first, size) in enumerate(places):
            for m, holder in enumerate((core, 1 - core)):
                there = pl.ds(pl.multiple_of(first + holder * half, 16), size)
                copies.append(self.start(pieces[1 + 2 * n + m], target.at[there]))
        return copies


def window_heads(scalars, count, rows, text_dev, gathered, width, extra, text, text_t=None):
    half = rows // 2
    for k in range(count):
        there = pl.ds(pl.multiple_of(k * rows + scalars[0] * half, 16), half)
        extra[k] = gathered[there, width:].astype(jnp.float32)
    for i in range(text.shape[0]):
        head = scalars[5] + i
        first = pl.ds(pl.multiple_of(head // 2 * text_dev, 8), text_dev)
        found = jnp.concatenate([extra[k, first, :] for k in range(count)], axis=0)
        found = jnp.where(head % 2 == 0, found[:, :HD], found[:, HD:])
        text[i] = found.astype(jnp.bfloat16)
        if text_t is not None:
            text_t[i] = found.T.astype(jnp.bfloat16)


def project_kernel(slots, count, rows, shard, width, text_dev, scalars, gain, *refs):
    refs = list(refs)
    take = lambda n: [refs.pop(0) for _ in range(n)]
    mod_in = take(9)
    w_in = take(8)
    qkv, k_t, raw_all, inv_all, text, text_t, w_keep, w_give = take(8)
    w_all, mod_all, sems, extra, qkv_s, k_t_s, raw_s, inv_s = take(8)
    inner = slots * HD
    core = scalars[0]
    copies = Copies(sems)
    w_copies = copies.weights(scalars, w_in, w_all, shard)
    row_copies = copies.rows(core, mod_in, mod_all, rows)

    lane = lax.broadcasted_iota(jnp.int32, (1, 2 * inner), 1)
    gains = head_gains(gain, slots) * jnp.where(lane < inner, HD ** (-0.5), 1.0)
    identity = equal_blocks(inner, 1)
    for copy in w_copies:
        copy.wait()
    half = width // 2
    out_copies = []
    for holder, target in ((core, w_keep), (1 - core, w_give)):
        source = w_all.at[pl.ds(pl.multiple_of(holder * half, 16), half)]
        out_copies.append(copies.start(source, target))
    for copy in row_copies:
        copy.wait()
    projected = jnp.dot(mod_all[:, :width], w_all[:, : 3 * inner], preferred_element_type=jnp.float32)
    raw = projected[:, : 2 * inner]
    raw_s[...] = raw
    out_copies.append(copies.start(raw_s, raw_all))
    inverse = lax.rsqrt(head_means(raw * raw) + 1e-06)
    inv_s[...] = inverse
    out_copies.append(copies.start(inv_s, inv_all))
    qkv_s[:, : 2 * inner] = (raw * inverse * gains).astype(jnp.bfloat16)
    qkv_s[:, 2 * inner :] = projected[:, 2 * inner :].astype(jnp.bfloat16)
    out_copies.append(copies.start(qkv_s, qkv))
    k_t_s[...] = dot(identity, qkv_s[:, inner : 2 * inner], NT).astype(jnp.bfloat16)
    out_copies.append(copies.start(k_t_s, k_t))
    window_heads(scalars, count, rows, text_dev, mod_all, width, extra, text, text_t)
    for copy in out_copies:
        copy.wait()


def attend_kernel(slots, count, rows, shard, width, text_dev, first_column, scalars, gain, *refs):
    refs = list(refs)
    take = lambda n: [refs.pop(0) for _ in range(n)]
    projected = take(8)
    cot_in = take(7)
    w_in = take(4)
    mine_out, theirs_out, rest_out = take(3)
    w_out, cot_all, sems, extra, values_text = take(5)
    d_all, grads, stacked = take(3)
    qkv, k_t, raw_all, inv_all, text, text_t, w_keep, w_give = refs
    inner = slots * HD
    tokens = rows * count
    core = scalars[0]
    copies = Copies(sems)
    w_copies = copies.weights(scalars, w_in, w_out, shard, first_column)
    row_copies = copies.rows(core, cot_in, cot_all, rows)
    local_copies = [copies.start(*one) for one in zip(projected, refs)]
    score_scale = HD ** (-0.5)
    span = 2 * rows

    text_rows = count * text_dev
    row = lax.broadcasted_iota(jnp.int32, (text_rows, span), 0)
    text_id = row
    for k in range(count):
        inside = (row >= k * text_dev) & (row < (k + 1) * text_dev)
        text_id = jnp.where(inside, row + (scalars[7 + k] - k) * text_dev, text_id)
    bias = jnp.where(text_id < scalars[6], 0.0, -1e30)

    for copy in w_copies:
        copy.wait()
    arrivals = [row_copies[:3], row_copies[3:]]
    for b in range(count // 2):
        for copy in arrivals[b]:
            copy.wait()
        here = slice(b * span, (b + 1) * span)
        out_grad = jnp.dot(cot_all[here, :width], w_out[...], preferred_element_type=jnp.float32)
        d_all[here, :] = out_grad.astype(jnp.bfloat16)
    window_heads(scalars, count, rows, text_dev, cot_all, width, extra, values_text)
    for copy in local_copies[:6]:
        copy.wait()

    d_first = d_all.shape[1] - inner
    for i in range(slots):
        columns = [slice(n * inner + i * HD, n * inner + (i + 1) * HD) for n in range(3)]
        keys, values = qkv[:, columns[1]], qkv[:, columns[2]]
        keys_t = k_t[i * HD : (i + 1) * HD, :]
        grad_k, grad_v = 0.0, 0.0
        for b in range(count // 2):
            here = slice(b * span, (b + 1) * span)
            query = qkv[here, columns[0]]
            grad = d_all[here, d_first + i * HD : d_first + (i + 1) * HD]
            scores = dot(keys, query, NT)
            text_scores = dot(text[i], query, NT) + bias
            col_max = jnp.maximum(
                jnp.max(scores, axis=0, keepdims=True), jnp.max(text_scores, axis=0, keepdims=True)
            )
            exps = jnp.exp(scores - col_max)
            text_exps = jnp.exp(text_scores - col_max)
            total = jnp.sum(exps, axis=0, keepdims=True) + jnp.sum(text_exps, axis=0, keepdims=True)
            inverse = 1.0 / total
            grad_w = dot(values, grad, NT)
            text_grad_w = dot(values_text[i], grad, NT)
            delta = inverse * (
                jnp.sum(exps * grad_w, axis=0, keepdims=True)
                + jnp.sum(text_exps * text_grad_w, axis=0, keepdims=True)
            )
            weights = exps * inverse
            grad_s = (weights * (grad_w - delta)).astype(jnp.bfloat16)
            text_grad_s = (text_exps * inverse * (text_grad_w - delta)).astype(jnp.bfloat16)
            grad_k += dot(grad_s, query, NN)
            grad_v += dot(weights.astype(jnp.bfloat16), grad, NN)
            grad_q = dot(keys_t, grad_s, NN) + dot(text_t[i], text_grad_s, NN)
            grads[here, columns[0]] = grad_q.T * score_scale
        grads[:, columns[1]] = grad_k
        grads[:, columns[2]] = grad_v

    lane = lax.broadcasted_iota(jnp.int32, (1, inner), 1)
    mine = jnp.zeros((1, inner), jnp.float32)
    for i in range(slots):
        inside = (lane >= i * HD) & (lane < (i + 1) * HD) & (scalars[7 + count + i] > 0)
        mine = jnp.where(inside, 1.0, mine)
    gains = head_gains(gain, slots)
    for b in range(count // 2):
        here = slice(b * span, (b + 1) * span)
        scaled = grads[here, : 2 * inner].astype(jnp.bfloat16).astype(jnp.float32) * gains
        raw, inverse = raw_all[here, :], inv_all[here, :]
        back = scaled * inverse - raw * head_means(scaled * raw) * (inverse * inverse * inverse)
        valid = jnp.concatenate([mine, mine], axis=1) > 0.0
        stacked[here, : 2 * inner] = jnp.where(valid, back, 0.0).astype(jnp.bfloat16)
        back = jnp.where(mine > 0.0, grads[here, 2 * inner :], 0.0).astype(jnp.bfloat16)
        stacked[here, 2 * inner : 3 * inner] = back
    stacked[:, 3 * inner :] = jnp.zeros((tokens, stacked.shape[1] - 3 * inner), jnp.bfloat16)
    first = stacked[rows : 2 * rows, :]
    rest_out[: (count - 2) * rows, :] = stacked[2 * rows :, :]
    rest_out[(count - 2) * rows :, :] = stacked[:rows, :]
    for copy in local_copies[6:]:
        copy.wait()
    theirs_out[...] = dot(first, w_give[...], NT).astype(jnp.bfloat16)
    mine_out[...] = dot(first, w_keep[...], NT)


def project_call(scalars, gain, mod, weights, slots, rows, text_dev, count):
    shard = weights[0].shape[0]
    columns = whole_tiles(3 * slots * HD)
    width = mod[0].shape[1] - EXTRA
    tokens = rows * count
    text_rows = text_dev * count
    f32, bf16 = jnp.float32, jnp.bfloat16
    vmem, hbm = spec(pltpu.VMEM), spec(pl.ANY)
    inner = slots * HD
    shapes = [((tokens, 3 * inner), bf16), ((inner, tokens), bf16)] + [((tokens, 2 * inner), f32)] * 2
    shapes += [((slots, text_rows, HD), bf16), ((slots, HD, text_rows), bf16)]
    shapes += [((width // 2, whole_tiles(3 * slots * HD)), bf16)] * 2
    return pl.pallas_call(
        functools.partial(project_kernel, slots, count, rows, shard, width, text_dev),
        out_shape=tuple(jax.ShapeDtypeStruct(*one) for one in shapes),
        in_specs=[spec(pltpu.SMEM), vmem] + [hbm] * (len(mod) + len(weights)),
        out_specs=(hbm,) * 4 + (vmem,) * 2 + (hbm,) * 2,
        scratch_shapes=[
            pltpu.VMEM((width, columns), bf16),
            pltpu.VMEM((tokens, width + EXTRA), bf16),
            pltpu.SemaphoreType.DMA((len(mod) + len(weights) + 10,)),
            pltpu.VMEM((count, rows // 2, EXTRA), f32),
        ]
        + [pltpu.VMEM(*one) for one in shapes[:4]],
        compiler_params=pltpu.CompilerParams(vmem_limit_bytes=GRANT),
        cost_estimate=pl.CostEstimate(
            flops=2 * tokens * width * 3 * slots * HD,
            bytes_accessed=2 * (tokens * width + columns * width) + 4 * tokens * columns,
            transcendentals=0,
        ),
    )(scalars, gain, *mod, *weights)


def attend_call(scalars, gain, operands, cot, weights, slots, rows, text_dev):
    count = operands[0].shape[0] // rows
    shard, columns = weights[0].shape
    width = cot[0].shape[1] - EXTRA
    tokens = rows * count
    inner = slots * HD
    stacked = whole_tiles(3 * inner)
    first = (columns - inner) // 128 * 128
    f32, bf16 = jnp.float32, jnp.bfloat16
    vmem, hbm = spec(pltpu.VMEM), spec(pl.ANY)
    shapes = [((rows, width // 2), f32), ((rows, width // 2), bf16), ((tokens - rows, stacked), bf16)]
    return pl.pallas_call(
        functools.partial(attend_kernel, slots, count, rows, shard, width, text_dev, first),
        out_shape=tuple(jax.ShapeDtypeStruct(*one) for one in shapes),
        in_specs=[spec(pltpu.SMEM), vmem] + [hbm] * (len(operands) + len(cot) + len(weights)),
        out_specs=(vmem,) * len(shapes),
        scratch_shapes=[
            pltpu.VMEM((width, columns - first), bf16),
            pltpu.VMEM((tokens, width + EXTRA), bf16),
            pltpu.SemaphoreType.DMA((len(operands) + len(cot) + len(weights),)),
            pltpu.VMEM((count, rows // 2, EXTRA), f32),
            pltpu.VMEM((slots, text_dev * count, HD), bf16),
            pltpu.VMEM((tokens, columns - first), bf16),
            pltpu.VMEM((tokens, 3 * inner), f32),
            pltpu.VMEM((tokens, stacked), bf16),
        ]
        + [pltpu.VMEM(one.shape, one.dtype) for one in operands],
        compiler_params=pltpu.CompilerParams(vmem_limit_bytes=GRANT),
        cost_estimate=pl.CostEstimate(
            flops=2 * tokens * width * inner + 10 * tokens * tokens * inner,
            bytes_accessed=2 * (tokens * width + columns * width),
            transcendentals=slots * tokens * tokens,
        ),
    )(scalars, gain, *operands, *cot, *weights)


def backward_kernel(own, other, w_own, w_other, *outs):
    total = dot(own[...], w_own[...], NT) + dot(other[...], w_other[...], NT)
    part = outs[0].shape[0]
    for n, out in enumerate(outs):
        out[...] = total[n * part : (n + 1) * part].astype(out.dtype)


def backward_call(own, other, w_own, w_other, part, dtype):
    rows, inner = own.shape
    half = w_own.shape[0]
    vmem = spec(pltpu.VMEM)
    return pl.pallas_call(
        backward_kernel,
        out_shape=(jax.ShapeDtypeStruct((part, half), dtype),) * (rows // part),
        in_specs=[vmem] * 4,
        out_specs=(vmem,) * (rows // part),
        compiler_params=pltpu.CompilerParams(vmem_limit_bytes=SMALL_GRANT),
        cost_estimate=pl.CostEstimate(
            flops=4 * rows * half * inner,
            bytes_accessed=4 * (rows + half) * inner + 4 * rows * half,
            transcendentals=0,
        ),
    )(own, other, w_own, w_other)


def sums_kernel(own_near, own_far, near, far, scale, normed, grad_out, sums_out):
    half = near.shape[0]
    for part, (own, moving) in enumerate(((own_near, near), (own_far, far))):
        here = slice(part * half, (part + 1) * half)
        grad = (own[...] + moving[...].astype(jnp.float32)) * scale[...]
        grad_out[here, :] = grad
        first = jnp.sum(grad, axis=-1, keepdims=True)
        second = jnp.sum(grad * normed[here, :], axis=-1, keepdims=True)
        lane = lax.broadcasted_iota(jnp.int32, (half, 128), 1)
        sums_out[here, :] = jnp.where(lane == 0, first, second)


def last_kernel(width, grad, sums, other, normed, base, inv_std, out):
    total = (sums[...] + other[...]) * (1.0 / width)
    rows = base[...] + inv_std[:, 0:1] * (
        grad[...] - total[:, 0:1] - normed[...] * total[:, 1:2]
    )
    out[...] = rows.T


def local_call(kernel, shapes, scalar_count, *operands, grant=SMALL_GRANT):
    vmem = spec(pltpu.VMEM)
    return pl.pallas_call(
        kernel,
        out_shape=tuple(jax.ShapeDtypeStruct(*one) for one in shapes),
        in_specs=[spec(pltpu.SMEM)] * scalar_count + [vmem] * (len(operands) - scalar_count),
        out_specs=(vmem,) * len(shapes),
        compiler_params=pltpu.CompilerParams(vmem_limit_bytes=grant),
        cost_estimate=pl.CostEstimate(
            flops=sum(one.size for one in operands),
            bytes_accessed=sum(one.size * one.dtype.itemsize for one in operands),
            transcendentals=0,
        ),
    )(*operands)


def shards_by_head(states, adjoint, text_kv, text_len, step_index, modulation, w_qkv, qk_gain, w_out):
    hidden_state = states[0]
    adjoint_rows = adjoint[0]
    tok_count, model_width = hidden_state.shape
    seq_count = lax.axis_size("seq")
    inner_dev = w_qkv.shape[2]
    heads_dev = inner_dev // HD
    shard = w_qkv.shape[0]
    slots = -(-heads_dev // seq_count)
    inner = slots * HD
    half_rows = tok_count // 2
    half_width = model_width // 2
    f32, bf16 = jnp.float32, jnp.bfloat16
    core = lax.axis_index("head").astype(jnp.int32)
    seq_index = lax.axis_index("seq")
    dp_index = lax.axis_index("dp")
    pin = lax.optimization_barrier

    seq_order = line_ring(seq_count)
    seq_place = ring_place(seq_order, seq_index)
    seq_next = ring_pairs(seq_order)
    swap = [(0, 1), (1, 0)]
    first_way = [(2 * p + c, 2 * (p ^ (1 + c)) + c) for p in range(4) for c in range(2)]
    second_way = [(2 * p + c, 2 * (p ^ (2 - c)) + c) for p in range(4) for c in range(2)]

    first = seq_index * heads_dev // seq_count
    stop = (seq_index + 1) * heads_dev // seq_count
    window = jnp.minimum(first, heads_dev - slots)
    valid = [(window + i >= first) & (window + i < stop) for i in range(slots)]
    owners = [ring_member(seq_order, (seq_place - k + seq_count) % seq_count) for k in range(seq_count)]
    w_index = [dp_index, dp_index ^ (1 + core), dp_index ^ (2 - core), dp_index ^ 3]
    scalars = [core] + w_index + [window, text_len[0]] + owners + valid
    scalars = jnp.stack([one.astype(jnp.int32) for one in scalars])

    def step(moving):
        return lax.ppermute(moving, "seq", seq_next)

    def other_core(moving):
        return lax.ppermute(moving, "head", swap)

    def step_back(moving):
        return lax.ppermute(moving, "seq", [(b, a) for a, b in seq_next])

    quarter = half_rows // 2

    def spread(moving):
        return [step(moving), step_back(moving)]

    def pass_on(received):
        return [step(received[0][:quarter]), step_back(received[1][quarter:])]

    mod_half, table_rows, extra = first_call(
        step_index, core[None], hidden_state, modulation.transpose(1, 0, 2), adjoint_rows, text_kv[0]
    )
    mod_near = spread(mod_half)

    w_qkv, w_out, mod_half = pin((w_qkv, w_out, mod_half))
    take = lambda c: lax.dynamic_slice(w_qkv, (0, c, window * HD), (shard, 1, inner))[:, 0]
    own_w = [
        jnp.concatenate([take(0), take(1)], axis=1),
        jnp.concatenate([take(2), lax.dynamic_slice_in_dim(w_out, window * HD, inner, 0).T], axis=1),
    ]
    w_first = [lax.ppermute(part, ("dp", "head"), first_way) for part in own_w]
    w_second = [lax.ppermute(part, ("dp", "head"), second_way) for part in own_w]

    text_dev = text_kv.shape[1]
    mod_far = pass_on(mod_near)
    clip_limit = 0.5 * (tok_count * seq_count * model_width) ** 0.5
    extra, *w_first = pin((extra, *w_first))
    cot_half, clip = cotangent_call(
        clip_limit, scalars, adjoint_rows, table_rows, text_kv[0], extra, *mod_near, mod_far[1]
    )
    cot_half, mod_far[0] = pin((cot_half, mod_far[0]))
    cot_near = spread(cot_half)
    modulated, cotangent, normed_share, scale_share, inv_std, base = local_call(
        own_kernel,
        [((tok_count, model_width + EXTRA), bf16)] * 2
        + [
            ((tok_count, half_width), f32),
            ((1, half_width), f32),
            ((tok_count, 128), f32),
            ((tok_count, half_width), f32),
        ],
        1,
        core[None],
        hidden_state,
        adjoint_rows,
        table_rows,
        text_kv[0],
        extra,
        clip,
        grant=GRANT,
    )
    def pieces(own, received):
        return [own] + [one for moved in received for one in (moved, other_core(moved))]

    mod_far = list(pin((*mod_far, modulated))[:2])
    mod_pieces = pieces(modulated, mod_near + mod_far)
    w_diagonal = [lax.ppermute(part, ("dp", "head"), second_way) for part in w_first]
    weights = [part[n] for n in range(2) for part in (own_w, w_first, w_second, w_diagonal)]
    cot_near[0] = pin((cot_near[0], w_second, w_diagonal))[0]
    cot_far = [step(cot_near[0])]

    cot_pieces = pieces(cotangent, cot_near)
    *cot_pieces, mod_pieces[-1] = pin((*cot_pieces, mod_pieces[-1]))
    *operands, w_keep, w_give = project_call(
        scalars, qk_gain, mod_pieces, weights, slots, tok_count, text_dev, seq_count
    )
    w_give, cot_far[0] = pin((w_give, *cot_far))
    cot_pieces += pieces(None, cot_far)[1:]
    given, *cot_pieces = pin((w_give, *cot_pieces))
    w_other = other_core(given)
    mine, theirs, rest = attend_call(
        scalars, qk_gain, operands + [w_keep, w_give], cot_pieces, weights[4:], slots, tok_count, text_dev
    )
    first = (mine + other_core(theirs).astype(f32)).astype(bf16)
    moving = [first[:half_rows], first[half_rows:]]
    other_rest = other_core(rest)
    rest, other_rest, *_ = pin((rest, other_rest, *moving))
    own = backward_call(rest, other_rest, w_keep, w_other, half_rows, f32)
    for j in range(2, seq_count):
        moving = [step(part) for part in moving]
        moving = [
            (a + b.astype(f32)).astype(bf16) for a, b in zip(own[2 * (j - 2) : 2 * (j - 1)], moving)
        ]
    moving = [step(part) for part in moving]

    grad_scaled, sums = local_call(
        sums_kernel,
        [((tok_count, half_width), f32), ((tok_count, 128), f32)],
        0,
        *own[-2:],
        *moving,
        scale_share,
        normed_share,
    )
    (pulled,) = local_call(
        functools.partial(last_kernel, model_width),
        [((half_width, tok_count), f32)],
        0,
        grad_scaled,
        sums,
        other_core(sums),
        normed_share,
        base,
        inv_std,
    )
    return pulled.T[None]


def qk_normalize(values, gains):
    inverse = lax.rsqrt(jnp.mean(values * values, axis=-1, keepdims=True) + 1e-06)
    return ((values * inverse * gains).astype(jnp.bfloat16), inverse)


def qk_backward(values, inverse, cotangent, gains):
    scaled = cotangent.astype(jnp.float32) * gains
    return (
        scaled * inverse - values * jnp.mean(scaled * values, axis=-1, keepdims=True) * inverse**3
    )


def shards_by_row(states, adjoint, text_kv, text_len, step_index, modulation, w_qkv, qk_gain, w_out):
    hidden_state = states[0]
    adjoint_rows = adjoint[0]
    tok_count, model_width = hidden_state.shape
    seq_count = lax.axis_size("seq")
    inner_dev = w_qkv.shape[2]
    heads_dev = inner_dev // HD
    score_scale = HD ** (-0.5)
    squares = lax.psum(jnp.sum(adjoint_rows * adjoint_rows), "seq")
    clip_limit = 0.5 * (tok_count * seq_count * model_width) ** 0.5
    clip_scale = jnp.minimum(1.0, clip_limit / jnp.sqrt(squares + 1e-06))
    table_row = lax.dynamic_index_in_dim(modulation, step_index[0], 0, keepdims=False)
    offset_row = table_row[0]
    stretch = table_row[1]
    gating = table_row[2]
    widened = hidden_state.astype(jnp.float32)
    centered = widened - jnp.mean(widened, axis=-1, keepdims=True)
    inv_std = lax.rsqrt(jnp.mean(centered * centered, axis=-1, keepdims=True) + 1e-06)
    normed = centered * inv_std
    modulated = (normed * (1.0 + stretch) + offset_row).astype(jnp.bfloat16)
    cotangent = (gating * (clip_scale * adjoint_rows)).astype(jnp.bfloat16)
    contract_last = (((1,), (1,)), ((), ()))
    full_weight = lax.all_gather(w_qkv, "dp", axis=0, tiled=True).reshape(
        model_width, 3 * inner_dev
    )
    projected = jnp.dot(modulated, full_weight, preferred_element_type=jnp.float32)
    out_raw = lax.dot_general(
        cotangent,
        lax.all_gather(w_out, "dp", axis=1, tiled=True),
        contract_last,
        preferred_element_type=jnp.float32,
    )
    projected = projected.reshape(tok_count, 3, heads_dev, HD)
    queries, query_inv = qk_normalize(projected[:, 0], qk_gain[0])
    own_keys, key_inv = qk_normalize(projected[:, 1], qk_gain[1])
    own_values = projected[:, 2].astype(jnp.bfloat16)
    out_grad = out_raw.astype(jnp.bfloat16).reshape(tok_count, heads_dev, HD)
    text_keys = text_kv[0, :, 0, :]
    text_values = text_kv[0, :, 1, :]
    text_dev = text_keys.shape[0]
    rows_dev = tok_count + text_dev
    key_local = jnp.concatenate([own_keys.reshape(tok_count, inner_dev), text_keys], axis=0)
    value_local = jnp.concatenate([own_values.reshape(tok_count, inner_dev), text_values], axis=0)
    key_all, value_all = (
        lax.all_gather(key_local, "seq", axis=0, tiled=True),
        lax.all_gather(value_local, "seq", axis=0, tiled=True),
    )
    all_rows = rows_dev * seq_count
    row_ids = jnp.arange(all_rows, dtype=jnp.int32)
    owner = row_ids // rows_dev
    within = row_ids % rows_dev
    allowed = (within < tok_count) | (owner * text_dev + within - tok_count < text_len[0])
    group = 1
    while group * 2 * rows_dev <= 512 and seq_count % (group * 2) == 0:
        group = group * 2
    block_rows = group * rows_dev
    block_count = all_rows // block_rows
    key_blocks = key_all.reshape(block_count, block_rows, heads_dev, HD)
    value_blocks = value_all.reshape(block_count, block_rows, heads_dev, HD)
    mask_blocks = allowed.reshape(block_count, block_rows)

    def block_scores(key_block, mask_block):
        scores = (
            jnp.einsum("qhd,khd->qhk", queries, key_block, preferred_element_type=jnp.float32)
            * score_scale
        )
        return jnp.where(mask_block[None, None, :], scores, -1e30)

    def first_pass(carry, block):
        row_max, row_sum, row_dot = carry
        key_block, value_block, mask_block = block
        scores = block_scores(key_block, mask_block)
        new_max = jnp.maximum(row_max, jnp.max(scores, axis=-1))
        rescale = jnp.exp(row_max - new_max)
        exps = jnp.exp(scores - new_max[:, :, None])
        grad_weights = jnp.einsum(
            "qhd,khd->qhk", out_grad, value_block, preferred_element_type=jnp.float32
        )
        return (
            (
                new_max,
                row_sum * rescale + jnp.sum(exps, axis=-1),
                row_dot * rescale + jnp.sum(exps * grad_weights, axis=-1),
            ),
            None,
        )

    start_state = (
        jnp.full((tok_count, heads_dev), -1e30, jnp.float32),
        jnp.zeros((tok_count, heads_dev), jnp.float32),
        jnp.zeros((tok_count, heads_dev), jnp.float32),
    )
    (row_max, row_sum, row_dot), unused = lax.scan(
        first_pass, start_state, (key_blocks, value_blocks, mask_blocks)
    )
    log_total = row_max + jnp.log(row_sum)
    delta_row = row_dot / row_sum

    def second_pass(running, block):
        key_block, value_block, mask_block = block
        weights = jnp.exp(block_scores(key_block, mask_block) - log_total[:, :, None])
        grad_weights = jnp.einsum(
            "qhd,khd->qhk", out_grad, value_block, preferred_element_type=jnp.float32
        )
        grad_scores = (weights * (grad_weights - delta_row[:, :, None])).astype(jnp.bfloat16)
        return (
            running
            + jnp.einsum(
                "qhk,khd->qhd", grad_scores, key_block, preferred_element_type=jnp.float32
            ),
            None,
        )

    query_sum, unused = lax.scan(
        second_pass,
        jnp.zeros((tok_count, heads_dev, HD), jnp.float32),
        (key_blocks, value_blocks, mask_blocks),
    )
    grad_query = (query_sum * score_scale).astype(jnp.bfloat16)
    log_all, delta_all = (
        lax.all_gather(log_total, "seq", axis=0, tiled=True),
        lax.all_gather(delta_row, "seq", axis=0, tiled=True),
    )
    local_ids = jnp.arange(rows_dev, dtype=jnp.int32)
    local_allowed = (local_ids < tok_count) | (
        lax.axis_index("seq") * text_dev + local_ids - tok_count < text_len[0]
    )
    key_three = key_local.reshape(rows_dev, heads_dev, HD)
    value_three = value_local.reshape(rows_dev, heads_dev, HD)
    query_piece = lax.all_gather(queries.reshape(tok_count, inner_dev), "seq", axis=0, tiled=True)
    grad_piece = lax.all_gather(out_grad.reshape(tok_count, inner_dev), "seq", axis=0, tiled=True)
    piece_rows = query_piece.shape[0]
    query_rows = query_piece.reshape(piece_rows, heads_dev, HD)
    grad_rows = grad_piece.reshape(piece_rows, heads_dev, HD)
    scores = (
        jnp.einsum("qhd,khd->qhk", query_rows, key_three, preferred_element_type=jnp.float32)
        * score_scale
    )
    scores = jnp.where(local_allowed[None, None, :], scores, -1e30)
    weights = jnp.exp(scores - log_all[:, :, None])
    grad_weights = jnp.einsum(
        "qhd,khd->qhk", grad_rows, value_three, preferred_element_type=jnp.float32
    )
    grad_scores = (weights * (grad_weights - delta_all[:, :, None])).astype(jnp.bfloat16)
    rounded = weights.astype(jnp.bfloat16)
    key_sum = jnp.einsum(
        "qhk,qhd->khd", grad_scores, query_rows, preferred_element_type=jnp.float32
    )
    value_sum = jnp.einsum("qhk,qhd->khd", rounded, grad_rows, preferred_element_type=jnp.float32)
    key_sum, value_sum = (key_sum, value_sum)
    grad_key = (key_sum[:tok_count] * score_scale).astype(jnp.bfloat16)
    grad_value = value_sum[:tok_count].astype(jnp.bfloat16)
    raw_query = qk_backward(projected[:, 0], query_inv, grad_query, qk_gain[0])
    raw_key = qk_backward(projected[:, 1], key_inv, grad_key, qk_gain[1])
    stacked = jnp.stack([raw_query, raw_key, grad_value.astype(jnp.float32)], axis=1).astype(
        jnp.bfloat16
    )
    stacked = stacked.reshape(tok_count, 3 * inner_dev)
    partial_grad = lax.dot_general(
        stacked, full_weight, contract_last, preferred_element_type=jnp.float32
    )
    half_width = model_width // lax.axis_size("head")
    first_col = lax.axis_index("head") * half_width
    grad_share = lax.psum_scatter(
        partial_grad.astype(jnp.bfloat16), "head", scatter_dimension=1, tiled=True
    ).astype(jnp.float32)
    normed_share = lax.dynamic_slice_in_dim(normed, first_col, half_width, 1)
    stretch_share = lax.dynamic_slice_in_dim(stretch, first_col, half_width, 0)
    adjoint_share = lax.dynamic_slice_in_dim(adjoint_rows, first_col, half_width, 1)
    grad_scaled = grad_share * (1.0 + stretch_share)
    row_sums = jnp.stack(
        [jnp.sum(grad_scaled, axis=-1), jnp.sum(grad_scaled * normed_share, axis=-1)], axis=-1
    )
    row_sums = lax.psum(row_sums, "head")
    grad_state = inv_std * (
        grad_scaled - row_sums[:, 0:1] / model_width - normed_share * row_sums[:, 1:2] / model_width
    )
    pulled = clip_scale * adjoint_share + grad_state
    return pulled[None]


def solution(mesh):
    in_specs = (
        P("dp", "seq", None),
        P("dp", "seq", None),
        P("dp", "seq", None, "head"),
        P("dp"),
        P("dp"),
        P(),
        P("dp", None, "head"),
        P(),
        P("head", "dp"),
    )
    out_specs = P("dp", "seq", "head")
    by_head = mesh.shape["seq"] == 4 and mesh.shape["dp"] == 4 and mesh.shape["head"] == 2
    shards = shards_by_head if by_head else shards_by_row
    return jax.shard_map(shards, mesh=mesh, in_specs=in_specs, out_specs=out_specs, check_vma=False)
```

```python
import functools

import jax
import jax.numpy as jnp
from jax import lax
from jax.experimental import pallas as pl
from jax.experimental.pallas import tpu as pltpu
from jax.sharding import PartitionSpec as P

HD = 64
GRANT = 60 * 1024 * 1024
SMALL_GRANT = 24 * 1024 * 1024
EXTRA = 128
NT = (((1,), (1,)), ((), ()))
NN = (((1,), (0,)), ((), ()))


def line_ring(count):
    return [0] + list(range(1, count, 2)) + [i for i in range(count - 1, 0, -1) if i % 2 == 0]


def ring_pairs(order):
    return [(order[i], order[(i + 1) % len(order)]) for i in range(len(order))]


def ring_place(order, index):
    place = jnp.int32(0)
    for position, member in enumerate(order):
        place = jnp.where(index == member, jnp.int32(position), place)
    return place


def ring_member(order, place):
    member = jnp.int32(order[0])
    for position, value in enumerate(order):
        member = jnp.where(place == position, jnp.int32(value), member)
    return member


def dot(a, b, dims):
    return lax.dot_general(a, b, dims, preferred_element_type=jnp.float32)


def equal_blocks(columns, block):
    row = lax.broadcasted_iota(jnp.int32, (columns, columns), 0)
    column = lax.broadcasted_iota(jnp.int32, (columns, columns), 1)
    return jnp.where(row // block == column // block, 1.0, 0.0).astype(jnp.bfloat16)


def head_means(values):
    parts = []
    for first in range(0, values.shape[1], 256):
        part = values[:, first : first + 256]
        ones = equal_blocks(part.shape[1], HD)
        high = part.astype(jnp.bfloat16)
        low = (part - high.astype(jnp.float32)).astype(jnp.bfloat16)
        parts.append(dot(high, ones, NN) + dot(low, ones, NN))
    return jnp.concatenate(parts, axis=1) * (1.0 / HD)


def head_gains(gain, slots):
    return jnp.concatenate([gain[0:1, :]] * slots + [gain[1:2, :]] * slots, axis=1)


def whole_tiles(columns):
    return -(-columns // 128) * 128


def spec(space):
    return pl.BlockSpec(memory_space=space)


def text_columns(text, part):
    rows = text[...].astype(jnp.float32)[:, part, :]
    return [rows[:, c * EXTRA : (c + 1) * EXTRA] for c in range(rows.shape[1] // EXTRA)]


def extra_columns(blocks, rows):
    filled = sum(one.shape[0] for one in blocks)
    blocks = blocks + [jnp.zeros((rows - filled, EXTRA), jnp.float32)]
    return jnp.concatenate(blocks, axis=0).astype(jnp.bfloat16)


def first_kernel(step, core, states, table, adjoint, text, out, rows_out, extra_out):
    rows = [table[c, pl.ds(step[0], 1), :] for c in range(3)]
    widened = states[...].astype(jnp.float32)
    centered = widened - jnp.mean(widened, axis=-1, keepdims=True)
    inv_std = lax.rsqrt(jnp.mean(centered * centered, axis=-1, keepdims=True) + 1e-06)
    half, width = states.shape
    out[:, :width] = (centered * inv_std * (1.0 + rows[1]) + rows[0]).astype(jnp.bfloat16)
    for c in range(3):
        rows_out[c : c + 1, :] = rows[c]
    squares = jnp.sum(adjoint[...] * adjoint[...], axis=0, keepdims=True)
    squares = jnp.sum(squares, axis=1, keepdims=True)
    terms = []
    for n in range(3):
        terms.append(squares.astype(jnp.bfloat16).astype(jnp.float32))
        squares = squares - terms[-1]
    lane = lax.broadcasted_iota(jnp.int32, (8, EXTRA), 1)
    sums = jnp.where(lane == 0, terms[0], jnp.where(lane == 1, terms[1], jnp.where(lane == 2, terms[2], 0.0)))
    extra = extra_columns(text_columns(text, 0) + [sums], half)
    out[:, width:] = extra
    extra_out[...] = extra


def first_call(step, core, states, table, adjoint, text):
    rows, width = states.shape
    half = rows // 2
    whole = lambda *shape: pl.BlockSpec(shape, lambda i, step, core: (0,) * len(shape))
    return pl.pallas_call(
        first_kernel,
        out_shape=(
            jax.ShapeDtypeStruct((half, width + EXTRA), jnp.bfloat16),
            jax.ShapeDtypeStruct((8, width), jnp.float32),
            jax.ShapeDtypeStruct((half, EXTRA), jnp.bfloat16),
        ),
        grid_spec=pltpu.PrefetchScalarGridSpec(
            num_scalar_prefetch=2,
            grid=(1,),
            in_specs=[
                pl.BlockSpec((half, width), lambda i, step, core: (core[0], 0)),
                whole(*table.shape),
                whole(*adjoint.shape),
                whole(*text.shape),
            ],
            out_specs=(whole(half, width + EXTRA), whole(8, width), whole(half, EXTRA)),
        ),
        compiler_params=pltpu.CompilerParams(vmem_limit_bytes=GRANT),
        cost_estimate=pl.CostEstimate(flops=8 * half * width, bytes_accessed=16 * half * width, transcendentals=0),
    )(step, core, states, table, adjoint, text)


def pick_half(core, rows):
    half = rows.shape[1] // 2
    return jnp.where(core == 0, rows[:, :half], rows[:, half:])


def cotangent_kernel(limit, core, adjoint, table_rows, text, extra, previous, following, opposite, out, clip_out):
    first = previous.shape[0] - opposite.shape[0]
    row = 8 * (text.shape[2] // EXTRA)
    squares = opposite[...].astype(jnp.float32)[row - first : row - first + 1, :]
    for terms in (extra, previous, following):
        squares = squares + terms[...].astype(jnp.float32)[row : row + 1, :]
    squares = jnp.sum(squares, axis=1, keepdims=True)
    clip_scale = jnp.minimum(1.0, limit / jnp.sqrt(squares + 1e-06))
    half, width = adjoint.shape
    out[:, :width] = (table_rows[2:3, :] * (clip_scale * adjoint[...])).astype(jnp.bfloat16)
    out[:, width:] = extra_columns(text_columns(text, 1), half)
    clip_out[...] = jnp.broadcast_to(clip_scale, clip_out.shape)


def cotangent_call(limit, core, adjoint, table_rows, text, extra, previous, following, opposite):
    rows, width = adjoint.shape
    half = rows // 2
    block = width // EXTRA
    whole = lambda one: pl.BlockSpec(one.shape, lambda i, core: (0,) * one.ndim)
    tail = lambda one: pl.BlockSpec((one.shape[0], EXTRA), lambda i, core: (0, block))
    outs = (
        jax.ShapeDtypeStruct((half, width + EXTRA), jnp.bfloat16),
        jax.ShapeDtypeStruct((8, EXTRA), jnp.float32),
    )
    return pl.pallas_call(
        functools.partial(cotangent_kernel, limit),
        out_shape=outs,
        grid_spec=pltpu.PrefetchScalarGridSpec(
            num_scalar_prefetch=1,
            grid=(1,),
            in_specs=[pl.BlockSpec((half, width), lambda i, core: (core[0], 0))]
            + [whole(table_rows), whole(text), whole(extra)]
            + [tail(one) for one in (previous, following, opposite)],
            out_specs=tuple(whole(one) for one in outs),
        ),
        compiler_params=pltpu.CompilerParams(vmem_limit_bytes=GRANT),
        cost_estimate=pl.CostEstimate(flops=4 * half * width, bytes_accessed=6 * half * width, transcendentals=0),
    )(core, adjoint, table_rows, text, extra, previous, following, opposite)


def own_kernel(
    core, states, adjoint, table_rows, text, extra, clip, out, cot_out, normed_out, stretch_out, inv_out, base_out
):
    rows, width = states.shape
    half = rows // 2
    widened = states[...].astype(jnp.float32)
    centered = widened - jnp.mean(widened, axis=-1, keepdims=True)
    inv_std = lax.rsqrt(jnp.mean(centered * centered, axis=-1, keepdims=True) + 1e-06)
    normed = centered * inv_std
    scale = 1.0 + table_rows[1:2, :]
    out[:, :width] = (normed * scale + table_rows[0:1, :]).astype(jnp.bfloat16)
    normed_out[...] = pick_half(core[0], normed)
    stretch_out[...] = pick_half(core[0], scale)
    inv_out[...] = jnp.broadcast_to(inv_std, inv_out.shape)
    clipped = clip[0:1, 0:1] * adjoint[...]
    cot_out[:, :width] = (table_rows[2:3, :] * clipped).astype(jnp.bfloat16)
    base_out[...] = pick_half(core[0], clipped)
    columns = extra_columns(text_columns(text, 1), half)
    for n in range(2):
        out[n * half : (n + 1) * half, width:] = extra[...]
        cot_out[n * half : (n + 1) * half, width:] = columns


class Copies:
    def __init__(self, sems):
        self.sems = sems
        self.count = 0

    def start(self, source, target):
        copy = pltpu.make_async_copy(source, target, self.sems.at[self.count])
        copy.start()
        self.count += 1
        return copy

    def weights(self, scalars, w_in, w_all, shard, first=0):
        part = w_in[0].shape[1]
        copies = []
        for n, piece in enumerate(w_in):
            there = n // 4 * (part - first)
            columns = min(part - first, w_all.shape[1] - there)
            copies.append(
                self.start(
                    piece.at[:, pl.ds(first, columns)],
                    w_all.at[
                        pl.ds(pl.multiple_of(scalars[1 + n % 4] * shard, 16), shard),
                        pl.ds(there, columns),
                    ],
                )
            )
        return copies

    def rows(self, core, pieces, target, rows):
        half = rows // 2
        copies = [self.start(pieces[0], target.at[pl.ds(0, rows)])]
        places = [(rows, half), (3 * rows, half)]
        parts = (len(pieces) - 5) // 2
        places += [(2 * rows + n * half // parts, half // parts) for n in range(parts)]
        for n, (first, size) in enumerate(places):
            for m, holder in enumerate((core, 1 - core)):
                there = pl.ds(pl.multiple_of(first + holder * half, 16), size)
                copies.append(self.start(pieces[1 + 2 * n + m], target.at[there]))
        return copies


def window_heads(scalars, count, rows, text_dev, gathered, width, extra, text, text_t=None):
    half = rows // 2
    for k in range(count):
        there = pl.ds(pl.multiple_of(k * rows + scalars[0] * half, 16), half)
        extra[k] = gathered[there, width:].astype(jnp.float32)
    for i in range(text.shape[0]):
        head = scalars[5] + i
        first = pl.ds(pl.multiple_of(head // 2 * text_dev, 8), text_dev)
        found = jnp.concatenate([extra[k, first, :] for k in range(count)], axis=0)
        found = jnp.where(head % 2 == 0, found[:, :HD], found[:, HD:])
        text[i] = found.astype(jnp.bfloat16)
        if text_t is not None:
            text_t[i] = found.T.astype(jnp.bfloat16)


def project_kernel(slots, count, rows, shard, width, text_dev, scalars, gain, *refs):
    refs = list(refs)
    take = lambda n: [refs.pop(0) for _ in range(n)]
    mod_in = take(9)
    w_in = take(8)
    qkv, k_t, raw_all, inv_all, text, text_t, w_keep, w_give = take(8)
    w_all, mod_all, sems, extra, qkv_s, k_t_s, raw_s, inv_s = take(8)
    inner = slots * HD
    core = scalars[0]
    copies = Copies(sems)
    row_copies = copies.rows(core, mod_in, mod_all, rows)
    w_copies = copies.weights(scalars, w_in, w_all, shard)

    lane = lax.broadcasted_iota(jnp.int32, (1, 2 * inner), 1)
    gains = head_gains(gain, slots) * jnp.where(lane < inner, HD ** (-0.5), 1.0)
    identity = equal_blocks(inner, 1)
    out_copies = []
    for copy in row_copies + w_copies[:4]:
        copy.wait()
    raw = dot(mod_all[:, :width], w_all[:, : 2 * inner], NN)
    raw_s[...] = raw
    out_copies.append(copies.start(raw_s, raw_all))
    inverse = lax.rsqrt(head_means(raw * raw) + 1e-06)
    inv_s[...] = inverse
    out_copies.append(copies.start(inv_s, inv_all))
    qkv_s[:, : 2 * inner] = (raw * inverse * gains).astype(jnp.bfloat16)
    for copy in w_copies[4:]:
        copy.wait()
    half = width // 2
    for holder, target in ((core, w_keep), (1 - core, w_give)):
        source = w_all.at[pl.ds(pl.multiple_of(holder * half, 16), half)]
        out_copies.append(copies.start(source, target))
    qkv_s[:, 2 * inner :] = dot(
        mod_all[:, :width], w_all[:, 2 * inner : 3 * inner], NN
    ).astype(jnp.bfloat16)
    out_copies.append(copies.start(qkv_s, qkv))
    k_t_s[...] = dot(identity, qkv_s[:, inner : 2 * inner], NT).astype(jnp.bfloat16)
    out_copies.append(copies.start(k_t_s, k_t))
    window_heads(scalars, count, rows, text_dev, mod_all, width, extra, text, text_t)
    for copy in out_copies:
        copy.wait()


def attend_kernel(slots, count, rows, shard, width, text_dev, first_column, scalars, gain, *refs):
    refs = list(refs)
    take = lambda n: [refs.pop(0) for _ in range(n)]
    projected = take(8)
    cot_in = take(7)
    w_in = take(4)
    mine_near, mine_far, theirs_near, theirs_far, rest_out = take(5)
    w_out, cot_all, sems, extra, values_text = take(5)
    d_all, grads, stacked = take(3)
    qkv, k_t, raw_all, inv_all, text, text_t, w_keep, w_give = refs
    inner = slots * HD
    tokens = rows * count
    core = scalars[0]
    copies = Copies(sems)
    w_copies = copies.weights(scalars, w_in, w_out, shard, first_column)
    row_copies = copies.rows(core, cot_in, cot_all, rows)
    local_copies = [copies.start(*one) for one in zip(projected, refs)]
    score_scale = HD ** (-0.5)
    span = 2 * rows

    text_rows = count * text_dev
    row = lax.broadcasted_iota(jnp.int32, (text_rows, span), 0)
    text_id = row
    for k in range(count):
        inside = (row >= k * text_dev) & (row < (k + 1) * text_dev)
        text_id = jnp.where(inside, row + (scalars[7 + k] - k) * text_dev, text_id)
    bias = jnp.where(text_id < scalars[6], 0.0, -1e30)

    for copy in w_copies:
        copy.wait()
    arrivals = [row_copies[:3], row_copies[3:]]
    for b in range(count // 2):
        for copy in arrivals[b]:
            copy.wait()
        here = slice(b * span, (b + 1) * span)
        out_grad = jnp.dot(cot_all[here, :width], w_out[...], preferred_element_type=jnp.float32)
        d_all[here, :] = out_grad.astype(jnp.bfloat16)
    window_heads(scalars, count, rows, text_dev, cot_all, width, extra, values_text)
    for copy in local_copies[:6]:
        copy.wait()

    d_first = d_all.shape[1] - inner
    for i in range(slots):
        columns = [slice(n * inner + i * HD, n * inner + (i + 1) * HD) for n in range(3)]
        keys, values = qkv[:, columns[1]], qkv[:, columns[2]]
        keys_t = k_t[i * HD : (i + 1) * HD, :]
        grad_k, grad_v = 0.0, 0.0
        for b in range(count // 2):
            here = slice(b * span, (b + 1) * span)
            query = qkv[here, columns[0]]
            grad = d_all[here, d_first + i * HD : d_first + (i + 1) * HD]
            scores = dot(keys, query, NT)
            text_scores = dot(text[i], query, NT) + bias
            col_max = jnp.maximum(
                jnp.max(scores, axis=0, keepdims=True), jnp.max(text_scores, axis=0, keepdims=True)
            )
            exps = jnp.exp(scores - col_max)
            text_exps = jnp.exp(text_scores - col_max)
            total = jnp.sum(exps, axis=0, keepdims=True) + jnp.sum(text_exps, axis=0, keepdims=True)
            inverse = 1.0 / total
            grad_w = dot(values, grad, NT)
            text_grad_w = dot(values_text[i], grad, NT)
            delta = inverse * (
                jnp.sum(exps * grad_w, axis=0, keepdims=True)
                + jnp.sum(text_exps * text_grad_w, axis=0, keepdims=True)
            )
            weights = exps * inverse
            grad_s = (weights * (grad_w - delta)).astype(jnp.bfloat16)
            text_grad_s = (text_exps * inverse * (text_grad_w - delta)).astype(jnp.bfloat16)
            grad_k += dot(grad_s, query, NN)
            grad_v += dot(weights.astype(jnp.bfloat16), grad, NN)
            grad_q = dot(keys_t, grad_s, NN) + dot(text_t[i], text_grad_s, NN)
            grads[here, columns[0]] = grad_q.T * score_scale
        grads[:, columns[1]] = grad_k
        grads[:, columns[2]] = grad_v

    lane = lax.broadcasted_iota(jnp.int32, (1, inner), 1)
    mine = jnp.zeros((1, inner), jnp.float32)
    for i in range(slots):
        inside = (lane >= i * HD) & (lane < (i + 1) * HD) & (scalars[7 + count + i] > 0)
        mine = jnp.where(inside, 1.0, mine)
    gains = head_gains(gain, slots)
    for b in range(count // 2):
        here = slice(b * span, (b + 1) * span)
        scaled = grads[here, : 2 * inner].astype(jnp.bfloat16).astype(jnp.float32) * gains
        raw, inverse = raw_all[here, :], inv_all[here, :]
        back = scaled * inverse - raw * head_means(scaled * raw) * (inverse * inverse * inverse)
        valid = jnp.concatenate([mine, mine], axis=1) > 0.0
        stacked[here, : 2 * inner] = jnp.where(valid, back, 0.0).astype(jnp.bfloat16)
        back = jnp.where(mine > 0.0, grads[here, 2 * inner :], 0.0).astype(jnp.bfloat16)
        stacked[here, 2 * inner : 3 * inner] = back
    stacked[:, 3 * inner :] = jnp.zeros((tokens, stacked.shape[1] - 3 * inner), jnp.bfloat16)
    first = stacked[rows : 2 * rows, :]
    rest_out[: (count - 2) * rows, :] = stacked[2 * rows :, :]
    rest_out[(count - 2) * rows :, :] = stacked[:rows, :]
    for copy in local_copies[6:]:
        copy.wait()
    theirs = dot(first, w_give[...], NT).astype(jnp.bfloat16)
    theirs_near[...] = theirs[: rows // 2]
    theirs_far[...] = theirs[rows // 2 :]
    mine = dot(first, w_keep[...], NT)
    mine_near[...] = mine[: rows // 2]
    mine_far[...] = mine[rows // 2 :]


def project_call(scalars, gain, mod, weights, slots, rows, text_dev, count):
    shard = weights[0].shape[0]
    columns = whole_tiles(3 * slots * HD)
    width = mod[0].shape[1] - EXTRA
    tokens = rows * count
    text_rows = text_dev * count
    f32, bf16 = jnp.float32, jnp.bfloat16
    vmem, hbm = spec(pltpu.VMEM), spec(pl.ANY)
    inner = slots * HD
    shapes = [((tokens, 3 * inner), bf16), ((inner, tokens), bf16)] + [((tokens, 2 * inner), f32)] * 2
    shapes += [((slots, text_rows, HD), bf16), ((slots, HD, text_rows), bf16)]
    shapes += [((width // 2, whole_tiles(3 * slots * HD)), bf16)] * 2
    return pl.pallas_call(
        functools.partial(project_kernel, slots, count, rows, shard, width, text_dev),
        out_shape=tuple(jax.ShapeDtypeStruct(*one) for one in shapes),
        in_specs=[spec(pltpu.SMEM), vmem] + [hbm] * (len(mod) + len(weights)),
        out_specs=(hbm,) * 4 + (vmem,) * 2 + (hbm,) * 2,
        scratch_shapes=[
            pltpu.VMEM((width, columns), bf16),
            pltpu.VMEM((tokens, width + EXTRA), bf16),
            pltpu.SemaphoreType.DMA((len(mod) + len(weights) + 10,)),
            pltpu.VMEM((count, rows // 2, EXTRA), f32),
        ]
        + [pltpu.VMEM(*one) for one in shapes[:4]],
        compiler_params=pltpu.CompilerParams(vmem_limit_bytes=GRANT),
        cost_estimate=pl.CostEstimate(
            flops=2 * tokens * width * 3 * slots * HD,
            bytes_accessed=2 * (tokens * width + columns * width) + 4 * tokens * columns,
            transcendentals=0,
        ),
    )(scalars, gain, *mod, *weights)


def attend_call(scalars, gain, operands, cot, weights, slots, rows, text_dev):
    count = operands[0].shape[0] // rows
    shard, columns = weights[0].shape
    width = cot[0].shape[1] - EXTRA
    tokens = rows * count
    inner = slots * HD
    stacked = whole_tiles(3 * inner)
    first = (columns - inner) // 128 * 128
    f32, bf16 = jnp.float32, jnp.bfloat16
    vmem, hbm = spec(pltpu.VMEM), spec(pl.ANY)
    part = (rows // 2, width // 2)
    shapes = [(part, f32)] * 2 + [(part, bf16)] * 2 + [((tokens - rows, stacked), bf16)]
    return pl.pallas_call(
        functools.partial(attend_kernel, slots, count, rows, shard, width, text_dev, first),
        out_shape=tuple(jax.ShapeDtypeStruct(*one) for one in shapes),
        in_specs=[spec(pltpu.SMEM), vmem] + [hbm] * (len(operands) + len(cot) + len(weights)),
        out_specs=(vmem,) * len(shapes),
        scratch_shapes=[
            pltpu.VMEM((width, columns - first), bf16),
            pltpu.VMEM((tokens, width + EXTRA), bf16),
            pltpu.SemaphoreType.DMA((len(operands) + len(cot) + len(weights),)),
            pltpu.VMEM((count, rows // 2, EXTRA), f32),
            pltpu.VMEM((slots, text_dev * count, HD), bf16),
            pltpu.VMEM((tokens, columns - first), bf16),
            pltpu.VMEM((tokens, 3 * inner), f32),
            pltpu.VMEM((tokens, stacked), bf16),
        ]
        + [pltpu.VMEM(one.shape, one.dtype) for one in operands],
        compiler_params=pltpu.CompilerParams(vmem_limit_bytes=GRANT),
        cost_estimate=pl.CostEstimate(
            flops=2 * tokens * width * inner + 10 * tokens * tokens * inner,
            bytes_accessed=2 * (tokens * width + columns * width),
            transcendentals=slots * tokens * tokens,
        ),
    )(scalars, gain, *operands, *cot, *weights)


def backward_kernel(own, other, w_own, w_other, *outs):
    total = dot(own[...], w_own[...], NT) + dot(other[...], w_other[...], NT)
    part = outs[0].shape[0]
    for n, out in enumerate(outs):
        out[...] = total[n * part : (n + 1) * part].astype(out.dtype)


def backward_call(own, other, w_own, w_other, part, dtype):
    rows, inner = own.shape
    half = w_own.shape[0]
    vmem = spec(pltpu.VMEM)
    return pl.pallas_call(
        backward_kernel,
        out_shape=(jax.ShapeDtypeStruct((part, half), dtype),) * (rows // part),
        in_specs=[vmem] * 4,
        out_specs=(vmem,) * (rows // part),
        compiler_params=pltpu.CompilerParams(vmem_limit_bytes=SMALL_GRANT),
        cost_estimate=pl.CostEstimate(
            flops=4 * rows * half * inner,
            bytes_accessed=4 * (rows + half) * inner + 4 * rows * half,
            transcendentals=0,
        ),
    )(own, other, w_own, w_other)


def sums_kernel(own_near, own_far, near, far, scale, normed, grad_out, sums_out):
    half = near.shape[0]
    for part, (own, moving) in enumerate(((own_near, near), (own_far, far))):
        here = slice(part * half, (part + 1) * half)
        grad = (own[...] + moving[...].astype(jnp.float32)) * scale[...]
        grad_out[here, :] = grad
        first = jnp.sum(grad, axis=-1, keepdims=True)
        second = jnp.sum(grad * normed[here, :], axis=-1, keepdims=True)
        lane = lax.broadcasted_iota(jnp.int32, (half, 128), 1)
        sums_out[here, :] = jnp.where(lane == 0, first, second)


def last_kernel(width, grad, sums, other, normed, base, inv_std, out):
    total = (sums[...] + other[...]) * (1.0 / width)
    rows = base[...] + inv_std[:, 0:1] * (
        grad[...] - total[:, 0:1] - normed[...] * total[:, 1:2]
    )
    out[...] = rows.T


def local_call(kernel, shapes, scalar_count, *operands, grant=SMALL_GRANT):
    vmem = spec(pltpu.VMEM)
    return pl.pallas_call(
        kernel,
        out_shape=tuple(jax.ShapeDtypeStruct(*one) for one in shapes),
        in_specs=[spec(pltpu.SMEM)] * scalar_count + [vmem] * (len(operands) - scalar_count),
        out_specs=(vmem,) * len(shapes),
        compiler_params=pltpu.CompilerParams(vmem_limit_bytes=grant),
        cost_estimate=pl.CostEstimate(
            flops=sum(one.size for one in operands),
            bytes_accessed=sum(one.size * one.dtype.itemsize for one in operands),
            transcendentals=0,
        ),
    )(*operands)


def shards_by_head(states, adjoint, text_kv, text_len, step_index, modulation, w_qkv, qk_gain, w_out):
    hidden_state = states[0]
    adjoint_rows = adjoint[0]
    tok_count, model_width = hidden_state.shape
    seq_count = lax.axis_size("seq")
    inner_dev = w_qkv.shape[2]
    heads_dev = inner_dev // HD
    shard = w_qkv.shape[0]
    slots = -(-heads_dev // seq_count)
    inner = slots * HD
    half_rows = tok_count // 2
    half_width = model_width // 2
    f32, bf16 = jnp.float32, jnp.bfloat16
    core = lax.axis_index("head").astype(jnp.int32)
    seq_index = lax.axis_index("seq")
    dp_index = lax.axis_index("dp")
    pin = lax.optimization_barrier

    seq_order = line_ring(seq_count)
    seq_place = ring_place(seq_order, seq_index)
    seq_next = ring_pairs(seq_order)
    swap = [(0, 1), (1, 0)]
    first_way = [(2 * p + c, 2 * (p ^ (1 + c)) + c) for p in range(4) for c in range(2)]
    second_way = [(2 * p + c, 2 * (p ^ (2 - c)) + c) for p in range(4) for c in range(2)]

    first = seq_index * heads_dev // seq_count
    stop = (seq_index + 1) * heads_dev // seq_count
    window = jnp.minimum(first, heads_dev - slots)
    valid = [(window + i >= first) & (window + i < stop) for i in range(slots)]
    owners = [ring_member(seq_order, (seq_place - k + seq_count) % seq_count) for k in range(seq_count)]
    w_index = [dp_index, dp_index ^ (1 + core), dp_index ^ (2 - core), dp_index ^ 3]
    scalars = [core] + w_index + [window, text_len[0]] + owners + valid
    scalars = jnp.stack([one.astype(jnp.int32) for one in scalars])

    def step(moving):
        return lax.ppermute(moving, "seq", seq_next)

    def other_core(moving):
        return lax.ppermute(moving, "head", swap)

    def step_back(moving):
        return lax.ppermute(moving, "seq", [(b, a) for a, b in seq_next])

    quarter = half_rows // 2

    def spread(moving):
        return [step(moving), step_back(moving)]

    def pass_on(received):
        return [step(received[0][:quarter]), step_back(received[1][quarter:])]

    mod_half, table_rows, extra = first_call(
        step_index, core[None], hidden_state, modulation.transpose(1, 0, 2), adjoint_rows, text_kv[0]
    )
    mod_near = spread(mod_half)

    w_qkv, w_out, mod_half = pin((w_qkv, w_out, mod_half))
    take = lambda c: lax.dynamic_slice(w_qkv, (0, c, window * HD), (shard, 1, inner))[:, 0]
    own_w = [
        jnp.concatenate([take(0), take(1)], axis=1),
        jnp.concatenate([take(2), lax.dynamic_slice_in_dim(w_out, window * HD, inner, 0).T], axis=1),
    ]
    w_first = [lax.ppermute(part, ("dp", "head"), first_way) for part in own_w]
    w_second = [lax.ppermute(part, ("dp", "head"), second_way) for part in own_w]

    text_dev = text_kv.shape[1]
    mod_far = pass_on(mod_near)
    clip_limit = 0.5 * (tok_count * seq_count * model_width) ** 0.5
    extra, *w_first = pin((extra, *w_first))
    cot_half, clip = cotangent_call(
        clip_limit, scalars, adjoint_rows, table_rows, text_kv[0], extra, *mod_near, mod_far[1]
    )
    cot_half, mod_far[0] = pin((cot_half, mod_far[0]))
    cot_near = spread(cot_half)
    modulated, cotangent, normed_share, scale_share, inv_std, base = local_call(
        own_kernel,
        [((tok_count, model_width + EXTRA), bf16)] * 2
        + [
            ((tok_count, half_width), f32),
            ((1, half_width), f32),
            ((tok_count, 128), f32),
            ((tok_count, half_width), f32),
        ],
        1,
        core[None],
        hidden_state,
        adjoint_rows,
        table_rows,
        text_kv[0],
        extra,
        clip,
        grant=GRANT,
    )
    def pieces(own, received):
        return [own] + [one for moved in received for one in (moved, other_core(moved))]

    mod_far = list(pin((*mod_far, modulated))[:2])
    mod_pieces = pieces(modulated, mod_near + mod_far)
    w_diagonal = [lax.ppermute(part, ("dp", "head"), second_way) for part in w_first]
    weights = [part[n] for n in range(2) for part in (own_w, w_first, w_second, w_diagonal)]
    cot_near[0] = pin((cot_near[0], w_second, w_diagonal))[0]
    cot_far = [step(cot_near[0])]

    cot_pieces = pieces(cotangent, cot_near)
    *cot_pieces, mod_pieces[-1] = pin((*cot_pieces, mod_pieces[-1]))
    *operands, w_keep, w_give = project_call(
        scalars, qk_gain, mod_pieces, weights, slots, tok_count, text_dev, seq_count
    )
    w_give, cot_far[0] = pin((w_give, *cot_far))
    cot_pieces += pieces(None, cot_far)[1:]
    given, *cot_pieces = pin((w_give, *cot_pieces))
    w_other = other_core(given)
    *first, rest = attend_call(
        scalars, qk_gain, operands + [w_keep, w_give], cot_pieces, weights[4:], slots, tok_count, text_dev
    )
    moving = [(a + other_core(b).astype(f32)).astype(bf16) for a, b in zip(first[:2], first[2:])]
    other_rest = other_core(rest)
    rest, other_rest, *_ = pin((rest, other_rest, *moving))
    own = backward_call(rest, other_rest, w_keep, w_other, half_rows, f32)
    for j in range(2, seq_count):
        moving = [step(part) for part in moving]
        moving = [
            (a + b.astype(f32)).astype(bf16) for a, b in zip(own[2 * (j - 2) : 2 * (j - 1)], moving)
        ]
    moving = [step(part) for part in moving]

    grad_scaled, sums = local_call(
        sums_kernel,
        [((tok_count, half_width), f32), ((tok_count, 128), f32)],
        0,
        *own[-2:],
        *moving,
        scale_share,
        normed_share,
    )
    (pulled,) = local_call(
        functools.partial(last_kernel, model_width),
        [((half_width, tok_count), f32)],
        0,
        grad_scaled,
        sums,
        other_core(sums),
        normed_share,
        base,
        inv_std,
    )
    return pulled.T[None]


def qk_normalize(values, gains):
    inverse = lax.rsqrt(jnp.mean(values * values, axis=-1, keepdims=True) + 1e-06)
    return ((values * inverse * gains).astype(jnp.bfloat16), inverse)


def qk_backward(values, inverse, cotangent, gains):
    scaled = cotangent.astype(jnp.float32) * gains
    return (
        scaled * inverse - values * jnp.mean(scaled * values, axis=-1, keepdims=True) * inverse**3
    )


def shards_by_row(states, adjoint, text_kv, text_len, step_index, modulation, w_qkv, qk_gain, w_out):
    hidden_state = states[0]
    adjoint_rows = adjoint[0]
    tok_count, model_width = hidden_state.shape
    seq_count = lax.axis_size("seq")
    inner_dev = w_qkv.shape[2]
    heads_dev = inner_dev // HD
    score_scale = HD ** (-0.5)
    squares = lax.psum(jnp.sum(adjoint_rows * adjoint_rows), "seq")
    clip_limit = 0.5 * (tok_count * seq_count * model_width) ** 0.5
    clip_scale = jnp.minimum(1.0, clip_limit / jnp.sqrt(squares + 1e-06))
    table_row = lax.dynamic_index_in_dim(modulation, step_index[0], 0, keepdims=False)
    offset_row = table_row[0]
    stretch = table_row[1]
    gating = table_row[2]
    widened = hidden_state.astype(jnp.float32)
    centered = widened - jnp.mean(widened, axis=-1, keepdims=True)
    inv_std = lax.rsqrt(jnp.mean(centered * centered, axis=-1, keepdims=True) + 1e-06)
    normed = centered * inv_std
    modulated = (normed * (1.0 + stretch) + offset_row).astype(jnp.bfloat16)
    cotangent = (gating * (clip_scale * adjoint_rows)).astype(jnp.bfloat16)
    contract_last = (((1,), (1,)), ((), ()))
    full_weight = lax.all_gather(w_qkv, "dp", axis=0, tiled=True).reshape(
        model_width, 3 * inner_dev
    )
    projected = jnp.dot(modulated, full_weight, preferred_element_type=jnp.float32)
    out_raw = lax.dot_general(
        cotangent,
        lax.all_gather(w_out, "dp", axis=1, tiled=True),
        contract_last,
        preferred_element_type=jnp.float32,
    )
    projected = projected.reshape(tok_count, 3, heads_dev, HD)
    queries, query_inv = qk_normalize(projected[:, 0], qk_gain[0])
    own_keys, key_inv = qk_normalize(projected[:, 1], qk_gain[1])
    own_values = projected[:, 2].astype(jnp.bfloat16)
    out_grad = out_raw.astype(jnp.bfloat16).reshape(tok_count, heads_dev, HD)
    text_keys = text_kv[0, :, 0, :]
    text_values = text_kv[0, :, 1, :]
    text_dev = text_keys.shape[0]
    rows_dev = tok_count + text_dev
    key_local = jnp.concatenate([own_keys.reshape(tok_count, inner_dev), text_keys], axis=0)
    value_local = jnp.concatenate([own_values.reshape(tok_count, inner_dev), text_values], axis=0)
    key_all, value_all = (
        lax.all_gather(key_local, "seq", axis=0, tiled=True),
        lax.all_gather(value_local, "seq", axis=0, tiled=True),
    )
    all_rows = rows_dev * seq_count
    row_ids = jnp.arange(all_rows, dtype=jnp.int32)
    owner = row_ids // rows_dev
    within = row_ids % rows_dev
    allowed = (within < tok_count) | (owner * text_dev + within - tok_count < text_len[0])
    group = 1
    while group * 2 * rows_dev <= 512 and seq_count % (group * 2) == 0:
        group = group * 2
    block_rows = group * rows_dev
    block_count = all_rows // block_rows
    key_blocks = key_all.reshape(block_count, block_rows, heads_dev, HD)
    value_blocks = value_all.reshape(block_count, block_rows, heads_dev, HD)
    mask_blocks = allowed.reshape(block_count, block_rows)

    def block_scores(key_block, mask_block):
        scores = (
            jnp.einsum("qhd,khd->qhk", queries, key_block, preferred_element_type=jnp.float32)
            * score_scale
        )
        return jnp.where(mask_block[None, None, :], scores, -1e30)

    def first_pass(carry, block):
        row_max, row_sum, row_dot = carry
        key_block, value_block, mask_block = block
        scores = block_scores(key_block, mask_block)
        new_max = jnp.maximum(row_max, jnp.max(scores, axis=-1))
        rescale = jnp.exp(row_max - new_max)
        exps = jnp.exp(scores - new_max[:, :, None])
        grad_weights = jnp.einsum(
            "qhd,khd->qhk", out_grad, value_block, preferred_element_type=jnp.float32
        )
        return (
            (
                new_max,
                row_sum * rescale + jnp.sum(exps, axis=-1),
                row_dot * rescale + jnp.sum(exps * grad_weights, axis=-1),
            ),
            None,
        )

    start_state = (
        jnp.full((tok_count, heads_dev), -1e30, jnp.float32),
        jnp.zeros((tok_count, heads_dev), jnp.float32),
        jnp.zeros((tok_count, heads_dev), jnp.float32),
    )
    (row_max, row_sum, row_dot), unused = lax.scan(
        first_pass, start_state, (key_blocks, value_blocks, mask_blocks)
    )
    log_total = row_max + jnp.log(row_sum)
    delta_row = row_dot / row_sum

    def second_pass(running, block):
        key_block, value_block, mask_block = block
        weights = jnp.exp(block_scores(key_block, mask_block) - log_total[:, :, None])
        grad_weights = jnp.einsum(
            "qhd,khd->qhk", out_grad, value_block, preferred_element_type=jnp.float32
        )
        grad_scores = (weights * (grad_weights - delta_row[:, :, None])).astype(jnp.bfloat16)
        return (
            running
            + jnp.einsum(
                "qhk,khd->qhd", grad_scores, key_block, preferred_element_type=jnp.float32
            ),
            None,
        )

    query_sum, unused = lax.scan(
        second_pass,
        jnp.zeros((tok_count, heads_dev, HD), jnp.float32),
        (key_blocks, value_blocks, mask_blocks),
    )
    grad_query = (query_sum * score_scale).astype(jnp.bfloat16)
    log_all, delta_all = (
        lax.all_gather(log_total, "seq", axis=0, tiled=True),
        lax.all_gather(delta_row, "seq", axis=0, tiled=True),
    )
    local_ids = jnp.arange(rows_dev, dtype=jnp.int32)
    local_allowed = (local_ids < tok_count) | (
        lax.axis_index("seq") * text_dev + local_ids - tok_count < text_len[0]
    )
    key_three = key_local.reshape(rows_dev, heads_dev, HD)
    value_three = value_local.reshape(rows_dev, heads_dev, HD)
    query_piece = lax.all_gather(queries.reshape(tok_count, inner_dev), "seq", axis=0, tiled=True)
    grad_piece = lax.all_gather(out_grad.reshape(tok_count, inner_dev), "seq", axis=0, tiled=True)
    piece_rows = query_piece.shape[0]
    query_rows = query_piece.reshape(piece_rows, heads_dev, HD)
    grad_rows = grad_piece.reshape(piece_rows, heads_dev, HD)
    scores = (
        jnp.einsum("qhd,khd->qhk", query_rows, key_three, preferred_element_type=jnp.float32)
        * score_scale
    )
    scores = jnp.where(local_allowed[None, None, :], scores, -1e30)
    weights = jnp.exp(scores - log_all[:, :, None])
    grad_weights = jnp.einsum(
        "qhd,khd->qhk", grad_rows, value_three, preferred_element_type=jnp.float32
    )
    grad_scores = (weights * (grad_weights - delta_all[:, :, None])).astype(jnp.bfloat16)
    rounded = weights.astype(jnp.bfloat16)
    key_sum = jnp.einsum(
        "qhk,qhd->khd", grad_scores, query_rows, preferred_element_type=jnp.float32
    )
    value_sum = jnp.einsum("qhk,qhd->khd", rounded, grad_rows, preferred_element_type=jnp.float32)
    key_sum, value_sum = (key_sum, value_sum)
    grad_key = (key_sum[:tok_count] * score_scale).astype(jnp.bfloat16)
    grad_value = value_sum[:tok_count].astype(jnp.bfloat16)
    raw_query = qk_backward(projected[:, 0], query_inv, grad_query, qk_gain[0])
    raw_key = qk_backward(projected[:, 1], key_inv, grad_key, qk_gain[1])
    stacked = jnp.stack([raw_query, raw_key, grad_value.astype(jnp.float32)], axis=1).astype(
        jnp.bfloat16
    )
    stacked = stacked.reshape(tok_count, 3 * inner_dev)
    partial_grad = lax.dot_general(
        stacked, full_weight, contract_last, preferred_element_type=jnp.float32
    )
    half_width = model_width // lax.axis_size("head")
    first_col = lax.axis_index("head") * half_width
    grad_share = lax.psum_scatter(
        partial_grad.astype(jnp.bfloat16), "head", scatter_dimension=1, tiled=True
    ).astype(jnp.float32)
    normed_share = lax.dynamic_slice_in_dim(normed, first_col, half_width, 1)
    stretch_share = lax.dynamic_slice_in_dim(stretch, first_col, half_width, 0)
    adjoint_share = lax.dynamic_slice_in_dim(adjoint_rows, first_col, half_width, 1)
    grad_scaled = grad_share * (1.0 + stretch_share)
    row_sums = jnp.stack(
        [jnp.sum(grad_scaled, axis=-1), jnp.sum(grad_scaled * normed_share, axis=-1)], axis=-1
    )
    row_sums = lax.psum(row_sums, "head")
    grad_state = inv_std * (
        grad_scaled - row_sums[:, 0:1] / model_width - normed_share * row_sums[:, 1:2] / model_width
    )
    pulled = clip_scale * adjoint_share + grad_state
    return pulled[None]


def solution(mesh):
    in_specs = (
        P("dp", "seq", None),
        P("dp", "seq", None),
        P("dp", "seq", None, "head"),
        P("dp"),
        P("dp"),
        P(),
        P("dp", None, "head"),
        P(),
        P("head", "dp"),
    )
    out_specs = P("dp", "seq", "head")
    by_head = mesh.shape["seq"] == 4 and mesh.shape["dp"] == 4 and mesh.shape["head"] == 2
    shards = shards_by_head if by_head else shards_by_row
    return jax.shard_map(shards, mesh=mesh, in_specs=in_specs, out_specs=out_specs, check_vma=False)
```

```python
import functools

import jax
import jax.numpy as jnp
from jax import lax
from jax.experimental import pallas as pl
from jax.experimental.pallas import tpu as pltpu
from jax.sharding import PartitionSpec as P

HD = 64
GRANT = 60 * 1024 * 1024
SMALL_GRANT = 24 * 1024 * 1024
EXTRA = 128
NT = (((1,), (1,)), ((), ()))
NN = (((1,), (0,)), ((), ()))


def line_ring(count):
    return [0] + list(range(1, count, 2)) + [i for i in range(count - 1, 0, -1) if i % 2 == 0]


def ring_pairs(order):
    return [(order[i], order[(i + 1) % len(order)]) for i in range(len(order))]


def ring_place(order, index):
    place = jnp.int32(0)
    for position, member in enumerate(order):
        place = jnp.where(index == member, jnp.int32(position), place)
    return place


def ring_member(order, place):
    member = jnp.int32(order[0])
    for position, value in enumerate(order):
        member = jnp.where(place == position, jnp.int32(value), member)
    return member


def dot(a, b, dims):
    return lax.dot_general(a, b, dims, preferred_element_type=jnp.float32)


def equal_blocks(columns, block):
    row = lax.broadcasted_iota(jnp.int32, (columns, columns), 0)
    column = lax.broadcasted_iota(jnp.int32, (columns, columns), 1)
    return jnp.where(row // block == column // block, 1.0, 0.0).astype(jnp.bfloat16)


def head_means(values):
    parts = []
    for first in range(0, values.shape[1], 256):
        part = values[:, first : first + 256]
        ones = equal_blocks(part.shape[1], HD)
        high = part.astype(jnp.bfloat16)
        low = (part - high.astype(jnp.float32)).astype(jnp.bfloat16)
        parts.append(dot(high, ones, NN) + dot(low, ones, NN))
    return jnp.concatenate(parts, axis=1) * (1.0 / HD)


def head_gains(gain, slots):
    return jnp.concatenate([gain[0:1, :]] * slots + [gain[1:2, :]] * slots, axis=1)


def whole_tiles(columns):
    return -(-columns // 128) * 128


def spec(space):
    return pl.BlockSpec(memory_space=space)


def text_columns(text, part):
    rows = text[...].astype(jnp.float32)[:, part, :]
    return [rows[:, c * EXTRA : (c + 1) * EXTRA] for c in range(rows.shape[1] // EXTRA)]


def extra_columns(blocks, rows):
    filled = sum(one.shape[0] for one in blocks)
    blocks = blocks + [jnp.zeros((rows - filled, EXTRA), jnp.float32)]
    return jnp.concatenate(blocks, axis=0).astype(jnp.bfloat16)


def first_kernel(step, core, states, table, adjoint, text, out, rows_out, extra_out):
    rows = [table[c, pl.ds(step[0], 1), :] for c in range(3)]
    widened = states[...].astype(jnp.float32)
    centered = widened - jnp.mean(widened, axis=-1, keepdims=True)
    inv_std = lax.rsqrt(jnp.mean(centered * centered, axis=-1, keepdims=True) + 1e-06)
    half, width = states.shape
    out[:, :width] = (centered * inv_std * (1.0 + rows[1]) + rows[0]).astype(jnp.bfloat16)
    for c in range(3):
        rows_out[c : c + 1, :] = rows[c]
    squares = jnp.sum(adjoint[...] * adjoint[...], axis=0, keepdims=True)
    squares = jnp.sum(squares, axis=1, keepdims=True)
    terms = []
    for n in range(3):
        terms.append(squares.astype(jnp.bfloat16).astype(jnp.float32))
        squares = squares - terms[-1]
    lane = lax.broadcasted_iota(jnp.int32, (8, EXTRA), 1)
    sums = jnp.where(lane == 0, terms[0], jnp.where(lane == 1, terms[1], jnp.where(lane == 2, terms[2], 0.0)))
    extra = extra_columns(text_columns(text, 0) + [sums], half)
    out[:, width:] = extra
    extra_out[...] = extra


def first_call(step, core, states, table, adjoint, text):
    rows, width = states.shape
    half = rows // 2
    whole = lambda *shape: pl.BlockSpec(shape, lambda i, step, core: (0,) * len(shape))
    return pl.pallas_call(
        first_kernel,
        out_shape=(
            jax.ShapeDtypeStruct((half, width + EXTRA), jnp.bfloat16),
            jax.ShapeDtypeStruct((8, width), jnp.float32),
            jax.ShapeDtypeStruct((half, EXTRA), jnp.bfloat16),
        ),
        grid_spec=pltpu.PrefetchScalarGridSpec(
            num_scalar_prefetch=2,
            grid=(1,),
            in_specs=[
                pl.BlockSpec((half, width), lambda i, step, core: (core[0], 0)),
                whole(*table.shape),
                whole(*adjoint.shape),
                whole(*text.shape),
            ],
            out_specs=(whole(half, width + EXTRA), whole(8, width), whole(half, EXTRA)),
        ),
        compiler_params=pltpu.CompilerParams(vmem_limit_bytes=GRANT),
        cost_estimate=pl.CostEstimate(flops=8 * half * width, bytes_accessed=16 * half * width, transcendentals=0),
    )(step, core, states, table, adjoint, text)


def pick_half(core, rows):
    half = rows.shape[1] // 2
    return jnp.where(core == 0, rows[:, :half], rows[:, half:])


def cotangent_kernel(limit, core, adjoint, table_rows, text, extra, previous, following, opposite, out, clip_out):
    first = previous.shape[0] - opposite.shape[0]
    row = 8 * (text.shape[2] // EXTRA)
    squares = opposite[...].astype(jnp.float32)[row - first : row - first + 1, :]
    for terms in (extra, previous, following):
        squares = squares + terms[...].astype(jnp.float32)[row : row + 1, :]
    squares = jnp.sum(squares, axis=1, keepdims=True)
    clip_scale = jnp.minimum(1.0, limit / jnp.sqrt(squares + 1e-06))
    half, width = adjoint.shape
    out[:, :width] = (table_rows[2:3, :] * (clip_scale * adjoint[...])).astype(jnp.bfloat16)
    out[:, width:] = extra_columns(text_columns(text, 1), half)
    clip_out[...] = jnp.broadcast_to(clip_scale, clip_out.shape)


def cotangent_call(limit, core, adjoint, table_rows, text, extra, previous, following, opposite):
    rows, width = adjoint.shape
    half = rows // 2
    block = width // EXTRA
    whole = lambda one: pl.BlockSpec(one.shape, lambda i, core: (0,) * one.ndim)
    tail = lambda one: pl.BlockSpec((one.shape[0], EXTRA), lambda i, core: (0, block))
    outs = (
        jax.ShapeDtypeStruct((half, width + EXTRA), jnp.bfloat16),
        jax.ShapeDtypeStruct((8, EXTRA), jnp.float32),
    )
    return pl.pallas_call(
        functools.partial(cotangent_kernel, limit),
        out_shape=outs,
        grid_spec=pltpu.PrefetchScalarGridSpec(
            num_scalar_prefetch=1,
            grid=(1,),
            in_specs=[pl.BlockSpec((half, width), lambda i, core: (core[0], 0))]
            + [whole(table_rows), whole(text), whole(extra)]
            + [tail(one) for one in (previous, following, opposite)],
            out_specs=tuple(whole(one) for one in outs),
        ),
        compiler_params=pltpu.CompilerParams(vmem_limit_bytes=GRANT),
        cost_estimate=pl.CostEstimate(flops=4 * half * width, bytes_accessed=6 * half * width, transcendentals=0),
    )(core, adjoint, table_rows, text, extra, previous, following, opposite)


def own_kernel(
    core, states, adjoint, table_rows, text, extra, clip, out, cot_out, normed_out, stretch_out, inv_out, base_out
):
    rows, width = states.shape
    half = rows // 2
    widened = states[...].astype(jnp.float32)
    centered = widened - jnp.mean(widened, axis=-1, keepdims=True)
    inv_std = lax.rsqrt(jnp.mean(centered * centered, axis=-1, keepdims=True) + 1e-06)
    normed = centered * inv_std
    scale = 1.0 + table_rows[1:2, :]
    out[:, :width] = (normed * scale + table_rows[0:1, :]).astype(jnp.bfloat16)
    normed_out[...] = pick_half(core[0], normed)
    stretch_out[...] = pick_half(core[0], scale)
    inv_out[...] = jnp.broadcast_to(inv_std, inv_out.shape)
    clipped = clip[0:1, 0:1] * adjoint[...]
    cot_out[:, :width] = (table_rows[2:3, :] * clipped).astype(jnp.bfloat16)
    base_out[...] = pick_half(core[0], clipped)
    columns = extra_columns(text_columns(text, 1), half)
    for n in range(2):
        out[n * half : (n + 1) * half, width:] = extra[...]
        cot_out[n * half : (n + 1) * half, width:] = columns


class Copies:
    def __init__(self, sems):
        self.sems = sems
        self.count = 0

    def start(self, source, target):
        copy = pltpu.make_async_copy(source, target, self.sems.at[self.count])
        copy.start()
        self.count += 1
        return copy

    def weights(self, scalars, w_in, w_all, shard, first=0):
        part = w_in[0].shape[1]
        copies = []
        for n, piece in enumerate(w_in):
            there = n // 4 * (part - first)
            columns = min(part - first, w_all.shape[1] - there)
            copies.append(
                self.start(
                    piece.at[:, pl.ds(first, columns)],
                    w_all.at[
                        pl.ds(pl.multiple_of(scalars[1 + n % 4] * shard, 16), shard),
                        pl.ds(there, columns),
                    ],
                )
            )
        return copies

    def rows(self, core, pieces, target, rows):
        half = rows // 2
        copies = [self.start(pieces[0], target.at[pl.ds(0, rows)])]
        places = [(rows, half), (3 * rows, half)]
        parts = (len(pieces) - 5) // 2
        places += [(2 * rows + n * half // parts, half // parts) for n in range(parts)]
        for n, (first, size) in enumerate(places):
            for m, holder in enumerate((core, 1 - core)):
                there = pl.ds(pl.multiple_of(first + holder * half, 16), size)
                copies.append(self.start(pieces[1 + 2 * n + m], target.at[there]))
        return copies


def window_heads(scalars, count, rows, text_dev, gathered, width, extra, text, text_t=None):
    half = rows // 2
    for k in range(count):
        there = pl.ds(pl.multiple_of(k * rows + scalars[0] * half, 16), half)
        extra[k] = gathered[there, width:].astype(jnp.float32)
    for i in range(text.shape[0]):
        head = scalars[5] + i
        first = pl.ds(pl.multiple_of(head // 2 * text_dev, 8), text_dev)
        found = jnp.concatenate([extra[k, first, :] for k in range(count)], axis=0)
        found = jnp.where(head % 2 == 0, found[:, :HD], found[:, HD:])
        text[i] = found.astype(jnp.bfloat16)
        if text_t is not None:
            text_t[i] = found.T.astype(jnp.bfloat16)


def project_kernel(slots, count, rows, shard, width, text_dev, scalars, gain, *refs):
    refs = list(refs)
    take = lambda n: [refs.pop(0) for _ in range(n)]
    mod_in = take(9)
    w_in = take(8)
    qkv, k_t, raw_all, inv_all, text, text_t, w_keep, w_give = take(8)
    w_all, mod_all, sems, extra, qkv_s, k_t_s, raw_s, inv_s = take(8)
    inner = slots * HD
    core = scalars[0]
    copies = Copies(sems)
    w_copies = copies.weights(scalars, w_in, w_all, shard)
    row_copies = copies.rows(core, mod_in, mod_all, rows)

    lane = lax.broadcasted_iota(jnp.int32, (1, 2 * inner), 1)
    gains = head_gains(gain, slots) * jnp.where(lane < inner, HD ** (-0.5), 1.0)
    identity = equal_blocks(inner, 1)
    for copy in w_copies:
        copy.wait()
    half = width // 2
    out_copies = []
    for holder, target in ((core, w_keep), (1 - core, w_give)):
        source = w_all.at[pl.ds(pl.multiple_of(holder * half, 16), half)]
        out_copies.append(copies.start(source, target))
    for copy in row_copies:
        copy.wait()
    projected = jnp.dot(mod_all[:, :width], w_all[:, : 3 * inner], preferred_element_type=jnp.float32)
    raw = projected[:, : 2 * inner]
    raw_s[...] = raw
    out_copies.append(copies.start(raw_s, raw_all))
    inverse = lax.rsqrt(head_means(raw * raw) + 1e-06)
    inv_s[...] = inverse
    out_copies.append(copies.start(inv_s, inv_all))
    qkv_s[:, : 2 * inner] = (raw * inverse * gains).astype(jnp.bfloat16)
    qkv_s[:, 2 * inner :] = projected[:, 2 * inner :].astype(jnp.bfloat16)
    out_copies.append(copies.start(qkv_s, qkv))
    k_t_s[...] = dot(identity, qkv_s[:, inner : 2 * inner], NT).astype(jnp.bfloat16)
    out_copies.append(copies.start(k_t_s, k_t))
    window_heads(scalars, count, rows, text_dev, mod_all, width, extra, text, text_t)
    for copy in out_copies:
        copy.wait()


def attend_kernel(slots, count, rows, shard, width, text_dev, first_column, scalars, gain, *refs):
    refs = list(refs)
    take = lambda n: [refs.pop(0) for _ in range(n)]
    projected = take(8)
    cot_in = take(7)
    w_in = take(4)
    mine_near, mine_far, theirs_near, theirs_far, rest_out = take(5)
    w_out, cot_all, sems, extra, values_text = take(5)
    d_all, grads, stacked = take(3)
    qkv, k_t, raw_all, inv_all, text, text_t, w_keep, w_give = refs
    inner = slots * HD
    tokens = rows * count
    core = scalars[0]
    copies = Copies(sems)
    w_copies = copies.weights(scalars, w_in, w_out, shard, first_column)
    row_copies = copies.rows(core, cot_in, cot_all, rows)
    local_copies = [copies.start(*one) for one in zip(projected, refs)]
    score_scale = HD ** (-0.5)
    span = 2 * rows

    text_rows = count * text_dev
    row = lax.broadcasted_iota(jnp.int32, (text_rows, span), 0)
    text_id = row
    for k in range(count):
        inside = (row >= k * text_dev) & (row < (k + 1) * text_dev)
        text_id = jnp.where(inside, row + (scalars[7 + k] - k) * text_dev, text_id)
    bias = jnp.where(text_id < scalars[6], 0.0, -1e30)

    for copy in w_copies:
        copy.wait()
    arrivals = [row_copies[:3], row_copies[3:]]
    for b in range(count // 2):
        for copy in arrivals[b]:
            copy.wait()
        here = slice(b * span, (b + 1) * span)
        out_grad = jnp.dot(cot_all[here, :width], w_out[...], preferred_element_type=jnp.float32)
        d_all[here, :] = out_grad.astype(jnp.bfloat16)
    window_heads(scalars, count, rows, text_dev, cot_all, width, extra, values_text)
    for copy in local_copies[:6]:
        copy.wait()

    d_first = d_all.shape[1] - inner
    for i in range(slots):
        columns = [slice(n * inner + i * HD, n * inner + (i + 1) * HD) for n in range(3)]
        keys, values = qkv[:, columns[1]], qkv[:, columns[2]]
        keys_t = k_t[i * HD : (i + 1) * HD, :]
        grad_k, grad_v = 0.0, 0.0
        for b in range(count // 2):
            here = slice(b * span, (b + 1) * span)
            query = qkv[here, columns[0]]
            grad = d_all[here, d_first + i * HD : d_first + (i + 1) * HD]
            scores = dot(keys, query, NT)
            text_scores = dot(text[i], query, NT) + bias
            col_max = jnp.maximum(
                jnp.max(scores, axis=0, keepdims=True), jnp.max(text_scores, axis=0, keepdims=True)
            )
            exps = jnp.exp(scores - col_max)
            text_exps = jnp.exp(text_scores - col_max)
            total = jnp.sum(exps, axis=0, keepdims=True) + jnp.sum(text_exps, axis=0, keepdims=True)
            inverse = 1.0 / total
            grad_w = dot(values, grad, NT)
            text_grad_w = dot(values_text[i], grad, NT)
            delta = inverse * (
                jnp.sum(exps * grad_w, axis=0, keepdims=True)
                + jnp.sum(text_exps * text_grad_w, axis=0, keepdims=True)
            )
            weights = exps * inverse
            grad_s = (weights * (grad_w - delta)).astype(jnp.bfloat16)
            text_grad_s = (text_exps * inverse * (text_grad_w - delta)).astype(jnp.bfloat16)
            grad_k += dot(grad_s, query, NN)
            grad_v += dot(weights.astype(jnp.bfloat16), grad, NN)
            grad_q = dot(keys_t, grad_s, NN) + dot(text_t[i], text_grad_s, NN)
            grads[here, columns[0]] = grad_q.T * score_scale
        grads[:, columns[1]] = grad_k
        grads[:, columns[2]] = grad_v

    lane = lax.broadcasted_iota(jnp.int32, (1, inner), 1)
    mine = jnp.zeros((1, inner), jnp.float32)
    for i in range(slots):
        inside = (lane >= i * HD) & (lane < (i + 1) * HD) & (scalars[7 + count + i] > 0)
        mine = jnp.where(inside, 1.0, mine)
    gains = head_gains(gain, slots)
    for b in range(count // 2):
        here = slice(b * span, (b + 1) * span)
        scaled = grads[here, : 2 * inner].astype(jnp.bfloat16).astype(jnp.float32) * gains
        raw, inverse = raw_all[here, :], inv_all[here, :]
        back = scaled * inverse - raw * head_means(scaled * raw) * (inverse * inverse * inverse)
        valid = jnp.concatenate([mine, mine], axis=1) > 0.0
        stacked[here, : 2 * inner] = jnp.where(valid, back, 0.0).astype(jnp.bfloat16)
        back = jnp.where(mine > 0.0, grads[here, 2 * inner :], 0.0).astype(jnp.bfloat16)
        stacked[here, 2 * inner : 3 * inner] = back
    stacked[:, 3 * inner :] = jnp.zeros((tokens, stacked.shape[1] - 3 * inner), jnp.bfloat16)
    first = stacked[rows : 2 * rows, :]
    rest_out[: (count - 2) * rows, :] = stacked[2 * rows :, :]
    rest_out[(count - 2) * rows :, :] = stacked[:rows, :]
    for copy in local_copies[6:]:
        copy.wait()
    theirs = dot(first, w_give[...], NT).astype(jnp.bfloat16)
    theirs_near[...] = theirs[: rows // 2]
    theirs_far[...] = theirs[rows // 2 :]
    mine = dot(first, w_keep[...], NT)
    mine_near[...] = mine[: rows // 2]
    mine_far[...] = mine[rows // 2 :]


def project_call(scalars, gain, mod, weights, slots, rows, text_dev, count):
    shard = weights[0].shape[0]
    columns = whole_tiles(3 * slots * HD)
    width = mod[0].shape[1] - EXTRA
    tokens = rows * count
    text_rows = text_dev * count
    f32, bf16 = jnp.float32, jnp.bfloat16
    vmem, hbm = spec(pltpu.VMEM), spec(pl.ANY)
    inner = slots * HD
    shapes = [((tokens, 3 * inner), bf16), ((inner, tokens), bf16)] + [((tokens, 2 * inner), f32)] * 2
    shapes += [((slots, text_rows, HD), bf16), ((slots, HD, text_rows), bf16)]
    shapes += [((width // 2, whole_tiles(3 * slots * HD)), bf16)] * 2
    return pl.pallas_call(
        functools.partial(project_kernel, slots, count, rows, shard, width, text_dev),
        out_shape=tuple(jax.ShapeDtypeStruct(*one) for one in shapes),
        in_specs=[spec(pltpu.SMEM), vmem] + [hbm] * (len(mod) + len(weights)),
        out_specs=(hbm,) * 4 + (vmem,) * 2 + (hbm,) * 2,
        scratch_shapes=[
            pltpu.VMEM((width, columns), bf16),
            pltpu.VMEM((tokens, width + EXTRA), bf16),
            pltpu.SemaphoreType.DMA((len(mod) + len(weights) + 10,)),
            pltpu.VMEM((count, rows // 2, EXTRA), f32),
        ]
        + [pltpu.VMEM(*one) for one in shapes[:4]],
        compiler_params=pltpu.CompilerParams(vmem_limit_bytes=GRANT),
        cost_estimate=pl.CostEstimate(
            flops=2 * tokens * width * 3 * slots * HD,
            bytes_accessed=2 * (tokens * width + columns * width) + 4 * tokens * columns,
            transcendentals=0,
        ),
    )(scalars, gain, *mod, *weights)


def attend_call(scalars, gain, operands, cot, weights, slots, rows, text_dev):
    count = operands[0].shape[0] // rows
    shard, columns = weights[0].shape
    width = cot[0].shape[1] - EXTRA
    tokens = rows * count
    inner = slots * HD
    stacked = whole_tiles(3 * inner)
    first = (columns - inner) // 128 * 128
    f32, bf16 = jnp.float32, jnp.bfloat16
    vmem, hbm = spec(pltpu.VMEM), spec(pl.ANY)
    part = (rows // 2, width // 2)
    shapes = [(part, f32)] * 2 + [(part, bf16)] * 2 + [((tokens - rows, stacked), bf16)]
    return pl.pallas_call(
        functools.partial(attend_kernel, slots, count, rows, shard, width, text_dev, first),
        out_shape=tuple(jax.ShapeDtypeStruct(*one) for one in shapes),
        in_specs=[spec(pltpu.SMEM), vmem] + [hbm] * (len(operands) + len(cot) + len(weights)),
        out_specs=(vmem,) * len(shapes),
        scratch_shapes=[
            pltpu.VMEM((width, columns - first), bf16),
            pltpu.VMEM((tokens, width + EXTRA), bf16),
            pltpu.SemaphoreType.DMA((len(operands) + len(cot) + len(weights),)),
            pltpu.VMEM((count, rows // 2, EXTRA), f32),
            pltpu.VMEM((slots, text_dev * count, HD), bf16),
            pltpu.VMEM((tokens, columns - first), bf16),
            pltpu.VMEM((tokens, 3 * inner), f32),
            pltpu.VMEM((tokens, stacked), bf16),
        ]
        + [pltpu.VMEM(one.shape, one.dtype) for one in operands],
        compiler_params=pltpu.CompilerParams(vmem_limit_bytes=GRANT),
        cost_estimate=pl.CostEstimate(
            flops=2 * tokens * width * inner + 10 * tokens * tokens * inner,
            bytes_accessed=2 * (tokens * width + columns * width),
            transcendentals=slots * tokens * tokens,
        ),
    )(scalars, gain, *operands, *cot, *weights)


def backward_kernel(own, other, w_own, w_other, *outs):
    total = dot(own[...], w_own[...], NT) + dot(other[...], w_other[...], NT)
    part = outs[0].shape[0]
    for n, out in enumerate(outs):
        out[...] = total[n * part : (n + 1) * part].astype(out.dtype)


def backward_call(own, other, w_own, w_other, part, dtype):
    rows, inner = own.shape
    half = w_own.shape[0]
    vmem = spec(pltpu.VMEM)
    return pl.pallas_call(
        backward_kernel,
        out_shape=(jax.ShapeDtypeStruct((part, half), dtype),) * (rows // part),
        in_specs=[vmem] * 4,
        out_specs=(vmem,) * (rows // part),
        compiler_params=pltpu.CompilerParams(vmem_limit_bytes=SMALL_GRANT),
        cost_estimate=pl.CostEstimate(
            flops=4 * rows * half * inner,
            bytes_accessed=4 * (rows + half) * inner + 4 * rows * half,
            transcendentals=0,
        ),
    )(own, other, w_own, w_other)


def sums_kernel(own_near, own_far, near, far, scale, normed, grad_out, sums_out):
    half = near.shape[0]
    for part, (own, moving) in enumerate(((own_near, near), (own_far, far))):
        here = slice(part * half, (part + 1) * half)
        grad = (own[...] + moving[...].astype(jnp.float32)) * scale[...]
        grad_out[here, :] = grad
        first = jnp.sum(grad, axis=-1, keepdims=True)
        second = jnp.sum(grad * normed[here, :], axis=-1, keepdims=True)
        lane = lax.broadcasted_iota(jnp.int32, (half, 128), 1)
        sums_out[here, :] = jnp.where(lane == 0, first, second)


def last_kernel(width, grad, sums, other, normed, base, inv_std, out):
    total = (sums[...] + other[...]) * (1.0 / width)
    rows = base[...] + inv_std[:, 0:1] * (
        grad[...] - total[:, 0:1] - normed[...] * total[:, 1:2]
    )
    out[...] = rows.T


def local_call(kernel, shapes, scalar_count, *operands, grant=SMALL_GRANT):
    vmem = spec(pltpu.VMEM)
    return pl.pallas_call(
        kernel,
        out_shape=tuple(jax.ShapeDtypeStruct(*one) for one in shapes),
        in_specs=[spec(pltpu.SMEM)] * scalar_count + [vmem] * (len(operands) - scalar_count),
        out_specs=(vmem,) * len(shapes),
        compiler_params=pltpu.CompilerParams(vmem_limit_bytes=grant),
        cost_estimate=pl.CostEstimate(
            flops=sum(one.size for one in operands),
            bytes_accessed=sum(one.size * one.dtype.itemsize for one in operands),
            transcendentals=0,
        ),
    )(*operands)


def shards_by_head(states, adjoint, text_kv, text_len, step_index, modulation, w_qkv, qk_gain, w_out):
    hidden_state = states[0]
    adjoint_rows = adjoint[0]
    tok_count, model_width = hidden_state.shape
    seq_count = lax.axis_size("seq")
    inner_dev = w_qkv.shape[2]
    heads_dev = inner_dev // HD
    shard = w_qkv.shape[0]
    slots = -(-heads_dev // seq_count)
    inner = slots * HD
    half_rows = tok_count // 2
    half_width = model_width // 2
    f32, bf16 = jnp.float32, jnp.bfloat16
    core = lax.axis_index("head").astype(jnp.int32)
    seq_index = lax.axis_index("seq")
    dp_index = lax.axis_index("dp")
    pin = lax.optimization_barrier

    seq_order = line_ring(seq_count)
    seq_place = ring_place(seq_order, seq_index)
    seq_next = ring_pairs(seq_order)
    swap = [(0, 1), (1, 0)]
    first_way = [(2 * p + c, 2 * (p ^ (1 + c)) + c) for p in range(4) for c in range(2)]
    second_way = [(2 * p + c, 2 * (p ^ (2 - c)) + c) for p in range(4) for c in range(2)]

    first = seq_index * heads_dev // seq_count
    stop = (seq_index + 1) * heads_dev // seq_count
    window = jnp.minimum(first, heads_dev - slots)
    valid = [(window + i >= first) & (window + i < stop) for i in range(slots)]
    owners = [ring_member(seq_order, (seq_place - k + seq_count) % seq_count) for k in range(seq_count)]
    w_index = [dp_index, dp_index ^ (1 + core), dp_index ^ (2 - core), dp_index ^ 3]
    scalars = [core] + w_index + [window, text_len[0]] + owners + valid
    scalars = jnp.stack([one.astype(jnp.int32) for one in scalars])

    def step(moving):
        return lax.ppermute(moving, "seq", seq_next)

    def other_core(moving):
        return lax.ppermute(moving, "head", swap)

    def step_back(moving):
        return lax.ppermute(moving, "seq", [(b, a) for a, b in seq_next])

    quarter = half_rows // 2

    def spread(moving):
        return [step(moving), step_back(moving)]

    def pass_on(received):
        return [step(received[0][:quarter]), step_back(received[1][quarter:])]

    mod_half, table_rows, extra = first_call(
        step_index, core[None], hidden_state, modulation.transpose(1, 0, 2), adjoint_rows, text_kv[0]
    )
    mod_near = spread(mod_half)

    w_qkv, w_out, mod_half = pin((w_qkv, w_out, mod_half))
    take = lambda c: lax.dynamic_slice(w_qkv, (0, c, window * HD), (shard, 1, inner))[:, 0]
    own_w = [
        jnp.concatenate([take(0), take(1)], axis=1),
        jnp.concatenate([take(2), lax.dynamic_slice_in_dim(w_out, window * HD, inner, 0).T], axis=1),
    ]
    w_first = [lax.ppermute(part, ("dp", "head"), first_way) for part in own_w]
    w_second = [lax.ppermute(part, ("dp", "head"), second_way) for part in own_w]

    text_dev = text_kv.shape[1]
    mod_far = pass_on(mod_near)
    clip_limit = 0.5 * (tok_count * seq_count * model_width) ** 0.5
    extra, *w_first = pin((extra, *w_first))
    cot_half, clip = cotangent_call(
        clip_limit, scalars, adjoint_rows, table_rows, text_kv[0], extra, *mod_near, mod_far[1]
    )
    cot_half, mod_far[0] = pin((cot_half, mod_far[0]))
    cot_near = spread(cot_half)
    modulated, cotangent, normed_share, scale_share, inv_std, base = local_call(
        own_kernel,
        [((tok_count, model_width + EXTRA), bf16)] * 2
        + [
            ((tok_count, half_width), f32),
            ((1, half_width), f32),
            ((tok_count, 128), f32),
            ((tok_count, half_width), f32),
        ],
        1,
        core[None],
        hidden_state,
        adjoint_rows,
        table_rows,
        text_kv[0],
        extra,
        clip,
        grant=GRANT,
    )
    def pieces(own, received):
        return [own] + [one for moved in received for one in (moved, other_core(moved))]

    mod_far = list(pin((*mod_far, modulated))[:2])
    mod_pieces = pieces(modulated, mod_near + mod_far)
    w_diagonal = [lax.ppermute(part, ("dp", "head"), second_way) for part in w_first]
    weights = [part[n] for n in range(2) for part in (own_w, w_first, w_second, w_diagonal)]
    cot_near[0] = pin((cot_near[0], w_second, w_diagonal))[0]
    cot_far = [step(cot_near[0])]

    cot_pieces = pieces(cotangent, cot_near)
    *cot_pieces, mod_pieces[-1] = pin((*cot_pieces, mod_pieces[-1]))
    *operands, w_keep, w_give = project_call(
        scalars, qk_gain, mod_pieces, weights, slots, tok_count, text_dev, seq_count
    )
    w_give, cot_far[0] = pin((w_give, *cot_far))
    cot_pieces += pieces(None, cot_far)[1:]
    given, *cot_pieces = pin((w_give, *cot_pieces))
    w_other = other_core(given)
    *first, rest = attend_call(
        scalars, qk_gain, operands + [w_keep, w_give], cot_pieces, weights[4:], slots, tok_count, text_dev
    )
    moving = [(a + other_core(b).astype(f32)).astype(bf16) for a, b in zip(first[:2], first[2:])]
    other_rest = other_core(rest)
    rest, other_rest, *_ = pin((rest, other_rest, *moving))
    own = backward_call(rest, other_rest, w_keep, w_other, half_rows, f32)
    for j in range(2, seq_count):
        moving = [step(part) for part in moving]
        moving = [
            (a + b.astype(f32)).astype(bf16) for a, b in zip(own[2 * (j - 2) : 2 * (j - 1)], moving)
        ]
    moving = [step(part) for part in moving]

    grad_scaled, sums = local_call(
        sums_kernel,
        [((tok_count, half_width), f32), ((tok_count, 128), f32)],
        0,
        *own[-2:],
        *moving,
        scale_share,
        normed_share,
    )
    (pulled,) = local_call(
        functools.partial(last_kernel, model_width),
        [((half_width, tok_count), f32)],
        0,
        grad_scaled,
        sums,
        other_core(sums),
        normed_share,
        base,
        inv_std,
    )
    return pulled.T[None]


def qk_normalize(values, gains):
    inverse = lax.rsqrt(jnp.mean(values * values, axis=-1, keepdims=True) + 1e-06)
    return ((values * inverse * gains).astype(jnp.bfloat16), inverse)


def qk_backward(values, inverse, cotangent, gains):
    scaled = cotangent.astype(jnp.float32) * gains
    return (
        scaled * inverse - values * jnp.mean(scaled * values, axis=-1, keepdims=True) * inverse**3
    )


def shards_by_row(states, adjoint, text_kv, text_len, step_index, modulation, w_qkv, qk_gain, w_out):
    hidden_state = states[0]
    adjoint_rows = adjoint[0]
    tok_count, model_width = hidden_state.shape
    seq_count = lax.axis_size("seq")
    inner_dev = w_qkv.shape[2]
    heads_dev = inner_dev // HD
    score_scale = HD ** (-0.5)
    squares = lax.psum(jnp.sum(adjoint_rows * adjoint_rows), "seq")
    clip_limit = 0.5 * (tok_count * seq_count * model_width) ** 0.5
    clip_scale = jnp.minimum(1.0, clip_limit / jnp.sqrt(squares + 1e-06))
    table_row = lax.dynamic_index_in_dim(modulation, step_index[0], 0, keepdims=False)
    offset_row = table_row[0]
    stretch = table_row[1]
    gating = table_row[2]
    widened = hidden_state.astype(jnp.float32)
    centered = widened - jnp.mean(widened, axis=-1, keepdims=True)
    inv_std = lax.rsqrt(jnp.mean(centered * centered, axis=-1, keepdims=True) + 1e-06)
    normed = centered * inv_std
    modulated = (normed * (1.0 + stretch) + offset_row).astype(jnp.bfloat16)
    cotangent = (gating * (clip_scale * adjoint_rows)).astype(jnp.bfloat16)
    contract_last = (((1,), (1,)), ((), ()))
    full_weight = lax.all_gather(w_qkv, "dp", axis=0, tiled=True).reshape(
        model_width, 3 * inner_dev
    )
    projected = jnp.dot(modulated, full_weight, preferred_element_type=jnp.float32)
    out_raw = lax.dot_general(
        cotangent,
        lax.all_gather(w_out, "dp", axis=1, tiled=True),
        contract_last,
        preferred_element_type=jnp.float32,
    )
    projected = projected.reshape(tok_count, 3, heads_dev, HD)
    queries, query_inv = qk_normalize(projected[:, 0], qk_gain[0])
    own_keys, key_inv = qk_normalize(projected[:, 1], qk_gain[1])
    own_values = projected[:, 2].astype(jnp.bfloat16)
    out_grad = out_raw.astype(jnp.bfloat16).reshape(tok_count, heads_dev, HD)
    text_keys = text_kv[0, :, 0, :]
    text_values = text_kv[0, :, 1, :]
    text_dev = text_keys.shape[0]
    rows_dev = tok_count + text_dev
    key_local = jnp.concatenate([own_keys.reshape(tok_count, inner_dev), text_keys], axis=0)
    value_local = jnp.concatenate([own_values.reshape(tok_count, inner_dev), text_values], axis=0)
    key_all, value_all = (
        lax.all_gather(key_local, "seq", axis=0, tiled=True),
        lax.all_gather(value_local, "seq", axis=0, tiled=True),
    )
    all_rows = rows_dev * seq_count
    row_ids = jnp.arange(all_rows, dtype=jnp.int32)
    owner = row_ids // rows_dev
    within = row_ids % rows_dev
    allowed = (within < tok_count) | (owner * text_dev + within - tok_count < text_len[0])
    group = 1
    while group * 2 * rows_dev <= 512 and seq_count % (group * 2) == 0:
        group = group * 2
    block_rows = group * rows_dev
    block_count = all_rows // block_rows
    key_blocks = key_all.reshape(block_count, block_rows, heads_dev, HD)
    value_blocks = value_all.reshape(block_count, block_rows, heads_dev, HD)
    mask_blocks = allowed.reshape(block_count, block_rows)

    def block_scores(key_block, mask_block):
        scores = (
            jnp.einsum("qhd,khd->qhk", queries, key_block, preferred_element_type=jnp.float32)
            * score_scale
        )
        return jnp.where(mask_block[None, None, :], scores, -1e30)

    def first_pass(carry, block):
        row_max, row_sum, row_dot = carry
        key_block, value_block, mask_block = block
        scores = block_scores(key_block, mask_block)
        new_max = jnp.maximum(row_max, jnp.max(scores, axis=-1))
        rescale = jnp.exp(row_max - new_max)
        exps = jnp.exp(scores - new_max[:, :, None])
        grad_weights = jnp.einsum(
            "qhd,khd->qhk", out_grad, value_block, preferred_element_type=jnp.float32
        )
        return (
            (
                new_max,
                row_sum * rescale + jnp.sum(exps, axis=-1),
                row_dot * rescale + jnp.sum(exps * grad_weights, axis=-1),
            ),
            None,
        )

    start_state = (
        jnp.full((tok_count, heads_dev), -1e30, jnp.float32),
        jnp.zeros((tok_count, heads_dev), jnp.float32),
        jnp.zeros((tok_count, heads_dev), jnp.float32),
    )
    (row_max, row_sum, row_dot), unused = lax.scan(
        first_pass, start_state, (key_blocks, value_blocks, mask_blocks)
    )
    log_total = row_max + jnp.log(row_sum)
    delta_row = row_dot / row_sum

    def second_pass(running, block):
        key_block, value_block, mask_block = block
        weights = jnp.exp(block_scores(key_block, mask_block) - log_total[:, :, None])
        grad_weights = jnp.einsum(
            "qhd,khd->qhk", out_grad, value_block, preferred_element_type=jnp.float32
        )
        grad_scores = (weights * (grad_weights - delta_row[:, :, None])).astype(jnp.bfloat16)
        return (
            running
            + jnp.einsum(
                "qhk,khd->qhd", grad_scores, key_block, preferred_element_type=jnp.float32
            ),
            None,
        )

    query_sum, unused = lax.scan(
        second_pass,
        jnp.zeros((tok_count, heads_dev, HD), jnp.float32),
        (key_blocks, value_blocks, mask_blocks),
    )
    grad_query = (query_sum * score_scale).astype(jnp.bfloat16)
    log_all, delta_all = (
        lax.all_gather(log_total, "seq", axis=0, tiled=True),
        lax.all_gather(delta_row, "seq", axis=0, tiled=True),
    )
    local_ids = jnp.arange(rows_dev, dtype=jnp.int32)
    local_allowed = (local_ids < tok_count) | (
        lax.axis_index("seq") * text_dev + local_ids - tok_count < text_len[0]
    )
    key_three = key_local.reshape(rows_dev, heads_dev, HD)
    value_three = value_local.reshape(rows_dev, heads_dev, HD)
    query_piece = lax.all_gather(queries.reshape(tok_count, inner_dev), "seq", axis=0, tiled=True)
    grad_piece = lax.all_gather(out_grad.reshape(tok_count, inner_dev), "seq", axis=0, tiled=True)
    piece_rows = query_piece.shape[0]
    query_rows = query_piece.reshape(piece_rows, heads_dev, HD)
    grad_rows = grad_piece.reshape(piece_rows, heads_dev, HD)
    scores = (
        jnp.einsum("qhd,khd->qhk", query_rows, key_three, preferred_element_type=jnp.float32)
        * score_scale
    )
    scores = jnp.where(local_allowed[None, None, :], scores, -1e30)
    weights = jnp.exp(scores - log_all[:, :, None])
    grad_weights = jnp.einsum(
        "qhd,khd->qhk", grad_rows, value_three, preferred_element_type=jnp.float32
    )
    grad_scores = (weights * (grad_weights - delta_all[:, :, None])).astype(jnp.bfloat16)
    rounded = weights.astype(jnp.bfloat16)
    key_sum = jnp.einsum(
        "qhk,qhd->khd", grad_scores, query_rows, preferred_element_type=jnp.float32
    )
    value_sum = jnp.einsum("qhk,qhd->khd", rounded, grad_rows, preferred_element_type=jnp.float32)
    key_sum, value_sum = (key_sum, value_sum)
    grad_key = (key_sum[:tok_count] * score_scale).astype(jnp.bfloat16)
    grad_value = value_sum[:tok_count].astype(jnp.bfloat16)
    raw_query = qk_backward(projected[:, 0], query_inv, grad_query, qk_gain[0])
    raw_key = qk_backward(projected[:, 1], key_inv, grad_key, qk_gain[1])
    stacked = jnp.stack([raw_query, raw_key, grad_value.astype(jnp.float32)], axis=1).astype(
        jnp.bfloat16
    )
    stacked = stacked.reshape(tok_count, 3 * inner_dev)
    partial_grad = lax.dot_general(
        stacked, full_weight, contract_last, preferred_element_type=jnp.float32
    )
    half_width = model_width // lax.axis_size("head")
    first_col = lax.axis_index("head") * half_width
    grad_share = lax.psum_scatter(
        partial_grad.astype(jnp.bfloat16), "head", scatter_dimension=1, tiled=True
    ).astype(jnp.float32)
    normed_share = lax.dynamic_slice_in_dim(normed, first_col, half_width, 1)
    stretch_share = lax.dynamic_slice_in_dim(stretch, first_col, half_width, 0)
    adjoint_share = lax.dynamic_slice_in_dim(adjoint_rows, first_col, half_width, 1)
    grad_scaled = grad_share * (1.0 + stretch_share)
    row_sums = jnp.stack(
        [jnp.sum(grad_scaled, axis=-1), jnp.sum(grad_scaled * normed_share, axis=-1)], axis=-1
    )
    row_sums = lax.psum(row_sums, "head")
    grad_state = inv_std * (
        grad_scaled - row_sums[:, 0:1] / model_width - normed_share * row_sums[:, 1:2] / model_width
    )
    pulled = clip_scale * adjoint_share + grad_state
    return pulled[None]


def solution(mesh):
    in_specs = (
        P("dp", "seq", None),
        P("dp", "seq", None),
        P("dp", "seq", None, "head"),
        P("dp"),
        P("dp"),
        P(),
        P("dp", None, "head"),
        P(),
        P("head", "dp"),
    )
    out_specs = P("dp", "seq", "head")
    by_head = mesh.shape["seq"] == 4 and mesh.shape["dp"] == 4 and mesh.shape["head"] == 2
    shards = shards_by_head if by_head else shards_by_row
    return jax.shard_map(shards, mesh=mesh, in_specs=in_specs, out_specs=out_specs, check_vma=False)
```

```python
import functools

import jax
import jax.numpy as jnp
from jax import lax
from jax.experimental import pallas as pl
from jax.experimental.pallas import tpu as pltpu
from jax.sharding import PartitionSpec as P

HD = 64
GRANT = 60 * 1024 * 1024
SMALL_GRANT = 24 * 1024 * 1024
EXTRA = 128
NT = (((1,), (1,)), ((), ()))
NN = (((1,), (0,)), ((), ()))


def line_ring(count):
    return [0] + list(range(1, count, 2)) + [i for i in range(count - 1, 0, -1) if i % 2 == 0]


def ring_pairs(order):
    return [(order[i], order[(i + 1) % len(order)]) for i in range(len(order))]


def ring_place(order, index):
    place = jnp.int32(0)
    for position, member in enumerate(order):
        place = jnp.where(index == member, jnp.int32(position), place)
    return place


def ring_member(order, place):
    member = jnp.int32(order[0])
    for position, value in enumerate(order):
        member = jnp.where(place == position, jnp.int32(value), member)
    return member


def dot(a, b, dims):
    return lax.dot_general(a, b, dims, preferred_element_type=jnp.float32)


def equal_blocks(columns, block):
    row = lax.broadcasted_iota(jnp.int32, (columns, columns), 0)
    column = lax.broadcasted_iota(jnp.int32, (columns, columns), 1)
    return jnp.where(row // block == column // block, 1.0, 0.0).astype(jnp.bfloat16)


def head_means(values):
    parts = []
    for first in range(0, values.shape[1], 256):
        part = values[:, first : first + 256]
        ones = equal_blocks(part.shape[1], HD)
        high = part.astype(jnp.bfloat16)
        low = (part - high.astype(jnp.float32)).astype(jnp.bfloat16)
        parts.append(dot(high, ones, NN) + dot(low, ones, NN))
    return jnp.concatenate(parts, axis=1) * (1.0 / HD)


def head_gains(gain, slots):
    return jnp.concatenate([gain[0:1, :]] * slots + [gain[1:2, :]] * slots, axis=1)


def whole_tiles(columns):
    return -(-columns // 128) * 128


def spec(space):
    return pl.BlockSpec(memory_space=space)


def text_columns(text, part):
    rows = text[...].astype(jnp.float32)[:, part, :]
    return [rows[:, c * EXTRA : (c + 1) * EXTRA] for c in range(rows.shape[1] // EXTRA)]


def extra_columns(blocks, rows):
    filled = sum(one.shape[0] for one in blocks)
    blocks = blocks + [jnp.zeros((rows - filled, EXTRA), jnp.float32)]
    return jnp.concatenate(blocks, axis=0).astype(jnp.bfloat16)


def first_kernel(step, core, states, table, adjoint, text, out, rows_out, extra_out):
    rows = [table[c, pl.ds(step[0] % 8, 1), :] for c in range(3)]
    widened = states[...].astype(jnp.float32)
    centered = widened - jnp.mean(widened, axis=-1, keepdims=True)
    inv_std = lax.rsqrt(jnp.mean(centered * centered, axis=-1, keepdims=True) + 1e-06)
    half, width = states.shape
    out[:, :width] = (centered * inv_std * (1.0 + rows[1]) + rows[0]).astype(jnp.bfloat16)
    for c in range(3):
        rows_out[c : c + 1, :] = rows[c]
    squares = jnp.sum(adjoint[...] * adjoint[...], axis=0, keepdims=True)
    squares = jnp.sum(squares, axis=1, keepdims=True)
    terms = []
    for n in range(3):
        terms.append(squares.astype(jnp.bfloat16).astype(jnp.float32))
        squares = squares - terms[-1]
    lane = lax.broadcasted_iota(jnp.int32, (8, EXTRA), 1)
    sums = jnp.where(lane == 0, terms[0], jnp.where(lane == 1, terms[1], jnp.where(lane == 2, terms[2], 0.0)))
    extra = extra_columns(text_columns(text, 0) + [sums], half)
    out[:, width:] = extra
    extra_out[...] = extra


def first_call(step, core, states, table, adjoint, text):
    rows, width = states.shape
    half = rows // 2
    whole = lambda *shape: pl.BlockSpec(shape, lambda i, step, core: (0,) * len(shape))
    return pl.pallas_call(
        first_kernel,
        out_shape=(
            jax.ShapeDtypeStruct((half, width + EXTRA), jnp.bfloat16),
            jax.ShapeDtypeStruct((8, width), jnp.float32),
            jax.ShapeDtypeStruct((half, EXTRA), jnp.bfloat16),
        ),
        grid_spec=pltpu.PrefetchScalarGridSpec(
            num_scalar_prefetch=2,
            grid=(1,),
            in_specs=[
                pl.BlockSpec((half, width), lambda i, step, core: (core[0], 0)),
                pl.BlockSpec((3, 8, width), lambda i, step, core: (0, step[0] // 8, 0)),
                whole(*adjoint.shape),
                whole(*text.shape),
            ],
            out_specs=(whole(half, width + EXTRA), whole(8, width), whole(half, EXTRA)),
        ),
        compiler_params=pltpu.CompilerParams(vmem_limit_bytes=GRANT),
        cost_estimate=pl.CostEstimate(flops=8 * half * width, bytes_accessed=16 * half * width, transcendentals=0),
    )(step, core, states, table, adjoint, text)


def pick_half(core, rows):
    half = rows.shape[1] // 2
    return jnp.where(core == 0, rows[:, :half], rows[:, half:])


def cotangent_kernel(limit, core, adjoint, table_rows, text, extra, previous, following, opposite, out, clip_out):
    first = previous.shape[0] - opposite.shape[0]
    row = 8 * (text.shape[2] // EXTRA)
    squares = opposite[...].astype(jnp.float32)[row - first : row - first + 1, :]
    for terms in (extra, previous, following):
        squares = squares + terms[...].astype(jnp.float32)[row : row + 1, :]
    squares = jnp.sum(squares, axis=1, keepdims=True)
    clip_scale = jnp.minimum(1.0, limit / jnp.sqrt(squares + 1e-06))
    half, width = adjoint.shape
    out[:, :width] = (table_rows[2:3, :] * (clip_scale * adjoint[...])).astype(jnp.bfloat16)
    out[:, width:] = extra_columns(text_columns(text, 1), half)
    clip_out[...] = jnp.broadcast_to(clip_scale, clip_out.shape)


def cotangent_call(limit, core, adjoint, table_rows, text, extra, previous, following, opposite):
    rows, width = adjoint.shape
    half = rows // 2
    block = width // EXTRA
    whole = lambda one: pl.BlockSpec(one.shape, lambda i, core: (0,) * one.ndim)
    tail = lambda one: pl.BlockSpec((one.shape[0], EXTRA), lambda i, core: (0, block))
    outs = (
        jax.ShapeDtypeStruct((half, width + EXTRA), jnp.bfloat16),
        jax.ShapeDtypeStruct((8, EXTRA), jnp.float32),
    )
    return pl.pallas_call(
        functools.partial(cotangent_kernel, limit),
        out_shape=outs,
        grid_spec=pltpu.PrefetchScalarGridSpec(
            num_scalar_prefetch=1,
            grid=(1,),
            in_specs=[pl.BlockSpec((half, width), lambda i, core: (core[0], 0))]
            + [whole(table_rows), whole(text), whole(extra)]
            + [tail(one) for one in (previous, following, opposite)],
            out_specs=tuple(whole(one) for one in outs),
        ),
        compiler_params=pltpu.CompilerParams(vmem_limit_bytes=GRANT),
        cost_estimate=pl.CostEstimate(flops=4 * half * width, bytes_accessed=6 * half * width, transcendentals=0),
    )(core, adjoint, table_rows, text, extra, previous, following, opposite)


def own_kernel(
    core, states, adjoint, table_rows, text, extra, clip, out, cot_out, normed_out, stretch_out, inv_out, base_out
):
    rows, width = states.shape
    half = rows // 2
    widened = states[...].astype(jnp.float32)
    centered = widened - jnp.mean(widened, axis=-1, keepdims=True)
    inv_std = lax.rsqrt(jnp.mean(centered * centered, axis=-1, keepdims=True) + 1e-06)
    normed = centered * inv_std
    scale = 1.0 + table_rows[1:2, :]
    out[:, :width] = (normed * scale + table_rows[0:1, :]).astype(jnp.bfloat16)
    normed_out[...] = pick_half(core[0], normed)
    stretch_out[...] = pick_half(core[0], scale)
    inv_out[...] = jnp.broadcast_to(inv_std, inv_out.shape)
    clipped = clip[0:1, 0:1] * adjoint[...]
    cot_out[:, :width] = (table_rows[2:3, :] * clipped).astype(jnp.bfloat16)
    base_out[...] = pick_half(core[0], clipped)
    columns = extra_columns(text_columns(text, 1), half)
    for n in range(2):
        out[n * half : (n + 1) * half, width:] = extra[...]
        cot_out[n * half : (n + 1) * half, width:] = columns


class Copies:
    def __init__(self, sems):
        self.sems = sems
        self.count = 0

    def start(self, source, target):
        copy = pltpu.make_async_copy(source, target, self.sems.at[self.count])
        copy.start()
        self.count += 1
        return copy

    def weights(self, scalars, w_in, w_all, shard, first=0):
        part = w_in[0].shape[1]
        copies = []
        for n, piece in enumerate(w_in):
            there = n // 4 * (part - first)
            columns = min(part - first, w_all.shape[1] - there)
            copies.append(
                self.start(
                    piece.at[:, pl.ds(first, columns)],
                    w_all.at[
                        pl.ds(pl.multiple_of(scalars[1 + n % 4] * shard, 16), shard),
                        pl.ds(there, columns),
                    ],
                )
            )
        return copies

    def rows(self, core, pieces, target, rows):
        half = rows // 2
        copies = [self.start(pieces[0], target.at[pl.ds(0, rows)])]
        places = [(rows, half), (3 * rows, half)]
        parts = (len(pieces) - 5) // 2
        places += [(2 * rows + n * half // parts, half // parts) for n in range(parts)]
        for n, (first, size) in enumerate(places):
            for m, holder in enumerate((core, 1 - core)):
                there = pl.ds(pl.multiple_of(first + holder * half, 16), size)
                copies.append(self.start(pieces[1 + 2 * n + m], target.at[there]))
        return copies


def window_heads(scalars, count, rows, text_dev, gathered, width, extra, text, text_t=None):
    half = rows // 2
    for k in range(count):
        there = pl.ds(pl.multiple_of(k * rows + scalars[0] * half, 16), half)
        extra[k] = gathered[there, width:].astype(jnp.float32)
    for i in range(text.shape[0]):
        head = scalars[5] + i
        first = pl.ds(pl.multiple_of(head // 2 * text_dev, 8), text_dev)
        found = jnp.concatenate([extra[k, first, :] for k in range(count)], axis=0)
        found = jnp.where(head % 2 == 0, found[:, :HD], found[:, HD:])
        text[i] = found.astype(jnp.bfloat16)
        if text_t is not None:
            text_t[i] = found.T.astype(jnp.bfloat16)


def project_kernel(slots, count, rows, shard, width, text_dev, scalars, gain, *refs):
    refs = list(refs)
    take = lambda n: [refs.pop(0) for _ in range(n)]
    mod_in = take(9)
    w_in = take(8)
    qkv, k_t, raw_all, inv_all, text, text_t, w_keep, w_give = take(8)
    w_all, mod_all, sems, extra, qkv_s, k_t_s, raw_s, inv_s = take(8)
    inner = slots * HD
    core = scalars[0]
    copies = Copies(sems)
    w_copies = copies.weights(scalars, w_in, w_all, shard)
    row_copies = copies.rows(core, mod_in, mod_all, rows)

    lane = lax.broadcasted_iota(jnp.int32, (1, 2 * inner), 1)
    gains = head_gains(gain, slots) * jnp.where(lane < inner, HD ** (-0.5), 1.0)
    identity = equal_blocks(inner, 1)
    for copy in w_copies:
        copy.wait()
    half = width // 2
    out_copies = []
    for holder, target in ((core, w_keep), (1 - core, w_give)):
        source = w_all.at[pl.ds(pl.multiple_of(holder * half, 16), half)]
        out_copies.append(copies.start(source, target))
    for copy in row_copies:
        copy.wait()
    projected = jnp.dot(mod_all[:, :width], w_all[:, : 3 * inner], preferred_element_type=jnp.float32)
    raw = projected[:, : 2 * inner]
    raw_s[...] = raw
    out_copies.append(copies.start(raw_s, raw_all))
    inverse = lax.rsqrt(head_means(raw * raw) + 1e-06)
    inv_s[...] = inverse
    out_copies.append(copies.start(inv_s, inv_all))
    qkv_s[:, : 2 * inner] = (raw * inverse * gains).astype(jnp.bfloat16)
    qkv_s[:, 2 * inner :] = projected[:, 2 * inner :].astype(jnp.bfloat16)
    out_copies.append(copies.start(qkv_s, qkv))
    k_t_s[...] = dot(identity, qkv_s[:, inner : 2 * inner], NT).astype(jnp.bfloat16)
    out_copies.append(copies.start(k_t_s, k_t))
    window_heads(scalars, count, rows, text_dev, mod_all, width, extra, text, text_t)
    for copy in out_copies:
        copy.wait()


def attend_kernel(slots, count, rows, shard, width, text_dev, first_column, scalars, gain, *refs):
    refs = list(refs)
    take = lambda n: [refs.pop(0) for _ in range(n)]
    projected = take(8)
    cot_in = take(7)
    w_in = take(4)
    mine_near, mine_far, theirs_near, theirs_far, rest_out = take(5)
    w_out, cot_all, sems, extra, values_text = take(5)
    d_all, grads, stacked = take(3)
    qkv, k_t, raw_all, inv_all, text, text_t, w_keep, w_give = refs
    inner = slots * HD
    tokens = rows * count
    core = scalars[0]
    copies = Copies(sems)
    w_copies = copies.weights(scalars, w_in, w_out, shard, first_column)
    row_copies = copies.rows(core, cot_in, cot_all, rows)
    local_copies = [copies.start(*one) for one in zip(projected, refs)]
    score_scale = HD ** (-0.5)
    span = 2 * rows

    text_rows = count * text_dev
    row = lax.broadcasted_iota(jnp.int32, (text_rows, span), 0)
    text_id = row
    for k in range(count):
        inside = (row >= k * text_dev) & (row < (k + 1) * text_dev)
        text_id = jnp.where(inside, row + (scalars[7 + k] - k) * text_dev, text_id)
    bias = jnp.where(text_id < scalars[6], 0.0, -1e30)

    for copy in w_copies:
        copy.wait()
    arrivals = [row_copies[:3], row_copies[3:]]
    for b in range(count // 2):
        for copy in arrivals[b]:
            copy.wait()
        here = slice(b * span, (b + 1) * span)
        out_grad = jnp.dot(cot_all[here, :width], w_out[...], preferred_element_type=jnp.float32)
        d_all[here, :] = out_grad.astype(jnp.bfloat16)
    window_heads(scalars, count, rows, text_dev, cot_all, width, extra, values_text)
    for copy in local_copies[:6]:
        copy.wait()

    d_first = d_all.shape[1] - inner
    for i in range(slots):
        columns = [slice(n * inner + i * HD, n * inner + (i + 1) * HD) for n in range(3)]
        keys = jnp.concatenate([qkv[:, columns[1]], text[i]], axis=0)
        values = jnp.concatenate([qkv[:, columns[2]], values_text[i]], axis=0)
        keys_t = k_t[i * HD : (i + 1) * HD, :]
        grad_k, grad_v = 0.0, 0.0
        for b in range(count // 2):
            here = slice(b * span, (b + 1) * span)
            query = qkv[here, columns[0]]
            grad = d_all[here, d_first + i * HD : d_first + (i + 1) * HD]
            scores = dot(keys, query, NT)
            text_scores = scores[tokens:] + bias
            scores = scores[:tokens]
            col_max = jnp.maximum(
                jnp.max(scores, axis=0, keepdims=True), jnp.max(text_scores, axis=0, keepdims=True)
            )
            exps = jnp.exp(scores - col_max)
            text_exps = jnp.exp(text_scores - col_max)
            total = jnp.sum(exps, axis=0, keepdims=True) + jnp.sum(text_exps, axis=0, keepdims=True)
            inverse = 1.0 / total
            grad_w = dot(values, grad, NT)
            text_grad_w = grad_w[tokens:]
            grad_w = grad_w[:tokens]
            delta = inverse * (
                jnp.sum(exps * grad_w, axis=0, keepdims=True)
                + jnp.sum(text_exps * text_grad_w, axis=0, keepdims=True)
            )
            weights = exps * inverse
            grad_s = (weights * (grad_w - delta)).astype(jnp.bfloat16)
            text_grad_s = (text_exps * inverse * (text_grad_w - delta)).astype(jnp.bfloat16)
            grad_k += dot(grad_s, query, NN)
            grad_v += dot(weights.astype(jnp.bfloat16), grad, NN)
            grad_q = dot(keys_t, grad_s, NN) + dot(text_t[i], text_grad_s, NN)
            grads[here, columns[0]] = grad_q.T * score_scale
        grads[:, columns[1]] = grad_k
        grads[:, columns[2]] = grad_v

    lane = lax.broadcasted_iota(jnp.int32, (1, inner), 1)
    mine = jnp.zeros((1, inner), jnp.float32)
    for i in range(slots):
        inside = (lane >= i * HD) & (lane < (i + 1) * HD) & (scalars[7 + count + i] > 0)
        mine = jnp.where(inside, 1.0, mine)
    gains = head_gains(gain, slots)
    for b in range(count // 2):
        here = slice(b * span, (b + 1) * span)
        scaled = grads[here, : 2 * inner].astype(jnp.bfloat16).astype(jnp.float32) * gains
        raw, inverse = raw_all[here, :], inv_all[here, :]
        back = scaled * inverse - raw * head_means(scaled * raw) * (inverse * inverse * inverse)
        valid = jnp.concatenate([mine, mine], axis=1) > 0.0
        stacked[here, : 2 * inner] = jnp.where(valid, back, 0.0).astype(jnp.bfloat16)
        back = jnp.where(mine > 0.0, grads[here, 2 * inner :], 0.0).astype(jnp.bfloat16)
        stacked[here, 2 * inner : 3 * inner] = back
    stacked[:, 3 * inner :] = jnp.zeros((tokens, stacked.shape[1] - 3 * inner), jnp.bfloat16)
    first = stacked[rows : 2 * rows, :]
    rest_out[: (count - 2) * rows, :] = stacked[2 * rows :, :]
    rest_out[(count - 2) * rows :, :] = stacked[:rows, :]
    for copy in local_copies[6:]:
        copy.wait()
    theirs = dot(first, w_give[...], NT).astype(jnp.bfloat16)
    theirs_near[...] = theirs[: rows // 2]
    theirs_far[...] = theirs[rows // 2 :]
    mine = dot(first, w_keep[...], NT)
    mine_near[...] = mine[: rows // 2]
    mine_far[...] = mine[rows // 2 :]


def project_call(scalars, gain, mod, weights, slots, rows, text_dev, count):
    shard = weights[0].shape[0]
    columns = whole_tiles(3 * slots * HD)
    width = mod[0].shape[1] - EXTRA
    tokens = rows * count
    text_rows = text_dev * count
    f32, bf16 = jnp.float32, jnp.bfloat16
    vmem, hbm = spec(pltpu.VMEM), spec(pl.ANY)
    inner = slots * HD
    shapes = [((tokens, 3 * inner), bf16), ((inner, tokens), bf16)] + [((tokens, 2 * inner), f32)] * 2
    shapes += [((slots, text_rows, HD), bf16), ((slots, HD, text_rows), bf16)]
    shapes += [((width // 2, whole_tiles(3 * slots * HD)), bf16)] * 2
    return pl.pallas_call(
        functools.partial(project_kernel, slots, count, rows, shard, width, text_dev),
        out_shape=tuple(jax.ShapeDtypeStruct(*one) for one in shapes),
        in_specs=[spec(pltpu.SMEM), vmem] + [hbm] * (len(mod) + len(weights)),
        out_specs=(hbm,) * 4 + (vmem,) * 2 + (hbm,) * 2,
        scratch_shapes=[
            pltpu.VMEM((width, columns), bf16),
            pltpu.VMEM((tokens, width + EXTRA), bf16),
            pltpu.SemaphoreType.DMA((len(mod) + len(weights) + 10,)),
            pltpu.VMEM((count, rows // 2, EXTRA), f32),
        ]
        + [pltpu.VMEM(*one) for one in shapes[:4]],
        compiler_params=pltpu.CompilerParams(vmem_limit_bytes=GRANT),
        cost_estimate=pl.CostEstimate(
            flops=2 * tokens * width * 3 * slots * HD,
            bytes_accessed=2 * (tokens * width + columns * width) + 4 * tokens * columns,
            transcendentals=0,
        ),
    )(scalars, gain, *mod, *weights)


def attend_call(scalars, gain, operands, cot, weights, slots, rows, text_dev):
    count = operands[0].shape[0] // rows
    shard, columns = weights[0].shape
    width = cot[0].shape[1] - EXTRA
    tokens = rows * count
    inner = slots * HD
    stacked = whole_tiles(3 * inner)
    first = (columns - inner) // 128 * 128
    f32, bf16 = jnp.float32, jnp.bfloat16
    vmem, hbm = spec(pltpu.VMEM), spec(pl.ANY)
    part = (rows // 2, width // 2)
    shapes = [(part, f32)] * 2 + [(part, bf16)] * 2 + [((tokens - rows, stacked), bf16)]
    return pl.pallas_call(
        functools.partial(attend_kernel, slots, count, rows, shard, width, text_dev, first),
        out_shape=tuple(jax.ShapeDtypeStruct(*one) for one in shapes),
        in_specs=[spec(pltpu.SMEM), vmem] + [hbm] * (len(operands) + len(cot) + len(weights)),
        out_specs=(vmem,) * len(shapes),
        scratch_shapes=[
            pltpu.VMEM((width, columns - first), bf16),
            pltpu.VMEM((tokens, width + EXTRA), bf16),
            pltpu.SemaphoreType.DMA((len(operands) + len(cot) + len(weights),)),
            pltpu.VMEM((count, rows // 2, EXTRA), f32),
            pltpu.VMEM((slots, text_dev * count, HD), bf16),
            pltpu.VMEM((tokens, columns - first), bf16),
            pltpu.VMEM((tokens, 3 * inner), f32),
            pltpu.VMEM((tokens, stacked), bf16),
        ]
        + [pltpu.VMEM(one.shape, one.dtype) for one in operands],
        compiler_params=pltpu.CompilerParams(vmem_limit_bytes=GRANT),
        cost_estimate=pl.CostEstimate(
            flops=2 * tokens * width * inner + 10 * tokens * tokens * inner,
            bytes_accessed=2 * (tokens * width + columns * width),
            transcendentals=slots * tokens * tokens,
        ),
    )(scalars, gain, *operands, *cot, *weights)


def backward_kernel(own, other, w_own, w_other, *outs):
    total = dot(own[...], w_own[...], NT) + dot(other[...], w_other[...], NT)
    part = outs[0].shape[0]
    for n, out in enumerate(outs):
        out[...] = total[n * part : (n + 1) * part].astype(out.dtype)


def backward_call(own, other, w_own, w_other, part, dtype):
    rows, inner = own.shape
    half = w_own.shape[0]
    vmem = spec(pltpu.VMEM)
    return pl.pallas_call(
        backward_kernel,
        out_shape=(jax.ShapeDtypeStruct((part, half), dtype),) * (rows // part),
        in_specs=[vmem] * 4,
        out_specs=(vmem,) * (rows // part),
        compiler_params=pltpu.CompilerParams(vmem_limit_bytes=SMALL_GRANT),
        cost_estimate=pl.CostEstimate(
            flops=4 * rows * half * inner,
            bytes_accessed=4 * (rows + half) * inner + 4 * rows * half,
            transcendentals=0,
        ),
    )(own, other, w_own, w_other)


def sums_kernel(own_near, own_far, near, far, scale, normed, grad_out, sums_out):
    half = near.shape[0]
    for part, (own, moving) in enumerate(((own_near, near), (own_far, far))):
        here = slice(part * half, (part + 1) * half)
        grad = (own[...] + moving[...].astype(jnp.float32)) * scale[...]
        grad_out[here, :] = grad
        first = jnp.sum(grad, axis=-1, keepdims=True)
        second = jnp.sum(grad * normed[here, :], axis=-1, keepdims=True)
        lane = lax.broadcasted_iota(jnp.int32, (half, 128), 1)
        sums_out[here, :] = jnp.where(lane == 0, first, second)


def last_kernel(width, grad, sums, other, normed, base, inv_std, out):
    total = (sums[...] + other[...]) * (1.0 / width)
    rows = base[...] + inv_std[:, 0:1] * (
        grad[...] - total[:, 0:1] - normed[...] * total[:, 1:2]
    )
    out[...] = rows.T


def local_call(kernel, shapes, scalar_count, *operands, grant=SMALL_GRANT):
    vmem = spec(pltpu.VMEM)
    return pl.pallas_call(
        kernel,
        out_shape=tuple(jax.ShapeDtypeStruct(*one) for one in shapes),
        in_specs=[spec(pltpu.SMEM)] * scalar_count + [vmem] * (len(operands) - scalar_count),
        out_specs=(vmem,) * len(shapes),
        compiler_params=pltpu.CompilerParams(vmem_limit_bytes=grant),
        cost_estimate=pl.CostEstimate(
            flops=sum(one.size for one in operands),
            bytes_accessed=sum(one.size * one.dtype.itemsize for one in operands),
            transcendentals=0,
        ),
    )(*operands)


def shards_by_head(states, adjoint, text_kv, text_len, step_index, modulation, w_qkv, qk_gain, w_out):
    hidden_state = states[0]
    adjoint_rows = adjoint[0]
    tok_count, model_width = hidden_state.shape
    seq_count = lax.axis_size("seq")
    inner_dev = w_qkv.shape[2]
    heads_dev = inner_dev // HD
    shard = w_qkv.shape[0]
    slots = -(-heads_dev // seq_count)
    inner = slots * HD
    half_rows = tok_count // 2
    half_width = model_width // 2
    f32, bf16 = jnp.float32, jnp.bfloat16
    core = lax.axis_index("head").astype(jnp.int32)
    seq_index = lax.axis_index("seq")
    dp_index = lax.axis_index("dp")
    pin = lax.optimization_barrier

    seq_order = line_ring(seq_count)
    seq_place = ring_place(seq_order, seq_index)
    seq_next = ring_pairs(seq_order)
    swap = [(0, 1), (1, 0)]
    first_way = [(2 * p + c, 2 * (p ^ (1 + c)) + c) for p in range(4) for c in range(2)]
    second_way = [(2 * p + c, 2 * (p ^ (2 - c)) + c) for p in range(4) for c in range(2)]

    first = seq_index * heads_dev // seq_count
    stop = (seq_index + 1) * heads_dev // seq_count
    window = jnp.minimum(first, heads_dev - slots)
    valid = [(window + i >= first) & (window + i < stop) for i in range(slots)]
    owners = [ring_member(seq_order, (seq_place - k + seq_count) % seq_count) for k in range(seq_count)]
    w_index = [dp_index, dp_index ^ (1 + core), dp_index ^ (2 - core), dp_index ^ 3]
    scalars = [core] + w_index + [window, text_len[0]] + owners + valid
    scalars = jnp.stack([one.astype(jnp.int32) for one in scalars])

    def step(moving):
        return lax.ppermute(moving, "seq", seq_next)

    def other_core(moving):
        return lax.ppermute(moving, "head", swap)

    def step_back(moving):
        return lax.ppermute(moving, "seq", [(b, a) for a, b in seq_next])

    quarter = half_rows // 2

    def spread(moving):
        return [step(moving), step_back(moving)]

    def pass_on(received):
        return [step(received[0][:quarter]), step_back(received[1][quarter:])]

    mod_half, table_rows, extra = first_call(
        step_index, core[None], hidden_state, modulation.transpose(1, 0, 2), adjoint_rows, text_kv[0]
    )
    mod_near = spread(mod_half)

    w_qkv, w_out, mod_half = pin((w_qkv, w_out, mod_half))
    take = lambda c: lax.dynamic_slice(w_qkv, (0, c, window * HD), (shard, 1, inner))[:, 0]
    own_w = [
        jnp.concatenate([take(0), take(1)], axis=1),
        jnp.concatenate([take(2), lax.dynamic_slice_in_dim(w_out, window * HD, inner, 0).T], axis=1),
    ]
    w_first = [lax.ppermute(part, ("dp", "head"), first_way) for part in own_w]
    w_second = [lax.ppermute(part, ("dp", "head"), second_way) for part in own_w]

    text_dev = text_kv.shape[1]
    mod_far = pass_on(mod_near)
    clip_limit = 0.5 * (tok_count * seq_count * model_width) ** 0.5
    extra, *w_first = pin((extra, *w_first))
    cot_half, clip = cotangent_call(
        clip_limit, scalars, adjoint_rows, table_rows, text_kv[0], extra, *mod_near, mod_far[1]
    )
    cot_half, mod_far[0] = pin((cot_half, mod_far[0]))
    cot_near = spread(cot_half)
    modulated, cotangent, normed_share, scale_share, inv_std, base = local_call(
        own_kernel,
        [((tok_count, model_width + EXTRA), bf16)] * 2
        + [
            ((tok_count, half_width), f32),
            ((1, half_width), f32),
            ((tok_count, 128), f32),
            ((tok_count, half_width), f32),
        ],
        1,
        core[None],
        hidden_state,
        adjoint_rows,
        table_rows,
        text_kv[0],
        extra,
        clip,
        grant=GRANT,
    )
    def pieces(own, received):
        return [own] + [one for moved in received for one in (moved, other_core(moved))]

    mod_far = list(pin((*mod_far, modulated))[:2])
    mod_pieces = pieces(modulated, mod_near + mod_far)
    w_diagonal = [lax.ppermute(part, ("dp", "head"), second_way) for part in w_first]
    weights = [part[n] for n in range(2) for part in (own_w, w_first, w_second, w_diagonal)]
    cot_near[0] = pin((cot_near[0], w_second, w_diagonal))[0]
    cot_far = [step(cot_near[0])]

    cot_pieces = pieces(cotangent, cot_near)
    *cot_pieces, mod_pieces[-1] = pin((*cot_pieces, mod_pieces[-1]))
    *operands, w_keep, w_give = project_call(
        scalars, qk_gain, mod_pieces, weights, slots, tok_count, text_dev, seq_count
    )
    w_give, cot_far[0] = pin((w_give, *cot_far))
    cot_pieces += pieces(None, cot_far)[1:]
    given, *cot_pieces = pin((w_give, *cot_pieces))
    w_other = other_core(given)
    *first, rest = attend_call(
        scalars, qk_gain, operands + [w_keep, w_give], cot_pieces, weights[4:], slots, tok_count, text_dev
    )
    moving = [(a + other_core(b).astype(f32)).astype(bf16) for a, b in zip(first[:2], first[2:])]
    other_rest = other_core(rest)
    rest, other_rest, *_ = pin((rest, other_rest, *moving))
    own = backward_call(rest, other_rest, w_keep, w_other, half_rows, f32)
    for j in range(2, seq_count):
        moving = [step(part) for part in moving]
        moving = [
            (a + b.astype(f32)).astype(bf16) for a, b in zip(own[2 * (j - 2) : 2 * (j - 1)], moving)
        ]
    moving = [step(part) for part in moving]

    grad_scaled, sums = local_call(
        sums_kernel,
        [((tok_count, half_width), f32), ((tok_count, 128), f32)],
        0,
        *own[-2:],
        *moving,
        scale_share,
        normed_share,
    )
    (pulled,) = local_call(
        functools.partial(last_kernel, model_width),
        [((half_width, tok_count), f32)],
        0,
        grad_scaled,
        sums,
        other_core(sums),
        normed_share,
        base,
        inv_std,
    )
    return pulled.T[None]


def qk_normalize(values, gains):
    inverse = lax.rsqrt(jnp.mean(values * values, axis=-1, keepdims=True) + 1e-06)
    return ((values * inverse * gains).astype(jnp.bfloat16), inverse)


def qk_backward(values, inverse, cotangent, gains):
    scaled = cotangent.astype(jnp.float32) * gains
    return (
        scaled * inverse - values * jnp.mean(scaled * values, axis=-1, keepdims=True) * inverse**3
    )


def shards_by_row(states, adjoint, text_kv, text_len, step_index, modulation, w_qkv, qk_gain, w_out):
    hidden_state = states[0]
    adjoint_rows = adjoint[0]
    tok_count, model_width = hidden_state.shape
    seq_count = lax.axis_size("seq")
    inner_dev = w_qkv.shape[2]
    heads_dev = inner_dev // HD
    score_scale = HD ** (-0.5)
    squares = lax.psum(jnp.sum(adjoint_rows * adjoint_rows), "seq")
    clip_limit = 0.5 * (tok_count * seq_count * model_width) ** 0.5
    clip_scale = jnp.minimum(1.0, clip_limit / jnp.sqrt(squares + 1e-06))
    table_row = lax.dynamic_index_in_dim(modulation, step_index[0], 0, keepdims=False)
    offset_row = table_row[0]
    stretch = table_row[1]
    gating = table_row[2]
    widened = hidden_state.astype(jnp.float32)
    centered = widened - jnp.mean(widened, axis=-1, keepdims=True)
    inv_std = lax.rsqrt(jnp.mean(centered * centered, axis=-1, keepdims=True) + 1e-06)
    normed = centered * inv_std
    modulated = (normed * (1.0 + stretch) + offset_row).astype(jnp.bfloat16)
    cotangent = (gating * (clip_scale * adjoint_rows)).astype(jnp.bfloat16)
    contract_last = (((1,), (1,)), ((), ()))
    full_weight = lax.all_gather(w_qkv, "dp", axis=0, tiled=True).reshape(
        model_width, 3 * inner_dev
    )
    projected = jnp.dot(modulated, full_weight, preferred_element_type=jnp.float32)
    out_raw = lax.dot_general(
        cotangent,
        lax.all_gather(w_out, "dp", axis=1, tiled=True),
        contract_last,
        preferred_element_type=jnp.float32,
    )
    projected = projected.reshape(tok_count, 3, heads_dev, HD)
    queries, query_inv = qk_normalize(projected[:, 0], qk_gain[0])
    own_keys, key_inv = qk_normalize(projected[:, 1], qk_gain[1])
    own_values = projected[:, 2].astype(jnp.bfloat16)
    out_grad = out_raw.astype(jnp.bfloat16).reshape(tok_count, heads_dev, HD)
    text_keys = text_kv[0, :, 0, :]
    text_values = text_kv[0, :, 1, :]
    text_dev = text_keys.shape[0]
    rows_dev = tok_count + text_dev
    key_local = jnp.concatenate([own_keys.reshape(tok_count, inner_dev), text_keys], axis=0)
    value_local = jnp.concatenate([own_values.reshape(tok_count, inner_dev), text_values], axis=0)
    key_all, value_all = (
        lax.all_gather(key_local, "seq", axis=0, tiled=True),
        lax.all_gather(value_local, "seq", axis=0, tiled=True),
    )
    all_rows = rows_dev * seq_count
    row_ids = jnp.arange(all_rows, dtype=jnp.int32)
    owner = row_ids // rows_dev
    within = row_ids % rows_dev
    allowed = (within < tok_count) | (owner * text_dev + within - tok_count < text_len[0])
    group = 1
    while group * 2 * rows_dev <= 512 and seq_count % (group * 2) == 0:
        group = group * 2
    block_rows = group * rows_dev
    block_count = all_rows // block_rows
    key_blocks = key_all.reshape(block_count, block_rows, heads_dev, HD)
    value_blocks = value_all.reshape(block_count, block_rows, heads_dev, HD)
    mask_blocks = allowed.reshape(block_count, block_rows)

    def block_scores(key_block, mask_block):
        scores = (
            jnp.einsum("qhd,khd->qhk", queries, key_block, preferred_element_type=jnp.float32)
            * score_scale
        )
        return jnp.where(mask_block[None, None, :], scores, -1e30)

    def first_pass(carry, block):
        row_max, row_sum, row_dot = carry
        key_block, value_block, mask_block = block
        scores = block_scores(key_block, mask_block)
        new_max = jnp.maximum(row_max, jnp.max(scores, axis=-1))
        rescale = jnp.exp(row_max - new_max)
        exps = jnp.exp(scores - new_max[:, :, None])
        grad_weights = jnp.einsum(
            "qhd,khd->qhk", out_grad, value_block, preferred_element_type=jnp.float32
        )
        return (
            (
                new_max,
                row_sum * rescale + jnp.sum(exps, axis=-1),
                row_dot * rescale + jnp.sum(exps * grad_weights, axis=-1),
            ),
            None,
        )

    start_state = (
        jnp.full((tok_count, heads_dev), -1e30, jnp.float32),
        jnp.zeros((tok_count, heads_dev), jnp.float32),
        jnp.zeros((tok_count, heads_dev), jnp.float32),
    )
    (row_max, row_sum, row_dot), unused = lax.scan(
        first_pass, start_state, (key_blocks, value_blocks, mask_blocks)
    )
    log_total = row_max + jnp.log(row_sum)
    delta_row = row_dot / row_sum

    def second_pass(running, block):
        key_block, value_block, mask_block = block
        weights = jnp.exp(block_scores(key_block, mask_block) - log_total[:, :, None])
        grad_weights = jnp.einsum(
            "qhd,khd->qhk", out_grad, value_block, preferred_element_type=jnp.float32
        )
        grad_scores = (weights * (grad_weights - delta_row[:, :, None])).astype(jnp.bfloat16)
        return (
            running
            + jnp.einsum(
                "qhk,khd->qhd", grad_scores, key_block, preferred_element_type=jnp.float32
            ),
            None,
        )

    query_sum, unused = lax.scan(
        second_pass,
        jnp.zeros((tok_count, heads_dev, HD), jnp.float32),
        (key_blocks, value_blocks, mask_blocks),
    )
    grad_query = (query_sum * score_scale).astype(jnp.bfloat16)
    log_all, delta_all = (
        lax.all_gather(log_total, "seq", axis=0, tiled=True),
        lax.all_gather(delta_row, "seq", axis=0, tiled=True),
    )
    local_ids = jnp.arange(rows_dev, dtype=jnp.int32)
    local_allowed = (local_ids < tok_count) | (
        lax.axis_index("seq") * text_dev + local_ids - tok_count < text_len[0]
    )
    key_three = key_local.reshape(rows_dev, heads_dev, HD)
    value_three = value_local.reshape(rows_dev, heads_dev, HD)
    query_piece = lax.all_gather(queries.reshape(tok_count, inner_dev), "seq", axis=0, tiled=True)
    grad_piece = lax.all_gather(out_grad.reshape(tok_count, inner_dev), "seq", axis=0, tiled=True)
    piece_rows = query_piece.shape[0]
    query_rows = query_piece.reshape(piece_rows, heads_dev, HD)
    grad_rows = grad_piece.reshape(piece_rows, heads_dev, HD)
    scores = (
        jnp.einsum("qhd,khd->qhk", query_rows, key_three, preferred_element_type=jnp.float32)
        * score_scale
    )
    scores = jnp.where(local_allowed[None, None, :], scores, -1e30)
    weights = jnp.exp(scores - log_all[:, :, None])
    grad_weights = jnp.einsum(
        "qhd,khd->qhk", grad_rows, value_three, preferred_element_type=jnp.float32
    )
    grad_scores = (weights * (grad_weights - delta_all[:, :, None])).astype(jnp.bfloat16)
    rounded = weights.astype(jnp.bfloat16)
    key_sum = jnp.einsum(
        "qhk,qhd->khd", grad_scores, query_rows, preferred_element_type=jnp.float32
    )
    value_sum = jnp.einsum("qhk,qhd->khd", rounded, grad_rows, preferred_element_type=jnp.float32)
    key_sum, value_sum = (key_sum, value_sum)
    grad_key = (key_sum[:tok_count] * score_scale).astype(jnp.bfloat16)
    grad_value = value_sum[:tok_count].astype(jnp.bfloat16)
    raw_query = qk_backward(projected[:, 0], query_inv, grad_query, qk_gain[0])
    raw_key = qk_backward(projected[:, 1], key_inv, grad_key, qk_gain[1])
    stacked = jnp.stack([raw_query, raw_key, grad_value.astype(jnp.float32)], axis=1).astype(
        jnp.bfloat16
    )
    stacked = stacked.reshape(tok_count, 3 * inner_dev)
    partial_grad = lax.dot_general(
        stacked, full_weight, contract_last, preferred_element_type=jnp.float32
    )
    half_width = model_width // lax.axis_size("head")
    first_col = lax.axis_index("head") * half_width
    grad_share = lax.psum_scatter(
        partial_grad.astype(jnp.bfloat16), "head", scatter_dimension=1, tiled=True
    ).astype(jnp.float32)
    normed_share = lax.dynamic_slice_in_dim(normed, first_col, half_width, 1)
    stretch_share = lax.dynamic_slice_in_dim(stretch, first_col, half_width, 0)
    adjoint_share = lax.dynamic_slice_in_dim(adjoint_rows, first_col, half_width, 1)
    grad_scaled = grad_share * (1.0 + stretch_share)
    row_sums = jnp.stack(
        [jnp.sum(grad_scaled, axis=-1), jnp.sum(grad_scaled * normed_share, axis=-1)], axis=-1
    )
    row_sums = lax.psum(row_sums, "head")
    grad_state = inv_std * (
        grad_scaled - row_sums[:, 0:1] / model_width - normed_share * row_sums[:, 1:2] / model_width
    )
    pulled = clip_scale * adjoint_share + grad_state
    return pulled[None]


def solution(mesh):
    in_specs = (
        P("dp", "seq", None),
        P("dp", "seq", None),
        P("dp", "seq", None, "head"),
        P("dp"),
        P("dp"),
        P(),
        P("dp", None, "head"),
        P(),
        P("head", "dp"),
    )
    out_specs = P("dp", "seq", "head")
    by_head = mesh.shape["seq"] == 4 and mesh.shape["dp"] == 4 and mesh.shape["head"] == 2
    shards = shards_by_head if by_head else shards_by_row
    return jax.shard_map(shards, mesh=mesh, in_specs=in_specs, out_specs=out_specs, check_vma=False)
```

```python
import functools

import jax
import jax.numpy as jnp
from jax import lax
from jax.experimental import pallas as pl
from jax.experimental.pallas import tpu as pltpu
from jax.sharding import PartitionSpec as P

HD = 64
GRANT = 60 * 1024 * 1024
SMALL_GRANT = 24 * 1024 * 1024
EXTRA = 128
NT = (((1,), (1,)), ((), ()))
NN = (((1,), (0,)), ((), ()))


def line_ring(count):
    return [0] + list(range(1, count, 2)) + [i for i in range(count - 1, 0, -1) if i % 2 == 0]


def ring_pairs(order):
    return [(order[i], order[(i + 1) % len(order)]) for i in range(len(order))]


def ring_place(order, index):
    place = jnp.int32(0)
    for position, member in enumerate(order):
        place = jnp.where(index == member, jnp.int32(position), place)
    return place


def ring_member(order, place):
    member = jnp.int32(order[0])
    for position, value in enumerate(order):
        member = jnp.where(place == position, jnp.int32(value), member)
    return member


def dot(a, b, dims):
    return lax.dot_general(a, b, dims, preferred_element_type=jnp.float32)


def equal_blocks(columns, block):
    row = lax.broadcasted_iota(jnp.int32, (columns, columns), 0)
    column = lax.broadcasted_iota(jnp.int32, (columns, columns), 1)
    return jnp.where((row ^ column) < block, 1.0, 0.0).astype(jnp.bfloat16)


def head_means(values):
    parts = []
    for first in range(0, values.shape[1], 256):
        part = values[:, first : first + 256]
        ones = equal_blocks(part.shape[1], HD)
        high = part.astype(jnp.bfloat16)
        low = (part - high.astype(jnp.float32)).astype(jnp.bfloat16)
        parts.append(dot(high, ones, NN) + dot(low, ones, NN))
    return jnp.concatenate(parts, axis=1) * (1.0 / HD)


def head_gains(gain, slots):
    return jnp.concatenate([gain[0:1, :]] * slots + [gain[1:2, :]] * slots, axis=1)


def whole_tiles(columns):
    return -(-columns // 128) * 128


def spec(space):
    return pl.BlockSpec(memory_space=space)


def text_columns(text, part):
    rows = text[...].astype(jnp.float32)[:, part, :]
    return [rows[:, c * EXTRA : (c + 1) * EXTRA] for c in range(rows.shape[1] // EXTRA)]


def extra_columns(blocks, rows):
    filled = sum(one.shape[0] for one in blocks)
    blocks = blocks + [jnp.zeros((rows - filled, EXTRA), jnp.float32)]
    return jnp.concatenate(blocks, axis=0).astype(jnp.bfloat16)


def first_kernel(step, core, states, table, adjoint, text, out, rows_out, extra_out):
    rows = [table[c, pl.ds(step[0], 1), :] for c in range(3)]
    widened = states[...].astype(jnp.float32)
    centered = widened - jnp.mean(widened, axis=-1, keepdims=True)
    inv_std = lax.rsqrt(jnp.mean(centered * centered, axis=-1, keepdims=True) + 1e-06)
    half, width = states.shape
    out[:, :width] = (centered * inv_std * (1.0 + rows[1]) + rows[0]).astype(jnp.bfloat16)
    for c in range(3):
        rows_out[c : c + 1, :] = rows[c]
    squares = jnp.sum(adjoint[...] * adjoint[...], axis=0, keepdims=True)
    squares = jnp.sum(squares, axis=1, keepdims=True)
    terms = []
    for n in range(3):
        terms.append(squares.astype(jnp.bfloat16).astype(jnp.float32))
        squares = squares - terms[-1]
    lane = lax.broadcasted_iota(jnp.int32, (8, EXTRA), 1)
    sums = jnp.where(lane == 0, terms[0], jnp.where(lane == 1, terms[1], jnp.where(lane == 2, terms[2], 0.0)))
    extra = extra_columns(text_columns(text, 0) + [sums], half)
    out[:, width:] = extra
    extra_out[...] = extra


def first_call(step, core, states, table, adjoint, text):
    rows, width = states.shape
    half = rows // 2
    whole = lambda *shape: pl.BlockSpec(shape, lambda i, step, core: (0,) * len(shape))
    return pl.pallas_call(
        first_kernel,
        out_shape=(
            jax.ShapeDtypeStruct((half, width + EXTRA), jnp.bfloat16),
            jax.ShapeDtypeStruct((8, width), jnp.float32),
            jax.ShapeDtypeStruct((half, EXTRA), jnp.bfloat16),
        ),
        grid_spec=pltpu.PrefetchScalarGridSpec(
            num_scalar_prefetch=2,
            grid=(1,),
            in_specs=[
                pl.BlockSpec((half, width), lambda i, step, core: (core[0], 0)),
                whole(*table.shape),
                whole(*adjoint.shape),
                whole(*text.shape),
            ],
            out_specs=(whole(half, width + EXTRA), whole(8, width), whole(half, EXTRA)),
        ),
        compiler_params=pltpu.CompilerParams(vmem_limit_bytes=GRANT),
        cost_estimate=pl.CostEstimate(flops=8 * half * width, bytes_accessed=16 * half * width, transcendentals=0),
    )(step, core, states, table, adjoint, text)


def pick_half(core, rows):
    half = rows.shape[1] // 2
    return jnp.where(core == 0, rows[:, :half], rows[:, half:])


def cotangent_kernel(limit, core, adjoint, table_rows, text, extra, previous, following, opposite, out, clip_out):
    first = previous.shape[0] - opposite.shape[0]
    row = 8 * (text.shape[2] // EXTRA)
    squares = opposite[...].astype(jnp.float32)[row - first : row - first + 1, :]
    for terms in (extra, previous, following):
        squares = squares + terms[...].astype(jnp.float32)[row : row + 1, :]
    squares = jnp.sum(squares, axis=1, keepdims=True)
    clip_scale = jnp.minimum(1.0, limit / jnp.sqrt(squares + 1e-06))
    half, width = adjoint.shape
    out[:, :width] = (table_rows[2:3, :] * (clip_scale * adjoint[...])).astype(jnp.bfloat16)
    out[:, width:] = extra_columns(text_columns(text, 1), half)
    clip_out[...] = jnp.broadcast_to(clip_scale, clip_out.shape)


def cotangent_call(limit, core, adjoint, table_rows, text, extra, previous, following, opposite):
    rows, width = adjoint.shape
    half = rows // 2
    block = width // EXTRA
    whole = lambda one: pl.BlockSpec(one.shape, lambda i, core: (0,) * one.ndim)
    tail = lambda one: pl.BlockSpec((one.shape[0], EXTRA), lambda i, core: (0, block))
    outs = (
        jax.ShapeDtypeStruct((half, width + EXTRA), jnp.bfloat16),
        jax.ShapeDtypeStruct((8, EXTRA), jnp.float32),
    )
    return pl.pallas_call(
        functools.partial(cotangent_kernel, limit),
        out_shape=outs,
        grid_spec=pltpu.PrefetchScalarGridSpec(
            num_scalar_prefetch=1,
            grid=(1,),
            in_specs=[pl.BlockSpec((half, width), lambda i, core: (core[0], 0))]
            + [whole(table_rows), whole(text), whole(extra)]
            + [tail(one) for one in (previous, following, opposite)],
            out_specs=tuple(whole(one) for one in outs),
        ),
        compiler_params=pltpu.CompilerParams(vmem_limit_bytes=GRANT),
        cost_estimate=pl.CostEstimate(flops=4 * half * width, bytes_accessed=6 * half * width, transcendentals=0),
    )(core, adjoint, table_rows, text, extra, previous, following, opposite)


def own_kernel(
    core, states, adjoint, table_rows, text, extra, clip, out, cot_out, normed_out, stretch_out, inv_out, base_out
):
    rows, width = states.shape
    half = rows // 2
    widened = states[...].astype(jnp.float32)
    centered = widened - jnp.mean(widened, axis=-1, keepdims=True)
    inv_std = lax.rsqrt(jnp.mean(centered * centered, axis=-1, keepdims=True) + 1e-06)
    normed = centered * inv_std
    scale = 1.0 + table_rows[1:2, :]
    out[:, :width] = (normed * scale + table_rows[0:1, :]).astype(jnp.bfloat16)
    normed_out[...] = pick_half(core[0], normed)
    stretch_out[...] = pick_half(core[0], scale)
    inv_out[...] = jnp.broadcast_to(inv_std, inv_out.shape)
    clipped = clip[0:1, 0:1] * adjoint[...]
    cot_out[:, :width] = (table_rows[2:3, :] * clipped).astype(jnp.bfloat16)
    base_out[...] = pick_half(core[0], clipped)
    columns = extra_columns(text_columns(text, 1), half)
    for n in range(2):
        out[n * half : (n + 1) * half, width:] = extra[...]
        cot_out[n * half : (n + 1) * half, width:] = columns


class Copies:
    def __init__(self, sems):
        self.sems = sems
        self.count = 0

    def start(self, source, target):
        copy = pltpu.make_async_copy(source, target, self.sems.at[self.count])
        copy.start()
        self.count += 1
        return copy

    def weights(self, scalars, w_in, w_all, shard, first=0):
        part = w_in[0].shape[1]
        copies = []
        for n, piece in enumerate(w_in):
            there = n // 4 * (part - first)
            columns = min(part - first, w_all.shape[1] - there)
            copies.append(
                self.start(
                    piece.at[:, pl.ds(first, columns)],
                    w_all.at[
                        pl.ds(pl.multiple_of(scalars[1 + n % 4] * shard, 16), shard),
                        pl.ds(there, columns),
                    ],
                )
            )
        return copies

    def rows(self, core, pieces, target, rows):
        half = rows // 2
        copies = [self.start(pieces[0], target.at[pl.ds(0, rows)])]
        places = [(rows, half), (3 * rows, half)]
        parts = (len(pieces) - 5) // 2
        places += [(2 * rows + n * half // parts, half // parts) for n in range(parts)]
        for n, (first, size) in enumerate(places):
            for m, holder in enumerate((core, 1 - core)):
                there = pl.ds(pl.multiple_of(first + holder * half, 16), size)
                copies.append(self.start(pieces[1 + 2 * n + m], target.at[there]))
        return copies


def window_heads(scalars, count, rows, text_dev, gathered, width, extra, text, text_t=None):
    half = rows // 2
    for k in range(count):
        there = pl.ds(pl.multiple_of(k * rows + scalars[0] * half, 16), half)
        extra[k] = gathered[there, width:].astype(jnp.float32)
    for i in range(text.shape[0]):
        head = scalars[5] + i
        first = pl.ds(pl.multiple_of(head // 2 * text_dev, 8), text_dev)
        found = jnp.concatenate([extra[k, first, :] for k in range(count)], axis=0)
        found = jnp.where(head % 2 == 0, found[:, :HD], found[:, HD:])
        text[i] = found.astype(jnp.bfloat16)
        if text_t is not None:
            text_t[i] = found.T.astype(jnp.bfloat16)


def project_kernel(slots, count, rows, shard, width, text_dev, scalars, gain, *refs):
    refs = list(refs)
    take = lambda n: [refs.pop(0) for _ in range(n)]
    mod_in = take(9)
    w_in = take(8)
    qkv, k_t, raw_all, inv_all, text, text_t, w_keep, w_give = take(8)
    w_all, mod_all, sems, extra, qkv_s, k_t_s, raw_s, inv_s = take(8)
    inner = slots * HD
    core = scalars[0]
    copies = Copies(sems)
    w_copies = copies.weights(scalars, w_in, w_all, shard)
    row_copies = copies.rows(core, mod_in, mod_all, rows)

    lane = lax.broadcasted_iota(jnp.int32, (1, 2 * inner), 1)
    gains = head_gains(gain, slots) * jnp.where(lane < inner, HD ** (-0.5), 1.0)
    identity = equal_blocks(inner, 1)
    for copy in w_copies:
        copy.wait()
    half = width // 2
    out_copies = []
    for holder, target in ((core, w_keep), (1 - core, w_give)):
        source = w_all.at[pl.ds(pl.multiple_of(holder * half, 16), half)]
        out_copies.append(copies.start(source, target))
    for copy in row_copies:
        copy.wait()
    projected = jnp.dot(mod_all[:, :width], w_all[:, : 3 * inner], preferred_element_type=jnp.float32)
    raw = projected[:, : 2 * inner]
    raw_s[...] = raw
    out_copies.append(copies.start(raw_s, raw_all))
    inverse = lax.rsqrt(head_means(raw * raw) + 1e-06)
    inv_s[...] = inverse
    out_copies.append(copies.start(inv_s, inv_all))
    qkv_s[:, : 2 * inner] = (raw * inverse * gains).astype(jnp.bfloat16)
    qkv_s[:, 2 * inner :] = projected[:, 2 * inner :].astype(jnp.bfloat16)
    out_copies.append(copies.start(qkv_s, qkv))
    k_t_s[...] = dot(identity, qkv_s[:, inner : 2 * inner], NT).astype(jnp.bfloat16)
    out_copies.append(copies.start(k_t_s, k_t))
    window_heads(scalars, count, rows, text_dev, mod_all, width, extra, text, text_t)
    for copy in out_copies:
        copy.wait()


def attend_kernel(slots, count, rows, shard, width, text_dev, first_column, scalars, gain, *refs):
    refs = list(refs)
    take = lambda n: [refs.pop(0) for _ in range(n)]
    projected = take(8)
    cot_in = take(7)
    w_in = take(4)
    mine_near, mine_far, theirs_near, theirs_far, rest_out = take(5)
    w_out, cot_all, sems, extra, values_text = take(5)
    d_all, grads, stacked = take(3)
    qkv, k_t, raw_all, inv_all, text, text_t, w_keep, w_give = refs
    inner = slots * HD
    tokens = rows * count
    core = scalars[0]
    copies = Copies(sems)
    w_copies = copies.weights(scalars, w_in, w_out, shard, first_column)
    row_copies = copies.rows(core, cot_in, cot_all, rows)
    local_copies = [copies.start(*one) for one in zip(projected, refs)]
    score_scale = HD ** (-0.5)
    span = 2 * rows

    text_rows = count * text_dev
    row = lax.broadcasted_iota(jnp.int32, (text_rows, span), 0)
    text_id = row
    for k in range(count):
        inside = (row >= k * text_dev) & (row < (k + 1) * text_dev)
        text_id = jnp.where(inside, row + (scalars[7 + k] - k) * text_dev, text_id)
    bias = jnp.where(text_id < scalars[6], 0.0, -1e30)

    for copy in w_copies:
        copy.wait()
    arrivals = [row_copies[:3], row_copies[3:]]
    for b in range(count // 2):
        for copy in arrivals[b]:
            copy.wait()
        here = slice(b * span, (b + 1) * span)
        out_grad = jnp.dot(cot_all[here, :width], w_out[...], preferred_element_type=jnp.float32)
        d_all[here, :] = out_grad.astype(jnp.bfloat16)
    window_heads(scalars, count, rows, text_dev, cot_all, width, extra, values_text)
    for copy in local_copies[:6]:
        copy.wait()

    d_first = d_all.shape[1] - inner
    for i in range(slots):
        columns = [slice(n * inner + i * HD, n * inner + (i + 1) * HD) for n in range(3)]
        keys = jnp.concatenate([qkv[:, columns[1]], text[i]], axis=0)
        values = jnp.concatenate([qkv[:, columns[2]], values_text[i]], axis=0)
        keys_t = k_t[i * HD : (i + 1) * HD, :]
        grad_k, grad_v = 0.0, 0.0
        for b in range(count // 2):
            here = slice(b * span, (b + 1) * span)
            query = qkv[here, columns[0]]
            grad = d_all[here, d_first + i * HD : d_first + (i + 1) * HD]
            scores = dot(keys, query, NT)
            text_scores = scores[tokens:] + bias
            scores = scores[:tokens]
            col_max = jnp.maximum(
                jnp.max(scores, axis=0, keepdims=True), jnp.max(text_scores, axis=0, keepdims=True)
            )
            exps = jnp.exp(scores - col_max)
            text_exps = jnp.exp(text_scores - col_max)
            total = jnp.sum(exps, axis=0, keepdims=True) + jnp.sum(text_exps, axis=0, keepdims=True)
            inverse = 1.0 / total
            grad_w = dot(values, grad, NT)
            text_grad_w = grad_w[tokens:]
            grad_w = grad_w[:tokens]
            delta = inverse * (
                jnp.sum(exps * grad_w, axis=0, keepdims=True)
                + jnp.sum(text_exps * text_grad_w, axis=0, keepdims=True)
            )
            weights = exps * inverse
            grad_s = (weights * (grad_w - delta)).astype(jnp.bfloat16)
            text_grad_s = (text_exps * inverse * (text_grad_w - delta)).astype(jnp.bfloat16)
            grad_k += dot(grad_s, query, NN)
            grad_v += dot(weights.astype(jnp.bfloat16), grad, NN)
            grad_q = dot(keys_t, grad_s, NN) + dot(text_t[i], text_grad_s, NN)
            grads[here, columns[0]] = grad_q.T * score_scale
        grads[:, columns[1]] = grad_k
        grads[:, columns[2]] = grad_v

    lane = lax.broadcasted_iota(jnp.int32, (1, inner), 1)
    mine = jnp.zeros((1, inner), jnp.float32)
    for i in range(slots):
        inside = (lane >= i * HD) & (lane < (i + 1) * HD) & (scalars[7 + count + i] > 0)
        mine = jnp.where(inside, 1.0, mine)
    gains = head_gains(gain, slots)
    for b in range(count // 2):
        here = slice(b * span, (b + 1) * span)
        scaled = grads[here, : 2 * inner].astype(jnp.bfloat16).astype(jnp.float32) * gains
        raw, inverse = raw_all[here, :], inv_all[here, :]
        back = scaled * inverse - raw * head_means(scaled * raw) * (inverse * inverse * inverse)
        valid = jnp.concatenate([mine, mine], axis=1) > 0.0
        stacked[here, : 2 * inner] = jnp.where(valid, back, 0.0).astype(jnp.bfloat16)
        back = jnp.where(mine > 0.0, grads[here, 2 * inner :], 0.0).astype(jnp.bfloat16)
        stacked[here, 2 * inner : 3 * inner] = back
    stacked[:, 3 * inner :] = jnp.zeros((tokens, stacked.shape[1] - 3 * inner), jnp.bfloat16)
    first = stacked[rows : 2 * rows, :]
    rest_out[: (count - 2) * rows, :] = stacked[2 * rows :, :]
    rest_out[(count - 2) * rows :, :] = stacked[:rows, :]
    for copy in local_copies[6:]:
        copy.wait()
    theirs = dot(first, w_give[...], NT).astype(jnp.bfloat16)
    theirs_near[...] = theirs[: rows // 2]
    theirs_far[...] = theirs[rows // 2 :]
    mine = dot(first, w_keep[...], NT)
    mine_near[...] = mine[: rows // 2]
    mine_far[...] = mine[rows // 2 :]


def project_call(scalars, gain, mod, weights, slots, rows, text_dev, count):
    shard = weights[0].shape[0]
    columns = whole_tiles(3 * slots * HD)
    width = mod[0].shape[1] - EXTRA
    tokens = rows * count
    text_rows = text_dev * count
    f32, bf16 = jnp.float32, jnp.bfloat16
    vmem, hbm = spec(pltpu.VMEM), spec(pl.ANY)
    inner = slots * HD
    shapes = [((tokens, 3 * inner), bf16), ((inner, tokens), bf16)] + [((tokens, 2 * inner), f32)] * 2
    shapes += [((slots, text_rows, HD), bf16), ((slots, HD, text_rows), bf16)]
    shapes += [((width // 2, whole_tiles(3 * slots * HD)), bf16)] * 2
    return pl.pallas_call(
        functools.partial(project_kernel, slots, count, rows, shard, width, text_dev),
        out_shape=tuple(jax.ShapeDtypeStruct(*one) for one in shapes),
        in_specs=[spec(pltpu.SMEM), vmem] + [hbm] * (len(mod) + len(weights)),
        out_specs=(hbm,) * 4 + (vmem,) * 2 + (hbm,) * 2,
        scratch_shapes=[
            pltpu.VMEM((width, columns), bf16),
            pltpu.VMEM((tokens, width + EXTRA), bf16),
            pltpu.SemaphoreType.DMA((len(mod) + len(weights) + 10,)),
            pltpu.VMEM((count, rows // 2, EXTRA), f32),
        ]
        + [pltpu.VMEM(*one) for one in shapes[:4]],
        compiler_params=pltpu.CompilerParams(vmem_limit_bytes=GRANT),
        cost_estimate=pl.CostEstimate(
            flops=2 * tokens * width * 3 * slots * HD,
            bytes_accessed=2 * (tokens * width + columns * width) + 4 * tokens * columns,
            transcendentals=0,
        ),
    )(scalars, gain, *mod, *weights)


def attend_call(scalars, gain, operands, cot, weights, slots, rows, text_dev):
    count = operands[0].shape[0] // rows
    shard, columns = weights[0].shape
    width = cot[0].shape[1] - EXTRA
    tokens = rows * count
    inner = slots * HD
    stacked = whole_tiles(3 * inner)
    first = (columns - inner) // 128 * 128
    f32, bf16 = jnp.float32, jnp.bfloat16
    vmem, hbm = spec(pltpu.VMEM), spec(pl.ANY)
    part = (rows // 2, width // 2)
    shapes = [(part, f32)] * 2 + [(part, bf16)] * 2 + [((tokens - rows, stacked), bf16)]
    return pl.pallas_call(
        functools.partial(attend_kernel, slots, count, rows, shard, width, text_dev, first),
        out_shape=tuple(jax.ShapeDtypeStruct(*one) for one in shapes),
        in_specs=[spec(pltpu.SMEM), vmem] + [hbm] * (len(operands) + len(cot) + len(weights)),
        out_specs=(vmem,) * len(shapes),
        scratch_shapes=[
            pltpu.VMEM((width, columns - first), bf16),
            pltpu.VMEM((tokens, width + EXTRA), bf16),
            pltpu.SemaphoreType.DMA((len(operands) + len(cot) + len(weights),)),
            pltpu.VMEM((count, rows // 2, EXTRA), f32),
            pltpu.VMEM((slots, text_dev * count, HD), bf16),
            pltpu.VMEM((tokens, columns - first), bf16),
            pltpu.VMEM((tokens, 3 * inner), f32),
            pltpu.VMEM((tokens, stacked), bf16),
        ]
        + [pltpu.VMEM(one.shape, one.dtype) for one in operands],
        compiler_params=pltpu.CompilerParams(vmem_limit_bytes=GRANT),
        cost_estimate=pl.CostEstimate(
            flops=2 * tokens * width * inner + 10 * tokens * tokens * inner,
            bytes_accessed=2 * (tokens * width + columns * width),
            transcendentals=slots * tokens * tokens,
        ),
    )(scalars, gain, *operands, *cot, *weights)


def backward_kernel(own, other, w_own, w_other, *outs):
    total = dot(own[...], w_own[...], NT) + dot(other[...], w_other[...], NT)
    part = outs[0].shape[0]
    for n, out in enumerate(outs):
        out[...] = total[n * part : (n + 1) * part].astype(out.dtype)


def backward_call(own, other, w_own, w_other, part, dtype):
    rows, inner = own.shape
    half = w_own.shape[0]
    vmem = spec(pltpu.VMEM)
    return pl.pallas_call(
        backward_kernel,
        out_shape=(jax.ShapeDtypeStruct((part, half), dtype),) * (rows // part),
        in_specs=[vmem] * 4,
        out_specs=(vmem,) * (rows // part),
        compiler_params=pltpu.CompilerParams(vmem_limit_bytes=SMALL_GRANT),
        cost_estimate=pl.CostEstimate(
            flops=4 * rows * half * inner,
            bytes_accessed=4 * (rows + half) * inner + 4 * rows * half,
            transcendentals=0,
        ),
    )(own, other, w_own, w_other)


def sums_kernel(own_near, own_far, near, far, scale, normed, grad_out, sums_out):
    half = near.shape[0]
    for part, (own, moving) in enumerate(((own_near, near), (own_far, far))):
        here = slice(part * half, (part + 1) * half)
        grad = (own[...] + moving[...].astype(jnp.float32)) * scale[...]
        grad_out[here, :] = grad
        first = jnp.sum(grad, axis=-1, keepdims=True)
        second = jnp.sum(grad * normed[here, :], axis=-1, keepdims=True)
        lane = lax.broadcasted_iota(jnp.int32, (half, 128), 1)
        sums_out[here, :] = jnp.where(lane == 0, first, second)


def last_kernel(width, grad, sums, other, normed, base, inv_std, out):
    total = (sums[...] + other[...]) * (1.0 / width)
    rows = base[...] + inv_std[:, 0:1] * (
        grad[...] - total[:, 0:1] - normed[...] * total[:, 1:2]
    )
    out[...] = rows.T


def local_call(kernel, shapes, scalar_count, *operands, grant=SMALL_GRANT):
    vmem = spec(pltpu.VMEM)
    return pl.pallas_call(
        kernel,
        out_shape=tuple(jax.ShapeDtypeStruct(*one) for one in shapes),
        in_specs=[spec(pltpu.SMEM)] * scalar_count + [vmem] * (len(operands) - scalar_count),
        out_specs=(vmem,) * len(shapes),
        compiler_params=pltpu.CompilerParams(vmem_limit_bytes=grant),
        cost_estimate=pl.CostEstimate(
            flops=sum(one.size for one in operands),
            bytes_accessed=sum(one.size * one.dtype.itemsize for one in operands),
            transcendentals=0,
        ),
    )(*operands)


def shards_by_head(states, adjoint, text_kv, text_len, step_index, modulation, w_qkv, qk_gain, w_out):
    hidden_state = states[0]
    adjoint_rows = adjoint[0]
    tok_count, model_width = hidden_state.shape
    seq_count = lax.axis_size("seq")
    inner_dev = w_qkv.shape[2]
    heads_dev = inner_dev // HD
    shard = w_qkv.shape[0]
    slots = -(-heads_dev // seq_count)
    inner = slots * HD
    half_rows = tok_count // 2
    half_width = model_width // 2
    f32, bf16 = jnp.float32, jnp.bfloat16
    core = lax.axis_index("head").astype(jnp.int32)
    seq_index = lax.axis_index("seq")
    dp_index = lax.axis_index("dp")
    pin = lax.optimization_barrier

    seq_order = line_ring(seq_count)
    seq_place = ring_place(seq_order, seq_index)
    seq_next = ring_pairs(seq_order)
    swap = [(0, 1), (1, 0)]
    first_way = [(2 * p + c, 2 * (p ^ (1 + c)) + c) for p in range(4) for c in range(2)]
    second_way = [(2 * p + c, 2 * (p ^ (2 - c)) + c) for p in range(4) for c in range(2)]

    first = seq_index * heads_dev // seq_count
    stop = (seq_index + 1) * heads_dev // seq_count
    window = jnp.minimum(first, heads_dev - slots)
    valid = [(window + i >= first) & (window + i < stop) for i in range(slots)]
    owners = [ring_member(seq_order, (seq_place - k + seq_count) % seq_count) for k in range(seq_count)]
    w_index = [dp_index, dp_index ^ (1 + core), dp_index ^ (2 - core), dp_index ^ 3]
    scalars = [core] + w_index + [window, text_len[0]] + owners + valid
    scalars = jnp.stack([one.astype(jnp.int32) for one in scalars])

    def step(moving):
        return lax.ppermute(moving, "seq", seq_next)

    def other_core(moving):
        return lax.ppermute(moving, "head", swap)

    def step_back(moving):
        return lax.ppermute(moving, "seq", [(b, a) for a, b in seq_next])

    quarter = half_rows // 2

    def spread(moving):
        return [step(moving), step_back(moving)]

    def pass_on(received):
        return [step(received[0][:quarter]), step_back(received[1][quarter:])]

    mod_half, table_rows, extra = first_call(
        step_index, core[None], hidden_state, modulation.transpose(1, 0, 2), adjoint_rows, text_kv[0]
    )
    mod_near = spread(mod_half)

    w_qkv, w_out, mod_half = pin((w_qkv, w_out, mod_half))
    take = lambda c: lax.dynamic_slice(w_qkv, (0, c, window * HD), (shard, 1, inner))[:, 0]
    own_w = [
        jnp.concatenate([take(0), take(1)], axis=1),
        jnp.concatenate([take(2), lax.dynamic_slice_in_dim(w_out, window * HD, inner, 0).T], axis=1),
    ]
    w_first = [lax.ppermute(part, ("dp", "head"), first_way) for part in own_w]
    w_second = [lax.ppermute(part, ("dp", "head"), second_way) for part in own_w]

    text_dev = text_kv.shape[1]
    mod_far = pass_on(mod_near)
    clip_limit = 0.5 * (tok_count * seq_count * model_width) ** 0.5
    extra, *w_first = pin((extra, *w_first))
    cot_half, clip = cotangent_call(
        clip_limit, scalars, adjoint_rows, table_rows, text_kv[0], extra, *mod_near, mod_far[1]
    )
    cot_half, mod_far[0] = pin((cot_half, mod_far[0]))
    cot_near = spread(cot_half)
    modulated, cotangent, normed_share, scale_share, inv_std, base = local_call(
        own_kernel,
        [((tok_count, model_width + EXTRA), bf16)] * 2
        + [
            ((tok_count, half_width), f32),
            ((1, half_width), f32),
            ((tok_count, 128), f32),
            ((tok_count, half_width), f32),
        ],
        1,
        core[None],
        hidden_state,
        adjoint_rows,
        table_rows,
        text_kv[0],
        extra,
        clip,
        grant=GRANT,
    )
    def pieces(own, received):
        return [own] + [one for moved in received for one in (moved, other_core(moved))]

    mod_far = list(pin((*mod_far, modulated))[:2])
    mod_pieces = pieces(modulated, mod_near + mod_far)
    w_diagonal = [lax.ppermute(part, ("dp", "head"), second_way) for part in w_first]
    weights = [part[n] for n in range(2) for part in (own_w, w_first, w_second, w_diagonal)]
    cot_near[0] = pin((cot_near[0], w_second, w_diagonal))[0]
    cot_far = [step(cot_near[0])]

    cot_pieces = pieces(cotangent, cot_near)
    *cot_pieces, mod_pieces[-1] = pin((*cot_pieces, mod_pieces[-1]))
    *operands, w_keep, w_give = project_call(
        scalars, qk_gain, mod_pieces, weights, slots, tok_count, text_dev, seq_count
    )
    w_give, cot_far[0] = pin((w_give, *cot_far))
    cot_pieces += pieces(None, cot_far)[1:]
    given, *cot_pieces = pin((w_give, *cot_pieces))
    w_other = other_core(given)
    *first, rest = attend_call(
        scalars, qk_gain, operands + [w_keep, w_give], cot_pieces, weights[4:], slots, tok_count, text_dev
    )
    moving = [(a + other_core(b).astype(f32)).astype(bf16) for a, b in zip(first[:2], first[2:])]
    other_rest = other_core(rest)
    rest, other_rest, *_ = pin((rest, other_rest, *moving))
    own = backward_call(rest, other_rest, w_keep, w_other, half_rows, f32)
    for j in range(2, seq_count):
        moving = [step(part) for part in moving]
        moving = [
            (a + b.astype(f32)).astype(bf16) for a, b in zip(own[2 * (j - 2) : 2 * (j - 1)], moving)
        ]
    moving = [step(part) for part in moving]

    grad_scaled, sums = local_call(
        sums_kernel,
        [((tok_count, half_width), f32), ((tok_count, 128), f32)],
        0,
        *own[-2:],
        *moving,
        scale_share,
        normed_share,
    )
    (pulled,) = local_call(
        functools.partial(last_kernel, model_width),
        [((half_width, tok_count), f32)],
        0,
        grad_scaled,
        sums,
        other_core(sums),
        normed_share,
        base,
        inv_std,
    )
    return pulled.T[None]


def qk_normalize(values, gains):
    inverse = lax.rsqrt(jnp.mean(values * values, axis=-1, keepdims=True) + 1e-06)
    return ((values * inverse * gains).astype(jnp.bfloat16), inverse)


def qk_backward(values, inverse, cotangent, gains):
    scaled = cotangent.astype(jnp.float32) * gains
    return (
        scaled * inverse - values * jnp.mean(scaled * values, axis=-1, keepdims=True) * inverse**3
    )


def shards_by_row(states, adjoint, text_kv, text_len, step_index, modulation, w_qkv, qk_gain, w_out):
    hidden_state = states[0]
    adjoint_rows = adjoint[0]
    tok_count, model_width = hidden_state.shape
    seq_count = lax.axis_size("seq")
    inner_dev = w_qkv.shape[2]
    heads_dev = inner_dev // HD
    score_scale = HD ** (-0.5)
    squares = lax.psum(jnp.sum(adjoint_rows * adjoint_rows), "seq")
    clip_limit = 0.5 * (tok_count * seq_count * model_width) ** 0.5
    clip_scale = jnp.minimum(1.0, clip_limit / jnp.sqrt(squares + 1e-06))
    table_row = lax.dynamic_index_in_dim(modulation, step_index[0], 0, keepdims=False)
    offset_row = table_row[0]
    stretch = table_row[1]
    gating = table_row[2]
    widened = hidden_state.astype(jnp.float32)
    centered = widened - jnp.mean(widened, axis=-1, keepdims=True)
    inv_std = lax.rsqrt(jnp.mean(centered * centered, axis=-1, keepdims=True) + 1e-06)
    normed = centered * inv_std
    modulated = (normed * (1.0 + stretch) + offset_row).astype(jnp.bfloat16)
    cotangent = (gating * (clip_scale * adjoint_rows)).astype(jnp.bfloat16)
    contract_last = (((1,), (1,)), ((), ()))
    full_weight = lax.all_gather(w_qkv, "dp", axis=0, tiled=True).reshape(
        model_width, 3 * inner_dev
    )
    projected = jnp.dot(modulated, full_weight, preferred_element_type=jnp.float32)
    out_raw = lax.dot_general(
        cotangent,
        lax.all_gather(w_out, "dp", axis=1, tiled=True),
        contract_last,
        preferred_element_type=jnp.float32,
    )
    projected = projected.reshape(tok_count, 3, heads_dev, HD)
    queries, query_inv = qk_normalize(projected[:, 0], qk_gain[0])
    own_keys, key_inv = qk_normalize(projected[:, 1], qk_gain[1])
    own_values = projected[:, 2].astype(jnp.bfloat16)
    out_grad = out_raw.astype(jnp.bfloat16).reshape(tok_count, heads_dev, HD)
    text_keys = text_kv[0, :, 0, :]
    text_values = text_kv[0, :, 1, :]
    text_dev = text_keys.shape[0]
    rows_dev = tok_count + text_dev
    key_local = jnp.concatenate([own_keys.reshape(tok_count, inner_dev), text_keys], axis=0)
    value_local = jnp.concatenate([own_values.reshape(tok_count, inner_dev), text_values], axis=0)
    key_all, value_all = (
        lax.all_gather(key_local, "seq", axis=0, tiled=True),
        lax.all_gather(value_local, "seq", axis=0, tiled=True),
    )
    all_rows = rows_dev * seq_count
    row_ids = jnp.arange(all_rows, dtype=jnp.int32)
    owner = row_ids // rows_dev
    within = row_ids % rows_dev
    allowed = (within < tok_count) | (owner * text_dev + within - tok_count < text_len[0])
    group = 1
    while group * 2 * rows_dev <= 512 and seq_count % (group * 2) == 0:
        group = group * 2
    block_rows = group * rows_dev
    block_count = all_rows // block_rows
    key_blocks = key_all.reshape(block_count, block_rows, heads_dev, HD)
    value_blocks = value_all.reshape(block_count, block_rows, heads_dev, HD)
    mask_blocks = allowed.reshape(block_count, block_rows)

    def block_scores(key_block, mask_block):
        scores = (
            jnp.einsum("qhd,khd->qhk", queries, key_block, preferred_element_type=jnp.float32)
            * score_scale
        )
        return jnp.where(mask_block[None, None, :], scores, -1e30)

    def first_pass(carry, block):
        row_max, row_sum, row_dot = carry
        key_block, value_block, mask_block = block
        scores = block_scores(key_block, mask_block)
        new_max = jnp.maximum(row_max, jnp.max(scores, axis=-1))
        rescale = jnp.exp(row_max - new_max)
        exps = jnp.exp(scores - new_max[:, :, None])
        grad_weights = jnp.einsum(
            "qhd,khd->qhk", out_grad, value_block, preferred_element_type=jnp.float32
        )
        return (
            (
                new_max,
                row_sum * rescale + jnp.sum(exps, axis=-1),
                row_dot * rescale + jnp.sum(exps * grad_weights, axis=-1),
            ),
            None,
        )

    start_state = (
        jnp.full((tok_count, heads_dev), -1e30, jnp.float32),
        jnp.zeros((tok_count, heads_dev), jnp.float32),
        jnp.zeros((tok_count, heads_dev), jnp.float32),
    )
    (row_max, row_sum, row_dot), unused = lax.scan(
        first_pass, start_state, (key_blocks, value_blocks, mask_blocks)
    )
    log_total = row_max + jnp.log(row_sum)
    delta_row = row_dot / row_sum

    def second_pass(running, block):
        key_block, value_block, mask_block = block
        weights = jnp.exp(block_scores(key_block, mask_block) - log_total[:, :, None])
        grad_weights = jnp.einsum(
            "qhd,khd->qhk", out_grad, value_block, preferred_element_type=jnp.float32
        )
        grad_scores = (weights * (grad_weights - delta_row[:, :, None])).astype(jnp.bfloat16)
        return (
            running
            + jnp.einsum(
                "qhk,khd->qhd", grad_scores, key_block, preferred_element_type=jnp.float32
            ),
            None,
        )

    query_sum, unused = lax.scan(
        second_pass,
        jnp.zeros((tok_count, heads_dev, HD), jnp.float32),
        (key_blocks, value_blocks, mask_blocks),
    )
    grad_query = (query_sum * score_scale).astype(jnp.bfloat16)
    log_all, delta_all = (
        lax.all_gather(log_total, "seq", axis=0, tiled=True),
        lax.all_gather(delta_row, "seq", axis=0, tiled=True),
    )
    local_ids = jnp.arange(rows_dev, dtype=jnp.int32)
    local_allowed = (local_ids < tok_count) | (
        lax.axis_index("seq") * text_dev + local_ids - tok_count < text_len[0]
    )
    key_three = key_local.reshape(rows_dev, heads_dev, HD)
    value_three = value_local.reshape(rows_dev, heads_dev, HD)
    query_piece = lax.all_gather(queries.reshape(tok_count, inner_dev), "seq", axis=0, tiled=True)
    grad_piece = lax.all_gather(out_grad.reshape(tok_count, inner_dev), "seq", axis=0, tiled=True)
    piece_rows = query_piece.shape[0]
    query_rows = query_piece.reshape(piece_rows, heads_dev, HD)
    grad_rows = grad_piece.reshape(piece_rows, heads_dev, HD)
    scores = (
        jnp.einsum("qhd,khd->qhk", query_rows, key_three, preferred_element_type=jnp.float32)
        * score_scale
    )
    scores = jnp.where(local_allowed[None, None, :], scores, -1e30)
    weights = jnp.exp(scores - log_all[:, :, None])
    grad_weights = jnp.einsum(
        "qhd,khd->qhk", grad_rows, value_three, preferred_element_type=jnp.float32
    )
    grad_scores = (weights * (grad_weights - delta_all[:, :, None])).astype(jnp.bfloat16)
    rounded = weights.astype(jnp.bfloat16)
    key_sum = jnp.einsum(
        "qhk,qhd->khd", grad_scores, query_rows, preferred_element_type=jnp.float32
    )
    value_sum = jnp.einsum("qhk,qhd->khd", rounded, grad_rows, preferred_element_type=jnp.float32)
    key_sum, value_sum = (key_sum, value_sum)
    grad_key = (key_sum[:tok_count] * score_scale).astype(jnp.bfloat16)
    grad_value = value_sum[:tok_count].astype(jnp.bfloat16)
    raw_query = qk_backward(projected[:, 0], query_inv, grad_query, qk_gain[0])
    raw_key = qk_backward(projected[:, 1], key_inv, grad_key, qk_gain[1])
    stacked = jnp.stack([raw_query, raw_key, grad_value.astype(jnp.float32)], axis=1).astype(
        jnp.bfloat16
    )
    stacked = stacked.reshape(tok_count, 3 * inner_dev)
    partial_grad = lax.dot_general(
        stacked, full_weight, contract_last, preferred_element_type=jnp.float32
    )
    half_width = model_width // lax.axis_size("head")
    first_col = lax.axis_index("head") * half_width
    grad_share = lax.psum_scatter(
        partial_grad.astype(jnp.bfloat16), "head", scatter_dimension=1, tiled=True
    ).astype(jnp.float32)
    normed_share = lax.dynamic_slice_in_dim(normed, first_col, half_width, 1)
    stretch_share = lax.dynamic_slice_in_dim(stretch, first_col, half_width, 0)
    adjoint_share = lax.dynamic_slice_in_dim(adjoint_rows, first_col, half_width, 1)
    grad_scaled = grad_share * (1.0 + stretch_share)
    row_sums = jnp.stack(
        [jnp.sum(grad_scaled, axis=-1), jnp.sum(grad_scaled * normed_share, axis=-1)], axis=-1
    )
    row_sums = lax.psum(row_sums, "head")
    grad_state = inv_std * (
        grad_scaled - row_sums[:, 0:1] / model_width - normed_share * row_sums[:, 1:2] / model_width
    )
    pulled = clip_scale * adjoint_share + grad_state
    return pulled[None]


def solution(mesh):
    in_specs = (
        P("dp", "seq", None),
        P("dp", "seq", None),
        P("dp", "seq", None, "head"),
        P("dp"),
        P("dp"),
        P(),
        P("dp", None, "head"),
        P(),
        P("head", "dp"),
    )
    out_specs = P("dp", "seq", "head")
    by_head = mesh.shape["seq"] == 4 and mesh.shape["dp"] == 4 and mesh.shape["head"] == 2
    shards = shards_by_head if by_head else shards_by_row
    return jax.shard_map(shards, mesh=mesh, in_specs=in_specs, out_specs=out_specs, check_vma=False)
```

```python
import functools

import jax
import jax.numpy as jnp
from jax import lax
from jax.experimental import pallas as pl
from jax.experimental.pallas import tpu as pltpu
from jax.sharding import PartitionSpec as P

HD = 64
GRANT = 60 * 1024 * 1024
SMALL_GRANT = 24 * 1024 * 1024
EXTRA = 128
NT = (((1,), (1,)), ((), ()))
NN = (((1,), (0,)), ((), ()))


def line_ring(count):
    return [0] + list(range(1, count, 2)) + [i for i in range(count - 1, 0, -1) if i % 2 == 0]


def ring_pairs(order):
    return [(order[i], order[(i + 1) % len(order)]) for i in range(len(order))]


def ring_place(order, index):
    place = jnp.int32(0)
    for position, member in enumerate(order):
        place = jnp.where(index == member, jnp.int32(position), place)
    return place


def ring_member(order, place):
    member = jnp.int32(order[0])
    for position, value in enumerate(order):
        member = jnp.where(place == position, jnp.int32(value), member)
    return member


def dot(a, b, dims):
    return lax.dot_general(a, b, dims, preferred_element_type=jnp.float32)


def equal_blocks(columns, block):
    row = lax.broadcasted_iota(jnp.int32, (columns, columns), 0)
    column = lax.broadcasted_iota(jnp.int32, (columns, columns), 1)
    return jnp.where((row ^ column) < block, 1.0, 0.0).astype(jnp.bfloat16)


def head_means(values):
    parts = []
    for first in range(0, values.shape[1], 256):
        part = values[:, first : first + 256]
        ones = equal_blocks(part.shape[1], HD)
        high = part.astype(jnp.bfloat16)
        low = (part - high.astype(jnp.float32)).astype(jnp.bfloat16)
        parts.append(dot(high, ones, NN) + dot(low, ones, NN))
    return jnp.concatenate(parts, axis=1) * (1.0 / HD)


def head_gains(gain, slots):
    return jnp.concatenate([gain[0:1, :]] * slots + [gain[1:2, :]] * slots, axis=1)


def whole_tiles(columns):
    return -(-columns // 128) * 128


def spec(space):
    return pl.BlockSpec(memory_space=space)


def text_columns(text, part):
    rows = text[...].astype(jnp.float32)[:, part, :]
    return [rows[:, c * EXTRA : (c + 1) * EXTRA] for c in range(rows.shape[1] // EXTRA)]


def extra_columns(blocks, rows):
    filled = sum(one.shape[0] for one in blocks)
    blocks = blocks + [jnp.zeros((rows - filled, EXTRA), jnp.float32)]
    return jnp.concatenate(blocks, axis=0).astype(jnp.bfloat16)


def first_kernel(step, core, states, table, adjoint, text, out, rows_out, extra_out):
    rows = [table[c, pl.ds(step[0], 1), :] for c in range(3)]
    widened = states[...].astype(jnp.float32)
    centered = widened - jnp.mean(widened, axis=-1, keepdims=True)
    inv_std = lax.rsqrt(jnp.mean(centered * centered, axis=-1, keepdims=True) + 1e-06)
    half, width = states.shape
    out[:, :width] = (centered * inv_std * (1.0 + rows[1]) + rows[0]).astype(jnp.bfloat16)
    for c in range(3):
        rows_out[c : c + 1, :] = rows[c]
    squares = jnp.sum(adjoint[...] * adjoint[...], axis=0, keepdims=True)
    squares = jnp.sum(squares, axis=1, keepdims=True)
    terms = []
    for n in range(3):
        terms.append(squares.astype(jnp.bfloat16).astype(jnp.float32))
        squares = squares - terms[-1]
    lane = lax.broadcasted_iota(jnp.int32, (8, EXTRA), 1)
    sums = jnp.where(lane == 0, terms[0], jnp.where(lane == 1, terms[1], jnp.where(lane == 2, terms[2], 0.0)))
    extra = extra_columns(text_columns(text, 0) + [sums], half)
    out[:, width:] = extra
    extra_out[...] = extra


def first_call(step, core, states, table, adjoint, text):
    rows, width = states.shape
    half = rows // 2
    whole = lambda *shape: pl.BlockSpec(shape, lambda i, step, core: (0,) * len(shape))
    return pl.pallas_call(
        first_kernel,
        out_shape=(
            jax.ShapeDtypeStruct((half, width + EXTRA), jnp.bfloat16),
            jax.ShapeDtypeStruct((8, width), jnp.float32),
            jax.ShapeDtypeStruct((half, EXTRA), jnp.bfloat16),
        ),
        grid_spec=pltpu.PrefetchScalarGridSpec(
            num_scalar_prefetch=2,
            grid=(1,),
            in_specs=[
                pl.BlockSpec((half, width), lambda i, step, core: (core[0], 0)),
                whole(*table.shape),
                whole(*adjoint.shape),
                whole(*text.shape),
            ],
            out_specs=(whole(half, width + EXTRA), whole(8, width), whole(half, EXTRA)),
        ),
        compiler_params=pltpu.CompilerParams(vmem_limit_bytes=GRANT),
        cost_estimate=pl.CostEstimate(flops=8 * half * width, bytes_accessed=16 * half * width, transcendentals=0),
    )(step, core, states, table, adjoint, text)


def pick_half(core, rows):
    half = rows.shape[1] // 2
    return jnp.where(core == 0, rows[:, :half], rows[:, half:])


def cotangent_kernel(limit, core, adjoint, table_rows, text, extra, previous, following, opposite, out, clip_out):
    first = previous.shape[0] - opposite.shape[0]
    row = 8 * (text.shape[2] // EXTRA)
    squares = opposite[...].astype(jnp.float32)[row - first : row - first + 1, :]
    for terms in (extra, previous, following):
        squares = squares + terms[...].astype(jnp.float32)[row : row + 1, :]
    squares = jnp.sum(squares, axis=1, keepdims=True)
    clip_scale = jnp.minimum(1.0, limit / jnp.sqrt(squares + 1e-06))
    half, width = adjoint.shape
    out[:, :width] = (table_rows[2:3, :] * (clip_scale * adjoint[...])).astype(jnp.bfloat16)
    out[:, width:] = extra_columns(text_columns(text, 1), half)
    clip_out[...] = jnp.broadcast_to(clip_scale, clip_out.shape)


def cotangent_call(limit, core, adjoint, table_rows, text, extra, previous, following, opposite):
    rows, width = adjoint.shape
    half = rows // 2
    block = width // EXTRA
    whole = lambda one: pl.BlockSpec(one.shape, lambda i, core: (0,) * one.ndim)
    tail = lambda one: pl.BlockSpec((one.shape[0], EXTRA), lambda i, core: (0, block))
    outs = (
        jax.ShapeDtypeStruct((half, width + EXTRA), jnp.bfloat16),
        jax.ShapeDtypeStruct((8, EXTRA), jnp.float32),
    )
    return pl.pallas_call(
        functools.partial(cotangent_kernel, limit),
        out_shape=outs,
        grid_spec=pltpu.PrefetchScalarGridSpec(
            num_scalar_prefetch=1,
            grid=(1,),
            in_specs=[pl.BlockSpec((half, width), lambda i, core: (core[0], 0))]
            + [whole(table_rows), whole(text), whole(extra)]
            + [tail(one) for one in (previous, following)]
            + [whole(opposite)],
            out_specs=tuple(whole(one) for one in outs),
        ),
        compiler_params=pltpu.CompilerParams(vmem_limit_bytes=GRANT),
        cost_estimate=pl.CostEstimate(flops=4 * half * width, bytes_accessed=6 * half * width, transcendentals=0),
    )(core, adjoint, table_rows, text, extra, previous, following, opposite)


def own_kernel(
    core, states, adjoint, table_rows, text, extra, clip, out, cot_out, normed_out, stretch_out, inv_out, base_out
):
    rows, width = states.shape
    half = rows // 2
    widened = states[...].astype(jnp.float32)
    centered = widened - jnp.mean(widened, axis=-1, keepdims=True)
    inv_std = lax.rsqrt(jnp.mean(centered * centered, axis=-1, keepdims=True) + 1e-06)
    normed = centered * inv_std
    scale = 1.0 + table_rows[1:2, :]
    out[:, :width] = (normed * scale + table_rows[0:1, :]).astype(jnp.bfloat16)
    normed_out[...] = pick_half(core[0], normed)
    stretch_out[...] = pick_half(core[0], scale)
    inv_out[...] = jnp.broadcast_to(inv_std, inv_out.shape)
    clipped = clip[0:1, 0:1] * adjoint[...]
    cot_out[:, :width] = (table_rows[2:3, :] * clipped).astype(jnp.bfloat16)
    base_out[...] = pick_half(core[0], clipped)
    columns = extra_columns(text_columns(text, 1), half)
    for n in range(2):
        out[n * half : (n + 1) * half, width:] = extra[...]
        cot_out[n * half : (n + 1) * half, width:] = columns


class Copies:
    def __init__(self, sems):
        self.sems = sems
        self.count = 0

    def start(self, source, target):
        copy = pltpu.make_async_copy(source, target, self.sems.at[self.count])
        copy.start()
        self.count += 1
        return copy

    def weights(self, scalars, w_in, w_all, shard, first=0):
        part = w_in[0].shape[1]
        copies = []
        for n, piece in enumerate(w_in):
            there = n // 4 * (part - first)
            columns = min(part - first, w_all.shape[1] - there)
            copies.append(
                self.start(
                    piece.at[:, pl.ds(first, columns)],
                    w_all.at[
                        pl.ds(pl.multiple_of(scalars[1 + n % 4] * shard, 16), shard),
                        pl.ds(there, columns),
                    ],
                )
            )
        return copies

    def rows(self, core, pieces, target, rows):
        half = rows // 2
        copies = [self.start(pieces[0], target.at[pl.ds(0, rows)])]
        places = [(rows, half), (3 * rows, half)]
        parts = (len(pieces) - 5) // 2
        places += [(2 * rows + n * half // parts, half // parts) for n in range(parts)]
        for n, (first, size) in enumerate(places):
            for m, holder in enumerate((core, 1 - core)):
                there = pl.ds(pl.multiple_of(first + holder * half, 16), size)
                copies.append(self.start(pieces[1 + 2 * n + m], target.at[there]))
        return copies


def window_heads(scalars, count, rows, text_dev, gathered, width, extra, text, text_t=None):
    half = rows // 2
    for k in range(count):
        there = pl.ds(pl.multiple_of(k * rows + scalars[0] * half, 16), half)
        extra[k] = gathered[there, width:].astype(jnp.float32)
    for i in range(text.shape[0]):
        head = scalars[5] + i
        first = pl.ds(pl.multiple_of(head // 2 * text_dev, 8), text_dev)
        found = jnp.concatenate([extra[k, first, :] for k in range(count)], axis=0)
        found = jnp.where(head % 2 == 0, found[:, :HD], found[:, HD:])
        text[i] = found.astype(jnp.bfloat16)
        if text_t is not None:
            text_t[i] = found.T.astype(jnp.bfloat16)


def project_kernel(slots, count, rows, shard, width, text_dev, scalars, gain, *refs):
    refs = list(refs)
    take = lambda n: [refs.pop(0) for _ in range(n)]
    mod_in = take(9)
    w_in = take(8)
    qkv, k_t, raw_all, inv_all, text, text_t, w_keep, w_give = take(8)
    w_all, mod_all, sems, extra, qkv_s, k_t_s, raw_s, inv_s = take(8)
    inner = slots * HD
    core = scalars[0]
    copies = Copies(sems)
    w_copies = copies.weights(scalars, w_in, w_all, shard)
    row_copies = copies.rows(core, mod_in, mod_all, rows)

    lane = lax.broadcasted_iota(jnp.int32, (1, 2 * inner), 1)
    gains = head_gains(gain, slots) * jnp.where(lane < inner, HD ** (-0.5), 1.0)
    identity = equal_blocks(inner, 1)
    for copy in w_copies:
        copy.wait()
    half = width // 2
    out_copies = []
    for holder, target in ((core, w_keep), (1 - core, w_give)):
        source = w_all.at[pl.ds(pl.multiple_of(holder * half, 16), half)]
        out_copies.append(copies.start(source, target))
    for copy in row_copies:
        copy.wait()
    projected = jnp.dot(mod_all[:, :width], w_all[:, : 3 * inner], preferred_element_type=jnp.float32)
    raw = projected[:, : 2 * inner]
    raw_s[...] = raw
    out_copies.append(copies.start(raw_s, raw_all))
    inverse = lax.rsqrt(head_means(raw * raw) + 1e-06)
    inv_s[...] = inverse
    out_copies.append(copies.start(inv_s, inv_all))
    qkv_s[:, : 2 * inner] = (raw * inverse * gains).astype(jnp.bfloat16)
    qkv_s[:, 2 * inner :] = projected[:, 2 * inner :].astype(jnp.bfloat16)
    out_copies.append(copies.start(qkv_s, qkv))
    k_t_s[...] = dot(identity, qkv_s[:, inner : 2 * inner], NT).astype(jnp.bfloat16)
    out_copies.append(copies.start(k_t_s, k_t))
    window_heads(scalars, count, rows, text_dev, mod_all, width, extra, text, text_t)
    for copy in out_copies:
        copy.wait()


def attend_kernel(slots, count, rows, shard, width, text_dev, first_column, scalars, gain, *refs):
    refs = list(refs)
    take = lambda n: [refs.pop(0) for _ in range(n)]
    projected = take(8)
    cot_in = take(7)
    w_in = take(4)
    mine_near, mine_far, theirs_near, theirs_far, rest_out = take(5)
    w_out, cot_all, sems, extra, values_text = take(5)
    d_all, grads, stacked = take(3)
    qkv, k_t, raw_all, inv_all, text, text_t, w_keep, w_give = refs
    inner = slots * HD
    tokens = rows * count
    core = scalars[0]
    copies = Copies(sems)
    w_copies = copies.weights(scalars, w_in, w_out, shard, first_column)
    row_copies = copies.rows(core, cot_in, cot_all, rows)
    local_copies = [copies.start(*one) for one in zip(projected, refs)]
    score_scale = HD ** (-0.5)
    span = 2 * rows

    text_rows = count * text_dev
    row = lax.broadcasted_iota(jnp.int32, (text_rows, span), 0)
    text_id = row
    for k in range(count):
        inside = (row >= k * text_dev) & (row < (k + 1) * text_dev)
        text_id = jnp.where(inside, row + (scalars[7 + k] - k) * text_dev, text_id)
    bias = jnp.where(text_id < scalars[6], 0.0, -1e30)

    for copy in w_copies:
        copy.wait()
    arrivals = [row_copies[:3], row_copies[3:]]
    for b in range(count // 2):
        for copy in arrivals[b]:
            copy.wait()
        here = slice(b * span, (b + 1) * span)
        out_grad = jnp.dot(cot_all[here, :width], w_out[...], preferred_element_type=jnp.float32)
        d_all[here, :] = out_grad.astype(jnp.bfloat16)
    window_heads(scalars, count, rows, text_dev, cot_all, width, extra, values_text)
    for copy in local_copies[:6]:
        copy.wait()

    d_first = d_all.shape[1] - inner
    for i in range(slots):
        columns = [slice(n * inner + i * HD, n * inner + (i + 1) * HD) for n in range(3)]
        keys = jnp.concatenate([qkv[:, columns[1]], text[i]], axis=0)
        values = jnp.concatenate([qkv[:, columns[2]], values_text[i]], axis=0)
        keys_t = k_t[i * HD : (i + 1) * HD, :]
        grad_k, grad_v = 0.0, 0.0
        for b in range(count // 2):
            here = slice(b * span, (b + 1) * span)
            query = qkv[here, columns[0]]
            grad = d_all[here, d_first + i * HD : d_first + (i + 1) * HD]
            scores = dot(keys, query, NT)
            text_scores = scores[tokens:] + bias
            scores = scores[:tokens]
            col_max = jnp.maximum(
                jnp.max(scores, axis=0, keepdims=True), jnp.max(text_scores, axis=0, keepdims=True)
            )
            exps = jnp.exp(scores - col_max)
            text_exps = jnp.exp(text_scores - col_max)
            total = jnp.sum(exps, axis=0, keepdims=True) + jnp.sum(text_exps, axis=0, keepdims=True)
            inverse = 1.0 / total
            grad_w = dot(values, grad, NT)
            text_grad_w = grad_w[tokens:]
            grad_w = grad_w[:tokens]
            delta = inverse * (
                jnp.sum(exps * grad_w, axis=0, keepdims=True)
                + jnp.sum(text_exps * text_grad_w, axis=0, keepdims=True)
            )
            weights = exps * inverse
            grad_s = (weights * (grad_w - delta)).astype(jnp.bfloat16)
            text_grad_s = (text_exps * inverse * (text_grad_w - delta)).astype(jnp.bfloat16)
            grad_k += dot(grad_s, query, NN)
            grad_v += dot(weights.astype(jnp.bfloat16), grad, NN)
            grad_q = dot(keys_t, grad_s, NN) + dot(text_t[i], text_grad_s, NN)
            grads[here, columns[0]] = grad_q.T * score_scale
        grads[:, columns[1]] = grad_k
        grads[:, columns[2]] = grad_v

    lane = lax.broadcasted_iota(jnp.int32, (1, inner), 1)
    mine = jnp.zeros((1, inner), jnp.float32)
    for i in range(slots):
        inside = (lane >= i * HD) & (lane < (i + 1) * HD) & (scalars[7 + count + i] > 0)
        mine = jnp.where(inside, 1.0, mine)
    gains = head_gains(gain, slots)
    for b in range(count // 2):
        here = slice(b * span, (b + 1) * span)
        scaled = grads[here, : 2 * inner].astype(jnp.bfloat16).astype(jnp.float32) * gains
        raw, inverse = raw_all[here, :], inv_all[here, :]
        back = scaled * inverse - raw * head_means(scaled * raw) * (inverse * inverse * inverse)
        valid = jnp.concatenate([mine, mine], axis=1) > 0.0
        stacked[here, : 2 * inner] = jnp.where(valid, back, 0.0).astype(jnp.bfloat16)
        back = jnp.where(mine > 0.0, grads[here, 2 * inner :], 0.0).astype(jnp.bfloat16)
        stacked[here, 2 * inner : 3 * inner] = back
    stacked[:, 3 * inner :] = jnp.zeros((tokens, stacked.shape[1] - 3 * inner), jnp.bfloat16)
    first = stacked[rows : 2 * rows, :]
    rest_out[: (count - 2) * rows, :] = stacked[2 * rows :, :]
    rest_out[(count - 2) * rows :, :] = stacked[:rows, :]
    for copy in local_copies[6:]:
        copy.wait()
    theirs = dot(first, w_give[...], NT).astype(jnp.bfloat16)
    theirs_near[...] = theirs[: rows // 2]
    theirs_far[...] = theirs[rows // 2 :]
    mine = dot(first, w_keep[...], NT)
    mine_near[...] = mine[: rows // 2]
    mine_far[...] = mine[rows // 2 :]


def project_call(scalars, gain, mod, weights, slots, rows, text_dev, count):
    shard = weights[0].shape[0]
    columns = whole_tiles(3 * slots * HD)
    width = mod[0].shape[1] - EXTRA
    tokens = rows * count
    text_rows = text_dev * count
    f32, bf16 = jnp.float32, jnp.bfloat16
    vmem, hbm = spec(pltpu.VMEM), spec(pl.ANY)
    inner = slots * HD
    shapes = [((tokens, 3 * inner), bf16), ((inner, tokens), bf16)] + [((tokens, 2 * inner), f32)] * 2
    shapes += [((slots, text_rows, HD), bf16), ((slots, HD, text_rows), bf16)]
    shapes += [((width // 2, whole_tiles(3 * slots * HD)), bf16)] * 2
    return pl.pallas_call(
        functools.partial(project_kernel, slots, count, rows, shard, width, text_dev),
        out_shape=tuple(jax.ShapeDtypeStruct(*one) for one in shapes),
        in_specs=[spec(pltpu.SMEM), vmem] + [hbm] * (len(mod) + len(weights)),
        out_specs=(hbm,) * 4 + (vmem,) * 2 + (hbm,) * 2,
        scratch_shapes=[
            pltpu.VMEM((width, columns), bf16),
            pltpu.VMEM((tokens, width + EXTRA), bf16),
            pltpu.SemaphoreType.DMA((len(mod) + len(weights) + 10,)),
            pltpu.VMEM((count, rows // 2, EXTRA), f32),
        ]
        + [pltpu.VMEM(*one) for one in shapes[:4]],
        compiler_params=pltpu.CompilerParams(vmem_limit_bytes=GRANT),
        cost_estimate=pl.CostEstimate(
            flops=2 * tokens * width * 3 * slots * HD,
            bytes_accessed=2 * (tokens * width + columns * width) + 4 * tokens * columns,
            transcendentals=0,
        ),
    )(scalars, gain, *mod, *weights)


def attend_call(scalars, gain, operands, cot, weights, slots, rows, text_dev):
    count = operands[0].shape[0] // rows
    shard, columns = weights[0].shape
    width = cot[0].shape[1] - EXTRA
    tokens = rows * count
    inner = slots * HD
    stacked = whole_tiles(3 * inner)
    first = (columns - inner) // 128 * 128
    f32, bf16 = jnp.float32, jnp.bfloat16
    vmem, hbm = spec(pltpu.VMEM), spec(pl.ANY)
    part = (rows // 2, width // 2)
    shapes = [(part, f32)] * 2 + [(part, bf16)] * 2 + [((tokens - rows, stacked), bf16)]
    return pl.pallas_call(
        functools.partial(attend_kernel, slots, count, rows, shard, width, text_dev, first),
        out_shape=tuple(jax.ShapeDtypeStruct(*one) for one in shapes),
        in_specs=[spec(pltpu.SMEM), vmem] + [hbm] * (len(operands) + len(cot) + len(weights)),
        out_specs=(vmem,) * len(shapes),
        scratch_shapes=[
            pltpu.VMEM((width, columns - first), bf16),
            pltpu.VMEM((tokens, width + EXTRA), bf16),
            pltpu.SemaphoreType.DMA((len(operands) + len(cot) + len(weights),)),
            pltpu.VMEM((count, rows // 2, EXTRA), f32),
            pltpu.VMEM((slots, text_dev * count, HD), bf16),
            pltpu.VMEM((tokens, columns - first), bf16),
            pltpu.VMEM((tokens, 3 * inner), f32),
            pltpu.VMEM((tokens, stacked), bf16),
        ]
        + [pltpu.VMEM(one.shape, one.dtype) for one in operands],
        compiler_params=pltpu.CompilerParams(vmem_limit_bytes=GRANT),
        cost_estimate=pl.CostEstimate(
            flops=2 * tokens * width * inner + 10 * tokens * tokens * inner,
            bytes_accessed=2 * (tokens * width + columns * width),
            transcendentals=slots * tokens * tokens,
        ),
    )(scalars, gain, *operands, *cot, *weights)


def backward_kernel(own, other, w_own, w_other, *outs):
    total = dot(own[...], w_own[...], NT) + dot(other[...], w_other[...], NT)
    part = outs[0].shape[0]
    for n, out in enumerate(outs):
        out[...] = total[n * part : (n + 1) * part].astype(out.dtype)


def backward_call(own, other, w_own, w_other, part, dtype):
    rows, inner = own.shape
    half = w_own.shape[0]
    vmem = spec(pltpu.VMEM)
    return pl.pallas_call(
        backward_kernel,
        out_shape=(jax.ShapeDtypeStruct((part, half), dtype),) * (rows // part),
        in_specs=[vmem] * 4,
        out_specs=(vmem,) * (rows // part),
        compiler_params=pltpu.CompilerParams(vmem_limit_bytes=SMALL_GRANT),
        cost_estimate=pl.CostEstimate(
            flops=4 * rows * half * inner,
            bytes_accessed=4 * (rows + half) * inner + 4 * rows * half,
            transcendentals=0,
        ),
    )(own, other, w_own, w_other)


def sums_kernel(own_near, own_far, near, far, scale, normed, grad_out, sums_out):
    half = near.shape[0]
    for part, (own, moving) in enumerate(((own_near, near), (own_far, far))):
        here = slice(part * half, (part + 1) * half)
        grad = (own[...] + moving[...].astype(jnp.float32)) * scale[...]
        grad_out[here, :] = grad
        first = jnp.sum(grad, axis=-1, keepdims=True)
        second = jnp.sum(grad * normed[here, :], axis=-1, keepdims=True)
        lane = lax.broadcasted_iota(jnp.int32, (half, 128), 1)
        sums_out[here, :] = jnp.where(lane == 0, first, second)


def last_kernel(width, grad, sums, other, normed, base, inv_std, out):
    total = (sums[...] + other[...]) * (1.0 / width)
    rows = base[...] + inv_std[:, 0:1] * (
        grad[...] - total[:, 0:1] - normed[...] * total[:, 1:2]
    )
    out[...] = rows.T


def local_call(kernel, shapes, scalar_count, *operands, grant=SMALL_GRANT):
    vmem = spec(pltpu.VMEM)
    return pl.pallas_call(
        kernel,
        out_shape=tuple(jax.ShapeDtypeStruct(*one) for one in shapes),
        in_specs=[spec(pltpu.SMEM)] * scalar_count + [vmem] * (len(operands) - scalar_count),
        out_specs=(vmem,) * len(shapes),
        compiler_params=pltpu.CompilerParams(vmem_limit_bytes=grant),
        cost_estimate=pl.CostEstimate(
            flops=sum(one.size for one in operands),
            bytes_accessed=sum(one.size * one.dtype.itemsize for one in operands),
            transcendentals=0,
        ),
    )(*operands)


def shards_by_head(states, adjoint, text_kv, text_len, step_index, modulation, w_qkv, qk_gain, w_out):
    hidden_state = states[0]
    adjoint_rows = adjoint[0]
    tok_count, model_width = hidden_state.shape
    seq_count = lax.axis_size("seq")
    inner_dev = w_qkv.shape[2]
    heads_dev = inner_dev // HD
    shard = w_qkv.shape[0]
    slots = -(-heads_dev // seq_count)
    inner = slots * HD
    half_rows = tok_count // 2
    half_width = model_width // 2
    f32, bf16 = jnp.float32, jnp.bfloat16
    core = lax.axis_index("head").astype(jnp.int32)
    seq_index = lax.axis_index("seq")
    dp_index = lax.axis_index("dp")
    pin = lax.optimization_barrier

    seq_order = line_ring(seq_count)
    seq_place = ring_place(seq_order, seq_index)
    seq_next = ring_pairs(seq_order)
    swap = [(0, 1), (1, 0)]
    first_way = [(2 * p + c, 2 * (p ^ (1 + c)) + c) for p in range(4) for c in range(2)]
    second_way = [(2 * p + c, 2 * (p ^ (2 - c)) + c) for p in range(4) for c in range(2)]

    first = seq_index * heads_dev // seq_count
    stop = (seq_index + 1) * heads_dev // seq_count
    window = jnp.minimum(first, heads_dev - slots)
    valid = [(window + i >= first) & (window + i < stop) for i in range(slots)]
    owners = [ring_member(seq_order, (seq_place - k + seq_count) % seq_count) for k in range(seq_count)]
    w_index = [dp_index, dp_index ^ (1 + core), dp_index ^ (2 - core), dp_index ^ 3]
    scalars = [core] + w_index + [window, text_len[0]] + owners + valid
    scalars = jnp.stack([one.astype(jnp.int32) for one in scalars])

    def step(moving):
        return lax.ppermute(moving, "seq", seq_next)

    def other_core(moving):
        return lax.ppermute(moving, "head", swap)

    def step_back(moving):
        return lax.ppermute(moving, "seq", [(b, a) for a, b in seq_next])

    quarter = half_rows // 2

    def spread(moving):
        return [step(moving), step_back(moving)]

    def pass_on(received):
        return [step(received[0][:quarter]), step_back(received[1][quarter:])]

    mod_half, table_rows, extra = first_call(
        step_index, core[None], hidden_state, modulation.transpose(1, 0, 2), adjoint_rows, text_kv[0]
    )
    mod_near = spread(mod_half)

    w_qkv, w_out, mod_half = pin((w_qkv, w_out, mod_half))
    take = lambda c: lax.dynamic_slice(w_qkv, (0, c, window * HD), (shard, 1, inner))[:, 0]
    own_w = [
        jnp.concatenate([take(0), take(1)], axis=1),
        jnp.concatenate([take(2), lax.dynamic_slice_in_dim(w_out, window * HD, inner, 0).T], axis=1),
    ]
    w_first = [lax.ppermute(part, ("dp", "head"), first_way) for part in own_w]
    w_second = [lax.ppermute(part, ("dp", "head"), second_way) for part in own_w]

    text_dev = text_kv.shape[1]
    mod_far = pass_on(mod_near)
    clip_limit = 0.5 * (tok_count * seq_count * model_width) ** 0.5
    extra, *w_first = pin((extra, *w_first))
    cot_half, clip = cotangent_call(
        clip_limit, scalars, adjoint_rows, table_rows, text_kv[0], extra, *mod_near, mod_far[1][:, model_width:]
    )
    cot_half, mod_far[0] = pin((cot_half, mod_far[0]))
    cot_near = spread(cot_half)
    modulated, cotangent, normed_share, scale_share, inv_std, base = local_call(
        own_kernel,
        [((tok_count, model_width + EXTRA), bf16)] * 2
        + [
            ((tok_count, half_width), f32),
            ((1, half_width), f32),
            ((tok_count, 128), f32),
            ((tok_count, half_width), f32),
        ],
        1,
        core[None],
        hidden_state,
        adjoint_rows,
        table_rows,
        text_kv[0],
        extra,
        clip,
        grant=GRANT,
    )
    def pieces(own, received):
        return [own] + [one for moved in received for one in (moved, other_core(moved))]

    mod_far = list(pin((*mod_far, modulated))[:2])
    mod_pieces = pieces(modulated, mod_near + mod_far)
    w_diagonal = [lax.ppermute(part, ("dp", "head"), second_way) for part in w_first]
    weights = [part[n] for n in range(2) for part in (own_w, w_first, w_second, w_diagonal)]
    cot_near[0] = pin((cot_near[0], w_second, w_diagonal))[0]
    cot_far = [step(cot_near[0])]

    cot_pieces = pieces(cotangent, cot_near)
    *cot_pieces, mod_pieces[-1] = pin((*cot_pieces, mod_pieces[-1]))
    *operands, w_keep, w_give = project_call(
        scalars, qk_gain, mod_pieces, weights, slots, tok_count, text_dev, seq_count
    )
    w_give, cot_far[0] = pin((w_give, *cot_far))
    cot_pieces += pieces(None, cot_far)[1:]
    given, *cot_pieces = pin((w_give, *cot_pieces))
    w_other = other_core(given)
    *first, rest = attend_call(
        scalars, qk_gain, operands + [w_keep, w_give], cot_pieces, weights[4:], slots, tok_count, text_dev
    )
    moving = [(a + other_core(b).astype(f32)).astype(bf16) for a, b in zip(first[:2], first[2:])]
    other_rest = other_core(rest)
    rest, other_rest, *_ = pin((rest, other_rest, *moving))
    own = backward_call(rest, other_rest, w_keep, w_other, half_rows, f32)
    for j in range(2, seq_count):
        moving = [step(part) for part in moving]
        moving = [
            (a + b.astype(f32)).astype(bf16) for a, b in zip(own[2 * (j - 2) : 2 * (j - 1)], moving)
        ]
    moving = [step(part) for part in moving]

    grad_scaled, sums = local_call(
        sums_kernel,
        [((tok_count, half_width), f32), ((tok_count, 128), f32)],
        0,
        *own[-2:],
        *moving,
        scale_share,
        normed_share,
    )
    (pulled,) = local_call(
        functools.partial(last_kernel, model_width),
        [((half_width, tok_count), f32)],
        0,
        grad_scaled,
        sums,
        other_core(sums),
        normed_share,
        base,
        inv_std,
    )
    return pulled.T[None]


def qk_normalize(values, gains):
    inverse = lax.rsqrt(jnp.mean(values * values, axis=-1, keepdims=True) + 1e-06)
    return ((values * inverse * gains).astype(jnp.bfloat16), inverse)


def qk_backward(values, inverse, cotangent, gains):
    scaled = cotangent.astype(jnp.float32) * gains
    return (
        scaled * inverse - values * jnp.mean(scaled * values, axis=-1, keepdims=True) * inverse**3
    )


def shards_by_row(states, adjoint, text_kv, text_len, step_index, modulation, w_qkv, qk_gain, w_out):
    hidden_state = states[0]
    adjoint_rows = adjoint[0]
    tok_count, model_width = hidden_state.shape
    seq_count = lax.axis_size("seq")
    inner_dev = w_qkv.shape[2]
    heads_dev = inner_dev // HD
    score_scale = HD ** (-0.5)
    squares = lax.psum(jnp.sum(adjoint_rows * adjoint_rows), "seq")
    clip_limit = 0.5 * (tok_count * seq_count * model_width) ** 0.5
    clip_scale = jnp.minimum(1.0, clip_limit / jnp.sqrt(squares + 1e-06))
    table_row = lax.dynamic_index_in_dim(modulation, step_index[0], 0, keepdims=False)
    offset_row = table_row[0]
    stretch = table_row[1]
    gating = table_row[2]
    widened = hidden_state.astype(jnp.float32)
    centered = widened - jnp.mean(widened, axis=-1, keepdims=True)
    inv_std = lax.rsqrt(jnp.mean(centered * centered, axis=-1, keepdims=True) + 1e-06)
    normed = centered * inv_std
    modulated = (normed * (1.0 + stretch) + offset_row).astype(jnp.bfloat16)
    cotangent = (gating * (clip_scale * adjoint_rows)).astype(jnp.bfloat16)
    contract_last = (((1,), (1,)), ((), ()))
    full_weight = lax.all_gather(w_qkv, "dp", axis=0, tiled=True).reshape(
        model_width, 3 * inner_dev
    )
    projected = jnp.dot(modulated, full_weight, preferred_element_type=jnp.float32)
    out_raw = lax.dot_general(
        cotangent,
        lax.all_gather(w_out, "dp", axis=1, tiled=True),
        contract_last,
        preferred_element_type=jnp.float32,
    )
    projected = projected.reshape(tok_count, 3, heads_dev, HD)
    queries, query_inv = qk_normalize(projected[:, 0], qk_gain[0])
    own_keys, key_inv = qk_normalize(projected[:, 1], qk_gain[1])
    own_values = projected[:, 2].astype(jnp.bfloat16)
    out_grad = out_raw.astype(jnp.bfloat16).reshape(tok_count, heads_dev, HD)
    text_keys = text_kv[0, :, 0, :]
    text_values = text_kv[0, :, 1, :]
    text_dev = text_keys.shape[0]
    rows_dev = tok_count + text_dev
    key_local = jnp.concatenate([own_keys.reshape(tok_count, inner_dev), text_keys], axis=0)
    value_local = jnp.concatenate([own_values.reshape(tok_count, inner_dev), text_values], axis=0)
    key_all, value_all = (
        lax.all_gather(key_local, "seq", axis=0, tiled=True),
        lax.all_gather(value_local, "seq", axis=0, tiled=True),
    )
    all_rows = rows_dev * seq_count
    row_ids = jnp.arange(all_rows, dtype=jnp.int32)
    owner = row_ids // rows_dev
    within = row_ids % rows_dev
    allowed = (within < tok_count) | (owner * text_dev + within - tok_count < text_len[0])
    group = 1
    while group * 2 * rows_dev <= 512 and seq_count % (group * 2) == 0:
        group = group * 2
    block_rows = group * rows_dev
    block_count = all_rows // block_rows
    key_blocks = key_all.reshape(block_count, block_rows, heads_dev, HD)
    value_blocks = value_all.reshape(block_count, block_rows, heads_dev, HD)
    mask_blocks = allowed.reshape(block_count, block_rows)

    def block_scores(key_block, mask_block):
        scores = (
            jnp.einsum("qhd,khd->qhk", queries, key_block, preferred_element_type=jnp.float32)
            * score_scale
        )
        return jnp.where(mask_block[None, None, :], scores, -1e30)

    def first_pass(carry, block):
        row_max, row_sum, row_dot = carry
        key_block, value_block, mask_block = block
        scores = block_scores(key_block, mask_block)
        new_max = jnp.maximum(row_max, jnp.max(scores, axis=-1))
        rescale = jnp.exp(row_max - new_max)
        exps = jnp.exp(scores - new_max[:, :, None])
        grad_weights = jnp.einsum(
            "qhd,khd->qhk", out_grad, value_block, preferred_element_type=jnp.float32
        )
        return (
            (
                new_max,
                row_sum * rescale + jnp.sum(exps, axis=-1),
                row_dot * rescale + jnp.sum(exps * grad_weights, axis=-1),
            ),
            None,
        )

    start_state = (
        jnp.full((tok_count, heads_dev), -1e30, jnp.float32),
        jnp.zeros((tok_count, heads_dev), jnp.float32),
        jnp.zeros((tok_count, heads_dev), jnp.float32),
    )
    (row_max, row_sum, row_dot), unused = lax.scan(
        first_pass, start_state, (key_blocks, value_blocks, mask_blocks)
    )
    log_total = row_max + jnp.log(row_sum)
    delta_row = row_dot / row_sum

    def second_pass(running, block):
        key_block, value_block, mask_block = block
        weights = jnp.exp(block_scores(key_block, mask_block) - log_total[:, :, None])
        grad_weights = jnp.einsum(
            "qhd,khd->qhk", out_grad, value_block, preferred_element_type=jnp.float32
        )
        grad_scores = (weights * (grad_weights - delta_row[:, :, None])).astype(jnp.bfloat16)
        return (
            running
            + jnp.einsum(
                "qhk,khd->qhd", grad_scores, key_block, preferred_element_type=jnp.float32
            ),
            None,
        )

    query_sum, unused = lax.scan(
        second_pass,
        jnp.zeros((tok_count, heads_dev, HD), jnp.float32),
        (key_blocks, value_blocks, mask_blocks),
    )
    grad_query = (query_sum * score_scale).astype(jnp.bfloat16)
    log_all, delta_all = (
        lax.all_gather(log_total, "seq", axis=0, tiled=True),
        lax.all_gather(delta_row, "seq", axis=0, tiled=True),
    )
    local_ids = jnp.arange(rows_dev, dtype=jnp.int32)
    local_allowed = (local_ids < tok_count) | (
        lax.axis_index("seq") * text_dev + local_ids - tok_count < text_len[0]
    )
    key_three = key_local.reshape(rows_dev, heads_dev, HD)
    value_three = value_local.reshape(rows_dev, heads_dev, HD)
    query_piece = lax.all_gather(queries.reshape(tok_count, inner_dev), "seq", axis=0, tiled=True)
    grad_piece = lax.all_gather(out_grad.reshape(tok_count, inner_dev), "seq", axis=0, tiled=True)
    piece_rows = query_piece.shape[0]
    query_rows = query_piece.reshape(piece_rows, heads_dev, HD)
    grad_rows = grad_piece.reshape(piece_rows, heads_dev, HD)
    scores = (
        jnp.einsum("qhd,khd->qhk", query_rows, key_three, preferred_element_type=jnp.float32)
        * score_scale
    )
    scores = jnp.where(local_allowed[None, None, :], scores, -1e30)
    weights = jnp.exp(scores - log_all[:, :, None])
    grad_weights = jnp.einsum(
        "qhd,khd->qhk", grad_rows, value_three, preferred_element_type=jnp.float32
    )
    grad_scores = (weights * (grad_weights - delta_all[:, :, None])).astype(jnp.bfloat16)
    rounded = weights.astype(jnp.bfloat16)
    key_sum = jnp.einsum(
        "qhk,qhd->khd", grad_scores, query_rows, preferred_element_type=jnp.float32
    )
    value_sum = jnp.einsum("qhk,qhd->khd", rounded, grad_rows, preferred_element_type=jnp.float32)
    key_sum, value_sum = (key_sum, value_sum)
    grad_key = (key_sum[:tok_count] * score_scale).astype(jnp.bfloat16)
    grad_value = value_sum[:tok_count].astype(jnp.bfloat16)
    raw_query = qk_backward(projected[:, 0], query_inv, grad_query, qk_gain[0])
    raw_key = qk_backward(projected[:, 1], key_inv, grad_key, qk_gain[1])
    stacked = jnp.stack([raw_query, raw_key, grad_value.astype(jnp.float32)], axis=1).astype(
        jnp.bfloat16
    )
    stacked = stacked.reshape(tok_count, 3 * inner_dev)
    partial_grad = lax.dot_general(
        stacked, full_weight, contract_last, preferred_element_type=jnp.float32
    )
    half_width = model_width // lax.axis_size("head")
    first_col = lax.axis_index("head") * half_width
    grad_share = lax.psum_scatter(
        partial_grad.astype(jnp.bfloat16), "head", scatter_dimension=1, tiled=True
    ).astype(jnp.float32)
    normed_share = lax.dynamic_slice_in_dim(normed, first_col, half_width, 1)
    stretch_share = lax.dynamic_slice_in_dim(stretch, first_col, half_width, 0)
    adjoint_share = lax.dynamic_slice_in_dim(adjoint_rows, first_col, half_width, 1)
    grad_scaled = grad_share * (1.0 + stretch_share)
    row_sums = jnp.stack(
        [jnp.sum(grad_scaled, axis=-1), jnp.sum(grad_scaled * normed_share, axis=-1)], axis=-1
    )
    row_sums = lax.psum(row_sums, "head")
    grad_state = inv_std * (
        grad_scaled - row_sums[:, 0:1] / model_width - normed_share * row_sums[:, 1:2] / model_width
    )
    pulled = clip_scale * adjoint_share + grad_state
    return pulled[None]


def solution(mesh):
    in_specs = (
        P("dp", "seq", None),
        P("dp", "seq", None),
        P("dp", "seq", None, "head"),
        P("dp"),
        P("dp"),
        P(),
        P("dp", None, "head"),
        P(),
        P("head", "dp"),
    )
    out_specs = P("dp", "seq", "head")
    by_head = mesh.shape["seq"] == 4 and mesh.shape["dp"] == 4 and mesh.shape["head"] == 2
    shards = shards_by_head if by_head else shards_by_row
    return jax.shard_map(shards, mesh=mesh, in_specs=in_specs, out_specs=out_specs, check_vma=False)
```
